32 devices in a mesh: dp: 8 (over z, y), tensor: 4 (over x, core).
Axes of the slice: x: 2, y: 2, z: 4, core: 2. Of those that a mesh axis runs over, the one named last changes fastest.
Arguments:
- block_in: bfloat16 [20480, 1024], P(('dp', 'tensor')), may hold values from -6 to 6
- encoder_out: bfloat16 [8192, 1024], P(('dp', 'tensor')), may hold values from -6 to 6
- out_grad: bfloat16 [20480, 1024], P(('dp', 'tensor')), may hold values from -6 to 6
- bounds: int32 [8, 2], P('dp'), may hold values from 1024 to 2304, as said below
- enc_lengths: int32 [8], P('dp'), may hold values from 512 to 1024, as said below
- norm_params: float32 [3, 2, 1024], replicated, may hold values from -0.3 to 1.4, as said below
- w_qkv: bfloat16 [1024, 3, 1024], P('dp', None, 'tensor'), may hold values from -0.1875 to 0.1875
- w_self_out: bfloat16 [1024, 1024], P('tensor', 'dp'), may hold values from -0.375 to 0.375
- w_cross_q: bfloat16 [1024, 1024], P('dp', 'tensor'), may hold values from -0.1875 to 0.1875
- w_cross_kv: bfloat16 [1024, 2, 1024], P('dp', None, 'tensor'), may hold values from -0.1875 to 0.1875
- w_cross_out: bfloat16 [1024, 1024], P('tensor', 'dp'), may hold values from -0.375 to 0.375
- w_up: bfloat16 [1024, 4096], P('dp', 'tensor'), may hold values from -0.1875 to 0.1875
- w_down: bfloat16 [4096, 1024], P('tensor', 'dp'), may hold values from -0.09375 to 0.09375
- biases: float32 [7, 1024], replicated, may hold values from -1 to 1
- up_bias: float32 [4096], replicated, may hold values from -1 to 1
Outputs:
- output: float32 [20480, 1024], P(('dp', 'tensor'))
- input_grad: float32 [20480, 1024], P(('dp', 'tensor'))
- encoder_grad: float32 [8192, 1024], P(('dp', 'tensor'))
- grad_norm_params: float32 [3, 2, 1024], replicated
- grad_qkv: float32 [1024, 3, 1024], P('dp', None, 'tensor')
- grad_self_out: float32 [1024, 1024], P('tensor', 'dp')
- grad_cross_q: float32 [1024, 1024], P('dp', 'tensor')
- grad_cross_kv: float32 [1024, 2, 1024], P('dp', None, 'tensor')
- grad_cross_out: float32 [1024, 1024], P('tensor', 'dp')
- grad_up: float32 [1024, 4096], P('dp', 'tensor')
- grad_down: float32 [4096, 1024], P('tensor', 'dp')
- grad_biases: float32 [7, 1024], replicated
- grad_up_bias: float32 [4096], replicated
The draws below stay inside these ranges and needn't reach their ends.
Inputs may be any that keep to these rules, and one draw needn't show every extreme that they name: bounds[g, 0] is the length of group g's prompt, between 1024 and 2048, and equals 2048 in some group; the 2 continuations that follow are of equal length, rise in position and fill the group's 2560 tokens. Group g's valid encoder outputs are its first enc_lengths[g] rows; some group has all 1024. norm_params[i, 0] are gains, norm_params[i, 1] shifts.
All inputs are finite; a program needn't handle non-finite values.
Results may differ from the reference program's by a relative error of at most 0.02.
Values may be sent and summed in bfloat16 or wider, within the bound.
A program may use at most 256 MiB of HBM per device.

```python
import math
import jax
import jax.numpy as jnp
from jax import lax

D = 1024
H = 16
HD = 64
FF = 4096
PROMPT = 2048
CLEN = 256
CONT = 2
ENC = 1024
GROUPS = 8
GROUP_TOK = 2560
TOKENS = 20480
ENC_ROWS = 8192


def draw_bounds(key, part):
    key_cut, key_top = jax.random.split(key)
    largest_cut = PROMPT // (2 * CONT)
    shortfall = jax.random.randint(key_cut, (GROUPS,), 0, largest_cut + 1)
    chosen = jax.random.randint(key_top, (), 0, GROUPS)
    places = jnp.arange(GROUPS)
    shortfall = jnp.where(places == chosen, 0, shortfall)
    shortfall = jnp.where(places == (chosen + 1) % GROUPS, largest_cut, shortfall)
    prompts = PROMPT - CONT * shortfall
    starts = prompts[:, None] + (CLEN + shortfall)[:, None] * jnp.arange(CONT)[None, :]
    return starts.astype(jnp.int32)


def draw_enc_lengths(key, part):
    key_len, key_top = jax.random.split(key)
    drawn = jax.random.randint(key_len, (GROUPS,), ENC // 2, ENC + 1)
    chosen = jax.random.randint(key_top, (), 0, GROUPS)
    places = jnp.arange(GROUPS)
    drawn = jnp.where(places == chosen, ENC, drawn)
    drawn = jnp.where(places == (chosen + 1) % GROUPS, ENC // 2, drawn)
    return drawn.astype(jnp.int32)


def draw_norm_params(key, part):
    key_gain, key_shift = jax.random.split(key)
    gain_rows = jax.random.uniform(key_gain, (3, D), jnp.float32, 0.6, 1.4)
    shift_rows = jax.random.uniform(key_shift, (3, D), jnp.float32, -0.3, 0.3)
    return jnp.stack([gain_rows, shift_rows], axis=1).astype(jnp.float32)


def levels(rng, extent, cuts, least, top_value):
    level, own = 1.0, jax.random.fold_in(rng, 6)
    for dim, shards_of in cuts:
        steps = jnp.exp(jax.random.uniform(jax.random.fold_in(own, dim), (shards_of,), jnp.float32, least / len(cuts), top_value / len(cuts)))
        level = level * jnp.repeat(steps, extent[dim] // shards_of).reshape([-1 if axis == dim else 1 for axis in range(len(extent))])
    return level


def bell_draw(key, shape, deviation, bound, shards=(), kind=jnp.bfloat16):
    values = deviation * jax.random.normal(key, shape, jnp.float32)
    if shards:
        values = values * levels(key, shape, shards, -0.22, 0.18)
    return jnp.clip(values, -bound, bound).astype(kind)


def setup_inputs(seed: int = 0) -> dict:
    seeds = jax.random.split(jax.random.key(seed), 16)
    block_in = bell_draw(seeds[0], (TOKENS, D), 1.0, 6.0, ((0, 32),))
    encoder_out = bell_draw(seeds[1], (ENC_ROWS, D), 1.0, 6.0, ((0, 32),))
    out_grad = bell_draw(seeds[2], (TOKENS, D), 1.0, 6.0, ((0, 32),))
    bounds = draw_bounds(jax.random.fold_in(seeds[15], 71), 0)
    enc_lengths = draw_enc_lengths(jax.random.fold_in(seeds[15], 71), 0)
    norm_params = draw_norm_params(jax.random.fold_in(seeds[15], 71), 0)
    w_qkv = bell_draw(seeds[6], (D, 3, D), D ** -0.5, 0.1875, ((0, 8), (2, 4)))
    w_self_out = bell_draw(seeds[7], (D, D), (D // 4) ** -0.5, 0.375, ((0, 4), (1, 8)))
    w_cross_q = bell_draw(seeds[8], (D, D), D ** -0.5, 0.1875, ((0, 8), (1, 4)))
    w_cross_kv = bell_draw(seeds[9], (D, 2, D), D ** -0.5, 0.1875, ((0, 8), (2, 4)))
    w_cross_out = bell_draw(seeds[10], (D, D), (D // 4) ** -0.5, 0.375, ((0, 4), (1, 8)))
    w_up = bell_draw(seeds[11], (D, FF), D ** -0.5, 0.1875, ((0, 8), (1, 4)))
    w_down = bell_draw(seeds[12], (FF, D), FF ** -0.5, 0.09375, ((0, 4), (1, 8)))
    biases = bell_draw(seeds[13], (7, D), 0.2, 1.0, (), jnp.float32)
    up_bias = bell_draw(seeds[14], (FF,), 0.2, 1.0, (), jnp.float32)
    return dict(block_in=block_in, encoder_out=encoder_out, out_grad=out_grad, bounds=bounds, enc_lengths=enc_lengths, norm_params=norm_params, w_qkv=w_qkv, w_self_out=w_self_out, w_cross_q=w_cross_q, w_cross_kv=w_cross_kv, w_cross_out=w_cross_out, w_up=w_up, w_down=w_down, biases=biases, up_bias=up_bias)


@jax.custom_vjp
def low(v):
    return lax.optimization_barrier(v.astype(jnp.bfloat16)).astype(jnp.float32)

@jax.custom_vjp
def low_back(v):
    return v

def low_keep(v):
    return (low(v), None)

def low_pass(kept, grad):
    return (grad,)

def back_keep(v):
    return (v, None)

def back_low(kept, grad):
    return (low(grad),)
low.defvjp(low_keep, low_pass)
low_back.defvjp(back_keep, back_low)
EPSILON = 1e-05
NEGATIVE = -1e+30
HIGHEST = lax.Precision.HIGHEST

def layer_norm(inputs, gain_row, shift_row):
    center = inputs - lax.optimization_barrier(jnp.mean(inputs, axis=-1, keepdims=True))
    spread = lax.optimization_barrier(jnp.mean(center * center, axis=-1, keepdims=True))
    return center * lax.rsqrt(spread + EPSILON) * gain_row + shift_row

def rounded(values_in):
    return low_back(low(values_in))

def self_rule(bound_row):
    columns = jnp.arange(GROUP_TOK, dtype=jnp.int32)
    prompt_len = bound_row[0]

    def segment(places):
        return lax.optimization_barrier(jnp.sum((places[:, None] >= bound_row[None, :]).astype(jnp.int32), axis=-1))
    column_segment = segment(columns)

    def allowed(row_places):
        causal = columns[None, :] <= row_places[:, None]
        shared = (columns[None, :] < prompt_len) | (column_segment[None, :] == segment(row_places)[:, None])
        return causal & shared
    return allowed

def cross_rule(enc_limit):
    columns = jnp.arange(ENC, dtype=jnp.int32)

    def allowed(row_places):
        return jnp.broadcast_to(columns[None, :] < enc_limit, (row_places.shape[0], ENC))
    return allowed

def attend(queries, key_rows, value_rows, allowed_fn):
    row_count = queries.shape[0]
    block_rows = min(512, row_count)
    block_count = row_count // block_rows
    score_scale = 1.0 / math.sqrt(HD)
    query_blocks = queries.reshape(block_count, block_rows, H, HD)
    key_heads = key_rows.reshape(key_rows.shape[0], H, HD)
    value_heads = value_rows.reshape(value_rows.shape[0], H, HD)
    block_starts = jnp.arange(block_count, dtype=jnp.int32) * block_rows

    def one_block(operands):
        query_block, block_start = operands
        scores = jnp.einsum('qhd,khd->hqk', query_block, key_heads, precision=HIGHEST) * score_scale
        scores = low_back(scores)
        allowed = allowed_fn(block_start + jnp.arange(block_rows, dtype=jnp.int32))
        scores = jnp.where(allowed[None], scores, NEGATIVE)
        weights = low(jax.nn.softmax(scores, axis=-1))
        return jnp.einsum('hqk,khd->qhd', weights, value_heads, precision=HIGHEST)
    outputs = lax.map(jax.checkpoint(one_block), (query_blocks, block_starts))
    return outputs.reshape(row_count, H * HD)

def forward(inputs, encoder, norm_params, w_qkv, w_self_out, w_cross_q, w_cross_kv, w_cross_out, w_up, w_down, biases, up_bias, bound_row, enc_limit):
    normed_one = low(layer_norm(inputs, norm_params[0, 0], norm_params[0, 1]))
    projected = jnp.einsum('nd,dke->nke', normed_one, w_qkv, precision=HIGHEST)
    queries = rounded(projected[:, 0] + biases[0])
    key_rows = rounded(projected[:, 1])
    value_rows = rounded(projected[:, 2] + biases[1])
    self_mixed = rounded(attend(queries, key_rows, value_rows, self_rule(bound_row)))
    after_self = inputs + low_back(jnp.dot(self_mixed, w_self_out, precision=HIGHEST) + biases[2])
    normed_two = low(layer_norm(after_self, norm_params[1, 0], norm_params[1, 1]))
    cross_queries = rounded(jnp.dot(normed_two, w_cross_q, precision=HIGHEST) + biases[3])
    cross_proj = jnp.einsum('nd,dke->nke', encoder, w_cross_kv, precision=HIGHEST)
    cross_keys = rounded(cross_proj[:, 0])
    cross_values = rounded(cross_proj[:, 1] + biases[4])
    cross_mixed = rounded(attend(cross_queries, cross_keys, cross_values, cross_rule(enc_limit)))
    after_cross = after_self + low_back(jnp.dot(cross_mixed, w_cross_out, precision=HIGHEST) + biases[5])
    normed_three = low(layer_norm(after_cross, norm_params[2, 0], norm_params[2, 1]))
    pre_act = low_back(jnp.dot(normed_three, w_up, precision=HIGHEST) + up_bias)
    hidden = low(jax.nn.gelu(pre_act, approximate=False))
    return after_cross + low_back(jnp.dot(hidden, w_down, precision=HIGHEST) + biases[6])

def reference(block_in, encoder_out, out_grad, bounds, enc_lengths, norm_params, w_qkv, w_self_out, w_cross_q, w_cross_kv, w_cross_out, w_up, w_down, biases, up_bias):
    params = (norm_params.astype(jnp.float32), w_qkv.astype(jnp.float32), w_self_out.astype(jnp.float32), w_cross_q.astype(jnp.float32), w_cross_kv.astype(jnp.float32), w_cross_out.astype(jnp.float32), w_up.astype(jnp.float32), w_down.astype(jnp.float32), biases.astype(jnp.float32), up_bias.astype(jnp.float32))
    inputs = block_in.astype(jnp.float32).reshape(GROUPS, GROUP_TOK, D)
    encoders = encoder_out.astype(jnp.float32).reshape(GROUPS, ENC, D)
    cotangent = out_grad.astype(jnp.float32).reshape(GROUPS, GROUP_TOK, D)

    def per_group(totals, operands):
        group_in, group_enc, group_cot, bound_row, enc_limit = operands

        def apply(group_rows, enc_rows, *weight_list):
            return forward(group_rows, enc_rows, *weight_list, bound_row, enc_limit)
        result, pull_back = jax.vjp(apply, group_in, group_enc, *params)
        grads = pull_back(group_cot)
        totals = tuple((accum_old + grad_new for accum_old, grad_new in zip(totals, grads[2:])))
        return (totals, (result, grads[0], grads[1]))
    zeros_init = tuple((jnp.zeros_like(each_param) for each_param in params))
    totals, (out_rows, input_grads, enc_grads) = lax.scan(per_group, zeros_init, (inputs, encoders, cotangent, bounds, enc_lengths))
    means = tuple((each_total / GROUPS for each_total in totals))
    return (out_rows.reshape(TOKENS, D), input_grads.reshape(TOKENS, D), enc_grads.reshape(ENC_ROWS, D), means[0], means[1], means[2], means[3], means[4], means[5], means[6], means[7], means[8], means[9])
```

```python
import functools
import math

import jax
import jax.numpy as jnp
from jax import lax
from jax.experimental import pallas as pl
from jax.experimental.pallas import tpu as pltpu
from jax.sharding import PartitionSpec as P

H = 16
EPSILON = 1e-05
NEGATIVE = -1e30
F32 = jnp.float32
BF16 = jnp.bfloat16
VMEM_LIMIT = 56 * 2**20


def dot_nt(a, b):
    return lax.dot_general(a, b, (((1,), (1,)), ((), ())), preferred_element_type=F32)


def dot_nn(a, b):
    return lax.dot_general(a, b, (((1,), (0,)), ((), ())), preferred_element_type=F32)


def dot_tn(a, b):
    return lax.dot_general(a, b, (((0,), (0,)), ((), ())), preferred_element_type=F32)


def layer_norm(inputs, gain_row, shift_row):
    center = inputs - jnp.mean(inputs, axis=-1, keepdims=True)
    spread = jnp.mean(center * center, axis=-1, keepdims=True)
    return center * lax.rsqrt(spread + EPSILON) * gain_row + shift_row


def gelu_slope(values_in):
    normal_cdf = 0.5 * (1.0 + lax.erf(values_in * (1.0 / math.sqrt(2.0))))
    density = jnp.exp(-0.5 * values_in * values_in) * (1.0 / math.sqrt(2.0 * math.pi))
    return normal_cdf + values_in * density


def head_only(x, h, size):
    lane = lax.broadcasted_iota(jnp.int32, x.shape, 1)
    return jnp.where((lane >= h * size) & (lane < (h + 1) * size), x, jnp.zeros_like(x))


def self_bad(b_ref, q_start, k_start, bq, bk, causal):
    qi = q_start + lax.broadcasted_iota(jnp.int32, (1, bq), 1)
    kj = k_start + lax.broadcasted_iota(jnp.int32, (bk, 1), 0)
    bad = (qi >= b_ref[0, 1]) & ((kj >= b_ref[0, 0]) & (kj < b_ref[0, 1]))
    if causal:
        bad = bad | (kj > qi)
    return bad


def over_keys(i, bq, bk, safe, block):
    first_mixed = jnp.minimum(i * bq // bk, safe // bk)
    diagonal = i * bq // bk

    def plain(j, c):
        block(j, "none")
        return c

    def split(j, c):
        block(j, "segment")
        return c

    lax.fori_loop(0, first_mixed, plain, 0)
    lax.fori_loop(first_mixed, diagonal, split, 0)
    for step in range(bq // bk):
        block(diagonal + step, "causal")


def self_forward_kernel(b_ref, q_ref, k_ref, vt_ref, ot_ref, lse_ref, m_s, l_s, acc, *, bk, heads, safe):
    i = pl.program_id(0)
    bq, width = q_ref.shape
    hd = width // heads
    m_s[...] = jnp.full_like(m_s, NEGATIVE)
    l_s[...] = jnp.zeros_like(l_s)
    acc[...] = jnp.zeros_like(acc)
    scaled = q_ref[...] * jnp.asarray(1.0 / math.sqrt(hd), BF16)
    q_heads = [head_only(scaled, h, hd) for h in range(heads)]

    def block(j, mode):
        rows = pl.ds(pl.multiple_of(j * bk, bk), bk)
        keys = k_ref[rows, :]
        m_old = m_s[...]
        l_old = l_s[...]
        scores = [dot_nt(keys, q_heads[h]) for h in range(heads)]
        if mode != "none":
            bad = self_bad(b_ref, i * bq, j * bk, bq, bk, mode == "causal")
            scores = [jnp.where(bad, NEGATIVE, s) for s in scores]
        m_out, l_out, a_out = [], [], []
        for h in range(heads):
            part = slice(h * hd, (h + 1) * hd)
            m_new = jnp.maximum(m_old[h : h + 1, :], jnp.max(scores[h], axis=0, keepdims=True))
            shrink = jnp.exp(m_old[h : h + 1, :] - m_new)
            expos = jnp.exp(scores[h] - m_new)
            l_out.append(l_old[h : h + 1, :] * shrink + jnp.sum(expos, axis=0, keepdims=True))
            m_out.append(m_new)
            a_out.append(acc[part, :] * shrink + dot_nn(vt_ref[part, rows], expos.astype(BF16)))
        m_s[...] = jnp.concatenate(m_out, 0)
        l_s[...] = jnp.concatenate(l_out, 0)
        for h in range(heads):
            acc[h * hd : (h + 1) * hd, :] = a_out[h]

    over_keys(i, bq, bk, safe, block)
    inverse = 1.0 / l_s[...]
    for h in range(heads):
        part = slice(h * hd, (h + 1) * hd)
        ot_ref[part, :] = (acc[part, :] * inverse[h : h + 1, :]).astype(BF16)
    lse_ref[...] = m_s[...] + jnp.log(l_s[...])


def self_forward(bounds, queries, keys, values_t, heads, safe):
    n, width = queries.shape
    bq = bk = 512
    return pl.pallas_call(
        functools.partial(self_forward_kernel, bk=bk, heads=heads, safe=safe),
        grid=(n // bq,),
        in_specs=[
            pl.BlockSpec(memory_space=pltpu.SMEM),
            pl.BlockSpec((bq, width), lambda i: (i, 0)),
            pl.BlockSpec((n, width), lambda i: (0, 0)),
            pl.BlockSpec((width, n), lambda i: (0, 0)),
        ],
        out_specs=[
            pl.BlockSpec((width, bq), lambda i: (0, i)),
            pl.BlockSpec((heads, bq), lambda i: (0, i)),
        ],
        out_shape=[
            jax.ShapeDtypeStruct((width, n), BF16),
            jax.ShapeDtypeStruct((heads, n), F32),
        ],
        scratch_shapes=[
            pltpu.VMEM((heads, bq), F32),
            pltpu.VMEM((heads, bq), F32),
            pltpu.VMEM((width, bq), F32),
        ],
        compiler_params=pltpu.CompilerParams(vmem_limit_bytes=VMEM_LIMIT),
        cost_estimate=pl.CostEstimate(
            flops=12 * n * n * width, bytes_accessed=8 * n * width, transcendentals=n * n * heads // 2
        ),
        name="self_forward",
    )(bounds, queries, keys, values_t)


def self_backward_kernel(
    b_ref, q_ref, k_ref, v_ref, kt_ref, do_ref, lse_ref, dl_ref, dqt_ref, dk_ref, dv_ref, dka, dva, dqa, *, bk, heads, safe
):
    i = pl.program_id(0)
    bq, width = q_ref.shape
    hd = width // heads
    scale = 1.0 / math.sqrt(hd)

    @pl.when(i == 0)
    def _():
        dka[...] = jnp.zeros_like(dka)
        dva[...] = jnp.zeros_like(dva)

    scaled = q_ref[...] * jnp.asarray(scale, BF16)
    grads = do_ref[...]
    q_heads = [head_only(scaled, h, hd) for h in range(heads)]
    d_heads = [head_only(grads, h, hd) for h in range(heads)]
    lse = lse_ref[...]
    inner = dl_ref[...]
    dqa[...] = jnp.zeros_like(dqa)

    def block(j, mode):
        rows = pl.ds(pl.multiple_of(j * bk, bk), bk)
        keys = k_ref[rows, :]
        values = v_ref[rows, :]
        scores = [dot_nt(keys, q_heads[h]) for h in range(heads)]
        dprobs = [dot_nt(values, d_heads[h]) for h in range(heads)]
        if mode != "none":
            bad = self_bad(b_ref, i * bq, j * bk, bq, bk, mode == "causal")
            scores = [jnp.where(bad, NEGATIVE, s) for s in scores]
        dv_sum, dk_sum = None, None
        for h in range(heads):
            part = slice(h * hd, (h + 1) * hd)
            probs = jnp.exp(scores[h] - lse[h : h + 1, :])
            ds = (probs * (dprobs[h] - inner[h : h + 1, :])).astype(BF16)
            dv_h = dot_nn(probs.astype(BF16), d_heads[h])
            dk_h = dot_nn(ds, q_heads[h])
            dv_sum = dv_h if dv_sum is None else dv_sum + dv_h
            dk_sum = dk_h if dk_sum is None else dk_sum + dk_h
            dqa[part, :] += dot_nn(kt_ref[part, rows], ds)
        dva[rows, :] += dv_sum
        dka[rows, :] += dk_sum

    over_keys(i, bq, bk, safe, block)
    dqt_ref[...] = (dqa[...] * scale).astype(BF16)

    @pl.when(i == pl.num_programs(0) - 1)
    def _():
        dk_ref[...] = dka[...].astype(BF16)
        dv_ref[...] = dva[...].astype(BF16)


def self_backward(bounds, queries, keys, values, keys_t, grads, lse, inner, heads, safe):
    n, width = queries.shape
    bq = bk = 512
    whole = pl.BlockSpec((n, width), lambda i: (0, 0))
    some = pl.BlockSpec((bq, width), lambda i: (i, 0))
    per_row = pl.BlockSpec((heads, bq), lambda i: (0, i))
    return pl.pallas_call(
        functools.partial(self_backward_kernel, bk=bk, heads=heads, safe=safe),
        grid=(n // bq,),
        in_specs=[
            pl.BlockSpec(memory_space=pltpu.SMEM),
            some,
            whole,
            whole,
            pl.BlockSpec((width, n), lambda i: (0, 0)),
            some,
            per_row,
            per_row,
        ],
        out_specs=[pl.BlockSpec((width, bq), lambda i: (0, i)), whole, whole],
        out_shape=[
            jax.ShapeDtypeStruct((width, n), BF16),
            jax.ShapeDtypeStruct((n, width), BF16),
            jax.ShapeDtypeStruct((n, width), BF16),
        ],
        scratch_shapes=[
            pltpu.VMEM((n, width), F32),
            pltpu.VMEM((n, width), F32),
            pltpu.VMEM((width, bq), F32),
        ],
        compiler_params=pltpu.CompilerParams(vmem_limit_bytes=VMEM_LIMIT),
        cost_estimate=pl.CostEstimate(
            flops=24 * n * n * width, bytes_accessed=16 * n * width, transcendentals=n * n * heads // 2
        ),
        name="self_backward",
    )(bounds, queries, keys, values, keys_t, grads, lse, inner)


def cross_forward_kernel(ok_ref, q_ref, k_ref, vt_ref, ot_ref, lse_ref, *, heads):
    rows, width = q_ref.shape[1:]
    hd = width // heads
    scaled = q_ref[0] * jnp.asarray(1.0 / math.sqrt(hd), BF16)
    keys = k_ref[0]
    ok = ok_ref[...] > 0.0
    scores = [dot_nt(keys, head_only(scaled, h, hd)) for h in range(heads)]
    for h in range(heads):
        part = slice(h * hd, (h + 1) * hd)
        s = jnp.where(ok, scores[h], NEGATIVE)
        largest = jnp.max(s, axis=0, keepdims=True)
        expos = jnp.exp(s - largest)
        total = jnp.sum(expos, axis=0, keepdims=True)
        mixed = dot_nn(vt_ref[0, part, :], expos.astype(BF16))
        ot_ref[0, part, :] = (mixed * (1.0 / total)).astype(BF16)
        lse_ref[0, h : h + 1, :] = largest + jnp.log(total)


def cross_forward(ok, queries, keys, values_t, heads):
    parts, rows, width = queries.shape
    n = keys.shape[1]
    return pl.pallas_call(
        functools.partial(cross_forward_kernel, heads=heads),
        grid=(parts,),
        in_specs=[
            pl.BlockSpec((n, 1), lambda i: (0, 0)),
            pl.BlockSpec((1, rows, width), lambda i: (i, 0, 0)),
            pl.BlockSpec((1, n, width), lambda i: (i, 0, 0)),
            pl.BlockSpec((1, width, n), lambda i: (i, 0, 0)),
        ],
        out_specs=[
            pl.BlockSpec((1, width, rows), lambda i: (i, 0, 0)),
            pl.BlockSpec((1, heads, rows), lambda i: (i, 0, 0)),
        ],
        out_shape=[
            jax.ShapeDtypeStruct((parts, width, rows), BF16),
            jax.ShapeDtypeStruct((parts, heads, rows), F32),
        ],
        compiler_params=pltpu.CompilerParams(vmem_limit_bytes=VMEM_LIMIT),
        cost_estimate=pl.CostEstimate(
            flops=24 * parts * rows * n * width,
            bytes_accessed=8 * parts * n * width,
            transcendentals=parts * rows * n * heads,
        ),
        name="cross_forward",
    )(ok, queries, keys, values_t)


def cross_backward_kernel(
    ok_ref, q_ref, k_ref, v_ref, kt_ref, do_ref, lse_ref, dl_ref, dqt_ref, dk_ref, dv_ref, *, heads, bk
):
    rows, width = q_ref.shape[1:]
    n = k_ref.shape[1]
    hd = width // heads
    scale = 1.0 / math.sqrt(hd)
    scaled = q_ref[0] * jnp.asarray(scale, BF16)
    grads = do_ref[0]
    q_heads = [head_only(scaled, h, hd) for h in range(heads)]
    d_heads = [head_only(grads, h, hd) for h in range(heads)]
    lse = lse_ref[0]
    inner = dl_ref[0]
    dq = [None] * heads
    for j in range(n // bk):
        span = slice(j * bk, (j + 1) * bk)
        keys = k_ref[0, span, :]
        values = v_ref[0, span, :]
        ok = ok_ref[span, :] > 0.0
        scores = [dot_nt(keys, q_heads[h]) for h in range(heads)]
        dprobs = [dot_nt(values, d_heads[h]) for h in range(heads)]
        dv_sum, dk_sum = None, None
        for h in range(heads):
            part = slice(h * hd, (h + 1) * hd)
            probs = jnp.exp(jnp.where(ok, scores[h], NEGATIVE) - lse[h : h + 1, :])
            ds = (probs * (dprobs[h] - inner[h : h + 1, :])).astype(BF16)
            dv_h = dot_nn(probs.astype(BF16), d_heads[h])
            dk_h = dot_nn(ds, q_heads[h])
            dv_sum = dv_h if dv_sum is None else dv_sum + dv_h
            dk_sum = dk_h if dk_sum is None else dk_sum + dk_h
            dq_h = dot_nn(kt_ref[0, part, span], ds)
            dq[h] = dq_h if dq[h] is None else dq[h] + dq_h
        dv_ref[0, span, :] = dv_sum.astype(BF16)
        dk_ref[0, span, :] = dk_sum.astype(BF16)
    for h in range(heads):
        dqt_ref[0, h * hd : (h + 1) * hd, :] = (dq[h] * scale).astype(BF16)


def cross_backward(ok, queries, keys, values, keys_t, grads, lse, inner, heads):
    parts, rows, width = queries.shape
    n = keys.shape[1]
    by_row = pl.BlockSpec((1, rows, width), lambda i: (i, 0, 0))
    by_key = pl.BlockSpec((1, n, width), lambda i: (i, 0, 0))
    stat = pl.BlockSpec((1, heads, rows), lambda i: (i, 0, 0))
    return pl.pallas_call(
        functools.partial(cross_backward_kernel, heads=heads, bk=512),
        grid=(parts,),
        in_specs=[
            pl.BlockSpec((n, 1), lambda i: (0, 0)),
            by_row,
            by_key,
            by_key,
            pl.BlockSpec((1, width, n), lambda i: (i, 0, 0)),
            by_row,
            stat,
            stat,
        ],
        out_specs=[pl.BlockSpec((1, width, rows), lambda i: (i, 0, 0)), by_key, by_key],
        out_shape=[
            jax.ShapeDtypeStruct((parts, width, rows), BF16),
            jax.ShapeDtypeStruct((parts, n, width), BF16),
            jax.ShapeDtypeStruct((parts, n, width), BF16),
        ],
        compiler_params=pltpu.CompilerParams(vmem_limit_bytes=VMEM_LIMIT),
        cost_estimate=pl.CostEstimate(
            flops=48 * parts * rows * n * width,
            bytes_accessed=16 * parts * n * width,
            transcendentals=parts * rows * n * heads,
        ),
        name="cross_backward",
    )(ok, queries, keys, values, keys_t, grads, lse, inner)


def swap(value, axis, distance):
    size = lax.axis_size(axis)
    return lax.ppermute(value, axis, [(i, i ^ distance) for i in range(size)])


def dp_distances():
    n = lax.axis_size("dp")
    found = []
    while n > 1:
        n //= 2
        found.append(n)
    return found


def reorder_kernel(order_ref, in_ref, out_ref):
    out_ref[...] = in_ref[0]


def in_order(stack):
    n, rows, columns = stack.shape
    place = jnp.arange(n, dtype=jnp.int32) ^ lax.axis_index("dp")
    order = jnp.zeros_like(place)
    for bit, distance in enumerate(dp_distances()):
        order = order + (place // distance % 2) * 2**bit
    return pl.pallas_call(
        reorder_kernel,
        grid_spec=pltpu.PrefetchScalarGridSpec(
            num_scalar_prefetch=1,
            grid=(n,),
            in_specs=[pl.BlockSpec((1, rows, columns), lambda i, order_ref: (order_ref[i], 0, 0))],
            out_specs=pl.BlockSpec((rows, columns), lambda i, order_ref: (i, 0)),
        ),
        out_shape=jax.ShapeDtypeStruct((n * rows, columns), stack.dtype),
        cost_estimate=pl.CostEstimate(flops=0, bytes_accessed=4 * n * rows * columns, transcendentals=0),
        name="in_order",
    )(order, stack)


def gather_dp(shard):
    stack = shard[None]
    for distance in dp_distances():
        stack = jnp.concatenate([stack, swap(stack, "dp", distance)], 0)
    return in_order(stack)


def gather_all(shard, x_last):
    distances = dp_distances()
    stack = shard[None]
    for distance in distances[:-1]:
        stack = jnp.concatenate([stack, swap(stack, "dp", distance)], 0)
    last = distances[-1]
    if x_last:
        near = in_order(jnp.concatenate([stack, swap(stack, "dp", last)], 0))
        far = swap(near, "tensor", 2)
    else:
        there = swap(stack, "tensor", 2)
        near = in_order(jnp.concatenate([stack, swap(stack, "dp", last)], 0))
        far = in_order(jnp.concatenate([there, swap(there, "dp", last)], 0))
    return [near, swap(near, "tensor", 1), far, swap(far, "tensor", 1)]


def add_low(a, b):
    return (a.astype(F32) + b.astype(F32)).astype(BF16)


def reduce_dp(total, distances):
    n = lax.axis_size("dp")
    me = lax.axis_index("dp")
    rows, columns = total.shape[0] // n, total.shape[1]
    shape = [2] * len(dp_distances()) + [rows, columns]
    axes = list(dp_distances())
    total = total.reshape(shape)
    for step, distance in enumerate(distances):
        axis = axes.index(distance)
        axes.pop(axis)
        mine = me // distance % 2
        keep = lax.dynamic_index_in_dim(total, mine, axis, keepdims=False)
        give = lax.dynamic_index_in_dim(total, 1 - mine, axis, keepdims=False)
        got = swap(give, "dp", distance)
        total = keep.astype(F32) + got.astype(F32)
        if step < len(distances) - 1:
            total = total.astype(BF16)
    return total


def reduce_all(pieces, x_first):
    near = add_low(pieces[0], swap(pieces[1], "tensor", 1))
    far = add_low(pieces[2], swap(pieces[3], "tensor", 1))
    order = dp_distances()[::-1]
    if x_first:
        return reduce_dp(add_low(near, swap(far, "tensor", 2)), order)
    n = lax.axis_size("dp")
    me = lax.axis_index("dp")
    rows, columns = near.shape[0] // n, near.shape[1]
    mine = me % 2

    def halve(total):
        total = total.reshape(n // 2, 2, rows, columns)
        keep = lax.dynamic_index_in_dim(total, mine, 1, keepdims=False)
        give = lax.dynamic_index_in_dim(total, 1 - mine, 1, keepdims=False)
        return add_low(keep, swap(give, "dp", 1))

    near, far = halve(near), halve(far)
    total = add_low(near, swap(far, "tensor", 2))
    axes = dp_distances()[:-1]
    total = total.reshape([2] * len(axes) + [rows, columns])
    for step, distance in enumerate(order[1:]):
        axis = axes.index(distance)
        axes.pop(axis)
        own = me // distance % 2
        keep = lax.dynamic_index_in_dim(total, own, axis, keepdims=False)
        give = lax.dynamic_index_in_dim(total, 1 - own, axis, keepdims=False)
        total = keep.astype(F32) + swap(give, "dp", distance).astype(F32)
        if step < len(order) - 2:
            total = total.astype(BF16)
    return total


def sum_everywhere(value):
    for distance in (1, 2):
        value = value + swap(value, "tensor", distance)
    for distance in dp_distances():
        value = value + swap(value, "dp", distance)
    return value


def widen(rows_low):
    member = lax.axis_index("tensor")
    count, width = rows_low.shape
    other = swap(rows_low, "tensor", 2)
    parts = [rows_low, swap(rows_low, "tensor", 1), other, swap(other, "tensor", 1)]
    out = jnp.zeros((4 * count, width), rows_low.dtype)
    for distance, part in enumerate(parts):
        out = lax.dynamic_update_slice(out, part, ((member ^ distance) * count, 0))
    return out


def narrow(rows_low):
    member = lax.axis_index("tensor")
    count = rows_low.shape[0] // 4
    parts = [
        lax.dynamic_slice_in_dim(rows_low, (member ^ distance) * count, count, 0)
        for distance in range(4)
    ]
    far = add_low(parts[2], swap(parts[3], "tensor", 1))
    got = swap(far, "tensor", 2)
    near = parts[0].astype(F32) + swap(parts[1], "tensor", 1).astype(F32)
    return near + got.astype(F32)


def on_device(
    block_in,
    encoder_out,
    out_grad,
    bounds,
    enc_lengths,
    norm_params,
    w_qkv,
    w_self_out,
    w_cross_q,
    w_cross_kv,
    w_cross_out,
    w_up,
    w_down,
    biases,
    up_bias,
):
    member = lax.axis_index("tensor")
    groups = float(lax.axis_size("dp"))
    width = w_cross_q.shape[1]
    hidden_width = w_up.shape[1]
    heads = H // 4
    own_rows, model_width = block_in.shape
    enc_rows = encoder_out.shape[0]
    w_rows = w_cross_q.shape[0]

    def block_of(vector, size, distance):
        return lax.dynamic_slice_in_dim(vector, (member ^ distance) * size, size)

    def blocks_placed(parts):
        size = parts[0].shape[0]
        out = jnp.zeros((4 * size,), F32)
        for distance, part in enumerate(parts):
            out = lax.dynamic_update_slice_in_dim(out, part, (member ^ distance) * size, 0)
        return out

    def norm_back(rows, incoming, which):
        _, pull_rows = jax.vjp(layer_norm, rows, norm_params[which, 0], norm_params[which, 1])
        return pull_rows(incoming)

    start_rows = block_in.astype(F32)
    first_in = widen(layer_norm(start_rows, norm_params[0, 0], norm_params[0, 1]).astype(BF16))
    self_w = gather_dp(jnp.concatenate([w_qkv.reshape(w_rows, 3 * width), w_self_out.T], axis=1))
    cross_w = gather_all(
        jnp.concatenate([w_cross_q, w_cross_kv.reshape(w_rows, 2 * width), w_cross_out.T], axis=1), False
    )
    up_w = gather_all(w_up, False)
    down_w = gather_all(w_down.T, True)
    w_query = [w[:, :width] for w in cross_w]
    w_keyval = [w[:, width : 3 * width] for w in cross_w]
    w_out = [w[:, 3 * width :] for w in cross_w]

    projected = dot_nn(first_in, self_w[:, : 3 * width])
    queries = (projected[:, :width] + block_of(biases[0], width, 0)).astype(BF16)
    key_rows = projected[:, width : 2 * width].astype(BF16)
    value_rows = (projected[:, 2 * width :] + block_of(biases[1], width, 0)).astype(BF16)
    self_safe = 1024
    self_mixed_t, self_lse = self_forward(bounds, queries, key_rows, value_rows.T, heads, self_safe)
    self_out_w = self_w[:, 3 * width :]
    after_self = (
        start_rows
        + narrow(lax.dot_general(self_mixed_t, self_out_w, (((0,), (1,)), ((), ())), preferred_element_type=F32).astype(BF16))
        + biases[2]
    )

    own_kv = []
    for distance in range(4):
        shift = jnp.concatenate([jnp.zeros((width,), F32), block_of(biases[4], width, distance)])
        own_kv.append((dot_nn(encoder_out, w_keyval[distance]) + shift).astype(BF16))
    own_kv = jnp.stack(own_kv)
    far_kv = swap(own_kv, "tensor", 2)
    kv_from = [own_kv, swap(own_kv, "tensor", 1), far_kv, swap(far_kv, "tensor", 1)]
    cross_kv = jnp.stack(
        [jnp.concatenate([kv_from[d][j ^ d] for d in range(4)], 0) for j in range(4)]
    )
    cross_keys = cross_kv[:, :, :width]
    cross_values = cross_kv[:, :, width:]
    places = jnp.concatenate(
        [(member ^ d) * enc_rows + jnp.arange(enc_rows, dtype=jnp.int32) for d in range(4)]
    )
    ok = (places < enc_lengths[0]).astype(F32)[:, None]

    second_in = layer_norm(after_self, norm_params[1, 0], norm_params[1, 1]).astype(BF16)
    cross_queries = jnp.stack(
        [
            (dot_nn(second_in, w_query[d]) + block_of(biases[3], width, d)).astype(BF16)
            for d in range(4)
        ]
    )
    cross_mixed_t, cross_lse = cross_forward(
        ok, cross_queries, cross_keys, jnp.swapaxes(cross_values, 1, 2), heads
    )
    after_cross = after_self + biases[5]
    for d in range(4):
        after_cross = after_cross + lax.dot_general(
            cross_mixed_t[d], w_out[d], (((0,), (1,)), ((), ())), preferred_element_type=F32
        )

    third_in = layer_norm(after_cross, norm_params[2, 0], norm_params[2, 1]).astype(BF16)
    cot_rows = out_grad.astype(F32)
    bias_down_grad = jnp.sum(cot_rows, axis=0)
    output = after_cross + biases[6]
    third_grad = 0.0
    down_pieces, up_pieces, bias_up_parts = [], [], []
    for d in range(4):
        pre_act = dot_nn(third_in, up_w[d]) + block_of(up_bias, hidden_width, d)
        hidden = jax.nn.gelu(pre_act, approximate=False).astype(BF16)
        output = output + dot_nt(hidden, down_w[d])
        hidden_grad = dot_nn(out_grad, down_w[d])
        pre_grad = (hidden_grad * gelu_slope(pre_act)).astype(BF16)
        down_pieces.append(dot_tn(out_grad, hidden).astype(BF16))
        up_pieces.append(dot_tn(third_in, pre_grad).astype(BF16))
        bias_up_parts.append(jnp.sum(pre_grad.astype(F32), axis=0))
        third_grad = third_grad + dot_nt(pre_grad, up_w[d])
    summed_up = reduce_all(up_pieces, False)
    summed_down = reduce_all(down_pieces, True).T
    rows_three, gain_three, shift_three = norm_back(after_cross, third_grad, 2)
    cross_rows_grad = cot_rows + rows_three

    cross_low = cross_rows_grad.astype(BF16)
    bias_co_grad = jnp.sum(cross_low.astype(F32), axis=0)
    cross_mixed_grad = jnp.stack([dot_nn(cross_low, w_out[d]).astype(BF16) for d in range(4)])
    cross_inner = jnp.sum(
        cross_mixed_t.reshape(4, heads, width // heads, own_rows).astype(F32)
        * jnp.swapaxes(cross_mixed_grad, 1, 2).reshape(4, heads, width // heads, own_rows).astype(F32),
        axis=2,
    )
    cross_dq_t, part_dk, part_dv = cross_backward(
        ok,
        cross_queries,
        cross_keys,
        cross_values,
        jnp.swapaxes(cross_keys, 1, 2),
        cross_mixed_grad,
        cross_lse,
        cross_inner,
        heads,
    )
    second_grad = 0.0
    for d in range(4):
        second_grad = second_grad + lax.dot_general(
            cross_dq_t[d], w_query[d], (((0,), (1,)), ((), ())), preferred_element_type=F32
        )
    rows_two, gain_two, shift_two = norm_back(after_self, second_grad, 1)
    self_rows_grad = cross_rows_grad + rows_two
    self_low = self_rows_grad.astype(BF16)
    bias_so_grad = jnp.sum(self_low.astype(F32), axis=0)
    self_wide = widen(self_low)

    part_kv = jnp.concatenate([part_dk, part_dv], axis=2).reshape(4, 4, enc_rows, 2 * width)

    def for_member(d):
        return jnp.stack([part_kv[j ^ d, d] for j in range(4)])

    far_dkv = add_low(for_member(2), swap(for_member(3), "tensor", 1))
    near_dkv = for_member(0).astype(F32) + swap(for_member(1), "tensor", 1).astype(F32)
    dkv = (near_dkv + swap(far_dkv, "tensor", 2).astype(F32)).astype(BF16)
    encoder_grad = 0.0
    for d in range(4):
        encoder_grad = encoder_grad + dot_nt(dkv[d], w_keyval[d])
    cross_pieces = []
    for d in range(4):
        cross_pieces.append(
            jnp.concatenate(
                [
                    lax.dot_general(
                        second_in, cross_dq_t[d], (((0,), (1,)), ((), ())), preferred_element_type=F32
                    ).astype(BF16),
                    dot_tn(encoder_out, dkv[d]).astype(BF16),
                    lax.dot_general(
                        cross_low, cross_mixed_t[d], (((0,), (1,)), ((), ())), preferred_element_type=F32
                    ).astype(BF16),
                ],
                axis=1,
            )
        )
    summed_cross = reduce_all(cross_pieces, False)
    bias_cq_grad = blocks_placed([jnp.sum(cross_dq_t[d].astype(F32), axis=1) for d in range(4)])
    bias_cv_grad = blocks_placed([jnp.sum(dkv[d, :, width:].astype(F32), axis=0) for d in range(4)])
    bias_up_grad = blocks_placed(bias_up_parts)

    self_mixed_grad = dot_nn(self_wide, self_out_w).astype(BF16)
    self_inner = jnp.sum(
        self_mixed_t.reshape(heads, width // heads, 4 * own_rows).astype(F32)
        * self_mixed_grad.T.reshape(heads, width // heads, 4 * own_rows).astype(F32),
        axis=1,
    )
    self_dq_t, self_dk, self_dv = self_backward(
        bounds, queries, key_rows, value_rows, key_rows.T, self_mixed_grad, self_lse, self_inner, heads, self_safe
    )
    grad_so_t = lax.dot_general(
        self_wide, self_mixed_t, (((0,), (1,)), ((), ())), preferred_element_type=F32
    ).astype(BF16)
    qkv_grad = jnp.concatenate([self_dq_t.T, self_dk, self_dv], axis=1)
    first_terms = dot_nt(qkv_grad, self_w[:, : 3 * width]).astype(BF16)
    first_grad = narrow(first_terms)
    summed_self = reduce_dp(
        jnp.concatenate([dot_tn(first_in, qkv_grad).astype(BF16), grad_so_t], axis=1), dp_distances()[::-1]
    )
    column_sums = jnp.sum(qkv_grad.astype(F32), axis=0)
    rows_one, gain_one, shift_one = norm_back(start_rows, first_grad, 0)
    input_grad = self_rows_grad + rows_one

    def only_own(part):
        out = jnp.zeros((model_width,), F32)
        return lax.dynamic_update_slice_in_dim(out, part, member * width, 0)

    early = sum_everywhere(
        jnp.concatenate(
            [
                gain_two,
                shift_two,
                gain_three,
                shift_three,
                bias_so_grad,
                bias_cq_grad,
                bias_cv_grad,
                bias_co_grad,
                bias_down_grad,
                bias_up_grad,
            ]
        ).reshape(-1, 128)
    ).reshape(-1, model_width)
    late = sum_everywhere(
        jnp.concatenate(
            [gain_one, shift_one, only_own(column_sums[:width]), only_own(column_sums[2 * width :])]
        ).reshape(-1, 128)
    ).reshape(-1, model_width)
    norm_total = jnp.stack([late[0], late[1], early[0], early[1], early[2], early[3]]).reshape(
        norm_params.shape
    )
    bias_total = jnp.stack([late[2], late[3], early[4], early[5], early[6], early[7], early[8]])
    up_total = early[9:].reshape(-1)
    scale = 1.0 / groups
    return (
        output,
        input_grad,
        encoder_grad,
        norm_total * scale,
        summed_self[:, : 3 * width].reshape(w_qkv.shape) * scale,
        summed_self[:, 3 * width :].T * scale,
        summed_cross[:, :width] * scale,
        summed_cross[:, width : 3 * width].reshape(w_cross_kv.shape) * scale,
        summed_cross[:, 3 * width :].T * scale,
        summed_up * scale,
        summed_down * scale,
        bias_total * scale,
        up_total * scale,
    )


def solution(mesh):
    rows = P(("dp", "tensor"), None)
    placed = (
        rows,
        rows,
        rows,
        P("dp", None),
        P("dp"),
        P(),
        P("dp", None, "tensor"),
        P("tensor", "dp"),
        P("dp", "tensor"),
        P("dp", None, "tensor"),
        P("tensor", "dp"),
        P("dp", "tensor"),
        P("tensor", "dp"),
        P(),
        P(),
    )
    return jax.shard_map(
        on_device,
        mesh=mesh,
        in_specs=placed,
        out_specs=(
            rows,
            rows,
            rows,
            P(),
            P("dp", None, "tensor"),
            P("tensor", "dp"),
            P("dp", "tensor"),
            P("dp", None, "tensor"),
            P("tensor", "dp"),
            P("dp", "tensor"),
            P("tensor", "dp"),
            P(),
            P(),
        ),
        check_vma=False,
    )
```

```python
import functools
import math

import jax
import jax.numpy as jnp
from jax import lax
from jax.experimental import pallas as pl
from jax.experimental.pallas import tpu as pltpu
from jax.sharding import PartitionSpec as P

H = 16
EPSILON = 1e-05
NEGATIVE = -1e30
F32 = jnp.float32
BF16 = jnp.bfloat16
VMEM_LIMIT = 56 * 2**20


def dot_nt(a, b):
    return lax.dot_general(a, b, (((1,), (1,)), ((), ())), preferred_element_type=F32)


def dot_nn(a, b):
    return lax.dot_general(a, b, (((1,), (0,)), ((), ())), preferred_element_type=F32)


def dot_tn(a, b):
    return lax.dot_general(a, b, (((0,), (0,)), ((), ())), preferred_element_type=F32)


def layer_norm(inputs, gain_row, shift_row):
    center = inputs - jnp.mean(inputs, axis=-1, keepdims=True)
    spread = jnp.mean(center * center, axis=-1, keepdims=True)
    return center * lax.rsqrt(spread + EPSILON) * gain_row + shift_row


def gelu_slope(values_in):
    normal_cdf = 0.5 * (1.0 + lax.erf(values_in * (1.0 / math.sqrt(2.0))))
    density = jnp.exp(-0.5 * values_in * values_in) * (1.0 / math.sqrt(2.0 * math.pi))
    return normal_cdf + values_in * density


def head_only(x, h, size):
    lane = lax.broadcasted_iota(jnp.int32, x.shape, 1)
    return jnp.where((lane >= h * size) & (lane < (h + 1) * size), x, jnp.zeros_like(x))


def self_bad(b_ref, q_start, k_start, bq, bk, causal):
    qi = q_start + lax.broadcasted_iota(jnp.int32, (1, bq), 1)
    kj = k_start + lax.broadcasted_iota(jnp.int32, (bk, 1), 0)
    bad = (qi >= b_ref[0, 1]) & ((kj >= b_ref[0, 0]) & (kj < b_ref[0, 1]))
    if causal:
        bad = bad | (kj > qi)
    return bad


def over_keys(i, bq, bk, safe, block):
    diagonal = i * (bq // bk)

    def visit(j, c):
        @pl.when(j < safe // bk)
        def _():
            block(j, "none")

        @pl.when(j >= safe // bk)
        def _():
            block(j, "segment")

        return c

    lax.fori_loop(0, diagonal, visit, 0)
    for step in range(bq // bk):
        block(diagonal + step, "causal")


CORE = ("tensor", 1)
X = ("tensor", 2)
Y = ("dp", 1)
ANY = pl.BlockSpec(memory_space=pl.ANY)


class Links:
    def __init__(self, send_sems, recv_sems, local_sems):
        self.dp = lax.axis_index("dp")
        self.tensor = lax.axis_index("tensor")
        self.send_sems, self.recv_sems, self.local_sems = send_sems, recv_sems, local_sems
        self.used = 0
        self.used_local = 0

    def partner(self, way):
        axis, distance = way
        if axis == "tensor":
            return (self.dp, self.tensor ^ distance)
        return (self.dp ^ distance, self.tensor)

    def greet(self, ways):
        barrier = pltpu.get_barrier_semaphore()
        for way in ways:
            pl.semaphore_signal(
                barrier, inc=1, device_id=self.partner(way), device_id_type=pl.DeviceIdType.MESH
            )
        pl.semaphore_wait(barrier, len(ways))

    def copy(self, source, target, way):
        k = self.used
        self.used += 1
        return pltpu.make_async_remote_copy(
            src_ref=source,
            dst_ref=target,
            send_sem=self.send_sems.at[k],
            recv_sem=self.recv_sems.at[k],
            device_id=self.partner(way),
            device_id_type=pl.DeviceIdType.MESH,
        )

    def local(self, source, target):
        k = self.used_local
        self.used_local += 1
        return pltpu.make_async_copy(source, target, self.local_sems.at[k])


def link_scratch(copies, local):
    return [
        pltpu.SemaphoreType.DMA((copies,)),
        pltpu.SemaphoreType.DMA((copies,)),
        pltpu.SemaphoreType.DMA((local,)),
    ]


def z_distances(n):
    found = []
    m = n // 2
    while m > 1:
        m //= 2
        found.append(m)
    return found


def z_ways(n):
    return [("dp", 2 * distance) for distance in z_distances(n)]


def column_stages(links, shard, column, n):
    z = links.dp // 2
    held = [z]
    stages = []
    for distance in z_distances(n):
        stages.append(
            [
                (
                    links.copy(shard if k == 0 else column.at[index], column.at[index], ("dp", 2 * distance)),
                    index ^ distance,
                )
                for k, index in enumerate(held)
            ]
        )
        held = held + [index ^ distance for index in held]
    return stages


class Spread:
    def __init__(self, links, column, whole):
        y = links.dp % 2
        half = column.shape[0] // 2
        low, high = pl.ds(0, half), pl.ds(half, half)
        near, near_core, far, far_core = whole
        self.own = links.local(column, near.at[:, y])
        self.first = [
            links.copy(column, near.at[:, y], Y),
            links.copy(column, far.at[:, y], X),
        ]
        self.core = [links.copy(column, near_core.at[:, y], CORE)]
        self.second = [
            links.copy(near.at[low, 1 - y], far.at[low, 1 - y], X),
            links.copy(far.at[high, y], far.at[high, y], Y),
        ]
        self.core_second = [
            links.copy(near.at[:, 1 - y], near_core.at[:, 1 - y], CORE),
            links.copy(far.at[:, y], far_core.at[:, y], CORE),
        ]
        self.core_third = [links.copy(far.at[:, 1 - y], far_core.at[:, 1 - y], CORE)]

    def start(self):
        self.own.start()
        for copy in self.first + self.core:
            copy.start()

    def middle(self):
        for copy in self.first:
            copy.wait_recv()
        for copy in self.second + self.core_second:
            copy.start()

    def end(self):
        for copy in self.second:
            copy.wait_recv()
        for copy in self.core_third:
            copy.start()
        self.own.wait()
        for copy in self.first + self.second:
            copy.wait_send()
        for copy in self.core + self.core_second + self.core_third:
            copy.wait()


def start_kernel(
    rows_ref, enc_ref, self_ref, cross_ref, rows_out, enc_out, self_out, cross_out, send_sems, recv_sems, local_sems, *, n
):
    links = Links(send_sems, recv_sems, local_sems)
    member, z, y = links.tensor, links.dp // 2, links.dp % 2
    links.greet([CORE, X, Y] + z_ways(n))

    def place(ref, index, size):
        return ref.at[pl.ds(pl.multiple_of(index * size, size), size)]

    groups = [(rows_ref, rows_out, rows_ref.shape[0]), (enc_ref, enc_out, enc_ref.shape[0])]
    local, started, arrived = [], [], []
    for source, target, size in groups:
        local.append(links.local(source, place(target, member, size)))
    local.append(links.local(self_ref, self_out.at[z, y]))
    local.append(links.local(cross_ref, cross_out.at[z]))
    for copy in local:
        copy.start()

    def go(copy):
        copy.start()
        started.append(copy)
        return copy

    def got(copy):
        copy.wait_recv()
        arrived.append(copy)

    along_x = [go(links.copy(source, place(target, member, size), X)) for source, target, size in groups]
    go(links.copy(self_ref, self_out.at[z, y], Y))
    for source, target, size in groups:
        go(links.copy(source, place(target, member, size), CORE))
    self_stages = column_stages(links, self_ref, self_out.at[:, y], n)
    cross_stages = column_stages(links, cross_ref, cross_out, n)
    for self_stage, cross_stage in zip(self_stages, cross_stages):
        for copy, _ in self_stage:
            go(copy)
        for copy, _ in cross_stage:
            go(copy)
        for copy, index in self_stage:
            got(copy)
            go(links.copy(self_out.at[index, y], self_out.at[index, y], Y))
        for copy, _ in cross_stage:
            got(copy)
    for copy, (_, target, size) in zip(along_x, groups):
        got(copy)
        there = place(target, member ^ 2, size)
        go(links.copy(there, there, CORE))
    for copy in local:
        copy.wait()
    for copy in started:
        copy.wait_send()
        if not any(copy is other for other in arrived):
            copy.wait_recv()


def start_gather(rows_low, enc_low, self_shard, cross_shard):
    n = lax.axis_size("dp")
    r, c = self_shard.shape
    copies = 3 * n + 8
    return pl.pallas_call(
        functools.partial(start_kernel, n=n),
        in_specs=[ANY] * 4,
        out_specs=[ANY] * 4,
        out_shape=[
            jax.ShapeDtypeStruct((4 * rows_low.shape[0], rows_low.shape[1]), BF16),
            jax.ShapeDtypeStruct((4 * enc_low.shape[0], enc_low.shape[1]), BF16),
            jax.ShapeDtypeStruct((n // 2, 2, r, c), BF16),
            jax.ShapeDtypeStruct((n // 2,) + cross_shard.shape, BF16),
        ],
        scratch_shapes=link_scratch(copies, 4),
        compiler_params=pltpu.CompilerParams(collective_id=0, has_side_effects=True),
        cost_estimate=pl.CostEstimate(flops=0, bytes_accessed=100 * 2**20, transcendentals=0),
        name="start_gather",
    )(rows_low, enc_low, self_shard, cross_shard)


def self_forward_kernel(
    b_ref, q_ref, k_ref, vt_ref, column_ref, shard_ref,
    ot_ref, lse_ref, w0, w1, w2, w3, next_column,
    m_s, l_s, acc, send_sems, recv_sems, local_sems, *, bk, heads, safe, n
):
    i = pl.program_id(0)
    last = pl.num_programs(0) - 1
    bq, width = q_ref.shape
    links = Links(send_sems, recv_sems, local_sems)
    spread = Spread(links, column_ref, (w0, w1, w2, w3))
    keep = links.local(shard_ref, next_column.at[links.dp // 2])
    stages = column_stages(links, shard_ref, next_column, n)

    @pl.when(i == 0)
    def _():
        links.greet([CORE, X, Y] + z_ways(n))
        spread.start()
        keep.start()
        for copy, _ in stages[0]:
            copy.start()

    @pl.when(i == last)
    def _():
        spread.middle()
        for k in range(1, len(stages)):
            for copy, _ in stages[k - 1]:
                copy.wait_recv()
            for copy, _ in stages[k]:
                copy.start()

    hd = width // heads
    m_s[...] = jnp.full_like(m_s, NEGATIVE)
    l_s[...] = jnp.zeros_like(l_s)
    acc[...] = jnp.zeros_like(acc)
    scaled = q_ref[...] * jnp.asarray(1.0 / math.sqrt(hd), BF16)
    q_heads = [head_only(scaled, h, hd) for h in range(heads)]

    def block(j, mode):
        rows = pl.ds(pl.multiple_of(j * bk, bk), bk)
        keys = k_ref[rows, :]
        m_old = m_s[...]
        l_old = l_s[...]
        scores = [dot_nt(keys, q_heads[h]) for h in range(heads)]
        if mode != "none":
            bad = self_bad(b_ref, i * bq, j * bk, bq, bk, mode == "causal")
            scores = [jnp.where(bad, NEGATIVE, s) for s in scores]
        m_out, l_out, a_out = [], [], []
        for h in range(heads):
            part = slice(h * hd, (h + 1) * hd)
            m_new = jnp.maximum(m_old[h : h + 1, :], jnp.max(scores[h], axis=0, keepdims=True))
            shrink = jnp.exp(m_old[h : h + 1, :] - m_new)
            expos = jnp.exp(scores[h] - m_new)
            l_out.append(l_old[h : h + 1, :] * shrink + jnp.sum(expos, axis=0, keepdims=True))
            m_out.append(m_new)
            a_out.append(acc[part, :] * shrink + dot_nn(vt_ref[part, rows], expos.astype(BF16)))
        m_s[...] = jnp.concatenate(m_out, 0)
        l_s[...] = jnp.concatenate(l_out, 0)
        for h in range(heads):
            acc[h * hd : (h + 1) * hd, :] = a_out[h]

    over_keys(i, bq, bk, safe, block)
    inverse = 1.0 / l_s[...]
    for h in range(heads):
        part = slice(h * hd, (h + 1) * hd)
        ot_ref[part, :] = (acc[part, :] * inverse[h : h + 1, :]).astype(BF16)
    lse_ref[...] = m_s[...] + jnp.log(l_s[...])

    @pl.when(i == last)
    def _():
        spread.end()
        keep.wait()
        for k, stage in enumerate(stages):
            for copy, _ in stage:
                copy.wait_send()
                if k == len(stages) - 1:
                    copy.wait_recv()


def self_forward(bounds, queries, keys, values_t, column, shard, heads, safe):
    n, width = queries.shape
    bq = bk = 512
    dp = lax.axis_size("dp")
    m, r, c = column.shape
    return pl.pallas_call(
        functools.partial(self_forward_kernel, bk=bk, heads=heads, safe=safe, n=dp),
        grid=(n // bq,),
        in_specs=[
            pl.BlockSpec(memory_space=pltpu.SMEM),
            pl.BlockSpec((bq, width), lambda i: (i, 0)),
            pl.BlockSpec((n, width), lambda i: (0, 0)),
            pl.BlockSpec((width, n), lambda i: (0, 0)),
            ANY,
            ANY,
        ],
        out_specs=[
            pl.BlockSpec((width, bq), lambda i: (0, i)),
            pl.BlockSpec((heads, bq), lambda i: (0, i)),
        ]
        + [ANY] * 5,
        out_shape=[
            jax.ShapeDtypeStruct((width, n), BF16),
            jax.ShapeDtypeStruct((heads, n), F32),
        ]
        + [jax.ShapeDtypeStruct((m, 2, r, c), BF16)] * 4
        + [jax.ShapeDtypeStruct((m,) + shard.shape, BF16)],
        scratch_shapes=[
            pltpu.VMEM((heads, bq), F32),
            pltpu.VMEM((heads, bq), F32),
            pltpu.VMEM((width, bq), F32),
        ]
        + link_scratch(8 + m, 2),
        compiler_params=pltpu.CompilerParams(
            vmem_limit_bytes=VMEM_LIMIT, collective_id=1, has_side_effects=True
        ),
        cost_estimate=pl.CostEstimate(
            flops=12 * n * n * width, bytes_accessed=8 * n * width, transcendentals=n * n * heads // 2
        ),
        name="self_forward",
    )(bounds, queries, keys, values_t, column, shard)


def self_backward_kernel(
    b_ref, q_ref, k_ref, v_ref, kt_ref, do_ref, lse_ref, dl_ref, dqt_ref, dk_ref, dv_ref, dka, dva, dqa, *, bk, heads, safe
):
    i = pl.program_id(0)
    bq, width = q_ref.shape
    hd = width // heads
    scale = 1.0 / math.sqrt(hd)

    @pl.when(i == 0)
    def _():
        dka[...] = jnp.zeros_like(dka)
        dva[...] = jnp.zeros_like(dva)

    scaled = q_ref[...] * jnp.asarray(scale, BF16)
    grads = do_ref[...]
    q_heads = [head_only(scaled, h, hd) for h in range(heads)]
    d_heads = [head_only(grads, h, hd) for h in range(heads)]
    lse = lse_ref[...]
    inner = dl_ref[...]
    dqa[...] = jnp.zeros_like(dqa)

    def block(j, mode):
        rows = pl.ds(pl.multiple_of(j * bk, bk), bk)
        keys = k_ref[rows, :]
        values = v_ref[rows, :]
        scores = [dot_nt(keys, q_heads[h]) for h in range(heads)]
        dprobs = [dot_nt(values, d_heads[h]) for h in range(heads)]
        if mode != "none":
            bad = self_bad(b_ref, i * bq, j * bk, bq, bk, mode == "causal")
            scores = [jnp.where(bad, NEGATIVE, s) for s in scores]
        dv_sum, dk_sum = None, None
        for h in range(heads):
            part = slice(h * hd, (h + 1) * hd)
            probs = jnp.exp(scores[h] - lse[h : h + 1, :])
            ds = (probs * (dprobs[h] - inner[h : h + 1, :])).astype(BF16)
            dv_h = dot_nn(probs.astype(BF16), d_heads[h])
            dk_h = dot_nn(ds, q_heads[h])
            dv_sum = dv_h if dv_sum is None else dv_sum + dv_h
            dk_sum = dk_h if dk_sum is None else dk_sum + dk_h
            dqa[part, :] += dot_nn(kt_ref[part, rows], ds)
        dva[rows, :] += dv_sum
        dka[rows, :] += dk_sum

    over_keys(i, bq, bk, safe, block)
    dqt_ref[...] = (dqa[...] * scale).astype(BF16)

    @pl.when(i == pl.num_programs(0) - 1)
    def _():
        dk_ref[...] = dka[...].astype(BF16)
        dv_ref[...] = dva[...].astype(BF16)


def self_backward(bounds, queries, keys, values, keys_t, grads, lse, inner, heads, safe):
    n, width = queries.shape
    bq = bk = 512
    whole = pl.BlockSpec((n, width), lambda i: (0, 0))
    some = pl.BlockSpec((bq, width), lambda i: (i, 0))
    per_row = pl.BlockSpec((heads, bq), lambda i: (0, i))
    return pl.pallas_call(
        functools.partial(self_backward_kernel, bk=bk, heads=heads, safe=safe),
        grid=(n // bq,),
        in_specs=[
            pl.BlockSpec(memory_space=pltpu.SMEM),
            some,
            whole,
            whole,
            pl.BlockSpec((width, n), lambda i: (0, 0)),
            some,
            per_row,
            per_row,
        ],
        out_specs=[pl.BlockSpec((width, bq), lambda i: (0, i)), whole, whole],
        out_shape=[
            jax.ShapeDtypeStruct((width, n), BF16),
            jax.ShapeDtypeStruct((n, width), BF16),
            jax.ShapeDtypeStruct((n, width), BF16),
        ],
        scratch_shapes=[
            pltpu.VMEM((n, width), F32),
            pltpu.VMEM((n, width), F32),
            pltpu.VMEM((width, bq), F32),
        ],
        compiler_params=pltpu.CompilerParams(vmem_limit_bytes=VMEM_LIMIT),
        cost_estimate=pl.CostEstimate(
            flops=24 * n * n * width, bytes_accessed=16 * n * width, transcendentals=n * n * heads // 2
        ),
        name="self_backward",
    )(bounds, queries, keys, values, keys_t, grads, lse, inner)


def cross_forward_kernel(
    ok_ref, q_ref, k_ref, vt_ref, column_ref, ot_ref, lse_ref, w0, w1, w2, w3, send_sems, recv_sems, local_sems, *, heads
):
    i = pl.program_id(0)
    last = pl.num_programs(0) - 1
    spread = Spread(links := Links(send_sems, recv_sems, local_sems), column_ref, (w0, w1, w2, w3))

    @pl.when(i == 0)
    def _():
        links.greet([CORE, X, Y])
        spread.start()

    rows, width = q_ref.shape[1:]
    hd = width // heads
    scaled = q_ref[0] * jnp.asarray(1.0 / math.sqrt(hd), BF16)
    keys = k_ref[0]
    ok = ok_ref[...] > 0.0
    scores = [dot_nt(keys, head_only(scaled, h, hd)) for h in range(heads)]
    for h in range(heads):
        part = slice(h * hd, (h + 1) * hd)
        s = jnp.where(ok, scores[h], NEGATIVE)
        largest = jnp.max(s, axis=0, keepdims=True)
        expos = jnp.exp(s - largest)
        total = jnp.sum(expos, axis=0, keepdims=True)
        mixed = dot_nn(vt_ref[0, part, :], expos.astype(BF16))
        ot_ref[0, part, :] = (mixed * (1.0 / total)).astype(BF16)
        lse_ref[0, h : h + 1, :] = largest + jnp.log(total)

    @pl.when(i == last)
    def _():
        spread.middle()
        spread.end()


def cross_forward(ok, queries, keys, values_t, column, heads):
    parts, rows, width = queries.shape
    m, r, c = column.shape
    n = keys.shape[1]
    return pl.pallas_call(
        functools.partial(cross_forward_kernel, heads=heads),
        grid=(parts,),
        in_specs=[
            pl.BlockSpec((n, 1), lambda i: (0, 0)),
            pl.BlockSpec((1, rows, width), lambda i: (i, 0, 0)),
            pl.BlockSpec((1, n, width), lambda i: (i, 0, 0)),
            pl.BlockSpec((1, width, n), lambda i: (i, 0, 0)),
            ANY,
        ],
        out_specs=[
            pl.BlockSpec((1, width, rows), lambda i: (i, 0, 0)),
            pl.BlockSpec((1, heads, rows), lambda i: (i, 0, 0)),
        ]
        + [ANY] * 4,
        out_shape=[
            jax.ShapeDtypeStruct((parts, width, rows), BF16),
            jax.ShapeDtypeStruct((parts, heads, rows), F32),
        ]
        + [jax.ShapeDtypeStruct((m, 2, r, c), BF16)] * 4,
        scratch_shapes=link_scratch(8, 1),
        compiler_params=pltpu.CompilerParams(
            vmem_limit_bytes=VMEM_LIMIT, collective_id=2, has_side_effects=True
        ),
        cost_estimate=pl.CostEstimate(
            flops=24 * parts * rows * n * width,
            bytes_accessed=8 * parts * n * width,
            transcendentals=parts * rows * n * heads,
        ),
        name="cross_forward",
    )(ok, queries, keys, values_t, column)


def cross_backward_kernel(
    ok_ref, q_ref, k_ref, v_ref, kt_ref, do_ref, lse_ref, dl_ref, dqt_ref, dk_ref, dv_ref, *, heads, bk
):
    rows, width = q_ref.shape[1:]
    n = k_ref.shape[1]
    hd = width // heads
    scale = 1.0 / math.sqrt(hd)
    scaled = q_ref[0] * jnp.asarray(scale, BF16)
    grads = do_ref[0]
    q_heads = [head_only(scaled, h, hd) for h in range(heads)]
    d_heads = [head_only(grads, h, hd) for h in range(heads)]
    lse = lse_ref[0]
    inner = dl_ref[0]
    dq = [None] * heads
    for j in range(n // bk):
        span = slice(j * bk, (j + 1) * bk)
        keys = k_ref[0, span, :]
        values = v_ref[0, span, :]
        ok = ok_ref[span, :] > 0.0
        scores = [dot_nt(keys, q_heads[h]) for h in range(heads)]
        dprobs = [dot_nt(values, d_heads[h]) for h in range(heads)]
        dv_sum, dk_sum = None, None
        for h in range(heads):
            part = slice(h * hd, (h + 1) * hd)
            probs = jnp.exp(jnp.where(ok, scores[h], NEGATIVE) - lse[h : h + 1, :])
            ds = (probs * (dprobs[h] - inner[h : h + 1, :])).astype(BF16)
            dv_h = dot_nn(probs.astype(BF16), d_heads[h])
            dk_h = dot_nn(ds, q_heads[h])
            dv_sum = dv_h if dv_sum is None else dv_sum + dv_h
            dk_sum = dk_h if dk_sum is None else dk_sum + dk_h
            dq_h = dot_nn(kt_ref[0, part, span], ds)
            dq[h] = dq_h if dq[h] is None else dq[h] + dq_h
        dv_ref[0, span, :] = dv_sum.astype(BF16)
        dk_ref[0, span, :] = dk_sum.astype(BF16)
    for h in range(heads):
        dqt_ref[0, h * hd : (h + 1) * hd, :] = (dq[h] * scale).astype(BF16)


def cross_backward(ok, queries, keys, values, keys_t, grads, lse, inner, heads):
    parts, rows, width = queries.shape
    n = keys.shape[1]
    by_row = pl.BlockSpec((1, rows, width), lambda i: (i, 0, 0))
    by_key = pl.BlockSpec((1, n, width), lambda i: (i, 0, 0))
    stat = pl.BlockSpec((1, heads, rows), lambda i: (i, 0, 0))
    return pl.pallas_call(
        functools.partial(cross_backward_kernel, heads=heads, bk=512),
        grid=(parts,),
        in_specs=[
            pl.BlockSpec((n, 1), lambda i: (0, 0)),
            by_row,
            by_key,
            by_key,
            pl.BlockSpec((1, width, n), lambda i: (i, 0, 0)),
            by_row,
            stat,
            stat,
        ],
        out_specs=[pl.BlockSpec((1, width, rows), lambda i: (i, 0, 0)), by_key, by_key],
        out_shape=[
            jax.ShapeDtypeStruct((parts, width, rows), BF16),
            jax.ShapeDtypeStruct((parts, n, width), BF16),
            jax.ShapeDtypeStruct((parts, n, width), BF16),
        ],
        compiler_params=pltpu.CompilerParams(vmem_limit_bytes=VMEM_LIMIT),
        cost_estimate=pl.CostEstimate(
            flops=48 * parts * rows * n * width,
            bytes_accessed=16 * parts * n * width,
            transcendentals=parts * rows * n * heads,
        ),
        name="cross_backward",
    )(ok, queries, keys, values, keys_t, grads, lse, inner)


def swap(value, axis, distance):
    size = lax.axis_size(axis)
    return lax.ppermute(value, axis, [(i, i ^ distance) for i in range(size)])


def dp_distances():
    n = lax.axis_size("dp")
    found = []
    while n > 1:
        n //= 2
        found.append(n)
    return found


def add_low(a, b):
    return (a.astype(F32) + b.astype(F32)).astype(BF16)


def reduce_dp(total, distances):
    n = lax.axis_size("dp")
    me = lax.axis_index("dp")
    rows, columns = total.shape[0] // n, total.shape[1]
    shape = [2] * len(dp_distances()) + [rows, columns]
    axes = list(dp_distances())
    total = total.reshape(shape)
    for step, distance in enumerate(distances):
        axis = axes.index(distance)
        axes.pop(axis)
        mine = me // distance % 2
        keep = lax.dynamic_index_in_dim(total, mine, axis, keepdims=False)
        give = lax.dynamic_index_in_dim(total, 1 - mine, axis, keepdims=False)
        got = swap(give, "dp", distance)
        total = keep.astype(F32) + got.astype(F32)
        if step < len(distances) - 1:
            total = total.astype(BF16)
    return total


def reduce_all(pieces, x_first):
    near = add_low(pieces[0], swap(pieces[1], "tensor", 1))
    far = add_low(pieces[2], swap(pieces[3], "tensor", 1))
    order = dp_distances()[::-1]
    if x_first:
        return reduce_dp(add_low(near, swap(far, "tensor", 2)), order)
    n = lax.axis_size("dp")
    me = lax.axis_index("dp")
    rows, columns = near.shape[0] // n, near.shape[1]
    mine = me % 2

    def halve(total):
        total = total.reshape(n // 2, 2, rows, columns)
        keep = lax.dynamic_index_in_dim(total, mine, 1, keepdims=False)
        give = lax.dynamic_index_in_dim(total, 1 - mine, 1, keepdims=False)
        return add_low(keep, swap(give, "dp", 1))

    near, far = halve(near), halve(far)
    total = add_low(near, swap(far, "tensor", 2))
    axes = dp_distances()[:-1]
    total = total.reshape([2] * len(axes) + [rows, columns])
    for step, distance in enumerate(order[1:]):
        axis = axes.index(distance)
        axes.pop(axis)
        own = me // distance % 2
        keep = lax.dynamic_index_in_dim(total, own, axis, keepdims=False)
        give = lax.dynamic_index_in_dim(total, 1 - own, axis, keepdims=False)
        total = keep.astype(F32) + swap(give, "dp", distance).astype(F32)
        if step < len(order) - 2:
            total = total.astype(BF16)
    return total


def sum_everywhere(value):
    for distance in (1, 2):
        value = value + swap(value, "tensor", distance)
    for distance in dp_distances():
        value = value + swap(value, "dp", distance)
    return value


def widen(rows_low):
    member = lax.axis_index("tensor")
    count, width = rows_low.shape
    other = swap(rows_low, "tensor", 2)
    parts = [rows_low, swap(rows_low, "tensor", 1), other, swap(other, "tensor", 1)]
    out = jnp.zeros((4 * count, width), rows_low.dtype)
    for distance, part in enumerate(parts):
        out = lax.dynamic_update_slice(out, part, ((member ^ distance) * count, 0))
    return out


def narrow(rows_low):
    member = lax.axis_index("tensor")
    count = rows_low.shape[0] // 4
    parts = [
        lax.dynamic_slice_in_dim(rows_low, (member ^ distance) * count, count, 0)
        for distance in range(4)
    ]
    far = add_low(parts[2], swap(parts[3], "tensor", 1))
    got = swap(far, "tensor", 2)
    near = parts[0].astype(F32) + swap(parts[1], "tensor", 1).astype(F32)
    return near + got.astype(F32)


def on_device(
    block_in,
    encoder_out,
    out_grad,
    bounds,
    enc_lengths,
    norm_params,
    w_qkv,
    w_self_out,
    w_cross_q,
    w_cross_kv,
    w_cross_out,
    w_up,
    w_down,
    biases,
    up_bias,
):
    member = lax.axis_index("tensor")
    groups = float(lax.axis_size("dp"))
    width = w_cross_q.shape[1]
    hidden_width = w_up.shape[1]
    heads = H // 4
    own_rows, model_width = block_in.shape
    enc_rows = encoder_out.shape[0]
    w_rows = w_cross_q.shape[0]

    def block_of(vector, size, distance):
        return lax.dynamic_slice_in_dim(vector, (member ^ distance) * size, size)

    def blocks_placed(parts):
        size = parts[0].shape[0]
        out = jnp.zeros((4 * size,), F32)
        for distance, part in enumerate(parts):
            out = lax.dynamic_update_slice_in_dim(out, part, (member ^ distance) * size, 0)
        return out

    def norm_back(rows, incoming, which):
        _, pull_rows = jax.vjp(layer_norm, rows, norm_params[which, 0], norm_params[which, 1])
        return pull_rows(incoming)

    start_rows = block_in.astype(F32)
    first_in, enc_all, self_w, cross_column = start_gather(
        layer_norm(start_rows, norm_params[0, 0], norm_params[0, 1]).astype(BF16),
        encoder_out,
        jnp.concatenate([w_qkv.reshape(w_rows, 3 * width), w_self_out.T], axis=1),
        jnp.concatenate([w_cross_q, w_cross_kv.reshape(w_rows, 2 * width), w_cross_out.T], axis=1),
    )
    self_w = self_w.reshape(model_width, 4 * width)

    projected = dot_nn(first_in, self_w[:, : 3 * width])
    queries = (projected[:, :width] + block_of(biases[0], width, 0)).astype(BF16)
    key_rows = projected[:, width : 2 * width].astype(BF16)
    value_rows = (projected[:, 2 * width :] + block_of(biases[1], width, 0)).astype(BF16)
    self_safe = 1024
    self_mixed_t, self_lse, *cross_w, ffn_column = self_forward(
        bounds,
        queries,
        key_rows,
        value_rows.T,
        cross_column,
        jnp.concatenate([w_up, w_down.T], axis=1),
        heads,
        self_safe,
    )
    cross_w = [w.reshape(model_width, 4 * width) for w in cross_w]
    w_query = [w[:, :width] for w in cross_w]
    w_keyval = [w[:, width : 3 * width] for w in cross_w]
    w_out = [w[:, 3 * width :] for w in cross_w]
    self_out_w = self_w[:, 3 * width :]
    after_self = (
        start_rows
        + narrow(lax.dot_general(self_mixed_t, self_out_w, (((0,), (1,)), ((), ())), preferred_element_type=F32).astype(BF16))
        + biases[2]
    )

    cross_keys, cross_values = [], []
    for d in range(4):
        projected = dot_nn(enc_all, w_keyval[d])
        cross_keys.append(projected[:, :width].astype(BF16))
        cross_values.append((projected[:, width:] + block_of(biases[4], width, d)).astype(BF16))
    cross_keys = jnp.stack(cross_keys)
    cross_values = jnp.stack(cross_values)
    ok = (jnp.arange(4 * enc_rows, dtype=jnp.int32) < enc_lengths[0]).astype(F32)[:, None]

    second_in = layer_norm(after_self, norm_params[1, 0], norm_params[1, 1]).astype(BF16)
    cross_queries = jnp.stack(
        [
            (dot_nn(second_in, w_query[d]) + block_of(biases[3], width, d)).astype(BF16)
            for d in range(4)
        ]
    )
    cross_mixed_t, cross_lse, *ffn_w = cross_forward(
        ok, cross_queries, cross_keys, jnp.swapaxes(cross_values, 1, 2), ffn_column, heads
    )
    ffn_w = [w.reshape(model_width, 2 * hidden_width) for w in ffn_w]
    up_w = [w[:, :hidden_width] for w in ffn_w]
    down_w = [w[:, hidden_width:] for w in ffn_w]
    after_cross = after_self + biases[5]
    for d in range(4):
        after_cross = after_cross + lax.dot_general(
            cross_mixed_t[d], w_out[d], (((0,), (1,)), ((), ())), preferred_element_type=F32
        )

    third_in = layer_norm(after_cross, norm_params[2, 0], norm_params[2, 1]).astype(BF16)
    cot_rows = out_grad.astype(F32)
    bias_down_grad = jnp.sum(cot_rows, axis=0)
    output = after_cross + biases[6]
    third_grad = 0.0
    down_pieces, up_pieces, bias_up_parts = [], [], []
    for d in range(4):
        pre_act = dot_nn(third_in, up_w[d]) + block_of(up_bias, hidden_width, d)
        hidden = jax.nn.gelu(pre_act, approximate=False).astype(BF16)
        output = output + dot_nt(hidden, down_w[d])
        hidden_grad = dot_nn(out_grad, down_w[d])
        pre_grad = (hidden_grad * gelu_slope(pre_act)).astype(BF16)
        down_pieces.append(dot_tn(out_grad, hidden).astype(BF16))
        up_pieces.append(dot_tn(third_in, pre_grad).astype(BF16))
        bias_up_parts.append(jnp.sum(pre_grad.astype(F32), axis=0))
        third_grad = third_grad + dot_nt(pre_grad, up_w[d])
    summed_up = reduce_all(up_pieces, False)
    summed_down = reduce_all(down_pieces, True).T
    rows_three, gain_three, shift_three = norm_back(after_cross, third_grad, 2)
    cross_rows_grad = cot_rows + rows_three

    cross_low = cross_rows_grad.astype(BF16)
    bias_co_grad = jnp.sum(cross_low.astype(F32), axis=0)
    cross_mixed_grad = jnp.stack([dot_nn(cross_low, w_out[d]).astype(BF16) for d in range(4)])
    cross_inner = jnp.sum(
        cross_mixed_t.reshape(4, heads, width // heads, own_rows).astype(F32)
        * jnp.swapaxes(cross_mixed_grad, 1, 2).reshape(4, heads, width // heads, own_rows).astype(F32),
        axis=2,
    )
    cross_dq_t, part_dk, part_dv = cross_backward(
        ok,
        cross_queries,
        cross_keys,
        cross_values,
        jnp.swapaxes(cross_keys, 1, 2),
        cross_mixed_grad,
        cross_lse,
        cross_inner,
        heads,
    )
    second_grad = 0.0
    for d in range(4):
        second_grad = second_grad + lax.dot_general(
            cross_dq_t[d], w_query[d], (((0,), (1,)), ((), ())), preferred_element_type=F32
        )
    rows_two, gain_two, shift_two = norm_back(after_self, second_grad, 1)
    self_rows_grad = cross_rows_grad + rows_two
    self_low = self_rows_grad.astype(BF16)
    bias_so_grad = jnp.sum(self_low.astype(F32), axis=0)
    self_wide = widen(self_low)

    part_kv = jnp.concatenate([part_dk, part_dv], axis=2).reshape(4, 4, enc_rows, 2 * width)

    def for_member(d):
        rows = lax.dynamic_index_in_dim(part_kv, member ^ d, 1, keepdims=False)
        return jnp.stack([rows[j ^ d] for j in range(4)])

    far_dkv = add_low(for_member(2), swap(for_member(3), "tensor", 1))
    near_dkv = for_member(0).astype(F32) + swap(for_member(1), "tensor", 1).astype(F32)
    dkv = (near_dkv + swap(far_dkv, "tensor", 2).astype(F32)).astype(BF16)
    encoder_grad = 0.0
    for d in range(4):
        encoder_grad = encoder_grad + dot_nt(dkv[d], w_keyval[d])
    cross_pieces = []
    for d in range(4):
        cross_pieces.append(
            jnp.concatenate(
                [
                    lax.dot_general(
                        second_in, cross_dq_t[d], (((0,), (1,)), ((), ())), preferred_element_type=F32
                    ).astype(BF16),
                    dot_tn(encoder_out, dkv[d]).astype(BF16),
                    lax.dot_general(
                        cross_low, cross_mixed_t[d], (((0,), (1,)), ((), ())), preferred_element_type=F32
                    ).astype(BF16),
                ],
                axis=1,
            )
        )
    summed_cross = reduce_all(cross_pieces, False)
    bias_cq_grad = blocks_placed([jnp.sum(cross_dq_t[d].astype(F32), axis=1) for d in range(4)])
    bias_cv_grad = blocks_placed([jnp.sum(dkv[d, :, width:].astype(F32), axis=0) for d in range(4)])
    bias_up_grad = blocks_placed(bias_up_parts)

    self_mixed_grad = dot_nn(self_wide, self_out_w).astype(BF16)
    self_inner = jnp.sum(
        self_mixed_t.reshape(heads, width // heads, 4 * own_rows).astype(F32)
        * self_mixed_grad.T.reshape(heads, width // heads, 4 * own_rows).astype(F32),
        axis=1,
    )
    self_dq_t, self_dk, self_dv = self_backward(
        bounds, queries, key_rows, value_rows, key_rows.T, self_mixed_grad, self_lse, self_inner, heads, self_safe
    )
    grad_so_t = lax.dot_general(
        self_wide, self_mixed_t, (((0,), (1,)), ((), ())), preferred_element_type=F32
    ).astype(BF16)
    qkv_grad = jnp.concatenate([self_dq_t.T, self_dk, self_dv], axis=1)
    first_terms = dot_nt(qkv_grad, self_w[:, : 3 * width]).astype(BF16)
    first_grad = narrow(first_terms)
    summed_self = reduce_dp(
        jnp.concatenate([dot_tn(first_in, qkv_grad).astype(BF16), grad_so_t], axis=1), dp_distances()[::-1]
    )
    column_sums = jnp.sum(qkv_grad.astype(F32), axis=0)
    rows_one, gain_one, shift_one = norm_back(start_rows, first_grad, 0)
    input_grad = self_rows_grad + rows_one

    def only_own(part):
        out = jnp.zeros((model_width,), F32)
        return lax.dynamic_update_slice_in_dim(out, part, member * width, 0)

    early = sum_everywhere(
        jnp.concatenate(
            [
                gain_two,
                shift_two,
                gain_three,
                shift_three,
                bias_so_grad,
                bias_cq_grad,
                bias_cv_grad,
                bias_co_grad,
                bias_down_grad,
                bias_up_grad,
            ]
        ).reshape(-1, 128)
    ).reshape(-1, model_width)
    late = sum_everywhere(
        jnp.concatenate(
            [gain_one, shift_one, only_own(column_sums[:width]), only_own(column_sums[2 * width :])]
        ).reshape(-1, 128)
    ).reshape(-1, model_width)
    norm_total = jnp.stack([late[0], late[1], early[0], early[1], early[2], early[3]]).reshape(
        norm_params.shape
    )
    bias_total = jnp.stack([late[2], late[3], early[4], early[5], early[6], early[7], early[8]])
    up_total = early[9:].reshape(-1)
    scale = 1.0 / groups
    return (
        output,
        input_grad,
        encoder_grad,
        norm_total * scale,
        summed_self[:, : 3 * width].reshape(w_qkv.shape) * scale,
        summed_self[:, 3 * width :].T * scale,
        summed_cross[:, :width] * scale,
        summed_cross[:, width : 3 * width].reshape(w_cross_kv.shape) * scale,
        summed_cross[:, 3 * width :].T * scale,
        summed_up * scale,
        summed_down * scale,
        bias_total * scale,
        up_total * scale,
    )


def solution(mesh):
    rows = P(("dp", "tensor"), None)
    placed = (
        rows,
        rows,
        rows,
        P("dp", None),
        P("dp"),
        P(),
        P("dp", None, "tensor"),
        P("tensor", "dp"),
        P("dp", "tensor"),
        P("dp", None, "tensor"),
        P("tensor", "dp"),
        P("dp", "tensor"),
        P("tensor", "dp"),
        P(),
        P(),
    )
    return jax.shard_map(
        on_device,
        mesh=mesh,
        in_specs=placed,
        out_specs=(
            rows,
            rows,
            rows,
            P(),
            P("dp", None, "tensor"),
            P("tensor", "dp"),
            P("dp", "tensor"),
            P("dp", None, "tensor"),
            P("tensor", "dp"),
            P("dp", "tensor"),
            P("tensor", "dp"),
            P(),
            P(),
        ),
        check_vma=False,
    )
```

```python
import functools
import math

import jax
import jax.numpy as jnp
from jax import lax
from jax.experimental import pallas as pl
from jax.experimental.pallas import tpu as pltpu
from jax.sharding import PartitionSpec as P

H = 16
EPSILON = 1e-05
NEGATIVE = -1e30
F32 = jnp.float32
BF16 = jnp.bfloat16
VMEM_LIMIT = 56 * 2**20


def dot_nt(a, b):
    return lax.dot_general(a, b, (((1,), (1,)), ((), ())), preferred_element_type=F32)


def dot_nn(a, b):
    return lax.dot_general(a, b, (((1,), (0,)), ((), ())), preferred_element_type=F32)


def dot_tn(a, b):
    return lax.dot_general(a, b, (((0,), (0,)), ((), ())), preferred_element_type=F32)


def layer_norm(inputs, gain_row, shift_row):
    center = inputs - jnp.mean(inputs, axis=-1, keepdims=True)
    spread = jnp.mean(center * center, axis=-1, keepdims=True)
    return center * lax.rsqrt(spread + EPSILON) * gain_row + shift_row


def gelu_slope(values_in):
    normal_cdf = 0.5 * (1.0 + lax.erf(values_in * (1.0 / math.sqrt(2.0))))
    density = jnp.exp(-0.5 * values_in * values_in) * (1.0 / math.sqrt(2.0 * math.pi))
    return normal_cdf + values_in * density


def head_only(x, h, size):
    lane = lax.broadcasted_iota(jnp.int32, x.shape, 1)
    return jnp.where((lane >= h * size) & (lane < (h + 1) * size), x, jnp.zeros_like(x))


def self_bad(b_ref, q_start, k_start, bq, bk, causal):
    qi = q_start + lax.broadcasted_iota(jnp.int32, (1, bq), 1)
    kj = k_start + lax.broadcasted_iota(jnp.int32, (bk, 1), 0)
    bad = (qi >= b_ref[0, 1]) & ((kj >= b_ref[0, 0]) & (kj < b_ref[0, 1]))
    if causal:
        bad = bad | (kj > qi)
    return bad


def over_keys(i, bq, bk, safe, block):
    diagonal = i * (bq // bk)

    def visit(j, c):
        @pl.when(j < safe // bk)
        def _():
            block(j, "none")

        @pl.when(j >= safe // bk)
        def _():
            block(j, "segment")

        return c

    lax.fori_loop(0, diagonal, visit, 0)
    for step in range(bq // bk):
        block(diagonal + step, "causal")


CORE = ("tensor", 1)
X = ("tensor", 2)
Y = ("dp", 1)
ANY = pl.BlockSpec(memory_space=pl.ANY)


class Links:
    def __init__(self, send_sems, recv_sems, local_sems):
        self.dp = lax.axis_index("dp")
        self.tensor = lax.axis_index("tensor")
        self.send_sems, self.recv_sems, self.local_sems = send_sems, recv_sems, local_sems
        self.used = 0
        self.used_local = 0

    def partner(self, way):
        axis, distance = way
        if axis == "tensor":
            return (self.dp, self.tensor ^ distance)
        return (self.dp ^ distance, self.tensor)

    def greet(self, ways):
        barrier = pltpu.get_barrier_semaphore()
        for way in ways:
            pl.semaphore_signal(
                barrier, inc=1, device_id=self.partner(way), device_id_type=pl.DeviceIdType.MESH
            )
        pl.semaphore_wait(barrier, len(ways))

    def copy(self, source, target, way):
        k = self.used
        self.used += 1
        return pltpu.make_async_remote_copy(
            src_ref=source,
            dst_ref=target,
            send_sem=self.send_sems.at[k],
            recv_sem=self.recv_sems.at[k],
            device_id=self.partner(way),
            device_id_type=pl.DeviceIdType.MESH,
        )

    def local(self, source, target):
        k = self.used_local
        self.used_local += 1
        return pltpu.make_async_copy(source, target, self.local_sems.at[k])


def link_scratch(copies, local):
    return [
        pltpu.SemaphoreType.DMA((copies,)),
        pltpu.SemaphoreType.DMA((copies,)),
        pltpu.SemaphoreType.DMA((local,)),
    ]


def z_distances(n):
    found = []
    m = n // 2
    while m > 1:
        m //= 2
        found.append(m)
    return found


def z_ways(n):
    return [("dp", 2 * distance) for distance in z_distances(n)]


def column_stages(links, shard, column, n):
    z = links.dp // 2
    held = [z]
    stages = []
    for distance in z_distances(n):
        stages.append(
            [
                (
                    links.copy(shard if k == 0 else column.at[index], column.at[index], ("dp", 2 * distance)),
                    index ^ distance,
                )
                for k, index in enumerate(held)
            ]
        )
        held = held + [index ^ distance for index in held]
    return stages


class Spread:
    def __init__(self, links, column, whole):
        y = links.dp % 2
        half = column.shape[0] // 2
        low, high = pl.ds(0, half), pl.ds(half, half)
        near, near_core, far, far_core = (whole.at[k] for k in range(4))
        self.own = links.local(column, near.at[:, y])
        self.first = [
            links.copy(column, near.at[:, y], Y),
            links.copy(column, far.at[:, y], X),
        ]
        self.core = [links.copy(column, near_core.at[:, y], CORE)]
        self.second = [
            links.copy(near.at[low, 1 - y], far.at[low, 1 - y], X),
            links.copy(far.at[high, y], far.at[high, y], Y),
        ]
        self.core_second = [
            links.copy(near.at[:, 1 - y], near_core.at[:, 1 - y], CORE),
            links.copy(far.at[:, y], far_core.at[:, y], CORE),
        ]
        self.core_third = [links.copy(far.at[:, 1 - y], far_core.at[:, 1 - y], CORE)]

    def start(self):
        self.own.start()
        for copy in self.first + self.core:
            copy.start()

    def middle(self):
        for copy in self.first:
            copy.wait_recv()
        for copy in self.second + self.core_second:
            copy.start()

    def end(self):
        for copy in self.second:
            copy.wait_recv()
        for copy in self.core_third:
            copy.start()
        self.own.wait()
        for copy in self.first + self.second:
            copy.wait_send()
        for copy in self.core + self.core_second + self.core_third:
            copy.wait()


def add_to(total_ref, other_ref):
    def one(k, c):
        total_ref[k] = (total_ref[k].astype(F32) + other_ref[k].astype(F32)).astype(BF16)
        return c

    lax.fori_loop(0, total_ref.shape[0], one, 0)


class Gather:
    def __init__(self, links, near, far, buffers, core=None):
        y = links.dp % 2
        self.column, self.over_y, self.over_x, self.got_y, self.got_x, self.sum_y, self.sum_x = buffers[:7]
        m = self.column.shape[0]
        low, high = pl.ds(0, m // 2), pl.ds(m // 2, m // 2)
        self.low, self.high = low, high
        self.loads = [
            links.local(near.at[:, y], self.column),
            links.local(near.at[:, 1 - y], self.over_y),
            links.local(far.at[:, y], self.over_x),
        ]
        self.core = []
        diagonal = far.at[:, 1 - y]
        if core is not None:
            diagonal, near_core, far_core = buffers[7:]
            self.loads.append(links.local(far.at[:, 1 - y], diagonal))
            self.core = [links.copy(core[0], near_core, CORE), links.copy(core[1], far_core, CORE)]
            self.core_sums = [
                (self.column, near_core.at[:, y]),
                (self.over_y, near_core.at[:, 1 - y]),
                (self.over_x, far_core.at[:, y]),
                (diagonal, far_core.at[:, 1 - y]),
            ]
        self.first = [
            links.copy(diagonal.at[low], self.got_y, X),
            links.copy(diagonal.at[high], self.got_x, Y),
        ]
        self.second = [
            links.copy(self.over_x, self.sum_x, X),
            links.copy(self.over_y, self.sum_y, Y),
        ]

    def start(self):
        for copy in self.loads + self.core:
            copy.start()
        if not self.core:
            for copy in self.first:
                copy.start()

    def after_core(self):
        for copy in self.loads:
            copy.wait()
        for copy in self.core:
            copy.wait_recv()
        for total, other in self.core_sums:
            add_to(total, other)
        for copy in self.first:
            copy.start()

    def middle(self):
        if not self.core:
            for copy in self.loads:
                copy.wait()
        for copy in self.first:
            copy.wait_recv()
        add_to(self.over_y.at[self.low], self.got_y)
        add_to(self.over_x.at[self.high], self.got_x)
        for copy in self.second:
            copy.start()

    def end(self):
        for copy in self.second:
            copy.wait_recv()
        add_to(self.column, self.sum_y)
        add_to(self.column, self.sum_x)
        for copy in self.first + self.second + self.core:
            copy.wait_send()


def gather_scratch(m, r, c, core):
    whole = pltpu.VMEM((m, r, c), BF16)
    half = pltpu.VMEM((m // 2, r, c), BF16)
    kept = [whole] * 3 + [half] * 2 + [whole] * 2
    if core:
        kept += [whole] + [pltpu.VMEM((m, 2, r, c), BF16)] * 2
    return kept


class Collect:
    def __init__(self, links, column, slots):
        z = links.dp // 2
        self.column, self.slots, self.z = column, slots, z
        m = column.shape[0]
        distances = z_distances(2 * m)[::-1]
        self.stages = []
        first = 0
        for step, distance in enumerate(distances):
            kept = [0]
            for other in distances[step + 1 :]:
                kept = kept + [k ^ other for k in kept]
            self.stages.append(
                [
                    (links.copy(column.at[z ^ distance ^ k], slots.at[first + i], ("dp", 2 * distance)), first + i, z ^ k)
                    for i, k in enumerate(kept)
                ]
            )
            first += len(kept)

    def start(self, step):
        for copy, _, _ in self.stages[step]:
            copy.start()

    def finish(self, step):
        for copy, slot, index in self.stages[step]:
            copy.wait_recv()
            self.column[index] = (self.column[index].astype(F32) + self.slots[slot].astype(F32)).astype(BF16)

    def drain(self):
        for stage in self.stages:
            for copy, _, _ in stage:
                copy.wait_send()


def start_kernel(
    rows_ref, enc_ref, self_ref, cross_ref, rows_out, enc_out, self_out, cross_out, send_sems, recv_sems, local_sems, *, n
):
    links = Links(send_sems, recv_sems, local_sems)
    member, z, y = links.tensor, links.dp // 2, links.dp % 2
    links.greet([CORE, X, Y] + z_ways(n))

    def place(ref, index, size):
        return ref.at[pl.ds(pl.multiple_of(index * size, size), size)]

    groups = [(rows_ref, rows_out, rows_ref.shape[0]), (enc_ref, enc_out, enc_ref.shape[0])]
    local, started, arrived = [], [], []
    for source, target, size in groups:
        local.append(links.local(source, place(target, member, size)))
    local.append(links.local(self_ref, self_out.at[z, y]))
    local.append(links.local(cross_ref, cross_out.at[z]))
    for copy in local:
        copy.start()

    def go(copy):
        copy.start()
        started.append(copy)
        return copy

    def got(copy):
        copy.wait_recv()
        arrived.append(copy)

    along_x = [go(links.copy(source, place(target, member, size), X)) for source, target, size in groups]
    go(links.copy(self_ref, self_out.at[z, y], Y))
    for source, target, size in groups:
        go(links.copy(source, place(target, member, size), CORE))
    self_stages = column_stages(links, self_ref, self_out.at[:, y], n)
    cross_stages = column_stages(links, cross_ref, cross_out, n)
    for self_stage, cross_stage in zip(self_stages, cross_stages):
        for copy, _ in self_stage:
            go(copy)
        for copy, _ in cross_stage:
            go(copy)
        for copy, index in self_stage:
            got(copy)
            go(links.copy(self_out.at[index, y], self_out.at[index, y], Y))
        for copy, _ in cross_stage:
            got(copy)
    for copy, (_, target, size) in zip(along_x, groups):
        got(copy)
        there = place(target, member ^ 2, size)
        go(links.copy(there, there, CORE))
    for copy in local:
        copy.wait()
    for copy in started:
        copy.wait_send()
        if not any(copy is other for other in arrived):
            copy.wait_recv()


def start_gather(rows_low, enc_low, self_shard, cross_shard):
    n = lax.axis_size("dp")
    r, c = self_shard.shape
    copies = 3 * n + 8
    return pl.pallas_call(
        functools.partial(start_kernel, n=n),
        in_specs=[ANY] * 4,
        out_specs=[ANY] * 4,
        out_shape=[
            jax.ShapeDtypeStruct((4 * rows_low.shape[0], rows_low.shape[1]), BF16),
            jax.ShapeDtypeStruct((4 * enc_low.shape[0], enc_low.shape[1]), BF16),
            jax.ShapeDtypeStruct((n // 2, 2, r, c), BF16),
            jax.ShapeDtypeStruct((n // 2,) + cross_shard.shape, BF16),
        ],
        scratch_shapes=link_scratch(copies, 4),
        compiler_params=pltpu.CompilerParams(collective_id=0, has_side_effects=True),
        cost_estimate=pl.CostEstimate(flops=0, bytes_accessed=100 * 2**20, transcendentals=0),
        name="start_gather",
    )(rows_low, enc_low, self_shard, cross_shard)


def self_forward_kernel(
    b_ref, q_ref, k_ref, vt_ref, column_ref, shard_ref,
    ot_ref, lse_ref, whole, next_column,
    m_s, l_s, acc, send_sems, recv_sems, local_sems, *, bk, heads, safe, n
):
    i = pl.program_id(0)
    last = pl.num_programs(0) - 1
    bq, width = q_ref.shape
    links = Links(send_sems, recv_sems, local_sems)
    spread = Spread(links, column_ref, whole)
    keep = links.local(shard_ref, next_column.at[links.dp // 2])
    stages = column_stages(links, shard_ref, next_column, n)

    @pl.when(i == 0)
    def _():
        links.greet([CORE, X, Y] + z_ways(n))
        spread.start()
        keep.start()
        for copy, _ in stages[0]:
            copy.start()

    @pl.when(i == last)
    def _():
        spread.middle()
        for k in range(1, len(stages)):
            for copy, _ in stages[k - 1]:
                copy.wait_recv()
            for copy, _ in stages[k]:
                copy.start()

    hd = width // heads
    m_s[...] = jnp.full_like(m_s, NEGATIVE)
    l_s[...] = jnp.zeros_like(l_s)
    acc[...] = jnp.zeros_like(acc)
    scaled = q_ref[...] * jnp.asarray(1.0 / math.sqrt(hd), BF16)
    q_heads = [head_only(scaled, h, hd) for h in range(heads)]

    def block(j, mode):
        rows = pl.ds(pl.multiple_of(j * bk, bk), bk)
        keys = k_ref[rows, :]
        m_old = m_s[...]
        l_old = l_s[...]
        scores = [dot_nt(keys, q_heads[h]) for h in range(heads)]
        if mode != "none":
            bad = self_bad(b_ref, i * bq, j * bk, bq, bk, mode == "causal")
            scores = [jnp.where(bad, NEGATIVE, s) for s in scores]
        m_out, l_out, a_out = [], [], []
        for h in range(heads):
            part = slice(h * hd, (h + 1) * hd)
            m_new = jnp.maximum(m_old[h : h + 1, :], jnp.max(scores[h], axis=0, keepdims=True))
            shrink = jnp.exp(m_old[h : h + 1, :] - m_new)
            expos = jnp.exp(scores[h] - m_new)
            l_out.append(l_old[h : h + 1, :] * shrink + jnp.sum(expos, axis=0, keepdims=True))
            m_out.append(m_new)
            a_out.append(acc[part, :] * shrink + dot_nn(vt_ref[part, rows], expos.astype(BF16)))
        m_s[...] = jnp.concatenate(m_out, 0)
        l_s[...] = jnp.concatenate(l_out, 0)
        for h in range(heads):
            acc[h * hd : (h + 1) * hd, :] = a_out[h]

    over_keys(i, bq, bk, safe, block)
    inverse = 1.0 / l_s[...]
    for h in range(heads):
        part = slice(h * hd, (h + 1) * hd)
        ot_ref[part, :] = (acc[part, :] * inverse[h : h + 1, :]).astype(BF16)
    lse_ref[...] = m_s[...] + jnp.log(l_s[...])

    @pl.when(i == last)
    def _():
        spread.end()
        keep.wait()
        for k, stage in enumerate(stages):
            for copy, _ in stage:
                copy.wait_send()
                if k == len(stages) - 1:
                    copy.wait_recv()


def self_forward(bounds, queries, keys, values_t, column, shard, heads, safe):
    n, width = queries.shape
    bq = bk = 512
    dp = lax.axis_size("dp")
    m, r, c = column.shape
    return pl.pallas_call(
        functools.partial(self_forward_kernel, bk=bk, heads=heads, safe=safe, n=dp),
        grid=(n // bq,),
        in_specs=[
            pl.BlockSpec(memory_space=pltpu.SMEM),
            pl.BlockSpec((bq, width), lambda i: (i, 0)),
            pl.BlockSpec((n, width), lambda i: (0, 0)),
            pl.BlockSpec((width, n), lambda i: (0, 0)),
            ANY,
            ANY,
        ],
        out_specs=[
            pl.BlockSpec((width, bq), lambda i: (0, i)),
            pl.BlockSpec((heads, bq), lambda i: (0, i)),
        ]
        + [ANY] * 2,
        out_shape=[
            jax.ShapeDtypeStruct((width, n), BF16),
            jax.ShapeDtypeStruct((heads, n), F32),
        ]
        + [jax.ShapeDtypeStruct((4, m, 2, r, c), BF16)]
        + [jax.ShapeDtypeStruct((m,) + shard.shape, BF16)],
        scratch_shapes=[
            pltpu.VMEM((heads, bq), F32),
            pltpu.VMEM((heads, bq), F32),
            pltpu.VMEM((width, bq), F32),
        ]
        + link_scratch(8 + m, 2),
        compiler_params=pltpu.CompilerParams(
            vmem_limit_bytes=VMEM_LIMIT, collective_id=1, has_side_effects=True
        ),
        cost_estimate=pl.CostEstimate(
            flops=12 * n * n * width, bytes_accessed=8 * n * width, transcendentals=n * n * heads // 2
        ),
        name="self_forward",
    )(bounds, queries, keys, values_t, column, shard)


def self_backward_kernel(
    b_ref, q_ref, k_ref, v_ref, kt_ref, do_ref, lse_ref, dl_ref, up_ref, down_ref, g0, g1, g2, g3,
    dqt_ref, dk_ref, dv_ref, up_out, down_out, cross_out, dka, dva, dqa, *scratch, bk, heads, safe
):
    i = pl.program_id(0)
    links = Links(*scratch[14:])
    columns = scratch[10:12]
    collects = [Collect(links, column, slots) for column, slots in zip(columns, scratch[12:14])]
    loads = [links.local(ref, column) for ref, column in zip((up_ref, down_ref), columns)]
    cross = Gather(links, g0, g2, scratch[:10], (g1, g3))
    leave = links.local(cross.column, cross_out)
    stages = len(collects[0].stages)

    @pl.when(i == 0)
    def _():
        links.greet([CORE, X, Y] + [("dp", 2 * d) for d in z_distances(2 * columns[0].shape[0])])
        cross.start()
        for copy in loads:
            copy.start()
        for copy in loads:
            copy.wait()
        for c in collects:
            c.start(0)

    @pl.when(i == 2)
    def _():
        cross.after_core()

    @pl.when(i == 3)
    def _():
        cross.middle()
        for step in range(stages - 1):
            for c in collects:
                c.finish(step)
            for c in collects:
                c.start(step + 1)

    bq, width = q_ref.shape
    hd = width // heads
    scale = 1.0 / math.sqrt(hd)

    @pl.when(i == 0)
    def _():
        dka[...] = jnp.zeros_like(dka)
        dva[...] = jnp.zeros_like(dva)

    scaled = q_ref[...] * jnp.asarray(scale, BF16)
    grads = do_ref[...]
    q_heads = [head_only(scaled, h, hd) for h in range(heads)]
    d_heads = [head_only(grads, h, hd) for h in range(heads)]
    lse = lse_ref[...]
    inner = dl_ref[...]
    dqa[...] = jnp.zeros_like(dqa)

    def block(j, mode):
        rows = pl.ds(pl.multiple_of(j * bk, bk), bk)
        keys = k_ref[rows, :]
        values = v_ref[rows, :]
        scores = [dot_nt(keys, q_heads[h]) for h in range(heads)]
        dprobs = [dot_nt(values, d_heads[h]) for h in range(heads)]
        if mode != "none":
            bad = self_bad(b_ref, i * bq, j * bk, bq, bk, mode == "causal")
            scores = [jnp.where(bad, NEGATIVE, s) for s in scores]
        dv_sum, dk_sum = None, None
        for h in range(heads):
            part = slice(h * hd, (h + 1) * hd)
            probs = jnp.exp(scores[h] - lse[h : h + 1, :])
            ds = (probs * (dprobs[h] - inner[h : h + 1, :])).astype(BF16)
            dv_h = dot_nn(probs.astype(BF16), d_heads[h])
            dk_h = dot_nn(ds, q_heads[h])
            dv_sum = dv_h if dv_sum is None else dv_sum + dv_h
            dk_sum = dk_h if dk_sum is None else dk_sum + dk_h
            dqa[part, :] += dot_nn(kt_ref[part, rows], ds)
        dva[rows, :] += dv_sum
        dka[rows, :] += dk_sum

    over_keys(i, bq, bk, safe, block)
    dqt_ref[...] = (dqa[...] * scale).astype(BF16)

    @pl.when(i == pl.num_programs(0) - 1)
    def _():
        dk_ref[...] = dka[...].astype(BF16)
        dv_ref[...] = dva[...].astype(BF16)
        cross.end()
        leave.start()
        for c, out in zip(collects, (up_out, down_out)):
            c.finish(stages - 1)
            out[...] = c.column[c.z].astype(F32)
        for c in collects:
            c.drain()
        leave.wait()


def self_backward(
    bounds, queries, keys, values, keys_t, grads, lse, inner, up_column, down_column, cross_pieces, heads, safe
):
    n, width = queries.shape
    m, r, c = up_column.shape
    cross_c = cross_pieces[0].shape[3]
    done = pl.BlockSpec((r, c), lambda i: (0, 0))
    bq = bk = 512
    whole = pl.BlockSpec((n, width), lambda i: (0, 0))
    some = pl.BlockSpec((bq, width), lambda i: (i, 0))
    per_row = pl.BlockSpec((heads, bq), lambda i: (0, i))
    return pl.pallas_call(
        functools.partial(self_backward_kernel, bk=bk, heads=heads, safe=safe),
        grid=(n // bq,),
        in_specs=[
            pl.BlockSpec(memory_space=pltpu.SMEM),
            some,
            whole,
            whole,
            pl.BlockSpec((width, n), lambda i: (0, 0)),
            some,
            per_row,
            per_row,
        ]
        + [ANY] * 6,
        out_specs=[pl.BlockSpec((width, bq), lambda i: (0, i)), whole, whole, done, done, ANY],
        out_shape=[
            jax.ShapeDtypeStruct((width, n), BF16),
            jax.ShapeDtypeStruct((n, width), BF16),
            jax.ShapeDtypeStruct((n, width), BF16),
            jax.ShapeDtypeStruct((r, c), F32),
            jax.ShapeDtypeStruct((r, c), F32),
            jax.ShapeDtypeStruct((m, r, cross_c), BF16),
        ],
        scratch_shapes=[
            pltpu.VMEM((n, width), F32),
            pltpu.VMEM((n, width), F32),
            pltpu.VMEM((width, bq), F32),
        ]
        + gather_scratch(m, r, cross_c, True)
        + [pltpu.VMEM((m, r, c), BF16)] * 2
        + [pltpu.VMEM((m, r, c), BF16)] * 2
        + link_scratch(6 + 2 * m, 7),
        compiler_params=pltpu.CompilerParams(
            vmem_limit_bytes=VMEM_LIMIT, collective_id=5, has_side_effects=True
        ),
        cost_estimate=pl.CostEstimate(
            flops=24 * n * n * width, bytes_accessed=16 * n * width, transcendentals=n * n * heads // 2
        ),
        name="self_backward",
    )(bounds, queries, keys, values, keys_t, grads, lse, inner, up_column, down_column, *cross_pieces)


def cross_forward_kernel(
    ok_ref, q_ref, k_ref, vt_ref, column_ref, ot_ref, lse_ref, whole, send_sems, recv_sems, local_sems, *, heads
):
    i = pl.program_id(0)
    last = pl.num_programs(0) - 1
    links = Links(send_sems, recv_sems, local_sems)
    spread = Spread(links, column_ref, whole)

    @pl.when(i == 0)
    def _():
        links.greet([CORE, X, Y])
        spread.start()

    rows, width = q_ref.shape[1:]
    hd = width // heads
    scaled = q_ref[0] * jnp.asarray(1.0 / math.sqrt(hd), BF16)
    keys = k_ref[0]
    ok = ok_ref[...] > 0.0
    scores = [dot_nt(keys, head_only(scaled, h, hd)) for h in range(heads)]
    for h in range(heads):
        part = slice(h * hd, (h + 1) * hd)
        s = jnp.where(ok, scores[h], NEGATIVE)
        largest = jnp.max(s, axis=0, keepdims=True)
        expos = jnp.exp(s - largest)
        total = jnp.sum(expos, axis=0, keepdims=True)
        mixed = dot_nn(vt_ref[0, part, :], expos.astype(BF16))
        ot_ref[0, part, :] = (mixed * (1.0 / total)).astype(BF16)
        lse_ref[0, h : h + 1, :] = largest + jnp.log(total)

    @pl.when(i == last)
    def _():
        spread.middle()
        spread.end()


def cross_forward(ok, queries, keys, values_t, column, heads):
    parts, rows, width = queries.shape
    m, r, c = column.shape
    n = keys.shape[1]
    return pl.pallas_call(
        functools.partial(cross_forward_kernel, heads=heads),
        grid=(parts,),
        in_specs=[
            pl.BlockSpec((n, 1), lambda i: (0, 0)),
            pl.BlockSpec((1, rows, width), lambda i: (i, 0, 0)),
            pl.BlockSpec((1, n, width), lambda i: (i, 0, 0)),
            pl.BlockSpec((1, width, n), lambda i: (i, 0, 0)),
            ANY,
        ],
        out_specs=[
            pl.BlockSpec((1, width, rows), lambda i: (i, 0, 0)),
            pl.BlockSpec((1, heads, rows), lambda i: (i, 0, 0)),
        ]
        + [ANY],
        out_shape=[
            jax.ShapeDtypeStruct((parts, width, rows), BF16),
            jax.ShapeDtypeStruct((parts, heads, rows), F32),
        ]
        + [jax.ShapeDtypeStruct((4, m, 2, r, c), BF16)],
        scratch_shapes=link_scratch(8, 1),
        compiler_params=pltpu.CompilerParams(
            vmem_limit_bytes=VMEM_LIMIT, collective_id=2, has_side_effects=True
        ),
        cost_estimate=pl.CostEstimate(
            flops=24 * parts * rows * n * width,
            bytes_accessed=8 * parts * n * width,
            transcendentals=parts * rows * n * heads,
        ),
        name="cross_forward",
    )(ok, queries, keys, values_t, column)


def feed_forward_kernel(
    x_ref, xt_ref, dy_ref, dyt_ref, up_ref, down_ref, b_ref,
    out_ref, back_ref, gup_ref, gdown_ref, bias_ref,
    give, got, send_sems, recv_sems, local_sems, *, chunks
):
    s = pl.program_id(0)
    links = Links(send_sems, recv_sems, local_sems)
    turn = s // chunks
    chunk = s % chunks
    pair = turn // 2
    slot = pair * chunks + chunk
    theirs = turn % 2 == 0
    to_core = pltpu.make_async_remote_copy(
        src_ref=give.at[chunk],
        dst_ref=got.at[slot],
        send_sem=send_sems.at[slot],
        recv_sem=recv_sems.at[slot],
        device_id=links.partner(CORE),
        device_id_type=pl.DeviceIdType.MESH,
    )

    @pl.when(s == 0)
    def _():
        links.greet([CORE])
        out_ref[...] = jnp.zeros_like(out_ref)
        back_ref[...] = jnp.zeros_like(back_ref)

    pre_act = dot_nn(x_ref[...], up_ref[0]) + b_ref[0]
    hidden_grad = dot_nn(dy_ref[...], down_ref[0])
    normal_cdf = 0.5 * (1.0 + lax.erf(pre_act * (1.0 / math.sqrt(2.0))))
    density = jnp.exp(-0.5 * pre_act * pre_act) * (1.0 / math.sqrt(2.0 * math.pi))
    hidden = (pre_act * normal_cdf).astype(BF16)
    pre_grad = (hidden_grad * (normal_cdf + pre_act * density)).astype(BF16)
    bias_ref[0] = jnp.sum(pre_grad.astype(F32), axis=0, keepdims=True)

    @pl.when(turn % 2 == 1)
    def _():
        to_core.wait_send()

    give[chunk, 0] = dot_nn(xt_ref[...], pre_grad).astype(BF16)
    give[chunk, 1] = dot_nn(dyt_ref[...], hidden).astype(BF16)
    out_ref[...] += dot_nt(hidden, down_ref[0])
    back_ref[...] += dot_nt(pre_grad, up_ref[0])

    @pl.when(theirs)
    def _():
        to_core.start()

    @pl.when(jnp.logical_not(theirs))
    def _():
        to_core.wait_recv()
        gup_ref[0] = (give[chunk, 0].astype(F32) + got[slot, 0].astype(F32)).astype(BF16)
        gdown_ref[0] = (give[chunk, 1].astype(F32) + got[slot, 1].astype(F32)).astype(BF16)


def feed_forward(x, dy, weights, bias):
    rows, width = x.shape
    hidden = weights.shape[2] // 2
    size = min(512, hidden)
    chunks = hidden // size

    def block(s):
        return (s // chunks) ^ 1

    def placed(s):
        turn = s // chunks
        return (turn // 2, 0, (s % chunks) * (turn % 2))

    rows_spec = pl.BlockSpec((rows, width), lambda s: (0, 0))
    columns_spec = pl.BlockSpec((width, rows), lambda s: (0, 0))
    grad_spec = pl.BlockSpec((1, width, size), placed)
    bias_spec = pl.BlockSpec((1, 1, size), lambda s: (block(s), 0, s % chunks))
    return pl.pallas_call(
        functools.partial(feed_forward_kernel, chunks=chunks),
        grid=(4 * chunks,),
        in_specs=[
            rows_spec,
            columns_spec,
            rows_spec,
            columns_spec,
            pl.BlockSpec((1, width, size), lambda s: (block(s), 0, s % chunks)),
            pl.BlockSpec((1, width, size), lambda s: (block(s), 0, chunks + s % chunks)),
            bias_spec,
        ],
        out_specs=[rows_spec, rows_spec, grad_spec, grad_spec, bias_spec],
        out_shape=[
            jax.ShapeDtypeStruct((rows, width), F32),
            jax.ShapeDtypeStruct((rows, width), F32),
            jax.ShapeDtypeStruct((2, width, hidden), BF16),
            jax.ShapeDtypeStruct((2, width, hidden), BF16),
            jax.ShapeDtypeStruct((4, 1, hidden), F32),
        ],
        scratch_shapes=[
            pltpu.VMEM((chunks, 2, width, size), BF16),
            pltpu.VMEM((2 * chunks, 2, width, size), BF16),
        ]
        + link_scratch(2 * chunks, 1),
        compiler_params=pltpu.CompilerParams(
            vmem_limit_bytes=VMEM_LIMIT, collective_id=3, has_side_effects=True
        ),
        cost_estimate=pl.CostEstimate(
            flops=48 * rows * width * hidden, bytes_accessed=40 * 2**20, transcendentals=8 * rows * hidden
        ),
        name="feed_forward",
    )(x, x.T, dy, dy.T, weights, weights, bias)


def cross_backward_kernel(
    ok_ref, q_ref, k_ref, v_ref, kt_ref, do_ref, lse_ref, dl_ref, up_ref, down_ref,
    dqt_ref, dk_ref, dv_ref, up_out, down_out, *scratch, heads, bk
):
    i = pl.program_id(0)
    links = Links(*scratch[14:])
    sums = [
        Gather(links, ref.at[0], ref.at[1], scratch[7 * k : 7 * k + 7]) for k, ref in enumerate((up_ref, down_ref))
    ]
    leave = [links.local(g.column, out) for g, out in zip(sums, (up_out, down_out))]

    @pl.when(i == 0)
    def _():
        links.greet([X, Y])
        for g in sums:
            g.start()

    @pl.when(i == 2)
    def _():
        for g in sums:
            g.middle()

    rows, width = q_ref.shape[1:]
    n = k_ref.shape[1]
    hd = width // heads
    scale = 1.0 / math.sqrt(hd)
    scaled = q_ref[0] * jnp.asarray(scale, BF16)
    grads = do_ref[0]
    q_heads = [head_only(scaled, h, hd) for h in range(heads)]
    d_heads = [head_only(grads, h, hd) for h in range(heads)]
    lse = lse_ref[0]
    inner = dl_ref[0]
    dq = [None] * heads
    for j in range(n // bk):
        span = slice(j * bk, (j + 1) * bk)
        keys = k_ref[0, span, :]
        values = v_ref[0, span, :]
        ok = ok_ref[span, :] > 0.0
        scores = [dot_nt(keys, q_heads[h]) for h in range(heads)]
        dprobs = [dot_nt(values, d_heads[h]) for h in range(heads)]
        dv_sum, dk_sum = None, None
        for h in range(heads):
            part = slice(h * hd, (h + 1) * hd)
            probs = jnp.exp(jnp.where(ok, scores[h], NEGATIVE) - lse[h : h + 1, :])
            ds = (probs * (dprobs[h] - inner[h : h + 1, :])).astype(BF16)
            dv_h = dot_nn(probs.astype(BF16), d_heads[h])
            dk_h = dot_nn(ds, q_heads[h])
            dv_sum = dv_h if dv_sum is None else dv_sum + dv_h
            dk_sum = dk_h if dk_sum is None else dk_sum + dk_h
            dq_h = dot_nn(kt_ref[0, part, span], ds)
            dq[h] = dq_h if dq[h] is None else dq[h] + dq_h
        dv_ref[0, span, :] = dv_sum.astype(BF16)
        dk_ref[0, span, :] = dk_sum.astype(BF16)
    for h in range(heads):
        dqt_ref[0, h * hd : (h + 1) * hd, :] = (dq[h] * scale).astype(BF16)

    @pl.when(i == pl.num_programs(0) - 1)
    def _():
        for g, copy in zip(sums, leave):
            g.end()
            copy.start()
        for copy in leave:
            copy.wait()


def cross_backward(ok, queries, keys, values, keys_t, grads, lse, inner, up_sum, down_sum, heads):
    parts, rows, width = queries.shape
    _, m, _, r, c = up_sum.shape
    n = keys.shape[1]
    by_row = pl.BlockSpec((1, rows, width), lambda i: (i, 0, 0))
    by_key = pl.BlockSpec((1, n, width), lambda i: (i, 0, 0))
    stat = pl.BlockSpec((1, heads, rows), lambda i: (i, 0, 0))
    return pl.pallas_call(
        functools.partial(cross_backward_kernel, heads=heads, bk=512),
        grid=(parts,),
        in_specs=[
            pl.BlockSpec((n, 1), lambda i: (0, 0)),
            by_row,
            by_key,
            by_key,
            pl.BlockSpec((1, width, n), lambda i: (i, 0, 0)),
            by_row,
            stat,
            stat,
            ANY,
            ANY,
        ],
        out_specs=[pl.BlockSpec((1, width, rows), lambda i: (i, 0, 0)), by_key, by_key, ANY, ANY],
        out_shape=[
            jax.ShapeDtypeStruct((parts, width, rows), BF16),
            jax.ShapeDtypeStruct((parts, n, width), BF16),
            jax.ShapeDtypeStruct((parts, n, width), BF16),
            jax.ShapeDtypeStruct((m, r, c), BF16),
            jax.ShapeDtypeStruct((m, r, c), BF16),
        ],
        scratch_shapes=gather_scratch(m, r, c, False) * 2 + link_scratch(8, 8),
        compiler_params=pltpu.CompilerParams(
            vmem_limit_bytes=VMEM_LIMIT, collective_id=4, has_side_effects=True
        ),
        cost_estimate=pl.CostEstimate(
            flops=48 * parts * rows * n * width,
            bytes_accessed=16 * parts * n * width,
            transcendentals=parts * rows * n * heads,
        ),
        name="cross_backward",
    )(ok, queries, keys, values, keys_t, grads, lse, inner, up_sum, down_sum)


def swap(value, axis, distance):
    size = lax.axis_size(axis)
    return lax.ppermute(value, axis, [(i, i ^ distance) for i in range(size)])


def dp_distances():
    n = lax.axis_size("dp")
    found = []
    while n > 1:
        n //= 2
        found.append(n)
    return found


def add_low(a, b):
    return (a.astype(F32) + b.astype(F32)).astype(BF16)


def reduce_dp(total, distances, axes):
    me = lax.axis_index("dp")
    rows, columns = total.shape[0] // 2 ** len(axes), total.shape[1]
    shape = [2] * len(axes) + [rows, columns]
    axes = list(axes)
    total = total.reshape(shape)
    for step, distance in enumerate(distances):
        axis = axes.index(distance)
        axes.pop(axis)
        mine = me // distance % 2
        keep = lax.dynamic_index_in_dim(total, mine, axis, keepdims=False)
        give = lax.dynamic_index_in_dim(total, 1 - mine, axis, keepdims=False)
        got = swap(give, "dp", distance)
        total = keep.astype(F32) + got.astype(F32)
        if step < len(distances) - 1:
            total = total.astype(BF16)
    return total


def sum_everywhere(value):
    for distance in (1, 2):
        value = value + swap(value, "tensor", distance)
    for distance in dp_distances():
        value = value + swap(value, "dp", distance)
    return value


def widen(rows_low):
    member = lax.axis_index("tensor")
    count, width = rows_low.shape
    other = swap(rows_low, "tensor", 2)
    parts = [rows_low, swap(rows_low, "tensor", 1), other, swap(other, "tensor", 1)]
    out = jnp.zeros((4 * count, width), rows_low.dtype)
    for distance, part in enumerate(parts):
        out = lax.dynamic_update_slice(out, part, ((member ^ distance) * count, 0))
    return out


def narrow(rows_low):
    member = lax.axis_index("tensor")
    count = rows_low.shape[0] // 4
    parts = [
        lax.dynamic_slice_in_dim(rows_low, (member ^ distance) * count, count, 0)
        for distance in range(4)
    ]
    far = add_low(parts[2], swap(parts[3], "tensor", 1))
    got = swap(far, "tensor", 2)
    near = parts[0].astype(F32) + swap(parts[1], "tensor", 1).astype(F32)
    return near + got.astype(F32)


def on_device(
    block_in,
    encoder_out,
    out_grad,
    bounds,
    enc_lengths,
    norm_params,
    w_qkv,
    w_self_out,
    w_cross_q,
    w_cross_kv,
    w_cross_out,
    w_up,
    w_down,
    biases,
    up_bias,
):
    member = lax.axis_index("tensor")
    groups_count = lax.axis_size("dp")
    groups = float(groups_count)
    width = w_cross_q.shape[1]
    hidden_width = w_up.shape[1]
    heads = H // 4
    own_rows, model_width = block_in.shape
    enc_rows = encoder_out.shape[0]
    w_rows = w_cross_q.shape[0]

    def block_of(vector, size, distance):
        return lax.dynamic_slice_in_dim(vector, (member ^ distance) * size, size)

    def blocks_placed(parts):
        size = parts[0].shape[0]
        out = jnp.zeros((4 * size,), F32)
        for distance, part in enumerate(parts):
            out = lax.dynamic_update_slice_in_dim(out, part, (member ^ distance) * size, 0)
        return out

    def norm_back(rows, incoming, which):
        _, pull_rows = jax.vjp(layer_norm, rows, norm_params[which, 0], norm_params[which, 1])
        return pull_rows(incoming)

    start_rows = block_in.astype(F32)
    first_in, enc_all, self_w, cross_column = start_gather(
        layer_norm(start_rows, norm_params[0, 0], norm_params[0, 1]).astype(BF16),
        encoder_out,
        jnp.concatenate([w_qkv.reshape(w_rows, 3 * width), w_self_out.T], axis=1),
        jnp.concatenate([w_cross_q, w_cross_kv.reshape(w_rows, 2 * width), w_cross_out.T], axis=1),
    )
    self_w = self_w.reshape(model_width, 4 * width)

    projected = dot_nn(first_in, self_w[:, : 3 * width])
    queries = (projected[:, :width] + block_of(biases[0], width, 0)).astype(BF16)
    key_rows = projected[:, width : 2 * width].astype(BF16)
    value_rows = (projected[:, 2 * width :] + block_of(biases[1], width, 0)).astype(BF16)
    self_safe = 1024
    self_mixed_t, self_lse, cross_w, ffn_column = self_forward(
        bounds,
        queries,
        key_rows,
        value_rows.T,
        cross_column,
        jnp.concatenate([w_up, w_down.T], axis=1),
        heads,
        self_safe,
    )
    cross_w = cross_w.reshape(4, model_width, 4 * width)
    w_query = [cross_w[d, :, :width] for d in range(4)]
    w_keyval = [cross_w[d, :, width : 3 * width] for d in range(4)]
    w_out = [cross_w[d, :, 3 * width :] for d in range(4)]
    self_out_w = self_w[:, 3 * width :]
    after_self = (
        start_rows
        + narrow(lax.dot_general(self_mixed_t, self_out_w, (((0,), (1,)), ((), ())), preferred_element_type=F32).astype(BF16))
        + biases[2]
    )

    cross_keys, cross_values = [], []
    for d in range(4):
        projected = dot_nn(enc_all, w_keyval[d])
        cross_keys.append(projected[:, :width].astype(BF16))
        cross_values.append((projected[:, width:] + block_of(biases[4], width, d)).astype(BF16))
    cross_keys = jnp.stack(cross_keys)
    cross_values = jnp.stack(cross_values)
    ok = (jnp.arange(4 * enc_rows, dtype=jnp.int32) < enc_lengths[0]).astype(F32)[:, None]

    second_in = layer_norm(after_self, norm_params[1, 0], norm_params[1, 1]).astype(BF16)
    cross_queries = jnp.stack(
        [
            (dot_nn(second_in, w_query[d]) + block_of(biases[3], width, d)).astype(BF16)
            for d in range(4)
        ]
    )
    cross_mixed_t, cross_lse, ffn_w = cross_forward(
        ok, cross_queries, cross_keys, jnp.swapaxes(cross_values, 1, 2), ffn_column, heads
    )
    after_cross = after_self + biases[5]
    for d in range(4):
        after_cross = after_cross + lax.dot_general(
            cross_mixed_t[d], w_out[d], (((0,), (1,)), ((), ())), preferred_element_type=F32
        )

    third_in = layer_norm(after_cross, norm_params[2, 0], norm_params[2, 1]).astype(BF16)
    cot_rows = out_grad.astype(F32)
    bias_down_grad = jnp.sum(cot_rows, axis=0)
    ffn_out, third_grad, up_sum, down_sum, bias_up_parts = feed_forward(
        third_in,
        out_grad,
        ffn_w.reshape(4, model_width, 2 * hidden_width),
        jnp.stack([block_of(up_bias, hidden_width, d) for d in range(4)])[:, None],
    )
    output = after_cross + biases[6] + ffn_out
    rows_three, gain_three, shift_three = norm_back(after_cross, third_grad, 2)
    cross_rows_grad = cot_rows + rows_three

    cross_low = cross_rows_grad.astype(BF16)
    bias_co_grad = jnp.sum(cross_low.astype(F32), axis=0)
    cross_mixed_grad = jnp.stack([dot_nn(cross_low, w_out[d]).astype(BF16) for d in range(4)])
    cross_inner = jnp.sum(
        cross_mixed_t.reshape(4, heads, width // heads, own_rows).astype(F32)
        * jnp.swapaxes(cross_mixed_grad, 1, 2).reshape(4, heads, width // heads, own_rows).astype(F32),
        axis=2,
    )
    by_shard = (2, groups_count // 2, 2, w_rows, hidden_width)
    cross_dq_t, part_dk, part_dv, up_column, down_column = cross_backward(
        ok,
        cross_queries,
        cross_keys,
        cross_values,
        jnp.swapaxes(cross_keys, 1, 2),
        cross_mixed_grad,
        cross_lse,
        cross_inner,
        up_sum.reshape(by_shard),
        down_sum.reshape(by_shard),
        heads,
    )
    second_grad = 0.0
    for d in range(4):
        second_grad = second_grad + lax.dot_general(
            cross_dq_t[d], w_query[d], (((0,), (1,)), ((), ())), preferred_element_type=F32
        )
    rows_two, gain_two, shift_two = norm_back(after_self, second_grad, 1)
    self_rows_grad = cross_rows_grad + rows_two
    self_low = self_rows_grad.astype(BF16)
    bias_so_grad = jnp.sum(self_low.astype(F32), axis=0)
    self_wide = widen(self_low)

    part_kv = jnp.concatenate([part_dk, part_dv], axis=2).reshape(4, 4, enc_rows, 2 * width)

    def for_member(d):
        rows = lax.dynamic_index_in_dim(part_kv, member ^ d, 1, keepdims=False)
        return jnp.stack([rows[j ^ d] for j in range(4)])

    far_dkv = add_low(for_member(2), swap(for_member(3), "tensor", 1))
    near_dkv = for_member(0).astype(F32) + swap(for_member(1), "tensor", 1).astype(F32)
    dkv = (near_dkv + swap(far_dkv, "tensor", 2).astype(F32)).astype(BF16)
    encoder_grad = 0.0
    for d in range(4):
        encoder_grad = encoder_grad + dot_nt(dkv[d], w_keyval[d])
    cross_pieces = []
    for d in range(4):
        cross_pieces.append(
            jnp.concatenate(
                [
                    lax.dot_general(
                        second_in, cross_dq_t[d], (((0,), (1,)), ((), ())), preferred_element_type=F32
                    ).astype(BF16),
                    dot_tn(encoder_out, dkv[d]).astype(BF16),
                    lax.dot_general(
                        cross_low, cross_mixed_t[d], (((0,), (1,)), ((), ())), preferred_element_type=F32
                    ).astype(BF16),
                ],
                axis=1,
            )
        )
    bias_cq_grad = blocks_placed([jnp.sum(cross_dq_t[d].astype(F32), axis=1) for d in range(4)])
    bias_cv_grad = blocks_placed([jnp.sum(dkv[d, :, width:].astype(F32), axis=0) for d in range(4)])
    bias_up_grad = blocks_placed([bias_up_parts[d, 0] for d in range(4)])

    self_mixed_grad = dot_nn(self_wide, self_out_w).astype(BF16)
    self_inner = jnp.sum(
        self_mixed_t.reshape(heads, width // heads, 4 * own_rows).astype(F32)
        * self_mixed_grad.T.reshape(heads, width // heads, 4 * own_rows).astype(F32),
        axis=1,
    )
    self_dq_t, self_dk, self_dv, summed_up, summed_down, cross_column = self_backward(
        bounds,
        queries,
        key_rows,
        value_rows,
        key_rows.T,
        self_mixed_grad,
        self_lse,
        self_inner,
        up_column,
        down_column,
        [piece.reshape(groups_count // 2, 2, w_rows, 4 * width) for piece in cross_pieces],
        heads,
        self_safe,
    )
    summed_cross = reduce_dp(cross_column.reshape(-1, 4 * width), dp_distances()[-2::-1], dp_distances()[:-1])
    grad_so_t = lax.dot_general(
        self_wide, self_mixed_t, (((0,), (1,)), ((), ())), preferred_element_type=F32
    ).astype(BF16)
    qkv_grad = jnp.concatenate([self_dq_t.T, self_dk, self_dv], axis=1)
    first_terms = dot_nt(qkv_grad, self_w[:, : 3 * width]).astype(BF16)
    first_grad = narrow(first_terms)
    summed_self = reduce_dp(
        jnp.concatenate([dot_tn(first_in, qkv_grad).astype(BF16), grad_so_t], axis=1),
        dp_distances()[::-1],
        dp_distances(),
    )
    column_sums = jnp.sum(qkv_grad.astype(F32), axis=0)
    rows_one, gain_one, shift_one = norm_back(start_rows, first_grad, 0)
    input_grad = self_rows_grad + rows_one

    def only_own(part):
        out = jnp.zeros((model_width,), F32)
        return lax.dynamic_update_slice_in_dim(out, part, member * width, 0)

    early = sum_everywhere(
        jnp.concatenate(
            [
                gain_two,
                shift_two,
                gain_three,
                shift_three,
                bias_so_grad,
                bias_cq_grad,
                bias_cv_grad,
                bias_co_grad,
                bias_down_grad,
                bias_up_grad,
            ]
        ).reshape(-1, 128)
    ).reshape(-1, model_width)
    late = sum_everywhere(
        jnp.concatenate(
            [gain_one, shift_one, only_own(column_sums[:width]), only_own(column_sums[2 * width :])]
        ).reshape(-1, 128)
    ).reshape(-1, model_width)
    norm_total = jnp.stack([late[0], late[1], early[0], early[1], early[2], early[3]]).reshape(
        norm_params.shape
    )
    bias_total = jnp.stack([late[2], late[3], early[4], early[5], early[6], early[7], early[8]])
    up_total = early[9:].reshape(-1)
    scale = 1.0 / groups
    return (
        output,
        input_grad,
        encoder_grad,
        norm_total * scale,
        summed_self[:, : 3 * width].reshape(w_qkv.shape) * scale,
        summed_self[:, 3 * width :].T * scale,
        summed_cross[:, :width] * scale,
        summed_cross[:, width : 3 * width].reshape(w_cross_kv.shape) * scale,
        summed_cross[:, 3 * width :].T * scale,
        summed_up * scale,
        summed_down.T * scale,
        bias_total * scale,
        up_total * scale,
    )


def solution(mesh):
    rows = P(("dp", "tensor"), None)
    placed = (
        rows,
        rows,
        rows,
        P("dp", None),
        P("dp"),
        P(),
        P("dp", None, "tensor"),
        P("tensor", "dp"),
        P("dp", "tensor"),
        P("dp", None, "tensor"),
        P("tensor", "dp"),
        P("dp", "tensor"),
        P("tensor", "dp"),
        P(),
        P(),
    )
    return jax.shard_map(
        on_device,
        mesh=mesh,
        in_specs=placed,
        out_specs=(
            rows,
            rows,
            rows,
            P(),
            P("dp", None, "tensor"),
            P("tensor", "dp"),
            P("dp", "tensor"),
            P("dp", None, "tensor"),
            P("tensor", "dp"),
            P("dp", "tensor"),
            P("tensor", "dp"),
            P(),
            P(),
        ),
        check_vma=False,
    )
```

```python
import functools
import math

import jax
import jax.numpy as jnp
from jax import lax
from jax.experimental import pallas as pl
from jax.experimental.pallas import tpu as pltpu
from jax.sharding import PartitionSpec as P

H = 16
EPSILON = 1e-05
NEGATIVE = -1e30
F32 = jnp.float32
BF16 = jnp.bfloat16
VMEM_LIMIT = 56 * 2**20


def dot_nt(a, b):
    return lax.dot_general(a, b, (((1,), (1,)), ((), ())), preferred_element_type=F32)


def dot_nn(a, b):
    return lax.dot_general(a, b, (((1,), (0,)), ((), ())), preferred_element_type=F32)


def dot_tn(a, b):
    return lax.dot_general(a, b, (((0,), (0,)), ((), ())), preferred_element_type=F32)


def layer_norm(inputs, gain_row, shift_row):
    center = inputs - jnp.mean(inputs, axis=-1, keepdims=True)
    spread = jnp.mean(center * center, axis=-1, keepdims=True)
    return center * lax.rsqrt(spread + EPSILON) * gain_row + shift_row


def gelu_slope(values_in):
    normal_cdf = 0.5 * (1.0 + lax.erf(values_in * (1.0 / math.sqrt(2.0))))
    density = jnp.exp(-0.5 * values_in * values_in) * (1.0 / math.sqrt(2.0 * math.pi))
    return normal_cdf + values_in * density


def head_only(x, h, size):
    lane = lax.broadcasted_iota(jnp.int32, x.shape, 1)
    return jnp.where((lane >= h * size) & (lane < (h + 1) * size), x, jnp.zeros_like(x))


def self_bad(b_ref, q_start, k_start, bq, bk, causal):
    qi = q_start + lax.broadcasted_iota(jnp.int32, (1, bq), 1)
    kj = k_start + lax.broadcasted_iota(jnp.int32, (bk, 1), 0)
    bad = (qi >= b_ref[0, 1]) & ((kj >= b_ref[0, 0]) & (kj < b_ref[0, 1]))
    if causal:
        bad = bad | (kj > qi)
    return bad


def over_keys(i, bq, bk, safe, block):
    diagonal = i * (bq // bk)

    def visit(j, c):
        @pl.when(j < safe // bk)
        def _():
            block(j, "none")

        @pl.when(j >= safe // bk)
        def _():
            block(j, "segment")

        return c

    lax.fori_loop(0, diagonal, visit, 0)
    for step in range(bq // bk):
        block(diagonal + step, "causal")


CORE = ("tensor", 1)
X = ("tensor", 2)
Y = ("dp", 1)
ANY = pl.BlockSpec(memory_space=pl.ANY)


class Links:
    def __init__(self, send_sems, recv_sems, local_sems):
        self.dp = lax.axis_index("dp")
        self.tensor = lax.axis_index("tensor")
        self.send_sems, self.recv_sems, self.local_sems = send_sems, recv_sems, local_sems
        self.used = 0
        self.used_local = 0

    def partner(self, way):
        axis, distance = way
        if axis == "tensor":
            return (self.dp, self.tensor ^ distance)
        return (self.dp ^ distance, self.tensor)

    def greet(self, ways):
        barrier = pltpu.get_barrier_semaphore()
        for way in ways:
            pl.semaphore_signal(
                barrier, inc=1, device_id=self.partner(way), device_id_type=pl.DeviceIdType.MESH
            )
        pl.semaphore_wait(barrier, len(ways))

    def copy(self, source, target, way):
        k = self.used
        self.used += 1
        return pltpu.make_async_remote_copy(
            src_ref=source,
            dst_ref=target,
            send_sem=self.send_sems.at[k],
            recv_sem=self.recv_sems.at[k],
            device_id=self.partner(way),
            device_id_type=pl.DeviceIdType.MESH,
        )

    def local(self, source, target):
        k = self.used_local
        self.used_local += 1
        return pltpu.make_async_copy(source, target, self.local_sems.at[k])


def link_scratch(copies, local):
    return [
        pltpu.SemaphoreType.DMA((copies,)),
        pltpu.SemaphoreType.DMA((copies,)),
        pltpu.SemaphoreType.DMA((local,)),
    ]


def z_distances(n):
    found = []
    m = n // 2
    while m > 1:
        m //= 2
        found.append(m)
    return found


def z_ways(n):
    return [("dp", 2 * distance) for distance in z_distances(n)]


def column_stages(links, shard, column, n):
    z = links.dp // 2
    held = [z]
    stages = []
    for distance in z_distances(n):
        stages.append(
            [
                (
                    links.copy(shard if k == 0 else column.at[index], column.at[index], ("dp", 2 * distance)),
                    index ^ distance,
                )
                for k, index in enumerate(held)
            ]
        )
        held = held + [index ^ distance for index in held]
    return stages


class Spread:
    def __init__(self, links, column, whole):
        y = links.dp % 2
        half = column.shape[0] // 2
        low, high = pl.ds(0, half), pl.ds(half, half)
        near, near_core, far, far_core = (whole.at[k] for k in range(4))
        self.own = links.local(column, near.at[:, y])
        self.first = [
            links.copy(column, near.at[:, y], Y),
            links.copy(column, far.at[:, y], X),
        ]
        self.core = [links.copy(column, near_core.at[:, y], CORE)]
        self.second = [
            links.copy(near.at[low, 1 - y], far.at[low, 1 - y], X),
            links.copy(far.at[high, y], far.at[high, y], Y),
        ]
        self.core_second = [
            links.copy(near.at[:, 1 - y], near_core.at[:, 1 - y], CORE),
            links.copy(far.at[:, y], far_core.at[:, y], CORE),
        ]
        self.core_third = [links.copy(far.at[:, 1 - y], far_core.at[:, 1 - y], CORE)]

    def start(self):
        self.own.start()
        for copy in self.first + self.core:
            copy.start()

    def middle(self):
        for copy in self.first:
            copy.wait_recv()
        for copy in self.second + self.core_second:
            copy.start()

    def end(self):
        for copy in self.second:
            copy.wait_recv()
        for copy in self.core_third:
            copy.start()
        self.own.wait()
        for copy in self.first + self.second:
            copy.wait_send()
        for copy in self.core + self.core_second + self.core_third:
            copy.wait()


def add_to(total_ref, other_ref):
    def one(k, c):
        total_ref[k] = (total_ref[k].astype(F32) + other_ref[k].astype(F32)).astype(BF16)
        return c

    lax.fori_loop(0, total_ref.shape[0], one, 0)


class Gather:
    def __init__(self, links, near, far, buffers):
        y = links.dp % 2
        self.column, self.over_y, self.over_x, self.got_y, self.got_x, self.sum_y, self.sum_x = buffers
        m = self.column.shape[0]
        low, high = pl.ds(0, m // 2), pl.ds(m // 2, m // 2)
        self.low, self.high = low, high
        self.loads = [
            links.local(near.at[:, y], self.column),
            links.local(near.at[:, 1 - y], self.over_y),
            links.local(far.at[:, y], self.over_x),
        ]
        diagonal = far.at[:, 1 - y]
        self.first = [
            links.copy(diagonal.at[low], self.got_y, X),
            links.copy(diagonal.at[high], self.got_x, Y),
        ]
        self.second = [
            links.copy(self.over_x, self.sum_x, X),
            links.copy(self.over_y, self.sum_y, Y),
        ]

    def start(self):
        for copy in self.loads + self.first:
            copy.start()

    def middle(self):
        for copy in self.loads:
            copy.wait()
        for copy in self.first:
            copy.wait_recv()
        add_to(self.over_y.at[self.low], self.got_y)
        add_to(self.over_x.at[self.high], self.got_x)
        for copy in self.second:
            copy.start()

    def end(self):
        for copy in self.second:
            copy.wait_recv()
        add_to(self.column, self.sum_y)
        add_to(self.column, self.sum_x)
        for copy in self.first + self.second:
            copy.wait_send()


def gather_scratch(m, r, c):
    whole = pltpu.VMEM((m, r, c), BF16)
    half = pltpu.VMEM((m // 2, r, c), BF16)
    return [whole] * 3 + [half] * 2 + [whole] * 2


class Collect:
    def __init__(self, links, column, slots):
        z = links.dp // 2
        self.column, self.slots, self.z = column, slots, z
        m = column.shape[0]
        distances = z_distances(2 * m)[::-1]
        self.stages = []
        first = 0
        for step, distance in enumerate(distances):
            kept = [0]
            for other in distances[step + 1 :]:
                kept = kept + [k ^ other for k in kept]
            self.stages.append(
                [
                    (links.copy(column.at[z ^ distance ^ k], slots.at[first + i], ("dp", 2 * distance)), first + i, z ^ k)
                    for i, k in enumerate(kept)
                ]
            )
            first += len(kept)

    def start(self, step):
        for copy, _, _ in self.stages[step]:
            copy.start()

    def finish(self, step):
        for copy, slot, index in self.stages[step]:
            copy.wait_recv()
            self.column[index] = (self.column[index].astype(F32) + self.slots[slot].astype(F32)).astype(BF16)

    def drain(self):
        for stage in self.stages:
            for copy, _, _ in stage:
                copy.wait_send()


def start_kernel(
    rows_ref, enc_ref, self_ref, cross_ref, rows_out, enc_out, self_out, cross_out, send_sems, recv_sems, local_sems, *, n
):
    links = Links(send_sems, recv_sems, local_sems)
    member, z, y = links.tensor, links.dp // 2, links.dp % 2
    links.greet([CORE, X, Y] + z_ways(n))

    def place(ref, index, size):
        return ref.at[pl.ds(pl.multiple_of(index * size, size), size)]

    groups = [(rows_ref, rows_out, rows_ref.shape[0]), (enc_ref, enc_out, enc_ref.shape[0])]
    local, started, arrived = [], [], []
    for source, target, size in groups:
        local.append(links.local(source, place(target, member, size)))
    local.append(links.local(self_ref, self_out.at[z, y]))
    local.append(links.local(cross_ref, cross_out.at[z]))
    for copy in local:
        copy.start()

    def go(copy):
        copy.start()
        started.append(copy)
        return copy

    def got(copy):
        copy.wait_recv()
        arrived.append(copy)

    along_x = [go(links.copy(source, place(target, member, size), X)) for source, target, size in groups]
    go(links.copy(self_ref, self_out.at[z, y], Y))
    for source, target, size in groups:
        go(links.copy(source, place(target, member, size), CORE))
    self_stages = column_stages(links, self_ref, self_out.at[:, y], n)
    cross_stages = column_stages(links, cross_ref, cross_out, n)
    for self_stage, cross_stage in zip(self_stages, cross_stages):
        for copy, _ in self_stage:
            go(copy)
        for copy, _ in cross_stage:
            go(copy)
        for copy, index in self_stage:
            got(copy)
            go(links.copy(self_out.at[index, y], self_out.at[index, y], Y))
        for copy, _ in cross_stage:
            got(copy)
    for copy, (_, target, size) in zip(along_x, groups):
        got(copy)
        there = place(target, member ^ 2, size)
        go(links.copy(there, there, CORE))
    for copy in local:
        copy.wait()
    for copy in started:
        copy.wait_send()
        if not any(copy is other for other in arrived):
            copy.wait_recv()


def start_gather(rows_low, enc_low, self_shard, cross_shard):
    n = lax.axis_size("dp")
    r, c = self_shard.shape
    copies = 3 * n + 8
    return pl.pallas_call(
        functools.partial(start_kernel, n=n),
        in_specs=[ANY] * 4,
        out_specs=[ANY] * 4,
        out_shape=[
            jax.ShapeDtypeStruct((4 * rows_low.shape[0], rows_low.shape[1]), BF16),
            jax.ShapeDtypeStruct((4 * enc_low.shape[0], enc_low.shape[1]), BF16),
            jax.ShapeDtypeStruct((n // 2, 2, r, c), BF16),
            jax.ShapeDtypeStruct((n // 2,) + cross_shard.shape, BF16),
        ],
        scratch_shapes=link_scratch(copies, 4),
        compiler_params=pltpu.CompilerParams(collective_id=0, has_side_effects=True),
        cost_estimate=pl.CostEstimate(flops=0, bytes_accessed=100 * 2**20, transcendentals=0),
        name="start_gather",
    )(rows_low, enc_low, self_shard, cross_shard)


def self_forward_kernel(
    b_ref, q_ref, k_ref, vt_ref, column_ref, shard_ref,
    ot_ref, lse_ref, whole, next_column,
    m_s, l_s, acc, send_sems, recv_sems, local_sems, *, bk, heads, safe, n
):
    i = pl.program_id(0)
    last = pl.num_programs(0) - 1
    bq, width = q_ref.shape
    links = Links(send_sems, recv_sems, local_sems)
    spread = Spread(links, column_ref, whole)
    keep = links.local(shard_ref, next_column.at[links.dp // 2])
    stages = column_stages(links, shard_ref, next_column, n)

    @pl.when(i == 0)
    def _():
        links.greet([CORE, X, Y] + z_ways(n))
        spread.start()
        keep.start()
        for copy, _ in stages[0]:
            copy.start()

    @pl.when(i == last)
    def _():
        spread.middle()
        for k in range(1, len(stages)):
            for copy, _ in stages[k - 1]:
                copy.wait_recv()
            for copy, _ in stages[k]:
                copy.start()

    hd = width // heads
    m_s[...] = jnp.full_like(m_s, NEGATIVE)
    l_s[...] = jnp.zeros_like(l_s)
    acc[...] = jnp.zeros_like(acc)
    scaled = q_ref[...] * jnp.asarray(1.0 / math.sqrt(hd), BF16)
    q_heads = [head_only(scaled, h, hd) for h in range(heads)]

    def block(j, mode):
        rows = pl.ds(pl.multiple_of(j * bk, bk), bk)
        keys = k_ref[rows, :]
        m_old = m_s[...]
        l_old = l_s[...]
        scores = [dot_nt(keys, q_heads[h]) for h in range(heads)]
        if mode != "none":
            bad = self_bad(b_ref, i * bq, j * bk, bq, bk, mode == "causal")
            scores = [jnp.where(bad, NEGATIVE, s) for s in scores]
        m_out, l_out, a_out = [], [], []
        for h in range(heads):
            part = slice(h * hd, (h + 1) * hd)
            m_new = jnp.maximum(m_old[h : h + 1, :], jnp.max(scores[h], axis=0, keepdims=True))
            shrink = jnp.exp(m_old[h : h + 1, :] - m_new)
            expos = jnp.exp(scores[h] - m_new)
            l_out.append(l_old[h : h + 1, :] * shrink + jnp.sum(expos, axis=0, keepdims=True))
            m_out.append(m_new)
            a_out.append(acc[part, :] * shrink + dot_nn(vt_ref[part, rows], expos.astype(BF16)))
        m_s[...] = jnp.concatenate(m_out, 0)
        l_s[...] = jnp.concatenate(l_out, 0)
        for h in range(heads):
            acc[h * hd : (h + 1) * hd, :] = a_out[h]

    over_keys(i, bq, bk, safe, block)
    inverse = 1.0 / l_s[...]
    for h in range(heads):
        part = slice(h * hd, (h + 1) * hd)
        ot_ref[part, :] = (acc[part, :] * inverse[h : h + 1, :]).astype(BF16)
    lse_ref[...] = m_s[...] + jnp.log(l_s[...])

    @pl.when(i == last)
    def _():
        spread.end()
        keep.wait()
        for k, stage in enumerate(stages):
            for copy, _ in stage:
                copy.wait_send()
                if k == len(stages) - 1:
                    copy.wait_recv()


def self_forward(bounds, queries, keys, values_t, column, shard, heads, safe):
    n, width = queries.shape
    bq = bk = 512
    dp = lax.axis_size("dp")
    m, r, c = column.shape
    return pl.pallas_call(
        functools.partial(self_forward_kernel, bk=bk, heads=heads, safe=safe, n=dp),
        grid=(n // bq,),
        in_specs=[
            pl.BlockSpec(memory_space=pltpu.SMEM),
            pl.BlockSpec((bq, width), lambda i: (i, 0)),
            pl.BlockSpec((n, width), lambda i: (0, 0)),
            pl.BlockSpec((width, n), lambda i: (0, 0)),
            ANY,
            ANY,
        ],
        out_specs=[
            pl.BlockSpec((width, bq), lambda i: (0, i)),
            pl.BlockSpec((heads, bq), lambda i: (0, i)),
        ]
        + [ANY] * 2,
        out_shape=[
            jax.ShapeDtypeStruct((width, n), BF16),
            jax.ShapeDtypeStruct((heads, n), F32),
        ]
        + [jax.ShapeDtypeStruct((4, m, 2, r, c), BF16)]
        + [jax.ShapeDtypeStruct((m,) + shard.shape, BF16)],
        scratch_shapes=[
            pltpu.VMEM((heads, bq), F32),
            pltpu.VMEM((heads, bq), F32),
            pltpu.VMEM((width, bq), F32),
        ]
        + link_scratch(8 + m, 2),
        compiler_params=pltpu.CompilerParams(
            vmem_limit_bytes=VMEM_LIMIT, collective_id=1, has_side_effects=True
        ),
        cost_estimate=pl.CostEstimate(
            flops=12 * n * n * width, bytes_accessed=8 * n * width, transcendentals=n * n * heads // 2
        ),
        name="self_forward",
    )(bounds, queries, keys, values_t, column, shard)


def self_backward_kernel(
    b_ref, q_ref, k_ref, v_ref, kt_ref, do_ref, lse_ref, dl_ref, up_ref, down_ref, cross_ref,
    dqt_ref, dk_ref, dv_ref, up_out, down_out, cross_out, dka, dva, dqa, *scratch, bk, heads, safe
):
    i = pl.program_id(0)
    links = Links(*scratch[11:])
    columns = scratch[7:9]
    collects = [Collect(links, column, slots) for column, slots in zip(columns, scratch[9:11])]
    loads = [links.local(ref, column) for ref, column in zip((up_ref, down_ref), columns)]
    cross = Gather(links, cross_ref.at[0], cross_ref.at[1], scratch[:7])
    leave = links.local(cross.column, cross_out)
    stages = len(collects[0].stages)

    @pl.when(i == 0)
    def _():
        links.greet([X, Y] + z_ways(2 * columns[0].shape[0]))
        cross.start()
        for copy in loads:
            copy.start()
        for copy in loads:
            copy.wait()
        for c in collects:
            c.start(0)

    @pl.when(i == 3)
    def _():
        cross.middle()
        for step in range(stages - 1):
            for c in collects:
                c.finish(step)
            for c in collects:
                c.start(step + 1)

    bq, width = q_ref.shape
    hd = width // heads
    scale = 1.0 / math.sqrt(hd)

    @pl.when(i == 0)
    def _():
        dka[...] = jnp.zeros_like(dka)
        dva[...] = jnp.zeros_like(dva)

    scaled = q_ref[...] * jnp.asarray(scale, BF16)
    grads = do_ref[...]
    q_heads = [head_only(scaled, h, hd) for h in range(heads)]
    d_heads = [head_only(grads, h, hd) for h in range(heads)]
    lse = lse_ref[...]
    inner = dl_ref[...]
    dqa[...] = jnp.zeros_like(dqa)

    def block(j, mode):
        rows = pl.ds(pl.multiple_of(j * bk, bk), bk)
        keys = k_ref[rows, :]
        values = v_ref[rows, :]
        scores = [dot_nt(keys, q_heads[h]) for h in range(heads)]
        dprobs = [dot_nt(values, d_heads[h]) for h in range(heads)]
        if mode != "none":
            bad = self_bad(b_ref, i * bq, j * bk, bq, bk, mode == "causal")
            scores = [jnp.where(bad, NEGATIVE, s) for s in scores]
        dv_sum, dk_sum = None, None
        for h in range(heads):
            part = slice(h * hd, (h + 1) * hd)
            probs = jnp.exp(scores[h] - lse[h : h + 1, :])
            ds = (probs * (dprobs[h] - inner[h : h + 1, :])).astype(BF16)
            dv_h = dot_nn(probs.astype(BF16), d_heads[h])
            dk_h = dot_nn(ds, q_heads[h])
            dv_sum = dv_h if dv_sum is None else dv_sum + dv_h
            dk_sum = dk_h if dk_sum is None else dk_sum + dk_h
            dqa[part, :] += dot_nn(kt_ref[part, rows], ds)
        dva[rows, :] += dv_sum
        dka[rows, :] += dk_sum

    over_keys(i, bq, bk, safe, block)
    dqt_ref[...] = (dqa[...] * scale).astype(BF16)

    @pl.when(i == pl.num_programs(0) - 1)
    def _():
        dk_ref[...] = dka[...].astype(BF16)
        dv_ref[...] = dva[...].astype(BF16)
        cross.end()
        leave.start()
        for c, out in zip(collects, (up_out, down_out)):
            c.finish(stages - 1)
            out[...] = c.column[c.z].astype(F32)
        for c in collects:
            c.drain()
        leave.wait()


def self_backward(
    bounds, queries, keys, values, keys_t, grads, lse, inner, up_column, down_column, cross_sum, heads, safe
):
    n, width = queries.shape
    m, r, c = up_column.shape
    cross_c = cross_sum.shape[4]
    done = pl.BlockSpec((r, c), lambda i: (0, 0))
    bq = bk = 512
    whole = pl.BlockSpec((n, width), lambda i: (0, 0))
    some = pl.BlockSpec((bq, width), lambda i: (i, 0))
    per_row = pl.BlockSpec((heads, bq), lambda i: (0, i))
    return pl.pallas_call(
        functools.partial(self_backward_kernel, bk=bk, heads=heads, safe=safe),
        grid=(n // bq,),
        in_specs=[
            pl.BlockSpec(memory_space=pltpu.SMEM),
            some,
            whole,
            whole,
            pl.BlockSpec((width, n), lambda i: (0, 0)),
            some,
            per_row,
            per_row,
        ]
        + [ANY] * 3,
        out_specs=[pl.BlockSpec((width, bq), lambda i: (0, i)), whole, whole, done, done, ANY],
        out_shape=[
            jax.ShapeDtypeStruct((width, n), BF16),
            jax.ShapeDtypeStruct((n, width), BF16),
            jax.ShapeDtypeStruct((n, width), BF16),
            jax.ShapeDtypeStruct((r, c), F32),
            jax.ShapeDtypeStruct((r, c), F32),
            jax.ShapeDtypeStruct((m, r, cross_c), BF16),
        ],
        scratch_shapes=[
            pltpu.VMEM((n, width), F32),
            pltpu.VMEM((n, width), F32),
            pltpu.VMEM((width, bq), F32),
        ]
        + gather_scratch(m, r, cross_c)
        + [pltpu.VMEM((m, r, c), BF16)] * 2
        + [pltpu.VMEM((m, r, c), BF16)] * 2
        + link_scratch(4 + 2 * m, 6),
        compiler_params=pltpu.CompilerParams(
            vmem_limit_bytes=VMEM_LIMIT, collective_id=5, has_side_effects=True
        ),
        cost_estimate=pl.CostEstimate(
            flops=24 * n * n * width, bytes_accessed=16 * n * width, transcendentals=n * n * heads // 2
        ),
        name="self_backward",
    )(bounds, queries, keys, values, keys_t, grads, lse, inner, up_column, down_column, cross_sum)


def const(shape):
    return pl.BlockSpec(shape, lambda *_: (0,) * len(shape), pipeline_mode=pl.Buffered(1))


def normalized(rows):
    center = rows - jnp.mean(rows, axis=-1, keepdims=True)
    scale = lax.rsqrt(jnp.mean(center * center, axis=-1, keepdims=True) + EPSILON)
    return center * scale, scale


def norm_rows_back(rows, incoming, gain):
    xhat, scale = normalized(rows)
    e = incoming * gain
    inner = jnp.mean(e * xhat, axis=-1, keepdims=True)
    return scale * (e - jnp.mean(e, axis=-1, keepdims=True) - xhat * inner), incoming * xhat


def by_rows(count, step, body):
    def one(k, c):
        body(pl.ds(pl.multiple_of(k * step, step), step))
        return c

    lax.fori_loop(0, count // step, one, 0)


def cross_forward_kernel(
    ok_ref, x_ref, enc_ref, w_ref, bq_ref, bv_ref, rows_ref, shift_ref, norm_ref, column_ref,
    q_out, k_out, v_out, ot_ref, lse_ref, after_ref, third_ref, whole, send_sems, recv_sems, local_sems, *, heads
):
    i = pl.program_id(0)
    last = pl.num_programs(0) - 1
    links = Links(send_sems, recv_sems, local_sems)
    spread = Spread(links, column_ref, whole)

    @pl.when(i == 0)
    def _():
        links.greet([CORE, X, Y])
        spread.start()
        after_ref[...] = rows_ref[...] + shift_ref[...]

    width = q_out.shape[2]
    hd = width // heads
    query = (dot_nn(x_ref[...], w_ref[0, :, :width]) + bq_ref[0]).astype(BF16)
    key_value = dot_nn(enc_ref[...], w_ref[0, :, width : 3 * width])
    keys = key_value[:, :width].astype(BF16)
    values = (key_value[:, width:] + bv_ref[0]).astype(BF16)
    q_out[0] = query
    k_out[0] = keys
    v_out[0] = values
    values_t = values.T
    scaled = query * jnp.asarray(1.0 / math.sqrt(hd), BF16)
    ok = ok_ref[...] > 0.0
    scores = [dot_nt(keys, head_only(scaled, h, hd)) for h in range(heads)]
    mixed = []
    for h in range(heads):
        part = slice(h * hd, (h + 1) * hd)
        s = jnp.where(ok, scores[h], NEGATIVE)
        largest = jnp.max(s, axis=0, keepdims=True)
        expos = jnp.exp(s - largest)
        total = jnp.sum(expos, axis=0, keepdims=True)
        mixed.append((dot_nn(values_t[part, :], expos.astype(BF16)) * (1.0 / total)).astype(BF16))
        ot_ref[0, part, :] = mixed[h]
        lse_ref[0, h : h + 1, :] = largest + jnp.log(total)
    after_ref[...] += dot_nt(jnp.concatenate(mixed, 0).T, w_ref[0, :, 3 * width :])

    @pl.when(i == last)
    def _():
        spread.middle()

        def norm(rows):
            xhat, _ = normalized(after_ref[rows, :])
            third_ref[rows, :] = (xhat * norm_ref[0:1, :] + norm_ref[1:2, :]).astype(BF16)

        by_rows(after_ref.shape[0], 128, norm)
        spread.end()


def cross_forward(ok, x, encoder, weights, q_shift, v_shift, rows, shift, norm, column, heads):
    count, model = x.shape
    n = encoder.shape[0]
    parts, _, columns = weights.shape
    width = columns // 4
    m, r, c = column.shape

    def by_part(*shape):
        return pl.BlockSpec((1,) + shape, lambda i: (i,) + (0,) * len(shape))

    return pl.pallas_call(
        functools.partial(cross_forward_kernel, heads=heads),
        grid=(parts,),
        in_specs=[
            const((n, 1)),
            const((count, model)),
            const((n, model)),
            by_part(model, columns),
            by_part(1, width),
            by_part(1, width),
            const((count, model)),
            const((1, model)),
            const((2, model)),
            ANY,
        ],
        out_specs=[
            by_part(count, width),
            by_part(n, width),
            by_part(n, width),
            by_part(width, count),
            by_part(heads, count),
            const((count, model)),
            const((count, model)),
            ANY,
        ],
        out_shape=[
            jax.ShapeDtypeStruct((parts, count, width), BF16),
            jax.ShapeDtypeStruct((parts, n, width), BF16),
            jax.ShapeDtypeStruct((parts, n, width), BF16),
            jax.ShapeDtypeStruct((parts, width, count), BF16),
            jax.ShapeDtypeStruct((parts, heads, count), F32),
            jax.ShapeDtypeStruct((count, model), F32),
            jax.ShapeDtypeStruct((count, model), BF16),
            jax.ShapeDtypeStruct((4, m, 2, r, c), BF16),
        ],
        scratch_shapes=link_scratch(8, 1),
        compiler_params=pltpu.CompilerParams(
            vmem_limit_bytes=VMEM_LIMIT, collective_id=2, has_side_effects=True
        ),
        cost_estimate=pl.CostEstimate(
            flops=24 * parts * count * n * width,
            bytes_accessed=8 * parts * n * width,
            transcendentals=parts * count * n * heads,
        ),
        name="cross_forward",
    )(ok, x, encoder, weights, q_shift, v_shift, rows, shift, norm, column)


def feed_forward_kernel(
    x_ref, dy_ref, up_ref, down_ref, b_ref, after_ref, shift_ref, norm_ref,
    out_ref, rows_out, low_out, sums_ref, gup_ref, gdown_ref, bias_ref,
    xt_ref, dyt_ref, back_ref, give, got, send_sems, recv_sems, local_sems, *, chunks
):
    s = pl.program_id(0)
    links = Links(send_sems, recv_sems, local_sems)
    turn = s // chunks
    chunk = s % chunks
    pair = turn // 2
    slot = pair * chunks + chunk
    theirs = turn % 2 == 0
    to_core = pltpu.make_async_remote_copy(
        src_ref=give.at[chunk],
        dst_ref=got.at[slot],
        send_sem=send_sems.at[slot],
        recv_sem=recv_sems.at[slot],
        device_id=links.partner(CORE),
        device_id_type=pl.DeviceIdType.MESH,
    )

    @pl.when(s == 0)
    def _():
        links.greet([CORE])
        out_ref[...] = after_ref[...] + shift_ref[...]
        back_ref[...] = jnp.zeros_like(back_ref)
        xt_ref[...] = x_ref[...].T
        dyt_ref[...] = dy_ref[...].T
        sums_ref[...] = jnp.zeros_like(sums_ref)

    pre_act = dot_nn(x_ref[...], up_ref[0]) + b_ref[0]
    hidden_grad = dot_nn(dy_ref[...], down_ref[0])
    normal_cdf = 0.5 * (1.0 + lax.erf(pre_act * (1.0 / math.sqrt(2.0))))
    density = jnp.exp(-0.5 * pre_act * pre_act) * (1.0 / math.sqrt(2.0 * math.pi))
    hidden = (pre_act * normal_cdf).astype(BF16)
    pre_grad = (hidden_grad * (normal_cdf + pre_act * density)).astype(BF16)
    bias_ref[0] = jnp.sum(pre_grad.astype(F32), axis=0, keepdims=True)

    @pl.when(turn % 2 == 1)
    def _():
        to_core.wait_send()

    give[chunk, 0] = dot_nn(xt_ref[...], pre_grad).astype(BF16)
    give[chunk, 1] = dot_nn(dyt_ref[...], hidden).astype(BF16)
    out_ref[...] += dot_nt(hidden, down_ref[0])
    back_ref[...] += dot_nt(pre_grad, up_ref[0])

    @pl.when(theirs)
    def _():
        to_core.start()

    @pl.when(jnp.logical_not(theirs))
    def _():
        to_core.wait_recv()
        gup_ref[0] = (give[chunk, 0].astype(F32) + got[slot, 0].astype(F32)).astype(BF16)
        gdown_ref[0] = (give[chunk, 1].astype(F32) + got[slot, 1].astype(F32)).astype(BF16)

    @pl.when(s == pl.num_programs(0) - 1)
    def _():
        def norm_back(rows):
            third = back_ref[rows, :]
            upstream = dy_ref[rows, :].astype(F32)
            rows_grad, gain_terms = norm_rows_back(after_ref[rows, :], third, norm_ref[0:1, :])
            rows_grad = rows_grad + upstream
            low = rows_grad.astype(BF16)
            rows_out[rows, :] = rows_grad
            low_out[rows, :] = low
            for k, terms in enumerate((gain_terms, third, low.astype(F32), upstream)):
                sums_ref[k : k + 1, :] += jnp.sum(terms, axis=0, keepdims=True)

        by_rows(x_ref.shape[0], 128, norm_back)


def feed_forward(x, dy, weights, bias, after, shift, norm):
    rows, width = x.shape
    hidden = weights.shape[2] // 2
    size = min(512, hidden)
    chunks = hidden // size

    def block(s):
        return (s // chunks) ^ 1

    def placed(s):
        turn = s // chunks
        return (turn // 2, 0, (s % chunks) * (turn % 2))

    rows_spec = const((rows, width))
    grad_spec = pl.BlockSpec((1, width, size), placed)
    bias_spec = pl.BlockSpec((1, 1, size), lambda s: (block(s), 0, s % chunks))
    return pl.pallas_call(
        functools.partial(feed_forward_kernel, chunks=chunks),
        grid=(4 * chunks,),
        in_specs=[
            rows_spec,
            rows_spec,
            pl.BlockSpec((1, width, size), lambda s: (block(s), 0, s % chunks)),
            pl.BlockSpec((1, width, size), lambda s: (block(s), 0, chunks + s % chunks)),
            bias_spec,
            rows_spec,
            const((1, width)),
            const((2, width)),
        ],
        out_specs=[rows_spec, rows_spec, rows_spec, const((8, width)), grad_spec, grad_spec, bias_spec],
        out_shape=[
            jax.ShapeDtypeStruct((rows, width), F32),
            jax.ShapeDtypeStruct((rows, width), F32),
            jax.ShapeDtypeStruct((rows, width), BF16),
            jax.ShapeDtypeStruct((8, width), F32),
            jax.ShapeDtypeStruct((2, width, hidden), BF16),
            jax.ShapeDtypeStruct((2, width, hidden), BF16),
            jax.ShapeDtypeStruct((4, 1, hidden), F32),
        ],
        scratch_shapes=[
            pltpu.VMEM((width, rows), BF16),
            pltpu.VMEM((width, rows), BF16),
            pltpu.VMEM((rows, width), F32),
            pltpu.VMEM((chunks, 2, width, size), BF16),
            pltpu.VMEM((2 * chunks, 2, width, size), BF16),
        ]
        + link_scratch(2 * chunks, 1),
        compiler_params=pltpu.CompilerParams(
            vmem_limit_bytes=VMEM_LIMIT, collective_id=3, has_side_effects=True
        ),
        cost_estimate=pl.CostEstimate(
            flops=48 * rows * width * hidden, bytes_accessed=40 * 2**20, transcendentals=8 * rows * hidden
        ),
        name="feed_forward",
    )(x, dy, weights, weights, bias, after, shift, norm)


def cross_backward_kernel(
    ok_ref, low_ref, x_ref, enc_ref, w_ref, q_ref, k_ref, v_ref, mt_ref, lse_ref, up_ref, down_ref,
    back_ref, enc_out, grad_ref, bq_ref, bv_ref, up_out, down_out,
    low_t, x_t, enc_t, enc_acc, give, got, *scratch, heads, bk
):
    i = pl.program_id(0)
    last = pl.num_programs(0) - 1
    links = Links(*scratch[14:])
    sums = [
        Gather(links, ref.at[0], ref.at[1], scratch[7 * k : 7 * k + 7]) for k, ref in enumerate((up_ref, down_ref))
    ]
    leave = [links.local(g.column, out) for g, out in zip(sums, (up_out, down_out))]
    pair = i // 2
    to_core = pltpu.make_async_remote_copy(
        src_ref=give,
        dst_ref=got.at[pair],
        send_sem=links.send_sems.at[links.used + pair],
        recv_sem=links.recv_sems.at[links.used + pair],
        device_id=links.partner(CORE),
        device_id_type=pl.DeviceIdType.MESH,
    )

    @pl.when(i == 0)
    def _():
        links.greet([CORE, X, Y])
        for g in sums:
            g.start()
        low_t[...] = low_ref[...].T
        x_t[...] = x_ref[...].T
        enc_t[...] = enc_ref[...].T
        back_ref[...] = jnp.zeros_like(back_ref)
        enc_acc[...] = jnp.zeros_like(enc_acc)

    @pl.when(i == 2)
    def _():
        for g in sums:
            g.middle()

    rows, width = q_ref.shape[1:]
    n = k_ref.shape[1]
    hd = width // heads
    scale = 1.0 / math.sqrt(hd)
    w_query, w_keyval, w_out = w_ref.at[0, :, :width], w_ref.at[0, :, width : 3 * width], w_ref.at[0, :, 3 * width :]
    grads = dot_nn(low_ref[...], w_out[...]).astype(BF16)
    mixed_t = mt_ref[0]
    products = grads.T.astype(F32) * mixed_t.astype(F32)
    inner = [jnp.sum(products[h * hd : (h + 1) * hd, :], axis=0, keepdims=True) for h in range(heads)]
    scaled = q_ref[0] * jnp.asarray(scale, BF16)
    q_heads = [head_only(scaled, h, hd) for h in range(heads)]
    d_heads = [head_only(grads, h, hd) for h in range(heads)]
    lse = lse_ref[0]
    keys_t = k_ref[0].T
    dq = [None] * heads
    dkv = []
    for j in range(n // bk):
        span = slice(j * bk, (j + 1) * bk)
        keys = k_ref[0, span, :]
        values = v_ref[0, span, :]
        ok = ok_ref[span, :] > 0.0
        scores = [dot_nt(keys, q_heads[h]) for h in range(heads)]
        dprobs = [dot_nt(values, d_heads[h]) for h in range(heads)]
        dv_sum, dk_sum = None, None
        for h in range(heads):
            part = slice(h * hd, (h + 1) * hd)
            probs = jnp.exp(jnp.where(ok, scores[h], NEGATIVE) - lse[h : h + 1, :])
            ds = (probs * (dprobs[h] - inner[h])).astype(BF16)
            dv_h = dot_nn(probs.astype(BF16), d_heads[h])
            dk_h = dot_nn(ds, q_heads[h])
            dv_sum = dv_h if dv_sum is None else dv_sum + dv_h
            dk_sum = dk_h if dk_sum is None else dk_sum + dk_h
            dq_h = dot_nn(keys_t[part, span], ds)
            dq[h] = dq_h if dq[h] is None else dq[h] + dq_h
        block = jnp.concatenate([dk_sum.astype(BF16), dv_sum.astype(BF16)], 1)
        enc_acc[span, :] += dot_nt(block, w_keyval[...])
        dkv.append(block)
    dq = (jnp.concatenate(dq, 0) * scale).astype(BF16).T
    dkv = jnp.concatenate(dkv, 0)
    bq_ref[0] = jnp.sum(dq.astype(F32), axis=0, keepdims=True)
    bv_ref[0] = jnp.sum(dkv[:, width:].astype(F32), axis=0, keepdims=True)
    back_ref[...] += dot_nt(dq, w_query[...])

    @pl.when(i % 2 == 1)
    def _():
        to_core.wait_send()

    give[:, :width] = dot_nn(x_t[...], dq).astype(BF16)
    give[:, width : 3 * width] = dot_nn(enc_t[...], dkv).astype(BF16)
    give[:, 3 * width :] = dot_nn(low_t[...], mixed_t.T).astype(BF16)

    @pl.when(i % 2 == 0)
    def _():
        to_core.start()

    @pl.when(i % 2 == 1)
    def _():
        to_core.wait_recv()
        grad_ref[0] = (give[...].astype(F32) + got[pair].astype(F32)).astype(BF16)

    @pl.when(i == last)
    def _():
        enc_out[...] = enc_acc[...].astype(BF16)
        for g, copy in zip(sums, leave):
            g.end()
            copy.start()
        for copy in leave:
            copy.wait()


def cross_backward(ok, low, x, encoder, weights, queries, keys, values, mixed_t, lse, up_sum, down_sum, heads):
    count, model = x.shape
    n = encoder.shape[0]
    parts, _, columns = weights.shape
    width = columns // 4
    _, m, _, r, c = up_sum.shape

    def by_part(*shape):
        return pl.BlockSpec((1,) + shape, lambda i: (i ^ 1,) + (0,) * len(shape))

    return pl.pallas_call(
        functools.partial(cross_backward_kernel, heads=heads, bk=256),
        grid=(parts,),
        in_specs=[
            const((n, 1)),
            const((count, model)),
            const((count, model)),
            const((n, model)),
            by_part(model, columns),
            by_part(count, width),
            by_part(n, width),
            by_part(n, width),
            by_part(width, count),
            by_part(heads, count),
            ANY,
            ANY,
        ],
        out_specs=[
            const((count, model)),
            const((n, model)),
            pl.BlockSpec((1, model, columns), lambda i: (i // 2, 0, 0), pipeline_mode=pl.Buffered(1)),
            by_part(1, width),
            by_part(1, width),
            ANY,
            ANY,
        ],
        out_shape=[
            jax.ShapeDtypeStruct((count, model), F32),
            jax.ShapeDtypeStruct((n, model), BF16),
            jax.ShapeDtypeStruct((2, model, columns), BF16),
            jax.ShapeDtypeStruct((parts, 1, width), F32),
            jax.ShapeDtypeStruct((parts, 1, width), F32),
            jax.ShapeDtypeStruct((m, r, c), BF16),
            jax.ShapeDtypeStruct((m, r, c), BF16),
        ],
        scratch_shapes=[
            pltpu.VMEM((model, count), BF16),
            pltpu.VMEM((model, count), BF16),
            pltpu.VMEM((model, n), BF16),
            pltpu.VMEM((n, model), F32),
            pltpu.VMEM((model, columns), BF16),
            pltpu.VMEM((2, model, columns), BF16),
        ]
        + gather_scratch(m, r, c) * 2
        + link_scratch(10, 8),
        compiler_params=pltpu.CompilerParams(
            vmem_limit_bytes=60 * 2**20, collective_id=4, has_side_effects=True
        ),
        cost_estimate=pl.CostEstimate(
            flops=48 * parts * count * n * width,
            bytes_accessed=16 * parts * n * width,
            transcendentals=parts * count * n * heads,
        ),
        name="cross_backward",
    )(ok, low, x, encoder, weights, queries, keys, values, mixed_t, lse, up_sum, down_sum)


def swap(value, axis, distance):
    size = lax.axis_size(axis)
    return lax.ppermute(value, axis, [(i, i ^ distance) for i in range(size)])


def dp_distances():
    n = lax.axis_size("dp")
    found = []
    while n > 1:
        n //= 2
        found.append(n)
    return found


def add_low(a, b):
    return (a.astype(F32) + b.astype(F32)).astype(BF16)


def reduce_dp(total, distances, axes):
    me = lax.axis_index("dp")
    rows, columns = total.shape[0] // 2 ** len(axes), total.shape[1]
    shape = [2] * len(axes) + [rows, columns]
    axes = list(axes)
    total = total.reshape(shape)
    for step, distance in enumerate(distances):
        axis = axes.index(distance)
        axes.pop(axis)
        mine = me // distance % 2
        keep = lax.dynamic_index_in_dim(total, mine, axis, keepdims=False)
        give = lax.dynamic_index_in_dim(total, 1 - mine, axis, keepdims=False)
        got = swap(give, "dp", distance)
        total = keep.astype(F32) + got.astype(F32)
        if step < len(distances) - 1:
            total = total.astype(BF16)
    return total


def sum_everywhere(value):
    for distance in (1, 2):
        value = value + swap(value, "tensor", distance)
    for distance in dp_distances():
        value = value + swap(value, "dp", distance)
    return value


def widen(rows_low):
    member = lax.axis_index("tensor")
    count, width = rows_low.shape
    other = swap(rows_low, "tensor", 2)
    parts = [rows_low, swap(rows_low, "tensor", 1), other, swap(other, "tensor", 1)]
    out = jnp.zeros((4 * count, width), rows_low.dtype)
    for distance, part in enumerate(parts):
        out = lax.dynamic_update_slice(out, part, ((member ^ distance) * count, 0))
    return out


def narrow(rows_low):
    member = lax.axis_index("tensor")
    count = rows_low.shape[0] // 4
    parts = [
        lax.dynamic_slice_in_dim(rows_low, (member ^ distance) * count, count, 0)
        for distance in range(4)
    ]
    far = add_low(parts[2], swap(parts[3], "tensor", 1))
    got = swap(far, "tensor", 2)
    near = parts[0].astype(F32) + swap(parts[1], "tensor", 1).astype(F32)
    return near + got.astype(F32)


def on_device(
    block_in,
    encoder_out,
    out_grad,
    bounds,
    enc_lengths,
    norm_params,
    w_qkv,
    w_self_out,
    w_cross_q,
    w_cross_kv,
    w_cross_out,
    w_up,
    w_down,
    biases,
    up_bias,
):
    member = lax.axis_index("tensor")
    groups_count = lax.axis_size("dp")
    groups = float(groups_count)
    width = w_cross_q.shape[1]
    hidden_width = w_up.shape[1]
    heads = H // 4
    own_rows, model_width = block_in.shape
    enc_rows = encoder_out.shape[0]
    w_rows = w_cross_q.shape[0]

    def block_of(vector, size, distance):
        return lax.dynamic_slice_in_dim(vector, (member ^ distance) * size, size)

    def blocks_placed(parts):
        size = parts[0].shape[0]
        out = jnp.zeros((4 * size,), F32)
        for distance, part in enumerate(parts):
            out = lax.dynamic_update_slice_in_dim(out, part, (member ^ distance) * size, 0)
        return out

    def norm_back(rows, incoming, which):
        _, pull_rows = jax.vjp(layer_norm, rows, norm_params[which, 0], norm_params[which, 1])
        return pull_rows(incoming)

    start_rows = block_in.astype(F32)
    first_in, enc_all, self_w, cross_column = start_gather(
        layer_norm(start_rows, norm_params[0, 0], norm_params[0, 1]).astype(BF16),
        encoder_out,
        jnp.concatenate([w_qkv.reshape(w_rows, 3 * width), w_self_out.T], axis=1),
        jnp.concatenate([w_cross_q, w_cross_kv.reshape(w_rows, 2 * width), w_cross_out.T], axis=1),
    )
    self_w = self_w.reshape(model_width, 4 * width)

    projected = dot_nn(first_in, self_w[:, : 3 * width])
    queries = (projected[:, :width] + block_of(biases[0], width, 0)).astype(BF16)
    key_rows = projected[:, width : 2 * width].astype(BF16)
    value_rows = (projected[:, 2 * width :] + block_of(biases[1], width, 0)).astype(BF16)
    self_safe = 1024
    self_mixed_t, self_lse, cross_w, ffn_column = self_forward(
        bounds,
        queries,
        key_rows,
        value_rows.T,
        cross_column,
        jnp.concatenate([w_up, w_down.T], axis=1),
        heads,
        self_safe,
    )
    cross_w = cross_w.reshape(4, model_width, 4 * width)
    self_out_w = self_w[:, 3 * width :]
    after_self = (
        start_rows
        + narrow(lax.dot_general(self_mixed_t, self_out_w, (((0,), (1,)), ((), ())), preferred_element_type=F32).astype(BF16))
        + biases[2]
    )

    ok = (jnp.arange(4 * enc_rows, dtype=jnp.int32) < enc_lengths[0]).astype(F32)[:, None]
    second_in = layer_norm(after_self, norm_params[1, 0], norm_params[1, 1]).astype(BF16)

    def all_blocks(vector, size):
        return jnp.stack([block_of(vector, size, d) for d in range(4)])[:, None]

    cross_q, cross_k, cross_v, cross_mixed_t, cross_lse, after_cross, third_in, ffn_w = cross_forward(
        ok,
        second_in,
        enc_all,
        cross_w,
        all_blocks(biases[3], width),
        all_blocks(biases[4], width),
        after_self,
        biases[5:6],
        norm_params[2],
        ffn_column,
        heads,
    )

    output, cross_rows_grad, cross_low, ffn_sums, up_sum, down_sum, bias_up_parts = feed_forward(
        third_in,
        out_grad,
        ffn_w.reshape(4, model_width, 2 * hidden_width),
        all_blocks(up_bias, hidden_width),
        after_cross,
        biases[6:7],
        norm_params[2],
    )
    gain_three, shift_three, bias_co_grad, bias_down_grad = (ffn_sums[k] for k in range(4))

    by_shard = (2, groups_count // 2, 2, w_rows, hidden_width)
    second_grad, enc_terms, cross_sum, bias_cq_parts, bias_cv_parts, up_column, down_column = cross_backward(
        ok,
        cross_low,
        second_in,
        enc_all,
        cross_w,
        cross_q,
        cross_k,
        cross_v,
        cross_mixed_t,
        cross_lse,
        up_sum.reshape(by_shard),
        down_sum.reshape(by_shard),
        heads,
    )
    rows_two, gain_two, shift_two = norm_back(after_self, second_grad, 1)
    self_rows_grad = cross_rows_grad + rows_two
    self_low = self_rows_grad.astype(BF16)
    bias_so_grad = jnp.sum(self_low.astype(F32), axis=0)
    self_wide = widen(self_low)
    encoder_grad = narrow(enc_terms)
    bias_cq_grad = blocks_placed([bias_cq_parts[d, 0] for d in range(4)])
    bias_cv_grad = blocks_placed([bias_cv_parts[d, 0] for d in range(4)])
    bias_up_grad = blocks_placed([bias_up_parts[d, 0] for d in range(4)])

    self_mixed_grad = dot_nn(self_wide, self_out_w).astype(BF16)
    self_inner = jnp.sum(
        self_mixed_t.reshape(heads, width // heads, 4 * own_rows).astype(F32)
        * self_mixed_grad.T.reshape(heads, width // heads, 4 * own_rows).astype(F32),
        axis=1,
    )
    self_dq_t, self_dk, self_dv, summed_up, summed_down, cross_column = self_backward(
        bounds,
        queries,
        key_rows,
        value_rows,
        key_rows.T,
        self_mixed_grad,
        self_lse,
        self_inner,
        up_column,
        down_column,
        cross_sum.reshape(2, groups_count // 2, 2, w_rows, 4 * width),
        heads,
        self_safe,
    )
    summed_cross = reduce_dp(cross_column.reshape(-1, 4 * width), dp_distances()[-2::-1], dp_distances()[:-1])
    grad_so_t = lax.dot_general(
        self_wide, self_mixed_t, (((0,), (1,)), ((), ())), preferred_element_type=F32
    ).astype(BF16)
    qkv_grad = jnp.concatenate([self_dq_t.T, self_dk, self_dv], axis=1)
    first_terms = dot_nt(qkv_grad, self_w[:, : 3 * width]).astype(BF16)
    first_grad = narrow(first_terms)
    summed_self = reduce_dp(
        jnp.concatenate([dot_tn(first_in, qkv_grad).astype(BF16), grad_so_t], axis=1),
        dp_distances()[::-1],
        dp_distances(),
    )
    column_sums = jnp.sum(qkv_grad.astype(F32), axis=0)
    rows_one, gain_one, shift_one = norm_back(start_rows, first_grad, 0)
    input_grad = self_rows_grad + rows_one

    def only_own(part):
        out = jnp.zeros((model_width,), F32)
        return lax.dynamic_update_slice_in_dim(out, part, member * width, 0)

    early = sum_everywhere(
        jnp.concatenate(
            [
                gain_two,
                shift_two,
                gain_three,
                shift_three,
                bias_so_grad,
                bias_cq_grad,
                bias_cv_grad,
                bias_co_grad,
                bias_down_grad,
                bias_up_grad,
            ]
        ).reshape(-1, 128)
    ).reshape(-1, model_width)
    late = sum_everywhere(
        jnp.concatenate(
            [gain_one, shift_one, only_own(column_sums[:width]), only_own(column_sums[2 * width :])]
        ).reshape(-1, 128)
    ).reshape(-1, model_width)
    norm_total = jnp.stack([late[0], late[1], early[0], early[1], early[2], early[3]]).reshape(
        norm_params.shape
    )
    bias_total = jnp.stack([late[2], late[3], early[4], early[5], early[6], early[7], early[8]])
    up_total = early[9:].reshape(-1)
    scale = 1.0 / groups
    return (
        output,
        input_grad,
        encoder_grad,
        norm_total * scale,
        summed_self[:, : 3 * width].reshape(w_qkv.shape) * scale,
        summed_self[:, 3 * width :].T * scale,
        summed_cross[:, :width] * scale,
        summed_cross[:, width : 3 * width].reshape(w_cross_kv.shape) * scale,
        summed_cross[:, 3 * width :].T * scale,
        summed_up * scale,
        summed_down.T * scale,
        bias_total * scale,
        up_total * scale,
    )


def solution(mesh):
    rows = P(("dp", "tensor"), None)
    placed = (
        rows,
        rows,
        rows,
        P("dp", None),
        P("dp"),
        P(),
        P("dp", None, "tensor"),
        P("tensor", "dp"),
        P("dp", "tensor"),
        P("dp", None, "tensor"),
        P("tensor", "dp"),
        P("dp", "tensor"),
        P("tensor", "dp"),
        P(),
        P(),
    )
    return jax.shard_map(
        on_device,
        mesh=mesh,
        in_specs=placed,
        out_specs=(
            rows,
            rows,
            rows,
            P(),
            P("dp", None, "tensor"),
            P("tensor", "dp"),
            P("dp", "tensor"),
            P("dp", None, "tensor"),
            P("tensor", "dp"),
            P("dp", "tensor"),
            P("tensor", "dp"),
            P(),
            P(),
        ),
        check_vma=False,
    )
```

```python
import functools
import math

import jax
import jax.numpy as jnp
from jax import lax
from jax.experimental import pallas as pl
from jax.experimental.pallas import tpu as pltpu
from jax.sharding import PartitionSpec as P

H = 16
EPSILON = 1e-05
NEGATIVE = -1e30
F32 = jnp.float32
BF16 = jnp.bfloat16
VMEM_LIMIT = 56 * 2**20


def dot_nt(a, b):
    return lax.dot_general(a, b, (((1,), (1,)), ((), ())), preferred_element_type=F32)


def dot_nn(a, b):
    return lax.dot_general(a, b, (((1,), (0,)), ((), ())), preferred_element_type=F32)


def dot_tn(a, b):
    return lax.dot_general(a, b, (((0,), (0,)), ((), ())), preferred_element_type=F32)


def layer_norm(inputs, gain_row, shift_row):
    center = inputs - jnp.mean(inputs, axis=-1, keepdims=True)
    spread = jnp.mean(center * center, axis=-1, keepdims=True)
    return center * lax.rsqrt(spread + EPSILON) * gain_row + shift_row


def gelu_slope(values_in):
    normal_cdf = 0.5 * (1.0 + lax.erf(values_in * (1.0 / math.sqrt(2.0))))
    density = jnp.exp(-0.5 * values_in * values_in) * (1.0 / math.sqrt(2.0 * math.pi))
    return normal_cdf + values_in * density


def head_only(x, h, size):
    lane = lax.broadcasted_iota(jnp.int32, x.shape, 1)
    return jnp.where((lane >= h * size) & (lane < (h + 1) * size), x, jnp.zeros_like(x))


def self_bad(b_ref, q_start, k_start, bq, bk, causal):
    qi = q_start + lax.broadcasted_iota(jnp.int32, (1, bq), 1)
    kj = k_start + lax.broadcasted_iota(jnp.int32, (bk, 1), 0)
    bad = (qi >= b_ref[0, 1]) & ((kj >= b_ref[0, 0]) & (kj < b_ref[0, 1]))
    if causal:
        bad = bad | (kj > qi)
    return bad


def over_keys(i, bq, bk, safe, block):
    diagonal = i * (bq // bk)

    def visit(j, c):
        @pl.when(j < safe // bk)
        def _():
            block(j, "none")

        @pl.when(j >= safe // bk)
        def _():
            block(j, "segment")

        return c

    lax.fori_loop(0, diagonal, visit, 0)
    for step in range(bq // bk):
        block(diagonal + step, "causal")


CORE = ("tensor", 1)
X = ("tensor", 2)
Y = ("dp", 1)
ANY = pl.BlockSpec(memory_space=pl.ANY)


class Links:
    def __init__(self, send_sems, recv_sems, local_sems):
        self.dp = lax.axis_index("dp")
        self.tensor = lax.axis_index("tensor")
        self.send_sems, self.recv_sems, self.local_sems = send_sems, recv_sems, local_sems
        self.used = 0
        self.used_local = 0

    def partner(self, way):
        axis, distance = way
        if axis == "tensor":
            return (self.dp, self.tensor ^ distance)
        return (self.dp ^ distance, self.tensor)

    def greet(self, ways):
        barrier = pltpu.get_barrier_semaphore()
        for way in ways:
            pl.semaphore_signal(
                barrier, inc=1, device_id=self.partner(way), device_id_type=pl.DeviceIdType.MESH
            )
        pl.semaphore_wait(barrier, len(ways))

    def copy(self, source, target, way):
        k = self.used
        self.used += 1
        return pltpu.make_async_remote_copy(
            src_ref=source,
            dst_ref=target,
            send_sem=self.send_sems.at[k],
            recv_sem=self.recv_sems.at[k],
            device_id=self.partner(way),
            device_id_type=pl.DeviceIdType.MESH,
        )

    def local(self, source, target):
        k = self.used_local
        self.used_local += 1
        return pltpu.make_async_copy(source, target, self.local_sems.at[k])


def link_scratch(copies, local):
    return [
        pltpu.SemaphoreType.DMA((copies,)),
        pltpu.SemaphoreType.DMA((copies,)),
        pltpu.SemaphoreType.DMA((local,)),
    ]


def z_distances(n):
    found = []
    m = n // 2
    while m > 1:
        m //= 2
        found.append(m)
    return found


def z_ways(n):
    return [("dp", 2 * distance) for distance in z_distances(n)]


def column_stages(links, shard, column, n):
    z = links.dp // 2
    held = [z]
    stages = []
    for distance in z_distances(n):
        stages.append(
            [
                (
                    links.copy(shard if k == 0 else column.at[index], column.at[index], ("dp", 2 * distance)),
                    index ^ distance,
                )
                for k, index in enumerate(held)
            ]
        )
        held = held + [index ^ distance for index in held]
    return stages


class Spread:
    def __init__(self, links, column, whole):
        y = links.dp % 2
        half = column.shape[0] // 2
        low, high = pl.ds(0, half), pl.ds(half, half)
        near, near_core, far, far_core = (whole.at[k] for k in range(4))
        self.own = links.local(column, near.at[:, y])
        self.first = [
            links.copy(column, near.at[:, y], Y),
            links.copy(column, far.at[:, y], X),
        ]
        self.core = [links.copy(column, near_core.at[:, y], CORE)]
        self.second = [
            links.copy(near.at[low, 1 - y], far.at[low, 1 - y], X),
            links.copy(far.at[high, y], far.at[high, y], Y),
        ]
        self.core_second = [
            links.copy(near.at[:, 1 - y], near_core.at[:, 1 - y], CORE),
            links.copy(far.at[:, y], far_core.at[:, y], CORE),
        ]
        self.core_third = [links.copy(far.at[:, 1 - y], far_core.at[:, 1 - y], CORE)]

    def start(self):
        self.own.start()
        for copy in self.first + self.core:
            copy.start()

    def middle(self):
        for copy in self.first:
            copy.wait_recv()
        for copy in self.second + self.core_second:
            copy.start()

    def end(self):
        for copy in self.second:
            copy.wait_recv()
        for copy in self.core_third:
            copy.start()
        self.own.wait()
        for copy in self.first + self.second:
            copy.wait_send()
        for copy in self.core + self.core_second + self.core_third:
            copy.wait()


def add_to(total_ref, other_ref):
    def one(k, c):
        total_ref[k] = (total_ref[k].astype(F32) + other_ref[k].astype(F32)).astype(BF16)
        return c

    lax.fori_loop(0, total_ref.shape[0], one, 0)


class Gather:
    def __init__(self, links, near, far, buffers):
        y = links.dp % 2
        self.column, self.over_y, self.over_x, self.got_y, self.got_x, self.sum_y, self.sum_x = buffers
        m = self.column.shape[0]
        low, high = pl.ds(0, m // 2), pl.ds(m // 2, m // 2)
        self.low, self.high = low, high
        self.loads = [
            links.local(near.at[:, y], self.column),
            links.local(near.at[:, 1 - y], self.over_y),
            links.local(far.at[:, y], self.over_x),
        ]
        diagonal = far.at[:, 1 - y]
        self.first = [
            links.copy(diagonal.at[low], self.got_y, X),
            links.copy(diagonal.at[high], self.got_x, Y),
        ]
        self.second = [
            links.copy(self.over_x, self.sum_x, X),
            links.copy(self.over_y, self.sum_y, Y),
        ]

    def start(self):
        for copy in self.loads + self.first:
            copy.start()

    def middle(self):
        for copy in self.loads:
            copy.wait()
        for copy in self.first:
            copy.wait_recv()
        add_to(self.over_y.at[self.low], self.got_y)
        add_to(self.over_x.at[self.high], self.got_x)
        for copy in self.second:
            copy.start()

    def end(self):
        for copy in self.second:
            copy.wait_recv()
        add_to(self.column, self.sum_y)
        add_to(self.column, self.sum_x)
        for copy in self.first + self.second:
            copy.wait_send()


def gather_scratch(m, r, c):
    whole = pltpu.VMEM((m, r, c), BF16)
    half = pltpu.VMEM((m // 2, r, c), BF16)
    return [whole] * 3 + [half] * 2 + [whole] * 2


class Collect:
    def __init__(self, links, column, slots):
        z = links.dp // 2
        self.column, self.slots, self.z = column, slots, z
        m = column.shape[0]
        distances = z_distances(2 * m)[::-1]
        self.stages = []
        first = 0
        for step, distance in enumerate(distances):
            kept = [0]
            for other in distances[step + 1 :]:
                kept = kept + [k ^ other for k in kept]
            self.stages.append(
                [
                    (links.copy(column.at[z ^ distance ^ k], slots.at[first + i], ("dp", 2 * distance)), first + i, z ^ k)
                    for i, k in enumerate(kept)
                ]
            )
            first += len(kept)

    def start(self, step):
        for copy, _, _ in self.stages[step]:
            copy.start()

    def finish(self, step):
        for copy, slot, index in self.stages[step]:
            copy.wait_recv()
            self.column[index] = (self.column[index].astype(F32) + self.slots[slot].astype(F32)).astype(BF16)

    def drain(self):
        for stage in self.stages:
            for copy, _, _ in stage:
                copy.wait_send()


class RowSum:
    def __init__(self, links, terms, buffers):
        self.near, self.far, self.got_near, self.got_far, self.got_x = buffers
        count = self.near.shape[0]

        def rows(distance):
            start = pl.multiple_of((links.tensor ^ distance) * count, count)
            return terms.at[pl.ds(start, count)]

        self.loads = [links.local(rows(0), self.near), links.local(rows(2), self.far)]
        self.core = [links.copy(rows(3), self.got_far, CORE), links.copy(rows(1), self.got_near, CORE)]
        self.over_x = links.copy(self.far, self.got_x, X)

    def start(self):
        for copy in self.loads[::-1] + self.core:
            copy.start()

    def middle(self):
        self.loads[1].wait()
        self.core[0].wait_recv()

        def add(rows):
            self.far[rows, :] = (self.far[rows, :].astype(F32) + self.got_far[rows, :].astype(F32)).astype(BF16)

        by_rows(self.far.shape[0], 64, add)
        self.over_x.start()

    def end(self):
        self.loads[0].wait()
        self.core[1].wait_recv()
        self.over_x.wait_recv()
        for copy in self.core + [self.over_x]:
            copy.wait_send()

    def total(self, rows):
        return self.near[rows, :].astype(F32) + self.got_near[rows, :].astype(F32) + self.got_x[rows, :].astype(F32)


def row_sum_scratch(count, width):
    return [pltpu.VMEM((count, width), BF16)] * 5


class Everywhere:
    def __init__(self, links, held, slots, n):
        self.held, self.slots = held, slots
        ways = everywhere_ways(n)
        self.copies = [links.copy(held.at[k], slots.at[k], way) for k, way in enumerate(ways)]

    def start(self, step):
        self.copies[step].start()

    def finish(self, step):
        self.copies[step].wait()
        self.held[step + 1] = self.held[step] + self.slots[step]


def everywhere_ways(n):
    return [CORE, X, Y] + z_ways(n)


def everywhere_scratch(k, c, n):
    steps = len(everywhere_ways(n))
    return [pltpu.VMEM((steps + 1, k, c), F32), pltpu.VMEM((steps, k, c), F32)]


def middle_kernel(
    back_ref, rows_ref, grad_ref, norm_ref, down_ref,
    wide_out, grad_out, sums_ref, down_out,
    low, column, slots, send_sems, recv_sems, local_sems, *, n
):
    links = Links(send_sems, recv_sems, local_sems)
    count = low.shape[0]
    load = links.local(down_ref, column)
    load.start()
    collect = Collect(links, column, slots)

    def place(distance):
        return wide_out.at[pl.ds(pl.multiple_of((links.tensor ^ distance) * count, count), count)]

    own = links.local(low, place(0))
    half = count // 2
    parts = [pl.ds(0, half), pl.ds(half, half)]
    over_x = [links.copy(low.at[part], place(0).at[part], X) for part in parts]
    over_core = links.copy(low, place(0), CORE)
    onward = [links.copy(place(2).at[part], place(2).at[part], CORE) for part in parts]
    links.greet([CORE, X] + z_ways(n))
    load.wait()
    collect.start(0)
    sums_ref[...] = jnp.zeros_like(sums_ref)

    def norm_back(rows):
        incoming = back_ref[rows, :]
        rows_grad, gain_terms = norm_rows_back(rows_ref[rows, :], incoming, norm_ref[0:1, :])
        rows_grad = rows_grad + grad_ref[rows, :]
        rounded = rows_grad.astype(BF16)
        grad_out[rows, :] = rows_grad
        low[rows, :] = rounded
        for k, terms in enumerate((gain_terms, incoming, rounded.astype(F32))):
            sums_ref[k : k + 1, :] += jnp.sum(terms, axis=0, keepdims=True)

    for part, copy in zip(parts, over_x):
        by_rows(half, 64, lambda rows, part=part: norm_back(pl.ds(pl.multiple_of(part.start + rows.start, 64), 64)))
        copy.start()
    own.start()
    over_core.start()
    for step in range(len(collect.stages) - 1):
        collect.finish(step)
        collect.start(step + 1)
    for copy, later in zip(over_x, onward):
        copy.wait_recv()
        later.start()
    collect.finish(len(collect.stages) - 1)
    down_out[...] = column[collect.z].astype(F32)
    collect.drain()
    own.wait()
    for copy in over_x:
        copy.wait_send()
    over_core.wait()
    for copy in onward:
        copy.wait()


def middle(back, rows, grad, norm, down_column):
    n = lax.axis_size("dp")
    count, width = rows.shape
    m, r, c = down_column.shape
    vmem = pl.BlockSpec(memory_space=pltpu.VMEM)
    return pl.pallas_call(
        functools.partial(middle_kernel, n=n),
        in_specs=[vmem, vmem, vmem, vmem, ANY],
        out_specs=[ANY, vmem, vmem, vmem],
        out_shape=[
            jax.ShapeDtypeStruct((4 * count, width), BF16),
            jax.ShapeDtypeStruct((count, width), F32),
            jax.ShapeDtypeStruct((8, width), F32),
            jax.ShapeDtypeStruct((r, c), F32),
        ],
        scratch_shapes=[
            pltpu.VMEM((count, width), BF16),
            pltpu.VMEM((m, r, c), BF16),
            pltpu.VMEM((m, r, c), BF16),
        ]
        + link_scratch(5 + m, 2),
        compiler_params=pltpu.CompilerParams(
            vmem_limit_bytes=VMEM_LIMIT, collective_id=6, has_side_effects=True
        ),
        cost_estimate=pl.CostEstimate(flops=0, bytes_accessed=100 * 2**20, transcendentals=0),
        name="middle",
    )(back, rows, grad, norm, down_column)


def tail_kernel(
    terms_ref, weights_ref, rows_ref, grad_ref, norm_ref, late_ref,
    grad_out, weights_out, late_out, *scratch, n
):
    links = Links(*scratch[-3:])
    rows_sum = RowSum(links, terms_ref, scratch[:5])
    columns, gots, slots = scratch[5:7], scratch[7:9], scratch[9:11]
    held, late_slots = scratch[11:13]
    y = links.dp % 2
    c = columns[0].shape[2]
    loads, over_y, collects = [], [], []
    for k, (column, got, slot) in enumerate(zip(columns, gots, slots)):
        part = pl.ds(k * c, c)
        loads.append(links.local(weights_ref.at[:, y, :, part], column))
        over_y.append(links.copy(weights_ref.at[:, 1 - y, :, part], got, Y))
        collects.append(Collect(links, column, slot))
    late = Everywhere(links, held, late_slots, n)
    links.greet(everywhere_ways(n))
    rows_sum.start()
    over_y[0].start()
    for load in loads:
        load.start()
    rows_sum.middle()
    for k in range(2):
        loads[k].wait()
        over_y[k].wait_recv()
        if k == 0:
            over_y[1].start()
        add_to(columns[k], gots[k])
        collects[k].start(0)
    stages = len(collects[0].stages)
    for step in range(stages):
        for k in range(2):
            collects[k].finish(step)
            if step < stages - 1:
                collects[k].start(step + 1)
    for k in range(2):
        weights_out[:, k * c : (k + 1) * c] = columns[k][collects[k].z].astype(F32)
    rows_sum.end()
    held[0] = late_ref[...]

    def norm_back(rows):
        incoming = rows_sum.total(rows)
        rows_grad, gain_terms = norm_rows_back(rows_ref[rows, :].astype(F32), incoming, norm_ref[0:1, :])
        grad_out[rows, :] = rows_grad + grad_ref[rows, :]
        held[0, 0:1, :] += jnp.sum(gain_terms, axis=0, keepdims=True)
        held[0, 1:2, :] += jnp.sum(incoming, axis=0, keepdims=True)

    by_rows(grad_out.shape[0], 64, norm_back)
    steps = len(late.copies)
    for step in range(steps):
        late.start(step)
        late.finish(step)
    late_out[...] = held[steps]
    for k in range(2):
        over_y[k].wait_send()
        collects[k].drain()


def tail(terms, weights, rows, grad, norm, late):
    n = lax.axis_size("dp")
    count, width = rows.shape
    m, _, r, c = weights.shape
    vmem = pl.BlockSpec(memory_space=pltpu.VMEM)
    part = pltpu.VMEM((m, r, c // 2), BF16)
    return pl.pallas_call(
        functools.partial(tail_kernel, n=n),
        in_specs=[ANY, ANY, vmem, vmem, vmem, vmem],
        out_specs=[vmem, vmem, vmem],
        out_shape=[
            jax.ShapeDtypeStruct((count, width), F32),
            jax.ShapeDtypeStruct((r, c), F32),
            jax.ShapeDtypeStruct(late.shape, F32),
        ],
        scratch_shapes=row_sum_scratch(count, width)
        + [part] * 6
        + everywhere_scratch(*late.shape, n)
        + link_scratch(5 + 2 * m + len(everywhere_ways(n)), 4),
        compiler_params=pltpu.CompilerParams(
            vmem_limit_bytes=VMEM_LIMIT, collective_id=7, has_side_effects=True
        ),
        cost_estimate=pl.CostEstimate(flops=0, bytes_accessed=100 * 2**20, transcendentals=0),
        name="tail",
    )(terms, weights, rows, grad, norm, late)


def start_kernel(
    rows_ref, enc_ref, self_ref, cross_ref, rows_out, enc_out, self_out, cross_out, send_sems, recv_sems, local_sems, *, n
):
    links = Links(send_sems, recv_sems, local_sems)
    member, z, y = links.tensor, links.dp // 2, links.dp % 2
    links.greet([CORE, X, Y] + z_ways(n))

    def place(ref, index, size):
        return ref.at[pl.ds(pl.multiple_of(index * size, size), size)]

    groups = [(rows_ref, rows_out, rows_ref.shape[0]), (enc_ref, enc_out, enc_ref.shape[0])]
    local, started, arrived = [], [], []
    for source, target, size in groups:
        local.append(links.local(source, place(target, member, size)))
    local.append(links.local(self_ref, self_out.at[z, y]))
    local.append(links.local(cross_ref, cross_out.at[z]))
    for copy in local:
        copy.start()

    def go(copy):
        copy.start()
        started.append(copy)
        return copy

    def got(copy):
        copy.wait_recv()
        arrived.append(copy)

    along_x = [go(links.copy(source, place(target, member, size), X)) for source, target, size in groups]
    go(links.copy(self_ref, self_out.at[z, y], Y))
    for source, target, size in groups:
        go(links.copy(source, place(target, member, size), CORE))
    self_stages = column_stages(links, self_ref, self_out.at[:, y], n)
    cross_stages = column_stages(links, cross_ref, cross_out, n)
    for self_stage in self_stages:
        for copy, _ in self_stage:
            go(copy)
        for copy, index in self_stage:
            got(copy)
            go(links.copy(self_out.at[index, y], self_out.at[index, y], Y))
        if self_stage is self_stages[0]:
            for copy, _ in cross_stages[0]:
                go(copy)
    for cross_stage, later in zip(cross_stages, cross_stages[1:]):
        for copy, _ in cross_stage:
            got(copy)
        for copy, _ in later:
            go(copy)
    for copy, (_, target, size) in zip(along_x, groups):
        got(copy)
        there = place(target, member ^ 2, size)
        go(links.copy(there, there, CORE))
    for copy in local:
        copy.wait()
    for copy in started:
        copy.wait_send()
        if not any(copy is other for other in arrived):
            copy.wait_recv()


def start_gather(rows_low, enc_low, self_shard, cross_shard):
    n = lax.axis_size("dp")
    r, c = self_shard.shape
    copies = 3 * n + 8
    return pl.pallas_call(
        functools.partial(start_kernel, n=n),
        in_specs=[ANY] * 4,
        out_specs=[ANY] * 4,
        out_shape=[
            jax.ShapeDtypeStruct((4 * rows_low.shape[0], rows_low.shape[1]), BF16),
            jax.ShapeDtypeStruct((4 * enc_low.shape[0], enc_low.shape[1]), BF16),
            jax.ShapeDtypeStruct((n // 2, 2, r, c), BF16),
            jax.ShapeDtypeStruct((n // 2,) + cross_shard.shape, BF16),
        ],
        scratch_shapes=link_scratch(copies, 4),
        compiler_params=pltpu.CompilerParams(collective_id=0, has_side_effects=True),
        cost_estimate=pl.CostEstimate(flops=0, bytes_accessed=100 * 2**20, transcendentals=0),
        name="start_gather",
    )(rows_low, enc_low, self_shard, cross_shard)


def self_forward_kernel(
    b_ref, q_ref, k_ref, vt_ref, column_ref, shard_ref,
    ot_ref, lse_ref, whole, next_column,
    m_s, l_s, acc, send_sems, recv_sems, local_sems, *, bk, heads, safe, n
):
    i = pl.program_id(0)
    last = pl.num_programs(0) - 1
    bq, width = q_ref.shape
    links = Links(send_sems, recv_sems, local_sems)
    spread = Spread(links, column_ref, whole)
    keep = links.local(shard_ref, next_column.at[links.dp // 2])
    stages = column_stages(links, shard_ref, next_column, n)

    @pl.when(i == 0)
    def _():
        links.greet([CORE, X, Y] + z_ways(n))
        spread.start()
        keep.start()
        for copy, _ in stages[0]:
            copy.start()

    @pl.when(i == last)
    def _():
        spread.middle()
        for k in range(1, len(stages)):
            for copy, _ in stages[k - 1]:
                copy.wait_recv()
            for copy, _ in stages[k]:
                copy.start()

    hd = width // heads
    m_s[...] = jnp.full_like(m_s, NEGATIVE)
    l_s[...] = jnp.zeros_like(l_s)
    acc[...] = jnp.zeros_like(acc)
    scaled = q_ref[...] * jnp.asarray(1.0 / math.sqrt(hd), BF16)
    q_heads = [head_only(scaled, h, hd) for h in range(heads)]

    def block(j, mode):
        rows = pl.ds(pl.multiple_of(j * bk, bk), bk)
        keys = k_ref[rows, :]
        m_old = m_s[...]
        l_old = l_s[...]
        scores = [dot_nt(keys, q_heads[h]) for h in range(heads)]
        if mode != "none":
            bad = self_bad(b_ref, i * bq, j * bk, bq, bk, mode == "causal")
            scores = [jnp.where(bad, NEGATIVE, s) for s in scores]
        m_out, l_out, a_out = [], [], []
        for h in range(heads):
            part = slice(h * hd, (h + 1) * hd)
            m_new = jnp.maximum(m_old[h : h + 1, :], jnp.max(scores[h], axis=0, keepdims=True))
            shrink = jnp.exp(m_old[h : h + 1, :] - m_new)
            expos = jnp.exp(scores[h] - m_new)
            l_out.append(l_old[h : h + 1, :] * shrink + jnp.sum(expos, axis=0, keepdims=True))
            m_out.append(m_new)
            a_out.append(acc[part, :] * shrink + dot_nn(vt_ref[part, rows], expos.astype(BF16)))
        m_s[...] = jnp.concatenate(m_out, 0)
        l_s[...] = jnp.concatenate(l_out, 0)
        for h in range(heads):
            acc[h * hd : (h + 1) * hd, :] = a_out[h]

    over_keys(i, bq, bk, safe, block)
    inverse = 1.0 / l_s[...]
    for h in range(heads):
        part = slice(h * hd, (h + 1) * hd)
        ot_ref[part, :] = (acc[part, :] * inverse[h : h + 1, :]).astype(BF16)
    lse_ref[...] = m_s[...] + jnp.log(l_s[...])

    @pl.when(i == last)
    def _():
        spread.end()
        keep.wait()
        for k, stage in enumerate(stages):
            for copy, _ in stage:
                copy.wait_send()
                if k == len(stages) - 1:
                    copy.wait_recv()


def self_forward(bounds, queries, keys, values_t, column, shard, heads, safe):
    n, width = queries.shape
    bq = bk = 512
    dp = lax.axis_size("dp")
    m, r, c = column.shape
    return pl.pallas_call(
        functools.partial(self_forward_kernel, bk=bk, heads=heads, safe=safe, n=dp),
        grid=(n // bq,),
        in_specs=[
            pl.BlockSpec(memory_space=pltpu.SMEM),
            pl.BlockSpec((bq, width), lambda i: (i, 0)),
            pl.BlockSpec((n, width), lambda i: (0, 0)),
            pl.BlockSpec((width, n), lambda i: (0, 0)),
            ANY,
            ANY,
        ],
        out_specs=[
            pl.BlockSpec((width, bq), lambda i: (0, i)),
            pl.BlockSpec((heads, bq), lambda i: (0, i)),
        ]
        + [ANY] * 2,
        out_shape=[
            jax.ShapeDtypeStruct((width, n), BF16),
            jax.ShapeDtypeStruct((heads, n), F32),
        ]
        + [jax.ShapeDtypeStruct((4, m, 2, r, c), BF16)]
        + [jax.ShapeDtypeStruct((m,) + shard.shape, BF16)],
        scratch_shapes=[
            pltpu.VMEM((heads, bq), F32),
            pltpu.VMEM((heads, bq), F32),
            pltpu.VMEM((width, bq), F32),
        ]
        + link_scratch(8 + m, 2),
        compiler_params=pltpu.CompilerParams(
            vmem_limit_bytes=VMEM_LIMIT, collective_id=1, has_side_effects=True
        ),
        cost_estimate=pl.CostEstimate(
            flops=12 * n * n * width, bytes_accessed=8 * n * width, transcendentals=n * n * heads // 2
        ),
        name="self_forward",
    )(bounds, queries, keys, values_t, column, shard)


def self_backward_kernel(
    b_ref, q_ref, k_ref, v_ref, kt_ref, do_ref, lse_ref, dl_ref, up_ref, cross_ref, enc_ref, early_ref,
    dqt_ref, dk_ref, dv_ref, up_out, cross_out, enc_out, early_out, dka, dva, dqa, *scratch, bk, heads, safe, n
):
    i = pl.program_id(0)
    last = pl.num_programs(0) - 1
    links = Links(*scratch[-3:])
    cross = Gather(links, cross_ref.at[0], cross_ref.at[1], scratch[:7])
    cross_z = Collect(links, cross.column, scratch[7])
    up_column = scratch[8]
    up_z = Collect(links, up_column, scratch[9])
    load = links.local(up_ref, up_column)
    enc = RowSum(links, enc_ref, scratch[10:15])
    held = scratch[15]
    early = Everywhere(links, held, scratch[16], n)
    stages = len(up_z.stages)
    steps = len(early.copies)

    @pl.when(i == 0)
    def _():
        links.greet(everywhere_ways(n))
        cross.start()
        enc.start()
        load.start()
        held[0] = early_ref[...]
        early.start(0)
        load.wait()
        up_z.start(0)

    @pl.when(i == 1)
    def _():
        enc.middle()
        early.finish(0)
        early.start(1)

    @pl.when(i == 2)
    def _():
        cross.middle()
        early.finish(1)
        early.start(2)

    @pl.when(i == 3)
    def _():
        for step in range(stages - 1):
            up_z.finish(step)
            up_z.start(step + 1)
        early.finish(2)
        early.start(3)

    @pl.when(i == last)
    def _():
        cross.end()
        cross_z.start(0)
        for step in range(3, steps - 1):
            early.finish(step)
            early.start(step + 1)

    bq, width = q_ref.shape
    hd = width // heads
    scale = 1.0 / math.sqrt(hd)

    @pl.when(i == 0)
    def _():
        dka[...] = jnp.zeros_like(dka)
        dva[...] = jnp.zeros_like(dva)

    scaled = q_ref[...] * jnp.asarray(scale, BF16)
    grads = do_ref[...]
    q_heads = [head_only(scaled, h, hd) for h in range(heads)]
    d_heads = [head_only(grads, h, hd) for h in range(heads)]
    lse = lse_ref[...]
    inner = dl_ref[...]
    dqa[...] = jnp.zeros_like(dqa)

    def block(j, mode):
        rows = pl.ds(pl.multiple_of(j * bk, bk), bk)
        keys = k_ref[rows, :]
        values = v_ref[rows, :]
        scores = [dot_nt(keys, q_heads[h]) for h in range(heads)]
        dprobs = [dot_nt(values, d_heads[h]) for h in range(heads)]
        if mode != "none":
            bad = self_bad(b_ref, i * bq, j * bk, bq, bk, mode == "causal")
            scores = [jnp.where(bad, NEGATIVE, s) for s in scores]
        dv_sum, dk_sum = None, None
        for h in range(heads):
            part = slice(h * hd, (h + 1) * hd)
            probs = jnp.exp(scores[h] - lse[h : h + 1, :])
            ds = (probs * (dprobs[h] - inner[h : h + 1, :])).astype(BF16)
            dv_h = dot_nn(probs.astype(BF16), d_heads[h])
            dk_h = dot_nn(ds, q_heads[h])
            dv_sum = dv_h if dv_sum is None else dv_sum + dv_h
            dk_sum = dk_h if dk_sum is None else dk_sum + dk_h
            dqa[part, :] += dot_nn(kt_ref[part, rows], ds)
        dva[rows, :] += dv_sum
        dka[rows, :] += dk_sum

    over_keys(i, bq, bk, safe, block)
    dqt_ref[...] = (dqa[...] * scale).astype(BF16)

    @pl.when(i == pl.num_programs(0) - 1)
    def _():
        dk_ref[...] = dka[...].astype(BF16)
        dv_ref[...] = dva[...].astype(BF16)
        up_z.finish(stages - 1)
        up_out[...] = up_column[up_z.z].astype(F32)
        for step in range(stages):
            cross_z.finish(step)
            if step < stages - 1:
                cross_z.start(step + 1)
        cross_out[...] = cross.column[cross_z.z].astype(F32)
        enc.end()

        def store(rows):
            enc_out[rows, :] = enc.total(rows)

        by_rows(enc_out.shape[0], 64, store)
        early.finish(steps - 1)
        early_out[...] = held[steps]
        up_z.drain()
        cross_z.drain()


def self_backward(
    bounds, queries, keys, values, keys_t, grads, lse, inner, up_column, cross_sum, enc_terms, early, heads, safe
):
    n, width = queries.shape
    dp = lax.axis_size("dp")
    m, r, c = up_column.shape
    cross_c = cross_sum.shape[4]
    enc_shape = (enc_terms.shape[0] // 4, enc_terms.shape[1])
    bq = bk = 512
    whole = pl.BlockSpec((n, width), lambda i: (0, 0))
    some = pl.BlockSpec((bq, width), lambda i: (i, 0))
    per_row = pl.BlockSpec((heads, bq), lambda i: (0, i))
    return pl.pallas_call(
        functools.partial(self_backward_kernel, bk=bk, heads=heads, safe=safe, n=dp),
        grid=(n // bq,),
        in_specs=[
            pl.BlockSpec(memory_space=pltpu.SMEM),
            some,
            whole,
            whole,
            pl.BlockSpec((width, n), lambda i: (0, 0)),
            some,
            per_row,
            per_row,
        ]
        + [ANY] * 3
        + [const(early.shape)],
        out_specs=[pl.BlockSpec((width, bq), lambda i: (0, i)), whole, whole]
        + [const((r, c)), const((r, cross_c)), const(enc_shape), const(early.shape)],
        out_shape=[
            jax.ShapeDtypeStruct((width, n), BF16),
            jax.ShapeDtypeStruct((n, width), BF16),
            jax.ShapeDtypeStruct((n, width), BF16),
            jax.ShapeDtypeStruct((r, c), F32),
            jax.ShapeDtypeStruct((r, cross_c), F32),
            jax.ShapeDtypeStruct(enc_shape, F32),
            jax.ShapeDtypeStruct(early.shape, F32),
        ],
        scratch_shapes=[
            pltpu.VMEM((n, width), F32),
            pltpu.VMEM((n, width), F32),
            pltpu.VMEM((width, bq), F32),
        ]
        + gather_scratch(m, r, cross_c)
        + [pltpu.VMEM((m, r, cross_c), BF16)]
        + [pltpu.VMEM((m, r, c), BF16)] * 2
        + row_sum_scratch(*enc_shape)
        + everywhere_scratch(*early.shape, dp)
        + link_scratch(7 + 2 * m + len(everywhere_ways(dp)), 6),
        compiler_params=pltpu.CompilerParams(
            vmem_limit_bytes=VMEM_LIMIT, collective_id=5, has_side_effects=True
        ),
        cost_estimate=pl.CostEstimate(
            flops=24 * n * n * width, bytes_accessed=16 * n * width, transcendentals=n * n * heads // 2
        ),
        name="self_backward",
    )(bounds, queries, keys, values, keys_t, grads, lse, inner, up_column, cross_sum, enc_terms, early)


def const(shape):
    return pl.BlockSpec(shape, lambda *_: (0,) * len(shape), pipeline_mode=pl.Buffered(1))


def normalized(rows):
    center = rows - jnp.mean(rows, axis=-1, keepdims=True)
    scale = lax.rsqrt(jnp.mean(center * center, axis=-1, keepdims=True) + EPSILON)
    return center * scale, scale


def norm_rows_back(rows, incoming, gain):
    xhat, scale = normalized(rows)
    e = incoming * gain
    inner = jnp.mean(e * xhat, axis=-1, keepdims=True)
    return scale * (e - jnp.mean(e, axis=-1, keepdims=True) - xhat * inner), incoming * xhat


def by_rows(count, step, body):
    def one(k, c):
        body(pl.ds(pl.multiple_of(k * step, step), step))
        return c

    lax.fori_loop(0, count // step, one, 0)


def cross_forward_kernel(
    ok_ref, x_ref, enc_ref, w_ref, bq_ref, bv_ref, rows_ref, shift_ref, norm_ref, column_ref,
    q_out, k_out, v_out, ot_ref, lse_ref, after_ref, third_ref, whole, send_sems, recv_sems, local_sems, *, heads
):
    i = pl.program_id(0)
    last = pl.num_programs(0) - 1
    links = Links(send_sems, recv_sems, local_sems)
    spread = Spread(links, column_ref, whole)

    @pl.when(i == 0)
    def _():
        links.greet([CORE, X, Y])
        spread.start()
        after_ref[...] = rows_ref[...] + shift_ref[...]

    width = q_out.shape[2]
    hd = width // heads
    query = (dot_nn(x_ref[...], w_ref[0, :, :width]) + bq_ref[0]).astype(BF16)
    key_value = dot_nn(enc_ref[...], w_ref[0, :, width : 3 * width])
    keys = key_value[:, :width].astype(BF16)
    values = (key_value[:, width:] + bv_ref[0]).astype(BF16)
    q_out[0] = query
    k_out[0] = keys
    v_out[0] = values
    values_t = values.T
    scaled = query * jnp.asarray(1.0 / math.sqrt(hd), BF16)
    ok = ok_ref[...] > 0.0
    scores = [dot_nt(keys, head_only(scaled, h, hd)) for h in range(heads)]
    mixed = []
    for h in range(heads):
        part = slice(h * hd, (h + 1) * hd)
        s = jnp.where(ok, scores[h], NEGATIVE)
        largest = jnp.max(s, axis=0, keepdims=True)
        expos = jnp.exp(s - largest)
        total = jnp.sum(expos, axis=0, keepdims=True)
        mixed.append((dot_nn(values_t[part, :], expos.astype(BF16)) * (1.0 / total)).astype(BF16))
        ot_ref[0, part, :] = mixed[h]
        lse_ref[0, h : h + 1, :] = largest + jnp.log(total)
    after_ref[...] += dot_nt(jnp.concatenate(mixed, 0).T, w_ref[0, :, 3 * width :])

    @pl.when(i == last)
    def _():
        spread.middle()

        def norm(rows):
            xhat, _ = normalized(after_ref[rows, :])
            third_ref[rows, :] = (xhat * norm_ref[0:1, :] + norm_ref[1:2, :]).astype(BF16)

        by_rows(after_ref.shape[0], 128, norm)
        spread.end()


def cross_forward(ok, x, encoder, weights, q_shift, v_shift, rows, shift, norm, column, heads):
    count, model = x.shape
    n = encoder.shape[0]
    parts, _, columns = weights.shape
    width = columns // 4
    m, r, c = column.shape

    def by_part(*shape):
        return pl.BlockSpec((1,) + shape, lambda i: (i,) + (0,) * len(shape))

    return pl.pallas_call(
        functools.partial(cross_forward_kernel, heads=heads),
        grid=(parts,),
        in_specs=[
            const((n, 1)),
            const((count, model)),
            const((n, model)),
            by_part(model, columns),
            by_part(1, width),
            by_part(1, width),
            const((count, model)),
            const((1, model)),
            const((2, model)),
            ANY,
        ],
        out_specs=[
            by_part(count, width),
            by_part(n, width),
            by_part(n, width),
            by_part(width, count),
            by_part(heads, count),
            const((count, model)),
            const((count, model)),
            ANY,
        ],
        out_shape=[
            jax.ShapeDtypeStruct((parts, count, width), BF16),
            jax.ShapeDtypeStruct((parts, n, width), BF16),
            jax.ShapeDtypeStruct((parts, n, width), BF16),
            jax.ShapeDtypeStruct((parts, width, count), BF16),
            jax.ShapeDtypeStruct((parts, heads, count), F32),
            jax.ShapeDtypeStruct((count, model), F32),
            jax.ShapeDtypeStruct((count, model), BF16),
            jax.ShapeDtypeStruct((4, m, 2, r, c), BF16),
        ],
        scratch_shapes=link_scratch(8, 1),
        compiler_params=pltpu.CompilerParams(
            vmem_limit_bytes=VMEM_LIMIT, collective_id=2, has_side_effects=True
        ),
        cost_estimate=pl.CostEstimate(
            flops=24 * parts * count * n * width,
            bytes_accessed=8 * parts * n * width,
            transcendentals=parts * count * n * heads,
        ),
        name="cross_forward",
    )(ok, x, encoder, weights, q_shift, v_shift, rows, shift, norm, column)


def feed_forward_kernel(
    x_ref, dy_ref, up_ref, down_ref, b_ref, after_ref, shift_ref, norm_ref,
    out_ref, rows_out, low_out, sums_ref, gup_ref, gdown_ref, bias_ref,
    xt_ref, dyt_ref, back_ref, give, got, send_sems, recv_sems, local_sems, *, chunks
):
    s = pl.program_id(0)
    links = Links(send_sems, recv_sems, local_sems)
    turn = s // chunks
    chunk = s % chunks
    pair = turn // 2
    slot = pair * chunks + chunk
    theirs = turn % 2 == 0
    to_core = pltpu.make_async_remote_copy(
        src_ref=give.at[chunk],
        dst_ref=got.at[slot],
        send_sem=send_sems.at[slot],
        recv_sem=recv_sems.at[slot],
        device_id=links.partner(CORE),
        device_id_type=pl.DeviceIdType.MESH,
    )

    @pl.when(s == 0)
    def _():
        links.greet([CORE])
        out_ref[...] = after_ref[...] + shift_ref[...]
        back_ref[...] = jnp.zeros_like(back_ref)
        xt_ref[...] = x_ref[...].T
        dyt_ref[...] = dy_ref[...].T
        sums_ref[...] = jnp.zeros_like(sums_ref)

    pre_act = dot_nn(x_ref[...], up_ref[0]) + b_ref[0]
    hidden_grad = dot_nn(dy_ref[...], down_ref[0])
    normal_cdf = 0.5 * (1.0 + lax.erf(pre_act * (1.0 / math.sqrt(2.0))))
    density = jnp.exp(-0.5 * pre_act * pre_act) * (1.0 / math.sqrt(2.0 * math.pi))
    hidden = (pre_act * normal_cdf).astype(BF16)
    pre_grad = (hidden_grad * (normal_cdf + pre_act * density)).astype(BF16)
    bias_ref[0] = jnp.sum(pre_grad.astype(F32), axis=0, keepdims=True)

    @pl.when(turn % 2 == 1)
    def _():
        to_core.wait_send()

    give[chunk, 0] = dot_nn(xt_ref[...], pre_grad).astype(BF16)
    give[chunk, 1] = dot_nn(dyt_ref[...], hidden).astype(BF16)
    out_ref[...] += dot_nt(hidden, down_ref[0])
    back_ref[...] += dot_nt(pre_grad, up_ref[0])

    @pl.when(theirs)
    def _():
        to_core.start()

    @pl.when(jnp.logical_not(theirs))
    def _():
        to_core.wait_recv()
        gup_ref[0] = (give[chunk, 0].astype(F32) + got[slot, 0].astype(F32)).astype(BF16)
        gdown_ref[0] = (give[chunk, 1].astype(F32) + got[slot, 1].astype(F32)).astype(BF16)

    @pl.when(s == pl.num_programs(0) - 1)
    def _():
        def norm_back(rows):
            third = back_ref[rows, :]
            upstream = dy_ref[rows, :].astype(F32)
            rows_grad, gain_terms = norm_rows_back(after_ref[rows, :], third, norm_ref[0:1, :])
            rows_grad = rows_grad + upstream
            low = rows_grad.astype(BF16)
            rows_out[rows, :] = rows_grad
            low_out[rows, :] = low
            for k, terms in enumerate((gain_terms, third, low.astype(F32), upstream)):
                sums_ref[k : k + 1, :] += jnp.sum(terms, axis=0, keepdims=True)

        by_rows(x_ref.shape[0], 128, norm_back)


def feed_forward(x, dy, weights, bias, after, shift, norm):
    rows, width = x.shape
    hidden = weights.shape[2] // 2
    size = min(512, hidden)
    chunks = hidden // size

    def block(s):
        return (s // chunks) ^ 1

    def placed(s):
        turn = s // chunks
        return (turn // 2, 0, (s % chunks) * (turn % 2))

    rows_spec = const((rows, width))
    grad_spec = pl.BlockSpec((1, width, size), placed)
    bias_spec = pl.BlockSpec((1, 1, size), lambda s: (block(s), 0, s % chunks))
    return pl.pallas_call(
        functools.partial(feed_forward_kernel, chunks=chunks),
        grid=(4 * chunks,),
        in_specs=[
            rows_spec,
            rows_spec,
            pl.BlockSpec((1, width, size), lambda s: (block(s), 0, s % chunks)),
            pl.BlockSpec((1, width, size), lambda s: (block(s), 0, chunks + s % chunks)),
            bias_spec,
            rows_spec,
            const((1, width)),
            const((2, width)),
        ],
        out_specs=[rows_spec, rows_spec, rows_spec, const((8, width)), grad_spec, grad_spec, bias_spec],
        out_shape=[
            jax.ShapeDtypeStruct((rows, width), F32),
            jax.ShapeDtypeStruct((rows, width), F32),
            jax.ShapeDtypeStruct((rows, width), BF16),
            jax.ShapeDtypeStruct((8, width), F32),
            jax.ShapeDtypeStruct((2, width, hidden), BF16),
            jax.ShapeDtypeStruct((2, width, hidden), BF16),
            jax.ShapeDtypeStruct((4, 1, hidden), F32),
        ],
        scratch_shapes=[
            pltpu.VMEM((width, rows), BF16),
            pltpu.VMEM((width, rows), BF16),
            pltpu.VMEM((rows, width), F32),
            pltpu.VMEM((chunks, 2, width, size), BF16),
            pltpu.VMEM((2 * chunks, 2, width, size), BF16),
        ]
        + link_scratch(2 * chunks, 1),
        compiler_params=pltpu.CompilerParams(
            vmem_limit_bytes=VMEM_LIMIT, collective_id=3, has_side_effects=True
        ),
        cost_estimate=pl.CostEstimate(
            flops=48 * rows * width * hidden, bytes_accessed=40 * 2**20, transcendentals=8 * rows * hidden
        ),
        name="feed_forward",
    )(x, dy, weights, weights, bias, after, shift, norm)


def cross_backward_kernel(
    ok_ref, low_ref, x_ref, enc_ref, w_ref, q_ref, k_ref, v_ref, mt_ref, lse_ref, up_ref, down_ref,
    back_ref, enc_out, grad_ref, bq_ref, bv_ref, up_out, down_out,
    low_t, x_t, enc_t, enc_acc, give, got, *scratch, heads, bk
):
    i = pl.program_id(0)
    last = pl.num_programs(0) - 1
    links = Links(*scratch[14:])
    sums = [
        Gather(links, ref.at[0], ref.at[1], scratch[7 * k : 7 * k + 7]) for k, ref in enumerate((up_ref, down_ref))
    ]
    leave = [links.local(g.column, out) for g, out in zip(sums, (up_out, down_out))]
    pair = i // 2
    to_core = pltpu.make_async_remote_copy(
        src_ref=give,
        dst_ref=got.at[pair],
        send_sem=links.send_sems.at[links.used + pair],
        recv_sem=links.recv_sems.at[links.used + pair],
        device_id=links.partner(CORE),
        device_id_type=pl.DeviceIdType.MESH,
    )

    @pl.when(i == 0)
    def _():
        links.greet([CORE, X, Y])
        for g in sums:
            g.start()
        low_t[...] = low_ref[...].T
        x_t[...] = x_ref[...].T
        enc_t[...] = enc_ref[...].T
        back_ref[...] = jnp.zeros_like(back_ref)
        enc_acc[...] = jnp.zeros_like(enc_acc)

    @pl.when(i == 1)
    def _():
        for g in sums:
            g.middle()

    rows, width = q_ref.shape[1:]
    n = k_ref.shape[1]
    hd = width // heads
    scale = 1.0 / math.sqrt(hd)
    w_query, w_keyval, w_out = w_ref.at[0, :, :width], w_ref.at[0, :, width : 3 * width], w_ref.at[0, :, 3 * width :]
    grads = dot_nn(low_ref[...], w_out[...]).astype(BF16)
    mixed_t = mt_ref[0]
    products = grads.T.astype(F32) * mixed_t.astype(F32)
    inner = [jnp.sum(products[h * hd : (h + 1) * hd, :], axis=0, keepdims=True) for h in range(heads)]
    scaled = q_ref[0] * jnp.asarray(scale, BF16)
    q_heads = [head_only(scaled, h, hd) for h in range(heads)]
    d_heads = [head_only(grads, h, hd) for h in range(heads)]
    lse = lse_ref[0]
    keys_t = k_ref[0].T
    dq = [None] * heads
    dkv = []
    for j in range(n // bk):
        span = slice(j * bk, (j + 1) * bk)
        keys = k_ref[0, span, :]
        values = v_ref[0, span, :]
        ok = ok_ref[span, :] > 0.0
        scores = [dot_nt(keys, q_heads[h]) for h in range(heads)]
        dprobs = [dot_nt(values, d_heads[h]) for h in range(heads)]
        dv_sum, dk_sum = None, None
        for h in range(heads):
            part = slice(h * hd, (h + 1) * hd)
            probs = jnp.exp(jnp.where(ok, scores[h], NEGATIVE) - lse[h : h + 1, :])
            ds = (probs * (dprobs[h] - inner[h])).astype(BF16)
            dv_h = dot_nn(probs.astype(BF16), d_heads[h])
            dk_h = dot_nn(ds, q_heads[h])
            dv_sum = dv_h if dv_sum is None else dv_sum + dv_h
            dk_sum = dk_h if dk_sum is None else dk_sum + dk_h
            dq_h = dot_nn(keys_t[part, span], ds)
            dq[h] = dq_h if dq[h] is None else dq[h] + dq_h
        block = jnp.concatenate([dk_sum.astype(BF16), dv_sum.astype(BF16)], 1)
        enc_acc[span, :] += dot_nt(block, w_keyval[...])
        dkv.append(block)
    dq = (jnp.concatenate(dq, 0) * scale).astype(BF16).T
    dkv = jnp.concatenate(dkv, 0)
    bq_ref[0] = jnp.sum(dq.astype(F32), axis=0, keepdims=True)
    bv_ref[0] = jnp.sum(dkv[:, width:].astype(F32), axis=0, keepdims=True)
    back_ref[...] += dot_nt(dq, w_query[...])

    @pl.when(i % 2 == 1)
    def _():
        to_core.wait_send()

    give[:, :width] = dot_nn(x_t[...], dq).astype(BF16)
    give[:, width : 3 * width] = dot_nn(enc_t[...], dkv).astype(BF16)
    give[:, 3 * width :] = dot_nn(low_t[...], mixed_t.T).astype(BF16)

    @pl.when(i % 2 == 0)
    def _():
        to_core.start()

    @pl.when(i % 2 == 1)
    def _():
        to_core.wait_recv()
        grad_ref[0] = (give[...].astype(F32) + got[pair].astype(F32)).astype(BF16)

    @pl.when(i == last)
    def _():
        enc_out[...] = enc_acc[...].astype(BF16)
        for g, copy in zip(sums, leave):
            g.end()
            copy.start()
        for copy in leave:
            copy.wait()


def cross_backward(ok, low, x, encoder, weights, queries, keys, values, mixed_t, lse, up_sum, down_sum, heads):
    count, model = x.shape
    n = encoder.shape[0]
    parts, _, columns = weights.shape
    width = columns // 4
    _, m, _, r, c = up_sum.shape

    def by_part(*shape):
        return pl.BlockSpec((1,) + shape, lambda i: (i ^ 1,) + (0,) * len(shape))

    return pl.pallas_call(
        functools.partial(cross_backward_kernel, heads=heads, bk=256),
        grid=(parts,),
        in_specs=[
            const((n, 1)),
            const((count, model)),
            const((count, model)),
            const((n, model)),
            by_part(model, columns),
            by_part(count, width),
            by_part(n, width),
            by_part(n, width),
            by_part(width, count),
            by_part(heads, count),
            ANY,
            ANY,
        ],
        out_specs=[
            const((count, model)),
            const((n, model)),
            pl.BlockSpec((1, model, columns), lambda i: (i // 2, 0, 0), pipeline_mode=pl.Buffered(1)),
            by_part(1, width),
            by_part(1, width),
            ANY,
            ANY,
        ],
        out_shape=[
            jax.ShapeDtypeStruct((count, model), F32),
            jax.ShapeDtypeStruct((n, model), BF16),
            jax.ShapeDtypeStruct((2, model, columns), BF16),
            jax.ShapeDtypeStruct((parts, 1, width), F32),
            jax.ShapeDtypeStruct((parts, 1, width), F32),
            jax.ShapeDtypeStruct((m, r, c), BF16),
            jax.ShapeDtypeStruct((m, r, c), BF16),
        ],
        scratch_shapes=[
            pltpu.VMEM((model, count), BF16),
            pltpu.VMEM((model, count), BF16),
            pltpu.VMEM((model, n), BF16),
            pltpu.VMEM((n, model), F32),
            pltpu.VMEM((model, columns), BF16),
            pltpu.VMEM((2, model, columns), BF16),
        ]
        + gather_scratch(m, r, c) * 2
        + link_scratch(10, 8),
        compiler_params=pltpu.CompilerParams(
            vmem_limit_bytes=60 * 2**20, collective_id=4, has_side_effects=True
        ),
        cost_estimate=pl.CostEstimate(
            flops=48 * parts * count * n * width,
            bytes_accessed=16 * parts * n * width,
            transcendentals=parts * count * n * heads,
        ),
        name="cross_backward",
    )(ok, low, x, encoder, weights, queries, keys, values, mixed_t, lse, up_sum, down_sum)


def swap(value, axis, distance):
    size = lax.axis_size(axis)
    return lax.ppermute(value, axis, [(i, i ^ distance) for i in range(size)])


def dp_distances():
    n = lax.axis_size("dp")
    found = []
    while n > 1:
        n //= 2
        found.append(n)
    return found


def add_low(a, b):
    return (a.astype(F32) + b.astype(F32)).astype(BF16)


def narrow(rows_low):
    member = lax.axis_index("tensor")
    count = rows_low.shape[0] // 4
    parts = [
        lax.dynamic_slice_in_dim(rows_low, (member ^ distance) * count, count, 0)
        for distance in range(4)
    ]
    far = add_low(parts[2], swap(parts[3], "tensor", 1))
    got = swap(far, "tensor", 2)
    near = parts[0].astype(F32) + swap(parts[1], "tensor", 1).astype(F32)
    return near + got.astype(F32)


def on_device(
    block_in,
    encoder_out,
    out_grad,
    bounds,
    enc_lengths,
    norm_params,
    w_qkv,
    w_self_out,
    w_cross_q,
    w_cross_kv,
    w_cross_out,
    w_up,
    w_down,
    biases,
    up_bias,
):
    member = lax.axis_index("tensor")
    groups_count = lax.axis_size("dp")
    groups = float(groups_count)
    width = w_cross_q.shape[1]
    hidden_width = w_up.shape[1]
    heads = H // 4
    own_rows, model_width = block_in.shape
    enc_rows = encoder_out.shape[0]
    w_rows = w_cross_q.shape[0]

    def block_of(vector, size, distance):
        return lax.dynamic_slice_in_dim(vector, (member ^ distance) * size, size)

    def blocks_placed(parts):
        size = parts[0].shape[0]
        out = jnp.zeros((4 * size,), F32)
        for distance, part in enumerate(parts):
            out = lax.dynamic_update_slice_in_dim(out, part, (member ^ distance) * size, 0)
        return out

    start_rows = block_in.astype(F32)
    first_in, enc_all, self_w, cross_column = start_gather(
        layer_norm(start_rows, norm_params[0, 0], norm_params[0, 1]).astype(BF16),
        encoder_out,
        jnp.concatenate([w_qkv.reshape(w_rows, 3 * width), w_self_out.T], axis=1),
        jnp.concatenate([w_cross_q, w_cross_kv.reshape(w_rows, 2 * width), w_cross_out.T], axis=1),
    )
    self_w = self_w.reshape(model_width, 4 * width)

    projected = dot_nn(first_in, self_w[:, : 3 * width])
    queries = (projected[:, :width] + block_of(biases[0], width, 0)).astype(BF16)
    key_rows = projected[:, width : 2 * width].astype(BF16)
    value_rows = (projected[:, 2 * width :] + block_of(biases[1], width, 0)).astype(BF16)
    self_safe = 1024
    self_mixed_t, self_lse, cross_w, ffn_column = self_forward(
        bounds,
        queries,
        key_rows,
        value_rows.T,
        cross_column,
        jnp.concatenate([w_up, w_down.T], axis=1),
        heads,
        self_safe,
    )
    cross_w = cross_w.reshape(4, model_width, 4 * width)
    self_out_w = self_w[:, 3 * width :]
    after_self = (
        start_rows
        + narrow(lax.dot_general(self_mixed_t, self_out_w, (((0,), (1,)), ((), ())), preferred_element_type=F32).astype(BF16))
        + biases[2]
    )

    ok = (jnp.arange(4 * enc_rows, dtype=jnp.int32) < enc_lengths[0]).astype(F32)[:, None]
    second_in = layer_norm(after_self, norm_params[1, 0], norm_params[1, 1]).astype(BF16)

    def all_blocks(vector, size):
        return jnp.stack([block_of(vector, size, d) for d in range(4)])[:, None]

    cross_q, cross_k, cross_v, cross_mixed_t, cross_lse, after_cross, third_in, ffn_w = cross_forward(
        ok,
        second_in,
        enc_all,
        cross_w,
        all_blocks(biases[3], width),
        all_blocks(biases[4], width),
        after_self,
        biases[5:6],
        norm_params[2],
        ffn_column,
        heads,
    )

    output, cross_rows_grad, cross_low, ffn_sums, up_sum, down_sum, bias_up_parts = feed_forward(
        third_in,
        out_grad,
        ffn_w.reshape(4, model_width, 2 * hidden_width),
        all_blocks(up_bias, hidden_width),
        after_cross,
        biases[6:7],
        norm_params[2],
    )

    by_shard = (2, groups_count // 2, 2, w_rows, hidden_width)
    second_grad, enc_terms, cross_sum, bias_cq_parts, bias_cv_parts, up_column, down_column = cross_backward(
        ok,
        cross_low,
        second_in,
        enc_all,
        cross_w,
        cross_q,
        cross_k,
        cross_v,
        cross_mixed_t,
        cross_lse,
        up_sum.reshape(by_shard),
        down_sum.reshape(by_shard),
        heads,
    )
    self_wide, self_rows_grad, self_sums, summed_down = middle(
        second_grad, after_self, cross_rows_grad, norm_params[1], down_column
    )
    bias_cq_grad = blocks_placed([bias_cq_parts[d, 0] for d in range(4)])
    bias_cv_grad = blocks_placed([bias_cv_parts[d, 0] for d in range(4)])
    bias_up_grad = blocks_placed([bias_up_parts[d, 0] for d in range(4)])

    early = jnp.concatenate(
        [
            self_sums[:3],
            ffn_sums[:4],
            jnp.stack([bias_cq_grad, bias_cv_grad]),
            bias_up_grad.reshape(-1, model_width),
        ]
    )
    early = jnp.pad(early, ((0, -early.shape[0] % 8), (0, 0)))

    self_mixed_grad = dot_nn(self_wide, self_out_w).astype(BF16)
    self_inner = jnp.sum(
        self_mixed_t.reshape(heads, width // heads, 4 * own_rows).astype(F32)
        * self_mixed_grad.T.reshape(heads, width // heads, 4 * own_rows).astype(F32),
        axis=1,
    )
    self_dq_t, self_dk, self_dv, summed_up, summed_cross, encoder_grad, early = self_backward(
        bounds,
        queries,
        key_rows,
        value_rows,
        key_rows.T,
        self_mixed_grad,
        self_lse,
        self_inner,
        up_column,
        cross_sum.reshape(2, groups_count // 2, 2, w_rows, 4 * width),
        enc_terms,
        early,
        heads,
        self_safe,
    )
    grad_so_t = lax.dot_general(
        self_wide, self_mixed_t, (((0,), (1,)), ((), ())), preferred_element_type=F32
    ).astype(BF16)
    qkv_grad = jnp.concatenate([self_dq_t.T, self_dk, self_dv], axis=1)
    first_terms = dot_nt(qkv_grad, self_w[:, : 3 * width]).astype(BF16)
    self_grads = jnp.concatenate([dot_tn(first_in, qkv_grad).astype(BF16), grad_so_t], axis=1)
    column_sums = jnp.sum(qkv_grad.astype(F32), axis=0)

    def only_own(part):
        out = jnp.zeros((model_width,), F32)
        return lax.dynamic_update_slice_in_dim(out, part, member * width, 0)

    late = jnp.zeros((8, model_width), F32)
    late = late.at[2].set(only_own(column_sums[:width])).at[3].set(only_own(column_sums[2 * width :]))
    input_grad, summed_self, late = tail(
        first_terms,
        self_grads.reshape(groups_count // 2, 2, w_rows, 4 * width),
        block_in,
        self_rows_grad,
        norm_params[0],
        late,
    )
    norm_total = jnp.stack([late[0], late[1], early[0], early[1], early[3], early[4]]).reshape(
        norm_params.shape
    )
    bias_total = jnp.stack([late[2], late[3], early[2], early[7], early[8], early[5], early[6]])
    up_total = early[9 : 9 + up_bias.shape[0] // model_width].reshape(-1)
    scale = 1.0 / groups
    return (
        output,
        input_grad,
        encoder_grad,
        norm_total * scale,
        summed_self[:, : 3 * width].reshape(w_qkv.shape) * scale,
        summed_self[:, 3 * width :].T * scale,
        summed_cross[:, :width] * scale,
        summed_cross[:, width : 3 * width].reshape(w_cross_kv.shape) * scale,
        summed_cross[:, 3 * width :].T * scale,
        summed_up * scale,
        summed_down.T * scale,
        bias_total * scale,
        up_total * scale,
    )


def solution(mesh):
    rows = P(("dp", "tensor"), None)
    placed = (
        rows,
        rows,
        rows,
        P("dp", None),
        P("dp"),
        P(),
        P("dp", None, "tensor"),
        P("tensor", "dp"),
        P("dp", "tensor"),
        P("dp", None, "tensor"),
        P("tensor", "dp"),
        P("dp", "tensor"),
        P("tensor", "dp"),
        P(),
        P(),
    )
    return jax.shard_map(
        on_device,
        mesh=mesh,
        in_specs=placed,
        out_specs=(
            rows,
            rows,
            rows,
            P(),
            P("dp", None, "tensor"),
            P("tensor", "dp"),
            P("dp", "tensor"),
            P("dp", None, "tensor"),
            P("tensor", "dp"),
            P("dp", "tensor"),
            P("tensor", "dp"),
            P(),
            P(),
        ),
        check_vma=False,
    )
```

```python
import functools
import math

import jax
import jax.numpy as jnp
from jax import lax
from jax.experimental import pallas as pl
from jax.experimental.pallas import tpu as pltpu
from jax.sharding import PartitionSpec as P

H = 16
EPSILON = 1e-05
NEGATIVE = -1e30
F32 = jnp.float32
BF16 = jnp.bfloat16
VMEM_LIMIT = 56 * 2**20


def dot_nt(a, b):
    return lax.dot_general(a, b, (((1,), (1,)), ((), ())), preferred_element_type=F32)


def dot_nn(a, b):
    return lax.dot_general(a, b, (((1,), (0,)), ((), ())), preferred_element_type=F32)


def dot_tn(a, b):
    return lax.dot_general(a, b, (((0,), (0,)), ((), ())), preferred_element_type=F32)


def layer_norm(inputs, gain_row, shift_row):
    center = inputs - jnp.mean(inputs, axis=-1, keepdims=True)
    spread = jnp.mean(center * center, axis=-1, keepdims=True)
    return center * lax.rsqrt(spread + EPSILON) * gain_row + shift_row


def gelu_slope(values_in):
    normal_cdf = 0.5 * (1.0 + lax.erf(values_in * (1.0 / math.sqrt(2.0))))
    density = jnp.exp(-0.5 * values_in * values_in) * (1.0 / math.sqrt(2.0 * math.pi))
    return normal_cdf + values_in * density


def head_only(x, h, size):
    lane = lax.broadcasted_iota(jnp.int32, x.shape, 1)
    return jnp.where((lane >= h * size) & (lane < (h + 1) * size), x, jnp.zeros_like(x))


def self_bad(b_ref, q_start, k_start, bq, bk, causal):
    qi = q_start + lax.broadcasted_iota(jnp.int32, (1, bq), 1)
    kj = k_start + lax.broadcasted_iota(jnp.int32, (bk, 1), 0)
    bad = (qi >= b_ref[0, 1]) & ((kj >= b_ref[0, 0]) & (kj < b_ref[0, 1]))
    if causal:
        bad = bad | (kj > qi)
    return bad


def over_keys(i, bq, bk, safe, block, between=()):
    diagonal = i * (bq // bk)

    def visit(j, c):
        for at_i, at_j, action in between:
            pl.when((i == at_i) & (j == at_j))(action)

        @pl.when(j < safe // bk)
        def _():
            block(j, "none")

        @pl.when(j >= safe // bk)
        def _():
            block(j, "segment")

        return c

    lax.fori_loop(0, diagonal, visit, 0)
    for step in range(bq // bk):
        block(diagonal + step, "causal")


CORE = ("tensor", 1)
X = ("tensor", 2)
Y = ("dp", 1)
ANY = pl.BlockSpec(memory_space=pl.ANY)


class Links:
    def __init__(self, send_sems, recv_sems, local_sems):
        self.dp = lax.axis_index("dp")
        self.tensor = lax.axis_index("tensor")
        self.send_sems, self.recv_sems, self.local_sems = send_sems, recv_sems, local_sems
        self.used = 0
        self.used_local = 0

    def partner(self, way):
        axis, distance = way
        if axis == "tensor":
            return (self.dp, self.tensor ^ distance)
        return (self.dp ^ distance, self.tensor)

    def greet(self, ways):
        barrier = pltpu.get_barrier_semaphore()
        for way in ways:
            pl.semaphore_signal(
                barrier, inc=1, device_id=self.partner(way), device_id_type=pl.DeviceIdType.MESH
            )
        pl.semaphore_wait(barrier, len(ways))

    def copy(self, source, target, way):
        k = self.used
        self.used += 1
        return pltpu.make_async_remote_copy(
            src_ref=source,
            dst_ref=target,
            send_sem=self.send_sems.at[k],
            recv_sem=self.recv_sems.at[k],
            device_id=self.partner(way),
            device_id_type=pl.DeviceIdType.MESH,
        )

    def local(self, source, target):
        k = self.used_local
        self.used_local += 1
        return pltpu.make_async_copy(source, target, self.local_sems.at[k])


def link_scratch(copies, local):
    return [
        pltpu.SemaphoreType.DMA((copies,)),
        pltpu.SemaphoreType.DMA((copies,)),
        pltpu.SemaphoreType.DMA((local,)),
    ]


def z_distances(n):
    found = []
    m = n // 2
    while m > 1:
        m //= 2
        found.append(m)
    return found


def z_ways(n):
    return [("dp", 2 * distance) for distance in z_distances(n)]


def column_stages(links, shard, column, n):
    z = links.dp // 2
    held = [z]
    stages = []
    for distance in z_distances(n):
        stages.append(
            [
                (
                    links.copy(shard if k == 0 else column.at[index], column.at[index], ("dp", 2 * distance)),
                    index ^ distance,
                )
                for k, index in enumerate(held)
            ]
        )
        held = held + [index ^ distance for index in held]
    return stages


class Spread:
    def __init__(self, links, column, whole):
        y = links.dp % 2
        half = column.shape[0] // 2
        low, high = pl.ds(0, half), pl.ds(half, half)
        near, near_core, far, far_core = (whole.at[k] for k in range(4))
        self.own = links.local(column, near.at[:, y])
        self.first = [
            links.copy(column, near.at[:, y], Y),
            links.copy(column, far.at[:, y], X),
        ]
        self.core = [links.copy(column, near_core.at[:, y], CORE)]
        self.second = [
            links.copy(near.at[low, 1 - y], far.at[low, 1 - y], X),
            links.copy(far.at[high, y], far.at[high, y], Y),
        ]
        self.core_second = [
            links.copy(near.at[:, 1 - y], near_core.at[:, 1 - y], CORE),
            links.copy(far.at[:, y], far_core.at[:, y], CORE),
        ]
        self.core_third = [links.copy(far.at[:, 1 - y], far_core.at[:, 1 - y], CORE)]

    def start(self):
        self.own.start()
        for copy in self.first + self.core:
            copy.start()

    def middle(self):
        for copy in self.first:
            copy.wait_recv()
        for copy in self.second + self.core_second:
            copy.start()

    def end(self):
        for copy in self.second:
            copy.wait_recv()
        for copy in self.core_third:
            copy.start()
        self.own.wait()
        for copy in self.first + self.second:
            copy.wait_send()
        for copy in self.core + self.core_second + self.core_third:
            copy.wait()


def add_to(total_ref, other_ref):
    def one(k, c):
        total_ref[k] = (total_ref[k].astype(F32) + other_ref[k].astype(F32)).astype(BF16)
        return c

    lax.fori_loop(0, total_ref.shape[0], one, 0)


class Gather:
    def __init__(self, links, near, far, buffers):
        y = links.dp % 2
        self.column, self.over_y, self.over_x, self.got_y, self.got_x, self.sum_y, self.sum_x = buffers
        m = self.column.shape[0]
        low, high = pl.ds(0, m // 2), pl.ds(m // 2, m // 2)
        self.low, self.high = low, high
        self.loads = [
            links.local(near.at[:, y], self.column),
            links.local(near.at[:, 1 - y], self.over_y),
            links.local(far.at[:, y], self.over_x),
        ]
        diagonal = far.at[:, 1 - y]
        self.first = [
            links.copy(diagonal.at[low], self.got_y, X),
            links.copy(diagonal.at[high], self.got_x, Y),
        ]
        self.second = [
            links.copy(self.over_x, self.sum_x, X),
            links.copy(self.over_y, self.sum_y, Y),
        ]

    def start(self):
        for copy in self.loads + self.first:
            copy.start()

    def middle(self):
        for copy in self.loads:
            copy.wait()
        for copy in self.first:
            copy.wait_recv()
        add_to(self.over_y.at[self.low], self.got_y)
        add_to(self.over_x.at[self.high], self.got_x)
        for copy in self.second:
            copy.start()

    def end(self):
        for copy in self.second:
            copy.wait_recv()
        add_to(self.column, self.sum_y)
        add_to(self.column, self.sum_x)
        for copy in self.first + self.second:
            copy.wait_send()


def gather_scratch(m, r, c):
    whole = pltpu.VMEM((m, r, c), BF16)
    half = pltpu.VMEM((m // 2, r, c), BF16)
    return [whole] * 3 + [half] * 2 + [whole] * 2


class GatherLast:
    def __init__(self, links, near, far, diagonal, buffers):
        y = links.dp % 2
        self.column, self.over_x, self.diagonal, self.sum_y, self.sum_x = buffers
        self.loads = [
            links.local(far.at[:, y], self.over_x),
            links.local(diagonal, self.diagonal),
            links.local(near.at[:, y], self.column),
        ]
        self.over_y = links.copy(near.at[:, 1 - y], self.sum_y, Y)
        self.along_x = links.copy(self.over_x, self.sum_x, X)

    def start(self):
        self.over_y.start()
        for copy in self.loads:
            copy.start()

    def middle(self):
        for copy in self.loads:
            copy.wait()
        add_to(self.over_x, self.diagonal)
        self.along_x.start()

    def end(self):
        self.over_y.wait_recv()
        self.along_x.wait_recv()
        add_to(self.column, self.sum_y)
        add_to(self.column, self.sum_x)
        self.over_y.wait_send()
        self.along_x.wait_send()


class Collect:
    def __init__(self, links, column, slots):
        z = links.dp // 2
        self.column, self.slots, self.z = column, slots, z
        m = column.shape[0]
        distances = z_distances(2 * m)[::-1]
        self.stages = []
        first = 0
        for step, distance in enumerate(distances):
            kept = [0]
            for other in distances[step + 1 :]:
                kept = kept + [k ^ other for k in kept]
            self.stages.append(
                [
                    (links.copy(column.at[z ^ distance ^ k], slots.at[first + i], ("dp", 2 * distance)), first + i, z ^ k)
                    for i, k in enumerate(kept)
                ]
            )
            first += len(kept)

    def start(self, step):
        for copy, _, _ in self.stages[step]:
            copy.start()

    def finish(self, step):
        for copy, slot, index in self.stages[step]:
            copy.wait_recv()
            self.column[index] = (self.column[index].astype(F32) + self.slots[slot].astype(F32)).astype(BF16)

    def drain(self):
        for stage in self.stages:
            for copy, _, _ in stage:
                copy.wait_send()


class RowSum:
    def __init__(self, links, terms, buffers):
        self.near, self.far, self.got_near, self.got_far, self.got_x = buffers
        count = self.near.shape[0]

        def rows(distance):
            start = pl.multiple_of((links.tensor ^ distance) * count, count)
            return terms.at[pl.ds(start, count)]

        self.loads = [links.local(rows(0), self.near), links.local(rows(2), self.far)]
        self.core = [links.copy(rows(3), self.got_far, CORE), links.copy(rows(1), self.got_near, CORE)]
        self.over_x = links.copy(self.far, self.got_x, X)

    def start(self):
        for copy in self.loads[::-1] + self.core:
            copy.start()

    def middle(self):
        self.loads[1].wait()
        self.core[0].wait_recv()

        def add(rows):
            self.far[rows, :] = (self.far[rows, :].astype(F32) + self.got_far[rows, :].astype(F32)).astype(BF16)

        by_rows(self.far.shape[0], 64, add)
        self.over_x.start()

    def end(self):
        self.loads[0].wait()
        self.core[1].wait_recv()
        self.over_x.wait_recv()
        for copy in self.core + [self.over_x]:
            copy.wait_send()

    def total(self, rows):
        return self.near[rows, :].astype(F32) + self.got_near[rows, :].astype(F32) + self.got_x[rows, :].astype(F32)


def row_sum_scratch(count, width):
    return [pltpu.VMEM((count, width), BF16)] * 5


class Everywhere:
    def __init__(self, links, held, slots, n):
        self.held, self.slots = held, slots
        ways = everywhere_ways(n)
        self.copies = [links.copy(held.at[k], slots.at[k], way) for k, way in enumerate(ways)]

    def start(self, step):
        self.copies[step].start()

    def finish(self, step):
        self.copies[step].wait()
        self.held[step + 1] = self.held[step] + self.slots[step]


def everywhere_ways(n):
    return [CORE, X, Y] + z_ways(n)


def everywhere_scratch(k, c, n):
    steps = len(everywhere_ways(n))
    return [pltpu.VMEM((steps + 1, k, c), F32), pltpu.VMEM((steps, k, c), F32)]


def middle_kernel(
    back_ref, rows_ref, grad_ref, norm_ref, down_ref, cross_ref,
    wide_out, grad_out, sums_ref, down_out, diagonal_out,
    low, column, slots, send_sems, recv_sems, local_sems, *, n
):
    links = Links(send_sems, recv_sems, local_sems)
    count = low.shape[0]
    load = links.local(down_ref, column)
    load.start()
    collect = Collect(links, column, slots)

    def place(distance):
        return wide_out.at[pl.ds(pl.multiple_of((links.tensor ^ distance) * count, count), count)]

    own = links.local(low, place(0))
    half = count // 2
    parts = [pl.ds(0, half), pl.ds(half, half)]
    over_x = [links.copy(low.at[part], place(0).at[part], X) for part in parts]
    over_core = links.copy(low, place(0), CORE)
    onward = [links.copy(place(2).at[part], place(2).at[part], CORE) for part in parts]
    over_y = links.copy(cross_ref.at[1, :, 1 - links.dp % 2], diagonal_out, Y)
    links.greet([CORE, X, Y] + z_ways(n))
    over_y.start()
    load.wait()
    collect.start(0)
    sums_ref[...] = jnp.zeros_like(sums_ref)

    def norm_back(rows):
        incoming = back_ref[rows, :]
        rows_grad, gain_terms = norm_rows_back(rows_ref[rows, :], incoming, norm_ref[0:1, :])
        rows_grad = rows_grad + grad_ref[rows, :]
        rounded = rows_grad.astype(BF16)
        grad_out[rows, :] = rows_grad
        low[rows, :] = rounded
        for k, terms in enumerate((gain_terms, incoming, rounded.astype(F32))):
            sums_ref[k : k + 1, :] += jnp.sum(terms, axis=0, keepdims=True)

    for part, copy in zip(parts, over_x):
        by_rows(half, 64, lambda rows, part=part: norm_back(pl.ds(pl.multiple_of(part.start + rows.start, 64), 64)))
        copy.start()
    own.start()
    over_core.start()
    for step in range(len(collect.stages) - 1):
        collect.finish(step)
        collect.start(step + 1)
    for copy, later in zip(over_x, onward):
        copy.wait_recv()
        later.start()
    collect.finish(len(collect.stages) - 1)
    down_out[...] = column[collect.z].astype(F32)
    collect.drain()
    own.wait()
    for copy in over_x:
        copy.wait_send()
    over_core.wait()
    for copy in onward:
        copy.wait()
    over_y.wait()


def middle(back, rows, grad, norm, down_column, cross_sum):
    n = lax.axis_size("dp")
    count, width = rows.shape
    m, r, c = down_column.shape
    vmem = pl.BlockSpec(memory_space=pltpu.VMEM)
    return pl.pallas_call(
        functools.partial(middle_kernel, n=n),
        in_specs=[vmem, vmem, vmem, vmem, ANY, ANY],
        out_specs=[ANY, vmem, vmem, vmem, ANY],
        out_shape=[
            jax.ShapeDtypeStruct((4 * count, width), BF16),
            jax.ShapeDtypeStruct((count, width), F32),
            jax.ShapeDtypeStruct((8, width), F32),
            jax.ShapeDtypeStruct((r, c), F32),
            jax.ShapeDtypeStruct((m, r, cross_sum.shape[4]), BF16),
        ],
        scratch_shapes=[
            pltpu.VMEM((count, width), BF16),
            pltpu.VMEM((m, r, c), BF16),
            pltpu.VMEM((m, r, c), BF16),
        ]
        + link_scratch(6 + m, 2),
        compiler_params=pltpu.CompilerParams(
            vmem_limit_bytes=VMEM_LIMIT, collective_id=6, has_side_effects=True
        ),
        cost_estimate=pl.CostEstimate(flops=0, bytes_accessed=100 * 2**20, transcendentals=0),
        name="middle",
    )(back, rows, grad, norm, down_column, cross_sum)


def tail_kernel(
    dq_ref, dk_ref, dv_ref, w_ref, first_ref, so_ref, rows_ref, grad_ref, norm_ref, late_ref,
    grad_out, weights_out, late_out, give, acc, weights, *scratch, n, step_rows
):
    links = Links(*scratch[-3:])
    near, far, got_near, got_far, got_x = scratch[:5]
    columns, gots, slots = scratch[5:7], scratch[7:9], scratch[9:11]
    held, late_slots = scratch[11:13]
    count, model = near.shape
    width = dq_ref.shape[1]
    y = links.dp % 2
    c = columns[0].shape[2]
    m, _, r, _ = weights.shape
    half = count // 2
    parts = [pl.ds(0, half), pl.ds(half, half)]
    core_far = links.copy(give.at[0], got_far, CORE)
    core_near = links.copy(give.at[1], got_near, CORE)
    over_x = [links.copy(far.at[part], got_x.at[part], X) for part in parts]
    over_y, collects = [], []
    for k, (column, got, slot) in enumerate(zip(columns, gots, slots)):
        over_y.append(links.copy(weights.at[:, 1 - y, :, pl.ds(k * c, c)], got, Y))
        collects.append(Collect(links, column, slot))
    late = Everywhere(links, held, late_slots, n)
    links.greet(everywhere_ways(n))

    def terms(distance, target):
        base = (links.tensor ^ distance) * count

        def one(rows):
            there = pl.ds(pl.multiple_of(base + rows.start, 128), 128)
            total = dot_nt(dq_ref[there, :], w_ref[:, :width])
            total = total + dot_nt(dk_ref[there, :], w_ref[:, width : 2 * width])
            target[rows, :] = (total + dot_nt(dv_ref[there, :], w_ref[:, 2 * width : 3 * width])).astype(BF16)

        by_rows(count, 128, one)

    terms(3, give.at[0])
    core_far.start()
    terms(2, far)
    core_far.wait_recv()
    for part, copy in zip(parts, over_x):

        def add(rows, part=part):
            there = pl.ds(pl.multiple_of(part.start + rows.start, 64), 64)
            far[there, :] = (far[there, :].astype(F32) + got_far[there, :].astype(F32)).astype(BF16)

        by_rows(half, 64, add)
        copy.start()

    acc[...] = jnp.zeros_like(acc)

    def products(rows):
        source = first_ref[rows, :].T
        for k, ref in enumerate((dq_ref, dk_ref, dv_ref)):
            acc[:, k * width : (k + 1) * width] += dot_nn(source, ref[rows, :])

    by_rows(dq_ref.shape[0], step_rows, products)
    for k in range(2 * m):
        span = slice(k * r, (k + 1) * r)
        weights[k // 2, k % 2, :, : 3 * width] = acc[span, :].astype(BF16)
        weights[k // 2, k % 2, :, 3 * width :] = so_ref[span, :]
    over_y[0].start()
    terms(1, give.at[1])
    core_near.start()
    terms(0, near)
    for k in range(2):
        columns[k][...] = weights[:, y, :, k * c : (k + 1) * c]
    for k in range(2):
        over_y[k].wait_recv()
        if k == 0:
            over_y[1].start()
        add_to(columns[k], gots[k])
        collects[k].start(0)
    stages = len(collects[0].stages)
    for step in range(stages - 1):
        for k in range(2):
            collects[k].finish(step)
            collects[k].start(step + 1)
    held[0] = late_ref[...]
    core_near.wait_recv()
    for part, copy in zip(parts, over_x):
        copy.wait_recv()

        def norm_back(rows, part=part):
            rows = pl.ds(pl.multiple_of(part.start + rows.start, 64), 64)
            incoming = near[rows, :].astype(F32) + got_near[rows, :].astype(F32) + got_x[rows, :].astype(F32)
            rows_grad, gain_terms = norm_rows_back(rows_ref[rows, :].astype(F32), incoming, norm_ref[0:1, :])
            grad_out[rows, :] = rows_grad + grad_ref[rows, :]
            held[0, 0:1, :] += jnp.sum(gain_terms, axis=0, keepdims=True)
            held[0, 1:2, :] += jnp.sum(incoming, axis=0, keepdims=True)

        by_rows(half, 64, norm_back)
    steps = len(late.copies)
    for step in range(steps):
        late.start(step)
        if step == 0:
            for k in range(2):
                collects[k].finish(stages - 1)
                weights_out[:, k * c : (k + 1) * c] = columns[k][collects[k].z].astype(F32)
        late.finish(step)
    late_out[...] = held[steps]
    for copy in over_x + over_y + [core_near, core_far]:
        copy.wait_send()
    for collect in collects:
        collect.drain()


def tail(dq, dk, dv, w, first, so_grad, rows, grad, norm, late):
    n = lax.axis_size("dp")
    count, model = rows.shape
    total, width = dq.shape
    m, r, c = n // 2, model // n, 4 * width
    vmem = pl.BlockSpec(memory_space=pltpu.VMEM)
    part = pltpu.VMEM((m, r, c // 2), BF16)
    return pl.pallas_call(
        functools.partial(tail_kernel, n=n, step_rows=512),
        in_specs=[vmem] * 10,
        out_specs=[vmem, vmem, vmem],
        out_shape=[
            jax.ShapeDtypeStruct((count, model), F32),
            jax.ShapeDtypeStruct((r, c), F32),
            jax.ShapeDtypeStruct(late.shape, F32),
        ],
        scratch_shapes=[
            pltpu.VMEM((2, count, model), BF16),
            pltpu.VMEM((model, 3 * width), F32),
            pltpu.VMEM((m, 2, r, c), BF16),
        ]
        + row_sum_scratch(count, model)
        + [part] * 6
        + everywhere_scratch(*late.shape, n)
        + link_scratch(6 + 2 * m + len(everywhere_ways(n)), 1),
        compiler_params=pltpu.CompilerParams(
            vmem_limit_bytes=VMEM_LIMIT, collective_id=7, has_side_effects=True
        ),
        cost_estimate=pl.CostEstimate(flops=0, bytes_accessed=100 * 2**20, transcendentals=0),
        name="tail",
    )(dq, dk, dv, w, first, so_grad, rows, grad, norm, late)


def start_kernel(
    rows_ref, enc_ref, self_ref, cross_ref, rows_out, enc_out, self_out, cross_out, send_sems, recv_sems, local_sems, *, n
):
    links = Links(send_sems, recv_sems, local_sems)
    member, z, y = links.tensor, links.dp // 2, links.dp % 2
    links.greet([CORE, X, Y] + z_ways(n))

    def place(ref, index, size):
        return ref.at[pl.ds(pl.multiple_of(index * size, size), size)]

    groups = [(rows_ref, rows_out, rows_ref.shape[0]), (enc_ref, enc_out, enc_ref.shape[0])]
    local, started, arrived = [], [], []
    for source, target, size in groups:
        local.append(links.local(source, place(target, member, size)))
    local.append(links.local(self_ref, self_out.at[z, y]))
    local.append(links.local(cross_ref, cross_out.at[z]))
    for copy in local:
        copy.start()

    def go(copy):
        copy.start()
        started.append(copy)
        return copy

    def got(copy):
        copy.wait_recv()
        arrived.append(copy)

    along_x = [go(links.copy(source, place(target, member, size), X)) for source, target, size in groups]
    go(links.copy(self_ref, self_out.at[z, y], Y))
    for source, target, size in groups:
        go(links.copy(source, place(target, member, size), CORE))
    self_stages = column_stages(links, self_ref, self_out.at[:, y], n)
    cross_stages = column_stages(links, cross_ref, cross_out, n)
    for self_stage in self_stages:
        for copy, _ in self_stage:
            go(copy)
        for copy, index in self_stage:
            got(copy)
            go(links.copy(self_out.at[index, y], self_out.at[index, y], Y))
        if self_stage is self_stages[0]:
            for copy, _ in cross_stages[0]:
                go(copy)
    for cross_stage, later in zip(cross_stages, cross_stages[1:]):
        for copy, _ in cross_stage:
            got(copy)
        for copy, _ in later:
            go(copy)
    for copy, (_, target, size) in zip(along_x, groups):
        got(copy)
        there = place(target, member ^ 2, size)
        go(links.copy(there, there, CORE))
    for copy in local:
        copy.wait()
    for copy in started:
        copy.wait_send()
        if not any(copy is other for other in arrived):
            copy.wait_recv()


def start_gather(rows_low, enc_low, self_shard, cross_shard):
    n = lax.axis_size("dp")
    r, c = self_shard.shape
    copies = 3 * n + 8
    return pl.pallas_call(
        functools.partial(start_kernel, n=n),
        in_specs=[ANY] * 4,
        out_specs=[ANY] * 4,
        out_shape=[
            jax.ShapeDtypeStruct((4 * rows_low.shape[0], rows_low.shape[1]), BF16),
            jax.ShapeDtypeStruct((4 * enc_low.shape[0], enc_low.shape[1]), BF16),
            jax.ShapeDtypeStruct((n // 2, 2, r, c), BF16),
            jax.ShapeDtypeStruct((n // 2,) + cross_shard.shape, BF16),
        ],
        scratch_shapes=link_scratch(copies, 4),
        compiler_params=pltpu.CompilerParams(collective_id=0, has_side_effects=True),
        cost_estimate=pl.CostEstimate(flops=0, bytes_accessed=100 * 2**20, transcendentals=0),
        name="start_gather",
    )(rows_low, enc_low, self_shard, cross_shard)


def self_forward_kernel(
    b_ref, q_ref, k_ref, vt_ref, column_ref, shard_ref,
    ot_ref, lse_ref, whole, next_column,
    m_s, l_s, acc, send_sems, recv_sems, local_sems, *, bk, heads, safe, n
):
    i = pl.program_id(0)
    last = pl.num_programs(0) - 1
    bq, width = q_ref.shape
    links = Links(send_sems, recv_sems, local_sems)
    spread = Spread(links, column_ref, whole)
    keep = links.local(shard_ref, next_column.at[links.dp // 2])
    stages = column_stages(links, shard_ref, next_column, n)

    @pl.when(i == 0)
    def _():
        links.greet([CORE, X, Y] + z_ways(n))
        spread.start()
        keep.start()
        for copy, _ in stages[0]:
            copy.start()

    @pl.when(i == last)
    def _():
        spread.middle()
        for k in range(1, len(stages)):
            for copy, _ in stages[k - 1]:
                copy.wait_recv()
            for copy, _ in stages[k]:
                copy.start()

    hd = width // heads
    m_s[...] = jnp.full_like(m_s, NEGATIVE)
    l_s[...] = jnp.zeros_like(l_s)
    acc[...] = jnp.zeros_like(acc)
    scaled = q_ref[...] * jnp.asarray(1.0 / math.sqrt(hd), BF16)
    q_heads = [head_only(scaled, h, hd) for h in range(heads)]

    def block(j, mode):
        rows = pl.ds(pl.multiple_of(j * bk, bk), bk)
        keys = k_ref[rows, :]
        m_old = m_s[...]
        l_old = l_s[...]
        scores = [dot_nt(keys, q_heads[h]) for h in range(heads)]
        if mode != "none":
            bad = self_bad(b_ref, i * bq, j * bk, bq, bk, mode == "causal")
            scores = [jnp.where(bad, NEGATIVE, s) for s in scores]
        m_out, l_out, a_out = [], [], []
        for h in range(heads):
            part = slice(h * hd, (h + 1) * hd)
            m_new = jnp.maximum(m_old[h : h + 1, :], jnp.max(scores[h], axis=0, keepdims=True))
            shrink = jnp.exp(m_old[h : h + 1, :] - m_new)
            expos = jnp.exp(scores[h] - m_new)
            l_out.append(l_old[h : h + 1, :] * shrink + jnp.sum(expos, axis=0, keepdims=True))
            m_out.append(m_new)
            a_out.append(acc[part, :] * shrink + dot_nn(vt_ref[part, rows], expos.astype(BF16)))
        m_s[...] = jnp.concatenate(m_out, 0)
        l_s[...] = jnp.concatenate(l_out, 0)
        for h in range(heads):
            acc[h * hd : (h + 1) * hd, :] = a_out[h]

    over_keys(i, bq, bk, safe, block)
    inverse = 1.0 / l_s[...]
    for h in range(heads):
        part = slice(h * hd, (h + 1) * hd)
        ot_ref[part, :] = (acc[part, :] * inverse[h : h + 1, :]).astype(BF16)
    lse_ref[...] = m_s[...] + jnp.log(l_s[...])

    @pl.when(i == last)
    def _():
        spread.end()
        keep.wait()
        for k, stage in enumerate(stages):
            for copy, _ in stage:
                copy.wait_send()
                if k == len(stages) - 1:
                    copy.wait_recv()


def self_forward(bounds, queries, keys, values_t, column, shard, heads, safe):
    n, width = queries.shape
    bq = bk = 512
    dp = lax.axis_size("dp")
    m, r, c = column.shape
    return pl.pallas_call(
        functools.partial(self_forward_kernel, bk=bk, heads=heads, safe=safe, n=dp),
        grid=(n // bq,),
        in_specs=[
            pl.BlockSpec(memory_space=pltpu.SMEM),
            pl.BlockSpec((bq, width), lambda i: (i, 0)),
            pl.BlockSpec((n, width), lambda i: (0, 0)),
            pl.BlockSpec((width, n), lambda i: (0, 0)),
            ANY,
            ANY,
        ],
        out_specs=[
            pl.BlockSpec((width, bq), lambda i: (0, i)),
            pl.BlockSpec((heads, bq), lambda i: (0, i)),
        ]
        + [ANY] * 2,
        out_shape=[
            jax.ShapeDtypeStruct((width, n), BF16),
            jax.ShapeDtypeStruct((heads, n), F32),
        ]
        + [jax.ShapeDtypeStruct((4, m, 2, r, c), BF16)]
        + [jax.ShapeDtypeStruct((m,) + shard.shape, BF16)],
        scratch_shapes=[
            pltpu.VMEM((heads, bq), F32),
            pltpu.VMEM((heads, bq), F32),
            pltpu.VMEM((width, bq), F32),
        ]
        + link_scratch(8 + m, 2),
        compiler_params=pltpu.CompilerParams(
            vmem_limit_bytes=VMEM_LIMIT, collective_id=1, has_side_effects=True
        ),
        cost_estimate=pl.CostEstimate(
            flops=12 * n * n * width, bytes_accessed=8 * n * width, transcendentals=n * n * heads // 2
        ),
        name="self_forward",
    )(bounds, queries, keys, values_t, column, shard)


def self_backward_kernel(
    b_ref, q_ref, k_ref, v_ref, kt_ref, wide_ref, w_ref, mt_ref, lse_ref,
    up_ref, cross_ref, diagonal_ref, enc_ref, early_ref,
    dq_ref, dk_ref, dv_ref, up_out, cross_out, enc_out, early_out, dka, dva, dqa, *scratch, bk, heads, safe, n
):
    i = pl.program_id(0)
    last = pl.num_programs(0) - 1
    links = Links(*scratch[-3:])
    cross = GatherLast(links, cross_ref.at[0], cross_ref.at[1], diagonal_ref, scratch[:5])
    cross_z = Collect(links, cross.column, scratch[5])
    up_column = scratch[6]
    up_z = Collect(links, up_column, scratch[7])
    load = links.local(up_ref, up_column)
    enc = RowSum(links, enc_ref, scratch[8:13])
    held = scratch[13]
    early = Everywhere(links, held, scratch[14], n)
    stages = len(up_z.stages)
    steps = len(early.copies)

    def next_early(step):
        early.finish(step)
        early.start(step + 1)

    @pl.when(i == 0)
    def _():
        links.greet(everywhere_ways(n))
        cross.start()
        enc.start()
        load.start()
        held[0] = early_ref[...]
        early.start(0)
        load.wait()
        up_z.start(0)
        dka[...] = jnp.zeros_like(dka)
        dva[...] = jnp.zeros_like(dva)

    @pl.when(i == 1)
    def _():
        cross.middle()
        next_early(0)

    @pl.when(i == 2)
    def _():
        for step in range(stages - 1):
            up_z.finish(step)
            up_z.start(step + 1)
        next_early(1)

    @pl.when(i == 3)
    def _():
        next_early(2)

    @pl.when(i == last)
    def _():
        for step in range(3, steps - 1):
            next_early(step)

    def sum_cross():
        cross.end()
        cross_z.start(0)
        enc.middle()

    def next_cross():
        for step in range(stages - 1):
            cross_z.finish(step)
            cross_z.start(step + 1)

    bq, width = q_ref.shape
    hd = width // heads
    scale = 1.0 / math.sqrt(hd)
    grads = dot_nn(wide_ref[...], w_ref[...]).astype(BF16)
    products = grads.T.astype(F32) * mt_ref[...].astype(F32)
    inner = [jnp.sum(products[h * hd : (h + 1) * hd, :], axis=0, keepdims=True) for h in range(heads)]
    scaled = q_ref[...] * jnp.asarray(scale, BF16)
    q_heads = [head_only(scaled, h, hd) for h in range(heads)]
    d_heads = [head_only(grads, h, hd) for h in range(heads)]
    lse = lse_ref[...]
    dqa[...] = jnp.zeros_like(dqa)

    def block(j, mode):
        rows = pl.ds(pl.multiple_of(j * bk, bk), bk)
        keys = k_ref[rows, :]
        values = v_ref[rows, :]
        scores = [dot_nt(keys, q_heads[h]) for h in range(heads)]
        dprobs = [dot_nt(values, d_heads[h]) for h in range(heads)]
        if mode != "none":
            bad = self_bad(b_ref, i * bq, j * bk, bq, bk, mode == "causal")
            scores = [jnp.where(bad, NEGATIVE, s) for s in scores]
        dv_sum, dk_sum = None, None
        for h in range(heads):
            part = slice(h * hd, (h + 1) * hd)
            probs = jnp.exp(scores[h] - lse[h : h + 1, :])
            ds = (probs * (dprobs[h] - inner[h])).astype(BF16)
            dv_h = dot_nn(probs.astype(BF16), d_heads[h])
            dk_h = dot_nn(ds, q_heads[h])
            dv_sum = dv_h if dv_sum is None else dv_sum + dv_h
            dk_sum = dk_h if dk_sum is None else dk_sum + dk_h
            dqa[part, :] += dot_nn(kt_ref[part, rows], ds)
        dva[rows, :] += dv_sum
        dka[rows, :] += dk_sum

    over_keys(i, bq, bk, safe, block, [(3, 2, sum_cross), (4, 2, next_cross)])
    dq_ref[...] = (dqa[...] * scale).astype(BF16).T

    @pl.when(i == pl.num_programs(0) - 1)
    def _():
        dk_ref[...] = dka[...].astype(BF16)
        dv_ref[...] = dva[...].astype(BF16)
        up_z.finish(stages - 1)
        up_out[...] = up_column[up_z.z].astype(F32)
        cross_z.finish(stages - 1)
        cross_out[...] = cross.column[cross_z.z].astype(F32)
        enc.end()

        def store(rows):
            enc_out[rows, :] = enc.total(rows)

        by_rows(enc_out.shape[0], 64, store)
        early.finish(steps - 1)
        early_out[...] = held[steps]
        up_z.drain()
        cross_z.drain()


def self_backward(
    bounds, queries, keys, values, keys_t, wide, w_out, mixed_t, lse,
    up_column, cross_sum, diagonal, enc_terms, early, heads, safe
):
    n, width = queries.shape
    model = wide.shape[1]
    dp = lax.axis_size("dp")
    m, r, c = up_column.shape
    cross_c = cross_sum.shape[4]
    enc_shape = (enc_terms.shape[0] // 4, enc_terms.shape[1])
    bq = bk = 512
    some = pl.BlockSpec((bq, width), lambda i: (i, 0))
    return pl.pallas_call(
        functools.partial(self_backward_kernel, bk=bk, heads=heads, safe=safe, n=dp),
        grid=(n // bq,),
        in_specs=[
            pl.BlockSpec(memory_space=pltpu.SMEM),
            some,
            const((n, width)),
            const((n, width)),
            const((width, n)),
            pl.BlockSpec((bq, model), lambda i: (i, 0)),
            const((model, width)),
            pl.BlockSpec((width, bq), lambda i: (0, i)),
            pl.BlockSpec((heads, bq), lambda i: (0, i)),
        ]
        + [ANY] * 4
        + [const(early.shape)],
        out_specs=[some, const((n, width)), const((n, width))]
        + [const((r, c)), const((r, cross_c)), const(enc_shape), const(early.shape)],
        out_shape=[
            jax.ShapeDtypeStruct((n, width), BF16),
            jax.ShapeDtypeStruct((n, width), BF16),
            jax.ShapeDtypeStruct((n, width), BF16),
            jax.ShapeDtypeStruct((r, c), F32),
            jax.ShapeDtypeStruct((r, cross_c), F32),
            jax.ShapeDtypeStruct(enc_shape, F32),
            jax.ShapeDtypeStruct(early.shape, F32),
        ],
        scratch_shapes=[
            pltpu.VMEM((n, width), F32),
            pltpu.VMEM((n, width), F32),
            pltpu.VMEM((width, bq), F32),
        ]
        + [pltpu.VMEM((m, r, cross_c), BF16)] * 6
        + [pltpu.VMEM((m, r, c), BF16)] * 2
        + row_sum_scratch(*enc_shape)
        + everywhere_scratch(*early.shape, dp)
        + link_scratch(5 + 2 * m + len(everywhere_ways(dp)), 6),
        compiler_params=pltpu.CompilerParams(
            vmem_limit_bytes=VMEM_LIMIT, collective_id=5, has_side_effects=True
        ),
        cost_estimate=pl.CostEstimate(
            flops=24 * n * n * width, bytes_accessed=16 * n * width, transcendentals=n * n * heads // 2
        ),
        name="self_backward",
    )(bounds, queries, keys, values, keys_t, wide, w_out, mixed_t, lse, up_column, cross_sum, diagonal, enc_terms, early)


def const(shape):
    return pl.BlockSpec(shape, lambda *_: (0,) * len(shape), pipeline_mode=pl.Buffered(1))


def normalized(rows):
    center = rows - jnp.mean(rows, axis=-1, keepdims=True)
    scale = lax.rsqrt(jnp.mean(center * center, axis=-1, keepdims=True) + EPSILON)
    return center * scale, scale


def norm_rows_back(rows, incoming, gain):
    xhat, scale = normalized(rows)
    e = incoming * gain
    inner = jnp.mean(e * xhat, axis=-1, keepdims=True)
    return scale * (e - jnp.mean(e, axis=-1, keepdims=True) - xhat * inner), incoming * xhat


def by_rows(count, step, body):
    def one(k, c):
        body(pl.ds(pl.multiple_of(k * step, step), step))
        return c

    lax.fori_loop(0, count // step, one, 0)


def cross_forward_kernel(
    ok_ref, x_ref, enc_ref, w_ref, bq_ref, bv_ref, rows_ref, shift_ref, norm_ref, column_ref,
    q_out, k_out, v_out, ot_ref, lse_ref, after_ref, third_ref, whole, send_sems, recv_sems, local_sems, *, heads
):
    i = pl.program_id(0)
    last = pl.num_programs(0) - 1
    links = Links(send_sems, recv_sems, local_sems)
    spread = Spread(links, column_ref, whole)

    @pl.when(i == 0)
    def _():
        links.greet([CORE, X, Y])
        spread.start()
        after_ref[...] = rows_ref[...] + shift_ref[...]

    width = q_out.shape[2]
    hd = width // heads
    query = (dot_nn(x_ref[...], w_ref[0, :, :width]) + bq_ref[0]).astype(BF16)
    key_value = dot_nn(enc_ref[...], w_ref[0, :, width : 3 * width])
    keys = key_value[:, :width].astype(BF16)
    values = (key_value[:, width:] + bv_ref[0]).astype(BF16)
    q_out[0] = query
    k_out[0] = keys
    v_out[0] = values
    values_t = values.T
    scaled = query * jnp.asarray(1.0 / math.sqrt(hd), BF16)
    ok = ok_ref[...] > 0.0
    scores = [dot_nt(keys, head_only(scaled, h, hd)) for h in range(heads)]
    mixed = []
    for h in range(heads):
        part = slice(h * hd, (h + 1) * hd)
        s = jnp.where(ok, scores[h], NEGATIVE)
        largest = jnp.max(s, axis=0, keepdims=True)
        expos = jnp.exp(s - largest)
        total = jnp.sum(expos, axis=0, keepdims=True)
        mixed.append((dot_nn(values_t[part, :], expos.astype(BF16)) * (1.0 / total)).astype(BF16))
        ot_ref[0, part, :] = mixed[h]
        lse_ref[0, h : h + 1, :] = largest + jnp.log(total)
    after_ref[...] += dot_nt(jnp.concatenate(mixed, 0).T, w_ref[0, :, 3 * width :])

    @pl.when(i == last)
    def _():
        spread.middle()

        def norm(rows):
            xhat, _ = normalized(after_ref[rows, :])
            third_ref[rows, :] = (xhat * norm_ref[0:1, :] + norm_ref[1:2, :]).astype(BF16)

        by_rows(after_ref.shape[0], 128, norm)
        spread.end()


def cross_forward(ok, x, encoder, weights, q_shift, v_shift, rows, shift, norm, column, heads):
    count, model = x.shape
    n = encoder.shape[0]
    parts, _, columns = weights.shape
    width = columns // 4
    m, r, c = column.shape

    def by_part(*shape):
        return pl.BlockSpec((1,) + shape, lambda i: (i,) + (0,) * len(shape))

    return pl.pallas_call(
        functools.partial(cross_forward_kernel, heads=heads),
        grid=(parts,),
        in_specs=[
            const((n, 1)),
            const((count, model)),
            const((n, model)),
            by_part(model, columns),
            by_part(1, width),
            by_part(1, width),
            const((count, model)),
            const((1, model)),
            const((2, model)),
            ANY,
        ],
        out_specs=[
            by_part(count, width),
            by_part(n, width),
            by_part(n, width),
            by_part(width, count),
            by_part(heads, count),
            const((count, model)),
            const((count, model)),
            ANY,
        ],
        out_shape=[
            jax.ShapeDtypeStruct((parts, count, width), BF16),
            jax.ShapeDtypeStruct((parts, n, width), BF16),
            jax.ShapeDtypeStruct((parts, n, width), BF16),
            jax.ShapeDtypeStruct((parts, width, count), BF16),
            jax.ShapeDtypeStruct((parts, heads, count), F32),
            jax.ShapeDtypeStruct((count, model), F32),
            jax.ShapeDtypeStruct((count, model), BF16),
            jax.ShapeDtypeStruct((4, m, 2, r, c), BF16),
        ],
        scratch_shapes=link_scratch(8, 1),
        compiler_params=pltpu.CompilerParams(
            vmem_limit_bytes=VMEM_LIMIT, collective_id=2, has_side_effects=True
        ),
        cost_estimate=pl.CostEstimate(
            flops=24 * parts * count * n * width,
            bytes_accessed=8 * parts * n * width,
            transcendentals=parts * count * n * heads,
        ),
        name="cross_forward",
    )(ok, x, encoder, weights, q_shift, v_shift, rows, shift, norm, column)


def feed_forward_kernel(
    x_ref, dy_ref, up_ref, down_ref, b_ref, after_ref, shift_ref, norm_ref,
    out_ref, rows_out, low_out, sums_ref, gup_ref, gdown_ref, bias_ref,
    xt_ref, dyt_ref, back_ref, give, got, send_sems, recv_sems, local_sems, *, chunks
):
    s = pl.program_id(0)
    links = Links(send_sems, recv_sems, local_sems)
    turn = s // chunks
    chunk = s % chunks
    pair = turn // 2
    slot = pair * chunks + chunk
    theirs = turn % 2 == 0
    to_core = pltpu.make_async_remote_copy(
        src_ref=give.at[chunk],
        dst_ref=got.at[slot],
        send_sem=send_sems.at[slot],
        recv_sem=recv_sems.at[slot],
        device_id=links.partner(CORE),
        device_id_type=pl.DeviceIdType.MESH,
    )

    @pl.when(s == 0)
    def _():
        links.greet([CORE])
        out_ref[...] = after_ref[...] + shift_ref[...]
        back_ref[...] = jnp.zeros_like(back_ref)
        xt_ref[...] = x_ref[...].T
        dyt_ref[...] = dy_ref[...].T
        sums_ref[...] = jnp.zeros_like(sums_ref)

    pre_act = dot_nn(x_ref[...], up_ref[0]) + b_ref[0]
    hidden_grad = dot_nn(dy_ref[...], down_ref[0])
    normal_cdf = 0.5 * (1.0 + lax.erf(pre_act * (1.0 / math.sqrt(2.0))))
    density = jnp.exp(-0.5 * pre_act * pre_act) * (1.0 / math.sqrt(2.0 * math.pi))
    hidden = (pre_act * normal_cdf).astype(BF16)
    pre_grad = (hidden_grad * (normal_cdf + pre_act * density)).astype(BF16)
    bias_ref[0] = jnp.sum(pre_grad.astype(F32), axis=0, keepdims=True)

    @pl.when(turn % 2 == 1)
    def _():
        to_core.wait_send()

    give[chunk, 0] = dot_nn(xt_ref[...], pre_grad).astype(BF16)
    give[chunk, 1] = dot_nn(dyt_ref[...], hidden).astype(BF16)
    out_ref[...] += dot_nt(hidden, down_ref[0])
    back_ref[...] += dot_nt(pre_grad, up_ref[0])

    @pl.when(theirs)
    def _():
        to_core.start()

    @pl.when(jnp.logical_not(theirs))
    def _():
        to_core.wait_recv()
        gup_ref[0] = (give[chunk, 0].astype(F32) + got[slot, 0].astype(F32)).astype(BF16)
        gdown_ref[0] = (give[chunk, 1].astype(F32) + got[slot, 1].astype(F32)).astype(BF16)

    @pl.when(s == pl.num_programs(0) - 1)
    def _():
        def norm_back(rows):
            third = back_ref[rows, :]
            upstream = dy_ref[rows, :].astype(F32)
            rows_grad, gain_terms = norm_rows_back(after_ref[rows, :], third, norm_ref[0:1, :])
            rows_grad = rows_grad + upstream
            low = rows_grad.astype(BF16)
            rows_out[rows, :] = rows_grad
            low_out[rows, :] = low
            for k, terms in enumerate((gain_terms, third, low.astype(F32), upstream)):
                sums_ref[k : k + 1, :] += jnp.sum(terms, axis=0, keepdims=True)

        by_rows(x_ref.shape[0], 128, norm_back)


def feed_forward(x, dy, weights, bias, after, shift, norm):
    rows, width = x.shape
    hidden = weights.shape[2] // 2
    size = min(512, hidden)
    chunks = hidden // size

    def block(s):
        return (s // chunks) ^ 1

    def placed(s):
        turn = s // chunks
        return (turn // 2, 0, (s % chunks) * (turn % 2))

    rows_spec = const((rows, width))
    grad_spec = pl.BlockSpec((1, width, size), placed)
    bias_spec = pl.BlockSpec((1, 1, size), lambda s: (block(s), 0, s % chunks))
    return pl.pallas_call(
        functools.partial(feed_forward_kernel, chunks=chunks),
        grid=(4 * chunks,),
        in_specs=[
            rows_spec,
            rows_spec,
            pl.BlockSpec((1, width, size), lambda s: (block(s), 0, s % chunks)),
            pl.BlockSpec((1, width, size), lambda s: (block(s), 0, chunks + s % chunks)),
            bias_spec,
            rows_spec,
            const((1, width)),
            const((2, width)),
        ],
        out_specs=[rows_spec, rows_spec, rows_spec, const((8, width)), grad_spec, grad_spec, bias_spec],
        out_shape=[
            jax.ShapeDtypeStruct((rows, width), F32),
            jax.ShapeDtypeStruct((rows, width), F32),
            jax.ShapeDtypeStruct((rows, width), BF16),
            jax.ShapeDtypeStruct((8, width), F32),
            jax.ShapeDtypeStruct((2, width, hidden), BF16),
            jax.ShapeDtypeStruct((2, width, hidden), BF16),
            jax.ShapeDtypeStruct((4, 1, hidden), F32),
        ],
        scratch_shapes=[
            pltpu.VMEM((width, rows), BF16),
            pltpu.VMEM((width, rows), BF16),
            pltpu.VMEM((rows, width), F32),
            pltpu.VMEM((chunks, 2, width, size), BF16),
            pltpu.VMEM((2 * chunks, 2, width, size), BF16),
        ]
        + link_scratch(2 * chunks, 1),
        compiler_params=pltpu.CompilerParams(
            vmem_limit_bytes=VMEM_LIMIT, collective_id=3, has_side_effects=True
        ),
        cost_estimate=pl.CostEstimate(
            flops=48 * rows * width * hidden, bytes_accessed=40 * 2**20, transcendentals=8 * rows * hidden
        ),
        name="feed_forward",
    )(x, dy, weights, weights, bias, after, shift, norm)


def cross_backward_kernel(
    ok_ref, low_ref, x_ref, enc_ref, w_ref, q_ref, k_ref, v_ref, mt_ref, lse_ref, up_ref, down_ref,
    back_ref, enc_out, grad_ref, bq_ref, bv_ref, up_out, down_out,
    low_t, x_t, enc_t, enc_acc, give, got, *scratch, heads, bk
):
    i = pl.program_id(0)
    last = pl.num_programs(0) - 1
    links = Links(*scratch[14:])
    sums = [
        Gather(links, ref.at[0], ref.at[1], scratch[7 * k : 7 * k + 7]) for k, ref in enumerate((up_ref, down_ref))
    ]
    leave = [links.local(g.column, out) for g, out in zip(sums, (up_out, down_out))]
    pair = i // 2
    to_core = pltpu.make_async_remote_copy(
        src_ref=give,
        dst_ref=got.at[pair],
        send_sem=links.send_sems.at[links.used + pair],
        recv_sem=links.recv_sems.at[links.used + pair],
        device_id=links.partner(CORE),
        device_id_type=pl.DeviceIdType.MESH,
    )

    @pl.when(i == 0)
    def _():
        links.greet([CORE, X, Y])
        for g in sums:
            g.start()
        low_t[...] = low_ref[...].T
        x_t[...] = x_ref[...].T
        enc_t[...] = enc_ref[...].T
        back_ref[...] = jnp.zeros_like(back_ref)
        enc_acc[...] = jnp.zeros_like(enc_acc)

    @pl.when(i == 1)
    def _():
        for g in sums:
            g.middle()

    rows, width = q_ref.shape[1:]
    n = k_ref.shape[1]
    hd = width // heads
    scale = 1.0 / math.sqrt(hd)
    w_query, w_keyval, w_out = w_ref.at[0, :, :width], w_ref.at[0, :, width : 3 * width], w_ref.at[0, :, 3 * width :]
    grads = dot_nn(low_ref[...], w_out[...]).astype(BF16)
    mixed_t = mt_ref[0]
    products = grads.T.astype(F32) * mixed_t.astype(F32)
    inner = [jnp.sum(products[h * hd : (h + 1) * hd, :], axis=0, keepdims=True) for h in range(heads)]
    scaled = q_ref[0] * jnp.asarray(scale, BF16)
    q_heads = [head_only(scaled, h, hd) for h in range(heads)]
    d_heads = [head_only(grads, h, hd) for h in range(heads)]
    lse = lse_ref[0]
    keys_t = k_ref[0].T
    dq = [None] * heads
    dkv = []
    for j in range(n // bk):
        span = slice(j * bk, (j + 1) * bk)
        keys = k_ref[0, span, :]
        values = v_ref[0, span, :]
        ok = ok_ref[span, :] > 0.0
        scores = [dot_nt(keys, q_heads[h]) for h in range(heads)]
        dprobs = [dot_nt(values, d_heads[h]) for h in range(heads)]
        dv_sum, dk_sum = None, None
        for h in range(heads):
            part = slice(h * hd, (h + 1) * hd)
            probs = jnp.exp(jnp.where(ok, scores[h], NEGATIVE) - lse[h : h + 1, :])
            ds = (probs * (dprobs[h] - inner[h])).astype(BF16)
            dv_h = dot_nn(probs.astype(BF16), d_heads[h])
            dk_h = dot_nn(ds, q_heads[h])
            dv_sum = dv_h if dv_sum is None else dv_sum + dv_h
            dk_sum = dk_h if dk_sum is None else dk_sum + dk_h
            dq_h = dot_nn(keys_t[part, span], ds)
            dq[h] = dq_h if dq[h] is None else dq[h] + dq_h
        block = jnp.concatenate([dk_sum.astype(BF16), dv_sum.astype(BF16)], 1)
        enc_acc[span, :] += dot_nt(block, w_keyval[...])
        dkv.append(block)
    dq = (jnp.concatenate(dq, 0) * scale).astype(BF16).T
    dkv = jnp.concatenate(dkv, 0)
    bq_ref[0] = jnp.sum(dq.astype(F32), axis=0, keepdims=True)
    bv_ref[0] = jnp.sum(dkv[:, width:].astype(F32), axis=0, keepdims=True)
    back_ref[...] += dot_nt(dq, w_query[...])

    @pl.when(i % 2 == 1)
    def _():
        to_core.wait_send()

    give[:, :width] = dot_nn(x_t[...], dq).astype(BF16)
    give[:, width : 3 * width] = dot_nn(enc_t[...], dkv).astype(BF16)
    give[:, 3 * width :] = dot_nn(low_t[...], mixed_t.T).astype(BF16)

    @pl.when(i % 2 == 0)
    def _():
        to_core.start()

    @pl.when(i % 2 == 1)
    def _():
        to_core.wait_recv()
        grad_ref[0] = (give[...].astype(F32) + got[pair].astype(F32)).astype(BF16)

    @pl.when(i == last)
    def _():
        enc_out[...] = enc_acc[...].astype(BF16)
        for g, copy in zip(sums, leave):
            g.end()
            copy.start()
        for copy in leave:
            copy.wait()


def cross_backward(ok, low, x, encoder, weights, queries, keys, values, mixed_t, lse, up_sum, down_sum, heads):
    count, model = x.shape
    n = encoder.shape[0]
    parts, _, columns = weights.shape
    width = columns // 4
    _, m, _, r, c = up_sum.shape

    def by_part(*shape):
        return pl.BlockSpec((1,) + shape, lambda i: (i ^ 1,) + (0,) * len(shape))

    return pl.pallas_call(
        functools.partial(cross_backward_kernel, heads=heads, bk=256),
        grid=(parts,),
        in_specs=[
            const((n, 1)),
            const((count, model)),
            const((count, model)),
            const((n, model)),
            by_part(model, columns),
            by_part(count, width),
            by_part(n, width),
            by_part(n, width),
            by_part(width, count),
            by_part(heads, count),
            ANY,
            ANY,
        ],
        out_specs=[
            const((count, model)),
            const((n, model)),
            pl.BlockSpec((1, model, columns), lambda i: (i // 2, 0, 0), pipeline_mode=pl.Buffered(1)),
            by_part(1, width),
            by_part(1, width),
            ANY,
            ANY,
        ],
        out_shape=[
            jax.ShapeDtypeStruct((count, model), F32),
            jax.ShapeDtypeStruct((n, model), BF16),
            jax.ShapeDtypeStruct((2, model, columns), BF16),
            jax.ShapeDtypeStruct((parts, 1, width), F32),
            jax.ShapeDtypeStruct((parts, 1, width), F32),
            jax.ShapeDtypeStruct((m, r, c), BF16),
            jax.ShapeDtypeStruct((m, r, c), BF16),
        ],
        scratch_shapes=[
            pltpu.VMEM((model, count), BF16),
            pltpu.VMEM((model, count), BF16),
            pltpu.VMEM((model, n), BF16),
            pltpu.VMEM((n, model), F32),
            pltpu.VMEM((model, columns), BF16),
            pltpu.VMEM((2, model, columns), BF16),
        ]
        + gather_scratch(m, r, c) * 2
        + link_scratch(10, 8),
        compiler_params=pltpu.CompilerParams(
            vmem_limit_bytes=60 * 2**20, collective_id=4, has_side_effects=True
        ),
        cost_estimate=pl.CostEstimate(
            flops=48 * parts * count * n * width,
            bytes_accessed=16 * parts * n * width,
            transcendentals=parts * count * n * heads,
        ),
        name="cross_backward",
    )(ok, low, x, encoder, weights, queries, keys, values, mixed_t, lse, up_sum, down_sum)


def swap(value, axis, distance):
    size = lax.axis_size(axis)
    return lax.ppermute(value, axis, [(i, i ^ distance) for i in range(size)])


def dp_distances():
    n = lax.axis_size("dp")
    found = []
    while n > 1:
        n //= 2
        found.append(n)
    return found


def add_low(a, b):
    return (a.astype(F32) + b.astype(F32)).astype(BF16)


def narrow(rows_low):
    member = lax.axis_index("tensor")
    count = rows_low.shape[0] // 4
    parts = [
        lax.dynamic_slice_in_dim(rows_low, (member ^ distance) * count, count, 0)
        for distance in range(4)
    ]
    far = add_low(parts[2], swap(parts[3], "tensor", 1))
    got = swap(far, "tensor", 2)
    near = parts[0].astype(F32) + swap(parts[1], "tensor", 1).astype(F32)
    return near + got.astype(F32)


def on_device(
    block_in,
    encoder_out,
    out_grad,
    bounds,
    enc_lengths,
    norm_params,
    w_qkv,
    w_self_out,
    w_cross_q,
    w_cross_kv,
    w_cross_out,
    w_up,
    w_down,
    biases,
    up_bias,
):
    member = lax.axis_index("tensor")
    groups_count = lax.axis_size("dp")
    groups = float(groups_count)
    width = w_cross_q.shape[1]
    hidden_width = w_up.shape[1]
    heads = H // 4
    own_rows, model_width = block_in.shape
    enc_rows = encoder_out.shape[0]
    w_rows = w_cross_q.shape[0]

    def block_of(vector, size, distance):
        return lax.dynamic_slice_in_dim(vector, (member ^ distance) * size, size)

    def blocks_placed(parts):
        size = parts[0].shape[0]
        out = jnp.zeros((4 * size,), F32)
        for distance, part in enumerate(parts):
            out = lax.dynamic_update_slice_in_dim(out, part, (member ^ distance) * size, 0)
        return out

    start_rows = block_in.astype(F32)
    first_in, enc_all, self_w, cross_column = start_gather(
        layer_norm(start_rows, norm_params[0, 0], norm_params[0, 1]).astype(BF16),
        encoder_out,
        jnp.concatenate([w_qkv.reshape(w_rows, 3 * width), w_self_out.T], axis=1),
        jnp.concatenate([w_cross_q, w_cross_kv.reshape(w_rows, 2 * width), w_cross_out.T], axis=1),
    )
    self_w = self_w.reshape(model_width, 4 * width)

    projected = dot_nn(first_in, self_w[:, : 3 * width])
    queries = (projected[:, :width] + block_of(biases[0], width, 0)).astype(BF16)
    key_rows = projected[:, width : 2 * width].astype(BF16)
    value_rows = (projected[:, 2 * width :] + block_of(biases[1], width, 0)).astype(BF16)
    self_safe = 1024
    self_mixed_t, self_lse, cross_w, ffn_column = self_forward(
        bounds,
        queries,
        key_rows,
        value_rows.T,
        cross_column,
        jnp.concatenate([w_up, w_down.T], axis=1),
        heads,
        self_safe,
    )
    cross_w = cross_w.reshape(4, model_width, 4 * width)
    self_out_w = self_w[:, 3 * width :]
    after_self = (
        start_rows
        + narrow(lax.dot_general(self_mixed_t, self_out_w, (((0,), (1,)), ((), ())), preferred_element_type=F32).astype(BF16))
        + biases[2]
    )

    ok = (jnp.arange(4 * enc_rows, dtype=jnp.int32) < enc_lengths[0]).astype(F32)[:, None]
    second_in = layer_norm(after_self, norm_params[1, 0], norm_params[1, 1]).astype(BF16)

    def all_blocks(vector, size):
        return jnp.stack([block_of(vector, size, d) for d in range(4)])[:, None]

    cross_q, cross_k, cross_v, cross_mixed_t, cross_lse, after_cross, third_in, ffn_w = cross_forward(
        ok,
        second_in,
        enc_all,
        cross_w,
        all_blocks(biases[3], width),
        all_blocks(biases[4], width),
        after_self,
        biases[5:6],
        norm_params[2],
        ffn_column,
        heads,
    )

    output, cross_rows_grad, cross_low, ffn_sums, up_sum, down_sum, bias_up_parts = feed_forward(
        third_in,
        out_grad,
        ffn_w.reshape(4, model_width, 2 * hidden_width),
        all_blocks(up_bias, hidden_width),
        after_cross,
        biases[6:7],
        norm_params[2],
    )

    by_shard = (2, groups_count // 2, 2, w_rows, hidden_width)
    second_grad, enc_terms, cross_sum, bias_cq_parts, bias_cv_parts, up_column, down_column = cross_backward(
        ok,
        cross_low,
        second_in,
        enc_all,
        cross_w,
        cross_q,
        cross_k,
        cross_v,
        cross_mixed_t,
        cross_lse,
        up_sum.reshape(by_shard),
        down_sum.reshape(by_shard),
        heads,
    )
    cross_sum = cross_sum.reshape(2, groups_count // 2, 2, w_rows, 4 * width)
    self_wide, self_rows_grad, self_sums, summed_down, diagonal = middle(
        second_grad, after_self, cross_rows_grad, norm_params[1], down_column, cross_sum
    )
    bias_cq_grad = blocks_placed([bias_cq_parts[d, 0] for d in range(4)])
    bias_cv_grad = blocks_placed([bias_cv_parts[d, 0] for d in range(4)])
    bias_up_grad = blocks_placed([bias_up_parts[d, 0] for d in range(4)])

    early = jnp.concatenate(
        [
            self_sums[:3],
            ffn_sums[:4],
            jnp.stack([bias_cq_grad, bias_cv_grad]),
            bias_up_grad.reshape(-1, model_width),
        ]
    )
    early = jnp.pad(early, ((0, -early.shape[0] % 8), (0, 0)))

    self_dq, self_dk, self_dv, summed_up, summed_cross, encoder_grad, early = self_backward(
        bounds,
        queries,
        key_rows,
        value_rows,
        key_rows.T,
        self_wide,
        self_out_w,
        self_mixed_t,
        self_lse,
        up_column,
        cross_sum,
        diagonal,
        enc_terms,
        early,
        heads,
        self_safe,
    )
    grad_so_t = lax.dot_general(
        self_wide, self_mixed_t, (((0,), (1,)), ((), ())), preferred_element_type=F32
    ).astype(BF16)

    def only_own(part):
        out = jnp.zeros((model_width,), F32)
        return lax.dynamic_update_slice_in_dim(out, part, member * width, 0)

    late = jnp.zeros((8, model_width), F32)
    late = late.at[2].set(only_own(jnp.sum(self_dq.astype(F32), axis=0)))
    late = late.at[3].set(only_own(jnp.sum(self_dv.astype(F32), axis=0)))
    input_grad, summed_self, late = tail(
        self_dq,
        self_dk,
        self_dv,
        self_w,
        first_in,
        grad_so_t,
        block_in,
        self_rows_grad,
        norm_params[0],
        late,
    )
    norm_total = jnp.stack([late[0], late[1], early[0], early[1], early[3], early[4]]).reshape(
        norm_params.shape
    )
    bias_total = jnp.stack([late[2], late[3], early[2], early[7], early[8], early[5], early[6]])
    up_total = early[9 : 9 + up_bias.shape[0] // model_width].reshape(-1)
    scale = 1.0 / groups
    return (
        output,
        input_grad,
        encoder_grad,
        norm_total * scale,
        summed_self[:, : 3 * width].reshape(w_qkv.shape) * scale,
        summed_self[:, 3 * width :].T * scale,
        summed_cross[:, :width] * scale,
        summed_cross[:, width : 3 * width].reshape(w_cross_kv.shape) * scale,
        summed_cross[:, 3 * width :].T * scale,
        summed_up * scale,
        summed_down.T * scale,
        bias_total * scale,
        up_total * scale,
    )


def solution(mesh):
    rows = P(("dp", "tensor"), None)
    placed = (
        rows,
        rows,
        rows,
        P("dp", None),
        P("dp"),
        P(),
        P("dp", None, "tensor"),
        P("tensor", "dp"),
        P("dp", "tensor"),
        P("dp", None, "tensor"),
        P("tensor", "dp"),
        P("dp", "tensor"),
        P("tensor", "dp"),
        P(),
        P(),
    )
    return jax.shard_map(
        on_device,
        mesh=mesh,
        in_specs=placed,
        out_specs=(
            rows,
            rows,
            rows,
            P(),
            P("dp", None, "tensor"),
            P("tensor", "dp"),
            P("dp", "tensor"),
            P("dp", None, "tensor"),
            P("tensor", "dp"),
            P("dp", "tensor"),
            P("tensor", "dp"),
            P(),
            P(),
        ),
        check_vma=False,
    )
```

```python
import functools
import math

import jax
import jax.numpy as jnp
from jax import lax
from jax.experimental import pallas as pl
from jax.experimental.pallas import tpu as pltpu
from jax.sharding import PartitionSpec as P

H = 16
EPSILON = 1e-05
NEGATIVE = -1e30
F32 = jnp.float32
BF16 = jnp.bfloat16
VMEM_LIMIT = 56 * 2**20


def dot_nt(a, b):
    return lax.dot_general(a, b, (((1,), (1,)), ((), ())), preferred_element_type=F32)


def dot_nn(a, b):
    return lax.dot_general(a, b, (((1,), (0,)), ((), ())), preferred_element_type=F32)


def dot_tn(a, b):
    return lax.dot_general(a, b, (((0,), (0,)), ((), ())), preferred_element_type=F32)


def layer_norm(inputs, gain_row, shift_row):
    center = inputs - jnp.mean(inputs, axis=-1, keepdims=True)
    spread = jnp.mean(center * center, axis=-1, keepdims=True)
    return center * lax.rsqrt(spread + EPSILON) * gain_row + shift_row


def gelu_slope(values_in):
    normal_cdf = 0.5 * (1.0 + lax.erf(values_in * (1.0 / math.sqrt(2.0))))
    density = jnp.exp(-0.5 * values_in * values_in) * (1.0 / math.sqrt(2.0 * math.pi))
    return normal_cdf + values_in * density


def head_only(x, h, size):
    lane = lax.broadcasted_iota(jnp.int32, x.shape, 1)
    return jnp.where((lane >= h * size) & (lane < (h + 1) * size), x, jnp.zeros_like(x))


def self_bad(b_ref, q_start, k_start, bq, bk, causal):
    qi = q_start + lax.broadcasted_iota(jnp.int32, (1, bq), 1)
    kj = k_start + lax.broadcasted_iota(jnp.int32, (bk, 1), 0)
    bad = (qi >= b_ref[0, 1]) & ((kj >= b_ref[0, 0]) & (kj < b_ref[0, 1]))
    if causal:
        bad = bad | (kj > qi)
    return bad


def over_keys(i, bq, bk, safe, block, between=()):
    diagonal = i * (bq // bk)

    def visit(j, c):
        for at_i, at_j, action in between:
            pl.when((i == at_i) & (j == at_j))(action)

        @pl.when(j < safe // bk)
        def _():
            block(j, "none")

        @pl.when(j >= safe // bk)
        def _():
            block(j, "segment")

        return c

    lax.fori_loop(0, diagonal, visit, 0)
    for step in range(bq // bk):
        block(diagonal + step, "causal")


CORE = ("tensor", 1)
X = ("tensor", 2)
Y = ("dp", 1)
ANY = pl.BlockSpec(memory_space=pl.ANY)


class Links:
    def __init__(self, send_sems, recv_sems, local_sems):
        self.dp = lax.axis_index("dp")
        self.tensor = lax.axis_index("tensor")
        self.send_sems, self.recv_sems, self.local_sems = send_sems, recv_sems, local_sems
        self.used = 0
        self.used_local = 0

    def partner(self, way):
        axis, distance = way
        if axis == "tensor":
            return (self.dp, self.tensor ^ distance)
        return (self.dp ^ distance, self.tensor)

    def greet(self, ways):
        barrier = pltpu.get_barrier_semaphore()
        for way in ways:
            pl.semaphore_signal(
                barrier, inc=1, device_id=self.partner(way), device_id_type=pl.DeviceIdType.MESH
            )
        pl.semaphore_wait(barrier, len(ways))

    def copy(self, source, target, way):
        k = self.used
        self.used += 1
        return pltpu.make_async_remote_copy(
            src_ref=source,
            dst_ref=target,
            send_sem=self.send_sems.at[k],
            recv_sem=self.recv_sems.at[k],
            device_id=self.partner(way),
            device_id_type=pl.DeviceIdType.MESH,
        )

    def local(self, source, target):
        k = self.used_local
        self.used_local += 1
        return pltpu.make_async_copy(source, target, self.local_sems.at[k])


def link_scratch(copies, local):
    return [
        pltpu.SemaphoreType.DMA((copies,)),
        pltpu.SemaphoreType.DMA((copies,)),
        pltpu.SemaphoreType.DMA((local,)),
    ]


def z_distances(n):
    found = []
    m = n // 2
    while m > 1:
        m //= 2
        found.append(m)
    return found


def z_ways(n):
    return [("dp", 2 * distance) for distance in z_distances(n)]


def column_stages(links, shard, column, n):
    z = links.dp // 2
    held = [z]
    stages = []
    for distance in z_distances(n):
        stages.append(
            [
                (
                    links.copy(shard if k == 0 else column.at[index], column.at[index], ("dp", 2 * distance)),
                    index ^ distance,
                )
                for k, index in enumerate(held)
            ]
        )
        held = held + [index ^ distance for index in held]
    return stages


class Spread:
    def __init__(self, links, column, whole):
        y = links.dp % 2
        half = column.shape[0] // 2
        low, high = pl.ds(0, half), pl.ds(half, half)
        near, near_core, far, far_core = (whole.at[k] for k in range(4))
        self.own = links.local(column, near.at[:, y])
        self.first = [
            links.copy(column, near.at[:, y], Y),
            links.copy(column, far.at[:, y], X),
        ]
        self.core = [links.copy(column, near_core.at[:, y], CORE)]
        self.second = [
            links.copy(near.at[low, 1 - y], far.at[low, 1 - y], X),
            links.copy(far.at[high, y], far.at[high, y], Y),
        ]
        self.core_second = [
            links.copy(near.at[:, 1 - y], near_core.at[:, 1 - y], CORE),
            links.copy(far.at[:, y], far_core.at[:, y], CORE),
        ]
        self.core_third = [links.copy(far.at[:, 1 - y], far_core.at[:, 1 - y], CORE)]

    def start(self):
        self.own.start()
        for copy in self.first + self.core:
            copy.start()

    def middle(self):
        for copy in self.first:
            copy.wait_recv()
        for copy in self.second + self.core_second:
            copy.start()

    def end(self):
        for copy in self.second:
            copy.wait_recv()
        for copy in self.core_third:
            copy.start()
        self.own.wait()
        for copy in self.first + self.second:
            copy.wait_send()
        for copy in self.core + self.core_second + self.core_third:
            copy.wait()


def add_to(total_ref, other_ref):
    def one(k, c):
        total_ref[k] = (total_ref[k].astype(F32) + other_ref[k].astype(F32)).astype(BF16)
        return c

    lax.fori_loop(0, total_ref.shape[0], one, 0)


class Gather:
    def __init__(self, links, near, far, from_x, from_y, buffers):
        y = links.dp % 2
        self.column, self.over_y, self.over_x, self.add_y, self.add_x, self.sum_y, self.sum_x = buffers
        m = self.column.shape[0]
        low, high = pl.ds(0, m // 2), pl.ds(m // 2, m - m // 2)
        self.loads = [
            links.local(near.at[low, 1 - y], self.over_y),
            links.local(far.at[high, y], self.over_x),
            links.local(from_x, self.add_y),
            links.local(from_y, self.add_x),
            links.local(near.at[:, y], self.column),
        ]
        self.first = [
            links.copy(far.at[low, y], self.sum_x.at[low], X),
            links.copy(near.at[high, 1 - y], self.sum_y.at[high], Y),
        ]
        self.second = [
            links.copy(self.over_x, self.sum_x.at[high], X),
            links.copy(self.over_y, self.sum_y.at[low], Y),
        ]

    def start(self):
        for copy in self.first + self.loads:
            copy.start()

    def middle(self):
        for copy in self.loads:
            copy.wait()
        add_to(self.over_x, self.add_x)
        add_to(self.over_y, self.add_y)
        for copy in self.second:
            copy.start()

    def end(self):
        for copy in self.first + self.second:
            copy.wait_recv()
        add_to(self.column, self.sum_y)
        add_to(self.column, self.sum_x)
        for copy in self.first + self.second:
            copy.wait_send()


def gather_scratch(m, r, c):
    whole = pltpu.VMEM((m, r, c), BF16)
    half = pltpu.VMEM((m // 2, r, c), BF16)
    return [whole] + [half] * 4 + [whole] * 2


class GatherLast:
    def __init__(self, links, near, far, diagonal, buffers):
        y = links.dp % 2
        self.column, self.over_x, self.diagonal, self.sum_y, self.sum_x = buffers
        self.loads = [
            links.local(far.at[:, y], self.over_x),
            links.local(diagonal, self.diagonal),
            links.local(near.at[:, y], self.column),
        ]
        self.over_y = links.copy(near.at[:, 1 - y], self.sum_y, Y)
        self.along_x = links.copy(self.over_x, self.sum_x, X)

    def start(self):
        self.over_y.start()
        for copy in self.loads:
            copy.start()

    def middle(self):
        for copy in self.loads:
            copy.wait()
        add_to(self.over_x, self.diagonal)
        self.along_x.start()

    def end(self):
        self.over_y.wait_recv()
        self.along_x.wait_recv()
        add_to(self.column, self.sum_y)
        add_to(self.column, self.sum_x)
        self.over_y.wait_send()
        self.along_x.wait_send()


class Collect:
    def __init__(self, links, column, slots):
        z = links.dp // 2
        self.column, self.slots, self.z = column, slots, z
        m = column.shape[0]
        distances = z_distances(2 * m)[::-1]
        self.stages = []
        first = 0
        for step, distance in enumerate(distances):
            kept = [0]
            for other in distances[step + 1 :]:
                kept = kept + [k ^ other for k in kept]
            self.stages.append(
                [
                    (links.copy(column.at[z ^ distance ^ k], slots.at[first + i], ("dp", 2 * distance)), first + i, z ^ k)
                    for i, k in enumerate(kept)
                ]
            )
            first += len(kept)

    def start(self, step):
        for copy, _, _ in self.stages[step]:
            copy.start()

    def finish(self, step):
        for copy, slot, index in self.stages[step]:
            copy.wait_recv()
            self.column[index] = (self.column[index].astype(F32) + self.slots[slot].astype(F32)).astype(BF16)

    def drain(self):
        for stage in self.stages:
            for copy, _, _ in stage:
                copy.wait_send()


class RowSum:
    def __init__(self, links, terms, buffers):
        self.near, self.far, self.got_near, self.got_far, self.got_x = buffers
        count = self.near.shape[0]

        def rows(distance):
            start = pl.multiple_of((links.tensor ^ distance) * count, count)
            return terms.at[pl.ds(start, count)]

        self.loads = [links.local(rows(0), self.near), links.local(rows(2), self.far)]
        self.core = [links.copy(rows(3), self.got_far, CORE), links.copy(rows(1), self.got_near, CORE)]
        self.over_x = links.copy(self.far, self.got_x, X)

    def start(self):
        for copy in self.loads[::-1] + self.core:
            copy.start()

    def middle(self):
        self.loads[1].wait()
        self.core[0].wait_recv()

        def add(rows):
            self.far[rows, :] = (self.far[rows, :].astype(F32) + self.got_far[rows, :].astype(F32)).astype(BF16)

        by_rows(self.far.shape[0], 64, add)
        self.over_x.start()

    def end(self):
        self.loads[0].wait()
        self.core[1].wait_recv()
        self.over_x.wait_recv()
        for copy in self.core + [self.over_x]:
            copy.wait_send()

    def total(self, rows):
        return self.near[rows, :].astype(F32) + self.got_near[rows, :].astype(F32) + self.got_x[rows, :].astype(F32)


def row_sum_scratch(count, width):
    return [pltpu.VMEM((count, width), BF16)] * 5


class Everywhere:
    def __init__(self, links, held, slots, n):
        self.held, self.slots = held, slots
        ways = everywhere_ways(n)
        self.copies = [links.copy(held.at[k], slots.at[k], way) for k, way in enumerate(ways)]

    def start(self, step):
        self.copies[step].start()

    def finish(self, step):
        self.copies[step].wait()
        self.held[step + 1] = self.held[step] + self.slots[step]


def everywhere_ways(n):
    return [CORE, X, Y] + z_ways(n)


def everywhere_scratch(k, c, n):
    steps = len(everywhere_ways(n))
    return [pltpu.VMEM((steps + 1, k, c), F32), pltpu.VMEM((steps, k, c), F32)]


def middle_kernel(
    back_ref, rows_ref, grad_ref, norm_ref, down_ref, cross_ref,
    wide_out, grad_out, sums_ref, down_out, diagonal_out,
    low, column, slots, send_sems, recv_sems, local_sems, *, n
):
    links = Links(send_sems, recv_sems, local_sems)
    count = low.shape[0]
    load = links.local(down_ref, column)
    load.start()
    collect = Collect(links, column, slots)

    def place(distance):
        return wide_out.at[pl.ds(pl.multiple_of((links.tensor ^ distance) * count, count), count)]

    own = links.local(low, place(0))
    half = count // 2
    parts = [pl.ds(0, half), pl.ds(half, half)]
    over_x = [links.copy(low.at[part], place(0).at[part], X) for part in parts]
    over_core = links.copy(low, place(0), CORE)
    onward = [links.copy(place(2).at[part], place(2).at[part], CORE) for part in parts]
    over_y = links.copy(cross_ref.at[1, :, 1 - links.dp % 2], diagonal_out, Y)
    links.greet([CORE, X, Y] + z_ways(n))
    over_y.start()
    load.wait()
    collect.start(0)
    sums_ref[...] = jnp.zeros_like(sums_ref)

    def norm_back(rows):
        incoming = back_ref[rows, :]
        rows_grad, gain_terms = norm_rows_back(rows_ref[rows, :], incoming, norm_ref[0:1, :])
        rows_grad = rows_grad + grad_ref[rows, :]
        rounded = rows_grad.astype(BF16)
        grad_out[rows, :] = rows_grad
        low[rows, :] = rounded
        for k, terms in enumerate((gain_terms, incoming, rounded.astype(F32))):
            sums_ref[k : k + 1, :] += jnp.sum(terms, axis=0, keepdims=True)

    for part, copy in zip(parts, over_x):
        by_rows(half, 64, lambda rows, part=part: norm_back(pl.ds(pl.multiple_of(part.start + rows.start, 64), 64)))
        copy.start()
    own.start()
    over_core.start()
    for step in range(len(collect.stages) - 1):
        collect.finish(step)
        collect.start(step + 1)
    for copy, later in zip(over_x, onward):
        copy.wait_recv()
        later.start()
    collect.finish(len(collect.stages) - 1)
    down_out[...] = column[collect.z].astype(F32)
    collect.drain()
    own.wait()
    for copy in over_x:
        copy.wait_send()
    over_core.wait()
    for copy in onward:
        copy.wait()
    over_y.wait()


def middle(back, rows, grad, norm, down_column, cross_sum):
    n = lax.axis_size("dp")
    count, width = rows.shape
    m, r, c = down_column.shape
    vmem = pl.BlockSpec(memory_space=pltpu.VMEM)
    return pl.pallas_call(
        functools.partial(middle_kernel, n=n),
        in_specs=[vmem, vmem, vmem, vmem, ANY, ANY],
        out_specs=[ANY, vmem, vmem, vmem, ANY],
        out_shape=[
            jax.ShapeDtypeStruct((4 * count, width), BF16),
            jax.ShapeDtypeStruct((count, width), F32),
            jax.ShapeDtypeStruct((8, width), F32),
            jax.ShapeDtypeStruct((r, c), F32),
            jax.ShapeDtypeStruct((m, r, cross_sum.shape[4]), BF16),
        ],
        scratch_shapes=[
            pltpu.VMEM((count, width), BF16),
            pltpu.VMEM((m, r, c), BF16),
            pltpu.VMEM((m, r, c), BF16),
        ]
        + link_scratch(6 + m, 2),
        compiler_params=pltpu.CompilerParams(
            vmem_limit_bytes=VMEM_LIMIT, collective_id=6, has_side_effects=True
        ),
        cost_estimate=pl.CostEstimate(flops=0, bytes_accessed=100 * 2**20, transcendentals=0),
        name="middle",
    )(back, rows, grad, norm, down_column, cross_sum)


def tail_kernel(
    dq_ref, dk_ref, dv_ref, w_ref, first_ref, so_ref, rows_ref, grad_ref, norm_ref, late_ref,
    grad_out, weights_out, late_out, give, acc, weights, *scratch, n, step_rows
):
    links = Links(*scratch[-3:])
    near, far, got_near, got_far, got_x = scratch[:5]
    columns, gots, slots = scratch[5:7], scratch[7:9], scratch[9:11]
    held, late_slots = scratch[11:13]
    count, model = near.shape
    width = dq_ref.shape[1]
    y = links.dp % 2
    c = columns[0].shape[2]
    m, _, r, _ = weights.shape
    half = count // 2
    parts = [pl.ds(0, half), pl.ds(half, half)]
    core_far = links.copy(give.at[0], got_far, CORE)
    core_near = links.copy(give.at[1], got_near, CORE)
    over_x = [links.copy(far.at[part], got_x.at[part], X) for part in parts]
    over_y, collects = [], []
    for k, (column, got, slot) in enumerate(zip(columns, gots, slots)):
        over_y.append(links.copy(weights.at[:, 1 - y, :, pl.ds(k * c, c)], got, Y))
        collects.append(Collect(links, column, slot))
    late = Everywhere(links, held, late_slots, n)
    links.greet(everywhere_ways(n))

    def terms(distance, target):
        base = (links.tensor ^ distance) * count

        def one(rows):
            there = pl.ds(pl.multiple_of(base + rows.start, 128), 128)
            total = dot_nt(dq_ref[there, :], w_ref[:, :width])
            total = total + dot_nt(dk_ref[there, :], w_ref[:, width : 2 * width])
            target[rows, :] = (total + dot_nt(dv_ref[there, :], w_ref[:, 2 * width : 3 * width])).astype(BF16)

        by_rows(count, 128, one)

    terms(3, give.at[0])
    core_far.start()
    terms(2, far)
    core_far.wait_recv()
    for part, copy in zip(parts, over_x):

        def add(rows, part=part):
            there = pl.ds(pl.multiple_of(part.start + rows.start, 64), 64)
            far[there, :] = (far[there, :].astype(F32) + got_far[there, :].astype(F32)).astype(BF16)

        by_rows(half, 64, add)
        copy.start()

    acc[...] = jnp.zeros_like(acc)

    def products(rows):
        source = first_ref[rows, :].T
        for k, ref in enumerate((dq_ref, dk_ref, dv_ref)):
            acc[:, k * width : (k + 1) * width] += dot_nn(source, ref[rows, :])

    by_rows(dq_ref.shape[0], step_rows, products)
    for k in range(2 * m):
        span = slice(k * r, (k + 1) * r)
        weights[k // 2, k % 2, :, : 3 * width] = acc[span, :].astype(BF16)
        weights[k // 2, k % 2, :, 3 * width :] = so_ref[span, :]
    over_y[0].start()
    terms(1, give.at[1])
    core_near.start()
    terms(0, near)
    for k in range(2):
        columns[k][...] = weights[:, y, :, k * c : (k + 1) * c]
    for k in range(2):
        over_y[k].wait_recv()
        if k == 0:
            over_y[1].start()
        add_to(columns[k], gots[k])
        collects[k].start(0)
    stages = len(collects[0].stages)
    held[0] = late_ref[...]
    core_near.wait_recv()
    for part, copy in zip(parts, over_x):
        copy.wait_recv()

        def norm_back(rows, part=part):
            rows = pl.ds(pl.multiple_of(part.start + rows.start, 64), 64)
            incoming = near[rows, :].astype(F32) + got_near[rows, :].astype(F32) + got_x[rows, :].astype(F32)
            rows_grad, gain_terms = norm_rows_back(rows_ref[rows, :].astype(F32), incoming, norm_ref[0:1, :])
            grad_out[rows, :] = rows_grad + grad_ref[rows, :]
            held[0, 0:1, :] += jnp.sum(gain_terms, axis=0, keepdims=True)
            held[0, 1:2, :] += jnp.sum(incoming, axis=0, keepdims=True)

        by_rows(half, 64, norm_back)
        if part is parts[0]:
            for step in range(stages - 1):
                for k in range(2):
                    collects[k].finish(step)
                    collects[k].start(step + 1)
    steps = len(late.copies)
    for step in range(steps):
        late.start(step)
        if step == 1:
            for k in range(2):
                collects[k].finish(stages - 1)
                weights_out[:, k * c : (k + 1) * c] = columns[k][collects[k].z].astype(F32)
        late.finish(step)
    late_out[...] = held[steps]
    for copy in over_x + over_y + [core_near, core_far]:
        copy.wait_send()
    for collect in collects:
        collect.drain()


def tail(dq, dk, dv, w, first, so_grad, rows, grad, norm, late):
    n = lax.axis_size("dp")
    count, model = rows.shape
    total, width = dq.shape
    m, r, c = n // 2, model // n, 4 * width
    vmem = pl.BlockSpec(memory_space=pltpu.VMEM)
    part = pltpu.VMEM((m, r, c // 2), BF16)
    return pl.pallas_call(
        functools.partial(tail_kernel, n=n, step_rows=512),
        in_specs=[vmem] * 10,
        out_specs=[vmem, vmem, vmem],
        out_shape=[
            jax.ShapeDtypeStruct((count, model), F32),
            jax.ShapeDtypeStruct((r, c), F32),
            jax.ShapeDtypeStruct(late.shape, F32),
        ],
        scratch_shapes=[
            pltpu.VMEM((2, count, model), BF16),
            pltpu.VMEM((model, 3 * width), F32),
            pltpu.VMEM((m, 2, r, c), BF16),
        ]
        + row_sum_scratch(count, model)
        + [part] * 6
        + everywhere_scratch(*late.shape, n)
        + link_scratch(6 + 2 * m + len(everywhere_ways(n)), 1),
        compiler_params=pltpu.CompilerParams(
            vmem_limit_bytes=VMEM_LIMIT, collective_id=7, has_side_effects=True
        ),
        cost_estimate=pl.CostEstimate(flops=0, bytes_accessed=100 * 2**20, transcendentals=0),
        name="tail",
    )(dq, dk, dv, w, first, so_grad, rows, grad, norm, late)


def start_kernel(
    rows_ref, enc_ref, self_ref, cross_ref, rows_out, enc_out, self_out, cross_out, send_sems, recv_sems, local_sems, *, n
):
    links = Links(send_sems, recv_sems, local_sems)
    member, z, y = links.tensor, links.dp // 2, links.dp % 2
    links.greet([CORE, X, Y] + z_ways(n))

    def place(ref, index, size):
        return ref.at[pl.ds(pl.multiple_of(index * size, size), size)]

    groups = [(rows_ref, rows_out, rows_ref.shape[0]), (enc_ref, enc_out, enc_ref.shape[0])]
    local, started, arrived = [], [], []
    for source, target, size in groups:
        local.append(links.local(source, place(target, member, size)))
    local.append(links.local(self_ref, self_out.at[z, y]))
    local.append(links.local(cross_ref, cross_out.at[z]))
    for copy in local:
        copy.start()

    def go(copy):
        copy.start()
        started.append(copy)
        return copy

    def got(copy):
        copy.wait_recv()
        arrived.append(copy)

    along_x = [go(links.copy(source, place(target, member, size), X)) for source, target, size in groups]
    go(links.copy(self_ref, self_out.at[z, y], Y))
    for source, target, size in groups:
        go(links.copy(source, place(target, member, size), CORE))
    self_stages = column_stages(links, self_ref, self_out.at[:, y], n)
    cross_stages = column_stages(links, cross_ref, cross_out, n)
    for self_stage in self_stages:
        for copy, _ in self_stage:
            go(copy)
        for copy, index in self_stage:
            got(copy)
            go(links.copy(self_out.at[index, y], self_out.at[index, y], Y))
        if self_stage is self_stages[0]:
            for copy, _ in cross_stages[0]:
                go(copy)
    for cross_stage, later in zip(cross_stages, cross_stages[1:]):
        for copy, _ in cross_stage:
            got(copy)
        for copy, _ in later:
            go(copy)
    for copy, (_, target, size) in zip(along_x, groups):
        got(copy)
        there = place(target, member ^ 2, size)
        go(links.copy(there, there, CORE))
    for copy in local:
        copy.wait()
    for copy in started:
        copy.wait_send()
        if not any(copy is other for other in arrived):
            copy.wait_recv()


def start_gather(rows_low, enc_low, self_shard, cross_shard):
    n = lax.axis_size("dp")
    r, c = self_shard.shape
    copies = 3 * n + 8
    return pl.pallas_call(
        functools.partial(start_kernel, n=n),
        in_specs=[ANY] * 4,
        out_specs=[ANY] * 4,
        out_shape=[
            jax.ShapeDtypeStruct((4 * rows_low.shape[0], rows_low.shape[1]), BF16),
            jax.ShapeDtypeStruct((4 * enc_low.shape[0], enc_low.shape[1]), BF16),
            jax.ShapeDtypeStruct((n // 2, 2, r, c), BF16),
            jax.ShapeDtypeStruct((n // 2,) + cross_shard.shape, BF16),
        ],
        scratch_shapes=link_scratch(copies, 4),
        compiler_params=pltpu.CompilerParams(collective_id=0, has_side_effects=True),
        cost_estimate=pl.CostEstimate(flops=0, bytes_accessed=100 * 2**20, transcendentals=0),
        name="start_gather",
    )(rows_low, enc_low, self_shard, cross_shard)


def self_forward_kernel(
    b_ref, q_ref, k_ref, vt_ref, column_ref, shard_ref,
    ot_ref, lse_ref, whole, next_column,
    m_s, l_s, acc, send_sems, recv_sems, local_sems, *, bk, heads, safe, n
):
    i = pl.program_id(0)
    last = pl.num_programs(0) - 1
    bq, width = q_ref.shape
    links = Links(send_sems, recv_sems, local_sems)
    spread = Spread(links, column_ref, whole)
    keep = links.local(shard_ref, next_column.at[links.dp // 2])
    stages = column_stages(links, shard_ref, next_column, n)

    @pl.when(i == 0)
    def _():
        links.greet([CORE, X, Y] + z_ways(n))
        spread.start()
        keep.start()
        for copy, _ in stages[0]:
            copy.start()

    @pl.when(i == last)
    def _():
        spread.middle()
        for k in range(1, len(stages)):
            for copy, _ in stages[k - 1]:
                copy.wait_recv()
            for copy, _ in stages[k]:
                copy.start()

    hd = width // heads
    m_s[...] = jnp.full_like(m_s, NEGATIVE)
    l_s[...] = jnp.zeros_like(l_s)
    acc[...] = jnp.zeros_like(acc)
    scaled = q_ref[...] * jnp.asarray(1.0 / math.sqrt(hd), BF16)
    q_heads = [head_only(scaled, h, hd) for h in range(heads)]

    def block(j, mode):
        rows = pl.ds(pl.multiple_of(j * bk, bk), bk)
        keys = k_ref[rows, :]
        m_old = m_s[...]
        l_old = l_s[...]
        scores = [dot_nt(keys, q_heads[h]) for h in range(heads)]
        if mode != "none":
            bad = self_bad(b_ref, i * bq, j * bk, bq, bk, mode == "causal")
            scores = [jnp.where(bad, NEGATIVE, s) for s in scores]
        m_out, l_out, a_out = [], [], []
        for h in range(heads):
            part = slice(h * hd, (h + 1) * hd)
            m_new = jnp.maximum(m_old[h : h + 1, :], jnp.max(scores[h], axis=0, keepdims=True))
            shrink = jnp.exp(m_old[h : h + 1, :] - m_new)
            expos = jnp.exp(scores[h] - m_new)
            l_out.append(l_old[h : h + 1, :] * shrink + jnp.sum(expos, axis=0, keepdims=True))
            m_out.append(m_new)
            a_out.append(acc[part, :] * shrink + dot_nn(vt_ref[part, rows], expos.astype(BF16)))
        m_s[...] = jnp.concatenate(m_out, 0)
        l_s[...] = jnp.concatenate(l_out, 0)
        for h in range(heads):
            acc[h * hd : (h + 1) * hd, :] = a_out[h]

    over_keys(i, bq, bk, safe, block)
    inverse = 1.0 / l_s[...]
    for h in range(heads):
        part = slice(h * hd, (h + 1) * hd)
        ot_ref[part, :] = (acc[part, :] * inverse[h : h + 1, :]).astype(BF16)
    lse_ref[...] = m_s[...] + jnp.log(l_s[...])

    @pl.when(i == last)
    def _():
        spread.end()
        keep.wait()
        for k, stage in enumerate(stages):
            for copy, _ in stage:
                copy.wait_send()
                if k == len(stages) - 1:
                    copy.wait_recv()


def self_forward(bounds, queries, keys, values_t, column, shard, heads, safe):
    n, width = queries.shape
    bq = bk = 512
    dp = lax.axis_size("dp")
    m, r, c = column.shape
    return pl.pallas_call(
        functools.partial(self_forward_kernel, bk=bk, heads=heads, safe=safe, n=dp),
        grid=(n // bq,),
        in_specs=[
            pl.BlockSpec(memory_space=pltpu.SMEM),
            pl.BlockSpec((bq, width), lambda i: (i, 0)),
            pl.BlockSpec((n, width), lambda i: (0, 0)),
            pl.BlockSpec((width, n), lambda i: (0, 0)),
            ANY,
            ANY,
        ],
        out_specs=[
            pl.BlockSpec((width, bq), lambda i: (0, i)),
            pl.BlockSpec((heads, bq), lambda i: (0, i)),
        ]
        + [ANY] * 2,
        out_shape=[
            jax.ShapeDtypeStruct((width, n), BF16),
            jax.ShapeDtypeStruct((heads, n), F32),
        ]
        + [jax.ShapeDtypeStruct((4, m, 2, r, c), BF16)]
        + [jax.ShapeDtypeStruct((m,) + shard.shape, BF16)],
        scratch_shapes=[
            pltpu.VMEM((heads, bq), F32),
            pltpu.VMEM((heads, bq), F32),
            pltpu.VMEM((width, bq), F32),
        ]
        + link_scratch(8 + m, 2),
        compiler_params=pltpu.CompilerParams(
            vmem_limit_bytes=VMEM_LIMIT, collective_id=1, has_side_effects=True
        ),
        cost_estimate=pl.CostEstimate(
            flops=12 * n * n * width, bytes_accessed=8 * n * width, transcendentals=n * n * heads // 2
        ),
        name="self_forward",
    )(bounds, queries, keys, values_t, column, shard)


def self_backward_kernel(
    b_ref, q_ref, k_ref, v_ref, kt_ref, wide_ref, w_ref, mt_ref, lse_ref,
    up_ref, cross_ref, diagonal_ref, enc_ref,
    dq_ref, dk_ref, dv_ref, up_out, cross_out, enc_out, dka, dva, dqa, *scratch, bk, heads, safe, n
):
    i = pl.program_id(0)
    links = Links(*scratch[-3:])
    cross = GatherLast(links, cross_ref.at[0], cross_ref.at[1], diagonal_ref, scratch[:5])
    cross_z = Collect(links, cross.column, scratch[5])
    up_column = scratch[6]
    up_z = Collect(links, up_column, scratch[7])
    load = links.local(up_ref, up_column)
    enc = RowSum(links, enc_ref, scratch[8:13])
    stages = len(up_z.stages)

    @pl.when(i == 0)
    def _():
        links.greet(everywhere_ways(n))
        cross.start()
        enc.start()
        load.start()
        load.wait()
        up_z.start(0)
        dka[...] = jnp.zeros_like(dka)
        dva[...] = jnp.zeros_like(dva)

    @pl.when(i == 1)
    def _():
        cross.middle()

    @pl.when(i == 2)
    def _():
        for step in range(stages - 1):
            up_z.finish(step)
            up_z.start(step + 1)

    def sum_cross():
        cross.end()
        cross_z.start(0)
        enc.middle()

    def next_cross():
        for step in range(stages - 1):
            cross_z.finish(step)
            cross_z.start(step + 1)

    bq, width = q_ref.shape
    hd = width // heads
    scale = 1.0 / math.sqrt(hd)
    grads = dot_nn(wide_ref[...], w_ref[...]).astype(BF16)
    products = grads.T.astype(F32) * mt_ref[...].astype(F32)
    inner = [jnp.sum(products[h * hd : (h + 1) * hd, :], axis=0, keepdims=True) for h in range(heads)]
    scaled = q_ref[...] * jnp.asarray(scale, BF16)
    q_heads = [head_only(scaled, h, hd) for h in range(heads)]
    d_heads = [head_only(grads, h, hd) for h in range(heads)]
    lse = lse_ref[...]
    dqa[...] = jnp.zeros_like(dqa)

    def block(j, mode):
        rows = pl.ds(pl.multiple_of(j * bk, bk), bk)
        keys = k_ref[rows, :]
        values = v_ref[rows, :]
        scores = [dot_nt(keys, q_heads[h]) for h in range(heads)]
        dprobs = [dot_nt(values, d_heads[h]) for h in range(heads)]
        if mode != "none":
            bad = self_bad(b_ref, i * bq, j * bk, bq, bk, mode == "causal")
            scores = [jnp.where(bad, NEGATIVE, s) for s in scores]
        dv_sum, dk_sum = None, None
        for h in range(heads):
            part = slice(h * hd, (h + 1) * hd)
            probs = jnp.exp(scores[h] - lse[h : h + 1, :])
            ds = (probs * (dprobs[h] - inner[h])).astype(BF16)
            dv_h = dot_nn(probs.astype(BF16), d_heads[h])
            dk_h = dot_nn(ds, q_heads[h])
            dv_sum = dv_h if dv_sum is None else dv_sum + dv_h
            dk_sum = dk_h if dk_sum is None else dk_sum + dk_h
            dqa[part, :] += dot_nn(kt_ref[part, rows], ds)
        dva[rows, :] += dv_sum
        dka[rows, :] += dk_sum

    over_keys(i, bq, bk, safe, block, [(3, 2, sum_cross), (4, 2, next_cross)])
    dq_ref[...] = (dqa[...] * scale).astype(BF16).T

    @pl.when(i == pl.num_programs(0) - 1)
    def _():
        dk_ref[...] = dka[...].astype(BF16)
        dv_ref[...] = dva[...].astype(BF16)
        up_z.finish(stages - 1)
        up_out[...] = up_column[up_z.z].astype(F32)
        cross_z.finish(stages - 1)
        cross_out[...] = cross.column[cross_z.z].astype(F32)
        enc.end()

        def store(rows):
            enc_out[rows, :] = enc.total(rows)

        by_rows(enc_out.shape[0], 64, store)
        up_z.drain()
        cross_z.drain()


def self_backward(
    bounds, queries, keys, values, keys_t, wide, w_out, mixed_t, lse,
    up_column, cross_sum, diagonal, enc_terms, heads, safe
):
    n, width = queries.shape
    model = wide.shape[1]
    dp = lax.axis_size("dp")
    m, r, c = up_column.shape
    cross_c = cross_sum.shape[4]
    enc_shape = (enc_terms.shape[0] // 4, enc_terms.shape[1])
    bq = bk = 512
    some = pl.BlockSpec((bq, width), lambda i: (i, 0))
    return pl.pallas_call(
        functools.partial(self_backward_kernel, bk=bk, heads=heads, safe=safe, n=dp),
        grid=(n // bq,),
        in_specs=[
            pl.BlockSpec(memory_space=pltpu.SMEM),
            some,
            const((n, width)),
            const((n, width)),
            const((width, n)),
            pl.BlockSpec((bq, model), lambda i: (i, 0)),
            const((model, width)),
            pl.BlockSpec((width, bq), lambda i: (0, i)),
            pl.BlockSpec((heads, bq), lambda i: (0, i)),
        ]
        + [ANY] * 4,
        out_specs=[some, const((n, width)), const((n, width))]
        + [const((r, c)), const((r, cross_c)), const(enc_shape)],
        out_shape=[
            jax.ShapeDtypeStruct((n, width), BF16),
            jax.ShapeDtypeStruct((n, width), BF16),
            jax.ShapeDtypeStruct((n, width), BF16),
            jax.ShapeDtypeStruct((r, c), F32),
            jax.ShapeDtypeStruct((r, cross_c), F32),
            jax.ShapeDtypeStruct(enc_shape, F32),
        ],
        scratch_shapes=[
            pltpu.VMEM((n, width), F32),
            pltpu.VMEM((n, width), F32),
            pltpu.VMEM((width, bq), F32),
        ]
        + [pltpu.VMEM((m, r, cross_c), BF16)] * 6
        + [pltpu.VMEM((m, r, c), BF16)] * 2
        + row_sum_scratch(*enc_shape)
        + link_scratch(5 + 2 * m, 6),
        compiler_params=pltpu.CompilerParams(
            vmem_limit_bytes=VMEM_LIMIT, collective_id=5, has_side_effects=True
        ),
        cost_estimate=pl.CostEstimate(
            flops=24 * n * n * width, bytes_accessed=16 * n * width, transcendentals=n * n * heads // 2
        ),
        name="self_backward",
    )(bounds, queries, keys, values, keys_t, wide, w_out, mixed_t, lse, up_column, cross_sum, diagonal, enc_terms)


def const(shape):
    return pl.BlockSpec(shape, lambda *_: (0,) * len(shape), pipeline_mode=pl.Buffered(1))


def normalized(rows):
    center = rows - jnp.mean(rows, axis=-1, keepdims=True)
    scale = lax.rsqrt(jnp.mean(center * center, axis=-1, keepdims=True) + EPSILON)
    return center * scale, scale


def norm_rows_back(rows, incoming, gain):
    xhat, scale = normalized(rows)
    e = incoming * gain
    inner = jnp.mean(e * xhat, axis=-1, keepdims=True)
    return scale * (e - jnp.mean(e, axis=-1, keepdims=True) - xhat * inner), incoming * xhat


def by_rows(count, step, body):
    def one(k, c):
        body(pl.ds(pl.multiple_of(k * step, step), step))
        return c

    lax.fori_loop(0, count // step, one, 0)


def cross_forward_kernel(
    ok_ref, x_ref, enc_ref, w_ref, bq_ref, bv_ref, rows_ref, shift_ref, norm_ref, column_ref,
    q_out, k_out, v_out, ot_ref, lse_ref, after_ref, third_ref, whole, send_sems, recv_sems, local_sems, *, heads
):
    i = pl.program_id(0)
    last = pl.num_programs(0) - 1
    links = Links(send_sems, recv_sems, local_sems)
    spread = Spread(links, column_ref, whole)

    @pl.when(i == 0)
    def _():
        links.greet([CORE, X, Y])
        spread.start()
        after_ref[...] = rows_ref[...] + shift_ref[...]

    width = q_out.shape[2]
    hd = width // heads
    query = (dot_nn(x_ref[...], w_ref[0, :, :width]) + bq_ref[0]).astype(BF16)
    key_value = dot_nn(enc_ref[...], w_ref[0, :, width : 3 * width])
    keys = key_value[:, :width].astype(BF16)
    values = (key_value[:, width:] + bv_ref[0]).astype(BF16)
    q_out[0] = query
    k_out[0] = keys
    v_out[0] = values
    values_t = values.T
    scaled = query * jnp.asarray(1.0 / math.sqrt(hd), BF16)
    ok = ok_ref[...] > 0.0
    scores = [dot_nt(keys, head_only(scaled, h, hd)) for h in range(heads)]
    mixed = []
    for h in range(heads):
        part = slice(h * hd, (h + 1) * hd)
        s = jnp.where(ok, scores[h], NEGATIVE)
        largest = jnp.max(s, axis=0, keepdims=True)
        expos = jnp.exp(s - largest)
        total = jnp.sum(expos, axis=0, keepdims=True)
        mixed.append((dot_nn(values_t[part, :], expos.astype(BF16)) * (1.0 / total)).astype(BF16))
        ot_ref[0, part, :] = mixed[h]
        lse_ref[0, h : h + 1, :] = largest + jnp.log(total)
    after_ref[...] += dot_nt(jnp.concatenate(mixed, 0).T, w_ref[0, :, 3 * width :])

    @pl.when(i == last)
    def _():
        spread.middle()

        def norm(rows):
            xhat, _ = normalized(after_ref[rows, :])
            third_ref[rows, :] = (xhat * norm_ref[0:1, :] + norm_ref[1:2, :]).astype(BF16)

        by_rows(after_ref.shape[0], 128, norm)
        spread.end()


def cross_forward(ok, x, encoder, weights, q_shift, v_shift, rows, shift, norm, column, heads):
    count, model = x.shape
    n = encoder.shape[0]
    parts, _, columns = weights.shape
    width = columns // 4
    m, r, c = column.shape

    def by_part(*shape):
        return pl.BlockSpec((1,) + shape, lambda i: (i,) + (0,) * len(shape))

    return pl.pallas_call(
        functools.partial(cross_forward_kernel, heads=heads),
        grid=(parts,),
        in_specs=[
            const((n, 1)),
            const((count, model)),
            const((n, model)),
            by_part(model, columns),
            by_part(1, width),
            by_part(1, width),
            const((count, model)),
            const((1, model)),
            const((2, model)),
            ANY,
        ],
        out_specs=[
            by_part(count, width),
            by_part(n, width),
            by_part(n, width),
            by_part(width, count),
            by_part(heads, count),
            const((count, model)),
            const((count, model)),
            ANY,
        ],
        out_shape=[
            jax.ShapeDtypeStruct((parts, count, width), BF16),
            jax.ShapeDtypeStruct((parts, n, width), BF16),
            jax.ShapeDtypeStruct((parts, n, width), BF16),
            jax.ShapeDtypeStruct((parts, width, count), BF16),
            jax.ShapeDtypeStruct((parts, heads, count), F32),
            jax.ShapeDtypeStruct((count, model), F32),
            jax.ShapeDtypeStruct((count, model), BF16),
            jax.ShapeDtypeStruct((4, m, 2, r, c), BF16),
        ],
        scratch_shapes=link_scratch(8, 1),
        compiler_params=pltpu.CompilerParams(
            vmem_limit_bytes=VMEM_LIMIT, collective_id=2, has_side_effects=True
        ),
        cost_estimate=pl.CostEstimate(
            flops=24 * parts * count * n * width,
            bytes_accessed=8 * parts * n * width,
            transcendentals=parts * count * n * heads,
        ),
        name="cross_forward",
    )(ok, x, encoder, weights, q_shift, v_shift, rows, shift, norm, column)


def feed_forward_kernel(
    x_ref, dy_ref, up_ref, down_ref, b_ref, after_ref, shift_ref, norm_ref,
    out_ref, rows_out, low_out, sums_ref, gup_ref, gdown_ref, bias_ref, from_x, from_y,
    xt_ref, dyt_ref, back_ref, give, got, diagonal, send_sems, recv_sems, local_sems, *, chunks
):
    s = pl.program_id(0)
    links = Links(send_sems, recv_sems, local_sems)
    turn = s // chunks
    chunk = s % chunks
    pair = turn // 2
    slot = pair * chunks + chunk
    theirs = turn % 2 == 0
    y = links.dp % 2
    m, r = diagonal.shape[1], diagonal.shape[2]
    low, high = pl.ds(0, m // 2), pl.ds(m // 2, m - m // 2)
    links.used = 2 * chunks
    across = [
        links.copy(diagonal.at[:, low], from_x, X),
        links.copy(diagonal.at[:, high], from_y, Y),
    ]
    to_core = pltpu.make_async_remote_copy(
        src_ref=give.at[chunk],
        dst_ref=got.at[slot],
        send_sem=send_sems.at[slot],
        recv_sem=recv_sems.at[slot],
        device_id=links.partner(CORE),
        device_id_type=pl.DeviceIdType.MESH,
    )

    @pl.when(s == 0)
    def _():
        links.greet([CORE, X, Y])
        out_ref[...] = after_ref[...] + shift_ref[...]
        back_ref[...] = jnp.zeros_like(back_ref)
        xt_ref[...] = x_ref[...].T
        dyt_ref[...] = dy_ref[...].T
        sums_ref[...] = jnp.zeros_like(sums_ref)

    pre_act = dot_nn(x_ref[...], up_ref[0]) + b_ref[0]
    hidden_grad = dot_nn(dy_ref[...], down_ref[0])
    normal_cdf = 0.5 * (1.0 + lax.erf(pre_act * (1.0 / math.sqrt(2.0))))
    density = jnp.exp(-0.5 * pre_act * pre_act) * (1.0 / math.sqrt(2.0 * math.pi))
    hidden = (pre_act * normal_cdf).astype(BF16)
    pre_grad = (hidden_grad * (normal_cdf + pre_act * density)).astype(BF16)
    bias_ref[0] = jnp.sum(pre_grad.astype(F32), axis=0, keepdims=True)

    @pl.when(turn % 2 == 1)
    def _():
        to_core.wait_send()

    give[chunk, 0] = dot_nn(xt_ref[...], pre_grad).astype(BF16)
    give[chunk, 1] = dot_nn(dyt_ref[...], hidden).astype(BF16)
    out_ref[...] += dot_nt(hidden, down_ref[0])
    back_ref[...] += dot_nt(pre_grad, up_ref[0])

    @pl.when(theirs)
    def _():
        to_core.start()

    @pl.when(jnp.logical_not(theirs))
    def _():
        to_core.wait_recv()
        gup_ref[0] = (give[chunk, 0].astype(F32) + got[slot, 0].astype(F32)).astype(BF16)
        gdown_ref[0] = (give[chunk, 1].astype(F32) + got[slot, 1].astype(F32)).astype(BF16)

    for k in range(chunks):

        @pl.when(s == chunks + k)
        def _():
            def keep(z, carry):
                rows = pl.ds(pl.multiple_of((2 * z + 1 - y) * r, r), r)
                size = gup_ref.shape[2]
                diagonal[0, z, :, k * size : (k + 1) * size] = gup_ref[0, rows, :]
                diagonal[1, z, :, k * size : (k + 1) * size] = gdown_ref[0, rows, :]
                return carry

            lax.fori_loop(0, m, keep, 0)
            if k == chunks - 1:
                for copy in across:
                    copy.start()

    @pl.when(s == pl.num_programs(0) - 1)
    def _():
        def norm_back(rows):
            third = back_ref[rows, :]
            upstream = dy_ref[rows, :].astype(F32)
            rows_grad, gain_terms = norm_rows_back(after_ref[rows, :], third, norm_ref[0:1, :])
            rows_grad = rows_grad + upstream
            low = rows_grad.astype(BF16)
            rows_out[rows, :] = rows_grad
            low_out[rows, :] = low
            for k, terms in enumerate((gain_terms, third, low.astype(F32), upstream)):
                sums_ref[k : k + 1, :] += jnp.sum(terms, axis=0, keepdims=True)

        by_rows(x_ref.shape[0], 128, norm_back)
        for copy in across:
            copy.wait()


def feed_forward(x, dy, weights, bias, after, shift, norm):
    rows, width = x.shape
    hidden = weights.shape[2] // 2
    size = min(512, hidden)
    chunks = hidden // size

    n = lax.axis_size("dp")
    m, r = n // 2, width // n

    def block(s):
        return 3 - s // chunks

    def placed(s):
        turn = s // chunks
        return (1 - turn // 2, 0, (s % chunks) * (turn % 2))

    rows_spec = const((rows, width))
    grad_spec = pl.BlockSpec((1, width, size), placed)
    bias_spec = pl.BlockSpec((1, 1, size), lambda s: (block(s), 0, s % chunks))
    return pl.pallas_call(
        functools.partial(feed_forward_kernel, chunks=chunks),
        grid=(4 * chunks,),
        in_specs=[
            rows_spec,
            rows_spec,
            pl.BlockSpec((1, width, size), lambda s: (block(s), 0, s % chunks)),
            pl.BlockSpec((1, width, size), lambda s: (block(s), 0, chunks + s % chunks)),
            bias_spec,
            rows_spec,
            const((1, width)),
            const((2, width)),
        ],
        out_specs=[rows_spec, rows_spec, rows_spec, const((8, width)), grad_spec, grad_spec, bias_spec, ANY, ANY],
        out_shape=[
            jax.ShapeDtypeStruct((rows, width), F32),
            jax.ShapeDtypeStruct((rows, width), F32),
            jax.ShapeDtypeStruct((rows, width), BF16),
            jax.ShapeDtypeStruct((8, width), F32),
            jax.ShapeDtypeStruct((2, width, hidden), BF16),
            jax.ShapeDtypeStruct((2, width, hidden), BF16),
            jax.ShapeDtypeStruct((4, 1, hidden), F32),
            jax.ShapeDtypeStruct((2, m // 2, r, hidden), BF16),
            jax.ShapeDtypeStruct((2, m - m // 2, r, hidden), BF16),
        ],
        scratch_shapes=[
            pltpu.VMEM((width, rows), BF16),
            pltpu.VMEM((width, rows), BF16),
            pltpu.VMEM((rows, width), F32),
            pltpu.VMEM((chunks, 2, width, size), BF16),
            pltpu.VMEM((2 * chunks, 2, width, size), BF16),
            pltpu.VMEM((2, m, r, hidden), BF16),
        ]
        + link_scratch(2 * chunks + 2, 1),
        compiler_params=pltpu.CompilerParams(
            vmem_limit_bytes=VMEM_LIMIT, collective_id=3, has_side_effects=True
        ),
        cost_estimate=pl.CostEstimate(
            flops=48 * rows * width * hidden, bytes_accessed=40 * 2**20, transcendentals=8 * rows * hidden
        ),
        name="feed_forward",
    )(x, dy, weights, weights, bias, after, shift, norm)


def cross_backward_kernel(
    ok_ref, low_ref, x_ref, enc_ref, w_ref, q_ref, k_ref, v_ref, mt_ref, lse_ref, up_ref, down_ref, from_x, from_y,
    back_ref, enc_out, grad_ref, bq_ref, bv_ref, up_out, down_out,
    low_t, x_t, enc_t, enc_acc, give, got, *scratch, heads, bk
):
    i = pl.program_id(0)
    last = pl.num_programs(0) - 1
    links = Links(*scratch[14:])
    sums = [
        Gather(links, ref.at[0], ref.at[1], from_x.at[k], from_y.at[k], scratch[7 * k : 7 * k + 7])
        for k, ref in enumerate((up_ref, down_ref))
    ]
    leave = [links.local(g.column, out) for g, out in zip(sums, (up_out, down_out))]
    pair = i // 2
    to_core = pltpu.make_async_remote_copy(
        src_ref=give,
        dst_ref=got.at[pair],
        send_sem=links.send_sems.at[links.used + pair],
        recv_sem=links.recv_sems.at[links.used + pair],
        device_id=links.partner(CORE),
        device_id_type=pl.DeviceIdType.MESH,
    )

    @pl.when(i == 0)
    def _():
        links.greet([CORE, X, Y])
        for g in sums:
            g.start()
        low_t[...] = low_ref[...].T
        x_t[...] = x_ref[...].T
        enc_t[...] = enc_ref[...].T
        back_ref[...] = jnp.zeros_like(back_ref)
        enc_acc[...] = jnp.zeros_like(enc_acc)

    @pl.when(i == 1)
    def _():
        for g in sums:
            g.middle()

    rows, width = q_ref.shape[1:]
    n = k_ref.shape[1]
    hd = width // heads
    scale = 1.0 / math.sqrt(hd)
    w_query, w_keyval, w_out = w_ref.at[0, :, :width], w_ref.at[0, :, width : 3 * width], w_ref.at[0, :, 3 * width :]
    grads = dot_nn(low_ref[...], w_out[...]).astype(BF16)
    mixed_t = mt_ref[0]
    products = grads.T.astype(F32) * mixed_t.astype(F32)
    inner = [jnp.sum(products[h * hd : (h + 1) * hd, :], axis=0, keepdims=True) for h in range(heads)]
    scaled = q_ref[0] * jnp.asarray(scale, BF16)
    q_heads = [head_only(scaled, h, hd) for h in range(heads)]
    d_heads = [head_only(grads, h, hd) for h in range(heads)]
    lse = lse_ref[0]
    keys_t = k_ref[0].T
    dq = [None] * heads
    dkv = []
    for j in range(n // bk):
        span = slice(j * bk, (j + 1) * bk)
        keys = k_ref[0, span, :]
        values = v_ref[0, span, :]
        ok = ok_ref[span, :] > 0.0
        scores = [dot_nt(keys, q_heads[h]) for h in range(heads)]
        dprobs = [dot_nt(values, d_heads[h]) for h in range(heads)]
        dv_sum, dk_sum = None, None
        for h in range(heads):
            part = slice(h * hd, (h + 1) * hd)
            probs = jnp.exp(jnp.where(ok, scores[h], NEGATIVE) - lse[h : h + 1, :])
            ds = (probs * (dprobs[h] - inner[h])).astype(BF16)
            dv_h = dot_nn(probs.astype(BF16), d_heads[h])
            dk_h = dot_nn(ds, q_heads[h])
            dv_sum = dv_h if dv_sum is None else dv_sum + dv_h
            dk_sum = dk_h if dk_sum is None else dk_sum + dk_h
            dq_h = dot_nn(keys_t[part, span], ds)
            dq[h] = dq_h if dq[h] is None else dq[h] + dq_h
        block = jnp.concatenate([dk_sum.astype(BF16), dv_sum.astype(BF16)], 1)
        enc_acc[span, :] += dot_nt(block, w_keyval[...])
        dkv.append(block)
    dq = (jnp.concatenate(dq, 0) * scale).astype(BF16).T
    dkv = jnp.concatenate(dkv, 0)
    bq_ref[0] = jnp.sum(dq.astype(F32), axis=0, keepdims=True)
    bv_ref[0] = jnp.sum(dkv[:, width:].astype(F32), axis=0, keepdims=True)
    back_ref[...] += dot_nt(dq, w_query[...])

    @pl.when(i % 2 == 1)
    def _():
        to_core.wait_send()

    give[:, :width] = dot_nn(x_t[...], dq).astype(BF16)
    give[:, width : 3 * width] = dot_nn(enc_t[...], dkv).astype(BF16)
    give[:, 3 * width :] = dot_nn(low_t[...], mixed_t.T).astype(BF16)

    @pl.when(i % 2 == 0)
    def _():
        to_core.start()

    @pl.when(i % 2 == 1)
    def _():
        to_core.wait_recv()
        grad_ref[0] = (give[...].astype(F32) + got[pair].astype(F32)).astype(BF16)

    @pl.when(i == last)
    def _():
        enc_out[...] = enc_acc[...].astype(BF16)
        for g, copy in zip(sums, leave):
            g.end()
            copy.start()
        for copy in leave:
            copy.wait()


def cross_backward(
    ok, low, x, encoder, weights, queries, keys, values, mixed_t, lse, up_sum, down_sum, from_x, from_y, heads
):
    count, model = x.shape
    n = encoder.shape[0]
    parts, _, columns = weights.shape
    width = columns // 4
    _, m, _, r, c = up_sum.shape

    def by_part(*shape):
        return pl.BlockSpec((1,) + shape, lambda i: (i ^ 1,) + (0,) * len(shape))

    return pl.pallas_call(
        functools.partial(cross_backward_kernel, heads=heads, bk=256),
        grid=(parts,),
        in_specs=[
            const((n, 1)),
            const((count, model)),
            const((count, model)),
            const((n, model)),
            by_part(model, columns),
            by_part(count, width),
            by_part(n, width),
            by_part(n, width),
            by_part(width, count),
            by_part(heads, count),
            ANY,
            ANY,
            ANY,
            ANY,
        ],
        out_specs=[
            const((count, model)),
            const((n, model)),
            pl.BlockSpec((1, model, columns), lambda i: (i // 2, 0, 0), pipeline_mode=pl.Buffered(1)),
            by_part(1, width),
            by_part(1, width),
            ANY,
            ANY,
        ],
        out_shape=[
            jax.ShapeDtypeStruct((count, model), F32),
            jax.ShapeDtypeStruct((n, model), BF16),
            jax.ShapeDtypeStruct((2, model, columns), BF16),
            jax.ShapeDtypeStruct((parts, 1, width), F32),
            jax.ShapeDtypeStruct((parts, 1, width), F32),
            jax.ShapeDtypeStruct((m, r, c), BF16),
            jax.ShapeDtypeStruct((m, r, c), BF16),
        ],
        scratch_shapes=[
            pltpu.VMEM((model, count), BF16),
            pltpu.VMEM((model, count), BF16),
            pltpu.VMEM((model, n), BF16),
            pltpu.VMEM((n, model), F32),
            pltpu.VMEM((model, columns), BF16),
            pltpu.VMEM((2, model, columns), BF16),
        ]
        + gather_scratch(m, r, c) * 2
        + link_scratch(10, 12),
        compiler_params=pltpu.CompilerParams(
            vmem_limit_bytes=60 * 2**20, collective_id=4, has_side_effects=True
        ),
        cost_estimate=pl.CostEstimate(
            flops=48 * parts * count * n * width,
            bytes_accessed=16 * parts * n * width,
            transcendentals=parts * count * n * heads,
        ),
        name="cross_backward",
    )(ok, low, x, encoder, weights, queries, keys, values, mixed_t, lse, up_sum, down_sum, from_x, from_y)


def swap(value, axis, distance):
    size = lax.axis_size(axis)
    return lax.ppermute(value, axis, [(i, i ^ distance) for i in range(size)])


def dp_distances():
    n = lax.axis_size("dp")
    found = []
    while n > 1:
        n //= 2
        found.append(n)
    return found


def add_low(a, b):
    return (a.astype(F32) + b.astype(F32)).astype(BF16)


def narrow(rows_low):
    member = lax.axis_index("tensor")
    count = rows_low.shape[0] // 4
    parts = [
        lax.dynamic_slice_in_dim(rows_low, (member ^ distance) * count, count, 0)
        for distance in range(4)
    ]
    far = add_low(parts[2], swap(parts[3], "tensor", 1))
    got = swap(far, "tensor", 2)
    near = parts[0].astype(F32) + swap(parts[1], "tensor", 1).astype(F32)
    return near + got.astype(F32)


def on_device(
    block_in,
    encoder_out,
    out_grad,
    bounds,
    enc_lengths,
    norm_params,
    w_qkv,
    w_self_out,
    w_cross_q,
    w_cross_kv,
    w_cross_out,
    w_up,
    w_down,
    biases,
    up_bias,
):
    member = lax.axis_index("tensor")
    groups_count = lax.axis_size("dp")
    groups = float(groups_count)
    width = w_cross_q.shape[1]
    hidden_width = w_up.shape[1]
    heads = H // 4
    own_rows, model_width = block_in.shape
    enc_rows = encoder_out.shape[0]
    w_rows = w_cross_q.shape[0]

    def block_of(vector, size, distance):
        return lax.dynamic_slice_in_dim(vector, (member ^ distance) * size, size)

    def blocks_placed(parts):
        size = parts[0].shape[0]
        out = jnp.zeros((4 * size,), F32)
        for distance, part in enumerate(parts):
            out = lax.dynamic_update_slice_in_dim(out, part, (member ^ distance) * size, 0)
        return out

    start_rows = block_in.astype(F32)
    first_in, enc_all, self_w, cross_column = start_gather(
        layer_norm(start_rows, norm_params[0, 0], norm_params[0, 1]).astype(BF16),
        encoder_out,
        jnp.concatenate([w_qkv.reshape(w_rows, 3 * width), w_self_out.T], axis=1),
        jnp.concatenate([w_cross_q, w_cross_kv.reshape(w_rows, 2 * width), w_cross_out.T], axis=1),
    )
    self_w = self_w.reshape(model_width, 4 * width)

    projected = dot_nn(first_in, self_w[:, : 3 * width])
    queries = (projected[:, :width] + block_of(biases[0], width, 0)).astype(BF16)
    key_rows = projected[:, width : 2 * width].astype(BF16)
    value_rows = (projected[:, 2 * width :] + block_of(biases[1], width, 0)).astype(BF16)
    self_safe = 1024
    self_mixed_t, self_lse, cross_w, ffn_column = self_forward(
        bounds,
        queries,
        key_rows,
        value_rows.T,
        cross_column,
        jnp.concatenate([w_up, w_down.T], axis=1),
        heads,
        self_safe,
    )
    cross_w = cross_w.reshape(4, model_width, 4 * width)
    self_out_w = self_w[:, 3 * width :]
    after_self = (
        start_rows
        + narrow(lax.dot_general(self_mixed_t, self_out_w, (((0,), (1,)), ((), ())), preferred_element_type=F32).astype(BF16))
        + biases[2]
    )

    ok = (jnp.arange(4 * enc_rows, dtype=jnp.int32) < enc_lengths[0]).astype(F32)[:, None]
    second_in = layer_norm(after_self, norm_params[1, 0], norm_params[1, 1]).astype(BF16)

    def all_blocks(vector, size):
        return jnp.stack([block_of(vector, size, d) for d in range(4)])[:, None]

    cross_q, cross_k, cross_v, cross_mixed_t, cross_lse, after_cross, third_in, ffn_w = cross_forward(
        ok,
        second_in,
        enc_all,
        cross_w,
        all_blocks(biases[3], width),
        all_blocks(biases[4], width),
        after_self,
        biases[5:6],
        norm_params[2],
        ffn_column,
        heads,
    )

    output, cross_rows_grad, cross_low, ffn_sums, up_sum, down_sum, bias_up_parts, from_x, from_y = feed_forward(
        third_in,
        out_grad,
        ffn_w.reshape(4, model_width, 2 * hidden_width),
        all_blocks(up_bias, hidden_width),
        after_cross,
        biases[6:7],
        norm_params[2],
    )

    by_shard = (2, groups_count // 2, 2, w_rows, hidden_width)
    second_grad, enc_terms, cross_sum, bias_cq_parts, bias_cv_parts, up_column, down_column = cross_backward(
        ok,
        cross_low,
        second_in,
        enc_all,
        cross_w,
        cross_q,
        cross_k,
        cross_v,
        cross_mixed_t,
        cross_lse,
        up_sum.reshape(by_shard),
        down_sum.reshape(by_shard),
        from_x,
        from_y,
        heads,
    )
    cross_sum = cross_sum.reshape(2, groups_count // 2, 2, w_rows, 4 * width)
    self_wide, self_rows_grad, self_sums, summed_down, diagonal = middle(
        second_grad, after_self, cross_rows_grad, norm_params[1], down_column, cross_sum
    )
    bias_cq_grad = blocks_placed([bias_cq_parts[d, 0] for d in range(4)])
    bias_cv_grad = blocks_placed([bias_cv_parts[d, 0] for d in range(4)])
    bias_up_grad = blocks_placed([bias_up_parts[d, 0] for d in range(4)])

    self_dq, self_dk, self_dv, summed_up, summed_cross, encoder_grad = self_backward(
        bounds,
        queries,
        key_rows,
        value_rows,
        key_rows.T,
        self_wide,
        self_out_w,
        self_mixed_t,
        self_lse,
        up_column,
        cross_sum,
        diagonal,
        enc_terms,
        heads,
        self_safe,
    )
    grad_so_t = lax.dot_general(
        self_wide, self_mixed_t, (((0,), (1,)), ((), ())), preferred_element_type=F32
    ).astype(BF16)

    def only_own(part):
        out = jnp.zeros((model_width,), F32)
        return lax.dynamic_update_slice_in_dim(out, part, member * width, 0)

    vectors = jnp.concatenate(
        [
            jnp.zeros((2, model_width), F32),
            self_sums[:2],
            ffn_sums[:2],
            jnp.stack(
                [
                    only_own(jnp.sum(self_dq.astype(F32), axis=0)),
                    only_own(jnp.sum(self_dv.astype(F32), axis=0)),
                    self_sums[2],
                    bias_cq_grad,
                    bias_cv_grad,
                    ffn_sums[2],
                    ffn_sums[3],
                ]
            ),
            bias_up_grad.reshape(-1, model_width),
        ]
    )
    vectors = jnp.pad(vectors, ((0, -vectors.shape[0] % 8), (0, 0)))
    input_grad, summed_self, vectors = tail(
        self_dq,
        self_dk,
        self_dv,
        self_w,
        first_in,
        grad_so_t,
        block_in,
        self_rows_grad,
        norm_params[0],
        vectors,
    )
    norm_total = vectors[:6].reshape(norm_params.shape)
    bias_total = vectors[6:13]
    up_total = vectors[13 : 13 + up_bias.shape[0] // model_width].reshape(-1)
    scale = 1.0 / groups
    return (
        output,
        input_grad,
        encoder_grad,
        norm_total * scale,
        summed_self[:, : 3 * width].reshape(w_qkv.shape) * scale,
        summed_self[:, 3 * width :].T * scale,
        summed_cross[:, :width] * scale,
        summed_cross[:, width : 3 * width].reshape(w_cross_kv.shape) * scale,
        summed_cross[:, 3 * width :].T * scale,
        summed_up * scale,
        summed_down.T * scale,
        bias_total * scale,
        up_total * scale,
    )


def solution(mesh):
    rows = P(("dp", "tensor"), None)
    placed = (
        rows,
        rows,
        rows,
        P("dp", None),
        P("dp"),
        P(),
        P("dp", None, "tensor"),
        P("tensor", "dp"),
        P("dp", "tensor"),
        P("dp", None, "tensor"),
        P("tensor", "dp"),
        P("dp", "tensor"),
        P("tensor", "dp"),
        P(),
        P(),
    )
    return jax.shard_map(
        on_device,
        mesh=mesh,
        in_specs=placed,
        out_specs=(
            rows,
            rows,
            rows,
            P(),
            P("dp", None, "tensor"),
            P("tensor", "dp"),
            P("dp", "tensor"),
            P("dp", None, "tensor"),
            P("tensor", "dp"),
            P("dp", "tensor"),
            P("tensor", "dp"),
            P(),
            P(),
        ),
        check_vma=False,
    )
```

```python
import functools
import math

import jax
import jax.numpy as jnp
from jax import lax
from jax.experimental import pallas as pl
from jax.experimental.pallas import tpu as pltpu
from jax.sharding import PartitionSpec as P

H = 16
EPSILON = 1e-05
NEGATIVE = -1e30
F32 = jnp.float32
BF16 = jnp.bfloat16
VMEM_LIMIT = 56 * 2**20


def dot_nt(a, b):
    return lax.dot_general(a, b, (((1,), (1,)), ((), ())), preferred_element_type=F32)


def dot_nn(a, b):
    return lax.dot_general(a, b, (((1,), (0,)), ((), ())), preferred_element_type=F32)


def dot_tn(a, b):
    return lax.dot_general(a, b, (((0,), (0,)), ((), ())), preferred_element_type=F32)


def layer_norm(inputs, gain_row, shift_row):
    center = inputs - jnp.mean(inputs, axis=-1, keepdims=True)
    spread = jnp.mean(center * center, axis=-1, keepdims=True)
    return center * lax.rsqrt(spread + EPSILON) * gain_row + shift_row


def gelu_slope(values_in):
    normal_cdf = 0.5 * (1.0 + lax.erf(values_in * (1.0 / math.sqrt(2.0))))
    density = jnp.exp(-0.5 * values_in * values_in) * (1.0 / math.sqrt(2.0 * math.pi))
    return normal_cdf + values_in * density


def head_only(x, h, size):
    lane = lax.broadcasted_iota(jnp.int32, x.shape, 1)
    return jnp.where((lane >= h * size) & (lane < (h + 1) * size), x, jnp.zeros_like(x))


def self_bad(b_ref, q_start, k_start, bq, bk, causal):
    qi = q_start + lax.broadcasted_iota(jnp.int32, (1, bq), 1)
    kj = k_start + lax.broadcasted_iota(jnp.int32, (bk, 1), 0)
    bad = (qi >= b_ref[0, 1]) & ((kj >= b_ref[0, 0]) & (kj < b_ref[0, 1]))
    if causal:
        bad = bad | (kj > qi)
    return bad


def over_keys(i, bq, bk, safe, block, between=()):
    diagonal = i * (bq // bk)

    def visit(j, c):
        for at_i, at_j, action in between:
            pl.when((i == at_i) & (j == at_j))(action)

        @pl.when(j < safe // bk)
        def _():
            block(j, "none")

        @pl.when(j >= safe // bk)
        def _():
            block(j, "segment")

        return c

    lax.fori_loop(0, diagonal, visit, 0)
    for step in range(bq // bk):
        block(diagonal + step, "causal")


CORE = ("tensor", 1)
X = ("tensor", 2)
Y = ("dp", 1)
ANY = pl.BlockSpec(memory_space=pl.ANY)


class Links:
    def __init__(self, send_sems, recv_sems, local_sems):
        self.dp = lax.axis_index("dp")
        self.tensor = lax.axis_index("tensor")
        self.send_sems, self.recv_sems, self.local_sems = send_sems, recv_sems, local_sems
        self.used = 0
        self.used_local = 0

    def partner(self, way):
        axis, distance = way
        if axis == "tensor":
            return (self.dp, self.tensor ^ distance)
        return (self.dp ^ distance, self.tensor)

    def greet(self, ways):
        barrier = pltpu.get_barrier_semaphore()
        for way in ways:
            pl.semaphore_signal(
                barrier, inc=1, device_id=self.partner(way), device_id_type=pl.DeviceIdType.MESH
            )
        pl.semaphore_wait(barrier, len(ways))

    def copy(self, source, target, way):
        k = self.used
        self.used += 1
        return pltpu.make_async_remote_copy(
            src_ref=source,
            dst_ref=target,
            send_sem=self.send_sems.at[k],
            recv_sem=self.recv_sems.at[k],
            device_id=self.partner(way),
            device_id_type=pl.DeviceIdType.MESH,
        )

    def local(self, source, target):
        k = self.used_local
        self.used_local += 1
        return pltpu.make_async_copy(source, target, self.local_sems.at[k])


def link_scratch(copies, local):
    return [
        pltpu.SemaphoreType.DMA((copies,)),
        pltpu.SemaphoreType.DMA((copies,)),
        pltpu.SemaphoreType.DMA((local,)),
    ]


def z_distances(n):
    found = []
    m = n // 2
    while m > 1:
        m //= 2
        found.append(m)
    return found


def z_ways(n):
    return [("dp", 2 * distance) for distance in z_distances(n)]


def column_stages(links, shard, column, n):
    z = links.dp // 2
    held = [z]
    stages = []
    for distance in z_distances(n):
        stages.append(
            [
                (
                    links.copy(shard if k == 0 else column.at[index], column.at[index], ("dp", 2 * distance)),
                    index ^ distance,
                )
                for k, index in enumerate(held)
            ]
        )
        held = held + [index ^ distance for index in held]
    return stages


class Spread:
    def __init__(self, links, column, whole):
        y = links.dp % 2
        half = column.shape[0] // 2
        low, high = pl.ds(0, half), pl.ds(half, half)
        near, near_core, far, far_core = (whole.at[k] for k in range(4))
        self.own = links.local(column, near.at[:, y])
        self.first = [
            links.copy(column, near.at[:, y], Y),
            links.copy(column, far.at[:, y], X),
        ]
        self.core = [links.copy(column, near_core.at[:, y], CORE)]
        self.second = [
            links.copy(near.at[low, 1 - y], far.at[low, 1 - y], X),
            links.copy(far.at[high, y], far.at[high, y], Y),
        ]
        self.core_second = [
            links.copy(near.at[:, 1 - y], near_core.at[:, 1 - y], CORE),
            links.copy(far.at[:, y], far_core.at[:, y], CORE),
        ]
        self.core_third = [links.copy(far.at[:, 1 - y], far_core.at[:, 1 - y], CORE)]

    def start(self):
        self.own.start()
        for copy in self.first + self.core:
            copy.start()

    def middle(self):
        for copy in self.first:
            copy.wait_recv()
        for copy in self.second + self.core_second:
            copy.start()

    def end(self):
        for copy in self.second:
            copy.wait_recv()
        for copy in self.core_third:
            copy.start()
        self.own.wait()
        for copy in self.first + self.second:
            copy.wait_send()
        for copy in self.core + self.core_second + self.core_third:
            copy.wait()


def add_to(total_ref, other_ref):
    def one(k, c):
        total_ref[k] = (total_ref[k].astype(F32) + other_ref[k].astype(F32)).astype(BF16)
        return c

    lax.fori_loop(0, total_ref.shape[0], one, 0)


class Gather:
    def __init__(self, links, near, far, from_x, from_y, buffers):
        y = links.dp % 2
        self.column, self.over_y, self.over_x, self.add_y, self.add_x, self.sum_y, self.sum_x = buffers
        m = self.column.shape[0]
        low, high = pl.ds(0, m // 2), pl.ds(m // 2, m - m // 2)
        self.loads = [
            links.local(near.at[low, 1 - y], self.over_y),
            links.local(far.at[high, y], self.over_x),
            links.local(from_x, self.add_y),
            links.local(from_y, self.add_x),
            links.local(near.at[:, y], self.column),
        ]
        self.first = [
            links.copy(far.at[low, y], self.sum_x.at[low], X),
            links.copy(near.at[high, 1 - y], self.sum_y.at[high], Y),
        ]
        self.second = [
            links.copy(self.over_x, self.sum_x.at[high], X),
            links.copy(self.over_y, self.sum_y.at[low], Y),
        ]

    def start(self):
        for copy in self.first + self.loads:
            copy.start()

    def middle(self):
        for copy in self.loads:
            copy.wait()
        add_to(self.over_x, self.add_x)
        add_to(self.over_y, self.add_y)
        for copy in self.second:
            copy.start()

    def end(self):
        for copy in self.first + self.second:
            copy.wait_recv()
        add_to(self.column, self.sum_y)
        add_to(self.column, self.sum_x)
        for copy in self.first + self.second:
            copy.wait_send()


def gather_scratch(m, r, c):
    whole = pltpu.VMEM((m, r, c), BF16)
    half = pltpu.VMEM((m // 2, r, c), BF16)
    return [whole] + [half] * 4 + [whole] * 2


class GatherLast:
    def __init__(self, links, near, far, diagonal, buffers):
        y = links.dp % 2
        self.column, self.over_x, self.diagonal, self.sum_y, self.sum_x = buffers
        self.loads = [
            links.local(far.at[:, y], self.over_x),
            links.local(diagonal, self.diagonal),
            links.local(near.at[:, y], self.column),
        ]
        self.over_y = links.copy(near.at[:, 1 - y], self.sum_y, Y)
        self.along_x = links.copy(self.over_x, self.sum_x, X)

    def start(self):
        self.over_y.start()
        for copy in self.loads:
            copy.start()

    def middle(self):
        for copy in self.loads:
            copy.wait()
        add_to(self.over_x, self.diagonal)
        self.along_x.start()

    def end(self):
        self.over_y.wait_recv()
        self.along_x.wait_recv()
        add_to(self.column, self.sum_y)
        add_to(self.column, self.sum_x)
        self.over_y.wait_send()
        self.along_x.wait_send()


class Collect:
    def __init__(self, links, column, slots):
        z = links.dp // 2
        self.column, self.slots, self.z = column, slots, z
        m = column.shape[0]
        distances = z_distances(2 * m)[::-1]
        self.stages = []
        first = 0
        for step, distance in enumerate(distances):
            kept = [0]
            for other in distances[step + 1 :]:
                kept = kept + [k ^ other for k in kept]
            self.stages.append(
                [
                    (links.copy(column.at[z ^ distance ^ k], slots.at[first + i], ("dp", 2 * distance)), first + i, z ^ k)
                    for i, k in enumerate(kept)
                ]
            )
            first += len(kept)

    def start(self, step):
        for copy, _, _ in self.stages[step]:
            copy.start()

    def finish(self, step):
        for copy, slot, index in self.stages[step]:
            copy.wait_recv()
            self.column[index] = (self.column[index].astype(F32) + self.slots[slot].astype(F32)).astype(BF16)

    def drain(self):
        for stage in self.stages:
            for copy, _, _ in stage:
                copy.wait_send()


class SpreadFar:
    def __init__(self, links, column, near, near_core, whole):
        y = links.dp % 2
        far, far_core = whole.at[2], whole.at[3]
        m, _, c = column.shape
        step = max(m // 4, 1)
        self.local = [links.local(near, whole.at[0]), links.local(near_core, whole.at[1])]
        self.over_x, self.over_y, self.core_x, self.core_y = [], [], [], []
        for k in range(m // step):
            for h in range(2):
                z, part = pl.ds(k * step, step), pl.ds(h * (c // 2), c // 2)
                own = far.at[z, y, :, part]
                other = far.at[z, 1 - y, :, part]
                self.over_x.append(links.copy(column.at[z, :, part], own, X))
                self.over_y.append(links.copy(own, own, Y))
                self.core_x.append(links.copy(own, far_core.at[z, y, :, part], CORE))
                self.core_y.append(links.copy(other, far_core.at[z, 1 - y, :, part], CORE))

    def start(self):
        for copy in self.over_x + self.local:
            copy.start()

    def onward(self, k):
        self.over_x[k].wait_recv()
        self.over_y[k].start()
        self.core_x[k].start()

    def last(self, k):
        self.over_y[k].wait_recv()
        self.core_y[k].start()

    def end(self):
        for copy in self.over_x + self.over_y:
            copy.wait_send()
        for copy in self.local + self.core_x + self.core_y:
            copy.wait()


class RowSum:
    def __init__(self, links, terms, buffers):
        self.near, self.far, self.got_near, self.got_far, self.got_x = buffers
        count = self.near.shape[0]

        def rows(distance):
            start = pl.multiple_of((links.tensor ^ distance) * count, count)
            return terms.at[pl.ds(start, count)]

        self.loads = [links.local(rows(0), self.near), links.local(rows(2), self.far)]
        self.core = [links.copy(rows(3), self.got_far, CORE), links.copy(rows(1), self.got_near, CORE)]
        self.over_x = links.copy(self.far, self.got_x, X)

    def start(self):
        for copy in self.loads[::-1] + self.core:
            copy.start()

    def middle(self):
        self.loads[1].wait()
        self.core[0].wait_recv()

        def add(rows):
            self.far[rows, :] = (self.far[rows, :].astype(F32) + self.got_far[rows, :].astype(F32)).astype(BF16)

        by_rows(self.far.shape[0], 64, add)
        self.over_x.start()

    def end(self):
        self.loads[0].wait()
        self.core[1].wait_recv()
        self.over_x.wait_recv()
        for copy in self.core + [self.over_x]:
            copy.wait_send()

    def total(self, rows):
        return self.near[rows, :].astype(F32) + self.got_near[rows, :].astype(F32) + self.got_x[rows, :].astype(F32)


def row_sum_scratch(count, width):
    return [pltpu.VMEM((count, width), BF16)] * 5


class Everywhere:
    def __init__(self, links, held, slots, n):
        self.held, self.slots = held, slots
        ways = everywhere_ways(n)
        self.copies = [links.copy(held.at[k], slots.at[k], way) for k, way in enumerate(ways)]

    def start(self, step):
        self.copies[step].start()

    def finish(self, step):
        self.copies[step].wait()
        self.held[step + 1] = self.held[step] + self.slots[step]


def everywhere_ways(n):
    return [CORE, X, Y] + z_ways(n)


def everywhere_scratch(k, c, n):
    steps = len(everywhere_ways(n))
    return [pltpu.VMEM((steps + 1, k, c), F32), pltpu.VMEM((steps, k, c), F32)]


def middle_kernel(
    back_ref, rows_ref, grad_ref, norm_ref, down_ref, cross_ref,
    wide_out, grad_out, sums_ref, down_out, diagonal_out,
    low, column, slots, send_sems, recv_sems, local_sems, *, n
):
    links = Links(send_sems, recv_sems, local_sems)
    count = low.shape[0]
    load = links.local(down_ref, column)
    load.start()
    collect = Collect(links, column, slots)

    def place(distance):
        return wide_out.at[pl.ds(pl.multiple_of((links.tensor ^ distance) * count, count), count)]

    own = links.local(low, place(0))
    half = count // 2
    parts = [pl.ds(0, half), pl.ds(half, half)]
    over_x = [links.copy(low.at[part], place(0).at[part], X) for part in parts]
    over_core = links.copy(low, place(0), CORE)
    onward = [links.copy(place(2).at[part], place(2).at[part], CORE) for part in parts]
    over_y = links.copy(cross_ref.at[1, :, 1 - links.dp % 2], diagonal_out, Y)
    links.greet([CORE, X, Y] + z_ways(n))
    over_y.start()
    load.wait()
    collect.start(0)
    sums_ref[...] = jnp.zeros_like(sums_ref)

    def norm_back(rows):
        incoming = back_ref[rows, :]
        rows_grad, gain_terms = norm_rows_back(rows_ref[rows, :], incoming, norm_ref[0:1, :])
        rows_grad = rows_grad + grad_ref[rows, :]
        rounded = rows_grad.astype(BF16)
        grad_out[rows, :] = rows_grad
        low[rows, :] = rounded
        for k, terms in enumerate((gain_terms, incoming, rounded.astype(F32))):
            sums_ref[k : k + 1, :] += jnp.sum(terms, axis=0, keepdims=True)

    for part, copy in zip(parts, over_x):
        by_rows(half, 64, lambda rows, part=part: norm_back(pl.ds(pl.multiple_of(part.start + rows.start, 64), 64)))
        copy.start()
    own.start()
    over_core.start()
    for step in range(len(collect.stages) - 1):
        collect.finish(step)
        collect.start(step + 1)
    for copy, later in zip(over_x, onward):
        copy.wait_recv()
        later.start()
    collect.finish(len(collect.stages) - 1)
    down_out[...] = column[collect.z].astype(F32)
    collect.drain()
    own.wait()
    for copy in over_x:
        copy.wait_send()
    over_core.wait()
    for copy in onward:
        copy.wait()
    over_y.wait()


def middle(back, rows, grad, norm, down_column, cross_sum):
    n = lax.axis_size("dp")
    count, width = rows.shape
    m, r, c = down_column.shape
    vmem = pl.BlockSpec(memory_space=pltpu.VMEM)
    return pl.pallas_call(
        functools.partial(middle_kernel, n=n),
        in_specs=[vmem, vmem, vmem, vmem, ANY, ANY],
        out_specs=[ANY, vmem, vmem, vmem, ANY],
        out_shape=[
            jax.ShapeDtypeStruct((4 * count, width), BF16),
            jax.ShapeDtypeStruct((count, width), F32),
            jax.ShapeDtypeStruct((8, width), F32),
            jax.ShapeDtypeStruct((r, c), F32),
            jax.ShapeDtypeStruct((m, r, cross_sum.shape[4]), BF16),
        ],
        scratch_shapes=[
            pltpu.VMEM((count, width), BF16),
            pltpu.VMEM((m, r, c), BF16),
            pltpu.VMEM((m, r, c), BF16),
        ]
        + link_scratch(6 + m, 2),
        compiler_params=pltpu.CompilerParams(
            vmem_limit_bytes=VMEM_LIMIT, collective_id=6, has_side_effects=True
        ),
        cost_estimate=pl.CostEstimate(flops=0, bytes_accessed=100 * 2**20, transcendentals=0),
        name="middle",
    )(back, rows, grad, norm, down_column, cross_sum)


def tail_kernel(
    dq_ref, dk_ref, dv_ref, w_ref, first_ref, so_ref, rows_ref, grad_ref, norm_ref, late_ref,
    grad_out, weights_out, late_out, give, acc, weights, *scratch, n, step_rows
):
    links = Links(*scratch[-3:])
    near, far, got_near, got_far, got_x = scratch[:5]
    columns, gots, slots = scratch[5:7], scratch[7:9], scratch[9:11]
    held, late_slots = scratch[11:13]
    count, model = near.shape
    width = dq_ref.shape[1]
    y = links.dp % 2
    c = columns[0].shape[2]
    m, _, r, _ = weights.shape
    half = count // 2
    parts = [pl.ds(0, half), pl.ds(half, half)]
    core_far = links.copy(give.at[0], got_far, CORE)
    core_near = links.copy(give.at[1], got_near, CORE)
    over_x = [links.copy(far.at[part], got_x.at[part], X) for part in parts]
    over_y, collects = [], []
    for k, (column, got, slot) in enumerate(zip(columns, gots, slots)):
        over_y.append(links.copy(weights.at[:, 1 - y, :, pl.ds(k * c, c)], got, Y))
        collects.append(Collect(links, column, slot))
    late = Everywhere(links, held, late_slots, n)
    links.greet(everywhere_ways(n))

    def terms(distance, target):
        base = (links.tensor ^ distance) * count

        def one(rows):
            there = pl.ds(pl.multiple_of(base + rows.start, 128), 128)
            total = dot_nt(dq_ref[there, :], w_ref[:, :width])
            total = total + dot_nt(dk_ref[there, :], w_ref[:, width : 2 * width])
            target[rows, :] = (total + dot_nt(dv_ref[there, :], w_ref[:, 2 * width : 3 * width])).astype(BF16)

        by_rows(count, 128, one)

    terms(3, give.at[0])
    core_far.start()
    terms(2, far)
    core_far.wait_recv()
    for part, copy in zip(parts, over_x):

        def add(rows, part=part):
            there = pl.ds(pl.multiple_of(part.start + rows.start, 64), 64)
            far[there, :] = (far[there, :].astype(F32) + got_far[there, :].astype(F32)).astype(BF16)

        by_rows(half, 64, add)
        copy.start()

    acc[...] = jnp.zeros_like(acc)

    def products(rows):
        source = first_ref[rows, :].T
        for k, ref in enumerate((dq_ref, dk_ref, dv_ref)):
            acc[:, k * width : (k + 1) * width] += dot_nn(source, ref[rows, :])

    by_rows(dq_ref.shape[0], step_rows, products)
    for k in range(2 * m):
        span = slice(k * r, (k + 1) * r)
        weights[k // 2, k % 2, :, : 3 * width] = acc[span, :].astype(BF16)
        weights[k // 2, k % 2, :, 3 * width :] = so_ref[span, :]
    over_y[0].start()
    terms(1, give.at[1])
    core_near.start()
    terms(0, near)
    for k in range(2):
        columns[k][...] = weights[:, y, :, k * c : (k + 1) * c]
    for k in range(2):
        over_y[k].wait_recv()
        if k == 0:
            over_y[1].start()
        add_to(columns[k], gots[k])
        collects[k].start(0)
    stages = len(collects[0].stages)
    held[0] = late_ref[...]
    core_near.wait_recv()
    for part, copy in zip(parts, over_x):
        copy.wait_recv()

        def norm_back(rows, part=part):
            rows = pl.ds(pl.multiple_of(part.start + rows.start, 64), 64)
            incoming = near[rows, :].astype(F32) + got_near[rows, :].astype(F32) + got_x[rows, :].astype(F32)
            rows_grad, gain_terms = norm_rows_back(rows_ref[rows, :].astype(F32), incoming, norm_ref[0:1, :])
            grad_out[rows, :] = rows_grad + grad_ref[rows, :]
            held[0, 0:1, :] += jnp.sum(gain_terms, axis=0, keepdims=True)
            held[0, 1:2, :] += jnp.sum(incoming, axis=0, keepdims=True)

        by_rows(half, 64, norm_back)
        if part is parts[0]:
            for step in range(stages - 1):
                for k in range(2):
                    collects[k].finish(step)
                    collects[k].start(step + 1)
    steps = len(late.copies)
    for step in range(steps):
        late.start(step)
        if step == 1:
            for k in range(2):
                collects[k].finish(stages - 1)
                weights_out[:, k * c : (k + 1) * c] = columns[k][collects[k].z].astype(F32)
        late.finish(step)
    late_out[...] = held[steps]
    for copy in over_x + over_y + [core_near, core_far]:
        copy.wait_send()
    for collect in collects:
        collect.drain()


def tail(dq, dk, dv, w, first, so_grad, rows, grad, norm, late):
    n = lax.axis_size("dp")
    count, model = rows.shape
    total, width = dq.shape
    m, r, c = n // 2, model // n, 4 * width
    vmem = pl.BlockSpec(memory_space=pltpu.VMEM)
    part = pltpu.VMEM((m, r, c // 2), BF16)
    return pl.pallas_call(
        functools.partial(tail_kernel, n=n, step_rows=512),
        in_specs=[vmem] * 10,
        out_specs=[vmem, vmem, vmem],
        out_shape=[
            jax.ShapeDtypeStruct((count, model), F32),
            jax.ShapeDtypeStruct((r, c), F32),
            jax.ShapeDtypeStruct(late.shape, F32),
        ],
        scratch_shapes=[
            pltpu.VMEM((2, count, model), BF16),
            pltpu.VMEM((model, 3 * width), F32),
            pltpu.VMEM((m, 2, r, c), BF16),
        ]
        + row_sum_scratch(count, model)
        + [part] * 6
        + everywhere_scratch(*late.shape, n)
        + link_scratch(6 + 2 * m + len(everywhere_ways(n)), 1),
        compiler_params=pltpu.CompilerParams(
            vmem_limit_bytes=VMEM_LIMIT, collective_id=7, has_side_effects=True
        ),
        cost_estimate=pl.CostEstimate(flops=0, bytes_accessed=100 * 2**20, transcendentals=0),
        name="tail",
    )(dq, dk, dv, w, first, so_grad, rows, grad, norm, late)


def start_kernel(rows_ref, self_ref, cross_ref, rows_out, self_out, cross_out, send_sems, recv_sems, local_sems, *, n):
    links = Links(send_sems, recv_sems, local_sems)
    member, z, y = links.tensor, links.dp // 2, links.dp % 2
    count = rows_ref.shape[0]
    half = count // 2
    parts = [pl.ds(0, half), pl.ds(half, half)]

    def place(distance):
        return rows_out.at[pl.ds(pl.multiple_of((member ^ distance) * count, count), count)]

    over_x = [links.copy(rows_ref.at[part], place(0).at[part], X) for part in parts]
    over_core = [links.copy(rows_ref, place(0), CORE)]
    over_core += [links.copy(place(2).at[part], place(2).at[part], CORE) for part in parts]
    self_stages = column_stages(links, self_ref, self_out.at[:, y], n)
    cross_stages = column_stages(links, cross_ref, cross_out, n)
    over_y = [links.copy(self_ref, self_out.at[z, y], Y)]
    local = [
        links.local(rows_ref, place(0)),
        links.local(self_ref, self_out.at[z, y]),
        links.local(cross_ref, cross_out.at[z]),
    ]
    links.greet([CORE, X, Y] + z_ways(n))
    for copy in over_x + over_y + over_core[:1] + local:
        copy.start()
    for self_stage in self_stages:
        for copy, _ in self_stage:
            copy.start()
        for copy, index in self_stage:
            copy.wait_recv()
            onward = links.copy(self_out.at[index, y], self_out.at[index, y], Y)
            onward.start()
            over_y.append(onward)
        if self_stage is self_stages[0]:
            for copy, _ in cross_stages[0]:
                copy.start()
    for cross_stage, later in zip(cross_stages, cross_stages[1:] + [[]]):
        for copy, _ in cross_stage:
            copy.wait_recv()
        for copy, _ in later:
            copy.start()
    for copy, onward in zip(over_x, over_core[1:]):
        copy.wait_recv()
        onward.start()
    for copy in local + over_y + over_core:
        copy.wait()
    for copy in over_x:
        copy.wait_send()
    for stage in self_stages + cross_stages:
        for copy, _ in stage:
            copy.wait_send()


def start_gather(rows_low, self_shard, cross_shard):
    n = lax.axis_size("dp")
    r, c = self_shard.shape
    return pl.pallas_call(
        functools.partial(start_kernel, n=n),
        in_specs=[ANY] * 3,
        out_specs=[ANY] * 3,
        out_shape=[
            jax.ShapeDtypeStruct((4 * rows_low.shape[0], rows_low.shape[1]), BF16),
            jax.ShapeDtypeStruct((n // 2, 2, r, c), BF16),
            jax.ShapeDtypeStruct((n // 2,) + cross_shard.shape, BF16),
        ],
        scratch_shapes=link_scratch(2 * n + 8, 3),
        compiler_params=pltpu.CompilerParams(collective_id=0, has_side_effects=True),
        cost_estimate=pl.CostEstimate(flops=0, bytes_accessed=100 * 2**20, transcendentals=0),
        name="start_gather",
    )(rows_low, self_shard, cross_shard)


def self_forward_kernel(
    b_ref, x_ref, w_ref, bq_ref, bv_ref, column_ref, shard_ref, enc_ref,
    q_out, k_ref, v_out, kt_out, ot_ref, lse_ref, terms_ref, whole, next_column, enc_out,
    vt_ref, m_s, l_s, acc, send_sems, recv_sems, local_sems, *, bk, heads, safe, n
):
    i = pl.program_id(0)
    last = pl.num_programs(0) - 1
    bq, width = q_out.shape
    links = Links(send_sems, recv_sems, local_sems)
    spread = Spread(links, column_ref, whole)
    stages = column_stages(links, shard_ref, next_column, n)
    enc_count = enc_ref.shape[0]

    def place(distance):
        return enc_out.at[pl.ds(pl.multiple_of((links.tensor ^ distance) * enc_count, enc_count), enc_count)]

    enc_x = links.copy(enc_ref, place(0), X)
    enc_core = [links.copy(enc_ref, place(0), CORE), links.copy(place(2), place(2), CORE)]
    local = [links.local(shard_ref, next_column.at[links.dp // 2]), links.local(enc_ref, place(0))]

    @pl.when(i == 0)
    def _():
        links.greet([CORE, X, Y] + z_ways(n))
        spread.start()
        for copy in local + enc_core[:1]:
            copy.start()
        for copy, _ in stages[0]:
            copy.start()

    @pl.when(i == last)
    def _():
        spread.middle()
        enc_x.start()
        for k in range(1, len(stages)):
            for copy, _ in stages[k - 1]:
                copy.wait_recv()
            for copy, _ in stages[k]:
                copy.start()

    projected = dot_nn(x_ref[...], w_ref[:, : 3 * width])
    query = (projected[:, :width] + bq_ref[...]).astype(BF16)
    key = projected[:, width : 2 * width].astype(BF16)
    value = (projected[:, 2 * width :] + bv_ref[...]).astype(BF16)
    here = pl.ds(pl.multiple_of(i * bq, bq), bq)
    q_out[...] = query
    v_out[...] = value
    kt_out[...] = key.T
    k_ref[here, :] = key
    vt_ref[:, here] = value.T

    m_s[...] = jnp.full_like(m_s, NEGATIVE)
    l_s[...] = jnp.zeros_like(l_s)
    acc[...] = jnp.zeros_like(acc)
    hd = width // heads
    scaled = query * jnp.asarray(1.0 / math.sqrt(hd), BF16)
    q_heads = [head_only(scaled, h, hd) for h in range(heads)]

    def block(j, mode):
        rows = pl.ds(pl.multiple_of(j * bk, bk), bk)
        keys = k_ref[rows, :]
        m_old = m_s[...]
        l_old = l_s[...]
        scores = [dot_nt(keys, q_heads[h]) for h in range(heads)]
        if mode != "none":
            bad = self_bad(b_ref, i * bq, j * bk, bq, bk, mode == "causal")
            scores = [jnp.where(bad, NEGATIVE, s) for s in scores]
        m_out, l_out, a_out = [], [], []
        for h in range(heads):
            part = slice(h * hd, (h + 1) * hd)
            m_new = jnp.maximum(m_old[h : h + 1, :], jnp.max(scores[h], axis=0, keepdims=True))
            shrink = jnp.exp(m_old[h : h + 1, :] - m_new)
            expos = jnp.exp(scores[h] - m_new)
            l_out.append(l_old[h : h + 1, :] * shrink + jnp.sum(expos, axis=0, keepdims=True))
            m_out.append(m_new)
            a_out.append(acc[part, :] * shrink + dot_nn(vt_ref[part, rows], expos.astype(BF16)))
        m_s[...] = jnp.concatenate(m_out, 0)
        l_s[...] = jnp.concatenate(l_out, 0)
        for h in range(heads):
            acc[h * hd : (h + 1) * hd, :] = a_out[h]

    over_keys(i, bq, bk, safe, block)
    inverse = 1.0 / l_s[...]
    for h in range(heads):
        part = slice(h * hd, (h + 1) * hd)
        ot_ref[part, :] = (acc[part, :] * inverse[h : h + 1, :]).astype(BF16)
    lse_ref[...] = m_s[...] + jnp.log(l_s[...])
    terms_ref[...] = dot_nt(ot_ref[...].T, w_ref[:, 3 * width :]).astype(BF16)

    @pl.when(i == last)
    def _():
        spread.end()
        enc_x.wait_recv()
        enc_core[1].start()
        for k, stage in enumerate(stages):
            for copy, _ in stage:
                copy.wait_send()
                if k == len(stages) - 1:
                    copy.wait_recv()
        enc_x.wait_send()
        for copy in local + enc_core:
            copy.wait()


def self_forward(bounds, x, w, q_shift, v_shift, column, shard, encoder, heads, safe):
    n, model = x.shape
    width = w.shape[1] // 4
    bq = bk = 512
    dp = lax.axis_size("dp")
    m, r, c = column.shape
    enc_count = encoder.shape[0]
    by_rows_spec = pl.BlockSpec((bq, width), lambda i: (i, 0))
    by_columns_spec = pl.BlockSpec((width, bq), lambda i: (0, i))
    return pl.pallas_call(
        functools.partial(self_forward_kernel, bk=bk, heads=heads, safe=safe, n=dp),
        grid=(n // bq,),
        in_specs=[
            pl.BlockSpec(memory_space=pltpu.SMEM),
            pl.BlockSpec((bq, model), lambda i: (i, 0)),
            const((model, 4 * width)),
            const((1, width)),
            const((1, width)),
            ANY,
            ANY,
            ANY,
        ],
        out_specs=[
            by_rows_spec,
            const((n, width)),
            by_rows_spec,
            by_columns_spec,
            by_columns_spec,
            pl.BlockSpec((heads, bq), lambda i: (0, i)),
            pl.BlockSpec((bq, model), lambda i: (i, 0)),
            ANY,
            ANY,
            ANY,
        ],
        out_shape=[
            jax.ShapeDtypeStruct((n, width), BF16),
            jax.ShapeDtypeStruct((n, width), BF16),
            jax.ShapeDtypeStruct((n, width), BF16),
            jax.ShapeDtypeStruct((width, n), BF16),
            jax.ShapeDtypeStruct((width, n), BF16),
            jax.ShapeDtypeStruct((heads, n), F32),
            jax.ShapeDtypeStruct((n, model), BF16),
            jax.ShapeDtypeStruct((4, m, 2, r, c), BF16),
            jax.ShapeDtypeStruct((m,) + shard.shape, BF16),
            jax.ShapeDtypeStruct((4 * enc_count, model), BF16),
        ],
        scratch_shapes=[
            pltpu.VMEM((width, n), BF16),
            pltpu.VMEM((heads, bq), F32),
            pltpu.VMEM((heads, bq), F32),
            pltpu.VMEM((width, bq), F32),
        ]
        + link_scratch(11 + m, 3),
        compiler_params=pltpu.CompilerParams(
            vmem_limit_bytes=VMEM_LIMIT, collective_id=1, has_side_effects=True
        ),
        cost_estimate=pl.CostEstimate(
            flops=12 * n * n * width, bytes_accessed=8 * n * width, transcendentals=n * n * heads // 2
        ),
        name="self_forward",
    )(bounds, x, w, q_shift, v_shift, column, shard, encoder)


def after_self_kernel(
    terms_ref, rows_ref, shift_ref, norm_ref, column_ref,
    after_out, second_out, near_out, core_out, *scratch
):
    links = Links(*scratch[-3:])
    rows_sum = RowSum(links, terms_ref, scratch[:5])
    y = links.dp % 2
    own = links.local(column_ref, near_out.at[:, y])
    over_y = links.copy(column_ref, near_out.at[:, y], Y)
    over_core = [
        links.copy(column_ref, core_out.at[:, y], CORE),
        links.copy(near_out.at[:, 1 - y], core_out.at[:, 1 - y], CORE),
    ]
    links.greet([CORE, X, Y])
    rows_sum.start()
    over_y.start()
    own.start()
    rows_sum.middle()
    over_core[0].start()
    rows_sum.end()

    def norm(rows):
        after = rows_ref[rows, :].astype(F32) + rows_sum.total(rows) + shift_ref[...]
        after_out[rows, :] = after
        xhat, _ = normalized(after)
        second_out[rows, :] = (xhat * norm_ref[0:1, :] + norm_ref[1:2, :]).astype(BF16)

    by_rows(after_out.shape[0], 64, norm)
    over_y.wait_recv()
    over_core[1].start()
    over_y.wait_send()
    own.wait()
    for copy in over_core:
        copy.wait()


def sum_after_self(terms, rows, shift, norm, column):
    count, model = rows.shape
    m, r, c = column.shape
    vmem = pl.BlockSpec(memory_space=pltpu.VMEM)
    return pl.pallas_call(
        after_self_kernel,
        in_specs=[ANY, vmem, vmem, vmem, ANY],
        out_specs=[vmem, vmem, ANY, ANY],
        out_shape=[
            jax.ShapeDtypeStruct((count, model), F32),
            jax.ShapeDtypeStruct((count, model), BF16),
            jax.ShapeDtypeStruct((m, 2, r, c), BF16),
            jax.ShapeDtypeStruct((m, 2, r, c), BF16),
        ],
        scratch_shapes=row_sum_scratch(count, model) + link_scratch(6, 3),
        compiler_params=pltpu.CompilerParams(
            vmem_limit_bytes=VMEM_LIMIT, collective_id=8, has_side_effects=True
        ),
        cost_estimate=pl.CostEstimate(flops=0, bytes_accessed=100 * 2**20, transcendentals=0),
        name="sum_after_self",
    )(terms, rows, shift, norm, column)


def self_backward_kernel(
    b_ref, q_ref, k_ref, v_ref, kt_ref, wide_ref, w_ref, mt_ref, lse_ref,
    up_ref, cross_ref, diagonal_ref, enc_ref,
    dq_ref, dk_ref, dv_ref, up_out, cross_out, enc_out, dka, dva, dqa, *scratch, bk, heads, safe, n
):
    i = pl.program_id(0)
    links = Links(*scratch[-3:])
    cross = GatherLast(links, cross_ref.at[0], cross_ref.at[1], diagonal_ref, scratch[:5])
    cross_z = Collect(links, cross.column, scratch[5])
    up_column = scratch[6]
    up_z = Collect(links, up_column, scratch[7])
    load = links.local(up_ref, up_column)
    enc = RowSum(links, enc_ref, scratch[8:13])
    stages = len(up_z.stages)

    @pl.when(i == 0)
    def _():
        links.greet(everywhere_ways(n))
        cross.start()
        enc.start()
        load.start()
        load.wait()
        up_z.start(0)
        dka[...] = jnp.zeros_like(dka)
        dva[...] = jnp.zeros_like(dva)

    @pl.when(i == 1)
    def _():
        cross.middle()

    @pl.when(i == 2)
    def _():
        for step in range(stages - 1):
            up_z.finish(step)
            up_z.start(step + 1)

    def sum_cross():
        cross.end()
        cross_z.start(0)
        enc.middle()

    def next_cross():
        for step in range(stages - 1):
            cross_z.finish(step)
            cross_z.start(step + 1)

    bq, width = q_ref.shape
    hd = width // heads
    scale = 1.0 / math.sqrt(hd)
    grads = dot_nn(wide_ref[...], w_ref[:, 3 * width :]).astype(BF16)
    products = grads.T.astype(F32) * mt_ref[...].astype(F32)
    inner = [jnp.sum(products[h * hd : (h + 1) * hd, :], axis=0, keepdims=True) for h in range(heads)]
    scaled = q_ref[...] * jnp.asarray(scale, BF16)
    q_heads = [head_only(scaled, h, hd) for h in range(heads)]
    d_heads = [head_only(grads, h, hd) for h in range(heads)]
    lse = lse_ref[...]
    dqa[...] = jnp.zeros_like(dqa)

    def block(j, mode):
        rows = pl.ds(pl.multiple_of(j * bk, bk), bk)
        keys = k_ref[rows, :]
        values = v_ref[rows, :]
        scores = [dot_nt(keys, q_heads[h]) for h in range(heads)]
        dprobs = [dot_nt(values, d_heads[h]) for h in range(heads)]
        if mode != "none":
            bad = self_bad(b_ref, i * bq, j * bk, bq, bk, mode == "causal")
            scores = [jnp.where(bad, NEGATIVE, s) for s in scores]
        dv_sum, dk_sum = None, None
        for h in range(heads):
            part = slice(h * hd, (h + 1) * hd)
            probs = jnp.exp(scores[h] - lse[h : h + 1, :])
            ds = (probs * (dprobs[h] - inner[h])).astype(BF16)
            dv_h = dot_nn(probs.astype(BF16), d_heads[h])
            dk_h = dot_nn(ds, q_heads[h])
            dv_sum = dv_h if dv_sum is None else dv_sum + dv_h
            dk_sum = dk_h if dk_sum is None else dk_sum + dk_h
            dqa[part, :] += dot_nn(kt_ref[part, rows], ds)
        dva[rows, :] += dv_sum
        dka[rows, :] += dk_sum

    over_keys(i, bq, bk, safe, block, [(3, 2, sum_cross), (4, 2, next_cross)])
    dq_ref[...] = (dqa[...] * scale).astype(BF16).T

    @pl.when(i == pl.num_programs(0) - 1)
    def _():
        dk_ref[...] = dka[...].astype(BF16)
        dv_ref[...] = dva[...].astype(BF16)
        up_z.finish(stages - 1)
        up_out[...] = up_column[up_z.z].astype(F32)
        cross_z.finish(stages - 1)
        cross_out[...] = cross.column[cross_z.z].astype(F32)
        enc.end()

        def store(rows):
            enc_out[rows, :] = enc.total(rows)

        by_rows(enc_out.shape[0], 64, store)
        up_z.drain()
        cross_z.drain()


def self_backward(
    bounds, queries, keys, values, keys_t, wide, w, mixed_t, lse,
    up_column, cross_sum, diagonal, enc_terms, heads, safe
):
    n, width = queries.shape
    model = wide.shape[1]
    dp = lax.axis_size("dp")
    m, r, c = up_column.shape
    cross_c = cross_sum.shape[4]
    enc_shape = (enc_terms.shape[0] // 4, enc_terms.shape[1])
    bq = bk = 512
    some = pl.BlockSpec((bq, width), lambda i: (i, 0))
    return pl.pallas_call(
        functools.partial(self_backward_kernel, bk=bk, heads=heads, safe=safe, n=dp),
        grid=(n // bq,),
        in_specs=[
            pl.BlockSpec(memory_space=pltpu.SMEM),
            some,
            const((n, width)),
            const((n, width)),
            const((width, n)),
            pl.BlockSpec((bq, model), lambda i: (i, 0)),
            const((model, 4 * width)),
            pl.BlockSpec((width, bq), lambda i: (0, i)),
            pl.BlockSpec((heads, bq), lambda i: (0, i)),
        ]
        + [ANY] * 4,
        out_specs=[some, const((n, width)), const((n, width))]
        + [const((r, c)), const((r, cross_c)), const(enc_shape)],
        out_shape=[
            jax.ShapeDtypeStruct((n, width), BF16),
            jax.ShapeDtypeStruct((n, width), BF16),
            jax.ShapeDtypeStruct((n, width), BF16),
            jax.ShapeDtypeStruct((r, c), F32),
            jax.ShapeDtypeStruct((r, cross_c), F32),
            jax.ShapeDtypeStruct(enc_shape, F32),
        ],
        scratch_shapes=[
            pltpu.VMEM((n, width), F32),
            pltpu.VMEM((n, width), F32),
            pltpu.VMEM((width, bq), F32),
        ]
        + [pltpu.VMEM((m, r, cross_c), BF16)] * 6
        + [pltpu.VMEM((m, r, c), BF16)] * 2
        + row_sum_scratch(*enc_shape)
        + link_scratch(5 + 2 * m, 6),
        compiler_params=pltpu.CompilerParams(
            vmem_limit_bytes=VMEM_LIMIT, collective_id=5, has_side_effects=True
        ),
        cost_estimate=pl.CostEstimate(
            flops=24 * n * n * width, bytes_accessed=16 * n * width, transcendentals=n * n * heads // 2
        ),
        name="self_backward",
    )(bounds, queries, keys, values, keys_t, wide, w, mixed_t, lse, up_column, cross_sum, diagonal, enc_terms)


def const(shape):
    return pl.BlockSpec(shape, lambda *_: (0,) * len(shape), pipeline_mode=pl.Buffered(1))


def normalized(rows):
    center = rows - jnp.mean(rows, axis=-1, keepdims=True)
    scale = lax.rsqrt(jnp.mean(center * center, axis=-1, keepdims=True) + EPSILON)
    return center * scale, scale


def norm_rows_back(rows, incoming, gain):
    xhat, scale = normalized(rows)
    e = incoming * gain
    inner = jnp.mean(e * xhat, axis=-1, keepdims=True)
    return scale * (e - jnp.mean(e, axis=-1, keepdims=True) - xhat * inner), incoming * xhat


def by_rows(count, step, body):
    def one(k, c):
        body(pl.ds(pl.multiple_of(k * step, step), step))
        return c

    lax.fori_loop(0, count // step, one, 0)


def cross_forward_kernel(
    ok_ref, x_ref, enc_ref, w_ref, bq_ref, bv_ref, rows_ref, shift_ref, norm_ref, column_ref, near_ref, core_ref,
    q_out, k_out, v_out, ot_ref, lse_ref, after_ref, third_ref, whole, send_sems, recv_sems, local_sems, *, heads
):
    i = pl.program_id(0)
    last = pl.num_programs(0) - 1
    links = Links(send_sems, recv_sems, local_sems)
    spread = SpreadFar(links, column_ref, near_ref, core_ref, whole)
    pieces = len(spread.over_x)

    @pl.when(i == 0)
    def _():
        links.greet([CORE, X, Y])
        spread.start()
        after_ref[...] = rows_ref[...] + shift_ref[...]

    for step, ready in ((1, (0,)), (2, (1, 2)), (3, (3,))):

        @pl.when(i == step)
        def _():
            for k in ready:
                spread.onward(k)

    width = q_out.shape[2]
    hd = width // heads
    query = (dot_nn(x_ref[...], w_ref[0, :, :width]) + bq_ref[0]).astype(BF16)
    key_value = dot_nn(enc_ref[...], w_ref[0, :, width : 3 * width])
    keys = key_value[:, :width].astype(BF16)
    values = (key_value[:, width:] + bv_ref[0]).astype(BF16)
    q_out[0] = query
    k_out[0] = keys
    v_out[0] = values
    values_t = values.T
    scaled = query * jnp.asarray(1.0 / math.sqrt(hd), BF16)
    ok = ok_ref[...] > 0.0
    scores = [dot_nt(keys, head_only(scaled, h, hd)) for h in range(heads)]
    mixed = []
    for h in range(heads):
        part = slice(h * hd, (h + 1) * hd)
        s = jnp.where(ok, scores[h], NEGATIVE)
        largest = jnp.max(s, axis=0, keepdims=True)
        expos = jnp.exp(s - largest)
        total = jnp.sum(expos, axis=0, keepdims=True)
        mixed.append((dot_nn(values_t[part, :], expos.astype(BF16)) * (1.0 / total)).astype(BF16))
        ot_ref[0, part, :] = mixed[h]
        lse_ref[0, h : h + 1, :] = largest + jnp.log(total)
    after_ref[...] += dot_nt(jnp.concatenate(mixed, 0).T, w_ref[0, :, 3 * width :])

    @pl.when(i == last)
    def _():
        def norm(rows):
            xhat, _ = normalized(after_ref[rows, :])
            third_ref[rows, :] = (xhat * norm_ref[0:1, :] + norm_ref[1:2, :]).astype(BF16)

        by_rows(after_ref.shape[0], 128, norm)
        for k in range(4, pieces):
            spread.onward(k)
        for k in range(pieces):
            spread.last(k)
        spread.end()


def cross_forward(ok, x, encoder, weights, q_shift, v_shift, rows, shift, norm, column, near, near_core, heads):
    count, model = x.shape
    n = encoder.shape[0]
    parts, _, columns = weights.shape
    width = columns // 4
    m, r, c = column.shape

    def by_part(*shape):
        return pl.BlockSpec((1,) + shape, lambda i: (i,) + (0,) * len(shape))

    return pl.pallas_call(
        functools.partial(cross_forward_kernel, heads=heads),
        grid=(parts,),
        in_specs=[
            const((n, 1)),
            const((count, model)),
            const((n, model)),
            by_part(model, columns),
            by_part(1, width),
            by_part(1, width),
            const((count, model)),
            const((1, model)),
            const((2, model)),
            ANY,
            ANY,
            ANY,
        ],
        out_specs=[
            by_part(count, width),
            by_part(n, width),
            by_part(n, width),
            by_part(width, count),
            by_part(heads, count),
            const((count, model)),
            const((count, model)),
            ANY,
        ],
        out_shape=[
            jax.ShapeDtypeStruct((parts, count, width), BF16),
            jax.ShapeDtypeStruct((parts, n, width), BF16),
            jax.ShapeDtypeStruct((parts, n, width), BF16),
            jax.ShapeDtypeStruct((parts, width, count), BF16),
            jax.ShapeDtypeStruct((parts, heads, count), F32),
            jax.ShapeDtypeStruct((count, model), F32),
            jax.ShapeDtypeStruct((count, model), BF16),
            jax.ShapeDtypeStruct((4, m, 2, r, c), BF16),
        ],
        scratch_shapes=link_scratch(32, 2),
        compiler_params=pltpu.CompilerParams(
            vmem_limit_bytes=VMEM_LIMIT, collective_id=2, has_side_effects=True
        ),
        cost_estimate=pl.CostEstimate(
            flops=24 * parts * count * n * width,
            bytes_accessed=8 * parts * n * width,
            transcendentals=parts * count * n * heads,
        ),
        name="cross_forward",
    )(ok, x, encoder, weights, q_shift, v_shift, rows, shift, norm, column, near, near_core)


def feed_forward_kernel(
    x_ref, dy_ref, up_ref, down_ref, b_ref, after_ref, shift_ref, norm_ref,
    out_ref, rows_out, low_out, sums_ref, gup_ref, gdown_ref, bias_ref, from_x, from_y,
    xt_ref, dyt_ref, back_ref, give, got, diagonal, send_sems, recv_sems, local_sems, *, chunks
):
    s = pl.program_id(0)
    links = Links(send_sems, recv_sems, local_sems)
    turn = s // chunks
    chunk = s % chunks
    pair = turn // 2
    slot = pair * chunks + chunk
    theirs = turn % 2 == 0
    y = links.dp % 2
    m, r = diagonal.shape[1], diagonal.shape[2]
    low, high = pl.ds(0, m // 2), pl.ds(m // 2, m - m // 2)
    links.used = 2 * chunks
    across = [
        links.copy(diagonal.at[:, low], from_x, X),
        links.copy(diagonal.at[:, high], from_y, Y),
    ]
    to_core = pltpu.make_async_remote_copy(
        src_ref=give.at[chunk],
        dst_ref=got.at[slot],
        send_sem=send_sems.at[slot],
        recv_sem=recv_sems.at[slot],
        device_id=links.partner(CORE),
        device_id_type=pl.DeviceIdType.MESH,
    )

    @pl.when(s == 0)
    def _():
        links.greet([CORE, X, Y])
        out_ref[...] = after_ref[...] + shift_ref[...]
        back_ref[...] = jnp.zeros_like(back_ref)
        xt_ref[...] = x_ref[...].T
        dyt_ref[...] = dy_ref[...].T
        sums_ref[...] = jnp.zeros_like(sums_ref)

    pre_act = dot_nn(x_ref[...], up_ref[0]) + b_ref[0]
    hidden_grad = dot_nn(dy_ref[...], down_ref[0])
    normal_cdf = 0.5 * (1.0 + lax.erf(pre_act * (1.0 / math.sqrt(2.0))))
    density = jnp.exp(-0.5 * pre_act * pre_act) * (1.0 / math.sqrt(2.0 * math.pi))
    hidden = (pre_act * normal_cdf).astype(BF16)
    pre_grad = (hidden_grad * (normal_cdf + pre_act * density)).astype(BF16)
    bias_ref[0] = jnp.sum(pre_grad.astype(F32), axis=0, keepdims=True)

    @pl.when(turn % 2 == 1)
    def _():
        to_core.wait_send()

    give[chunk, 0] = dot_nn(xt_ref[...], pre_grad).astype(BF16)
    give[chunk, 1] = dot_nn(dyt_ref[...], hidden).astype(BF16)
    out_ref[...] += dot_nt(hidden, down_ref[0])
    back_ref[...] += dot_nt(pre_grad, up_ref[0])

    @pl.when(theirs)
    def _():
        to_core.start()

    @pl.when(jnp.logical_not(theirs))
    def _():
        to_core.wait_recv()
        gup_ref[0] = (give[chunk, 0].astype(F32) + got[slot, 0].astype(F32)).astype(BF16)
        gdown_ref[0] = (give[chunk, 1].astype(F32) + got[slot, 1].astype(F32)).astype(BF16)

    for k in range(chunks):

        @pl.when(s == chunks + k)
        def _():
            def keep(z, carry):
                rows = pl.ds(pl.multiple_of((2 * z + 1 - y) * r, r), r)
                size = gup_ref.shape[2]
                diagonal[0, z, :, k * size : (k + 1) * size] = gup_ref[0, rows, :]
                diagonal[1, z, :, k * size : (k + 1) * size] = gdown_ref[0, rows, :]
                return carry

            lax.fori_loop(0, m, keep, 0)
            if k == chunks - 1:
                for copy in across:
                    copy.start()

    @pl.when(s == pl.num_programs(0) - 1)
    def _():
        def norm_back(rows):
            third = back_ref[rows, :]
            upstream = dy_ref[rows, :].astype(F32)
            rows_grad, gain_terms = norm_rows_back(after_ref[rows, :], third, norm_ref[0:1, :])
            rows_grad = rows_grad + upstream
            low = rows_grad.astype(BF16)
            rows_out[rows, :] = rows_grad
            low_out[rows, :] = low
            for k, terms in enumerate((gain_terms, third, low.astype(F32), upstream)):
                sums_ref[k : k + 1, :] += jnp.sum(terms, axis=0, keepdims=True)

        by_rows(x_ref.shape[0], 128, norm_back)
        for copy in across:
            copy.wait()


def feed_forward(x, dy, weights, bias, after, shift, norm):
    rows, width = x.shape
    hidden = weights.shape[2] // 2
    size = min(512, hidden)
    chunks = hidden // size

    n = lax.axis_size("dp")
    m, r = n // 2, width // n

    def block(s):
        return 3 - s // chunks

    def placed(s):
        turn = s // chunks
        return (1 - turn // 2, 0, (s % chunks) * (turn % 2))

    rows_spec = const((rows, width))
    grad_spec = pl.BlockSpec((1, width, size), placed)
    bias_spec = pl.BlockSpec((1, 1, size), lambda s: (block(s), 0, s % chunks))
    return pl.pallas_call(
        functools.partial(feed_forward_kernel, chunks=chunks),
        grid=(4 * chunks,),
        in_specs=[
            rows_spec,
            rows_spec,
            pl.BlockSpec((1, width, size), lambda s: (block(s), 0, s % chunks)),
            pl.BlockSpec((1, width, size), lambda s: (block(s), 0, chunks + s % chunks)),
            bias_spec,
            rows_spec,
            const((1, width)),
            const((2, width)),
        ],
        out_specs=[rows_spec, rows_spec, rows_spec, const((8, width)), grad_spec, grad_spec, bias_spec, ANY, ANY],
        out_shape=[
            jax.ShapeDtypeStruct((rows, width), F32),
            jax.ShapeDtypeStruct((rows, width), F32),
            jax.ShapeDtypeStruct((rows, width), BF16),
            jax.ShapeDtypeStruct((8, width), F32),
            jax.ShapeDtypeStruct((2, width, hidden), BF16),
            jax.ShapeDtypeStruct((2, width, hidden), BF16),
            jax.ShapeDtypeStruct((4, 1, hidden), F32),
            jax.ShapeDtypeStruct((2, m // 2, r, hidden), BF16),
            jax.ShapeDtypeStruct((2, m - m // 2, r, hidden), BF16),
        ],
        scratch_shapes=[
            pltpu.VMEM((width, rows), BF16),
            pltpu.VMEM((width, rows), BF16),
            pltpu.VMEM((rows, width), F32),
            pltpu.VMEM((chunks, 2, width, size), BF16),
            pltpu.VMEM((2 * chunks, 2, width, size), BF16),
            pltpu.VMEM((2, m, r, hidden), BF16),
        ]
        + link_scratch(2 * chunks + 2, 1),
        compiler_params=pltpu.CompilerParams(
            vmem_limit_bytes=VMEM_LIMIT, collective_id=3, has_side_effects=True
        ),
        cost_estimate=pl.CostEstimate(
            flops=48 * rows * width * hidden, bytes_accessed=40 * 2**20, transcendentals=8 * rows * hidden
        ),
        name="feed_forward",
    )(x, dy, weights, weights, bias, after, shift, norm)


def cross_backward_kernel(
    ok_ref, low_ref, x_ref, enc_ref, w_ref, q_ref, k_ref, v_ref, mt_ref, lse_ref, up_ref, down_ref, from_x, from_y,
    back_ref, enc_out, grad_ref, bq_ref, bv_ref, up_out, down_out,
    low_t, x_t, enc_t, enc_acc, give, got, *scratch, heads, bk
):
    i = pl.program_id(0)
    last = pl.num_programs(0) - 1
    links = Links(*scratch[14:])
    sums = [
        Gather(links, ref.at[0], ref.at[1], from_x.at[k], from_y.at[k], scratch[7 * k : 7 * k + 7])
        for k, ref in enumerate((up_ref, down_ref))
    ]
    leave = [links.local(g.column, out) for g, out in zip(sums, (up_out, down_out))]
    pair = i // 2
    to_core = pltpu.make_async_remote_copy(
        src_ref=give,
        dst_ref=got.at[pair],
        send_sem=links.send_sems.at[links.used + pair],
        recv_sem=links.recv_sems.at[links.used + pair],
        device_id=links.partner(CORE),
        device_id_type=pl.DeviceIdType.MESH,
    )

    @pl.when(i == 0)
    def _():
        links.greet([CORE, X, Y])
        for g in sums:
            g.start()
        low_t[...] = low_ref[...].T
        x_t[...] = x_ref[...].T
        enc_t[...] = enc_ref[...].T
        back_ref[...] = jnp.zeros_like(back_ref)
        enc_acc[...] = jnp.zeros_like(enc_acc)

    @pl.when(i == 1)
    def _():
        for g in sums:
            g.middle()

    rows, width = q_ref.shape[1:]
    n = k_ref.shape[1]
    hd = width // heads
    scale = 1.0 / math.sqrt(hd)
    w_query, w_keyval, w_out = w_ref.at[0, :, :width], w_ref.at[0, :, width : 3 * width], w_ref.at[0, :, 3 * width :]
    grads = dot_nn(low_ref[...], w_out[...]).astype(BF16)
    mixed_t = mt_ref[0]
    products = grads.T.astype(F32) * mixed_t.astype(F32)
    inner = [jnp.sum(products[h * hd : (h + 1) * hd, :], axis=0, keepdims=True) for h in range(heads)]
    scaled = q_ref[0] * jnp.asarray(scale, BF16)
    q_heads = [head_only(scaled, h, hd) for h in range(heads)]
    d_heads = [head_only(grads, h, hd) for h in range(heads)]
    lse = lse_ref[0]
    keys_t = k_ref[0].T
    dq = [None] * heads
    dkv = []
    for j in range(n // bk):
        span = slice(j * bk, (j + 1) * bk)
        keys = k_ref[0, span, :]
        values = v_ref[0, span, :]
        ok = ok_ref[span, :] > 0.0
        scores = [dot_nt(keys, q_heads[h]) for h in range(heads)]
        dprobs = [dot_nt(values, d_heads[h]) for h in range(heads)]
        dv_sum, dk_sum = None, None
        for h in range(heads):
            part = slice(h * hd, (h + 1) * hd)
            probs = jnp.exp(jnp.where(ok, scores[h], NEGATIVE) - lse[h : h + 1, :])
            ds = (probs * (dprobs[h] - inner[h])).astype(BF16)
            dv_h = dot_nn(probs.astype(BF16), d_heads[h])
            dk_h = dot_nn(ds, q_heads[h])
            dv_sum = dv_h if dv_sum is None else dv_sum + dv_h
            dk_sum = dk_h if dk_sum is None else dk_sum + dk_h
            dq_h = dot_nn(keys_t[part, span], ds)
            dq[h] = dq_h if dq[h] is None else dq[h] + dq_h
        block = jnp.concatenate([dk_sum.astype(BF16), dv_sum.astype(BF16)], 1)
        enc_acc[span, :] += dot_nt(block, w_keyval[...])
        dkv.append(block)
    dq = (jnp.concatenate(dq, 0) * scale).astype(BF16).T
    dkv = jnp.concatenate(dkv, 0)
    bq_ref[0] = jnp.sum(dq.astype(F32), axis=0, keepdims=True)
    bv_ref[0] = jnp.sum(dkv[:, width:].astype(F32), axis=0, keepdims=True)
    back_ref[...] += dot_nt(dq, w_query[...])

    @pl.when(i % 2 == 1)
    def _():
        to_core.wait_send()

    give[:, :width] = dot_nn(x_t[...], dq).astype(BF16)
    give[:, width : 3 * width] = dot_nn(enc_t[...], dkv).astype(BF16)
    give[:, 3 * width :] = dot_nn(low_t[...], mixed_t.T).astype(BF16)

    @pl.when(i % 2 == 0)
    def _():
        to_core.start()

    @pl.when(i % 2 == 1)
    def _():
        to_core.wait_recv()
        grad_ref[0] = (give[...].astype(F32) + got[pair].astype(F32)).astype(BF16)

    @pl.when(i == last)
    def _():
        enc_out[...] = enc_acc[...].astype(BF16)
        for g, copy in zip(sums, leave):
            g.end()
            copy.start()
        for copy in leave:
            copy.wait()


def cross_backward(
    ok, low, x, encoder, weights, queries, keys, values, mixed_t, lse, up_sum, down_sum, from_x, from_y, heads
):
    count, model = x.shape
    n = encoder.shape[0]
    parts, _, columns = weights.shape
    width = columns // 4
    _, m, _, r, c = up_sum.shape

    def by_part(*shape):
        return pl.BlockSpec((1,) + shape, lambda i: (i ^ 1,) + (0,) * len(shape))

    return pl.pallas_call(
        functools.partial(cross_backward_kernel, heads=heads, bk=256),
        grid=(parts,),
        in_specs=[
            const((n, 1)),
            const((count, model)),
            const((count, model)),
            const((n, model)),
            by_part(model, columns),
            by_part(count, width),
            by_part(n, width),
            by_part(n, width),
            by_part(width, count),
            by_part(heads, count),
            ANY,
            ANY,
            ANY,
            ANY,
        ],
        out_specs=[
            const((count, model)),
            const((n, model)),
            pl.BlockSpec((1, model, columns), lambda i: (i // 2, 0, 0), pipeline_mode=pl.Buffered(1)),
            by_part(1, width),
            by_part(1, width),
            ANY,
            ANY,
        ],
        out_shape=[
            jax.ShapeDtypeStruct((count, model), F32),
            jax.ShapeDtypeStruct((n, model), BF16),
            jax.ShapeDtypeStruct((2, model, columns), BF16),
            jax.ShapeDtypeStruct((parts, 1, width), F32),
            jax.ShapeDtypeStruct((parts, 1, width), F32),
            jax.ShapeDtypeStruct((m, r, c), BF16),
            jax.ShapeDtypeStruct((m, r, c), BF16),
        ],
        scratch_shapes=[
            pltpu.VMEM((model, count), BF16),
            pltpu.VMEM((model, count), BF16),
            pltpu.VMEM((model, n), BF16),
            pltpu.VMEM((n, model), F32),
            pltpu.VMEM((model, columns), BF16),
            pltpu.VMEM((2, model, columns), BF16),
        ]
        + gather_scratch(m, r, c) * 2
        + link_scratch(10, 12),
        compiler_params=pltpu.CompilerParams(
            vmem_limit_bytes=60 * 2**20, collective_id=4, has_side_effects=True
        ),
        cost_estimate=pl.CostEstimate(
            flops=48 * parts * count * n * width,
            bytes_accessed=16 * parts * n * width,
            transcendentals=parts * count * n * heads,
        ),
        name="cross_backward",
    )(ok, low, x, encoder, weights, queries, keys, values, mixed_t, lse, up_sum, down_sum, from_x, from_y)


def on_device(
    block_in,
    encoder_out,
    out_grad,
    bounds,
    enc_lengths,
    norm_params,
    w_qkv,
    w_self_out,
    w_cross_q,
    w_cross_kv,
    w_cross_out,
    w_up,
    w_down,
    biases,
    up_bias,
):
    member = lax.axis_index("tensor")
    groups_count = lax.axis_size("dp")
    groups = float(groups_count)
    width = w_cross_q.shape[1]
    hidden_width = w_up.shape[1]
    heads = H // 4
    own_rows, model_width = block_in.shape
    enc_rows = encoder_out.shape[0]
    w_rows = w_cross_q.shape[0]

    def block_of(vector, size, distance):
        return lax.dynamic_slice_in_dim(vector, (member ^ distance) * size, size)

    def blocks_placed(parts):
        size = parts[0].shape[0]
        out = jnp.zeros((4 * size,), F32)
        for distance, part in enumerate(parts):
            out = lax.dynamic_update_slice_in_dim(out, part, (member ^ distance) * size, 0)
        return out

    first_in, self_w, cross_column = start_gather(
        layer_norm(block_in.astype(F32), norm_params[0, 0], norm_params[0, 1]).astype(BF16),
        jnp.concatenate([w_qkv.reshape(w_rows, 3 * width), w_self_out.T], axis=1),
        jnp.concatenate([w_cross_q, w_cross_kv.reshape(w_rows, 2 * width), w_cross_out.T], axis=1),
    )
    self_w = self_w.reshape(model_width, 4 * width)

    self_safe = 1024
    queries, key_rows, value_rows, keys_t, self_mixed_t, self_lse, terms, cross_w, ffn_column, enc_all = self_forward(
        bounds,
        first_in,
        self_w,
        block_of(biases[0], width, 0)[None],
        block_of(biases[1], width, 0)[None],
        cross_column,
        jnp.concatenate([w_up, w_down.T], axis=1),
        encoder_out,
        heads,
        self_safe,
    )
    cross_w = cross_w.reshape(4, model_width, 4 * width)
    after_self, second_in, ffn_near, ffn_near_core = sum_after_self(
        terms, block_in, biases[2:3], norm_params[1], ffn_column
    )

    ok = (jnp.arange(4 * enc_rows, dtype=jnp.int32) < enc_lengths[0]).astype(F32)[:, None]

    def all_blocks(vector, size):
        return jnp.stack([block_of(vector, size, d) for d in range(4)])[:, None]

    cross_q, cross_k, cross_v, cross_mixed_t, cross_lse, after_cross, third_in, ffn_w = cross_forward(
        ok,
        second_in,
        enc_all,
        cross_w,
        all_blocks(biases[3], width),
        all_blocks(biases[4], width),
        after_self,
        biases[5:6],
        norm_params[2],
        ffn_column,
        ffn_near,
        ffn_near_core,
        heads,
    )

    output, cross_rows_grad, cross_low, ffn_sums, up_sum, down_sum, bias_up_parts, from_x, from_y = feed_forward(
        third_in,
        out_grad,
        ffn_w.reshape(4, model_width, 2 * hidden_width),
        all_blocks(up_bias, hidden_width),
        after_cross,
        biases[6:7],
        norm_params[2],
    )

    by_shard = (2, groups_count // 2, 2, w_rows, hidden_width)
    second_grad, enc_terms, cross_sum, bias_cq_parts, bias_cv_parts, up_column, down_column = cross_backward(
        ok,
        cross_low,
        second_in,
        enc_all,
        cross_w,
        cross_q,
        cross_k,
        cross_v,
        cross_mixed_t,
        cross_lse,
        up_sum.reshape(by_shard),
        down_sum.reshape(by_shard),
        from_x,
        from_y,
        heads,
    )
    cross_sum = cross_sum.reshape(2, groups_count // 2, 2, w_rows, 4 * width)
    self_wide, self_rows_grad, self_sums, summed_down, diagonal = middle(
        second_grad, after_self, cross_rows_grad, norm_params[1], down_column, cross_sum
    )
    bias_cq_grad = blocks_placed([bias_cq_parts[d, 0] for d in range(4)])
    bias_cv_grad = blocks_placed([bias_cv_parts[d, 0] for d in range(4)])
    bias_up_grad = blocks_placed([bias_up_parts[d, 0] for d in range(4)])

    self_dq, self_dk, self_dv, summed_up, summed_cross, encoder_grad = self_backward(
        bounds,
        queries,
        key_rows,
        value_rows,
        keys_t,
        self_wide,
        self_w,
        self_mixed_t,
        self_lse,
        up_column,
        cross_sum,
        diagonal,
        enc_terms,
        heads,
        self_safe,
    )
    grad_so_t = lax.dot_general(
        self_wide, self_mixed_t, (((0,), (1,)), ((), ())), preferred_element_type=F32
    ).astype(BF16)

    def only_own(part):
        out = jnp.zeros((model_width,), F32)
        return lax.dynamic_update_slice_in_dim(out, part, member * width, 0)

    vectors = jnp.concatenate(
        [
            jnp.zeros((2, model_width), F32),
            self_sums[:2],
            ffn_sums[:2],
            jnp.stack(
                [
                    only_own(jnp.sum(self_dq.astype(F32), axis=0)),
                    only_own(jnp.sum(self_dv.astype(F32), axis=0)),
                    self_sums[2],
                    bias_cq_grad,
                    bias_cv_grad,
                    ffn_sums[2],
                    ffn_sums[3],
                ]
            ),
            bias_up_grad.reshape(-1, model_width),
        ]
    )
    vectors = jnp.pad(vectors, ((0, -vectors.shape[0] % 8), (0, 0)))
    input_grad, summed_self, vectors = tail(
        self_dq,
        self_dk,
        self_dv,
        self_w,
        first_in,
        grad_so_t,
        block_in,
        self_rows_grad,
        norm_params[0],
        vectors,
    )
    norm_total = vectors[:6].reshape(norm_params.shape)
    bias_total = vectors[6:13]
    up_total = vectors[13 : 13 + up_bias.shape[0] // model_width].reshape(-1)
    scale = 1.0 / groups
    return (
        output,
        input_grad,
        encoder_grad,
        norm_total * scale,
        summed_self[:, : 3 * width].reshape(w_qkv.shape) * scale,
        summed_self[:, 3 * width :].T * scale,
        summed_cross[:, :width] * scale,
        summed_cross[:, width : 3 * width].reshape(w_cross_kv.shape) * scale,
        summed_cross[:, 3 * width :].T * scale,
        summed_up * scale,
        summed_down.T * scale,
        bias_total * scale,
        up_total * scale,
    )


def solution(mesh):
    rows = P(("dp", "tensor"), None)
    placed = (
        rows,
        rows,
        rows,
        P("dp", None),
        P("dp"),
        P(),
        P("dp", None, "tensor"),
        P("tensor", "dp"),
        P("dp", "tensor"),
        P("dp", None, "tensor"),
        P("tensor", "dp"),
        P("dp", "tensor"),
        P("tensor", "dp"),
        P(),
        P(),
    )
    return jax.shard_map(
        on_device,
        mesh=mesh,
        in_specs=placed,
        out_specs=(
            rows,
            rows,
            rows,
            P(),
            P("dp", None, "tensor"),
            P("tensor", "dp"),
            P("dp", "tensor"),
            P("dp", None, "tensor"),
            P("tensor", "dp"),
            P("dp", "tensor"),
            P("tensor", "dp"),
            P(),
            P(),
        ),
        check_vma=False,
    )
```

```python
import functools
import math

import jax
import jax.numpy as jnp
from jax import lax
from jax.experimental import pallas as pl
from jax.experimental.pallas import tpu as pltpu
from jax.sharding import PartitionSpec as P

H = 16
EPSILON = 1e-05
NEGATIVE = -1e30
F32 = jnp.float32
BF16 = jnp.bfloat16
VMEM_LIMIT = 56 * 2**20


def dot_nt(a, b):
    return lax.dot_general(a, b, (((1,), (1,)), ((), ())), preferred_element_type=F32)


def dot_nn(a, b):
    return lax.dot_general(a, b, (((1,), (0,)), ((), ())), preferred_element_type=F32)


def dot_tn(a, b):
    return lax.dot_general(a, b, (((0,), (0,)), ((), ())), preferred_element_type=F32)


def layer_norm(inputs, gain_row, shift_row):
    center = inputs - jnp.mean(inputs, axis=-1, keepdims=True)
    spread = jnp.mean(center * center, axis=-1, keepdims=True)
    return center * lax.rsqrt(spread + EPSILON) * gain_row + shift_row


def gelu_slope(values_in):
    normal_cdf = 0.5 * (1.0 + lax.erf(values_in * (1.0 / math.sqrt(2.0))))
    density = jnp.exp(-0.5 * values_in * values_in) * (1.0 / math.sqrt(2.0 * math.pi))
    return normal_cdf + values_in * density


def head_only(x, h, size):
    lane = lax.broadcasted_iota(jnp.int32, x.shape, 1)
    return jnp.where((lane >= h * size) & (lane < (h + 1) * size), x, jnp.zeros_like(x))


def self_bad(b_ref, q_start, k_start, bq, bk, causal):
    qi = q_start + lax.broadcasted_iota(jnp.int32, (1, bq), 1)
    kj = k_start + lax.broadcasted_iota(jnp.int32, (bk, 1), 0)
    bad = (qi >= b_ref[0, 1]) & ((kj >= b_ref[0, 0]) & (kj < b_ref[0, 1]))
    if causal:
        bad = bad | (kj > qi)
    return bad


def over_keys(i, bq, bk, safe, block, between=()):
    diagonal = i * (bq // bk)

    def visit(j, c):
        for at_i, at_j, action in between:
            pl.when((i == at_i) & (j == at_j))(action)

        @pl.when(j < safe // bk)
        def _():
            block(j, "none")

        @pl.when(j >= safe // bk)
        def _():
            block(j, "segment")

        return c

    lax.fori_loop(0, diagonal, visit, 0)
    for step in range(bq // bk):
        block(diagonal + step, "causal")


CORE = ("tensor", 1)
X = ("tensor", 2)
Y = ("dp", 1)
ANY = pl.BlockSpec(memory_space=pl.ANY)


class Links:
    def __init__(self, send_sems, recv_sems, local_sems):
        self.dp = lax.axis_index("dp")
        self.tensor = lax.axis_index("tensor")
        self.send_sems, self.recv_sems, self.local_sems = send_sems, recv_sems, local_sems
        self.used = 0
        self.used_local = 0

    def partner(self, way):
        axis, distance = way
        if axis == "tensor":
            return (self.dp, self.tensor ^ distance)
        return (self.dp ^ distance, self.tensor)

    def greet(self, ways):
        barrier = pltpu.get_barrier_semaphore()
        for way in ways:
            pl.semaphore_signal(
                barrier, inc=1, device_id=self.partner(way), device_id_type=pl.DeviceIdType.MESH
            )
        pl.semaphore_wait(barrier, len(ways))

    def copy(self, source, target, way):
        k = self.used
        self.used += 1
        return pltpu.make_async_remote_copy(
            src_ref=source,
            dst_ref=target,
            send_sem=self.send_sems.at[k],
            recv_sem=self.recv_sems.at[k],
            device_id=self.partner(way),
            device_id_type=pl.DeviceIdType.MESH,
        )

    def local(self, source, target):
        k = self.used_local
        self.used_local += 1
        return pltpu.make_async_copy(source, target, self.local_sems.at[k])


def link_scratch(copies, local):
    return [
        pltpu.SemaphoreType.DMA((copies,)),
        pltpu.SemaphoreType.DMA((copies,)),
        pltpu.SemaphoreType.DMA((local,)),
    ]


def z_distances(n):
    found = []
    m = n // 2
    while m > 1:
        m //= 2
        found.append(m)
    return found


def z_ways(n):
    return [("dp", 2 * distance) for distance in z_distances(n)]


def column_stages(links, shard, column, n):
    z = links.dp // 2
    held = [z]
    stages = []
    for distance in z_distances(n):
        stages.append(
            [
                (
                    links.copy(shard if k == 0 else column.at[index], column.at[index], ("dp", 2 * distance)),
                    index ^ distance,
                )
                for k, index in enumerate(held)
            ]
        )
        held = held + [index ^ distance for index in held]
    return stages


class Spread:
    def __init__(self, links, source, column, whole):
        y = links.dp % 2
        half = column.shape[0] // 2
        low, high = pl.ds(0, half), pl.ds(half, half)
        near, near_core, far, far_core = (whole.at[k] for k in range(4))
        self.load = links.local(source, column)
        self.own = links.local(column, near.at[:, y])
        self.first = [
            links.copy(column, near.at[:, y], Y),
            links.copy(column, far.at[:, y], X),
        ]
        self.core = [links.copy(column, near_core.at[:, y], CORE)]
        self.second = [
            links.copy(near.at[low, 1 - y], far.at[low, 1 - y], X),
            links.copy(far.at[high, y], far.at[high, y], Y),
        ]
        self.core_second = [
            links.copy(near.at[:, 1 - y], near_core.at[:, 1 - y], CORE),
            links.copy(far.at[:, y], far_core.at[:, y], CORE),
        ]
        self.core_third = [links.copy(far.at[:, 1 - y], far_core.at[:, 1 - y], CORE)]

    def start(self):
        self.load.start()
        self.load.wait()
        for copy in self.first + self.core + [self.own]:
            copy.start()

    def middle(self):
        for copy in self.first:
            copy.wait_recv()
        for copy in self.second + self.core_second:
            copy.start()

    def end(self):
        for copy in self.second:
            copy.wait_recv()
        for copy in self.core_third:
            copy.start()
        self.own.wait()
        for copy in self.first + self.second:
            copy.wait_send()
        for copy in self.core + self.core_second + self.core_third:
            copy.wait()


def add_to(total_ref, other_ref):
    def one(k, c):
        total_ref[k] = (total_ref[k].astype(F32) + other_ref[k].astype(F32)).astype(BF16)
        return c

    lax.fori_loop(0, total_ref.shape[0], one, 0)


class Gather:
    def __init__(self, links, near, far, from_x, from_y, buffers):
        y = links.dp % 2
        self.column, self.over_y, self.over_x, self.add_y, self.add_x, self.sum_y, self.sum_x = buffers
        m = self.column.shape[0]
        low, high = pl.ds(0, m // 2), pl.ds(m // 2, m - m // 2)
        self.loads = [
            links.local(near.at[low, 1 - y], self.over_y),
            links.local(far.at[high, y], self.over_x),
            links.local(from_x, self.add_y),
            links.local(from_y, self.add_x),
            links.local(near.at[:, y], self.column),
        ]
        self.first = [
            links.copy(far.at[low, y], self.sum_x.at[low], X),
            links.copy(near.at[high, 1 - y], self.sum_y.at[high], Y),
        ]
        self.second = [
            links.copy(self.over_x, self.sum_x.at[high], X),
            links.copy(self.over_y, self.sum_y.at[low], Y),
        ]

    def start(self):
        for copy in self.first + self.loads:
            copy.start()

    def middle(self):
        for copy in self.loads:
            copy.wait()
        add_to(self.over_x, self.add_x)
        add_to(self.over_y, self.add_y)
        for copy in self.second:
            copy.start()

    def end(self):
        for copy in self.first + self.second:
            copy.wait_recv()
        add_to(self.column, self.sum_y)
        add_to(self.column, self.sum_x)
        for copy in self.first + self.second:
            copy.wait_send()


def gather_scratch(m, r, c):
    whole = pltpu.VMEM((m, r, c), BF16)
    half = pltpu.VMEM((m // 2, r, c), BF16)
    return [whole] + [half] * 4 + [whole] * 2


class GatherLast:
    def __init__(self, links, near, far, diagonal, buffers):
        y = links.dp % 2
        self.column, self.over_x, self.diagonal, self.sum_y, self.sum_x = buffers
        self.loads = [
            links.local(far.at[:, y], self.over_x),
            links.local(diagonal, self.diagonal),
            links.local(near.at[:, y], self.column),
        ]
        self.over_y = links.copy(near.at[:, 1 - y], self.sum_y, Y)
        self.along_x = links.copy(self.over_x, self.sum_x, X)

    def start(self):
        self.over_y.start()
        for copy in self.loads:
            copy.start()

    def middle(self):
        for copy in self.loads:
            copy.wait()
        add_to(self.over_x, self.diagonal)
        self.along_x.start()

    def end(self):
        self.over_y.wait_recv()
        self.along_x.wait_recv()
        add_to(self.column, self.sum_y)
        add_to(self.column, self.sum_x)
        self.over_y.wait_send()
        self.along_x.wait_send()


class Collect:
    def __init__(self, links, column, slots):
        z = links.dp // 2
        self.column, self.slots, self.z = column, slots, z
        m = column.shape[0]
        distances = z_distances(2 * m)[::-1]
        self.stages = []
        first = 0
        for step, distance in enumerate(distances):
            kept = [0]
            for other in distances[step + 1 :]:
                kept = kept + [k ^ other for k in kept]
            self.stages.append(
                [
                    (links.copy(column.at[z ^ distance ^ k], slots.at[first + i], ("dp", 2 * distance)), first + i, z ^ k)
                    for i, k in enumerate(kept)
                ]
            )
            first += len(kept)

    def start(self, step):
        for copy, _, _ in self.stages[step]:
            copy.start()

    def finish(self, step):
        for copy, slot, index in self.stages[step]:
            copy.wait_recv()
            self.column[index] = (self.column[index].astype(F32) + self.slots[slot].astype(F32)).astype(BF16)

    def drain(self):
        for stage in self.stages:
            for copy, _, _ in stage:
                copy.wait_send()


class SpreadFar:
    def __init__(self, links, column, whole):
        y = links.dp % 2
        far, far_core = whole.at[0], whole.at[1]
        m, _, c = column.shape
        step = max(m // 4, 1)
        self.over_x, self.over_y, self.core_x, self.core_y = [], [], [], []
        for k in range(m // step):
            for h in range(2):
                z, part = pl.ds(k * step, step), pl.ds(h * (c // 2), c // 2)
                own = far.at[z, y, :, part]
                other = far.at[z, 1 - y, :, part]
                self.over_x.append(links.copy(column.at[z, :, part], own, X))
                self.over_y.append(links.copy(own, own, Y))
                self.core_x.append(links.copy(own, far_core.at[z, y, :, part], CORE))
                self.core_y.append(links.copy(other, far_core.at[z, 1 - y, :, part], CORE))

    def start(self):
        for copy in self.over_x:
            copy.start()

    def onward(self, k):
        self.over_x[k].wait_recv()
        self.over_y[k].start()
        self.core_x[k].start()

    def last(self, k):
        self.over_y[k].wait_recv()
        self.core_y[k].start()

    def end(self):
        for copy in self.over_x + self.over_y:
            copy.wait_send()
        for copy in self.core_x + self.core_y:
            copy.wait()


class RowSum:
    def __init__(self, links, terms, buffers):
        self.near, self.far, self.got_near, self.got_far, self.got_x = buffers
        count = self.near.shape[0]

        def rows(distance):
            start = pl.multiple_of((links.tensor ^ distance) * count, count)
            return terms.at[pl.ds(start, count)]

        self.loads = [links.local(rows(0), self.near), links.local(rows(2), self.far)]
        self.core = [links.copy(rows(3), self.got_far, CORE), links.copy(rows(1), self.got_near, CORE)]
        self.over_x = links.copy(self.far, self.got_x, X)

    def start(self):
        for copy in self.loads[::-1] + self.core:
            copy.start()

    def middle(self):
        self.loads[1].wait()
        self.core[0].wait_recv()

        def add(rows):
            self.far[rows, :] = (self.far[rows, :].astype(F32) + self.got_far[rows, :].astype(F32)).astype(BF16)

        by_rows(self.far.shape[0], 64, add)
        self.over_x.start()

    def end(self):
        self.loads[0].wait()
        self.core[1].wait_recv()
        self.over_x.wait_recv()
        for copy in self.core + [self.over_x]:
            copy.wait_send()

    def total(self, rows):
        return self.near[rows, :].astype(F32) + self.got_near[rows, :].astype(F32) + self.got_x[rows, :].astype(F32)


def row_sum_scratch(count, width):
    return [pltpu.VMEM((count, width), BF16)] * 5


class Everywhere:
    def __init__(self, links, held, slots, n):
        self.held, self.slots = held, slots
        ways = everywhere_ways(n)
        self.copies = [links.copy(held.at[k], slots.at[k], way) for k, way in enumerate(ways)]

    def start(self, step):
        self.copies[step].start()

    def finish(self, step):
        self.copies[step].wait()
        self.held[step + 1] = self.held[step] + self.slots[step]


def everywhere_ways(n):
    return [CORE, X, Y] + z_ways(n)


def everywhere_scratch(k, c, n):
    steps = len(everywhere_ways(n))
    return [pltpu.VMEM((steps + 1, k, c), F32), pltpu.VMEM((steps, k, c), F32)]


def middle_kernel(
    back_ref, rows_ref, grad_ref, norm_ref, down_ref, cross_ref,
    wide_out, grad_out, sums_ref, down_out, diagonal_out,
    low, column, slots, send_sems, recv_sems, local_sems, *, n
):
    links = Links(send_sems, recv_sems, local_sems)
    count = low.shape[0]
    load = links.local(down_ref, column)
    load.start()
    collect = Collect(links, column, slots)

    def place(distance):
        return wide_out.at[pl.ds(pl.multiple_of((links.tensor ^ distance) * count, count), count)]

    own = links.local(low, place(0))
    half = count // 2
    parts = [pl.ds(0, half), pl.ds(half, half)]
    over_x = [links.copy(low.at[part], place(0).at[part], X) for part in parts]
    over_core = links.copy(low, place(0), CORE)
    onward = [links.copy(place(2).at[part], place(2).at[part], CORE) for part in parts]
    over_y = links.copy(cross_ref.at[1, :, 1 - links.dp % 2], diagonal_out, Y)
    links.greet([CORE, X, Y] + z_ways(n))
    over_y.start()
    load.wait()
    collect.start(0)
    sums_ref[...] = jnp.zeros_like(sums_ref)

    def norm_back(rows):
        incoming = back_ref[rows, :]
        rows_grad, gain_terms = norm_rows_back(rows_ref[rows, :], incoming, norm_ref[0:1, :])
        rows_grad = rows_grad + grad_ref[rows, :]
        rounded = rows_grad.astype(BF16)
        grad_out[rows, :] = rows_grad
        low[rows, :] = rounded
        for k, terms in enumerate((gain_terms, incoming, rounded.astype(F32))):
            sums_ref[k : k + 1, :] += jnp.sum(terms, axis=0, keepdims=True)

    for part, copy in zip(parts, over_x):
        by_rows(half, 64, lambda rows, part=part: norm_back(pl.ds(pl.multiple_of(part.start + rows.start, 64), 64)))
        copy.start()
    own.start()
    over_core.start()
    for step in range(len(collect.stages) - 1):
        collect.finish(step)
        collect.start(step + 1)
    for copy, later in zip(over_x, onward):
        copy.wait_recv()
        later.start()
    collect.finish(len(collect.stages) - 1)
    down_out[...] = column[collect.z].astype(F32)
    collect.drain()
    own.wait()
    for copy in over_x:
        copy.wait_send()
    over_core.wait()
    for copy in onward:
        copy.wait()
    over_y.wait()


def middle(back, rows, grad, norm, down_column, cross_sum):
    n = lax.axis_size("dp")
    count, width = rows.shape
    m, r, c = down_column.shape
    vmem = pl.BlockSpec(memory_space=pltpu.VMEM)
    return pl.pallas_call(
        functools.partial(middle_kernel, n=n),
        in_specs=[vmem, vmem, vmem, vmem, ANY, ANY],
        out_specs=[ANY, vmem, vmem, vmem, ANY],
        out_shape=[
            jax.ShapeDtypeStruct((4 * count, width), BF16),
            jax.ShapeDtypeStruct((count, width), F32),
            jax.ShapeDtypeStruct((8, width), F32),
            jax.ShapeDtypeStruct((r, c), F32),
            jax.ShapeDtypeStruct((m, r, cross_sum.shape[4]), BF16),
        ],
        scratch_shapes=[
            pltpu.VMEM((count, width), BF16),
            pltpu.VMEM((m, r, c), BF16),
            pltpu.VMEM((m, r, c), BF16),
        ]
        + link_scratch(6 + m, 2),
        compiler_params=pltpu.CompilerParams(
            vmem_limit_bytes=VMEM_LIMIT, collective_id=6, has_side_effects=True
        ),
        cost_estimate=pl.CostEstimate(flops=0, bytes_accessed=100 * 2**20, transcendentals=0),
        name="middle",
    )(back, rows, grad, norm, down_column, cross_sum)


def tail_kernel(
    dq_ref, dk_ref, dv_ref, w_ref, first_ref, so_ref, rows_ref, grad_ref, norm_ref, late_ref,
    grad_out, weights_out, late_out, give, acc, weights, *scratch, n, step_rows
):
    links = Links(*scratch[-3:])
    near, far, got_near, got_far, got_x = scratch[:5]
    columns, gots, slots = scratch[5:7], scratch[7:9], scratch[9:11]
    held, late_slots = scratch[11:13]
    count, model = near.shape
    width = dq_ref.shape[1]
    y = links.dp % 2
    c = columns[0].shape[2]
    m, _, r, _ = weights.shape
    half = count // 2
    parts = [pl.ds(0, half), pl.ds(half, half)]
    core_far = links.copy(give.at[0], got_far, CORE)
    core_near = links.copy(give.at[1], got_near, CORE)
    over_x = [links.copy(far.at[part], got_x.at[part], X) for part in parts]
    over_y, collects = [], []
    for k, (column, got, slot) in enumerate(zip(columns, gots, slots)):
        over_y.append(links.copy(weights.at[:, 1 - y, :, pl.ds(k * c, c)], got, Y))
        collects.append(Collect(links, column, slot))
    late = Everywhere(links, held, late_slots, n)
    links.greet(everywhere_ways(n))

    def terms(distance, target):
        base = (links.tensor ^ distance) * count

        def one(rows):
            there = pl.ds(pl.multiple_of(base + rows.start, 128), 128)
            total = dot_nt(dq_ref[there, :], w_ref[:, :width])
            total = total + dot_nt(dk_ref[there, :], w_ref[:, width : 2 * width])
            target[rows, :] = (total + dot_nt(dv_ref[there, :], w_ref[:, 2 * width : 3 * width])).astype(BF16)

        by_rows(count, 128, one)

    terms(3, give.at[0])
    core_far.start()
    terms(2, far)
    core_far.wait_recv()
    for part, copy in zip(parts, over_x):

        def add(rows, part=part):
            there = pl.ds(pl.multiple_of(part.start + rows.start, 64), 64)
            far[there, :] = (far[there, :].astype(F32) + got_far[there, :].astype(F32)).astype(BF16)

        by_rows(half, 64, add)
        copy.start()

    acc[...] = jnp.zeros_like(acc)

    def products(rows):
        source = first_ref[rows, :].T
        for k, ref in enumerate((dq_ref, dk_ref, dv_ref)):
            acc[:, k * width : (k + 1) * width] += dot_nn(source, ref[rows, :])

    by_rows(dq_ref.shape[0], step_rows, products)
    for k in range(2 * m):
        span = slice(k * r, (k + 1) * r)
        weights[k // 2, k % 2, :, : 3 * width] = acc[span, :].astype(BF16)
        weights[k // 2, k % 2, :, 3 * width :] = so_ref[span, :]
    over_y[0].start()
    terms(1, give.at[1])
    core_near.start()
    terms(0, near)
    for k in range(2):
        columns[k][...] = weights[:, y, :, k * c : (k + 1) * c]
    for k in range(2):
        over_y[k].wait_recv()
        if k == 0:
            over_y[1].start()
        add_to(columns[k], gots[k])
        collects[k].start(0)
    stages = len(collects[0].stages)
    held[0] = late_ref[...]
    core_near.wait_recv()
    for part, copy in zip(parts, over_x):
        copy.wait_recv()

        def norm_back(rows, part=part):
            rows = pl.ds(pl.multiple_of(part.start + rows.start, 64), 64)
            incoming = near[rows, :].astype(F32) + got_near[rows, :].astype(F32) + got_x[rows, :].astype(F32)
            rows_grad, gain_terms = norm_rows_back(rows_ref[rows, :].astype(F32), incoming, norm_ref[0:1, :])
            grad_out[rows, :] = rows_grad + grad_ref[rows, :]
            held[0, 0:1, :] += jnp.sum(gain_terms, axis=0, keepdims=True)
            held[0, 1:2, :] += jnp.sum(incoming, axis=0, keepdims=True)

        by_rows(half, 64, norm_back)
        if part is parts[0]:
            for step in range(stages - 1):
                for k in range(2):
                    collects[k].finish(step)
                    collects[k].start(step + 1)
    steps = len(late.copies)
    for step in range(steps):
        late.start(step)
        if step == 1:
            for k in range(2):
                collects[k].finish(stages - 1)
                weights_out[:, k * c : (k + 1) * c] = columns[k][collects[k].z].astype(F32)
        late.finish(step)
    late_out[...] = held[steps]
    for copy in over_x + over_y + [core_near, core_far]:
        copy.wait_send()
    for collect in collects:
        collect.drain()


def tail(dq, dk, dv, w, first, so_grad, rows, grad, norm, late):
    n = lax.axis_size("dp")
    count, model = rows.shape
    total, width = dq.shape
    m, r, c = n // 2, model // n, 4 * width
    vmem = pl.BlockSpec(memory_space=pltpu.VMEM)
    part = pltpu.VMEM((m, r, c // 2), BF16)
    return pl.pallas_call(
        functools.partial(tail_kernel, n=n, step_rows=512),
        in_specs=[vmem] * 10,
        out_specs=[vmem, vmem, vmem],
        out_shape=[
            jax.ShapeDtypeStruct((count, model), F32),
            jax.ShapeDtypeStruct((r, c), F32),
            jax.ShapeDtypeStruct(late.shape, F32),
        ],
        scratch_shapes=[
            pltpu.VMEM((2, count, model), BF16),
            pltpu.VMEM((model, 3 * width), F32),
            pltpu.VMEM((m, 2, r, c), BF16),
        ]
        + row_sum_scratch(count, model)
        + [part] * 6
        + everywhere_scratch(*late.shape, n)
        + link_scratch(6 + 2 * m + len(everywhere_ways(n)), 1),
        compiler_params=pltpu.CompilerParams(
            vmem_limit_bytes=VMEM_LIMIT, collective_id=7, has_side_effects=True
        ),
        cost_estimate=pl.CostEstimate(flops=0, bytes_accessed=100 * 2**20, transcendentals=0),
        name="tail",
    )(dq, dk, dv, w, first, so_grad, rows, grad, norm, late)


def start_kernel(rows_ref, self_ref, cross_ref, rows_out, self_out, cross_out, send_sems, recv_sems, local_sems, *, n):
    links = Links(send_sems, recv_sems, local_sems)
    member, z, y = links.tensor, links.dp // 2, links.dp % 2
    count = rows_ref.shape[0]
    half = count // 2
    parts = [pl.ds(0, half), pl.ds(half, half)]

    def place(distance):
        return rows_out.at[pl.ds(pl.multiple_of((member ^ distance) * count, count), count)]

    over_x = [links.copy(rows_ref.at[part], place(0).at[part], X) for part in parts]
    over_core = [links.copy(rows_ref, place(0), CORE)]
    over_core += [links.copy(place(2).at[part], place(2).at[part], CORE) for part in parts]
    self_stages = column_stages(links, self_ref, self_out.at[:, y], n)
    cross_stages = column_stages(links, cross_ref, cross_out, n)
    over_y = [links.copy(self_ref, self_out.at[z, y], Y)]
    local = [
        links.local(rows_ref, place(0)),
        links.local(self_ref, self_out.at[z, y]),
        links.local(cross_ref, cross_out.at[z]),
    ]
    links.greet([CORE, X, Y] + z_ways(n))
    for copy in over_x + over_y + over_core[:1] + local:
        copy.start()
    for self_stage in self_stages:
        for copy, _ in self_stage:
            copy.start()
        for copy, index in self_stage:
            copy.wait_recv()
            onward = links.copy(self_out.at[index, y], self_out.at[index, y], Y)
            onward.start()
            over_y.append(onward)
        if self_stage is self_stages[0]:
            for copy, _ in cross_stages[0]:
                copy.start()
    for cross_stage, later in zip(cross_stages, cross_stages[1:] + [[]]):
        for copy, _ in cross_stage:
            copy.wait_recv()
        for copy, _ in later:
            copy.start()
    for copy, onward in zip(over_x, over_core[1:]):
        copy.wait_recv()
        onward.start()
    for copy in local + over_y + over_core:
        copy.wait()
    for copy in over_x:
        copy.wait_send()
    for stage in self_stages + cross_stages:
        for copy, _ in stage:
            copy.wait_send()


def start_gather(rows_low, self_shard, cross_shard):
    n = lax.axis_size("dp")
    r, c = self_shard.shape
    return pl.pallas_call(
        functools.partial(start_kernel, n=n),
        in_specs=[pl.BlockSpec(memory_space=pltpu.VMEM)] * 3,
        out_specs=[ANY] * 3,
        out_shape=[
            jax.ShapeDtypeStruct((4 * rows_low.shape[0], rows_low.shape[1]), BF16),
            jax.ShapeDtypeStruct((n // 2, 2, r, c), BF16),
            jax.ShapeDtypeStruct((n // 2,) + cross_shard.shape, BF16),
        ],
        scratch_shapes=link_scratch(2 * n + 8, 3),
        compiler_params=pltpu.CompilerParams(collective_id=0, has_side_effects=True),
        cost_estimate=pl.CostEstimate(flops=0, bytes_accessed=100 * 2**20, transcendentals=0),
        name="start_gather",
    )(rows_low, self_shard, cross_shard)


def self_forward_kernel(
    b_ref, x_ref, w_ref, bq_ref, bv_ref, column_ref, shard_ref, enc_ref,
    q_out, k_ref, v_out, kt_out, ot_ref, lse_ref, terms_ref, whole, next_column, enc_out,
    vt_ref, m_s, l_s, acc, column, send_sems, recv_sems, local_sems, *, bk, heads, safe, n
):
    i = pl.program_id(0)
    last = pl.num_programs(0) - 1
    bq, width = q_out.shape
    links = Links(send_sems, recv_sems, local_sems)
    spread = Spread(links, column_ref, column, whole)
    stages = column_stages(links, shard_ref, next_column, n)
    enc_count = enc_ref.shape[0]

    def place(distance):
        return enc_out.at[pl.ds(pl.multiple_of((links.tensor ^ distance) * enc_count, enc_count), enc_count)]

    enc_x = links.copy(enc_ref, place(0), X)
    enc_core = [links.copy(enc_ref, place(0), CORE), links.copy(place(2), place(2), CORE)]
    local = [links.local(shard_ref, next_column.at[links.dp // 2]), links.local(enc_ref, place(0))]

    @pl.when(i == 0)
    def _():
        links.greet([CORE, X, Y] + z_ways(n))
        spread.start()
        for copy in local + enc_core[:1]:
            copy.start()
        for copy, _ in stages[0]:
            copy.start()

    @pl.when(i == last)
    def _():
        spread.middle()
        enc_x.start()
        for k in range(1, len(stages)):
            for copy, _ in stages[k - 1]:
                copy.wait_recv()
            for copy, _ in stages[k]:
                copy.start()

    projected = dot_nn(x_ref[...], w_ref[:, : 3 * width])
    query = (projected[:, :width] + bq_ref[...]).astype(BF16)
    key = projected[:, width : 2 * width].astype(BF16)
    value = (projected[:, 2 * width :] + bv_ref[...]).astype(BF16)
    here = pl.ds(pl.multiple_of(i * bq, bq), bq)
    q_out[...] = query
    v_out[...] = value
    kt_out[...] = key.T
    k_ref[here, :] = key
    vt_ref[:, here] = value.T

    m_s[...] = jnp.full_like(m_s, NEGATIVE)
    l_s[...] = jnp.zeros_like(l_s)
    acc[...] = jnp.zeros_like(acc)
    hd = width // heads
    scaled = query * jnp.asarray(1.0 / math.sqrt(hd), BF16)
    q_heads = [head_only(scaled, h, hd) for h in range(heads)]

    def block(j, mode):
        rows = pl.ds(pl.multiple_of(j * bk, bk), bk)
        keys = k_ref[rows, :]
        m_old = m_s[...]
        l_old = l_s[...]
        scores = [dot_nt(keys, q_heads[h]) for h in range(heads)]
        if mode != "none":
            bad = self_bad(b_ref, i * bq, j * bk, bq, bk, mode == "causal")
            scores = [jnp.where(bad, NEGATIVE, s) for s in scores]
        m_out, l_out, a_out = [], [], []
        for h in range(heads):
            part = slice(h * hd, (h + 1) * hd)
            m_new = jnp.maximum(m_old[h : h + 1, :], jnp.max(scores[h], axis=0, keepdims=True))
            shrink = jnp.exp(m_old[h : h + 1, :] - m_new)
            expos = jnp.exp(scores[h] - m_new)
            l_out.append(l_old[h : h + 1, :] * shrink + jnp.sum(expos, axis=0, keepdims=True))
            m_out.append(m_new)
            a_out.append(acc[part, :] * shrink + dot_nn(vt_ref[part, rows], expos.astype(BF16)))
        m_s[...] = jnp.concatenate(m_out, 0)
        l_s[...] = jnp.concatenate(l_out, 0)
        for h in range(heads):
            acc[h * hd : (h + 1) * hd, :] = a_out[h]

    over_keys(i, bq, bk, safe, block)
    inverse = 1.0 / l_s[...]
    for h in range(heads):
        part = slice(h * hd, (h + 1) * hd)
        ot_ref[part, :] = (acc[part, :] * inverse[h : h + 1, :]).astype(BF16)
    lse_ref[...] = m_s[...] + jnp.log(l_s[...])
    terms_ref[...] = dot_nt(ot_ref[...].T, w_ref[:, 3 * width :]).astype(BF16)

    @pl.when(i == last)
    def _():
        spread.end()
        enc_x.wait_recv()
        enc_core[1].start()
        for k, stage in enumerate(stages):
            for copy, _ in stage:
                copy.wait_send()
                if k == len(stages) - 1:
                    copy.wait_recv()
        enc_x.wait_send()
        for copy in local + enc_core:
            copy.wait()


def self_forward(bounds, x, w, q_shift, v_shift, column, shard, encoder, heads, safe):
    n, model = x.shape
    width = w.shape[1] // 4
    bq = bk = 512
    dp = lax.axis_size("dp")
    m, r, c = column.shape
    enc_count = encoder.shape[0]
    by_rows_spec = pl.BlockSpec((bq, width), lambda i: (i, 0))
    by_columns_spec = pl.BlockSpec((width, bq), lambda i: (0, i))
    return pl.pallas_call(
        functools.partial(self_forward_kernel, bk=bk, heads=heads, safe=safe, n=dp),
        grid=(n // bq,),
        in_specs=[
            pl.BlockSpec(memory_space=pltpu.SMEM),
            pl.BlockSpec((bq, model), lambda i: (i, 0)),
            const((model, 4 * width)),
            const((1, width)),
            const((1, width)),
            ANY,
            const(shard.shape),
            const(encoder.shape),
        ],
        out_specs=[
            by_rows_spec,
            const((n, width)),
            by_rows_spec,
            by_columns_spec,
            by_columns_spec,
            pl.BlockSpec((heads, bq), lambda i: (0, i)),
            pl.BlockSpec((bq, model), lambda i: (i, 0)),
            ANY,
            ANY,
            ANY,
        ],
        out_shape=[
            jax.ShapeDtypeStruct((n, width), BF16),
            jax.ShapeDtypeStruct((n, width), BF16),
            jax.ShapeDtypeStruct((n, width), BF16),
            jax.ShapeDtypeStruct((width, n), BF16),
            jax.ShapeDtypeStruct((width, n), BF16),
            jax.ShapeDtypeStruct((heads, n), F32),
            jax.ShapeDtypeStruct((n, model), BF16),
            jax.ShapeDtypeStruct((4, m, 2, r, c), BF16),
            jax.ShapeDtypeStruct((m,) + shard.shape, BF16),
            jax.ShapeDtypeStruct((4 * enc_count, model), BF16),
        ],
        scratch_shapes=[
            pltpu.VMEM((width, n), BF16),
            pltpu.VMEM((heads, bq), F32),
            pltpu.VMEM((heads, bq), F32),
            pltpu.VMEM((width, bq), F32),
            pltpu.VMEM((m, r, c), BF16),
        ]
        + link_scratch(11 + m, 4),
        compiler_params=pltpu.CompilerParams(
            vmem_limit_bytes=VMEM_LIMIT, collective_id=1, has_side_effects=True
        ),
        cost_estimate=pl.CostEstimate(
            flops=12 * n * n * width, bytes_accessed=8 * n * width, transcendentals=n * n * heads // 2
        ),
        name="self_forward",
    )(bounds, x, w, q_shift, v_shift, column, shard, encoder)


def after_self_kernel(
    terms_ref, rows_ref, shift_ref, norm_ref, column_ref,
    after_out, second_out, whole_out, *scratch
):
    links = Links(*scratch[-3:])
    rows_sum = RowSum(links, terms_ref, scratch[:5])
    column = scratch[5]
    y = links.dp % 2
    near_out, core_out = whole_out.at[0], whole_out.at[1]
    load = links.local(column_ref, column)
    own = links.local(column, near_out.at[:, y])
    over_y = links.copy(column, near_out.at[:, y], Y)
    over_core = [
        links.copy(column, core_out.at[:, y], CORE),
        links.copy(near_out.at[:, 1 - y], core_out.at[:, 1 - y], CORE),
    ]
    links.greet([CORE, X, Y])
    rows_sum.start()
    load.start()
    load.wait()
    over_y.start()
    own.start()
    rows_sum.middle()
    over_core[0].start()
    rows_sum.end()

    def norm(rows):
        after = rows_ref[rows, :].astype(F32) + rows_sum.total(rows) + shift_ref[...]
        after_out[rows, :] = after
        xhat, _ = normalized(after)
        second_out[rows, :] = (xhat * norm_ref[0:1, :] + norm_ref[1:2, :]).astype(BF16)

    by_rows(after_out.shape[0], 64, norm)
    over_y.wait_recv()
    over_core[1].start()
    over_y.wait_send()
    own.wait()
    for copy in over_core:
        copy.wait()


def sum_after_self(terms, rows, shift, norm, column):
    count, model = rows.shape
    m, r, c = column.shape
    vmem = pl.BlockSpec(memory_space=pltpu.VMEM)
    return pl.pallas_call(
        after_self_kernel,
        in_specs=[ANY, vmem, vmem, vmem, ANY],
        out_specs=[vmem, vmem, ANY],
        out_shape=[
            jax.ShapeDtypeStruct((count, model), F32),
            jax.ShapeDtypeStruct((count, model), BF16),
            jax.ShapeDtypeStruct((2, m, 2, r, c), BF16),
        ],
        scratch_shapes=row_sum_scratch(count, model) + [pltpu.VMEM((m, r, c), BF16)] + link_scratch(6, 4),
        compiler_params=pltpu.CompilerParams(
            vmem_limit_bytes=VMEM_LIMIT, collective_id=8, has_side_effects=True
        ),
        cost_estimate=pl.CostEstimate(flops=0, bytes_accessed=100 * 2**20, transcendentals=0),
        name="sum_after_self",
    )(terms, rows, shift, norm, column)


def self_backward_kernel(
    b_ref, q_ref, k_ref, v_ref, kt_ref, wide_ref, w_ref, mt_ref, lse_ref,
    up_ref, cross_ref, diagonal_ref, enc_ref,
    dq_ref, dk_ref, dv_ref, up_out, cross_out, enc_out, dka, dva, dqa, *scratch, bk, heads, safe, n
):
    i = pl.program_id(0)
    links = Links(*scratch[-3:])
    cross = GatherLast(links, cross_ref.at[0], cross_ref.at[1], diagonal_ref, scratch[:5])
    cross_z = Collect(links, cross.column, scratch[5])
    up_column = scratch[6]
    up_z = Collect(links, up_column, scratch[7])
    load = links.local(up_ref, up_column)
    enc = RowSum(links, enc_ref, scratch[8:13])
    stages = len(up_z.stages)

    @pl.when(i == 0)
    def _():
        links.greet(everywhere_ways(n))
        cross.start()
        enc.start()
        load.start()
        load.wait()
        up_z.start(0)
        dka[...] = jnp.zeros_like(dka)
        dva[...] = jnp.zeros_like(dva)

    @pl.when(i == 1)
    def _():
        cross.middle()

    @pl.when(i == 2)
    def _():
        for step in range(stages - 1):
            up_z.finish(step)
            up_z.start(step + 1)

    def sum_cross():
        cross.end()
        cross_z.start(0)
        enc.middle()

    def next_cross():
        for step in range(stages - 1):
            cross_z.finish(step)
            cross_z.start(step + 1)

    bq, width = q_ref.shape
    hd = width // heads
    scale = 1.0 / math.sqrt(hd)
    grads = dot_nn(wide_ref[...], w_ref[:, 3 * width :]).astype(BF16)
    products = grads.T.astype(F32) * mt_ref[...].astype(F32)
    inner = [jnp.sum(products[h * hd : (h + 1) * hd, :], axis=0, keepdims=True) for h in range(heads)]
    scaled = q_ref[...] * jnp.asarray(scale, BF16)
    q_heads = [head_only(scaled, h, hd) for h in range(heads)]
    d_heads = [head_only(grads, h, hd) for h in range(heads)]
    lse = lse_ref[...]
    dqa[...] = jnp.zeros_like(dqa)

    def block(j, mode):
        rows = pl.ds(pl.multiple_of(j * bk, bk), bk)
        keys = k_ref[rows, :]
        values = v_ref[rows, :]
        scores = [dot_nt(keys, q_heads[h]) for h in range(heads)]
        dprobs = [dot_nt(values, d_heads[h]) for h in range(heads)]
        if mode != "none":
            bad = self_bad(b_ref, i * bq, j * bk, bq, bk, mode == "causal")
            scores = [jnp.where(bad, NEGATIVE, s) for s in scores]
        dv_sum, dk_sum = None, None
        for h in range(heads):
            part = slice(h * hd, (h + 1) * hd)
            probs = jnp.exp(scores[h] - lse[h : h + 1, :])
            ds = (probs * (dprobs[h] - inner[h])).astype(BF16)
            dv_h = dot_nn(probs.astype(BF16), d_heads[h])
            dk_h = dot_nn(ds, q_heads[h])
            dv_sum = dv_h if dv_sum is None else dv_sum + dv_h
            dk_sum = dk_h if dk_sum is None else dk_sum + dk_h
            dqa[part, :] += dot_nn(kt_ref[part, rows], ds)
        dva[rows, :] += dv_sum
        dka[rows, :] += dk_sum

    over_keys(i, bq, bk, safe, block, [(3, 2, sum_cross), (4, 2, next_cross)])
    dq_ref[...] = (dqa[...] * scale).astype(BF16).T

    @pl.when(i == pl.num_programs(0) - 1)
    def _():
        dk_ref[...] = dka[...].astype(BF16)
        dv_ref[...] = dva[...].astype(BF16)
        up_z.finish(stages - 1)
        up_out[...] = up_column[up_z.z].astype(F32)
        cross_z.finish(stages - 1)
        cross_out[...] = cross.column[cross_z.z].astype(F32)
        enc.end()

        def store(rows):
            enc_out[rows, :] = enc.total(rows)

        by_rows(enc_out.shape[0], 64, store)
        up_z.drain()
        cross_z.drain()


def self_backward(
    bounds, queries, keys, values, keys_t, wide, w, mixed_t, lse,
    up_column, cross_sum, diagonal, enc_terms, heads, safe
):
    n, width = queries.shape
    model = wide.shape[1]
    dp = lax.axis_size("dp")
    m, r, c = up_column.shape
    cross_c = cross_sum.shape[4]
    enc_shape = (enc_terms.shape[0] // 4, enc_terms.shape[1])
    bq = bk = 512
    some = pl.BlockSpec((bq, width), lambda i: (i, 0))
    return pl.pallas_call(
        functools.partial(self_backward_kernel, bk=bk, heads=heads, safe=safe, n=dp),
        grid=(n // bq,),
        in_specs=[
            pl.BlockSpec(memory_space=pltpu.SMEM),
            some,
            const((n, width)),
            const((n, width)),
            const((width, n)),
            pl.BlockSpec((bq, model), lambda i: (i, 0)),
            const((model, 4 * width)),
            pl.BlockSpec((width, bq), lambda i: (0, i)),
            pl.BlockSpec((heads, bq), lambda i: (0, i)),
        ]
        + [ANY] * 4,
        out_specs=[some, const((n, width)), const((n, width))]
        + [const((r, c)), const((r, cross_c)), const(enc_shape)],
        out_shape=[
            jax.ShapeDtypeStruct((n, width), BF16),
            jax.ShapeDtypeStruct((n, width), BF16),
            jax.ShapeDtypeStruct((n, width), BF16),
            jax.ShapeDtypeStruct((r, c), F32),
            jax.ShapeDtypeStruct((r, cross_c), F32),
            jax.ShapeDtypeStruct(enc_shape, F32),
        ],
        scratch_shapes=[
            pltpu.VMEM((n, width), F32),
            pltpu.VMEM((n, width), F32),
            pltpu.VMEM((width, bq), F32),
        ]
        + [pltpu.VMEM((m, r, cross_c), BF16)] * 6
        + [pltpu.VMEM((m, r, c), BF16)] * 2
        + row_sum_scratch(*enc_shape)
        + link_scratch(5 + 2 * m, 6),
        compiler_params=pltpu.CompilerParams(
            vmem_limit_bytes=VMEM_LIMIT, collective_id=5, has_side_effects=True
        ),
        cost_estimate=pl.CostEstimate(
            flops=24 * n * n * width, bytes_accessed=16 * n * width, transcendentals=n * n * heads // 2
        ),
        name="self_backward",
    )(bounds, queries, keys, values, keys_t, wide, w, mixed_t, lse, up_column, cross_sum, diagonal, enc_terms)


def const(shape):
    return pl.BlockSpec(shape, lambda *_: (0,) * len(shape), pipeline_mode=pl.Buffered(1))


def normalized(rows):
    center = rows - jnp.mean(rows, axis=-1, keepdims=True)
    scale = lax.rsqrt(jnp.mean(center * center, axis=-1, keepdims=True) + EPSILON)
    return center * scale, scale


def norm_rows_back(rows, incoming, gain):
    xhat, scale = normalized(rows)
    e = incoming * gain
    inner = jnp.mean(e * xhat, axis=-1, keepdims=True)
    return scale * (e - jnp.mean(e, axis=-1, keepdims=True) - xhat * inner), incoming * xhat


def by_rows(count, step, body):
    def one(k, c):
        body(pl.ds(pl.multiple_of(k * step, step), step))
        return c

    lax.fori_loop(0, count // step, one, 0)


def cross_forward_kernel(
    ok_ref, x_ref, enc_ref, w_ref, bq_ref, bv_ref, rows_ref, shift_ref, norm_ref, column_ref,
    q_out, k_out, v_out, ot_ref, lse_ref, after_ref, third_ref, whole, send_sems, recv_sems, local_sems, *, heads
):
    i = pl.program_id(0)
    last = pl.num_programs(0) - 1
    links = Links(send_sems, recv_sems, local_sems)
    spread = SpreadFar(links, column_ref, whole)
    pieces = len(spread.over_x)

    @pl.when(i == 0)
    def _():
        links.greet([CORE, X, Y])
        spread.start()
        after_ref[...] = rows_ref[...] + shift_ref[...]

    for step, ready in ((1, (0,)), (2, (1, 2)), (3, (3,))):

        @pl.when(i == step)
        def _():
            for k in ready:
                spread.onward(k)

    width = q_out.shape[2]
    hd = width // heads
    query = (dot_nn(x_ref[...], w_ref[0, :, :width]) + bq_ref[0]).astype(BF16)
    key_value = dot_nn(enc_ref[...], w_ref[0, :, width : 3 * width])
    keys = key_value[:, :width].astype(BF16)
    values = (key_value[:, width:] + bv_ref[0]).astype(BF16)
    q_out[0] = query
    k_out[0] = keys
    v_out[0] = values
    values_t = values.T
    scaled = query * jnp.asarray(1.0 / math.sqrt(hd), BF16)
    ok = ok_ref[...] > 0.0
    scores = [dot_nt(keys, head_only(scaled, h, hd)) for h in range(heads)]
    mixed = []
    for h in range(heads):
        part = slice(h * hd, (h + 1) * hd)
        s = jnp.where(ok, scores[h], NEGATIVE)
        largest = jnp.max(s, axis=0, keepdims=True)
        expos = jnp.exp(s - largest)
        total = jnp.sum(expos, axis=0, keepdims=True)
        mixed.append((dot_nn(values_t[part, :], expos.astype(BF16)) * (1.0 / total)).astype(BF16))
        ot_ref[0, part, :] = mixed[h]
        lse_ref[0, h : h + 1, :] = largest + jnp.log(total)
    after_ref[...] += dot_nt(jnp.concatenate(mixed, 0).T, w_ref[0, :, 3 * width :])

    @pl.when(i == last)
    def _():
        def norm(rows):
            xhat, _ = normalized(after_ref[rows, :])
            third_ref[rows, :] = (xhat * norm_ref[0:1, :] + norm_ref[1:2, :]).astype(BF16)

        by_rows(after_ref.shape[0], 128, norm)
        for k in range(4, pieces):
            spread.onward(k)
        for k in range(pieces):
            spread.last(k)
        spread.end()


def cross_forward(ok, x, encoder, weights, q_shift, v_shift, rows, shift, norm, column, heads):
    count, model = x.shape
    n = encoder.shape[0]
    parts, _, columns = weights.shape
    width = columns // 4
    m, r, c = column.shape

    def by_part(*shape):
        return pl.BlockSpec((1,) + shape, lambda i: (i,) + (0,) * len(shape))

    return pl.pallas_call(
        functools.partial(cross_forward_kernel, heads=heads),
        grid=(parts,),
        in_specs=[
            const((n, 1)),
            const((count, model)),
            const((n, model)),
            by_part(model, columns),
            by_part(1, width),
            by_part(1, width),
            const((count, model)),
            const((1, model)),
            const((2, model)),
            ANY,
        ],
        out_specs=[
            by_part(count, width),
            by_part(n, width),
            by_part(n, width),
            by_part(width, count),
            by_part(heads, count),
            const((count, model)),
            const((count, model)),
            ANY,
        ],
        out_shape=[
            jax.ShapeDtypeStruct((parts, count, width), BF16),
            jax.ShapeDtypeStruct((parts, n, width), BF16),
            jax.ShapeDtypeStruct((parts, n, width), BF16),
            jax.ShapeDtypeStruct((parts, width, count), BF16),
            jax.ShapeDtypeStruct((parts, heads, count), F32),
            jax.ShapeDtypeStruct((count, model), F32),
            jax.ShapeDtypeStruct((count, model), BF16),
            jax.ShapeDtypeStruct((2, m, 2, r, c), BF16),
        ],
        scratch_shapes=link_scratch(32, 1),
        compiler_params=pltpu.CompilerParams(
            vmem_limit_bytes=VMEM_LIMIT, collective_id=2, has_side_effects=True
        ),
        cost_estimate=pl.CostEstimate(
            flops=24 * parts * count * n * width,
            bytes_accessed=8 * parts * n * width,
            transcendentals=parts * count * n * heads,
        ),
        name="cross_forward",
    )(ok, x, encoder, weights, q_shift, v_shift, rows, shift, norm, column)


def feed_forward_kernel(
    x_ref, dy_ref, near_ref, far_ref, b_ref, after_ref, shift_ref, norm_ref,
    out_ref, rows_out, low_out, sums_ref, gup_ref, gdown_ref, bias_ref, from_x, from_y,
    xt_ref, dyt_ref, back_ref, give, got, diagonal, loaded, load_sems, send_sems, recv_sems, local_sems, *, chunks
):
    s = pl.program_id(0)
    links = Links(send_sems, recv_sems, local_sems)
    turn = s // chunks
    chunk = s % chunks
    pair = turn // 2
    slot = pair * chunks + chunk
    theirs = turn % 2 == 0
    y = links.dp % 2
    m, r = diagonal.shape[1], diagonal.shape[2]
    low, high = pl.ds(0, m // 2), pl.ds(m // 2, m - m // 2)
    links.used = 2 * chunks
    across = [
        links.copy(diagonal.at[:, low], from_x, X),
        links.copy(diagonal.at[:, high], from_y, Y),
    ]
    to_core = pltpu.make_async_remote_copy(
        src_ref=give.at[chunk],
        dst_ref=got.at[slot],
        send_sem=send_sems.at[slot],
        recv_sem=recv_sems.at[slot],
        device_id=links.partner(CORE),
        device_id_type=pl.DeviceIdType.MESH,
    )

    size = loaded.shape[3]

    def fetch(step, act):
        block = 3 - step // chunks
        slot = step % 2
        first = (step % chunks) * size

        def both(source):
            for k in range(2):
                columns = pl.ds(pl.multiple_of(first + k * chunks * size, size), size)
                act(pltpu.make_async_copy(source.at[:, columns], loaded.at[slot, k], load_sems.at[slot, k]))

        @pl.when(block >= 2)
        def _():
            both(far_ref.at[block - 2])

        @pl.when(block < 2)
        def _():
            both(near_ref.at[block])

    @pl.when(s == 0)
    def _():
        fetch(0, lambda copy: copy.start())
        links.greet([CORE, X, Y])
        out_ref[...] = after_ref[...] + shift_ref[...]
        back_ref[...] = jnp.zeros_like(back_ref)
        xt_ref[...] = x_ref[...].T
        dyt_ref[...] = dy_ref[...].T
        sums_ref[...] = jnp.zeros_like(sums_ref)

    fetch(s, lambda copy: copy.wait())

    @pl.when(s + 1 < pl.num_programs(0))
    def _():
        fetch(s + 1, lambda copy: copy.start())

    up_ref, down_ref = loaded.at[s % 2, 0], loaded.at[s % 2, 1]
    pre_act = dot_nn(x_ref[...], up_ref[...]) + b_ref[0]
    hidden_grad = dot_nn(dy_ref[...], down_ref[...])
    normal_cdf = 0.5 * (1.0 + lax.erf(pre_act * (1.0 / math.sqrt(2.0))))
    density = jnp.exp(-0.5 * pre_act * pre_act) * (1.0 / math.sqrt(2.0 * math.pi))
    hidden = (pre_act * normal_cdf).astype(BF16)
    pre_grad = (hidden_grad * (normal_cdf + pre_act * density)).astype(BF16)
    bias_ref[0] = jnp.sum(pre_grad.astype(F32), axis=0, keepdims=True)

    @pl.when(turn % 2 == 1)
    def _():
        to_core.wait_send()

    give[chunk, 0] = dot_nn(xt_ref[...], pre_grad).astype(BF16)
    give[chunk, 1] = dot_nn(dyt_ref[...], hidden).astype(BF16)
    out_ref[...] += dot_nt(hidden, down_ref[...])
    back_ref[...] += dot_nt(pre_grad, up_ref[...])

    @pl.when(theirs)
    def _():
        to_core.start()

    @pl.when(jnp.logical_not(theirs))
    def _():
        to_core.wait_recv()
        gup_ref[0] = (give[chunk, 0].astype(F32) + got[slot, 0].astype(F32)).astype(BF16)
        gdown_ref[0] = (give[chunk, 1].astype(F32) + got[slot, 1].astype(F32)).astype(BF16)

    for k in range(chunks):

        @pl.when(s == chunks + k)
        def _():
            def keep(z, carry):
                rows = pl.ds(pl.multiple_of((2 * z + 1 - y) * r, r), r)
                size = gup_ref.shape[2]
                diagonal[0, z, :, k * size : (k + 1) * size] = gup_ref[0, rows, :]
                diagonal[1, z, :, k * size : (k + 1) * size] = gdown_ref[0, rows, :]
                return carry

            lax.fori_loop(0, m, keep, 0)
            if k == chunks - 1:
                for copy in across:
                    copy.start()

    @pl.when(s == pl.num_programs(0) - 1)
    def _():
        def norm_back(rows):
            third = back_ref[rows, :]
            upstream = dy_ref[rows, :].astype(F32)
            rows_grad, gain_terms = norm_rows_back(after_ref[rows, :], third, norm_ref[0:1, :])
            rows_grad = rows_grad + upstream
            low = rows_grad.astype(BF16)
            rows_out[rows, :] = rows_grad
            low_out[rows, :] = low
            for k, terms in enumerate((gain_terms, third, low.astype(F32), upstream)):
                sums_ref[k : k + 1, :] += jnp.sum(terms, axis=0, keepdims=True)

        by_rows(x_ref.shape[0], 128, norm_back)
        for copy in across:
            copy.wait()


def feed_forward(x, dy, near, far, bias, after, shift, norm):
    rows, width = x.shape
    hidden = near.shape[2] // 2
    size = min(512, hidden)
    chunks = hidden // size

    n = lax.axis_size("dp")
    m, r = n // 2, width // n

    def block(s):
        return 3 - s // chunks

    def placed(s):
        turn = s // chunks
        return (1 - turn // 2, 0, (s % chunks) * (turn % 2))

    rows_spec = const((rows, width))
    grad_spec = pl.BlockSpec((1, width, size), placed)
    bias_spec = pl.BlockSpec((1, 1, size), lambda s: (block(s), 0, s % chunks))
    return pl.pallas_call(
        functools.partial(feed_forward_kernel, chunks=chunks),
        grid=(4 * chunks,),
        in_specs=[
            rows_spec,
            rows_spec,
            ANY,
            ANY,
            bias_spec,
            rows_spec,
            const((1, width)),
            const((2, width)),
        ],
        out_specs=[rows_spec, rows_spec, rows_spec, const((8, width)), grad_spec, grad_spec, bias_spec, ANY, ANY],
        out_shape=[
            jax.ShapeDtypeStruct((rows, width), F32),
            jax.ShapeDtypeStruct((rows, width), F32),
            jax.ShapeDtypeStruct((rows, width), BF16),
            jax.ShapeDtypeStruct((8, width), F32),
            jax.ShapeDtypeStruct((2, width, hidden), BF16),
            jax.ShapeDtypeStruct((2, width, hidden), BF16),
            jax.ShapeDtypeStruct((4, 1, hidden), F32),
            jax.ShapeDtypeStruct((2, m // 2, r, hidden), BF16),
            jax.ShapeDtypeStruct((2, m - m // 2, r, hidden), BF16),
        ],
        scratch_shapes=[
            pltpu.VMEM((width, rows), BF16),
            pltpu.VMEM((width, rows), BF16),
            pltpu.VMEM((rows, width), F32),
            pltpu.VMEM((chunks, 2, width, size), BF16),
            pltpu.VMEM((2 * chunks, 2, width, size), BF16),
            pltpu.VMEM((2, m, r, hidden), BF16),
            pltpu.VMEM((2, 2, width, size), BF16),
            pltpu.SemaphoreType.DMA((2, 2)),
        ]
        + link_scratch(2 * chunks + 2, 1),
        compiler_params=pltpu.CompilerParams(
            vmem_limit_bytes=VMEM_LIMIT, collective_id=3, has_side_effects=True
        ),
        cost_estimate=pl.CostEstimate(
            flops=48 * rows * width * hidden, bytes_accessed=40 * 2**20, transcendentals=8 * rows * hidden
        ),
        name="feed_forward",
    )(x, dy, near, far, bias, after, shift, norm)


def cross_backward_kernel(
    ok_ref, low_ref, x_ref, enc_ref, w_ref, q_ref, k_ref, v_ref, mt_ref, lse_ref, up_ref, down_ref, from_x, from_y,
    back_ref, enc_out, grad_ref, bq_ref, bv_ref, up_out, down_out,
    low_t, x_t, enc_t, enc_acc, give, got, *scratch, heads, bk
):
    i = pl.program_id(0)
    last = pl.num_programs(0) - 1
    links = Links(*scratch[14:])
    sums = [
        Gather(links, ref.at[0], ref.at[1], from_x.at[k], from_y.at[k], scratch[7 * k : 7 * k + 7])
        for k, ref in enumerate((up_ref, down_ref))
    ]
    leave = [links.local(g.column, out) for g, out in zip(sums, (up_out, down_out))]
    pair = i // 2
    to_core = pltpu.make_async_remote_copy(
        src_ref=give,
        dst_ref=got.at[pair],
        send_sem=links.send_sems.at[links.used + pair],
        recv_sem=links.recv_sems.at[links.used + pair],
        device_id=links.partner(CORE),
        device_id_type=pl.DeviceIdType.MESH,
    )

    @pl.when(i == 0)
    def _():
        links.greet([CORE, X, Y])
        for g in sums:
            g.start()
        low_t[...] = low_ref[...].T
        x_t[...] = x_ref[...].T
        enc_t[...] = enc_ref[...].T
        back_ref[...] = jnp.zeros_like(back_ref)
        enc_acc[...] = jnp.zeros_like(enc_acc)

    @pl.when(i == 1)
    def _():
        for g in sums:
            g.middle()

    rows, width = q_ref.shape[1:]
    n = k_ref.shape[1]
    hd = width // heads
    scale = 1.0 / math.sqrt(hd)
    w_query, w_keyval, w_out = w_ref.at[0, :, :width], w_ref.at[0, :, width : 3 * width], w_ref.at[0, :, 3 * width :]
    grads = dot_nn(low_ref[...], w_out[...]).astype(BF16)
    mixed_t = mt_ref[0]
    products = grads.T.astype(F32) * mixed_t.astype(F32)
    inner = [jnp.sum(products[h * hd : (h + 1) * hd, :], axis=0, keepdims=True) for h in range(heads)]
    scaled = q_ref[0] * jnp.asarray(scale, BF16)
    q_heads = [head_only(scaled, h, hd) for h in range(heads)]
    d_heads = [head_only(grads, h, hd) for h in range(heads)]
    lse = lse_ref[0]
    keys_t = k_ref[0].T
    dq = [None] * heads
    dkv = []
    for j in range(n // bk):
        span = slice(j * bk, (j + 1) * bk)
        keys = k_ref[0, span, :]
        values = v_ref[0, span, :]
        ok = ok_ref[span, :] > 0.0
        scores = [dot_nt(keys, q_heads[h]) for h in range(heads)]
        dprobs = [dot_nt(values, d_heads[h]) for h in range(heads)]
        dv_sum, dk_sum = None, None
        for h in range(heads):
            part = slice(h * hd, (h + 1) * hd)
            probs = jnp.exp(jnp.where(ok, scores[h], NEGATIVE) - lse[h : h + 1, :])
            ds = (probs * (dprobs[h] - inner[h])).astype(BF16)
            dv_h = dot_nn(probs.astype(BF16), d_heads[h])
            dk_h = dot_nn(ds, q_heads[h])
            dv_sum = dv_h if dv_sum is None else dv_sum + dv_h
            dk_sum = dk_h if dk_sum is None else dk_sum + dk_h
            dq_h = dot_nn(keys_t[part, span], ds)
            dq[h] = dq_h if dq[h] is None else dq[h] + dq_h
        block = jnp.concatenate([dk_sum.astype(BF16), dv_sum.astype(BF16)], 1)
        enc_acc[span, :] += dot_nt(block, w_keyval[...])
        dkv.append(block)
    dq = (jnp.concatenate(dq, 0) * scale).astype(BF16).T
    dkv = jnp.concatenate(dkv, 0)
    bq_ref[0] = jnp.sum(dq.astype(F32), axis=0, keepdims=True)
    bv_ref[0] = jnp.sum(dkv[:, width:].astype(F32), axis=0, keepdims=True)
    back_ref[...] += dot_nt(dq, w_query[...])

    @pl.when(i % 2 == 1)
    def _():
        to_core.wait_send()

    give[:, :width] = dot_nn(x_t[...], dq).astype(BF16)
    give[:, width : 3 * width] = dot_nn(enc_t[...], dkv).astype(BF16)
    give[:, 3 * width :] = dot_nn(low_t[...], mixed_t.T).astype(BF16)

    @pl.when(i % 2 == 0)
    def _():
        to_core.start()

    @pl.when(i % 2 == 1)
    def _():
        to_core.wait_recv()
        grad_ref[0] = (give[...].astype(F32) + got[pair].astype(F32)).astype(BF16)

    @pl.when(i == last)
    def _():
        enc_out[...] = enc_acc[...].astype(BF16)
        for g, copy in zip(sums, leave):
            g.end()
            copy.start()
        for copy in leave:
            copy.wait()


def cross_backward(
    ok, low, x, encoder, weights, queries, keys, values, mixed_t, lse, up_sum, down_sum, from_x, from_y, heads
):
    count, model = x.shape
    n = encoder.shape[0]
    parts, _, columns = weights.shape
    width = columns // 4
    _, m, _, r, c = up_sum.shape

    def by_part(*shape):
        return pl.BlockSpec((1,) + shape, lambda i: (i ^ 1,) + (0,) * len(shape))

    return pl.pallas_call(
        functools.partial(cross_backward_kernel, heads=heads, bk=256),
        grid=(parts,),
        in_specs=[
            const((n, 1)),
            const((count, model)),
            const((count, model)),
            const((n, model)),
            by_part(model, columns),
            by_part(count, width),
            by_part(n, width),
            by_part(n, width),
            by_part(width, count),
            by_part(heads, count),
            ANY,
            ANY,
            ANY,
            ANY,
        ],
        out_specs=[
            const((count, model)),
            const((n, model)),
            pl.BlockSpec((1, model, columns), lambda i: (i // 2, 0, 0), pipeline_mode=pl.Buffered(1)),
            by_part(1, width),
            by_part(1, width),
            ANY,
            ANY,
        ],
        out_shape=[
            jax.ShapeDtypeStruct((count, model), F32),
            jax.ShapeDtypeStruct((n, model), BF16),
            jax.ShapeDtypeStruct((2, model, columns), BF16),
            jax.ShapeDtypeStruct((parts, 1, width), F32),
            jax.ShapeDtypeStruct((parts, 1, width), F32),
            jax.ShapeDtypeStruct((m, r, c), BF16),
            jax.ShapeDtypeStruct((m, r, c), BF16),
        ],
        scratch_shapes=[
            pltpu.VMEM((model, count), BF16),
            pltpu.VMEM((model, count), BF16),
            pltpu.VMEM((model, n), BF16),
            pltpu.VMEM((n, model), F32),
            pltpu.VMEM((model, columns), BF16),
            pltpu.VMEM((2, model, columns), BF16),
        ]
        + gather_scratch(m, r, c) * 2
        + link_scratch(10, 12),
        compiler_params=pltpu.CompilerParams(
            vmem_limit_bytes=60 * 2**20, collective_id=4, has_side_effects=True
        ),
        cost_estimate=pl.CostEstimate(
            flops=48 * parts * count * n * width,
            bytes_accessed=16 * parts * n * width,
            transcendentals=parts * count * n * heads,
        ),
        name="cross_backward",
    )(ok, low, x, encoder, weights, queries, keys, values, mixed_t, lse, up_sum, down_sum, from_x, from_y)


def on_device(
    block_in,
    encoder_out,
    out_grad,
    bounds,
    enc_lengths,
    norm_params,
    w_qkv,
    w_self_out,
    w_cross_q,
    w_cross_kv,
    w_cross_out,
    w_up,
    w_down,
    biases,
    up_bias,
):
    member = lax.axis_index("tensor")
    groups_count = lax.axis_size("dp")
    groups = float(groups_count)
    width = w_cross_q.shape[1]
    hidden_width = w_up.shape[1]
    heads = H // 4
    own_rows, model_width = block_in.shape
    enc_rows = encoder_out.shape[0]
    w_rows = w_cross_q.shape[0]

    def block_of(vector, size, distance):
        return lax.dynamic_slice_in_dim(vector, (member ^ distance) * size, size)

    def blocks_placed(parts):
        size = parts[0].shape[0]
        out = jnp.zeros((4 * size,), F32)
        for distance, part in enumerate(parts):
            out = lax.dynamic_update_slice_in_dim(out, part, (member ^ distance) * size, 0)
        return out

    first_in, self_w, cross_column = start_gather(
        layer_norm(block_in.astype(F32), norm_params[0, 0], norm_params[0, 1]).astype(BF16),
        jnp.concatenate([w_qkv.reshape(w_rows, 3 * width), w_self_out.T], axis=1),
        jnp.concatenate([w_cross_q, w_cross_kv.reshape(w_rows, 2 * width), w_cross_out.T], axis=1),
    )
    self_w = self_w.reshape(model_width, 4 * width)

    self_safe = 1024
    queries, key_rows, value_rows, keys_t, self_mixed_t, self_lse, terms, cross_w, ffn_column, enc_all = self_forward(
        bounds,
        first_in,
        self_w,
        block_of(biases[0], width, 0)[None],
        block_of(biases[1], width, 0)[None],
        cross_column,
        jnp.concatenate([w_up, w_down.T], axis=1),
        encoder_out,
        heads,
        self_safe,
    )
    cross_w = cross_w.reshape(4, model_width, 4 * width)
    after_self, second_in, ffn_near = sum_after_self(
        terms, block_in, biases[2:3], norm_params[1], ffn_column
    )

    ok = (jnp.arange(4 * enc_rows, dtype=jnp.int32) < enc_lengths[0]).astype(F32)[:, None]

    def all_blocks(vector, size):
        return jnp.stack([block_of(vector, size, d) for d in range(4)])[:, None]

    cross_q, cross_k, cross_v, cross_mixed_t, cross_lse, after_cross, third_in, ffn_far = cross_forward(
        ok,
        second_in,
        enc_all,
        cross_w,
        all_blocks(biases[3], width),
        all_blocks(biases[4], width),
        after_self,
        biases[5:6],
        norm_params[2],
        ffn_column,
        heads,
    )

    output, cross_rows_grad, cross_low, ffn_sums, up_sum, down_sum, bias_up_parts, from_x, from_y = feed_forward(
        third_in,
        out_grad,
        ffn_near.reshape(2, model_width, 2 * hidden_width),
        ffn_far.reshape(2, model_width, 2 * hidden_width),
        all_blocks(up_bias, hidden_width),
        after_cross,
        biases[6:7],
        norm_params[2],
    )

    by_shard = (2, groups_count // 2, 2, w_rows, hidden_width)
    second_grad, enc_terms, cross_sum, bias_cq_parts, bias_cv_parts, up_column, down_column = cross_backward(
        ok,
        cross_low,
        second_in,
        enc_all,
        cross_w,
        cross_q,
        cross_k,
        cross_v,
        cross_mixed_t,
        cross_lse,
        up_sum.reshape(by_shard),
        down_sum.reshape(by_shard),
        from_x,
        from_y,
        heads,
    )
    cross_sum = cross_sum.reshape(2, groups_count // 2, 2, w_rows, 4 * width)
    self_wide, self_rows_grad, self_sums, summed_down, diagonal = middle(
        second_grad, after_self, cross_rows_grad, norm_params[1], down_column, cross_sum
    )
    bias_cq_grad = blocks_placed([bias_cq_parts[d, 0] for d in range(4)])
    bias_cv_grad = blocks_placed([bias_cv_parts[d, 0] for d in range(4)])
    bias_up_grad = blocks_placed([bias_up_parts[d, 0] for d in range(4)])

    self_dq, self_dk, self_dv, summed_up, summed_cross, encoder_grad = self_backward(
        bounds,
        queries,
        key_rows,
        value_rows,
        keys_t,
        self_wide,
        self_w,
        self_mixed_t,
        self_lse,
        up_column,
        cross_sum,
        diagonal,
        enc_terms,
        heads,
        self_safe,
    )
    grad_so_t = lax.dot_general(
        self_wide, self_mixed_t, (((0,), (1,)), ((), ())), preferred_element_type=F32
    ).astype(BF16)

    def only_own(part):
        out = jnp.zeros((model_width,), F32)
        return lax.dynamic_update_slice_in_dim(out, part, member * width, 0)

    vectors = jnp.concatenate(
        [
            jnp.zeros((2, model_width), F32),
            self_sums[:2],
            ffn_sums[:2],
            jnp.stack(
                [
                    only_own(jnp.sum(self_dq.astype(F32), axis=0)),
                    only_own(jnp.sum(self_dv.astype(F32), axis=0)),
                    self_sums[2],
                    bias_cq_grad,
                    bias_cv_grad,
                    ffn_sums[2],
                    ffn_sums[3],
                ]
            ),
            bias_up_grad.reshape(-1, model_width),
        ]
    )
    vectors = jnp.pad(vectors, ((0, -vectors.shape[0] % 8), (0, 0)))
    input_grad, summed_self, vectors = tail(
        self_dq,
        self_dk,
        self_dv,
        self_w,
        first_in,
        grad_so_t,
        block_in,
        self_rows_grad,
        norm_params[0],
        vectors,
    )
    norm_total = vectors[:6].reshape(norm_params.shape)
    bias_total = vectors[6:13]
    up_total = vectors[13 : 13 + up_bias.shape[0] // model_width].reshape(-1)
    scale = 1.0 / groups
    return (
        output,
        input_grad,
        encoder_grad,
        norm_total * scale,
        summed_self[:, : 3 * width].reshape(w_qkv.shape) * scale,
        summed_self[:, 3 * width :].T * scale,
        summed_cross[:, :width] * scale,
        summed_cross[:, width : 3 * width].reshape(w_cross_kv.shape) * scale,
        summed_cross[:, 3 * width :].T * scale,
        summed_up * scale,
        summed_down.T * scale,
        bias_total * scale,
        up_total * scale,
    )


def solution(mesh):
    rows = P(("dp", "tensor"), None)
    placed = (
        rows,
        rows,
        rows,
        P("dp", None),
        P("dp"),
        P(),
        P("dp", None, "tensor"),
        P("tensor", "dp"),
        P("dp", "tensor"),
        P("dp", None, "tensor"),
        P("tensor", "dp"),
        P("dp", "tensor"),
        P("tensor", "dp"),
        P(),
        P(),
    )
    return jax.shard_map(
        on_device,
        mesh=mesh,
        in_specs=placed,
        out_specs=(
            rows,
            rows,
            rows,
            P(),
            P("dp", None, "tensor"),
            P("tensor", "dp"),
            P("dp", "tensor"),
            P("dp", None, "tensor"),
            P("tensor", "dp"),
            P("dp", "tensor"),
            P("tensor", "dp"),
            P(),
            P(),
        ),
        check_vma=False,
    )
```

```python
import functools
import math

import jax
import jax.numpy as jnp
from jax import lax
from jax.experimental import pallas as pl
from jax.experimental.pallas import tpu as pltpu
from jax.sharding import PartitionSpec as P

H = 16
EPSILON = 1e-05
NEGATIVE = -1e30
F32 = jnp.float32
BF16 = jnp.bfloat16
VMEM_LIMIT = 56 * 2**20


def dot_nt(a, b):
    return lax.dot_general(a, b, (((1,), (1,)), ((), ())), preferred_element_type=F32)


def dot_nn(a, b):
    return lax.dot_general(a, b, (((1,), (0,)), ((), ())), preferred_element_type=F32)


def dot_tn(a, b):
    return lax.dot_general(a, b, (((0,), (0,)), ((), ())), preferred_element_type=F32)


def head_only(x, h, size):
    lane = lax.broadcasted_iota(jnp.int32, x.shape, 1)
    return jnp.where((lane >= h * size) & (lane < (h + 1) * size), x, jnp.zeros_like(x))


def self_bad(b_ref, q_start, k_start, bq, bk, causal):
    qi = q_start + lax.broadcasted_iota(jnp.int32, (1, bq), 1)
    kj = k_start + lax.broadcasted_iota(jnp.int32, (bk, 1), 0)
    bad = (qi >= b_ref[0, 1]) & ((kj >= b_ref[0, 0]) & (kj < b_ref[0, 1]))
    if causal:
        bad = bad | (kj > qi)
    return bad


def over_keys(i, bq, bk, safe, block, between=()):
    diagonal = i * (bq // bk)

    def visit(j, c):
        for at_i, at_j, action in between:
            pl.when((i == at_i) & (j == at_j))(action)

        @pl.when(j < safe // bk)
        def _():
            block(j, "none")

        @pl.when(j >= safe // bk)
        def _():
            block(j, "segment")

        return c

    lax.fori_loop(0, diagonal, visit, 0)
    for step in range(bq // bk):
        block(diagonal + step, "causal")


CORE = ("tensor", 1)
X = ("tensor", 2)
Y = ("dp", 1)
ANY = pl.BlockSpec(memory_space=pl.ANY)


class Links:
    def __init__(self, send_sems, recv_sems, local_sems):
        self.dp = lax.axis_index("dp")
        self.tensor = lax.axis_index("tensor")
        self.send_sems, self.recv_sems, self.local_sems = send_sems, recv_sems, local_sems
        self.used = 0
        self.used_local = 0

    def partner(self, way):
        axis, distance = way
        if axis == "tensor":
            return (self.dp, self.tensor ^ distance)
        return (self.dp ^ distance, self.tensor)

    def greet(self, ways):
        barrier = pltpu.get_barrier_semaphore()
        for way in ways:
            pl.semaphore_signal(
                barrier, inc=1, device_id=self.partner(way), device_id_type=pl.DeviceIdType.MESH
            )
        pl.semaphore_wait(barrier, len(ways))

    def copy(self, source, target, way):
        k = self.used
        self.used += 1
        return pltpu.make_async_remote_copy(
            src_ref=source,
            dst_ref=target,
            send_sem=self.send_sems.at[k],
            recv_sem=self.recv_sems.at[k],
            device_id=self.partner(way),
            device_id_type=pl.DeviceIdType.MESH,
        )

    def local(self, source, target):
        k = self.used_local
        self.used_local += 1
        return pltpu.make_async_copy(source, target, self.local_sems.at[k])


def link_scratch(copies, local):
    return [
        pltpu.SemaphoreType.DMA((copies,)),
        pltpu.SemaphoreType.DMA((copies,)),
        pltpu.SemaphoreType.DMA((local,)),
    ]


def z_distances(n):
    found = []
    m = n // 2
    while m > 1:
        m //= 2
        found.append(m)
    return found


def z_ways(n):
    return [("dp", 2 * distance) for distance in z_distances(n)]


def column_stages(links, shard, column, n):
    z = links.dp // 2
    held = [z]
    stages = []
    for distance in z_distances(n):
        stages.append(
            [
                (
                    links.copy(shard if k == 0 else column.at[index], column.at[index], ("dp", 2 * distance)),
                    index ^ distance,
                )
                for k, index in enumerate(held)
            ]
        )
        held = held + [index ^ distance for index in held]
    return stages


class Spread:
    def __init__(self, links, source, column, whole):
        y = links.dp % 2
        half = column.shape[0] // 2
        low, high = pl.ds(0, half), pl.ds(half, half)
        near, near_core, far, far_core = (whole.at[k] for k in range(4))
        self.load = links.local(source, column)
        self.own = links.local(column, near.at[:, y])
        self.first = [
            links.copy(column, near.at[:, y], Y),
            links.copy(column, far.at[:, y], X),
        ]
        self.core = [links.copy(column, near_core.at[:, y], CORE)]
        self.second = [
            links.copy(near.at[low, 1 - y], far.at[low, 1 - y], X),
            links.copy(far.at[high, y], far.at[high, y], Y),
        ]
        self.core_second = [
            links.copy(near.at[:, 1 - y], near_core.at[:, 1 - y], CORE),
            links.copy(far.at[:, y], far_core.at[:, y], CORE),
        ]
        self.core_third = [links.copy(far.at[:, 1 - y], far_core.at[:, 1 - y], CORE)]

    def start(self):
        self.load.start()
        self.load.wait()
        for copy in self.first + self.core + [self.own]:
            copy.start()

    def middle(self):
        for copy in self.first:
            copy.wait_recv()
        for copy in self.second + self.core_second:
            copy.start()

    def end(self):
        for copy in self.second:
            copy.wait_recv()
        for copy in self.core_third:
            copy.start()
        self.own.wait()
        for copy in self.first + self.second:
            copy.wait_send()
        for copy in self.core + self.core_second + self.core_third:
            copy.wait()


def add_to(total_ref, other_ref):
    def one(k, c):
        total_ref[k] = (total_ref[k].astype(F32) + other_ref[k].astype(F32)).astype(BF16)
        return c

    lax.fori_loop(0, total_ref.shape[0], one, 0)


class Gather:
    def __init__(self, links, near, far, from_x, from_y, buffers):
        y = links.dp % 2
        self.column, self.over_y, self.over_x, self.add_y, self.add_x, self.sum_y, self.sum_x = buffers
        m = self.column.shape[0]
        low, high = pl.ds(0, m // 2), pl.ds(m // 2, m - m // 2)
        self.loads = [
            links.local(near.at[low, 1 - y], self.over_y),
            links.local(far.at[high, y], self.over_x),
            links.local(from_x, self.add_y),
            links.local(from_y, self.add_x),
            links.local(near.at[:, y], self.column),
        ]
        self.first = [
            links.copy(far.at[low, y], self.sum_x.at[low], X),
            links.copy(near.at[high, 1 - y], self.sum_y.at[high], Y),
        ]
        self.second = [
            links.copy(self.over_x, self.sum_x.at[high], X),
            links.copy(self.over_y, self.sum_y.at[low], Y),
        ]

    def start(self):
        for copy in self.first + self.loads:
            copy.start()

    def middle(self):
        for copy in self.loads:
            copy.wait()
        add_to(self.over_x, self.add_x)
        add_to(self.over_y, self.add_y)
        for copy in self.second:
            copy.start()

    def end(self):
        for copy in self.first + self.second:
            copy.wait_recv()
        add_to(self.column, self.sum_y)
        add_to(self.column, self.sum_x)
        for copy in self.first + self.second:
            copy.wait_send()


def gather_scratch(m, r, c):
    whole = pltpu.VMEM((m, r, c), BF16)
    half = pltpu.VMEM((m // 2, r, c), BF16)
    return [whole] + [half] * 4 + [whole] * 2


class GatherLast:
    def __init__(self, links, near, far, diagonal, buffers):
        y = links.dp % 2
        self.column, self.over_x, self.diagonal, self.sum_y, self.sum_x = buffers
        self.loads = [
            links.local(far.at[:, y], self.over_x),
            links.local(diagonal, self.diagonal),
            links.local(near.at[:, y], self.column),
        ]
        self.over_y = links.copy(near.at[:, 1 - y], self.sum_y, Y)
        self.along_x = links.copy(self.over_x, self.sum_x, X)

    def start(self):
        self.over_y.start()
        for copy in self.loads:
            copy.start()

    def middle(self):
        for copy in self.loads:
            copy.wait()
        add_to(self.over_x, self.diagonal)
        self.along_x.start()

    def end(self):
        self.over_y.wait_recv()
        self.along_x.wait_recv()
        add_to(self.column, self.sum_y)
        add_to(self.column, self.sum_x)
        self.over_y.wait_send()
        self.along_x.wait_send()


class Collect:
    def __init__(self, links, column, slots):
        z = links.dp // 2
        self.column, self.slots, self.z = column, slots, z
        m = column.shape[0]
        distances = z_distances(2 * m)[::-1]
        self.stages = []
        first = 0
        for step, distance in enumerate(distances):
            kept = [0]
            for other in distances[step + 1 :]:
                kept = kept + [k ^ other for k in kept]
            self.stages.append(
                [
                    (links.copy(column.at[z ^ distance ^ k], slots.at[first + i], ("dp", 2 * distance)), first + i, z ^ k)
                    for i, k in enumerate(kept)
                ]
            )
            first += len(kept)

    def start(self, step):
        for copy, _, _ in self.stages[step]:
            copy.start()

    def finish(self, step):
        for copy, slot, index in self.stages[step]:
            copy.wait_recv()
            self.column[index] = (self.column[index].astype(F32) + self.slots[slot].astype(F32)).astype(BF16)

    def drain(self):
        for stage in self.stages:
            for copy, _, _ in stage:
                copy.wait_send()


class SpreadFar:
    def __init__(self, links, column, whole):
        y = links.dp % 2
        far, far_core = whole.at[0], whole.at[1]
        m, _, c = column.shape
        step = max(m // 4, 1)
        self.over_x, self.over_y, self.core_x, self.core_y = [], [], [], []
        for k in range(m // step):
            for h in range(2):
                z, part = pl.ds(k * step, step), pl.ds(h * (c // 2), c // 2)
                own = far.at[z, y, :, part]
                other = far.at[z, 1 - y, :, part]
                self.over_x.append(links.copy(column.at[z, :, part], own, X))
                self.over_y.append(links.copy(own, own, Y))
                self.core_x.append(links.copy(own, far_core.at[z, y, :, part], CORE))
                self.core_y.append(links.copy(other, far_core.at[z, 1 - y, :, part], CORE))

    def start(self):
        for copy in self.over_x:
            copy.start()

    def onward(self, k):
        self.over_x[k].wait_recv()
        self.over_y[k].start()
        self.core_x[k].start()

    def last(self, k):
        self.over_y[k].wait_recv()
        self.core_y[k].start()

    def end(self):
        for copy in self.over_x + self.over_y:
            copy.wait_send()
        for copy in self.core_x + self.core_y:
            copy.wait()


class RowSum:
    def __init__(self, links, terms, buffers):
        self.near, self.far, self.got_near, self.got_far, self.got_x = buffers
        count = self.near.shape[0]

        def rows(distance):
            start = pl.multiple_of((links.tensor ^ distance) * count, count)
            return terms.at[pl.ds(start, count)]

        self.loads = [links.local(rows(0), self.near), links.local(rows(2), self.far)]
        self.core = [links.copy(rows(3), self.got_far, CORE), links.copy(rows(1), self.got_near, CORE)]
        self.over_x = links.copy(self.far, self.got_x, X)

    def start(self):
        for copy in self.loads[::-1] + self.core:
            copy.start()

    def middle(self):
        self.loads[1].wait()
        self.core[0].wait_recv()

        def add(rows):
            self.far[rows, :] = (self.far[rows, :].astype(F32) + self.got_far[rows, :].astype(F32)).astype(BF16)

        by_rows(self.far.shape[0], 64, add)
        self.over_x.start()

    def end(self):
        self.loads[0].wait()
        self.core[1].wait_recv()
        self.over_x.wait_recv()
        for copy in self.core + [self.over_x]:
            copy.wait_send()

    def total(self, rows):
        return self.near[rows, :].astype(F32) + self.got_near[rows, :].astype(F32) + self.got_x[rows, :].astype(F32)


def row_sum_scratch(count, width):
    return [pltpu.VMEM((count, width), BF16)] * 5


class Everywhere:
    def __init__(self, links, held, slots, n):
        self.held, self.slots = held, slots
        ways = everywhere_ways(n)
        self.copies = [links.copy(held.at[k], slots.at[k], way) for k, way in enumerate(ways)]

    def start(self, step):
        self.copies[step].start()

    def finish(self, step):
        self.copies[step].wait()
        self.held[step + 1] = self.held[step] + self.slots[step]


def everywhere_ways(n):
    return [CORE, X, Y] + z_ways(n)


def everywhere_scratch(k, c, n):
    steps = len(everywhere_ways(n))
    return [pltpu.VMEM((steps + 1, k, c), F32), pltpu.VMEM((steps, k, c), F32)]


def middle_kernel(
    back_ref, rows_ref, grad_ref, norm_ref, down_ref, cross_ref,
    wide_out, grad_out, sums_ref, down_out, diagonal_out,
    low, column, slots, send_sems, recv_sems, local_sems, *, n
):
    links = Links(send_sems, recv_sems, local_sems)
    count = low.shape[0]
    load = links.local(down_ref, column)
    load.start()
    collect = Collect(links, column, slots)

    def place(distance):
        return wide_out.at[pl.ds(pl.multiple_of((links.tensor ^ distance) * count, count), count)]

    own = links.local(low, place(0))
    half = count // 2
    parts = [pl.ds(0, half), pl.ds(half, half)]
    over_x = [links.copy(low.at[part], place(0).at[part], X) for part in parts]
    over_core = links.copy(low, place(0), CORE)
    onward = [links.copy(place(2).at[part], place(2).at[part], CORE) for part in parts]
    over_y = links.copy(cross_ref.at[1, :, 1 - links.dp % 2], diagonal_out, Y)
    links.greet([CORE, X, Y] + z_ways(n))
    over_y.start()
    load.wait()
    collect.start(0)
    sums_ref[...] = jnp.zeros_like(sums_ref)

    def norm_back(rows):
        incoming = back_ref[rows, :]
        rows_grad, gain_terms = norm_rows_back(rows_ref[rows, :], incoming, norm_ref[1, 0:1, :])
        rows_grad = rows_grad + grad_ref[rows, :]
        rounded = rows_grad.astype(BF16)
        grad_out[rows, :] = rows_grad
        low[rows, :] = rounded
        for k, terms in enumerate((gain_terms, incoming, rounded.astype(F32))):
            sums_ref[k : k + 1, :] += jnp.sum(terms, axis=0, keepdims=True)

    for part, copy in zip(parts, over_x):
        by_rows(half, 64, lambda rows, part=part: norm_back(pl.ds(pl.multiple_of(part.start + rows.start, 64), 64)))
        copy.start()
    own.start()
    over_core.start()
    for step in range(len(collect.stages) - 1):
        collect.finish(step)
        collect.start(step + 1)
    for copy, later in zip(over_x, onward):
        copy.wait_recv()
        later.start()
    collect.finish(len(collect.stages) - 1)
    down_out[...] = column[collect.z].astype(F32)
    collect.drain()
    own.wait()
    for copy in over_x:
        copy.wait_send()
    over_core.wait()
    for copy in onward:
        copy.wait()
    over_y.wait()


def middle(back, rows, grad, norm, down_column, cross_sum):
    n = lax.axis_size("dp")
    count, width = rows.shape
    m, r, c = down_column.shape
    vmem = pl.BlockSpec(memory_space=pltpu.VMEM)
    return pl.pallas_call(
        functools.partial(middle_kernel, n=n),
        in_specs=[vmem, vmem, vmem, vmem, ANY, ANY],
        out_specs=[ANY, vmem, vmem, vmem, ANY],
        out_shape=[
            jax.ShapeDtypeStruct((4 * count, width), BF16),
            jax.ShapeDtypeStruct((count, width), F32),
            jax.ShapeDtypeStruct((8, width), F32),
            jax.ShapeDtypeStruct((r, c), F32),
            jax.ShapeDtypeStruct((m, r, cross_sum.shape[4]), BF16),
        ],
        scratch_shapes=[
            pltpu.VMEM((count, width), BF16),
            pltpu.VMEM((m, r, c), BF16),
            pltpu.VMEM((m, r, c), BF16),
        ]
        + link_scratch(6 + m, 2),
        compiler_params=pltpu.CompilerParams(
            vmem_limit_bytes=VMEM_LIMIT, collective_id=6, has_side_effects=True
        ),
        cost_estimate=pl.CostEstimate(flops=0, bytes_accessed=100 * 2**20, transcendentals=0),
        name="middle",
    )(back, rows, grad, norm, down_column, cross_sum)


def tail_kernel(
    dq_ref, dk_ref, dv_ref, w_ref, first_ref, wide_ref, mt_ref, rows_ref, grad_ref, norm_ref,
    self_ref, ffn_ref, cq_ref, cv_ref, up_ref,
    grad_out, weights_out, late_out, give, acc, weights, *scratch, n, step_rows
):
    links = Links(*scratch[-3:])
    member = links.tensor
    near, far, got_near, got_far, got_x = scratch[:5]
    columns, gots, slots = scratch[5:7], scratch[7:9], scratch[9:11]
    held, late_slots = scratch[11:13]
    count, model = near.shape
    width = dq_ref.shape[1]
    y = links.dp % 2
    c = columns[0].shape[2]
    m, _, r, _ = weights.shape
    half = count // 2
    parts = [pl.ds(0, half), pl.ds(half, half)]
    core_far = links.copy(give.at[0], got_far, CORE)
    core_near = links.copy(give.at[1], got_near, CORE)
    over_x = [links.copy(far.at[part], got_x.at[part], X) for part in parts]
    over_y, collects = [], []
    for k, (column, got, slot) in enumerate(zip(columns, gots, slots)):
        over_y.append(links.copy(weights.at[:, 1 - y, :, pl.ds(k * c, c)], got, Y))
        collects.append(Collect(links, column, slot))
    stages = len(collects[0].stages)
    late = Everywhere(links, held, late_slots, n)
    steps = len(late.copies)
    links.greet(everywhere_ways(n))

    def terms(distance, target):
        base = (member ^ distance) * count

        def one(rows):
            there = pl.ds(pl.multiple_of(base + rows.start, 128), 128)
            total = dot_nt(dq_ref[there, :], w_ref[:, :width])
            total = total + dot_nt(dk_ref[there, :], w_ref[:, width : 2 * width])
            target[rows, :] = (total + dot_nt(dv_ref[there, :], w_ref[:, 2 * width : 3 * width])).astype(BF16)

        by_rows(count, 128, one)

    def packed(k):
        for block in range(2 * m):
            span = slice(block * r, (block + 1) * r)
            weights[block // 2, block % 2, :, k * c : (k + 1) * c] = acc[span, k * c : (k + 1) * c].astype(BF16)
        columns[k][...] = weights[:, y, :, k * c : (k + 1) * c]

    terms(3, give.at[0])
    core_far.start()
    terms(2, far)
    core_far.wait_recv()
    for part, copy in zip(parts, over_x):

        def add(rows, part=part):
            there = pl.ds(pl.multiple_of(part.start + rows.start, 64), 64)
            far[there, :] = (far[there, :].astype(F32) + got_far[there, :].astype(F32)).astype(BF16)

        by_rows(half, 64, add)
        copy.start()

    acc[...] = jnp.zeros_like(acc)

    def products(rows):
        source = first_ref[rows, :].T
        for k, ref in enumerate((dq_ref, dk_ref, dv_ref)):
            acc[:, k * width : (k + 1) * width] += dot_nn(source, ref[rows, :])

    by_rows(dq_ref.shape[0], step_rows, products)
    packed(0)
    over_y[0].start()
    terms(1, give.at[1])
    core_near.start()
    terms(0, near)

    def products_out(rows):
        acc[:, 3 * width :] += dot_nn(wide_ref[rows, :].T, mt_ref[:, rows].T)

    by_rows(dq_ref.shape[0], step_rows, products_out)
    packed(1)

    held[0] = jnp.zeros(held.shape[1:], F32)
    held[0, 2:4, :] = self_ref[0:2, :]
    held[0, 4:6, :] = ffn_ref[0:2, :]
    held[0, 8:9, :] = self_ref[2:3, :]
    held[0, 11:13, :] = ffn_ref[2:4, :]
    for distance in range(4):
        there = pl.ds(pl.multiple_of((member ^ distance) * width, width), width)
        held[0, 9:10, there] = cq_ref[distance]
        held[0, 10:11, there] = cv_ref[distance]
        held[0, pl.ds(13 + (member ^ distance), 1), :] = up_ref[distance]
    here = pl.ds(pl.multiple_of(member * width, width), width)

    def column_sums(rows):
        held[0, 6:7, here] += jnp.sum(dq_ref[rows, :].astype(F32), axis=0, keepdims=True)
        held[0, 7:8, here] += jnp.sum(dv_ref[rows, :].astype(F32), axis=0, keepdims=True)

    by_rows(dq_ref.shape[0], step_rows, column_sums)

    def norm_back(part):
        def one(rows):
            rows = pl.ds(pl.multiple_of(part.start + rows.start, 64), 64)
            incoming = near[rows, :].astype(F32) + got_near[rows, :].astype(F32) + got_x[rows, :].astype(F32)
            rows_grad, gain_terms = norm_rows_back(rows_ref[rows, :].astype(F32), incoming, norm_ref[0, 0:1, :])
            grad_out[rows, :] = rows_grad + grad_ref[rows, :]
            held[0, 0:1, :] += jnp.sum(gain_terms, axis=0, keepdims=True)
            held[0, 1:2, :] += jnp.sum(incoming, axis=0, keepdims=True)

        by_rows(half, 64, one)

    def summed_y(k):
        over_y[k].wait_recv()
        add_to(columns[k], gots[k])
        collects[k].start(0)

    def next_z(k):
        for step in range(stages - 1):
            collects[k].finish(step)
            collects[k].start(step + 1)

    def last_z(k):
        collects[k].finish(stages - 1)
        weights_out[:, k * c : (k + 1) * c] = columns[k][collects[k].z].astype(F32)

    summed_y(0)
    over_y[1].start()
    core_near.wait_recv()
    over_x[0].wait_recv()
    norm_back(parts[0])
    next_z(0)
    over_x[1].wait_recv()
    norm_back(parts[1])
    late.start(0)
    summed_y(1)
    late.finish(0)
    late.start(1)
    last_z(0)
    late.finish(1)
    late.start(2)
    next_z(1)
    late.finish(2)
    for step in range(3, steps):
        late.start(step)
        late.finish(step)
    last_z(1)
    late_out[...] = held[steps]
    for copy in over_x + over_y + [core_near, core_far]:
        copy.wait_send()
    for collect in collects:
        collect.drain()


def tail(dq, dk, dv, w, first, wide, mixed_t, rows, grad, norm, self_sums, ffn_sums, cq_sums, cv_sums, up_sums):
    n = lax.axis_size("dp")
    count, model = rows.shape
    width = dq.shape[1]
    m, r, c = n // 2, model // n, 4 * width
    vectors = (24, model)
    vmem = pl.BlockSpec(memory_space=pltpu.VMEM)
    part = pltpu.VMEM((m, r, c // 2), BF16)
    return pl.pallas_call(
        functools.partial(tail_kernel, n=n, step_rows=512),
        in_specs=[vmem] * 15,
        out_specs=[vmem, vmem, vmem],
        out_shape=[
            jax.ShapeDtypeStruct((count, model), F32),
            jax.ShapeDtypeStruct((r, c), F32),
            jax.ShapeDtypeStruct(vectors, F32),
        ],
        scratch_shapes=[
            pltpu.VMEM((2, count, model), BF16),
            pltpu.VMEM((model, c), F32),
            pltpu.VMEM((m, 2, r, c), BF16),
        ]
        + row_sum_scratch(count, model)
        + [part] * 6
        + everywhere_scratch(*vectors, n)
        + link_scratch(6 + 2 * m + len(everywhere_ways(n)), 1),
        compiler_params=pltpu.CompilerParams(
            vmem_limit_bytes=VMEM_LIMIT, collective_id=7, has_side_effects=True
        ),
        cost_estimate=pl.CostEstimate(flops=0, bytes_accessed=100 * 2**20, transcendentals=0),
        name="tail",
    )(dq, dk, dv, w, first, wide, mixed_t, rows, grad, norm, self_sums, ffn_sums, cq_sums, cv_sums, up_sums)


def results_kernel(
    output_ref, grad_ref, enc_ref, self_ref, cross_ref, up_ref, down_ref,
    output_out, grad_out, enc_out, qkv_out, so_out, cq_out, ckv_out, co_out, up_out, down_out, *, scale
):
    output_out[...] = output_ref[...]
    grad_out[...] = grad_ref[...]
    enc_out[...] = enc_ref[...]
    width = cq_out.shape[1]

    @pl.when(pl.program_id(0) == 0)
    def _():
        for k in range(3):
            qkv_out[:, k, :] = self_ref[:, k * width : (k + 1) * width] * scale
        so_out[...] = self_ref[:, 3 * width :] * scale
        cq_out[...] = cross_ref[:, :width] * scale
        for k in range(2):
            ckv_out[:, k, :] = cross_ref[:, (k + 1) * width : (k + 2) * width] * scale
        co_out[...] = cross_ref[:, 3 * width :] * scale
        up_out[...] = up_ref[...] * scale
        down_out[...] = down_ref[...] * scale


def results(output, grad, encoder, self_w, cross_w, up, down, scale):
    r, c = self_w.shape
    width = c // 4
    steps = 4

    def rows(value):
        return pl.BlockSpec((value.shape[0] // steps, value.shape[1]), lambda i: (i, 0))

    shapes = [(r, 3, width), (r, width), (r, width), (r, 2, width), (r, width), up.shape, down.shape]
    return pl.pallas_call(
        functools.partial(results_kernel, scale=scale),
        grid=(steps,),
        in_specs=[rows(output), rows(grad), rows(encoder)] + [const(v.shape) for v in (self_w, cross_w, up, down)],
        out_specs=[rows(output), rows(grad), rows(encoder)] + [const(shape) for shape in shapes],
        out_shape=[jax.ShapeDtypeStruct(v.shape, F32) for v in (output, grad, encoder)]
        + [jax.ShapeDtypeStruct(shape, F32) for shape in shapes],
        compiler_params=pltpu.CompilerParams(vmem_limit_bytes=VMEM_LIMIT),
        cost_estimate=pl.CostEstimate(flops=0, bytes_accessed=20 * 2**20, transcendentals=0),
        name="results",
    )(output, grad, encoder, self_w, cross_w, up, down)


def start_kernel(
    in_ref, norm_ref, self_ref, cross_ref, rows_out, self_out, cross_out, rows_ref, send_sems, recv_sems, local_sems, *, n
):
    links = Links(send_sems, recv_sems, local_sems)
    member, z, y = links.tensor, links.dp // 2, links.dp % 2
    count = rows_ref.shape[0]
    half = count // 2
    parts = [pl.ds(0, half), pl.ds(half, half)]

    def place(distance):
        return rows_out.at[pl.ds(pl.multiple_of((member ^ distance) * count, count), count)]

    over_x = [links.copy(rows_ref.at[part], place(0).at[part], X) for part in parts]
    over_core = [links.copy(rows_ref, place(0), CORE)]
    over_core += [links.copy(place(2).at[part], place(2).at[part], CORE) for part in parts]
    self_stages = column_stages(links, self_ref, self_out.at[:, y], n)
    cross_stages = column_stages(links, cross_ref, cross_out, n)
    over_y = [links.copy(self_ref, self_out.at[z, y], Y)]
    local = [
        links.local(rows_ref, place(0)),
        links.local(self_ref, self_out.at[z, y]),
        links.local(cross_ref, cross_out.at[z]),
    ]
    links.greet([CORE, X, Y] + z_ways(n))
    for copy in over_y + local[1:]:
        copy.start()
    for copy, _ in self_stages[0]:
        copy.start()
    for part, copy in zip(parts, over_x):

        def norm(rows, part=part):
            rows = pl.ds(pl.multiple_of(part.start + rows.start, 64), 64)
            xhat, _ = normalized(in_ref[rows, :].astype(F32))
            rows_ref[rows, :] = (xhat * norm_ref[0, 0:1, :] + norm_ref[0, 1:2, :]).astype(BF16)

        by_rows(half, 64, norm)
        copy.start()
    for copy in local[:1] + over_core[:1]:
        copy.start()
    for self_stage in self_stages:
        if self_stage is not self_stages[0]:
            for copy, _ in self_stage:
                copy.start()
        for copy, index in self_stage:
            copy.wait_recv()
            onward = links.copy(self_out.at[index, y], self_out.at[index, y], Y)
            onward.start()
            over_y.append(onward)
        if self_stage is self_stages[0]:
            for copy, _ in cross_stages[0]:
                copy.start()
    for cross_stage, later in zip(cross_stages, cross_stages[1:] + [[]]):
        for copy, _ in cross_stage:
            copy.wait_recv()
        for copy, _ in later:
            copy.start()
    for copy, onward in zip(over_x, over_core[1:]):
        copy.wait_recv()
        onward.start()
    for copy in local + over_y + over_core:
        copy.wait()
    for copy in over_x:
        copy.wait_send()
    for stage in self_stages + cross_stages:
        for copy, _ in stage:
            copy.wait_send()


def start_gather(rows, norm, self_shard, cross_shard):
    n = lax.axis_size("dp")
    r, c = self_shard.shape
    return pl.pallas_call(
        functools.partial(start_kernel, n=n),
        in_specs=[pl.BlockSpec(memory_space=pltpu.VMEM)] * 4,
        out_specs=[ANY] * 3,
        out_shape=[
            jax.ShapeDtypeStruct((4 * rows.shape[0], rows.shape[1]), BF16),
            jax.ShapeDtypeStruct((n // 2, 2, r, c), BF16),
            jax.ShapeDtypeStruct((n // 2,) + cross_shard.shape, BF16),
        ],
        scratch_shapes=[pltpu.VMEM(rows.shape, BF16)] + link_scratch(2 * n + 8, 3),
        compiler_params=pltpu.CompilerParams(
            vmem_limit_bytes=VMEM_LIMIT, collective_id=0, has_side_effects=True
        ),
        cost_estimate=pl.CostEstimate(flops=0, bytes_accessed=100 * 2**20, transcendentals=0),
        name="start_gather",
    )(rows, norm, self_shard, cross_shard)


def self_forward_kernel(
    b_ref, x_ref, w_ref, biases_ref, column_ref, shard_ref, enc_ref,
    q_out, k_ref, v_out, kt_out, ot_ref, lse_ref, terms_ref, whole, next_column, enc_out,
    vt_ref, m_s, l_s, acc, column, send_sems, recv_sems, local_sems, *, bk, heads, safe, n
):
    i = pl.program_id(0)
    last = pl.num_programs(0) - 1
    bq, width = q_out.shape
    links = Links(send_sems, recv_sems, local_sems)
    spread = Spread(links, column_ref, column, whole)
    stages = column_stages(links, shard_ref, next_column, n)
    enc_count = enc_ref.shape[0]

    def place(distance):
        return enc_out.at[pl.ds(pl.multiple_of((links.tensor ^ distance) * enc_count, enc_count), enc_count)]

    enc_x = links.copy(enc_ref, place(0), X)
    enc_core = [links.copy(enc_ref, place(0), CORE), links.copy(place(2), place(2), CORE)]
    local = [links.local(shard_ref, next_column.at[links.dp // 2]), links.local(enc_ref, place(0))]

    @pl.when(i == 0)
    def _():
        links.greet([CORE, X, Y] + z_ways(n))
        spread.start()
        for copy in local + enc_core[:1]:
            copy.start()
        for copy, _ in stages[0]:
            copy.start()

    def onward():
        spread.middle()
        enc_x.start()
        for k in range(1, len(stages)):
            for copy, _ in stages[k - 1]:
                copy.wait_recv()
            for copy, _ in stages[k]:
                copy.start()

    mine = pl.ds(pl.multiple_of(links.tensor * width, width), width)
    projected = dot_nn(x_ref[...], w_ref[:, : 3 * width])
    query = (projected[:, :width] + biases_ref[0:1, mine]).astype(BF16)
    key = projected[:, width : 2 * width].astype(BF16)
    value = (projected[:, 2 * width :] + biases_ref[1:2, mine]).astype(BF16)
    here = pl.ds(pl.multiple_of(i * bq, bq), bq)
    q_out[...] = query
    v_out[...] = value
    kt_out[...] = key.T
    k_ref[here, :] = key
    vt_ref[:, here] = value.T

    m_s[...] = jnp.full_like(m_s, NEGATIVE)
    l_s[...] = jnp.zeros_like(l_s)
    acc[...] = jnp.zeros_like(acc)
    hd = width // heads
    scaled = query * jnp.asarray(1.0 / math.sqrt(hd), BF16)
    q_heads = [head_only(scaled, h, hd) for h in range(heads)]

    def block(j, mode):
        rows = pl.ds(pl.multiple_of(j * bk, bk), bk)
        keys = k_ref[rows, :]
        m_old = m_s[...]
        l_old = l_s[...]
        scores = [dot_nt(keys, q_heads[h]) for h in range(heads)]
        if mode != "none":
            bad = self_bad(b_ref, i * bq, j * bk, bq, bk, mode == "causal")
            scores = [jnp.where(bad, NEGATIVE, s) for s in scores]
        m_out, l_out, a_out = [], [], []
        for h in range(heads):
            part = slice(h * hd, (h + 1) * hd)
            m_new = jnp.maximum(m_old[h : h + 1, :], jnp.max(scores[h], axis=0, keepdims=True))
            shrink = jnp.exp(m_old[h : h + 1, :] - m_new)
            expos = jnp.exp(scores[h] - m_new)
            l_out.append(l_old[h : h + 1, :] * shrink + jnp.sum(expos, axis=0, keepdims=True))
            m_out.append(m_new)
            a_out.append(acc[part, :] * shrink + dot_nn(vt_ref[part, rows], expos.astype(BF16)))
        m_s[...] = jnp.concatenate(m_out, 0)
        l_s[...] = jnp.concatenate(l_out, 0)
        for h in range(heads):
            acc[h * hd : (h + 1) * hd, :] = a_out[h]

    over_keys(i, bq, bk, safe, block, [(3, 2, onward)])
    inverse = 1.0 / l_s[...]
    for h in range(heads):
        part = slice(h * hd, (h + 1) * hd)
        ot_ref[part, :] = (acc[part, :] * inverse[h : h + 1, :]).astype(BF16)
    lse_ref[...] = m_s[...] + jnp.log(l_s[...])
    terms_ref[...] = dot_nt(ot_ref[...].T, w_ref[:, 3 * width :]).astype(BF16)

    @pl.when(i == last)
    def _():
        spread.end()
        enc_x.wait_recv()
        enc_core[1].start()
        for k, stage in enumerate(stages):
            for copy, _ in stage:
                copy.wait_send()
                if k == len(stages) - 1:
                    copy.wait_recv()
        enc_x.wait_send()
        for copy in local + enc_core:
            copy.wait()


def self_forward(bounds, x, w, biases, column, shard, encoder, heads, safe):
    n, model = x.shape
    width = w.shape[1] // 4
    bq = bk = 512
    dp = lax.axis_size("dp")
    m, r, c = column.shape
    enc_count = encoder.shape[0]
    by_rows_spec = pl.BlockSpec((bq, width), lambda i: (i, 0))
    by_columns_spec = pl.BlockSpec((width, bq), lambda i: (0, i))
    return pl.pallas_call(
        functools.partial(self_forward_kernel, bk=bk, heads=heads, safe=safe, n=dp),
        grid=(n // bq,),
        in_specs=[
            pl.BlockSpec(memory_space=pltpu.SMEM),
            pl.BlockSpec((bq, model), lambda i: (i, 0)),
            const((model, 4 * width)),
            const(biases.shape),
            ANY,
            const(shard.shape),
            const(encoder.shape),
        ],
        out_specs=[
            by_rows_spec,
            const((n, width)),
            by_rows_spec,
            by_columns_spec,
            by_columns_spec,
            pl.BlockSpec((heads, bq), lambda i: (0, i)),
            pl.BlockSpec((bq, model), lambda i: (i, 0)),
            ANY,
            ANY,
            ANY,
        ],
        out_shape=[
            jax.ShapeDtypeStruct((n, width), BF16),
            jax.ShapeDtypeStruct((n, width), BF16),
            jax.ShapeDtypeStruct((n, width), BF16),
            jax.ShapeDtypeStruct((width, n), BF16),
            jax.ShapeDtypeStruct((width, n), BF16),
            jax.ShapeDtypeStruct((heads, n), F32),
            jax.ShapeDtypeStruct((n, model), BF16),
            jax.ShapeDtypeStruct((4, m, 2, r, c), BF16),
            jax.ShapeDtypeStruct((m,) + shard.shape, BF16),
            jax.ShapeDtypeStruct((4 * enc_count, model), BF16),
        ],
        scratch_shapes=[
            pltpu.VMEM((width, n), BF16),
            pltpu.VMEM((heads, bq), F32),
            pltpu.VMEM((heads, bq), F32),
            pltpu.VMEM((width, bq), F32),
            pltpu.VMEM((m, r, c), BF16),
        ]
        + link_scratch(11 + m, 4),
        compiler_params=pltpu.CompilerParams(
            vmem_limit_bytes=VMEM_LIMIT, collective_id=1, has_side_effects=True
        ),
        cost_estimate=pl.CostEstimate(
            flops=12 * n * n * width, bytes_accessed=8 * n * width, transcendentals=n * n * heads // 2
        ),
        name="self_forward",
    )(bounds, x, w, biases, column, shard, encoder)


def after_self_kernel(
    terms_ref, rows_ref, biases_ref, norm_ref, column_ref,
    after_out, second_out, whole_out, *scratch
):
    links = Links(*scratch[-3:])
    rows_sum = RowSum(links, terms_ref, scratch[:5])
    column = scratch[5]
    y = links.dp % 2
    near_out, core_out = whole_out.at[0], whole_out.at[1]
    load = links.local(column_ref, column)
    own = links.local(column, near_out.at[:, y])
    over_y = links.copy(column, near_out.at[:, y], Y)
    over_core = [
        links.copy(column, core_out.at[:, y], CORE),
        links.copy(near_out.at[:, 1 - y], core_out.at[:, 1 - y], CORE),
    ]
    links.greet([CORE, X, Y])
    rows_sum.start()
    load.start()
    load.wait()
    over_y.start()
    own.start()
    rows_sum.middle()
    over_core[0].start()
    rows_sum.end()

    def norm(rows):
        after = rows_ref[rows, :].astype(F32) + rows_sum.total(rows) + biases_ref[2:3, :]
        after_out[rows, :] = after
        xhat, _ = normalized(after)
        second_out[rows, :] = (xhat * norm_ref[1, 0:1, :] + norm_ref[1, 1:2, :]).astype(BF16)

    by_rows(after_out.shape[0], 64, norm)
    over_y.wait_recv()
    over_core[1].start()
    over_y.wait_send()
    own.wait()
    for copy in over_core:
        copy.wait()


def sum_after_self(terms, rows, biases, norm, column):
    count, model = rows.shape
    m, r, c = column.shape
    vmem = pl.BlockSpec(memory_space=pltpu.VMEM)
    return pl.pallas_call(
        after_self_kernel,
        in_specs=[ANY, vmem, vmem, vmem, ANY],
        out_specs=[vmem, vmem, ANY],
        out_shape=[
            jax.ShapeDtypeStruct((count, model), F32),
            jax.ShapeDtypeStruct((count, model), BF16),
            jax.ShapeDtypeStruct((2, m, 2, r, c), BF16),
        ],
        scratch_shapes=row_sum_scratch(count, model) + [pltpu.VMEM((m, r, c), BF16)] + link_scratch(6, 4),
        compiler_params=pltpu.CompilerParams(
            vmem_limit_bytes=VMEM_LIMIT, collective_id=8, has_side_effects=True
        ),
        cost_estimate=pl.CostEstimate(flops=0, bytes_accessed=100 * 2**20, transcendentals=0),
        name="sum_after_self",
    )(terms, rows, biases, norm, column)


def self_backward_kernel(
    b_ref, q_ref, k_ref, v_ref, kt_ref, wide_ref, w_ref, mt_ref, lse_ref,
    up_ref, cross_ref, diagonal_ref, enc_ref,
    dq_ref, dk_ref, dv_ref, up_out, cross_out, enc_out, dka, dva, dqa, *scratch, bk, heads, safe, n
):
    i = pl.program_id(0)
    links = Links(*scratch[-3:])
    cross = GatherLast(links, cross_ref.at[0], cross_ref.at[1], diagonal_ref, scratch[:5])
    cross_z = Collect(links, cross.column, scratch[5])
    up_column = scratch[6]
    up_z = Collect(links, up_column, scratch[7])
    load = links.local(up_ref, up_column)
    enc = RowSum(links, enc_ref, scratch[8:13])
    stages = len(up_z.stages)

    @pl.when(i == 0)
    def _():
        links.greet(everywhere_ways(n))
        cross.start()
        enc.start()
        load.start()
        load.wait()
        up_z.start(0)
        dka[...] = jnp.zeros_like(dka)
        dva[...] = jnp.zeros_like(dva)

    @pl.when(i == 1)
    def _():
        cross.middle()

    @pl.when(i == 2)
    def _():
        for step in range(stages - 1):
            up_z.finish(step)
            up_z.start(step + 1)

    def sum_cross():
        cross.end()
        cross_z.start(0)
        enc.middle()

    def next_cross():
        for step in range(stages - 1):
            cross_z.finish(step)
            cross_z.start(step + 1)

    bq, width = q_ref.shape
    hd = width // heads
    scale = 1.0 / math.sqrt(hd)
    grads = dot_nn(wide_ref[...], w_ref[:, 3 * width :]).astype(BF16)
    products = grads.T.astype(F32) * mt_ref[...].astype(F32)
    inner = [jnp.sum(products[h * hd : (h + 1) * hd, :], axis=0, keepdims=True) for h in range(heads)]
    scaled = q_ref[...] * jnp.asarray(scale, BF16)
    q_heads = [head_only(scaled, h, hd) for h in range(heads)]
    d_heads = [head_only(grads, h, hd) for h in range(heads)]
    lse = lse_ref[...]
    dqa[...] = jnp.zeros_like(dqa)

    def block(j, mode):
        rows = pl.ds(pl.multiple_of(j * bk, bk), bk)
        keys = k_ref[rows, :]
        values = v_ref[rows, :]
        scores = [dot_nt(keys, q_heads[h]) for h in range(heads)]
        dprobs = [dot_nt(values, d_heads[h]) for h in range(heads)]
        if mode != "none":
            bad = self_bad(b_ref, i * bq, j * bk, bq, bk, mode == "causal")
            scores = [jnp.where(bad, NEGATIVE, s) for s in scores]
        dv_sum, dk_sum = None, None
        for h in range(heads):
            part = slice(h * hd, (h + 1) * hd)
            probs = jnp.exp(scores[h] - lse[h : h + 1, :])
            ds = (probs * (dprobs[h] - inner[h])).astype(BF16)
            dv_h = dot_nn(probs.astype(BF16), d_heads[h])
            dk_h = dot_nn(ds, q_heads[h])
            dv_sum = dv_h if dv_sum is None else dv_sum + dv_h
            dk_sum = dk_h if dk_sum is None else dk_sum + dk_h
            dqa[part, :] += dot_nn(kt_ref[part, rows], ds)
        dva[rows, :] += dv_sum
        dka[rows, :] += dk_sum

    over_keys(i, bq, bk, safe, block, [(3, 2, sum_cross), (4, 2, next_cross)])
    dq_ref[...] = (dqa[...] * scale).astype(BF16).T

    @pl.when(i == pl.num_programs(0) - 1)
    def _():
        dk_ref[...] = dka[...].astype(BF16)
        dv_ref[...] = dva[...].astype(BF16)
        up_z.finish(stages - 1)
        up_out[...] = up_column[up_z.z].astype(F32)
        cross_z.finish(stages - 1)
        cross_out[...] = cross.column[cross_z.z].astype(F32)
        enc.end()

        def store(rows):
            enc_out[rows, :] = enc.total(rows)

        by_rows(enc_out.shape[0], 64, store)
        up_z.drain()
        cross_z.drain()


def self_backward(
    bounds, queries, keys, values, keys_t, wide, w, mixed_t, lse,
    up_column, cross_sum, diagonal, enc_terms, heads, safe
):
    n, width = queries.shape
    model = wide.shape[1]
    dp = lax.axis_size("dp")
    m, r, c = up_column.shape
    cross_c = cross_sum.shape[4]
    enc_shape = (enc_terms.shape[0] // 4, enc_terms.shape[1])
    bq = bk = 512
    some = pl.BlockSpec((bq, width), lambda i: (i, 0))
    return pl.pallas_call(
        functools.partial(self_backward_kernel, bk=bk, heads=heads, safe=safe, n=dp),
        grid=(n // bq,),
        in_specs=[
            pl.BlockSpec(memory_space=pltpu.SMEM),
            some,
            const((n, width)),
            const((n, width)),
            const((width, n)),
            pl.BlockSpec((bq, model), lambda i: (i, 0)),
            const((model, 4 * width)),
            pl.BlockSpec((width, bq), lambda i: (0, i)),
            pl.BlockSpec((heads, bq), lambda i: (0, i)),
        ]
        + [ANY] * 4,
        out_specs=[some, const((n, width)), const((n, width))]
        + [const((r, c)), const((r, cross_c)), const(enc_shape)],
        out_shape=[
            jax.ShapeDtypeStruct((n, width), BF16),
            jax.ShapeDtypeStruct((n, width), BF16),
            jax.ShapeDtypeStruct((n, width), BF16),
            jax.ShapeDtypeStruct((r, c), F32),
            jax.ShapeDtypeStruct((r, cross_c), F32),
            jax.ShapeDtypeStruct(enc_shape, F32),
        ],
        scratch_shapes=[
            pltpu.VMEM((n, width), F32),
            pltpu.VMEM((n, width), F32),
            pltpu.VMEM((width, bq), F32),
        ]
        + [pltpu.VMEM((m, r, cross_c), BF16)] * 6
        + [pltpu.VMEM((m, r, c), BF16)] * 2
        + row_sum_scratch(*enc_shape)
        + link_scratch(5 + 2 * m, 6),
        compiler_params=pltpu.CompilerParams(
            vmem_limit_bytes=VMEM_LIMIT, collective_id=5, has_side_effects=True
        ),
        cost_estimate=pl.CostEstimate(
            flops=24 * n * n * width, bytes_accessed=16 * n * width, transcendentals=n * n * heads // 2
        ),
        name="self_backward",
    )(bounds, queries, keys, values, keys_t, wide, w, mixed_t, lse, up_column, cross_sum, diagonal, enc_terms)


def const(shape):
    return pl.BlockSpec(shape, lambda *_: (0,) * len(shape), pipeline_mode=pl.Buffered(1))


def normalized(rows):
    center = rows - jnp.mean(rows, axis=-1, keepdims=True)
    scale = lax.rsqrt(jnp.mean(center * center, axis=-1, keepdims=True) + EPSILON)
    return center * scale, scale


def norm_rows_back(rows, incoming, gain):
    xhat, scale = normalized(rows)
    e = incoming * gain
    inner = jnp.mean(e * xhat, axis=-1, keepdims=True)
    return scale * (e - jnp.mean(e, axis=-1, keepdims=True) - xhat * inner), incoming * xhat


def by_rows(count, step, body):
    def one(k, c):
        body(pl.ds(pl.multiple_of(k * step, step), step))
        return c

    lax.fori_loop(0, count // step, one, 0)


def cross_forward_kernel(
    len_ref, x_ref, enc_ref, w_ref, biases_ref, rows_ref, norm_ref, column_ref,
    q_out, k_out, v_out, ot_ref, lse_ref, after_ref, third_ref, whole, send_sems, recv_sems, local_sems, *, heads
):
    i = pl.program_id(0)
    last = pl.num_programs(0) - 1
    links = Links(send_sems, recv_sems, local_sems)
    spread = SpreadFar(links, column_ref, whole)
    pieces = len(spread.over_x)

    @pl.when(i == 0)
    def _():
        links.greet([CORE, X, Y])
        spread.start()
        after_ref[...] = rows_ref[...] + biases_ref[5:6, :]

    for step, ready in ((1, (0,)), (2, (1, 2)), (3, (3,))):

        @pl.when(i == step)
        def _():
            for k in ready:
                spread.onward(k)

    width = q_out.shape[2]
    hd = width // heads
    mine = pl.ds(pl.multiple_of((links.tensor ^ i) * width, width), width)
    query = (dot_nn(x_ref[...], w_ref[0, :, :width]) + biases_ref[3:4, mine]).astype(BF16)
    key_value = dot_nn(enc_ref[...], w_ref[0, :, width : 3 * width])
    keys = key_value[:, :width].astype(BF16)
    values = (key_value[:, width:] + biases_ref[4:5, mine]).astype(BF16)
    q_out[0] = query
    k_out[0] = keys
    v_out[0] = values
    values_t = values.T
    scaled = query * jnp.asarray(1.0 / math.sqrt(hd), BF16)
    ok = lax.broadcasted_iota(jnp.int32, (keys.shape[0], 1), 0) < len_ref[0]
    scores = [dot_nt(keys, head_only(scaled, h, hd)) for h in range(heads)]
    mixed = []
    for h in range(heads):
        part = slice(h * hd, (h + 1) * hd)
        s = jnp.where(ok, scores[h], NEGATIVE)
        largest = jnp.max(s, axis=0, keepdims=True)
        expos = jnp.exp(s - largest)
        total = jnp.sum(expos, axis=0, keepdims=True)
        mixed.append((dot_nn(values_t[part, :], expos.astype(BF16)) * (1.0 / total)).astype(BF16))
        ot_ref[0, part, :] = mixed[h]
        lse_ref[0, h : h + 1, :] = largest + jnp.log(total)
    after_ref[...] += dot_nt(jnp.concatenate(mixed, 0).T, w_ref[0, :, 3 * width :])

    @pl.when(i == last)
    def _():
        def norm(rows):
            xhat, _ = normalized(after_ref[rows, :])
            third_ref[rows, :] = (xhat * norm_ref[2, 0:1, :] + norm_ref[2, 1:2, :]).astype(BF16)

        by_rows(after_ref.shape[0], 128, norm)
        for k in range(4, pieces):
            spread.onward(k)
        for k in range(pieces):
            spread.last(k)
        spread.end()


def cross_forward(lengths, x, encoder, weights, biases, rows, norm, column, heads):
    count, model = x.shape
    n = encoder.shape[0]
    parts, _, columns = weights.shape
    width = columns // 4
    m, r, c = column.shape

    def by_part(*shape):
        return pl.BlockSpec((1,) + shape, lambda i: (i,) + (0,) * len(shape))

    return pl.pallas_call(
        functools.partial(cross_forward_kernel, heads=heads),
        grid=(parts,),
        in_specs=[
            pl.BlockSpec(memory_space=pltpu.SMEM),
            const((count, model)),
            const((n, model)),
            by_part(model, columns),
            const(biases.shape),
            const((count, model)),
            const(norm.shape),
            ANY,
        ],
        out_specs=[
            by_part(count, width),
            by_part(n, width),
            by_part(n, width),
            by_part(width, count),
            by_part(heads, count),
            const((count, model)),
            const((count, model)),
            ANY,
        ],
        out_shape=[
            jax.ShapeDtypeStruct((parts, count, width), BF16),
            jax.ShapeDtypeStruct((parts, n, width), BF16),
            jax.ShapeDtypeStruct((parts, n, width), BF16),
            jax.ShapeDtypeStruct((parts, width, count), BF16),
            jax.ShapeDtypeStruct((parts, heads, count), F32),
            jax.ShapeDtypeStruct((count, model), F32),
            jax.ShapeDtypeStruct((count, model), BF16),
            jax.ShapeDtypeStruct((2, m, 2, r, c), BF16),
        ],
        scratch_shapes=link_scratch(32, 1),
        compiler_params=pltpu.CompilerParams(
            vmem_limit_bytes=VMEM_LIMIT, collective_id=2, has_side_effects=True
        ),
        cost_estimate=pl.CostEstimate(
            flops=24 * parts * count * n * width,
            bytes_accessed=8 * parts * n * width,
            transcendentals=parts * count * n * heads,
        ),
        name="cross_forward",
    )(lengths, x, encoder, weights, biases, rows, norm, column)


def feed_forward_kernel(
    x_ref, dy_ref, near_ref, far_ref, b_ref, after_ref, biases_ref, norm_ref,
    out_ref, rows_out, low_out, sums_ref, gup_ref, gdown_ref, bias_ref, from_x, from_y,
    xt_ref, dyt_ref, back_ref, give, got, diagonal, loaded, load_sems, send_sems, recv_sems, local_sems, *, chunks
):
    s = pl.program_id(0)
    links = Links(send_sems, recv_sems, local_sems)
    turn = s // chunks
    chunk = s % chunks
    pair = turn // 2
    slot = pair * chunks + chunk
    theirs = turn % 2 == 0
    y = links.dp % 2
    m, r = diagonal.shape[1], diagonal.shape[2]
    low, high = pl.ds(0, m // 2), pl.ds(m // 2, m - m // 2)
    links.used = 2 * chunks
    across = [
        links.copy(diagonal.at[:, low], from_x, X),
        links.copy(diagonal.at[:, high], from_y, Y),
    ]
    to_core = pltpu.make_async_remote_copy(
        src_ref=give.at[chunk],
        dst_ref=got.at[slot],
        send_sem=send_sems.at[slot],
        recv_sem=recv_sems.at[slot],
        device_id=links.partner(CORE),
        device_id_type=pl.DeviceIdType.MESH,
    )

    size = loaded.shape[3]

    def fetch(step, act):
        block = 3 - step // chunks
        slot = step % 2
        first = (step % chunks) * size

        def both(source):
            for k in range(2):
                columns = pl.ds(pl.multiple_of(first + k * chunks * size, size), size)
                act(pltpu.make_async_copy(source.at[:, columns], loaded.at[slot, k], load_sems.at[slot, k]))

        @pl.when(block >= 2)
        def _():
            both(far_ref.at[block - 2])

        @pl.when(block < 2)
        def _():
            both(near_ref.at[block])

    @pl.when(s == 0)
    def _():
        fetch(0, lambda copy: copy.start())
        links.greet([CORE, X, Y])
        out_ref[...] = after_ref[...] + biases_ref[6:7, :]
        back_ref[...] = jnp.zeros_like(back_ref)
        xt_ref[...] = x_ref[...].T
        dyt_ref[...] = dy_ref[...].T
        sums_ref[...] = jnp.zeros_like(sums_ref)

    fetch(s, lambda copy: copy.wait())

    @pl.when(s + 1 < pl.num_programs(0))
    def _():
        fetch(s + 1, lambda copy: copy.start())

    up_ref, down_ref = loaded.at[s % 2, 0], loaded.at[s % 2, 1]
    shift = b_ref[pl.ds(links.tensor ^ (3 - turn), 1), pl.ds(pl.multiple_of(chunk * size, size), size)]
    pre_act = dot_nn(x_ref[...], up_ref[...]) + shift
    hidden_grad = dot_nn(dy_ref[...], down_ref[...])
    normal_cdf = 0.5 * (1.0 + lax.erf(pre_act * (1.0 / math.sqrt(2.0))))
    density = jnp.exp(-0.5 * pre_act * pre_act) * (1.0 / math.sqrt(2.0 * math.pi))
    hidden = (pre_act * normal_cdf).astype(BF16)
    pre_grad = (hidden_grad * (normal_cdf + pre_act * density)).astype(BF16)
    bias_ref[0] = jnp.sum(pre_grad.astype(F32), axis=0, keepdims=True)

    @pl.when(turn % 2 == 1)
    def _():
        to_core.wait_send()

    give[chunk, 0] = dot_nn(xt_ref[...], pre_grad).astype(BF16)
    give[chunk, 1] = dot_nn(dyt_ref[...], hidden).astype(BF16)
    out_ref[...] += dot_nt(hidden, down_ref[...])
    back_ref[...] += dot_nt(pre_grad, up_ref[...])

    @pl.when(theirs)
    def _():
        to_core.start()

    @pl.when(jnp.logical_not(theirs))
    def _():
        to_core.wait_recv()
        gup_ref[0] = (give[chunk, 0].astype(F32) + got[slot, 0].astype(F32)).astype(BF16)
        gdown_ref[0] = (give[chunk, 1].astype(F32) + got[slot, 1].astype(F32)).astype(BF16)

    for k in range(chunks):

        @pl.when(s == chunks + k)
        def _():
            def keep(z, carry):
                rows = pl.ds(pl.multiple_of((2 * z + 1 - y) * r, r), r)
                size = gup_ref.shape[2]
                diagonal[0, z, :, k * size : (k + 1) * size] = gup_ref[0, rows, :]
                diagonal[1, z, :, k * size : (k + 1) * size] = gdown_ref[0, rows, :]
                return carry

            lax.fori_loop(0, m, keep, 0)
            if k == chunks - 1:
                for copy in across:
                    copy.start()

    @pl.when(s == pl.num_programs(0) - 1)
    def _():
        def norm_back(rows):
            third = back_ref[rows, :]
            upstream = dy_ref[rows, :].astype(F32)
            rows_grad, gain_terms = norm_rows_back(after_ref[rows, :], third, norm_ref[2, 0:1, :])
            rows_grad = rows_grad + upstream
            low = rows_grad.astype(BF16)
            rows_out[rows, :] = rows_grad
            low_out[rows, :] = low
            for k, terms in enumerate((gain_terms, third, low.astype(F32), upstream)):
                sums_ref[k : k + 1, :] += jnp.sum(terms, axis=0, keepdims=True)

        by_rows(x_ref.shape[0], 128, norm_back)
        for copy in across:
            copy.wait()


def feed_forward(x, dy, near, far, bias, after, biases, norm):
    rows, width = x.shape
    hidden = near.shape[2] // 2
    size = min(512, hidden)
    chunks = hidden // size

    n = lax.axis_size("dp")
    m, r = n // 2, width // n

    def block(s):
        return 3 - s // chunks

    def placed(s):
        turn = s // chunks
        return (1 - turn // 2, 0, (s % chunks) * (turn % 2))

    rows_spec = const((rows, width))
    grad_spec = pl.BlockSpec((1, width, size), placed)
    bias_spec = pl.BlockSpec((1, 1, size), lambda s: (block(s), 0, s % chunks))
    return pl.pallas_call(
        functools.partial(feed_forward_kernel, chunks=chunks),
        grid=(4 * chunks,),
        in_specs=[
            rows_spec,
            rows_spec,
            ANY,
            ANY,
            const(bias.shape),
            rows_spec,
            const(biases.shape),
            const(norm.shape),
        ],
        out_specs=[rows_spec, rows_spec, rows_spec, const((8, width)), grad_spec, grad_spec, bias_spec, ANY, ANY],
        out_shape=[
            jax.ShapeDtypeStruct((rows, width), F32),
            jax.ShapeDtypeStruct((rows, width), F32),
            jax.ShapeDtypeStruct((rows, width), BF16),
            jax.ShapeDtypeStruct((8, width), F32),
            jax.ShapeDtypeStruct((2, width, hidden), BF16),
            jax.ShapeDtypeStruct((2, width, hidden), BF16),
            jax.ShapeDtypeStruct((4, 1, hidden), F32),
            jax.ShapeDtypeStruct((2, m // 2, r, hidden), BF16),
            jax.ShapeDtypeStruct((2, m - m // 2, r, hidden), BF16),
        ],
        scratch_shapes=[
            pltpu.VMEM((width, rows), BF16),
            pltpu.VMEM((width, rows), BF16),
            pltpu.VMEM((rows, width), F32),
            pltpu.VMEM((chunks, 2, width, size), BF16),
            pltpu.VMEM((2 * chunks, 2, width, size), BF16),
            pltpu.VMEM((2, m, r, hidden), BF16),
            pltpu.VMEM((2, 2, width, size), BF16),
            pltpu.SemaphoreType.DMA((2, 2)),
        ]
        + link_scratch(2 * chunks + 2, 1),
        compiler_params=pltpu.CompilerParams(
            vmem_limit_bytes=VMEM_LIMIT, collective_id=3, has_side_effects=True
        ),
        cost_estimate=pl.CostEstimate(
            flops=48 * rows * width * hidden, bytes_accessed=40 * 2**20, transcendentals=8 * rows * hidden
        ),
        name="feed_forward",
    )(x, dy, near, far, bias, after, biases, norm)


def cross_backward_kernel(
    len_ref, low_ref, x_ref, enc_ref, w_ref, q_ref, k_ref, v_ref, mt_ref, lse_ref, up_ref, down_ref, from_x, from_y,
    back_ref, enc_out, grad_ref, bq_ref, bv_ref, up_out, down_out,
    low_t, x_t, enc_t, enc_acc, give, got, *scratch, heads, bk
):
    i = pl.program_id(0)
    last = pl.num_programs(0) - 1
    links = Links(*scratch[14:])
    sums = [
        Gather(links, ref.at[0], ref.at[1], from_x.at[k], from_y.at[k], scratch[7 * k : 7 * k + 7])
        for k, ref in enumerate((up_ref, down_ref))
    ]
    leave = [links.local(g.column, out) for g, out in zip(sums, (up_out, down_out))]
    pair = i // 2
    to_core = pltpu.make_async_remote_copy(
        src_ref=give,
        dst_ref=got.at[pair],
        send_sem=links.send_sems.at[links.used + pair],
        recv_sem=links.recv_sems.at[links.used + pair],
        device_id=links.partner(CORE),
        device_id_type=pl.DeviceIdType.MESH,
    )

    @pl.when(i == 0)
    def _():
        links.greet([CORE, X, Y])
        for g in sums:
            g.start()
        low_t[...] = low_ref[...].T
        x_t[...] = x_ref[...].T
        enc_t[...] = enc_ref[...].T
        back_ref[...] = jnp.zeros_like(back_ref)
        enc_acc[...] = jnp.zeros_like(enc_acc)

    @pl.when(i == 1)
    def _():
        for g in sums:
            g.middle()

    rows, width = q_ref.shape[1:]
    n = k_ref.shape[1]
    hd = width // heads
    scale = 1.0 / math.sqrt(hd)
    w_query, w_keyval, w_out = w_ref.at[0, :, :width], w_ref.at[0, :, width : 3 * width], w_ref.at[0, :, 3 * width :]
    grads = dot_nn(low_ref[...], w_out[...]).astype(BF16)
    mixed_t = mt_ref[0]
    products = grads.T.astype(F32) * mixed_t.astype(F32)
    inner = [jnp.sum(products[h * hd : (h + 1) * hd, :], axis=0, keepdims=True) for h in range(heads)]
    scaled = q_ref[0] * jnp.asarray(scale, BF16)
    q_heads = [head_only(scaled, h, hd) for h in range(heads)]
    d_heads = [head_only(grads, h, hd) for h in range(heads)]
    lse = lse_ref[0]
    keys_t = k_ref[0].T
    dq = [None] * heads
    dkv = []
    for j in range(n // bk):
        span = slice(j * bk, (j + 1) * bk)
        keys = k_ref[0, span, :]
        values = v_ref[0, span, :]
        ok = j * bk + lax.broadcasted_iota(jnp.int32, (bk, 1), 0) < len_ref[0]
        scores = [dot_nt(keys, q_heads[h]) for h in range(heads)]
        dprobs = [dot_nt(values, d_heads[h]) for h in range(heads)]
        dv_sum, dk_sum = None, None
        for h in range(heads):
            part = slice(h * hd, (h + 1) * hd)
            probs = jnp.exp(jnp.where(ok, scores[h], NEGATIVE) - lse[h : h + 1, :])
            ds = (probs * (dprobs[h] - inner[h])).astype(BF16)
            dv_h = dot_nn(probs.astype(BF16), d_heads[h])
            dk_h = dot_nn(ds, q_heads[h])
            dv_sum = dv_h if dv_sum is None else dv_sum + dv_h
            dk_sum = dk_h if dk_sum is None else dk_sum + dk_h
            dq_h = dot_nn(keys_t[part, span], ds)
            dq[h] = dq_h if dq[h] is None else dq[h] + dq_h
        block = jnp.concatenate([dk_sum.astype(BF16), dv_sum.astype(BF16)], 1)
        enc_acc[span, :] += dot_nt(block, w_keyval[...])
        dkv.append(block)
    dq = (jnp.concatenate(dq, 0) * scale).astype(BF16).T
    dkv = jnp.concatenate(dkv, 0)
    bq_ref[0] = jnp.sum(dq.astype(F32), axis=0, keepdims=True)
    bv_ref[0] = jnp.sum(dkv[:, width:].astype(F32), axis=0, keepdims=True)
    back_ref[...] += dot_nt(dq, w_query[...])

    @pl.when(i % 2 == 1)
    def _():
        to_core.wait_send()

    give[:, :width] = dot_nn(x_t[...], dq).astype(BF16)
    give[:, width : 3 * width] = dot_nn(enc_t[...], dkv).astype(BF16)
    give[:, 3 * width :] = dot_nn(low_t[...], mixed_t.T).astype(BF16)

    @pl.when(i % 2 == 0)
    def _():
        to_core.start()

    @pl.when(i % 2 == 1)
    def _():
        to_core.wait_recv()
        grad_ref[0] = (give[...].astype(F32) + got[pair].astype(F32)).astype(BF16)

    @pl.when(i == last)
    def _():
        enc_out[...] = enc_acc[...].astype(BF16)
        for g, copy in zip(sums, leave):
            g.end()
            copy.start()
        for copy in leave:
            copy.wait()


def cross_backward(
    lengths, low, x, encoder, weights, queries, keys, values, mixed_t, lse, up_sum, down_sum, from_x, from_y, heads
):
    count, model = x.shape
    n = encoder.shape[0]
    parts, _, columns = weights.shape
    width = columns // 4
    _, m, _, r, c = up_sum.shape

    def by_part(*shape):
        return pl.BlockSpec((1,) + shape, lambda i: (i ^ 1,) + (0,) * len(shape))

    return pl.pallas_call(
        functools.partial(cross_backward_kernel, heads=heads, bk=256),
        grid=(parts,),
        in_specs=[
            pl.BlockSpec(memory_space=pltpu.SMEM),
            const((count, model)),
            const((count, model)),
            const((n, model)),
            by_part(model, columns),
            by_part(count, width),
            by_part(n, width),
            by_part(n, width),
            by_part(width, count),
            by_part(heads, count),
            ANY,
            ANY,
            ANY,
            ANY,
        ],
        out_specs=[
            const((count, model)),
            const((n, model)),
            pl.BlockSpec((1, model, columns), lambda i: (i // 2, 0, 0), pipeline_mode=pl.Buffered(1)),
            by_part(1, width),
            by_part(1, width),
            ANY,
            ANY,
        ],
        out_shape=[
            jax.ShapeDtypeStruct((count, model), F32),
            jax.ShapeDtypeStruct((n, model), BF16),
            jax.ShapeDtypeStruct((2, model, columns), BF16),
            jax.ShapeDtypeStruct((parts, 1, width), F32),
            jax.ShapeDtypeStruct((parts, 1, width), F32),
            jax.ShapeDtypeStruct((m, r, c), BF16),
            jax.ShapeDtypeStruct((m, r, c), BF16),
        ],
        scratch_shapes=[
            pltpu.VMEM((model, count), BF16),
            pltpu.VMEM((model, count), BF16),
            pltpu.VMEM((model, n), BF16),
            pltpu.VMEM((n, model), F32),
            pltpu.VMEM((model, columns), BF16),
            pltpu.VMEM((2, model, columns), BF16),
        ]
        + gather_scratch(m, r, c) * 2
        + link_scratch(10, 12),
        compiler_params=pltpu.CompilerParams(
            vmem_limit_bytes=60 * 2**20, collective_id=4, has_side_effects=True
        ),
        cost_estimate=pl.CostEstimate(
            flops=48 * parts * count * n * width,
            bytes_accessed=16 * parts * n * width,
            transcendentals=parts * count * n * heads,
        ),
        name="cross_backward",
    )(lengths, low, x, encoder, weights, queries, keys, values, mixed_t, lse, up_sum, down_sum, from_x, from_y)


def on_device(
    block_in,
    encoder_out,
    out_grad,
    bounds,
    enc_lengths,
    norm_params,
    w_qkv,
    w_self_out,
    w_cross_q,
    w_cross_kv,
    w_cross_out,
    w_up,
    w_down,
    biases,
    up_bias,
):
    groups_count = lax.axis_size("dp")
    width = w_cross_q.shape[1]
    hidden_width = w_up.shape[1]
    heads = H // 4
    own_rows, model_width = block_in.shape
    w_rows = w_cross_q.shape[0]

    first_in, self_w, cross_column = start_gather(
        block_in,
        norm_params,
        jnp.concatenate([w_qkv.reshape(w_rows, 3 * width), w_self_out.T], axis=1),
        jnp.concatenate([w_cross_q, w_cross_kv.reshape(w_rows, 2 * width), w_cross_out.T], axis=1),
    )
    self_w = self_w.reshape(model_width, 4 * width)

    self_safe = 1024
    queries, key_rows, value_rows, keys_t, self_mixed_t, self_lse, terms, cross_w, ffn_column, enc_all = self_forward(
        bounds,
        first_in,
        self_w,
        biases,
        cross_column,
        jnp.concatenate([w_up, w_down.T], axis=1),
        encoder_out,
        heads,
        self_safe,
    )
    cross_w = cross_w.reshape(4, model_width, 4 * width)
    after_self, second_in, ffn_near = sum_after_self(
        terms, block_in, biases, norm_params, ffn_column
    )

    cross_q, cross_k, cross_v, cross_mixed_t, cross_lse, after_cross, third_in, ffn_far = cross_forward(
        enc_lengths,
        second_in,
        enc_all,
        cross_w,
        biases,
        after_self,
        norm_params,
        ffn_column,
        heads,
    )

    output, cross_rows_grad, cross_low, ffn_sums, up_sum, down_sum, bias_up_parts, from_x, from_y = feed_forward(
        third_in,
        out_grad,
        ffn_near.reshape(2, model_width, 2 * hidden_width),
        ffn_far.reshape(2, model_width, 2 * hidden_width),
        up_bias.reshape(4, hidden_width),
        after_cross,
        biases,
        norm_params,
    )

    by_shard = (2, groups_count // 2, 2, w_rows, hidden_width)
    second_grad, enc_terms, cross_sum, bias_cq_parts, bias_cv_parts, up_column, down_column = cross_backward(
        enc_lengths,
        cross_low,
        second_in,
        enc_all,
        cross_w,
        cross_q,
        cross_k,
        cross_v,
        cross_mixed_t,
        cross_lse,
        up_sum.reshape(by_shard),
        down_sum.reshape(by_shard),
        from_x,
        from_y,
        heads,
    )
    cross_sum = cross_sum.reshape(2, groups_count // 2, 2, w_rows, 4 * width)
    self_wide, self_rows_grad, self_sums, summed_down, diagonal = middle(
        second_grad, after_self, cross_rows_grad, norm_params, down_column, cross_sum
    )
    self_dq, self_dk, self_dv, summed_up, summed_cross, encoder_grad = self_backward(
        bounds,
        queries,
        key_rows,
        value_rows,
        keys_t,
        self_wide,
        self_w,
        self_mixed_t,
        self_lse,
        up_column,
        cross_sum,
        diagonal,
        enc_terms,
        heads,
        self_safe,
    )
    input_grad, summed_self, vectors = tail(
        self_dq,
        self_dk,
        self_dv,
        self_w,
        first_in,
        self_wide,
        self_mixed_t,
        block_in,
        self_rows_grad,
        norm_params,
        self_sums,
        ffn_sums,
        bias_cq_parts,
        bias_cv_parts,
        bias_up_parts,
    )
    scale = 1.0 / groups_count
    output, input_grad, encoder_grad, g_qkv, g_so, g_cq, g_ckv, g_co, g_up, g_down = results(
        output, input_grad, encoder_grad, summed_self, summed_cross, summed_up, summed_down, scale
    )
    vectors = vectors * scale
    return (
        output,
        input_grad,
        encoder_grad,
        vectors[:6].reshape(norm_params.shape),
        g_qkv,
        g_so.T,
        g_cq,
        g_ckv,
        g_co.T,
        g_up,
        g_down.T,
        vectors[6:13],
        vectors[13:17].reshape(-1),
    )


def solution(mesh):
    rows = P(("dp", "tensor"), None)
    placed = (
        rows,
        rows,
        rows,
        P("dp", None),
        P("dp"),
        P(),
        P("dp", None, "tensor"),
        P("tensor", "dp"),
        P("dp", "tensor"),
        P("dp", None, "tensor"),
        P("tensor", "dp"),
        P("dp", "tensor"),
        P("tensor", "dp"),
        P(),
        P(),
    )
    return jax.shard_map(
        on_device,
        mesh=mesh,
        in_specs=placed,
        out_specs=(
            rows,
            rows,
            rows,
            P(),
            P("dp", None, "tensor"),
            P("tensor", "dp"),
            P("dp", "tensor"),
            P("dp", None, "tensor"),
            P("tensor", "dp"),
            P("dp", "tensor"),
            P("tensor", "dp"),
            P(),
            P(),
        ),
        check_vma=False,
    )
```

```python
import functools
import math

import jax
import jax.numpy as jnp
from jax import lax
from jax.experimental import pallas as pl
from jax.experimental.pallas import tpu as pltpu
from jax.sharding import PartitionSpec as P

H = 16
EPSILON = 1e-05
NEGATIVE = -1e30
F32 = jnp.float32
BF16 = jnp.bfloat16
VMEM_LIMIT = 56 * 2**20


def dot_nt(a, b):
    return lax.dot_general(a, b, (((1,), (1,)), ((), ())), preferred_element_type=F32)


def dot_nn(a, b):
    return lax.dot_general(a, b, (((1,), (0,)), ((), ())), preferred_element_type=F32)


def dot_tn(a, b):
    return lax.dot_general(a, b, (((0,), (0,)), ((), ())), preferred_element_type=F32)


LANES = 128


def lanes_of(h, size):
    group = h * size // LANES
    return group, slice(group * LANES, (group + 1) * LANES)


def head_only(x, h, size):
    group, part = lanes_of(h, size)
    lane = group * LANES + lax.broadcasted_iota(jnp.int32, (x.shape[0], LANES), 1)
    return jnp.where((lane >= h * size) & (lane < (h + 1) * size), x[:, part], jnp.zeros((), x.dtype))


def add_group(sums, group, value):
    sums[group] = value if group not in sums else sums[group] + value


def self_bad(b_ref, q_start, k_start, bq, bk, causal):
    qi = q_start + lax.broadcasted_iota(jnp.int32, (1, bq), 1)
    kj = k_start + lax.broadcasted_iota(jnp.int32, (bk, 1), 0)
    bad = (qi >= b_ref[0, 1]) & ((kj >= b_ref[0, 0]) & (kj < b_ref[0, 1]))
    if causal:
        bad = bad | (kj > qi)
    return bad


def over_keys(i, bq, safe, block, between=()):
    def visit(j, c):
        for at_i, at_j, action in between:
            pl.when((i == at_i) & (j == at_j))(action)

        @pl.when(j < safe // bq)
        def _():
            block(j * bq, bq, 0, "none")

        @pl.when(j >= safe // bq)
        def _():
            block(j * bq, bq, 0, "segment")

        return c

    lax.fori_loop(0, i, visit, 0)
    half = bq // 2
    block(i * bq, half, 0, "causal")
    block(i * bq + half, half, half, "causal")


CORE = ("tensor", 1)
X = ("tensor", 2)
Y = ("dp", 1)
ANY = pl.BlockSpec(memory_space=pl.ANY)


class Links:
    def __init__(self, send_sems, recv_sems, local_sems):
        self.dp = lax.axis_index("dp")
        self.tensor = lax.axis_index("tensor")
        self.send_sems, self.recv_sems, self.local_sems = send_sems, recv_sems, local_sems
        self.used = 0
        self.used_local = 0

    def partner(self, way):
        axis, distance = way
        if axis == "tensor":
            return (self.dp, self.tensor ^ distance)
        return (self.dp ^ distance, self.tensor)

    def greet(self, ways):
        barrier = pltpu.get_barrier_semaphore()
        for way in ways:
            pl.semaphore_signal(
                barrier, inc=1, device_id=self.partner(way), device_id_type=pl.DeviceIdType.MESH
            )
        pl.semaphore_wait(barrier, len(ways))

    def copy(self, source, target, way):
        k = self.used
        self.used += 1
        return pltpu.make_async_remote_copy(
            src_ref=source,
            dst_ref=target,
            send_sem=self.send_sems.at[k],
            recv_sem=self.recv_sems.at[k],
            device_id=self.partner(way),
            device_id_type=pl.DeviceIdType.MESH,
        )

    def local(self, source, target):
        k = self.used_local
        self.used_local += 1
        return pltpu.make_async_copy(source, target, self.local_sems.at[k])


def link_scratch(copies, local):
    return [
        pltpu.SemaphoreType.DMA((copies,)),
        pltpu.SemaphoreType.DMA((copies,)),
        pltpu.SemaphoreType.DMA((local,)),
    ]


def z_distances(n):
    found = []
    m = n // 2
    while m > 1:
        m //= 2
        found.append(m)
    return found


def z_ways(n):
    return [("dp", 2 * distance) for distance in z_distances(n)]


def column_stages(links, shard, column, n):
    z = links.dp // 2
    held = [z]
    stages = []
    for distance in z_distances(n):
        stages.append(
            [
                (
                    links.copy(shard if k == 0 else column.at[index], column.at[index], ("dp", 2 * distance)),
                    index ^ distance,
                )
                for k, index in enumerate(held)
            ]
        )
        held = held + [index ^ distance for index in held]
    return stages


class Spread:
    def __init__(self, links, source, column, whole):
        y = links.dp % 2
        half = column.shape[0] // 2
        low, high = pl.ds(0, half), pl.ds(half, half)
        near, near_core, far, far_core = (whole.at[k] for k in range(4))
        self.load = links.local(source, column)
        self.own = links.local(column, near.at[:, y])
        self.first = [
            links.copy(column, near.at[:, y], Y),
            links.copy(column, far.at[:, y], X),
        ]
        self.core = [links.copy(column, near_core.at[:, y], CORE)]
        self.second = [
            links.copy(near.at[low, 1 - y], far.at[low, 1 - y], X),
            links.copy(far.at[high, y], far.at[high, y], Y),
        ]
        self.core_second = [
            links.copy(near.at[:, 1 - y], near_core.at[:, 1 - y], CORE),
            links.copy(far.at[:, y], far_core.at[:, y], CORE),
        ]
        self.core_third = [links.copy(far.at[:, 1 - y], far_core.at[:, 1 - y], CORE)]

    def start(self):
        self.load.start()
        self.load.wait()
        for copy in self.first + self.core + [self.own]:
            copy.start()

    def middle(self):
        for copy in self.first:
            copy.wait_recv()
        for copy in self.second + self.core_second:
            copy.start()

    def last(self):
        for copy in self.second:
            copy.wait_recv()
        for copy in self.core_third:
            copy.start()

    def end(self):
        self.own.wait()
        for copy in self.first + self.second:
            copy.wait_send()
        for copy in self.core + self.core_second + self.core_third:
            copy.wait()


def add_to(total_ref, other_ref):
    def one(k, c):
        total_ref[k] = (total_ref[k].astype(F32) + other_ref[k].astype(F32)).astype(BF16)
        return c

    lax.fori_loop(0, total_ref.shape[0], one, 0)


class Gather:
    def __init__(self, links, near, far, from_x, from_y, buffers):
        y = links.dp % 2
        self.column, self.over_y, self.over_x, self.add_y, self.add_x, self.sum_y, self.sum_x = buffers
        m = self.column.shape[0]
        low, high = pl.ds(0, m // 2), pl.ds(m // 2, m - m // 2)
        self.loads = [
            links.local(near.at[low, 1 - y], self.over_y),
            links.local(far.at[high, y], self.over_x),
            links.local(from_x, self.add_y),
            links.local(from_y, self.add_x),
            links.local(near.at[:, y], self.column),
        ]
        self.first = [
            links.copy(far.at[low, y], self.sum_x.at[low], X),
            links.copy(near.at[high, 1 - y], self.sum_y.at[high], Y),
        ]
        self.second = [
            links.copy(self.over_x, self.sum_x.at[high], X),
            links.copy(self.over_y, self.sum_y.at[low], Y),
        ]

    def start(self):
        for copy in self.first + self.loads:
            copy.start()

    def middle(self):
        for copy in self.loads:
            copy.wait()
        add_to(self.over_x, self.add_x)
        add_to(self.over_y, self.add_y)
        for copy in self.second:
            copy.start()

    def end(self):
        for copy in self.first + self.second:
            copy.wait_recv()
        add_to(self.column, self.sum_y)
        add_to(self.column, self.sum_x)
        for copy in self.first + self.second:
            copy.wait_send()


def gather_scratch(m, r, c):
    whole = pltpu.VMEM((m, r, c), BF16)
    half = pltpu.VMEM((m // 2, r, c), BF16)
    return [whole] + [half] * 4 + [whole] * 2


class GatherLast:
    def __init__(self, links, near, far, diagonal, buffers):
        y = links.dp % 2
        self.column, self.over_x, self.diagonal, self.sum_y, self.sum_x = buffers
        self.loads = [
            links.local(far.at[:, y], self.over_x),
            links.local(diagonal, self.diagonal),
            links.local(near.at[:, y], self.column),
        ]
        self.over_y = links.copy(near.at[:, 1 - y], self.sum_y, Y)
        self.along_x = links.copy(self.over_x, self.sum_x, X)

    def start(self):
        self.over_y.start()
        for copy in self.loads:
            copy.start()

    def middle(self):
        for copy in self.loads:
            copy.wait()
        add_to(self.over_x, self.diagonal)
        self.along_x.start()

    def end(self):
        self.over_y.wait_recv()
        self.along_x.wait_recv()
        add_to(self.column, self.sum_y)
        add_to(self.column, self.sum_x)
        self.over_y.wait_send()
        self.along_x.wait_send()


class Collect:
    def __init__(self, links, column, slots):
        z = links.dp // 2
        self.column, self.slots, self.z = column, slots, z
        m = column.shape[0]
        distances = z_distances(2 * m)[::-1]
        self.stages = []
        first = 0
        for step, distance in enumerate(distances):
            kept = [0]
            for other in distances[step + 1 :]:
                kept = kept + [k ^ other for k in kept]
            self.stages.append(
                [
                    (links.copy(column.at[z ^ distance ^ k], slots.at[first + i], ("dp", 2 * distance)), first + i, z ^ k)
                    for i, k in enumerate(kept)
                ]
            )
            first += len(kept)

    def start(self, step):
        for copy, _, _ in self.stages[step]:
            copy.start()

    def finish(self, step):
        for copy, slot, index in self.stages[step]:
            copy.wait_recv()
            self.column[index] = (self.column[index].astype(F32) + self.slots[slot].astype(F32)).astype(BF16)

    def drain(self):
        for stage in self.stages:
            for copy, _, _ in stage:
                copy.wait_send()


class SpreadFar:
    def __init__(self, links, column, whole):
        y = links.dp % 2
        far, far_core = whole.at[0], whole.at[1]
        m, _, c = column.shape
        step = max(m // 4, 1)
        self.over_x, self.over_y, self.core_x, self.core_y = [], [], [], []
        for k in range(m // step):
            for h in range(2):
                z, part = pl.ds(k * step, step), pl.ds(h * (c // 2), c // 2)
                own = far.at[z, y, :, part]
                other = far.at[z, 1 - y, :, part]
                self.over_x.append(links.copy(column.at[z, :, part], own, X))
                self.over_y.append(links.copy(own, own, Y))
                self.core_x.append(links.copy(own, far_core.at[z, y, :, part], CORE))
                self.core_y.append(links.copy(other, far_core.at[z, 1 - y, :, part], CORE))

    def start(self):
        for copy in self.over_x:
            copy.start()

    def onward(self, k):
        self.over_x[k].wait_recv()
        self.over_y[k].start()
        self.core_x[k].start()

    def last(self, k):
        self.over_y[k].wait_recv()
        self.core_y[k].start()

    def end(self):
        for copy in self.over_x + self.over_y:
            copy.wait_send()
        for copy in self.core_x + self.core_y:
            copy.wait()


class RowSum:
    def __init__(self, links, terms, buffers, left=False):
        self.left = left
        self.near, self.far, self.got_near, self.got_far, self.got_x = buffers
        count = self.near.shape[0]

        def rows(distance):
            start = pl.multiple_of((links.tensor ^ distance) * count, count)
            return terms.at[pl.ds(start, count)]

        self.loads = [links.local(rows(0), self.near), links.local(rows(2), self.far)]
        self.core = [links.copy(rows(3), self.got_far, CORE), links.copy(rows(1), self.got_near, CORE)]
        self.over_x = links.copy(self.far, self.got_x, X)

    def start(self):
        for copy in self.loads[::-1] + self.core:
            copy.start()

    def middle(self):
        self.loads[1].wait()
        self.core[0].wait_recv()

        def add(rows):
            self.far[rows, :] = (self.far[rows, :].astype(F32) + self.got_far[rows, :].astype(F32)).astype(BF16)

        by_rows(self.far.shape[0], 64, add)
        self.over_x.start()

    def end(self):
        self.loads[0].wait()
        self.core[1].wait_recv()
        self.over_x.wait_recv()
        for copy in self.core + ([] if self.left else [self.over_x]):
            copy.wait_send()

    def total(self, rows):
        return self.near[rows, :].astype(F32) + self.got_near[rows, :].astype(F32) + self.got_x[rows, :].astype(F32)


def row_sum_scratch(count, width):
    return [pltpu.VMEM((count, width), BF16)] * 5


class Everywhere:
    def __init__(self, links, held, slots, n):
        self.held, self.slots = held, slots
        ways = everywhere_ways(n)
        self.copies = [links.copy(held.at[k], slots.at[k], way) for k, way in enumerate(ways)]

    def start(self, step):
        self.copies[step].start()

    def finish(self, step):
        self.copies[step].wait()
        self.held[step + 1] = self.held[step] + self.slots[step]


def everywhere_ways(n):
    return [CORE, X, Y] + z_ways(n)


def everywhere_scratch(k, c, n):
    steps = len(everywhere_ways(n))
    return [pltpu.VMEM((steps + 1, k, c), F32), pltpu.VMEM((steps, k, c), F32)]


def middle_kernel(
    back_ref, rows_ref, grad_ref, norm_ref, down_ref, cross_ref,
    wide_out, grad_out, sums_ref, down_out, diagonal_out,
    low, column, slots, send_sems, recv_sems, local_sems, *, n
):
    links = Links(send_sems, recv_sems, local_sems)
    count = low.shape[0]
    load = links.local(down_ref, column)
    load.start()
    collect = Collect(links, column, slots)

    def place(distance):
        return wide_out.at[pl.ds(pl.multiple_of((links.tensor ^ distance) * count, count), count)]

    own = links.local(low, place(0))
    half = count // 2
    parts = [pl.ds(0, half), pl.ds(half, half)]
    over_x = [links.copy(low.at[part], place(0).at[part], X) for part in parts]
    over_core = links.copy(low, place(0), CORE)
    onward = [links.copy(place(2).at[part], place(2).at[part], CORE) for part in parts]
    over_y = links.copy(cross_ref.at[1, :, 1 - links.dp % 2], diagonal_out, Y)
    links.greet([CORE, X, Y] + z_ways(n))
    over_y.start()
    load.wait()
    collect.start(0)
    sums_ref[...] = jnp.zeros_like(sums_ref)

    def norm_back(rows):
        incoming = back_ref[rows, :]
        rows_grad, gain_terms = norm_rows_back(rows_ref[rows, :], incoming, norm_ref[1, 0:1, :])
        rows_grad = rows_grad + grad_ref[rows, :]
        rounded = rows_grad.astype(BF16)
        grad_out[rows, :] = rows_grad
        low[rows, :] = rounded
        for k, terms in enumerate((gain_terms, incoming, rounded.astype(F32))):
            sums_ref[k : k + 1, :] += jnp.sum(terms, axis=0, keepdims=True)

    for part, copy in zip(parts, over_x):
        by_rows(half, 64, lambda rows, part=part: norm_back(pl.ds(pl.multiple_of(part.start + rows.start, 64), 64)))
        copy.start()
    own.start()
    over_core.start()
    for step in range(len(collect.stages) - 1):
        collect.finish(step)
        collect.start(step + 1)
    for copy, later in zip(over_x, onward):
        copy.wait_recv()
        later.start()
    collect.finish(len(collect.stages) - 1)
    down_out[...] = column[collect.z].astype(F32)
    collect.drain()
    own.wait()
    for copy in over_x:
        copy.wait_send()
    over_core.wait()
    for copy in onward:
        copy.wait()
    over_y.wait()


def middle(back, rows, grad, norm, down_column, cross_sum):
    n = lax.axis_size("dp")
    count, width = rows.shape
    m, r, c = down_column.shape
    vmem = pl.BlockSpec(memory_space=pltpu.VMEM)
    return pl.pallas_call(
        functools.partial(middle_kernel, n=n),
        in_specs=[vmem, vmem, vmem, vmem, ANY, ANY],
        out_specs=[ANY, vmem, vmem, vmem, ANY],
        out_shape=[
            jax.ShapeDtypeStruct((4 * count, width), BF16),
            jax.ShapeDtypeStruct((count, width), F32),
            jax.ShapeDtypeStruct((8, width), F32),
            jax.ShapeDtypeStruct((r, c), F32),
            jax.ShapeDtypeStruct((m, r, cross_sum.shape[4]), BF16),
        ],
        scratch_shapes=[
            pltpu.VMEM((count, width), BF16),
            pltpu.VMEM((m, r, c), BF16),
            pltpu.VMEM((m, r, c), BF16),
        ]
        + link_scratch(6 + m, 2),
        compiler_params=pltpu.CompilerParams(
            vmem_limit_bytes=VMEM_LIMIT, collective_id=6, has_side_effects=True
        ),
        cost_estimate=pl.CostEstimate(flops=0, bytes_accessed=100 * 2**20, transcendentals=0),
        name="middle",
    )(back, rows, grad, norm, down_column, cross_sum)


def tail_kernel(
    dq_ref, dk_ref, dv_ref, w_ref, first_ref, wide_ref, mt_ref, rows_ref, grad_ref, norm_ref,
    self_ref, ffn_ref, cq_ref, cv_ref, up_ref,
    grad_out, weights_out, late_out, give, acc, weights, *scratch, n, step_rows
):
    links = Links(*scratch[-3:])
    member = links.tensor
    near, far, got_near, got_far, got_x = scratch[:5]
    columns, gots, slots = scratch[5:7], scratch[7:9], scratch[9:11]
    held, late_slots = scratch[11:13]
    count, model = near.shape
    width = dq_ref.shape[1]
    y = links.dp % 2
    c = columns[0].shape[2]
    m, _, r, _ = weights.shape
    half = count // 2
    parts = [pl.ds(0, half), pl.ds(half, half)]
    core_far = links.copy(give.at[0], got_far, CORE)
    core_near = links.copy(give.at[1], got_near, CORE)
    over_x = [links.copy(far.at[part], got_x.at[part], X) for part in parts]
    over_y, collects = [], []
    for k, (column, got, slot) in enumerate(zip(columns, gots, slots)):
        over_y.append(links.copy(weights.at[:, 1 - y, :, pl.ds(k * c, c)], got, Y))
        collects.append(Collect(links, column, slot))
    stages = len(collects[0].stages)
    late = Everywhere(links, held, late_slots, n)
    steps = len(late.copies)
    links.greet(everywhere_ways(n))

    def terms(distance, target):
        base = (member ^ distance) * count

        def one(rows):
            there = pl.ds(pl.multiple_of(base + rows.start, 128), 128)
            total = dot_nt(dq_ref[there, :], w_ref[:, :width])
            total = total + dot_nt(dk_ref[there, :], w_ref[:, width : 2 * width])
            target[rows, :] = (total + dot_nt(dv_ref[there, :], w_ref[:, 2 * width : 3 * width])).astype(BF16)

        by_rows(count, 128, one)

    def packed(k):
        for block in range(2 * m):
            span = slice(block * r, (block + 1) * r)
            weights[block // 2, block % 2, :, k * c : (k + 1) * c] = acc[span, k * c : (k + 1) * c].astype(BF16)
        columns[k][...] = weights[:, y, :, k * c : (k + 1) * c]

    terms(3, give.at[0])
    core_far.start()
    terms(2, far)
    core_far.wait_recv()
    for part, copy in zip(parts, over_x):

        def add(rows, part=part):
            there = pl.ds(pl.multiple_of(part.start + rows.start, 64), 64)
            far[there, :] = (far[there, :].astype(F32) + got_far[there, :].astype(F32)).astype(BF16)

        by_rows(half, 64, add)
        copy.start()

    acc[...] = jnp.zeros_like(acc)

    def products(rows):
        source = first_ref[rows, :].T
        for k, ref in enumerate((dq_ref, dk_ref, dv_ref)):
            acc[:, k * width : (k + 1) * width] += dot_nn(source, ref[rows, :])

    by_rows(dq_ref.shape[0], step_rows, products)
    packed(0)
    over_y[0].start()
    terms(1, give.at[1])
    core_near.start()
    terms(0, near)

    def products_out(rows):
        acc[:, 3 * width :] += dot_nn(wide_ref[rows, :].T, mt_ref[:, rows].T)

    by_rows(dq_ref.shape[0], step_rows, products_out)
    packed(1)

    held[0] = jnp.zeros(held.shape[1:], F32)
    held[0, 2:4, :] = self_ref[0:2, :]
    held[0, 4:6, :] = ffn_ref[0:2, :]
    held[0, 8:9, :] = self_ref[2:3, :]
    held[0, 11:13, :] = ffn_ref[2:4, :]
    for distance in range(4):
        there = pl.ds(pl.multiple_of((member ^ distance) * width, width), width)
        held[0, 9:10, there] = cq_ref[distance]
        held[0, 10:11, there] = cv_ref[distance]
        held[0, pl.ds(13 + (member ^ distance), 1), :] = up_ref[distance]
    here = pl.ds(pl.multiple_of(member * width, width), width)

    def column_sums(rows):
        held[0, 6:7, here] += jnp.sum(dq_ref[rows, :].astype(F32), axis=0, keepdims=True)
        held[0, 7:8, here] += jnp.sum(dv_ref[rows, :].astype(F32), axis=0, keepdims=True)

    by_rows(dq_ref.shape[0], step_rows, column_sums)

    def norm_back(part):
        def one(rows):
            rows = pl.ds(pl.multiple_of(part.start + rows.start, 64), 64)
            incoming = near[rows, :].astype(F32) + got_near[rows, :].astype(F32) + got_x[rows, :].astype(F32)
            rows_grad, gain_terms = norm_rows_back(rows_ref[rows, :].astype(F32), incoming, norm_ref[0, 0:1, :])
            grad_out[rows, :] = rows_grad + grad_ref[rows, :]
            held[0, 0:1, :] += jnp.sum(gain_terms, axis=0, keepdims=True)
            held[0, 1:2, :] += jnp.sum(incoming, axis=0, keepdims=True)

        by_rows(half, 64, one)

    def summed_y(k):
        over_y[k].wait_recv()
        add_to(columns[k], gots[k])
        collects[k].start(0)

    def next_z(k):
        for step in range(stages - 1):
            collects[k].finish(step)
            collects[k].start(step + 1)

    def last_z(k):
        collects[k].finish(stages - 1)
        weights_out[:, k * c : (k + 1) * c] = columns[k][collects[k].z].astype(F32)

    summed_y(0)
    over_y[1].start()
    core_near.wait_recv()
    over_x[0].wait_recv()
    norm_back(parts[0])
    next_z(0)
    over_x[1].wait_recv()
    norm_back(parts[1])
    late.start(0)
    summed_y(1)
    late.finish(0)
    late.start(1)
    last_z(0)
    late.finish(1)
    late.start(2)
    next_z(1)
    late.finish(2)
    for step in range(3, steps):
        late.start(step)
        late.finish(step)
    last_z(1)
    late_out[...] = held[steps]
    for copy in over_x + over_y + [core_near, core_far]:
        copy.wait_send()
    for collect in collects:
        collect.drain()


def tail(dq, dk, dv, w, first, wide, mixed_t, rows, grad, norm, self_sums, ffn_sums, cq_sums, cv_sums, up_sums):
    n = lax.axis_size("dp")
    count, model = rows.shape
    width = dq.shape[1]
    m, r, c = n // 2, model // n, 4 * width
    vectors = (24, model)
    vmem = pl.BlockSpec(memory_space=pltpu.VMEM)
    part = pltpu.VMEM((m, r, c // 2), BF16)
    return pl.pallas_call(
        functools.partial(tail_kernel, n=n, step_rows=512),
        in_specs=[vmem] * 15,
        out_specs=[vmem, vmem, vmem],
        out_shape=[
            jax.ShapeDtypeStruct((count, model), F32),
            jax.ShapeDtypeStruct((r, c), F32),
            jax.ShapeDtypeStruct(vectors, F32),
        ],
        scratch_shapes=[
            pltpu.VMEM((2, count, model), BF16),
            pltpu.VMEM((model, c), F32),
            pltpu.VMEM((m, 2, r, c), BF16),
        ]
        + row_sum_scratch(count, model)
        + [part] * 6
        + everywhere_scratch(*vectors, n)
        + link_scratch(6 + 2 * m + len(everywhere_ways(n)), 1),
        compiler_params=pltpu.CompilerParams(
            vmem_limit_bytes=VMEM_LIMIT, collective_id=7, has_side_effects=True
        ),
        cost_estimate=pl.CostEstimate(flops=0, bytes_accessed=100 * 2**20, transcendentals=0),
        name="tail",
    )(dq, dk, dv, w, first, wide, mixed_t, rows, grad, norm, self_sums, ffn_sums, cq_sums, cv_sums, up_sums)


def results_kernel(
    output_ref, grad_ref, enc_ref, self_ref, cross_ref, up_ref, down_ref,
    output_out, grad_out, enc_out, qkv_out, so_out, cq_out, ckv_out, co_out, up_out, down_out, *, scale
):
    output_out[...] = output_ref[...]
    grad_out[...] = grad_ref[...]
    enc_out[...] = enc_ref[...]
    width = cq_out.shape[1]

    @pl.when(pl.program_id(0) == 0)
    def _():
        for k in range(3):
            qkv_out[:, k, :] = self_ref[:, k * width : (k + 1) * width] * scale
        so_out[...] = (self_ref[:, 3 * width :] * scale).T
        cq_out[...] = cross_ref[:, :width] * scale
        for k in range(2):
            ckv_out[:, k, :] = cross_ref[:, (k + 1) * width : (k + 2) * width] * scale
        co_out[...] = (cross_ref[:, 3 * width :] * scale).T
        up_out[...] = up_ref[...] * scale
        down_out[...] = (down_ref[...] * scale).T


def results(output, grad, encoder, self_w, cross_w, up, down, scale):
    r, c = self_w.shape
    width = c // 4
    steps = 4

    def rows(value):
        return pl.BlockSpec((value.shape[0] // steps, value.shape[1]), lambda i: (i, 0))

    shapes = [(r, 3, width), (width, r), (r, width), (r, 2, width), (width, r), up.shape, down.shape[::-1]]
    return pl.pallas_call(
        functools.partial(results_kernel, scale=scale),
        grid=(steps,),
        in_specs=[rows(output), rows(grad), rows(encoder)] + [const(v.shape) for v in (self_w, cross_w, up, down)],
        out_specs=[rows(output), rows(grad), rows(encoder)] + [const(shape) for shape in shapes],
        out_shape=[jax.ShapeDtypeStruct(v.shape, F32) for v in (output, grad, encoder)]
        + [jax.ShapeDtypeStruct(shape, F32) for shape in shapes],
        compiler_params=pltpu.CompilerParams(vmem_limit_bytes=VMEM_LIMIT),
        cost_estimate=pl.CostEstimate(flops=0, bytes_accessed=20 * 2**20, transcendentals=0),
        name="results",
    )(output, grad, encoder, self_w, cross_w, up, down)


def start_kernel(
    in_ref, norm_ref, qkv_ref, so_ref, cq_ref, ckv_ref, co_ref,
    rows_out, self_out, cross_out, rows_ref, self_ref, cross_ref, send_sems, recv_sems, local_sems, *, n
):
    links = Links(send_sems, recv_sems, local_sems)
    member, z, y = links.tensor, links.dp // 2, links.dp % 2
    count = rows_ref.shape[0]
    half = count // 2
    parts = [pl.ds(0, half), pl.ds(half, half)]

    def place(distance):
        return rows_out.at[pl.ds(pl.multiple_of((member ^ distance) * count, count), count)]

    over_x = [links.copy(rows_ref.at[part], place(0).at[part], X) for part in parts]
    over_core = [links.copy(rows_ref, place(0), CORE)]
    over_core += [links.copy(place(2).at[part], place(2).at[part], CORE) for part in parts]
    self_stages = column_stages(links, self_ref, self_out.at[:, y], n)
    cross_stages = column_stages(links, cross_ref, cross_out, n)
    over_y = [links.copy(self_ref, self_out.at[z, y], Y)]
    local = [
        links.local(rows_ref, place(0)),
        links.local(self_ref, self_out.at[z, y]),
        links.local(cross_ref, cross_out.at[z]),
    ]
    width = cq_ref.shape[1]
    for k in range(3):
        self_ref[:, k * width : (k + 1) * width] = qkv_ref[:, k, :]
    self_ref[:, 3 * width :] = so_ref[...].T
    cross_ref[:, :width] = cq_ref[...]
    for k in range(2):
        cross_ref[:, (k + 1) * width : (k + 2) * width] = ckv_ref[:, k, :]
    cross_ref[:, 3 * width :] = co_ref[...].T
    links.greet([CORE, X, Y] + z_ways(n))
    for copy in over_y + local[1:]:
        copy.start()
    for copy, _ in self_stages[0]:
        copy.start()
    for part, copy in zip(parts, over_x):

        def norm(rows, part=part):
            rows = pl.ds(pl.multiple_of(part.start + rows.start, 64), 64)
            xhat, _ = normalized(in_ref[rows, :].astype(F32))
            rows_ref[rows, :] = (xhat * norm_ref[0, 0:1, :] + norm_ref[0, 1:2, :]).astype(BF16)

        by_rows(half, 64, norm)
        copy.start()
    for copy in local[:1] + over_core[:1]:
        copy.start()
    for self_stage in self_stages:
        if self_stage is not self_stages[0]:
            for copy, _ in self_stage:
                copy.start()
        for copy, index in self_stage:
            copy.wait_recv()
            onward = links.copy(self_out.at[index, y], self_out.at[index, y], Y)
            onward.start()
            over_y.append(onward)
        if self_stage is self_stages[0]:
            for copy, _ in cross_stages[0]:
                copy.start()
    for cross_stage, later in zip(cross_stages, cross_stages[1:] + [[]]):
        for copy, _ in cross_stage:
            copy.wait_recv()
        for copy, _ in later:
            copy.start()
    for copy, onward in zip(over_x, over_core[1:]):
        copy.wait_recv()
        onward.start()
    for copy in local + over_y + over_core:
        copy.wait()
    for copy in over_x:
        copy.wait_send()
    for stage in self_stages + cross_stages:
        for copy, _ in stage:
            copy.wait_send()


def start_gather(rows, norm, qkv, self_out, cross_q, cross_kv, cross_out):
    n = lax.axis_size("dp")
    r, c = cross_q.shape[0], 4 * cross_q.shape[1]
    return pl.pallas_call(
        functools.partial(start_kernel, n=n),
        in_specs=[pl.BlockSpec(memory_space=pltpu.VMEM)] * 7,
        out_specs=[ANY] * 3,
        out_shape=[
            jax.ShapeDtypeStruct((4 * rows.shape[0], rows.shape[1]), BF16),
            jax.ShapeDtypeStruct((n // 2, 2, r, c), BF16),
            jax.ShapeDtypeStruct((n // 2, r, c), BF16),
        ],
        scratch_shapes=[pltpu.VMEM(rows.shape, BF16)] + [pltpu.VMEM((r, c), BF16)] * 2 + link_scratch(2 * n + 8, 3),
        compiler_params=pltpu.CompilerParams(
            vmem_limit_bytes=VMEM_LIMIT, collective_id=0, has_side_effects=True
        ),
        cost_estimate=pl.CostEstimate(flops=0, bytes_accessed=100 * 2**20, transcendentals=0),
        name="start_gather",
    )(rows, norm, qkv, self_out, cross_q, cross_kv, cross_out)


def self_forward_kernel(
    b_ref, x_ref, w_ref, biases_ref, column_ref, up_ref, down_ref,
    q_out, k_ref, v_out, kt_out, ot_ref, lse_ref, terms_ref, whole, next_column,
    vt_ref, m_s, l_s, acc, column, shard, send_sems, recv_sems, local_sems, *, heads, safe, n
):
    i = pl.program_id(0)
    last = pl.num_programs(0) - 1
    bq, width = q_out.shape
    links = Links(send_sems, recv_sems, local_sems)
    spread = Spread(links, column_ref, column, whole)
    hidden = up_ref.shape[1]
    halves = []
    for k in range(2):
        part = pl.ds(k * hidden, hidden)
        halves.append(column_stages(links, shard.at[:, part], next_column.at[:, :, part], n))
    keep = links.local(shard, next_column.at[links.dp // 2])

    def start_stage(k, step):
        for copy, _ in halves[k][step]:
            copy.start()

    def next_stage(k, step):
        for copy, _ in halves[k][step]:
            copy.wait_recv()
        if step + 1 < len(halves[k]):
            start_stage(k, step + 1)

    @pl.when(i == 0)
    def _():
        shard[:, :hidden] = up_ref[...]
        shard[:, hidden:] = down_ref[...].T
        links.greet([CORE, X, Y] + z_ways(n))
        start_stage(0, 0)
        spread.start()
        keep.start()

    def onward_one():
        next_stage(0, 0)
        start_stage(1, 0)

    @pl.when(i == last)
    def _():
        next_stage(1, 0)

    mine = pl.ds(pl.multiple_of(links.tensor * width, width), width)
    projected = dot_nn(x_ref[...], w_ref[:, : 3 * width])
    query = (projected[:, :width] + biases_ref[0:1, mine]).astype(BF16)
    key = projected[:, width : 2 * width].astype(BF16)
    value = (projected[:, 2 * width :] + biases_ref[1:2, mine]).astype(BF16)
    here = pl.ds(pl.multiple_of(i * bq, bq), bq)
    q_out[...] = query
    v_out[...] = value
    kt_out[...] = key.T
    k_ref[here, :] = key
    vt_ref[:, here] = value.T

    m_s[...] = jnp.full_like(m_s, NEGATIVE)
    l_s[...] = jnp.zeros_like(l_s)
    acc[...] = jnp.zeros_like(acc)
    hd = width // heads
    scaled = query * jnp.asarray(1.0 / math.sqrt(hd), BF16)
    q_heads = [head_only(scaled, h, hd) for h in range(heads)]

    def block(first, size, skip, mode):
        rows = pl.ds(pl.multiple_of(first, size), size)
        m_old = m_s[:, skip:]
        l_old = l_s[:, skip:]
        scores = [dot_nt(k_ref[rows, lanes_of(h, hd)[1]], q_heads[h][skip:]) for h in range(heads)]
        if mode != "none":
            bad = self_bad(b_ref, i * bq + skip, first, bq - skip, size, mode == "causal")
            scores = [jnp.where(bad, NEGATIVE, s) for s in scores]
        m_out, l_out, a_out = [], [], []
        for h in range(heads):
            part = slice(h * hd, (h + 1) * hd)
            m_new = jnp.maximum(m_old[h : h + 1, :], jnp.max(scores[h], axis=0, keepdims=True))
            shrink = jnp.exp(m_old[h : h + 1, :] - m_new)
            expos = jnp.exp(scores[h] - m_new)
            l_out.append(l_old[h : h + 1, :] * shrink + jnp.sum(expos, axis=0, keepdims=True))
            m_out.append(m_new)
            a_out.append(acc[part, skip:] * shrink + dot_nn(vt_ref[part, rows], expos.astype(BF16)))
        m_s[:, skip:] = jnp.concatenate(m_out, 0)
        l_s[:, skip:] = jnp.concatenate(l_out, 0)
        for h in range(heads):
            acc[h * hd : (h + 1) * hd, skip:] = a_out[h]

    over_keys(i, bq, safe, block, [(2, 0, onward_one), (3, 2, spread.middle), (4, 3, spread.last)])
    inverse = 1.0 / l_s[...]
    for h in range(heads):
        part = slice(h * hd, (h + 1) * hd)
        ot_ref[part, :] = (acc[part, :] * inverse[h : h + 1, :]).astype(BF16)
    lse_ref[...] = m_s[...] + jnp.log(l_s[...])
    terms_ref[...] = dot_nt(ot_ref[...].T, w_ref[:, 3 * width :]).astype(BF16)

    @pl.when(i == last)
    def _():
        for k in range(2):
            for step in range(1, len(halves[k])):
                next_stage(k, step)
        spread.end()
        for stages in halves:
            for stage in stages:
                for copy, _ in stage:
                    copy.wait_send()
        keep.wait()


def self_forward(bounds, x, w, biases, column, up, down, heads, safe):
    n, model = x.shape
    width = w.shape[1] // 4
    bq = 512
    dp = lax.axis_size("dp")
    m, r, c = column.shape
    shard = (up.shape[0], 2 * up.shape[1])
    by_rows_spec = pl.BlockSpec((bq, width), lambda i: (i, 0))
    by_columns_spec = pl.BlockSpec((width, bq), lambda i: (0, i))
    return pl.pallas_call(
        functools.partial(self_forward_kernel, heads=heads, safe=safe, n=dp),
        grid=(n // bq,),
        in_specs=[
            pl.BlockSpec(memory_space=pltpu.SMEM),
            pl.BlockSpec((bq, model), lambda i: (i, 0)),
            const((model, 4 * width)),
            const(biases.shape),
            ANY,
            const(up.shape),
            const(down.shape),
        ],
        out_specs=[
            by_rows_spec,
            const((n, width)),
            by_rows_spec,
            by_columns_spec,
            by_columns_spec,
            pl.BlockSpec((heads, bq), lambda i: (0, i)),
            pl.BlockSpec((bq, model), lambda i: (i, 0)),
            ANY,
            ANY,
        ],
        out_shape=[
            jax.ShapeDtypeStruct((n, width), BF16),
            jax.ShapeDtypeStruct((n, width), BF16),
            jax.ShapeDtypeStruct((n, width), BF16),
            jax.ShapeDtypeStruct((width, n), BF16),
            jax.ShapeDtypeStruct((width, n), BF16),
            jax.ShapeDtypeStruct((heads, n), F32),
            jax.ShapeDtypeStruct((n, model), BF16),
            jax.ShapeDtypeStruct((4, m, 2, r, c), BF16),
            jax.ShapeDtypeStruct((m,) + shard, BF16),
        ],
        scratch_shapes=[
            pltpu.VMEM((width, n), BF16),
            pltpu.VMEM((heads, bq), F32),
            pltpu.VMEM((heads, bq), F32),
            pltpu.VMEM((width, bq), F32),
            pltpu.VMEM((m, r, c), BF16),
            pltpu.VMEM(shard, BF16),
        ]
        + link_scratch(8 + 2 * m, 3),
        compiler_params=pltpu.CompilerParams(
            vmem_limit_bytes=VMEM_LIMIT, collective_id=1, has_side_effects=True
        ),
        cost_estimate=pl.CostEstimate(
            flops=12 * n * n * width, bytes_accessed=8 * n * width, transcendentals=n * n * heads // 2
        ),
        name="self_forward",
    )(bounds, x, w, biases, column, up, down)


def after_self_kernel(
    terms_ref, rows_ref, biases_ref, norm_ref, column_ref, enc_ref,
    after_out, second_out, whole_out, enc_out, *scratch
):
    links = Links(*scratch[-3:])
    rows_sum = RowSum(links, terms_ref, scratch[:5], left=True)
    column = scratch[5]
    y = links.dp % 2
    near_out, core_out = whole_out.at[0], whole_out.at[1]
    load = links.local(column_ref, column)
    own = links.local(column, near_out.at[:, y])
    over_y = links.copy(column, near_out.at[:, y], Y)
    over_core = [
        links.copy(column, core_out.at[:, y], CORE),
        links.copy(near_out.at[:, 1 - y], core_out.at[:, 1 - y], CORE),
    ]
    enc_count = enc_ref.shape[0]

    def place(distance):
        return enc_out.at[pl.ds(pl.multiple_of((links.tensor ^ distance) * enc_count, enc_count), enc_count)]

    enc_x = links.copy(enc_ref, place(0), X)
    enc_core = [links.copy(enc_ref, place(0), CORE), links.copy(place(2), place(2), CORE)]
    enc_own = links.local(enc_ref, place(0))
    links.greet([CORE, X, Y])
    rows_sum.start()
    load.start()
    load.wait()
    over_y.start()
    own.start()
    enc_own.start()
    rows_sum.middle()
    over_core[0].start()
    enc_core[0].start()
    rows_sum.over_x.wait_send()
    enc_x.start()
    rows_sum.end()

    def norm(rows):
        after = rows_ref[rows, :].astype(F32) + rows_sum.total(rows) + biases_ref[2:3, :]
        after_out[rows, :] = after
        xhat, _ = normalized(after)
        second_out[rows, :] = (xhat * norm_ref[1, 0:1, :] + norm_ref[1, 1:2, :]).astype(BF16)

    by_rows(after_out.shape[0], 64, norm)
    enc_x.wait_recv()
    enc_core[1].start()
    over_y.wait_recv()
    over_core[1].start()
    enc_x.wait_send()
    over_y.wait_send()
    for copy in [own, enc_own] + over_core + enc_core:
        copy.wait()


def sum_after_self(terms, rows, biases, norm, column, encoder):
    count, model = rows.shape
    m, r, c = column.shape
    vmem = pl.BlockSpec(memory_space=pltpu.VMEM)
    return pl.pallas_call(
        after_self_kernel,
        in_specs=[ANY, vmem, vmem, vmem, ANY, vmem],
        out_specs=[vmem, vmem, ANY, ANY],
        out_shape=[
            jax.ShapeDtypeStruct((count, model), F32),
            jax.ShapeDtypeStruct((count, model), BF16),
            jax.ShapeDtypeStruct((2, m, 2, r, c), BF16),
            jax.ShapeDtypeStruct((4 * encoder.shape[0], model), BF16),
        ],
        scratch_shapes=row_sum_scratch(count, model) + [pltpu.VMEM((m, r, c), BF16)] + link_scratch(9, 5),
        compiler_params=pltpu.CompilerParams(
            vmem_limit_bytes=VMEM_LIMIT, collective_id=8, has_side_effects=True
        ),
        cost_estimate=pl.CostEstimate(flops=0, bytes_accessed=100 * 2**20, transcendentals=0),
        name="sum_after_self",
    )(terms, rows, biases, norm, column, encoder)


def self_backward_kernel(
    b_ref, q_ref, k_ref, v_ref, kt_ref, wide_ref, w_ref, mt_ref, lse_ref,
    up_ref, cross_ref, diagonal_ref, enc_ref,
    dq_ref, dk_ref, dv_ref, up_out, cross_out, enc_out, dka, dva, dqa, *scratch, heads, safe, n
):
    i = pl.program_id(0)
    links = Links(*scratch[-3:])
    cross = GatherLast(links, cross_ref.at[0], cross_ref.at[1], diagonal_ref, scratch[:5])
    cross_z = Collect(links, cross.column, scratch[5])
    up_column = scratch[6]
    up_z = Collect(links, up_column, scratch[7])
    load = links.local(up_ref, up_column)
    enc = RowSum(links, enc_ref, scratch[8:13])
    stages = len(up_z.stages)

    @pl.when(i == 0)
    def _():
        links.greet(everywhere_ways(n))
        cross.start()
        enc.start()
        load.start()
        load.wait()
        up_z.start(0)
        dka[...] = jnp.zeros_like(dka)
        dva[...] = jnp.zeros_like(dva)

    @pl.when(i == 1)
    def _():
        cross.middle()

    @pl.when(i == 2)
    def _():
        for step in range(stages - 1):
            up_z.finish(step)
            up_z.start(step + 1)

    def sum_cross():
        cross.end()
        cross_z.start(0)
        enc.middle()

    def next_cross():
        for step in range(stages - 1):
            cross_z.finish(step)
            cross_z.start(step + 1)

    bq, width = q_ref.shape
    hd = width // heads
    scale = 1.0 / math.sqrt(hd)
    grads = dot_nn(wide_ref[...], w_ref[:, 3 * width :]).astype(BF16)
    products = grads.T.astype(F32) * mt_ref[...].astype(F32)
    inner = [jnp.sum(products[h * hd : (h + 1) * hd, :], axis=0, keepdims=True) for h in range(heads)]
    scaled = q_ref[...] * jnp.asarray(scale, BF16)
    q_heads = [head_only(scaled, h, hd) for h in range(heads)]
    d_heads = [head_only(grads, h, hd) for h in range(heads)]
    lse = lse_ref[...]
    dqa[...] = jnp.zeros_like(dqa)

    def block(first, size, skip, mode):
        rows = pl.ds(pl.multiple_of(first, size), size)
        scores = [dot_nt(k_ref[rows, lanes_of(h, hd)[1]], q_heads[h][skip:]) for h in range(heads)]
        dprobs = [dot_nt(v_ref[rows, lanes_of(h, hd)[1]], d_heads[h][skip:]) for h in range(heads)]
        if mode != "none":
            bad = self_bad(b_ref, i * bq + skip, first, bq - skip, size, mode == "causal")
            scores = [jnp.where(bad, NEGATIVE, s) for s in scores]
        dv_sums, dk_sums = {}, {}
        for h in range(heads):
            part = slice(h * hd, (h + 1) * hd)
            group, _ = lanes_of(h, hd)
            probs = jnp.exp(scores[h] - lse[h : h + 1, skip:])
            ds = (probs * (dprobs[h] - inner[h][:, skip:])).astype(BF16)
            add_group(dv_sums, group, dot_nn(probs.astype(BF16), d_heads[h][skip:]))
            add_group(dk_sums, group, dot_nn(ds, q_heads[h][skip:]))
            dqa[part, skip:] += dot_nn(kt_ref[part, rows], ds)
        for group in dv_sums:
            part = slice(group * LANES, (group + 1) * LANES)
            dva[rows, part] += dv_sums[group]
            dka[rows, part] += dk_sums[group]

    over_keys(i, bq, safe, block, [(3, 2, sum_cross), (4, 2, next_cross)])
    dq_ref[...] = (dqa[...] * scale).astype(BF16).T

    @pl.when(i == pl.num_programs(0) - 1)
    def _():
        dk_ref[...] = dka[...].astype(BF16)
        dv_ref[...] = dva[...].astype(BF16)
        up_z.finish(stages - 1)
        up_out[...] = up_column[up_z.z].astype(F32)
        cross_z.finish(stages - 1)
        cross_out[...] = cross.column[cross_z.z].astype(F32)
        enc.end()

        def store(rows):
            enc_out[rows, :] = enc.total(rows)

        by_rows(enc_out.shape[0], 64, store)
        up_z.drain()
        cross_z.drain()


def self_backward(
    bounds, queries, keys, values, keys_t, wide, w, mixed_t, lse,
    up_column, cross_sum, diagonal, enc_terms, heads, safe
):
    n, width = queries.shape
    model = wide.shape[1]
    dp = lax.axis_size("dp")
    m, r, c = up_column.shape
    cross_c = cross_sum.shape[4]
    enc_shape = (enc_terms.shape[0] // 4, enc_terms.shape[1])
    bq = 512
    some = pl.BlockSpec((bq, width), lambda i: (i, 0))
    return pl.pallas_call(
        functools.partial(self_backward_kernel, heads=heads, safe=safe, n=dp),
        grid=(n // bq,),
        in_specs=[
            pl.BlockSpec(memory_space=pltpu.SMEM),
            some,
            const((n, width)),
            const((n, width)),
            const((width, n)),
            pl.BlockSpec((bq, model), lambda i: (i, 0)),
            const((model, 4 * width)),
            pl.BlockSpec((width, bq), lambda i: (0, i)),
            pl.BlockSpec((heads, bq), lambda i: (0, i)),
        ]
        + [ANY] * 4,
        out_specs=[some, const((n, width)), const((n, width))]
        + [const((r, c)), const((r, cross_c)), const(enc_shape)],
        out_shape=[
            jax.ShapeDtypeStruct((n, width), BF16),
            jax.ShapeDtypeStruct((n, width), BF16),
            jax.ShapeDtypeStruct((n, width), BF16),
            jax.ShapeDtypeStruct((r, c), F32),
            jax.ShapeDtypeStruct((r, cross_c), F32),
            jax.ShapeDtypeStruct(enc_shape, F32),
        ],
        scratch_shapes=[
            pltpu.VMEM((n, width), F32),
            pltpu.VMEM((n, width), F32),
            pltpu.VMEM((width, bq), F32),
        ]
        + [pltpu.VMEM((m, r, cross_c), BF16)] * 6
        + [pltpu.VMEM((m, r, c), BF16)] * 2
        + row_sum_scratch(*enc_shape)
        + link_scratch(5 + 2 * m, 6),
        compiler_params=pltpu.CompilerParams(
            vmem_limit_bytes=VMEM_LIMIT, collective_id=5, has_side_effects=True
        ),
        cost_estimate=pl.CostEstimate(
            flops=24 * n * n * width, bytes_accessed=16 * n * width, transcendentals=n * n * heads // 2
        ),
        name="self_backward",
    )(bounds, queries, keys, values, keys_t, wide, w, mixed_t, lse, up_column, cross_sum, diagonal, enc_terms)


def const(shape):
    return pl.BlockSpec(shape, lambda *_: (0,) * len(shape), pipeline_mode=pl.Buffered(1))


def normalized(rows):
    center = rows - jnp.mean(rows, axis=-1, keepdims=True)
    scale = lax.rsqrt(jnp.mean(center * center, axis=-1, keepdims=True) + EPSILON)
    return center * scale, scale


def norm_rows_back(rows, incoming, gain):
    xhat, scale = normalized(rows)
    e = incoming * gain
    inner = jnp.mean(e * xhat, axis=-1, keepdims=True)
    return scale * (e - jnp.mean(e, axis=-1, keepdims=True) - xhat * inner), incoming * xhat


def by_rows(count, step, body):
    def one(k, c):
        body(pl.ds(pl.multiple_of(k * step, step), step))
        return c

    lax.fori_loop(0, count // step, one, 0)


def cross_forward_kernel(
    len_ref, x_ref, enc_ref, w_ref, biases_ref, rows_ref, norm_ref, column_ref,
    q_out, k_out, v_out, ot_ref, lse_ref, after_ref, third_ref, whole, send_sems, recv_sems, local_sems, *, heads
):
    i = pl.program_id(0)
    last = pl.num_programs(0) - 1
    links = Links(send_sems, recv_sems, local_sems)
    spread = SpreadFar(links, column_ref, whole)
    pieces = len(spread.over_x)

    @pl.when(i == 0)
    def _():
        links.greet([CORE, X, Y])
        spread.start()
        after_ref[...] = rows_ref[...] + biases_ref[5:6, :]

    def onward(*when):
        for step, k in when:
            pl.when(i == step)(functools.partial(spread.onward, k))

    onward((1, 0), (3, 3))

    width = q_out.shape[2]
    hd = width // heads
    mine = pl.ds(pl.multiple_of((links.tensor ^ i) * width, width), width)
    query = (dot_nn(x_ref[...], w_ref[0, :, :width]) + biases_ref[3:4, mine]).astype(BF16)
    key_value = dot_nn(enc_ref[...], w_ref[0, :, width : 3 * width])
    keys = key_value[:, :width].astype(BF16)
    values = (key_value[:, width:] + biases_ref[4:5, mine]).astype(BF16)
    q_out[0] = query
    k_out[0] = keys
    v_out[0] = values
    values_t = values.T
    scaled = query * jnp.asarray(1.0 / math.sqrt(hd), BF16)
    ok = lax.broadcasted_iota(jnp.int32, (keys.shape[0], 1), 0) < len_ref[0]
    scores = [dot_nt(keys[:, lanes_of(h, hd)[1]], head_only(scaled, h, hd)) for h in range(heads)]
    mixed = []
    for h in range(heads):
        part = slice(h * hd, (h + 1) * hd)
        s = jnp.where(ok, scores[h], NEGATIVE)
        largest = jnp.max(s, axis=0, keepdims=True)
        expos = jnp.exp(s - largest)
        total = jnp.sum(expos, axis=0, keepdims=True)
        mixed.append((dot_nn(values_t[part, :], expos.astype(BF16)) * (1.0 / total)).astype(BF16))
        ot_ref[0, part, :] = mixed[h]
        lse_ref[0, h : h + 1, :] = largest + jnp.log(total)
        if h == heads // 2 - 1:
            onward((1, 1), (2, 2), (3, 4))
    after_ref[...] += dot_nt(jnp.concatenate(mixed, 0).T, w_ref[0, :, 3 * width :])

    @pl.when(i == last)
    def _():
        def norm(rows):
            xhat, _ = normalized(after_ref[rows, :])
            third_ref[rows, :] = (xhat * norm_ref[2, 0:1, :] + norm_ref[2, 1:2, :]).astype(BF16)

        by_rows(after_ref.shape[0], 128, norm)
        for k in range(5, pieces):
            spread.onward(k)
        for k in range(pieces):
            spread.last(k)
        spread.end()


def cross_forward(lengths, x, encoder, weights, biases, rows, norm, column, heads):
    count, model = x.shape
    n = encoder.shape[0]
    parts, _, columns = weights.shape
    width = columns // 4
    m, r, c = column.shape

    def by_part(*shape):
        return pl.BlockSpec((1,) + shape, lambda i: (i,) + (0,) * len(shape))

    return pl.pallas_call(
        functools.partial(cross_forward_kernel, heads=heads),
        grid=(parts,),
        in_specs=[
            pl.BlockSpec(memory_space=pltpu.SMEM),
            const((count, model)),
            const((n, model)),
            by_part(model, columns),
            const(biases.shape),
            const((count, model)),
            const(norm.shape),
            ANY,
        ],
        out_specs=[
            by_part(count, width),
            by_part(n, width),
            by_part(n, width),
            by_part(width, count),
            by_part(heads, count),
            const((count, model)),
            const((count, model)),
            ANY,
        ],
        out_shape=[
            jax.ShapeDtypeStruct((parts, count, width), BF16),
            jax.ShapeDtypeStruct((parts, n, width), BF16),
            jax.ShapeDtypeStruct((parts, n, width), BF16),
            jax.ShapeDtypeStruct((parts, width, count), BF16),
            jax.ShapeDtypeStruct((parts, heads, count), F32),
            jax.ShapeDtypeStruct((count, model), F32),
            jax.ShapeDtypeStruct((count, model), BF16),
            jax.ShapeDtypeStruct((2, m, 2, r, c), BF16),
        ],
        scratch_shapes=link_scratch(32, 1),
        compiler_params=pltpu.CompilerParams(
            vmem_limit_bytes=VMEM_LIMIT, collective_id=2, has_side_effects=True
        ),
        cost_estimate=pl.CostEstimate(
            flops=24 * parts * count * n * width,
            bytes_accessed=8 * parts * n * width,
            transcendentals=parts * count * n * heads,
        ),
        name="cross_forward",
    )(lengths, x, encoder, weights, biases, rows, norm, column)


def feed_forward_kernel(
    x_ref, dy_ref, near_ref, far_ref, b_ref, after_ref, biases_ref, norm_ref,
    out_ref, rows_out, low_out, sums_ref, gup_ref, gdown_ref, bias_ref, from_x, from_y,
    xt_ref, dyt_ref, back_ref, give, got, diagonal, loaded, load_sems, send_sems, recv_sems, local_sems, *, chunks
):
    s = pl.program_id(0)
    links = Links(send_sems, recv_sems, local_sems)
    turn = s // chunks
    chunk = s % chunks
    pair = turn // 2
    slot = pair * chunks + chunk
    theirs = turn % 2 == 0
    y = links.dp % 2
    m, r = diagonal.shape[1], diagonal.shape[2]
    low, high = pl.ds(0, m // 2), pl.ds(m // 2, m - m // 2)
    links.used = 2 * chunks
    across = [
        links.copy(diagonal.at[:, low], from_x, X),
        links.copy(diagonal.at[:, high], from_y, Y),
    ]
    to_core = pltpu.make_async_remote_copy(
        src_ref=give.at[chunk],
        dst_ref=got.at[slot],
        send_sem=send_sems.at[slot],
        recv_sem=recv_sems.at[slot],
        device_id=links.partner(CORE),
        device_id_type=pl.DeviceIdType.MESH,
    )

    size = loaded.shape[3]

    def fetch(step, act):
        block = 3 - step // chunks
        slot = step % 2
        first = (step % chunks) * size

        def both(source):
            for k in range(2):
                columns = pl.ds(pl.multiple_of(first + k * chunks * size, size), size)
                act(pltpu.make_async_copy(source.at[:, columns], loaded.at[slot, k], load_sems.at[slot, k]))

        @pl.when(block >= 2)
        def _():
            both(far_ref.at[block - 2])

        @pl.when(block < 2)
        def _():
            both(near_ref.at[block])

    @pl.when(s == 0)
    def _():
        fetch(0, lambda copy: copy.start())
        links.greet([CORE, X, Y])
        out_ref[...] = after_ref[...] + biases_ref[6:7, :]
        back_ref[...] = jnp.zeros_like(back_ref)
        xt_ref[...] = x_ref[...].T
        dyt_ref[...] = dy_ref[...].T
        sums_ref[...] = jnp.zeros_like(sums_ref)

    fetch(s, lambda copy: copy.wait())

    @pl.when(s + 1 < pl.num_programs(0))
    def _():
        fetch(s + 1, lambda copy: copy.start())

    up_ref, down_ref = loaded.at[s % 2, 0], loaded.at[s % 2, 1]
    lines = size // LANES
    line = ((links.tensor ^ (3 - turn)) * chunks + chunk) * lines
    shift = jnp.concatenate([b_ref[pl.ds(line + k, 1), :] for k in range(lines)], axis=1)
    pre_act = dot_nn(x_ref[...], up_ref[...]) + shift
    hidden_grad = dot_nn(dy_ref[...], down_ref[...])
    normal_cdf = 0.5 * (1.0 + lax.erf(pre_act * (1.0 / math.sqrt(2.0))))
    density = jnp.exp(-0.5 * pre_act * pre_act) * (1.0 / math.sqrt(2.0 * math.pi))
    hidden = (pre_act * normal_cdf).astype(BF16)
    pre_grad = (hidden_grad * (normal_cdf + pre_act * density)).astype(BF16)
    bias_ref[0] = jnp.sum(pre_grad.astype(F32), axis=0, keepdims=True)

    @pl.when(turn % 2 == 1)
    def _():
        to_core.wait_send()

    give[chunk, 0] = dot_nn(xt_ref[...], pre_grad).astype(BF16)
    give[chunk, 1] = dot_nn(dyt_ref[...], hidden).astype(BF16)
    out_ref[...] += dot_nt(hidden, down_ref[...])
    back_ref[...] += dot_nt(pre_grad, up_ref[...])

    @pl.when(theirs)
    def _():
        to_core.start()

    @pl.when(jnp.logical_not(theirs))
    def _():
        to_core.wait_recv()
        gup_ref[0] = (give[chunk, 0].astype(F32) + got[slot, 0].astype(F32)).astype(BF16)
        gdown_ref[0] = (give[chunk, 1].astype(F32) + got[slot, 1].astype(F32)).astype(BF16)

    for k in range(chunks):

        @pl.when(s == chunks + k)
        def _():
            def keep(z, carry):
                rows = pl.ds(pl.multiple_of((2 * z + 1 - y) * r, r), r)
                size = gup_ref.shape[2]
                diagonal[0, z, :, k * size : (k + 1) * size] = gup_ref[0, rows, :]
                diagonal[1, z, :, k * size : (k + 1) * size] = gdown_ref[0, rows, :]
                return carry

            lax.fori_loop(0, m, keep, 0)
            if k == chunks - 1:
                for copy in across:
                    copy.start()

    @pl.when(s == pl.num_programs(0) - 1)
    def _():
        def norm_back(rows):
            third = back_ref[rows, :]
            upstream = dy_ref[rows, :].astype(F32)
            rows_grad, gain_terms = norm_rows_back(after_ref[rows, :], third, norm_ref[2, 0:1, :])
            rows_grad = rows_grad + upstream
            low = rows_grad.astype(BF16)
            rows_out[rows, :] = rows_grad
            low_out[rows, :] = low
            for k, terms in enumerate((gain_terms, third, low.astype(F32), upstream)):
                sums_ref[k : k + 1, :] += jnp.sum(terms, axis=0, keepdims=True)

        by_rows(x_ref.shape[0], 128, norm_back)
        for copy in across:
            copy.wait()


def feed_forward(x, dy, near, far, bias, after, biases, norm):
    rows, width = x.shape
    hidden = near.shape[2] // 2
    size = min(512, hidden)
    chunks = hidden // size

    n = lax.axis_size("dp")
    m, r = n // 2, width // n

    def block(s):
        return 3 - s // chunks

    def placed(s):
        turn = s // chunks
        return (1 - turn // 2, 0, (s % chunks) * (turn % 2))

    rows_spec = const((rows, width))
    grad_spec = pl.BlockSpec((1, width, size), placed)
    bias_spec = pl.BlockSpec((1, 1, size), lambda s: (block(s), 0, s % chunks))
    return pl.pallas_call(
        functools.partial(feed_forward_kernel, chunks=chunks),
        grid=(4 * chunks,),
        in_specs=[
            rows_spec,
            rows_spec,
            ANY,
            ANY,
            const(bias.shape),
            rows_spec,
            const(biases.shape),
            const(norm.shape),
        ],
        out_specs=[rows_spec, rows_spec, rows_spec, const((8, width)), grad_spec, grad_spec, bias_spec, ANY, ANY],
        out_shape=[
            jax.ShapeDtypeStruct((rows, width), F32),
            jax.ShapeDtypeStruct((rows, width), F32),
            jax.ShapeDtypeStruct((rows, width), BF16),
            jax.ShapeDtypeStruct((8, width), F32),
            jax.ShapeDtypeStruct((2, width, hidden), BF16),
            jax.ShapeDtypeStruct((2, width, hidden), BF16),
            jax.ShapeDtypeStruct((4, 1, hidden), F32),
            jax.ShapeDtypeStruct((2, m // 2, r, hidden), BF16),
            jax.ShapeDtypeStruct((2, m - m // 2, r, hidden), BF16),
        ],
        scratch_shapes=[
            pltpu.VMEM((width, rows), BF16),
            pltpu.VMEM((width, rows), BF16),
            pltpu.VMEM((rows, width), F32),
            pltpu.VMEM((chunks, 2, width, size), BF16),
            pltpu.VMEM((2 * chunks, 2, width, size), BF16),
            pltpu.VMEM((2, m, r, hidden), BF16),
            pltpu.VMEM((2, 2, width, size), BF16),
            pltpu.SemaphoreType.DMA((2, 2)),
        ]
        + link_scratch(2 * chunks + 2, 1),
        compiler_params=pltpu.CompilerParams(
            vmem_limit_bytes=VMEM_LIMIT, collective_id=3, has_side_effects=True
        ),
        cost_estimate=pl.CostEstimate(
            flops=48 * rows * width * hidden, bytes_accessed=40 * 2**20, transcendentals=8 * rows * hidden
        ),
        name="feed_forward",
    )(x, dy, near, far, bias, after, biases, norm)


def cross_backward_kernel(
    len_ref, low_ref, x_ref, enc_ref, w_ref, q_ref, k_ref, v_ref, mt_ref, lse_ref, up_ref, down_ref, from_x, from_y,
    back_ref, enc_out, grad_ref, bq_ref, bv_ref, up_out, down_out,
    low_t, x_t, enc_t, enc_acc, give, got, *scratch, heads, bk
):
    i = pl.program_id(0)
    last = pl.num_programs(0) - 1
    links = Links(*scratch[14:])
    sums = [
        Gather(links, ref.at[0], ref.at[1], from_x.at[k], from_y.at[k], scratch[7 * k : 7 * k + 7])
        for k, ref in enumerate((up_ref, down_ref))
    ]
    leave = [links.local(g.column, out) for g, out in zip(sums, (up_out, down_out))]
    pair = i // 2
    to_core = pltpu.make_async_remote_copy(
        src_ref=give,
        dst_ref=got.at[pair],
        send_sem=links.send_sems.at[links.used + pair],
        recv_sem=links.recv_sems.at[links.used + pair],
        device_id=links.partner(CORE),
        device_id_type=pl.DeviceIdType.MESH,
    )

    @pl.when(i == 0)
    def _():
        links.greet([CORE, X, Y])
        for g in sums:
            g.start()
        low_t[...] = low_ref[...].T
        x_t[...] = x_ref[...].T
        enc_t[...] = enc_ref[...].T
        back_ref[...] = jnp.zeros_like(back_ref)
        enc_acc[...] = jnp.zeros_like(enc_acc)

    @pl.when(i == 1)
    def _():
        for g in sums:
            g.middle()

    rows, width = q_ref.shape[1:]
    n = k_ref.shape[1]
    hd = width // heads
    scale = 1.0 / math.sqrt(hd)
    w_query, w_keyval, w_out = w_ref.at[0, :, :width], w_ref.at[0, :, width : 3 * width], w_ref.at[0, :, 3 * width :]
    grads = dot_nn(low_ref[...], w_out[...]).astype(BF16)
    mixed_t = mt_ref[0]
    products = grads.T.astype(F32) * mixed_t.astype(F32)
    inner = [jnp.sum(products[h * hd : (h + 1) * hd, :], axis=0, keepdims=True) for h in range(heads)]
    scaled = q_ref[0] * jnp.asarray(scale, BF16)
    q_heads = [head_only(scaled, h, hd) for h in range(heads)]
    d_heads = [head_only(grads, h, hd) for h in range(heads)]
    lse = lse_ref[0]
    keys_t = k_ref[0].T
    dq = [None] * heads
    dkv = []
    for j in range(n // bk):
        span = slice(j * bk, (j + 1) * bk)
        ok = j * bk + lax.broadcasted_iota(jnp.int32, (bk, 1), 0) < len_ref[0]
        scores = [dot_nt(k_ref[0, span, lanes_of(h, hd)[1]], q_heads[h]) for h in range(heads)]
        dprobs = [dot_nt(v_ref[0, span, lanes_of(h, hd)[1]], d_heads[h]) for h in range(heads)]
        dv_sums, dk_sums = {}, {}
        for h in range(heads):
            part = slice(h * hd, (h + 1) * hd)
            group, _ = lanes_of(h, hd)
            probs = jnp.exp(jnp.where(ok, scores[h], NEGATIVE) - lse[h : h + 1, :])
            ds = (probs * (dprobs[h] - inner[h])).astype(BF16)
            add_group(dv_sums, group, dot_nn(probs.astype(BF16), d_heads[h]))
            add_group(dk_sums, group, dot_nn(ds, q_heads[h]))
            dq_h = dot_nn(keys_t[part, span], ds)
            dq[h] = dq_h if dq[h] is None else dq[h] + dq_h
        block = jnp.concatenate([sums_of[g].astype(BF16) for sums_of in (dk_sums, dv_sums) for g in sorted(sums_of)], 1)
        enc_acc[span, :] += dot_nt(block, w_keyval[...])
        dkv.append(block)
    dq = (jnp.concatenate(dq, 0) * scale).astype(BF16).T
    dkv = jnp.concatenate(dkv, 0)
    bq_ref[0] = jnp.sum(dq.astype(F32), axis=0, keepdims=True)
    bv_ref[0] = jnp.sum(dkv[:, width:].astype(F32), axis=0, keepdims=True)
    back_ref[...] += dot_nt(dq, w_query[...])

    @pl.when(i % 2 == 1)
    def _():
        to_core.wait_send()

    give[:, :width] = dot_nn(x_t[...], dq).astype(BF16)
    give[:, width : 3 * width] = dot_nn(enc_t[...], dkv).astype(BF16)
    give[:, 3 * width :] = dot_nn(low_t[...], mixed_t.T).astype(BF16)

    @pl.when(i % 2 == 0)
    def _():
        to_core.start()

    @pl.when(i % 2 == 1)
    def _():
        to_core.wait_recv()
        grad_ref[0] = (give[...].astype(F32) + got[pair].astype(F32)).astype(BF16)

    @pl.when(i == last)
    def _():
        enc_out[...] = enc_acc[...].astype(BF16)
        for g, copy in zip(sums, leave):
            g.end()
            copy.start()
        for copy in leave:
            copy.wait()


def cross_backward(
    lengths, low, x, encoder, weights, queries, keys, values, mixed_t, lse, up_sum, down_sum, from_x, from_y, heads
):
    count, model = x.shape
    n = encoder.shape[0]
    parts, _, columns = weights.shape
    width = columns // 4
    _, m, _, r, c = up_sum.shape

    def by_part(*shape):
        return pl.BlockSpec((1,) + shape, lambda i: (i ^ 1,) + (0,) * len(shape))

    return pl.pallas_call(
        functools.partial(cross_backward_kernel, heads=heads, bk=256),
        grid=(parts,),
        in_specs=[
            pl.BlockSpec(memory_space=pltpu.SMEM),
            const((count, model)),
            const((count, model)),
            const((n, model)),
            by_part(model, columns),
            by_part(count, width),
            by_part(n, width),
            by_part(n, width),
            by_part(width, count),
            by_part(heads, count),
            ANY,
            ANY,
            ANY,
            ANY,
        ],
        out_specs=[
            const((count, model)),
            const((n, model)),
            pl.BlockSpec((1, model, columns), lambda i: (i // 2, 0, 0), pipeline_mode=pl.Buffered(1)),
            by_part(1, width),
            by_part(1, width),
            ANY,
            ANY,
        ],
        out_shape=[
            jax.ShapeDtypeStruct((count, model), F32),
            jax.ShapeDtypeStruct((n, model), BF16),
            jax.ShapeDtypeStruct((2, model, columns), BF16),
            jax.ShapeDtypeStruct((parts, 1, width), F32),
            jax.ShapeDtypeStruct((parts, 1, width), F32),
            jax.ShapeDtypeStruct((m, r, c), BF16),
            jax.ShapeDtypeStruct((m, r, c), BF16),
        ],
        scratch_shapes=[
            pltpu.VMEM((model, count), BF16),
            pltpu.VMEM((model, count), BF16),
            pltpu.VMEM((model, n), BF16),
            pltpu.VMEM((n, model), F32),
            pltpu.VMEM((model, columns), BF16),
            pltpu.VMEM((2, model, columns), BF16),
        ]
        + gather_scratch(m, r, c) * 2
        + link_scratch(10, 12),
        compiler_params=pltpu.CompilerParams(
            vmem_limit_bytes=60 * 2**20, collective_id=4, has_side_effects=True
        ),
        cost_estimate=pl.CostEstimate(
            flops=48 * parts * count * n * width,
            bytes_accessed=16 * parts * n * width,
            transcendentals=parts * count * n * heads,
        ),
        name="cross_backward",
    )(lengths, low, x, encoder, weights, queries, keys, values, mixed_t, lse, up_sum, down_sum, from_x, from_y)


def on_device(
    block_in,
    encoder_out,
    out_grad,
    bounds,
    enc_lengths,
    norm_params,
    w_qkv,
    w_self_out,
    w_cross_q,
    w_cross_kv,
    w_cross_out,
    w_up,
    w_down,
    biases,
    up_bias,
):
    groups_count = lax.axis_size("dp")
    width = w_cross_q.shape[1]
    hidden_width = w_up.shape[1]
    heads = H // 4
    own_rows, model_width = block_in.shape
    w_rows = w_cross_q.shape[0]

    first_in, self_w, cross_column = start_gather(
        block_in,
        norm_params,
        w_qkv,
        w_self_out,
        w_cross_q,
        w_cross_kv,
        w_cross_out,
    )
    self_w = self_w.reshape(model_width, 4 * width)

    self_safe = 1024
    queries, key_rows, value_rows, keys_t, self_mixed_t, self_lse, terms, cross_w, ffn_column = self_forward(
        bounds,
        first_in,
        self_w,
        biases,
        cross_column,
        w_up,
        w_down,
        heads,
        self_safe,
    )
    cross_w = cross_w.reshape(4, model_width, 4 * width)
    after_self, second_in, ffn_near, enc_all = sum_after_self(
        terms, block_in, biases, norm_params, ffn_column, encoder_out
    )

    cross_q, cross_k, cross_v, cross_mixed_t, cross_lse, after_cross, third_in, ffn_far = cross_forward(
        enc_lengths,
        second_in,
        enc_all,
        cross_w,
        biases,
        after_self,
        norm_params,
        ffn_column,
        heads,
    )

    output, cross_rows_grad, cross_low, ffn_sums, up_sum, down_sum, bias_up_parts, from_x, from_y = feed_forward(
        third_in,
        out_grad,
        ffn_near.reshape(2, model_width, 2 * hidden_width),
        ffn_far.reshape(2, model_width, 2 * hidden_width),
        up_bias.reshape(-1, LANES),
        after_cross,
        biases,
        norm_params,
    )

    by_shard = (2, groups_count // 2, 2, w_rows, hidden_width)
    second_grad, enc_terms, cross_sum, bias_cq_parts, bias_cv_parts, up_column, down_column = cross_backward(
        enc_lengths,
        cross_low,
        second_in,
        enc_all,
        cross_w,
        cross_q,
        cross_k,
        cross_v,
        cross_mixed_t,
        cross_lse,
        up_sum.reshape(by_shard),
        down_sum.reshape(by_shard),
        from_x,
        from_y,
        heads,
    )
    cross_sum = cross_sum.reshape(2, groups_count // 2, 2, w_rows, 4 * width)
    self_wide, self_rows_grad, self_sums, summed_down, diagonal = middle(
        second_grad, after_self, cross_rows_grad, norm_params, down_column, cross_sum
    )
    self_dq, self_dk, self_dv, summed_up, summed_cross, encoder_grad = self_backward(
        bounds,
        queries,
        key_rows,
        value_rows,
        keys_t,
        self_wide,
        self_w,
        self_mixed_t,
        self_lse,
        up_column,
        cross_sum,
        diagonal,
        enc_terms,
        heads,
        self_safe,
    )
    input_grad, summed_self, vectors = tail(
        self_dq,
        self_dk,
        self_dv,
        self_w,
        first_in,
        self_wide,
        self_mixed_t,
        block_in,
        self_rows_grad,
        norm_params,
        self_sums,
        ffn_sums,
        bias_cq_parts,
        bias_cv_parts,
        bias_up_parts,
    )
    scale = 1.0 / groups_count
    output, input_grad, encoder_grad, g_qkv, g_so, g_cq, g_ckv, g_co, g_up, g_down = results(
        output, input_grad, encoder_grad, summed_self, summed_cross, summed_up, summed_down, scale
    )
    vectors = vectors * scale
    return (
        output,
        input_grad,
        encoder_grad,
        vectors[:6].reshape(norm_params.shape),
        g_qkv,
        g_so,
        g_cq,
        g_ckv,
        g_co,
        g_up,
        g_down,
        vectors[6:13],
        vectors[13:17].reshape(-1),
    )


def solution(mesh):
    rows = P(("dp", "tensor"), None)
    placed = (
        rows,
        rows,
        rows,
        P("dp", None),
        P("dp"),
        P(),
        P("dp", None, "tensor"),
        P("tensor", "dp"),
        P("dp", "tensor"),
        P("dp", None, "tensor"),
        P("tensor", "dp"),
        P("dp", "tensor"),
        P("tensor", "dp"),
        P(),
        P(),
    )
    return jax.shard_map(
        on_device,
        mesh=mesh,
        in_specs=placed,
        out_specs=(
            rows,
            rows,
            rows,
            P(),
            P("dp", None, "tensor"),
            P("tensor", "dp"),
            P("dp", "tensor"),
            P("dp", None, "tensor"),
            P("tensor", "dp"),
            P("dp", "tensor"),
            P("tensor", "dp"),
            P(),
            P(),
        ),
        check_vma=False,
    )
```

```python
import functools
import math

import jax
import jax.numpy as jnp
from jax import lax
from jax.experimental import pallas as pl
from jax.experimental.pallas import tpu as pltpu
from jax.sharding import PartitionSpec as P

H = 16
EPSILON = 1e-05
NEGATIVE = -1e30
F32 = jnp.float32
BF16 = jnp.bfloat16
VMEM_LIMIT = 56 * 2**20


def dot_nt(a, b):
    return lax.dot_general(a, b, (((1,), (1,)), ((), ())), preferred_element_type=F32)


def dot_nn(a, b):
    return lax.dot_general(a, b, (((1,), (0,)), ((), ())), preferred_element_type=F32)


def dot_tn(a, b):
    return lax.dot_general(a, b, (((0,), (0,)), ((), ())), preferred_element_type=F32)


LANES = 128


def lanes_of(h, size):
    group = h * size // LANES
    return group, slice(group * LANES, (group + 1) * LANES)


def head_only(x, h, size):
    group, part = lanes_of(h, size)
    lane = group * LANES + lax.broadcasted_iota(jnp.int32, (x.shape[0], LANES), 1)
    return jnp.where((lane >= h * size) & (lane < (h + 1) * size), x[:, part], jnp.zeros((), x.dtype))


def add_group(sums, group, value):
    sums[group] = value if group not in sums else sums[group] + value


def self_bad(b_ref, q_start, k_start, bq, bk, causal):
    qi = q_start + lax.broadcasted_iota(jnp.int32, (1, bq), 1)
    kj = k_start + lax.broadcasted_iota(jnp.int32, (bk, 1), 0)
    bad = (qi >= b_ref[0, 1]) & ((kj >= b_ref[0, 0]) & (kj < b_ref[0, 1]))
    if causal:
        bad = bad | (kj > qi)
    return bad


def over_keys(i, bq, safe, block, between=()):
    def visit(j, c):
        for at_i, at_j, action in between:
            pl.when((i == at_i) & (j == at_j))(action)

        @pl.when(j < safe // bq)
        def _():
            block(j * bq, bq, 0, "none")

        @pl.when(j >= safe // bq)
        def _():
            block(j * bq, bq, 0, "segment")

        return c

    lax.fori_loop(0, i, visit, 0)
    half = bq // 2
    block(i * bq, half, 0, "causal")
    block(i * bq + half, half, half, "causal")


CORE = ("tensor", 1)
X = ("tensor", 2)
Y = ("dp", 1)
ANY = pl.BlockSpec(memory_space=pl.ANY)


class Links:
    def __init__(self, send_sems, recv_sems, local_sems):
        self.dp = lax.axis_index("dp")
        self.tensor = lax.axis_index("tensor")
        self.send_sems, self.recv_sems, self.local_sems = send_sems, recv_sems, local_sems
        self.used = 0
        self.used_local = 0

    def partner(self, way):
        axis, distance = way
        if axis == "tensor":
            return (self.dp, self.tensor ^ distance)
        return (self.dp ^ distance, self.tensor)

    def greet(self, ways):
        barrier = pltpu.get_barrier_semaphore()
        for way in ways:
            pl.semaphore_signal(
                barrier, inc=1, device_id=self.partner(way), device_id_type=pl.DeviceIdType.MESH
            )
        pl.semaphore_wait(barrier, len(ways))

    def copy(self, source, target, way):
        k = self.used
        self.used += 1
        return pltpu.make_async_remote_copy(
            src_ref=source,
            dst_ref=target,
            send_sem=self.send_sems.at[k],
            recv_sem=self.recv_sems.at[k],
            device_id=self.partner(way),
            device_id_type=pl.DeviceIdType.MESH,
        )

    def local(self, source, target):
        k = self.used_local
        self.used_local += 1
        return pltpu.make_async_copy(source, target, self.local_sems.at[k])


def link_scratch(copies, local):
    return [
        pltpu.SemaphoreType.DMA((copies,)),
        pltpu.SemaphoreType.DMA((copies,)),
        pltpu.SemaphoreType.DMA((local,)),
    ]


def z_distances(n):
    found = []
    m = n // 2
    while m > 1:
        m //= 2
        found.append(m)
    return found


def z_ways(n):
    return [("dp", 2 * distance) for distance in z_distances(n)]


def column_stages(links, shard, column, n):
    z = links.dp // 2
    held = [z]
    stages = []
    for distance in z_distances(n):
        stages.append(
            [
                (
                    links.copy(shard if k == 0 else column.at[index], column.at[index], ("dp", 2 * distance)),
                    index ^ distance,
                )
                for k, index in enumerate(held)
            ]
        )
        held = held + [index ^ distance for index in held]
    return stages


class Spread:
    def __init__(self, links, source, column, whole):
        y = links.dp % 2
        half = column.shape[0] // 2
        low, high = pl.ds(0, half), pl.ds(half, half)
        near, near_core, far, far_core = (whole.at[k] for k in range(4))
        self.load = links.local(source, column)
        self.own = links.local(column, near.at[:, y])
        self.first = [
            links.copy(column, near.at[:, y], Y),
            links.copy(column, far.at[:, y], X),
        ]
        self.core = [links.copy(column, near_core.at[:, y], CORE)]
        self.second = [
            links.copy(near.at[low, 1 - y], far.at[low, 1 - y], X),
            links.copy(far.at[high, y], far.at[high, y], Y),
        ]
        self.core_second = [
            links.copy(near.at[:, 1 - y], near_core.at[:, 1 - y], CORE),
            links.copy(far.at[:, y], far_core.at[:, y], CORE),
        ]
        self.core_third = [links.copy(far.at[:, 1 - y], far_core.at[:, 1 - y], CORE)]

    def start(self):
        self.load.start()
        self.load.wait()
        for copy in self.first + self.core + [self.own]:
            copy.start()

    def middle(self):
        for copy in self.first:
            copy.wait_recv()
        for copy in self.second + self.core_second:
            copy.start()

    def last(self):
        for copy in self.second:
            copy.wait_recv()
        for copy in self.core_third:
            copy.start()

    def end(self):
        self.own.wait()
        for copy in self.first + self.second:
            copy.wait_send()
        for copy in self.core + self.core_second + self.core_third:
            copy.wait()


def add_to(total_ref, other_ref):
    def one(k, c):
        total_ref[k] = (total_ref[k].astype(F32) + other_ref[k].astype(F32)).astype(BF16)
        return c

    lax.fori_loop(0, total_ref.shape[0], one, 0)


class Gather:
    def __init__(self, links, near, far, from_x, from_y, buffers):
        y = links.dp % 2
        self.column, self.over_y, self.over_x, self.add_y, self.add_x, self.sum_y, self.sum_x = buffers
        m = self.column.shape[0]
        low, high = pl.ds(0, m // 2), pl.ds(m // 2, m - m // 2)
        self.loads = [
            links.local(near.at[low, 1 - y], self.over_y),
            links.local(far.at[high, y], self.over_x),
            links.local(from_x, self.add_y),
            links.local(from_y, self.add_x),
            links.local(near.at[:, y], self.column),
        ]
        self.first = [
            links.copy(far.at[low, y], self.sum_x.at[low], X),
            links.copy(near.at[high, 1 - y], self.sum_y.at[high], Y),
        ]
        self.second = [
            links.copy(self.over_x, self.sum_x.at[high], X),
            links.copy(self.over_y, self.sum_y.at[low], Y),
        ]

    def start(self):
        for copy in self.first + self.loads:
            copy.start()

    def middle(self):
        for copy in self.loads:
            copy.wait()
        add_to(self.over_x, self.add_x)
        add_to(self.over_y, self.add_y)
        for copy in self.second:
            copy.start()

    def end(self):
        for copy in self.first + self.second:
            copy.wait_recv()
        add_to(self.column, self.sum_y)
        add_to(self.column, self.sum_x)
        for copy in self.first + self.second:
            copy.wait_send()


def gather_scratch(m, r, c):
    whole = pltpu.VMEM((m, r, c), BF16)
    half = pltpu.VMEM((m // 2, r, c), BF16)
    return [whole] + [half] * 4 + [whole] * 2


class GatherLast:
    def __init__(self, links, near, far, diagonal, buffers):
        y = links.dp % 2
        self.column, self.over_x, self.diagonal, self.sum_y, self.sum_x = buffers
        self.loads = [
            links.local(far.at[:, y], self.over_x),
            links.local(diagonal, self.diagonal),
            links.local(near.at[:, y], self.column),
        ]
        self.over_y = links.copy(near.at[:, 1 - y], self.sum_y, Y)
        self.along_x = links.copy(self.over_x, self.sum_x, X)

    def start(self):
        self.over_y.start()
        for copy in self.loads:
            copy.start()

    def middle(self):
        for copy in self.loads:
            copy.wait()
        add_to(self.over_x, self.diagonal)
        self.along_x.start()

    def end(self):
        self.over_y.wait_recv()
        self.along_x.wait_recv()
        add_to(self.column, self.sum_y)
        add_to(self.column, self.sum_x)
        self.over_y.wait_send()
        self.along_x.wait_send()


class Collect:
    def __init__(self, links, column, slots):
        z = links.dp // 2
        self.column, self.slots, self.z = column, slots, z
        m = column.shape[0]
        distances = z_distances(2 * m)[::-1]
        self.stages = []
        first = 0
        for step, distance in enumerate(distances):
            kept = [0]
            for other in distances[step + 1 :]:
                kept = kept + [k ^ other for k in kept]
            self.stages.append(
                [
                    (links.copy(column.at[z ^ distance ^ k], slots.at[first + i], ("dp", 2 * distance)), first + i, z ^ k)
                    for i, k in enumerate(kept)
                ]
            )
            first += len(kept)

    def start(self, step):
        for copy, _, _ in self.stages[step]:
            copy.start()

    def finish(self, step):
        for copy, slot, index in self.stages[step]:
            copy.wait_recv()
            self.column[index] = (self.column[index].astype(F32) + self.slots[slot].astype(F32)).astype(BF16)

    def drain(self):
        for stage in self.stages:
            for copy, _, _ in stage:
                copy.wait_send()


class Square:
    def __init__(self, links, shard, out):
        y = links.dp % 2
        c = shard.shape[1]
        low, high = pl.ds(0, c // 2), pl.ds(c // 2, c // 2)
        self.own = links.local(shard, out.at[0, y])
        self.first = [links.copy(shard, out.at[0, y], Y), links.copy(shard, out.at[1, y], X)]
        self.second = [
            links.copy(out.at[0, 1 - y, :, low], out.at[1, 1 - y, :, low], X),
            links.copy(out.at[1, y, :, high], out.at[1, y, :, high], Y),
        ]

    def start(self):
        for copy in self.first + [self.own]:
            copy.start()

    def middle(self):
        for copy in self.first:
            copy.wait_recv()
        for copy in self.second:
            copy.start()

    def end(self):
        for copy in self.first:
            copy.wait_send()
        for copy in self.second:
            copy.wait()
        self.own.wait()


class SpreadZ:
    def __init__(self, links, own, other, hold, whole, n):
        z = links.dp // 2
        distances = z_distances(n)
        there = z ^ distances[0]
        final, core = whole.at[0], whole.at[1]
        self.loads = [links.local(own, hold.at[0]), links.local(other, hold.at[1])]
        self.stores = [links.local(hold.at[0], final.at[z]), links.local(hold.at[1], final.at[there])]
        self.core = [links.copy(hold.at[0], core.at[z], CORE), links.copy(hold.at[1], core.at[there], CORE)]
        held = [(hold.at[0], z), (hold.at[1], there)]
        self.stages, self.core_stages = [], []
        for distance in distances[1:]:
            came = [index ^ distance for _, index in held]
            self.stages.append([links.copy(ref, final.at[index], ("dp", 2 * distance)) for ref, index in held])
            self.core_stages.append([links.copy(final.at[index], core.at[index], CORE) for index in came])
            held = held + [(final.at[index], index) for index in came]

    def start(self):
        for copy in self.loads:
            copy.start()
        for copy in self.loads:
            copy.wait()
        for copy in self.stages[0] + self.stores + self.core:
            copy.start()

    def end(self):
        for step, (stage, core_stage) in enumerate(zip(self.stages, self.core_stages)):
            for copy, onward in zip(stage, core_stage):
                copy.wait_recv()
                onward.start()
            for copy in self.stages[step + 1] if step + 1 < len(self.stages) else []:
                copy.start()
        for copy in self.stores + self.core:
            copy.wait()
        for stage, core_stage in zip(self.stages, self.core_stages):
            for copy in stage:
                copy.wait_send()
            for copy in core_stage:
                copy.wait()


def spread_z_copies(n):
    return 2 * n


class SpreadFar:
    def __init__(self, links, column, whole):
        y = links.dp % 2
        far, far_core = whole.at[0], whole.at[1]
        m, _, c = column.shape
        step = max(m // 4, 1)
        self.over_x, self.over_y, self.core_x, self.core_y = [], [], [], []
        for k in range(m // step):
            for h in range(2):
                z, part = pl.ds(k * step, step), pl.ds(h * (c // 2), c // 2)
                own = far.at[z, y, :, part]
                other = far.at[z, 1 - y, :, part]
                self.over_x.append(links.copy(column.at[z, :, part], own, X))
                self.over_y.append(links.copy(own, own, Y))
                self.core_x.append(links.copy(own, far_core.at[z, y, :, part], CORE))
                self.core_y.append(links.copy(other, far_core.at[z, 1 - y, :, part], CORE))

    def start(self):
        for copy in self.over_x:
            copy.start()

    def onward(self, k):
        self.over_x[k].wait_recv()
        self.over_y[k].start()
        self.core_x[k].start()

    def last(self, k):
        self.over_y[k].wait_recv()
        self.core_y[k].start()

    def end(self):
        for copy in self.over_x + self.over_y:
            copy.wait_send()
        for copy in self.core_x + self.core_y:
            copy.wait()


class RowSum:
    def __init__(self, links, terms, buffers, left=False):
        self.left = left
        self.near, self.far, self.got_near, self.got_far, self.got_x = buffers
        count = self.near.shape[0]

        def rows(distance):
            start = pl.multiple_of((links.tensor ^ distance) * count, count)
            return terms.at[pl.ds(start, count)]

        self.loads = [links.local(rows(0), self.near), links.local(rows(2), self.far)]
        self.core = [links.copy(rows(3), self.got_far, CORE), links.copy(rows(1), self.got_near, CORE)]
        self.over_x = links.copy(self.far, self.got_x, X)

    def start(self):
        for copy in self.loads[::-1] + self.core:
            copy.start()

    def middle(self):
        self.loads[1].wait()
        self.core[0].wait_recv()

        def add(rows):
            self.far[rows, :] = (self.far[rows, :].astype(F32) + self.got_far[rows, :].astype(F32)).astype(BF16)

        by_rows(self.far.shape[0], 64, add)
        self.over_x.start()

    def end(self):
        self.loads[0].wait()
        self.core[1].wait_recv()
        self.over_x.wait_recv()
        for copy in self.core + ([] if self.left else [self.over_x]):
            copy.wait_send()

    def total(self, rows):
        return self.near[rows, :].astype(F32) + self.got_near[rows, :].astype(F32) + self.got_x[rows, :].astype(F32)


def row_sum_scratch(count, width):
    return [pltpu.VMEM((count, width), BF16)] * 5


class Everywhere:
    def __init__(self, links, held, slots, ways):
        self.held, self.slots = held, slots
        self.copies = [links.copy(held.at[k], slots.at[k], way) for k, way in enumerate(ways)]

    def start(self, step):
        self.copies[step].start()

    def finish(self, step):
        self.copies[step].wait()
        self.held[step + 1] = self.held[step] + self.slots[step]


def everywhere_ways(n):
    return [CORE, X, Y] + z_ways(n)


def everywhere_scratch(k, c, n):
    steps = len(everywhere_ways(n))
    return [pltpu.VMEM((steps + 1, k, c), F32), pltpu.VMEM((steps, k, c), F32)]


def middle_kernel(
    back_ref, rows_ref, grad_ref, norm_ref, down_ref, cross_ref,
    wide_out, grad_out, sums_ref, down_out, diagonal_out,
    low, column, slots, send_sems, recv_sems, local_sems, *, n
):
    links = Links(send_sems, recv_sems, local_sems)
    count = low.shape[0]
    load = links.local(down_ref, column)
    load.start()
    collect = Collect(links, column, slots)

    def place(distance):
        return wide_out.at[pl.ds(pl.multiple_of((links.tensor ^ distance) * count, count), count)]

    own = links.local(low, place(0))
    half = count // 2
    parts = [pl.ds(0, half), pl.ds(half, half)]
    over_x = [links.copy(low.at[part], place(0).at[part], X) for part in parts]
    over_core = links.copy(low, place(0), CORE)
    onward = [links.copy(place(2).at[part], place(2).at[part], CORE) for part in parts]
    over_y = links.copy(cross_ref.at[1, :, 1 - links.dp % 2], diagonal_out, Y)
    links.greet([CORE, X, Y] + z_ways(n))
    over_y.start()
    load.wait()
    collect.start(0)
    sums_ref[...] = jnp.zeros_like(sums_ref)

    def norm_back(rows):
        incoming = back_ref[rows, :]
        rows_grad, gain_terms = norm_rows_back(rows_ref[rows, :], incoming, norm_ref[1, 0:1, :])
        rows_grad = rows_grad + grad_ref[rows, :]
        rounded = rows_grad.astype(BF16)
        grad_out[rows, :] = rows_grad
        low[rows, :] = rounded
        for k, terms in enumerate((gain_terms, incoming, rounded.astype(F32))):
            sums_ref[k : k + 1, :] += jnp.sum(terms, axis=0, keepdims=True)

    for part, copy in zip(parts, over_x):
        by_rows(half, 64, lambda rows, part=part: norm_back(pl.ds(pl.multiple_of(part.start + rows.start, 64), 64)))
        copy.start()
    own.start()
    over_core.start()
    for step in range(len(collect.stages) - 1):
        collect.finish(step)
        collect.start(step + 1)
    for copy, later in zip(over_x, onward):
        copy.wait_recv()
        later.start()
    collect.finish(len(collect.stages) - 1)
    down_out[...] = column[collect.z].astype(F32)
    collect.drain()
    own.wait()
    for copy in over_x:
        copy.wait_send()
    over_core.wait()
    for copy in onward:
        copy.wait()
    over_y.wait()


def middle(back, rows, grad, norm, down_column, cross_sum):
    n = lax.axis_size("dp")
    count, width = rows.shape
    m, r, c = down_column.shape
    vmem = pl.BlockSpec(memory_space=pltpu.VMEM)
    return pl.pallas_call(
        functools.partial(middle_kernel, n=n),
        in_specs=[vmem, vmem, vmem, vmem, ANY, ANY],
        out_specs=[ANY, vmem, vmem, vmem, ANY],
        out_shape=[
            jax.ShapeDtypeStruct((4 * count, width), BF16),
            jax.ShapeDtypeStruct((count, width), F32),
            jax.ShapeDtypeStruct((8, width), F32),
            jax.ShapeDtypeStruct((r, c), F32),
            jax.ShapeDtypeStruct((m, r, cross_sum.shape[4]), BF16),
        ],
        scratch_shapes=[
            pltpu.VMEM((count, width), BF16),
            pltpu.VMEM((m, r, c), BF16),
            pltpu.VMEM((m, r, c), BF16),
        ]
        + link_scratch(6 + m, 2),
        compiler_params=pltpu.CompilerParams(
            vmem_limit_bytes=VMEM_LIMIT, collective_id=6, has_side_effects=True
        ),
        cost_estimate=pl.CostEstimate(flops=0, bytes_accessed=100 * 2**20, transcendentals=0),
        name="middle",
    )(back, rows, grad, norm, down_column, cross_sum)


def tail_kernel(
    dq_ref, dk_ref, dv_ref, w_ref, first_hbm, wide_hbm, mt_hbm, rows_hbm, grad_hbm, norm_ref,
    self_ref, ffn_ref, cq_ref, cv_ref, up_ref,
    grad_out, weights_out, late_out, give, acc, weights,
    first_ref, wide_ref, mt_ref, rows_ref, grad_ref, *scratch, n, step_rows
):
    links = Links(*scratch[-3:])
    loads = [
        links.local(source, target)
        for source, target in (
            (first_hbm, first_ref), (wide_hbm, wide_ref), (mt_hbm, mt_ref), (rows_hbm, rows_ref), (grad_hbm, grad_ref)
        )
    ]
    for copy in loads:
        copy.start()
    member = links.tensor
    near, far, got_near, got_far, got_x = scratch[:5]
    columns, gots, slots = scratch[5:7], scratch[7:9], scratch[9:11]
    held, late_slots, sums, early_slots = scratch[11:15]
    count, model = near.shape
    width = dq_ref.shape[1]
    y = links.dp % 2
    c = columns[0].shape[2]
    m, _, r, _ = weights.shape
    half = count // 2
    parts = [pl.ds(0, half), pl.ds(half, half)]
    core_far = links.copy(give.at[0], got_far, CORE)
    core_near = links.copy(give.at[1], got_near, CORE)
    over_x = [links.copy(far.at[part], got_x.at[part], X) for part in parts]
    over_y, collects = [], []
    for k, (column, got, slot) in enumerate(zip(columns, gots, slots)):
        over_y.append(links.copy(weights.at[:, 1 - y, :, pl.ds(k * c, c)], got, Y))
        collects.append(Collect(links, column, slot))
    stages = len(collects[0].stages)
    late = Everywhere(links, held, late_slots, everywhere_ways(n))
    early = Everywhere(links, sums, early_slots, [CORE] + z_ways(n) + [Y, X])
    steps = len(late.copies)
    links.greet(everywhere_ways(n))

    def terms(distance, target):
        base = (member ^ distance) * count

        def one(rows):
            there = pl.ds(pl.multiple_of(base + rows.start, 128), 128)
            total = dot_nt(dq_ref[there, :], w_ref[:, :width])
            total = total + dot_nt(dk_ref[there, :], w_ref[:, width : 2 * width])
            target[rows, :] = (total + dot_nt(dv_ref[there, :], w_ref[:, 2 * width : 3 * width])).astype(BF16)

        by_rows(count, 128, one)

    def packed(k):
        for block in range(2 * m):
            span = slice(block * r, (block + 1) * r)
            weights[block // 2, block % 2, :, k * c : (k + 1) * c] = acc[span, k * c : (k + 1) * c].astype(BF16)
        columns[k][...] = weights[:, y, :, k * c : (k + 1) * c]

    terms(3, give.at[0])
    core_far.start()
    terms(2, far)
    core_far.wait_recv()
    for part, copy in zip(parts, over_x):

        def add(rows, part=part):
            there = pl.ds(pl.multiple_of(part.start + rows.start, 64), 64)
            far[there, :] = (far[there, :].astype(F32) + got_far[there, :].astype(F32)).astype(BF16)

        by_rows(half, 64, add)
        copy.start()

    acc[...] = jnp.zeros_like(acc)
    for copy in loads:
        copy.wait()

    def products(rows):
        source = first_ref[rows, :].T
        for k, ref in enumerate((dq_ref, dk_ref, dv_ref)):
            acc[:, k * width : (k + 1) * width] += dot_nn(source, ref[rows, :])

    by_rows(dq_ref.shape[0], step_rows, products)
    packed(0)
    over_y[0].start()
    terms(1, give.at[1])
    core_near.start()
    terms(0, near)

    def products_out(rows):
        acc[:, 3 * width :] += dot_nn(wide_ref[rows, :].T, mt_ref[:, rows].T)

    by_rows(dq_ref.shape[0], step_rows, products_out)
    packed(1)

    held[0] = jnp.zeros(held.shape[1:], F32)
    sums[0] = jnp.zeros(sums.shape[1:], F32)
    sums[0, 0:2, :] = self_ref[0:2, :]
    sums[0, 2:4, :] = ffn_ref[0:2, :]
    sums[0, 6:7, :] = self_ref[2:3, :]
    sums[0, 9:11, :] = ffn_ref[2:4, :]
    for distance in range(4):
        there = pl.ds(pl.multiple_of((member ^ distance) * width, width), width)
        sums[0, 7:8, there] = cq_ref[distance]
        sums[0, 8:9, there] = cv_ref[distance]
        sums[0, pl.ds(11 + (member ^ distance), 1), :] = up_ref[distance]
    here = pl.ds(pl.multiple_of(member * width, width), width)

    def column_sums(rows):
        sums[0, 4:5, here] += jnp.sum(dq_ref[rows, :].astype(F32), axis=0, keepdims=True)
        sums[0, 5:6, here] += jnp.sum(dv_ref[rows, :].astype(F32), axis=0, keepdims=True)

    by_rows(dq_ref.shape[0], step_rows, column_sums)
    early.start(0)

    def norm_back(part):
        def one(rows):
            rows = pl.ds(pl.multiple_of(part.start + rows.start, 64), 64)
            incoming = near[rows, :].astype(F32) + got_near[rows, :].astype(F32) + got_x[rows, :].astype(F32)
            rows_grad, gain_terms = norm_rows_back(rows_ref[rows, :].astype(F32), incoming, norm_ref[0, 0:1, :])
            grad_out[rows, :] = rows_grad + grad_ref[rows, :]
            held[0, 0:1, :] += jnp.sum(gain_terms, axis=0, keepdims=True)
            held[0, 1:2, :] += jnp.sum(incoming, axis=0, keepdims=True)

        by_rows(half, 64, one)

    def summed_y(k):
        over_y[k].wait_recv()
        add_to(columns[k], gots[k])
        collects[k].start(0)

    def next_z(k):
        for step in range(stages - 1):
            collects[k].finish(step)
            collects[k].start(step + 1)

    def last_z(k):
        collects[k].finish(stages - 1)
        weights_out[:, k * c : (k + 1) * c] = columns[k][collects[k].z].astype(F32)

    summed_y(0)
    over_y[1].start()
    early.finish(0)
    core_near.wait_recv()
    over_x[0].wait_recv()
    norm_back(parts[0])
    next_z(0)
    for step in range(1, steps - 2):
        early.start(step)
        early.finish(step)
    over_x[1].wait_recv()
    norm_back(parts[1])
    late.start(0)
    summed_y(1)
    late.finish(0)
    late.start(1)
    early.start(steps - 2)
    last_z(0)
    early.finish(steps - 2)
    late.finish(1)
    late.start(2)
    early.start(steps - 1)
    next_z(1)
    early.finish(steps - 1)
    late.finish(2)
    late_out[2:, :] = sums[steps]
    for step in range(3, steps):
        late.start(step)
        late.finish(step)
    last_z(1)
    late_out[0:2, :] = held[steps, 0:2, :]
    for copy in over_x + over_y + [core_near, core_far]:
        copy.wait_send()
    for collect in collects:
        collect.drain()


def tail(dq, dk, dv, w, first, wide, mixed_t, rows, grad, norm, self_sums, ffn_sums, cq_sums, cv_sums, up_sums):
    n = lax.axis_size("dp")
    count, model = rows.shape
    width = dq.shape[1]
    m, r, c = n // 2, model // n, 4 * width
    vectors = (16, model)
    vmem = pl.BlockSpec(memory_space=pltpu.VMEM)
    part = pltpu.VMEM((m, r, c // 2), BF16)
    return pl.pallas_call(
        functools.partial(tail_kernel, n=n, step_rows=512),
        in_specs=[vmem] * 4 + [ANY] * 5 + [vmem] * 6,
        out_specs=[vmem, vmem, vmem],
        out_shape=[
            jax.ShapeDtypeStruct((count, model), F32),
            jax.ShapeDtypeStruct((r, c), F32),
            jax.ShapeDtypeStruct((vectors[0] + 2, model), F32),
        ],
        scratch_shapes=[
            pltpu.VMEM((2, count, model), BF16),
            pltpu.VMEM((model, c), F32),
            pltpu.VMEM((m, 2, r, c), BF16),
        ]
        + [pltpu.VMEM(v.shape, v.dtype) for v in (first, wide, mixed_t, rows, grad)]
        + row_sum_scratch(count, model)
        + [part] * 6
        + everywhere_scratch(8, model, n)
        + everywhere_scratch(*vectors, n)
        + link_scratch(6 + 2 * m + 2 * len(everywhere_ways(n)), 5),
        compiler_params=pltpu.CompilerParams(
            vmem_limit_bytes=VMEM_LIMIT, collective_id=7, has_side_effects=True
        ),
        cost_estimate=pl.CostEstimate(flops=0, bytes_accessed=100 * 2**20, transcendentals=0),
        name="tail",
    )(dq, dk, dv, w, first, wide, mixed_t, rows, grad, norm, self_sums, ffn_sums, cq_sums, cv_sums, up_sums)


def results_kernel(
    output_ref, grad_ref, enc_ref, self_ref, cross_ref, up_ref, down_ref,
    output_out, grad_out, enc_out, qkv_out, so_out, cq_out, ckv_out, co_out, up_out, down_out, *, scale
):
    output_out[...] = output_ref[...]
    grad_out[...] = grad_ref[...]
    enc_out[...] = enc_ref[...]
    width = cq_out.shape[1]

    @pl.when(pl.program_id(0) == 0)
    def _():
        for k in range(3):
            qkv_out[:, k, :] = self_ref[:, k * width : (k + 1) * width] * scale
        so_out[...] = (self_ref[:, 3 * width :] * scale).T
        cq_out[...] = cross_ref[:, :width] * scale
        for k in range(2):
            ckv_out[:, k, :] = cross_ref[:, (k + 1) * width : (k + 2) * width] * scale
        co_out[...] = (cross_ref[:, 3 * width :] * scale).T
        up_out[...] = up_ref[...] * scale
        down_out[...] = (down_ref[...] * scale).T


def results(output, grad, encoder, self_w, cross_w, up, down, scale):
    r, c = self_w.shape
    width = c // 4
    steps = 4

    def rows(value):
        return pl.BlockSpec((value.shape[0] // steps, value.shape[1]), lambda i: (i, 0))

    shapes = [(r, 3, width), (width, r), (r, width), (r, 2, width), (width, r), up.shape, down.shape[::-1]]
    return pl.pallas_call(
        functools.partial(results_kernel, scale=scale),
        grid=(steps,),
        in_specs=[rows(output), rows(grad), rows(encoder)] + [const(v.shape) for v in (self_w, cross_w, up, down)],
        out_specs=[rows(output), rows(grad), rows(encoder)] + [const(shape) for shape in shapes],
        out_shape=[jax.ShapeDtypeStruct(v.shape, F32) for v in (output, grad, encoder)]
        + [jax.ShapeDtypeStruct(shape, F32) for shape in shapes],
        compiler_params=pltpu.CompilerParams(vmem_limit_bytes=VMEM_LIMIT),
        cost_estimate=pl.CostEstimate(flops=0, bytes_accessed=20 * 2**20, transcendentals=0),
        name="results",
    )(output, grad, encoder, self_w, cross_w, up, down)


def start_kernel(
    in_ref, norm_ref, qkv_ref, so_ref, cq_ref, ckv_ref, co_ref, down_ref,
    rows_out, self_out, cross_out, down_out, rows_ref, self_ref, cross_ref, shard_ref, send_sems, recv_sems, local_sems, *, n
):
    links = Links(send_sems, recv_sems, local_sems)
    member, z, y = links.tensor, links.dp // 2, links.dp % 2
    count = rows_ref.shape[0]
    half = count // 2
    parts = [pl.ds(0, half), pl.ds(half, half)]

    def place(distance):
        return rows_out.at[pl.ds(pl.multiple_of((member ^ distance) * count, count), count)]

    over_x = [links.copy(rows_ref.at[part], place(0).at[part], X) for part in parts]
    over_core = [links.copy(rows_ref, place(0), CORE)]
    over_core += [links.copy(place(2).at[part], place(2).at[part], CORE) for part in parts]
    self_stages = column_stages(links, self_ref, self_out.at[:, y], n)
    cross_stages = column_stages(links, cross_ref, cross_out, n)
    over_y = [links.copy(self_ref, self_out.at[z, y], Y)]
    local = [
        links.local(rows_ref, place(0)),
        links.local(self_ref, self_out.at[z, y]),
        links.local(cross_ref, cross_out.at[z]),
    ]
    width = cq_ref.shape[1]
    for k in range(3):
        self_ref[:, k * width : (k + 1) * width] = qkv_ref[:, k, :]
    self_ref[:, 3 * width :] = so_ref[...].T
    cross_ref[:, :width] = cq_ref[...]
    for k in range(2):
        cross_ref[:, (k + 1) * width : (k + 2) * width] = ckv_ref[:, k, :]
    cross_ref[:, 3 * width :] = co_ref[...].T
    shard_ref[...] = down_ref[...].T
    square = Square(links, shard_ref, down_out)
    links.greet([CORE, X, Y] + z_ways(n))
    for copy in over_y + local[1:]:
        copy.start()
    for copy, _ in self_stages[0]:
        copy.start()
    for part, copy in zip(parts, over_x):

        def norm(rows, part=part):
            rows = pl.ds(pl.multiple_of(part.start + rows.start, 64), 64)
            xhat, _ = normalized(in_ref[rows, :].astype(F32))
            rows_ref[rows, :] = (xhat * norm_ref[0, 0:1, :] + norm_ref[0, 1:2, :]).astype(BF16)

        by_rows(half, 64, norm)
        copy.start()
    for copy in local[:1] + over_core[:1]:
        copy.start()
    square.start()
    for self_stage in self_stages:
        if self_stage is not self_stages[0]:
            for copy, _ in self_stage:
                copy.start()
        for copy, index in self_stage:
            copy.wait_recv()
            onward = links.copy(self_out.at[index, y], self_out.at[index, y], Y)
            onward.start()
            over_y.append(onward)
        if self_stage is self_stages[0]:
            for copy, _ in cross_stages[0]:
                copy.start()
    for cross_stage, later in zip(cross_stages, cross_stages[1:] + [[]]):
        for copy, _ in cross_stage:
            copy.wait_recv()
        for copy, _ in later:
            copy.start()
    for copy, onward in zip(over_x, over_core[1:]):
        copy.wait_recv()
        onward.start()
    square.middle()
    square.end()
    for copy in local + over_y + over_core:
        copy.wait()
    for copy in over_x:
        copy.wait_send()
    for stage in self_stages + cross_stages:
        for copy, _ in stage:
            copy.wait_send()


def start_gather(rows, norm, qkv, self_out, cross_q, cross_kv, cross_out, down):
    n = lax.axis_size("dp")
    r, c = cross_q.shape[0], 4 * cross_q.shape[1]
    return pl.pallas_call(
        functools.partial(start_kernel, n=n),
        in_specs=[pl.BlockSpec(memory_space=pltpu.VMEM)] * 8,
        out_specs=[ANY] * 4,
        out_shape=[
            jax.ShapeDtypeStruct((4 * rows.shape[0], rows.shape[1]), BF16),
            jax.ShapeDtypeStruct((n // 2, 2, r, c), BF16),
            jax.ShapeDtypeStruct((n // 2, r, c), BF16),
            jax.ShapeDtypeStruct((2, 2, r, down.shape[0]), BF16),
        ],
        scratch_shapes=[pltpu.VMEM(rows.shape, BF16)]
        + [pltpu.VMEM((r, c), BF16)] * 2
        + [pltpu.VMEM((r, down.shape[0]), BF16)]
        + link_scratch(2 * n + 12, 4),
        compiler_params=pltpu.CompilerParams(
            vmem_limit_bytes=VMEM_LIMIT, collective_id=0, has_side_effects=True
        ),
        cost_estimate=pl.CostEstimate(flops=0, bytes_accessed=100 * 2**20, transcendentals=0),
        name="start_gather",
    )(rows, norm, qkv, self_out, cross_q, cross_kv, cross_out, down)


def self_forward_kernel(
    b_ref, x_ref, w_ref, biases_ref, column_ref, up_ref, down_ref,
    q_out, k_ref, v_out, kt_out, ot_ref, lse_ref, terms_ref, whole, next_column, far_down,
    vt_ref, m_s, l_s, acc, column, send_sems, recv_sems, local_sems, *, heads, safe, n
):
    i = pl.program_id(0)
    last = pl.num_programs(0) - 1
    bq, width = q_out.shape
    links = Links(send_sems, recv_sems, local_sems)
    spread = Spread(links, column_ref, column, whole)
    stages = column_stages(links, up_ref, next_column, n)
    keep = links.local(up_ref, next_column.at[links.dp // 2])
    over_z = links.copy(down_ref.at[0], far_down, z_ways(n)[0])

    def next_stage(step):
        for copy, _ in stages[step]:
            copy.wait_recv()
        for copy, _ in stages[step + 1] if step + 1 < len(stages) else []:
            copy.start()

    @pl.when(i == 0)
    def _():
        links.greet([CORE, X, Y] + z_ways(n))
        for copy, _ in stages[0]:
            copy.start()
        spread.start()
        keep.start()

    def onward():
        next_stage(0)
        over_z.start()

    mine = pl.ds(pl.multiple_of(links.tensor * width, width), width)
    projected = dot_nn(x_ref[...], w_ref[:, : 3 * width])
    query = (projected[:, :width] + biases_ref[0:1, mine]).astype(BF16)
    key = projected[:, width : 2 * width].astype(BF16)
    value = (projected[:, 2 * width :] + biases_ref[1:2, mine]).astype(BF16)
    here = pl.ds(pl.multiple_of(i * bq, bq), bq)
    q_out[...] = query
    v_out[...] = value
    kt_out[...] = key.T
    k_ref[here, :] = key
    vt_ref[:, here] = value.T

    m_s[...] = jnp.full_like(m_s, NEGATIVE)
    l_s[...] = jnp.zeros_like(l_s)
    acc[...] = jnp.zeros_like(acc)
    hd = width // heads
    scaled = query * jnp.asarray(1.0 / math.sqrt(hd), BF16)
    q_heads = [head_only(scaled, h, hd) for h in range(heads)]

    def block(first, size, skip, mode):
        rows = pl.ds(pl.multiple_of(first, size), size)
        m_old = m_s[:, skip:]
        l_old = l_s[:, skip:]
        scores = [dot_nt(k_ref[rows, lanes_of(h, hd)[1]], q_heads[h][skip:]) for h in range(heads)]
        if mode != "none":
            bad = self_bad(b_ref, i * bq + skip, first, bq - skip, size, mode == "causal")
            scores = [jnp.where(bad, NEGATIVE, s) for s in scores]
        m_out, l_out, a_out = [], [], []
        for h in range(heads):
            part = slice(h * hd, (h + 1) * hd)
            m_new = jnp.maximum(m_old[h : h + 1, :], jnp.max(scores[h], axis=0, keepdims=True))
            shrink = jnp.exp(m_old[h : h + 1, :] - m_new)
            expos = jnp.exp(scores[h] - m_new)
            l_out.append(l_old[h : h + 1, :] * shrink + jnp.sum(expos, axis=0, keepdims=True))
            m_out.append(m_new)
            a_out.append(acc[part, skip:] * shrink + dot_nn(vt_ref[part, rows], expos.astype(BF16)))
        m_s[:, skip:] = jnp.concatenate(m_out, 0)
        l_s[:, skip:] = jnp.concatenate(l_out, 0)
        for h in range(heads):
            acc[h * hd : (h + 1) * hd, skip:] = a_out[h]

    over_keys(i, bq, safe, block, [(2, 0, onward), (3, 2, spread.middle), (4, 3, spread.last)])
    inverse = 1.0 / l_s[...]
    for h in range(heads):
        part = slice(h * hd, (h + 1) * hd)
        ot_ref[part, :] = (acc[part, :] * inverse[h : h + 1, :]).astype(BF16)
    lse_ref[...] = m_s[...] + jnp.log(l_s[...])
    terms_ref[...] = dot_nt(ot_ref[...].T, w_ref[:, 3 * width :]).astype(BF16)

    @pl.when(i == last)
    def _():
        for step in range(1, len(stages)):
            next_stage(step)
        over_z.wait()
        spread.end()
        for stage in stages:
            for copy, _ in stage:
                copy.wait_send()
        keep.wait()


def self_forward(bounds, x, w, biases, column, up, down, heads, safe):
    n, model = x.shape
    width = w.shape[1] // 4
    bq = 512
    dp = lax.axis_size("dp")
    m, r, c = column.shape
    by_rows_spec = pl.BlockSpec((bq, width), lambda i: (i, 0))
    by_columns_spec = pl.BlockSpec((width, bq), lambda i: (0, i))
    return pl.pallas_call(
        functools.partial(self_forward_kernel, heads=heads, safe=safe, n=dp),
        grid=(n // bq,),
        in_specs=[
            pl.BlockSpec(memory_space=pltpu.SMEM),
            pl.BlockSpec((bq, model), lambda i: (i, 0)),
            const((model, 4 * width)),
            const(biases.shape),
            ANY,
            const(up.shape),
            ANY,
        ],
        out_specs=[
            by_rows_spec,
            const((n, width)),
            by_rows_spec,
            by_columns_spec,
            by_columns_spec,
            pl.BlockSpec((heads, bq), lambda i: (0, i)),
            pl.BlockSpec((bq, model), lambda i: (i, 0)),
            ANY,
            ANY,
            ANY,
        ],
        out_shape=[
            jax.ShapeDtypeStruct((n, width), BF16),
            jax.ShapeDtypeStruct((n, width), BF16),
            jax.ShapeDtypeStruct((n, width), BF16),
            jax.ShapeDtypeStruct((width, n), BF16),
            jax.ShapeDtypeStruct((width, n), BF16),
            jax.ShapeDtypeStruct((heads, n), F32),
            jax.ShapeDtypeStruct((n, model), BF16),
            jax.ShapeDtypeStruct((4, m, 2, r, c), BF16),
            jax.ShapeDtypeStruct((m,) + up.shape, BF16),
            jax.ShapeDtypeStruct(down.shape[1:], BF16),
        ],
        scratch_shapes=[
            pltpu.VMEM((width, n), BF16),
            pltpu.VMEM((heads, bq), F32),
            pltpu.VMEM((heads, bq), F32),
            pltpu.VMEM((width, bq), F32),
            pltpu.VMEM((m, r, c), BF16),
        ]
        + link_scratch(9 + m, 3),
        compiler_params=pltpu.CompilerParams(
            vmem_limit_bytes=VMEM_LIMIT, collective_id=1, has_side_effects=True
        ),
        cost_estimate=pl.CostEstimate(
            flops=12 * n * n * width, bytes_accessed=8 * n * width, transcendentals=n * n * heads // 2
        ),
        name="self_forward",
    )(bounds, x, w, biases, column, up, down)


def after_self_kernel(
    terms_ref, rows_ref, biases_ref, norm_ref, column_ref, enc_ref, down_ref, from_z,
    after_out, second_out, whole_out, enc_out, down_out, far_down, *scratch, n
):
    links = Links(*scratch[-3:])
    rows_sum = RowSum(links, terms_ref, scratch[:5], left=True)
    column = scratch[5]
    spread = SpreadZ(links, down_ref.at[0], from_z, scratch[6], down_out, n)
    over_z = links.copy(down_ref.at[1], far_down, z_ways(n)[0])
    y = links.dp % 2
    near_out, core_out = whole_out.at[0], whole_out.at[1]
    load = links.local(column_ref, column)
    own = links.local(column, near_out.at[:, y])
    over_y = links.copy(column, near_out.at[:, y], Y)
    over_core = [
        links.copy(column, core_out.at[:, y], CORE),
        links.copy(near_out.at[:, 1 - y], core_out.at[:, 1 - y], CORE),
    ]
    enc_count = enc_ref.shape[0]

    def place(distance):
        return enc_out.at[pl.ds(pl.multiple_of((links.tensor ^ distance) * enc_count, enc_count), enc_count)]

    enc_x = links.copy(enc_ref, place(0), X)
    enc_core = [links.copy(enc_ref, place(0), CORE), links.copy(place(2), place(2), CORE)]
    enc_own = links.local(enc_ref, place(0))
    links.greet([CORE, X, Y] + z_ways(n))
    rows_sum.start()
    load.start()
    over_z.start()
    load.wait()
    over_y.start()
    own.start()
    enc_own.start()
    spread.start()
    rows_sum.middle()
    over_core[0].start()
    enc_core[0].start()
    rows_sum.over_x.wait_send()
    enc_x.start()
    rows_sum.end()

    def norm(rows):
        after = rows_ref[rows, :].astype(F32) + rows_sum.total(rows) + biases_ref[2:3, :]
        after_out[rows, :] = after
        xhat, _ = normalized(after)
        second_out[rows, :] = (xhat * norm_ref[1, 0:1, :] + norm_ref[1, 1:2, :]).astype(BF16)

    by_rows(after_out.shape[0], 64, norm)
    enc_x.wait_recv()
    enc_core[1].start()
    over_y.wait_recv()
    over_core[1].start()
    enc_x.wait_send()
    over_y.wait_send()
    spread.end()
    over_z.wait()
    for copy in [own, enc_own] + over_core + enc_core:
        copy.wait()


def sum_after_self(terms, rows, biases, norm, column, encoder, down, from_z):
    count, model = rows.shape
    m, r, c = column.shape
    vmem = pl.BlockSpec(memory_space=pltpu.VMEM)
    return pl.pallas_call(
        functools.partial(after_self_kernel, n=2 * m),
        in_specs=[ANY, vmem, vmem, vmem, ANY, vmem, ANY, ANY],
        out_specs=[vmem, vmem, ANY, ANY, ANY, ANY],
        out_shape=[
            jax.ShapeDtypeStruct((count, model), F32),
            jax.ShapeDtypeStruct((count, model), BF16),
            jax.ShapeDtypeStruct((2, m, 2, r, c), BF16),
            jax.ShapeDtypeStruct((4 * encoder.shape[0], model), BF16),
            jax.ShapeDtypeStruct((2, m, 2, r, c), BF16),
            jax.ShapeDtypeStruct((2, r, c), BF16),
        ],
        scratch_shapes=row_sum_scratch(count, model)
        + [pltpu.VMEM((m, r, c), BF16), pltpu.VMEM((2, 2, r, c), BF16)]
        + link_scratch(10 + spread_z_copies(2 * m), 9),
        compiler_params=pltpu.CompilerParams(
            vmem_limit_bytes=VMEM_LIMIT, collective_id=8, has_side_effects=True
        ),
        cost_estimate=pl.CostEstimate(flops=0, bytes_accessed=100 * 2**20, transcendentals=0),
        name="sum_after_self",
    )(terms, rows, biases, norm, column, encoder, down, from_z)


def self_backward_kernel(
    b_ref, q_ref, k_ref, v_ref, kt_ref, wide_ref, w_ref, mt_ref, lse_ref,
    up_ref, cross_ref, diagonal_ref, enc_ref,
    dq_ref, dk_ref, dv_ref, up_out, cross_out, enc_out, dka, dva, dqa, *scratch, heads, safe, n
):
    i = pl.program_id(0)
    links = Links(*scratch[-3:])
    cross = GatherLast(links, cross_ref.at[0], cross_ref.at[1], diagonal_ref, scratch[:5])
    cross_z = Collect(links, cross.column, scratch[5])
    up_column = scratch[6]
    up_z = Collect(links, up_column, scratch[7])
    load = links.local(up_ref, up_column)
    enc = RowSum(links, enc_ref, scratch[8:13])
    stages = len(up_z.stages)

    @pl.when(i == 0)
    def _():
        links.greet(everywhere_ways(n))
        cross.start()
        enc.start()
        load.start()
        load.wait()
        up_z.start(0)
        dka[...] = jnp.zeros_like(dka)
        dva[...] = jnp.zeros_like(dva)

    @pl.when(i == 1)
    def _():
        cross.middle()

    @pl.when(i == 2)
    def _():
        for step in range(stages - 1):
            up_z.finish(step)
            up_z.start(step + 1)

    def sum_cross():
        cross.end()
        cross_z.start(0)
        enc.middle()

    def next_cross():
        for step in range(stages - 1):
            cross_z.finish(step)
            cross_z.start(step + 1)

    bq, width = q_ref.shape
    hd = width // heads
    scale = 1.0 / math.sqrt(hd)
    grads = dot_nn(wide_ref[...], w_ref[:, 3 * width :]).astype(BF16)
    products = grads.T.astype(F32) * mt_ref[...].astype(F32)
    inner = [jnp.sum(products[h * hd : (h + 1) * hd, :], axis=0, keepdims=True) for h in range(heads)]
    scaled = q_ref[...] * jnp.asarray(scale, BF16)
    q_heads = [head_only(scaled, h, hd) for h in range(heads)]
    d_heads = [head_only(grads, h, hd) for h in range(heads)]
    lse = lse_ref[...]
    dqa[...] = jnp.zeros_like(dqa)

    def block(first, size, skip, mode):
        rows = pl.ds(pl.multiple_of(first, size), size)
        scores = [dot_nt(k_ref[rows, lanes_of(h, hd)[1]], q_heads[h][skip:]) for h in range(heads)]
        dprobs = [dot_nt(v_ref[rows, lanes_of(h, hd)[1]], d_heads[h][skip:]) for h in range(heads)]
        if mode != "none":
            bad = self_bad(b_ref, i * bq + skip, first, bq - skip, size, mode == "causal")
            scores = [jnp.where(bad, NEGATIVE, s) for s in scores]
        dv_sums, dk_sums = {}, {}
        for h in range(heads):
            part = slice(h * hd, (h + 1) * hd)
            group, _ = lanes_of(h, hd)
            probs = jnp.exp(scores[h] - lse[h : h + 1, skip:])
            ds = (probs * (dprobs[h] - inner[h][:, skip:])).astype(BF16)
            add_group(dv_sums, group, dot_nn(probs.astype(BF16), d_heads[h][skip:]))
            add_group(dk_sums, group, dot_nn(ds, q_heads[h][skip:]))
            dqa[part, skip:] += dot_nn(kt_ref[part, rows], ds)
        for group in dv_sums:
            part = slice(group * LANES, (group + 1) * LANES)
            dva[rows, part] += dv_sums[group]
            dka[rows, part] += dk_sums[group]

    over_keys(i, bq, safe, block, [(3, 2, sum_cross), (4, 2, next_cross)])
    dq_ref[...] = (dqa[...] * scale).astype(BF16).T

    @pl.when(i == pl.num_programs(0) - 1)
    def _():
        dk_ref[...] = dka[...].astype(BF16)
        dv_ref[...] = dva[...].astype(BF16)
        up_z.finish(stages - 1)
        up_out[...] = up_column[up_z.z].astype(F32)
        cross_z.finish(stages - 1)
        cross_out[...] = cross.column[cross_z.z].astype(F32)
        enc.end()

        def store(rows):
            enc_out[rows, :] = enc.total(rows)

        by_rows(enc_out.shape[0], 64, store)
        up_z.drain()
        cross_z.drain()


def self_backward(
    bounds, queries, keys, values, keys_t, wide, w, mixed_t, lse,
    up_column, cross_sum, diagonal, enc_terms, heads, safe
):
    n, width = queries.shape
    model = wide.shape[1]
    dp = lax.axis_size("dp")
    m, r, c = up_column.shape
    cross_c = cross_sum.shape[4]
    enc_shape = (enc_terms.shape[0] // 4, enc_terms.shape[1])
    bq = 512
    some = pl.BlockSpec((bq, width), lambda i: (i, 0))
    return pl.pallas_call(
        functools.partial(self_backward_kernel, heads=heads, safe=safe, n=dp),
        grid=(n // bq,),
        in_specs=[
            pl.BlockSpec(memory_space=pltpu.SMEM),
            some,
            const((n, width)),
            const((n, width)),
            const((width, n)),
            pl.BlockSpec((bq, model), lambda i: (i, 0)),
            const((model, 4 * width)),
            pl.BlockSpec((width, bq), lambda i: (0, i)),
            pl.BlockSpec((heads, bq), lambda i: (0, i)),
        ]
        + [ANY] * 4,
        out_specs=[some, const((n, width)), const((n, width))]
        + [const((r, c)), const((r, cross_c)), const(enc_shape)],
        out_shape=[
            jax.ShapeDtypeStruct((n, width), BF16),
            jax.ShapeDtypeStruct((n, width), BF16),
            jax.ShapeDtypeStruct((n, width), BF16),
            jax.ShapeDtypeStruct((r, c), F32),
            jax.ShapeDtypeStruct((r, cross_c), F32),
            jax.ShapeDtypeStruct(enc_shape, F32),
        ],
        scratch_shapes=[
            pltpu.VMEM((n, width), F32),
            pltpu.VMEM((n, width), F32),
            pltpu.VMEM((width, bq), F32),
        ]
        + [pltpu.VMEM((m, r, cross_c), BF16)] * 6
        + [pltpu.VMEM((m, r, c), BF16)] * 2
        + row_sum_scratch(*enc_shape)
        + link_scratch(5 + 2 * m, 6),
        compiler_params=pltpu.CompilerParams(
            vmem_limit_bytes=VMEM_LIMIT, collective_id=5, has_side_effects=True
        ),
        cost_estimate=pl.CostEstimate(
            flops=24 * n * n * width, bytes_accessed=16 * n * width, transcendentals=n * n * heads // 2
        ),
        name="self_backward",
    )(bounds, queries, keys, values, keys_t, wide, w, mixed_t, lse, up_column, cross_sum, diagonal, enc_terms)


def const(shape):
    return pl.BlockSpec(shape, lambda *_: (0,) * len(shape), pipeline_mode=pl.Buffered(1))


def normalized(rows):
    center = rows - jnp.mean(rows, axis=-1, keepdims=True)
    scale = lax.rsqrt(jnp.mean(center * center, axis=-1, keepdims=True) + EPSILON)
    return center * scale, scale


def norm_rows_back(rows, incoming, gain):
    xhat, scale = normalized(rows)
    e = incoming * gain
    inner = jnp.mean(e * xhat, axis=-1, keepdims=True)
    return scale * (e - jnp.mean(e, axis=-1, keepdims=True) - xhat * inner), incoming * xhat


def by_rows(count, step, body):
    def one(k, c):
        body(pl.ds(pl.multiple_of(k * step, step), step))
        return c

    lax.fori_loop(0, count // step, one, 0)


def cross_forward_kernel(
    len_ref, x_ref, enc_ref, w_ref, biases_ref, rows_ref, norm_ref, column_ref, down_ref, from_z,
    q_out, k_out, v_out, ot_ref, lse_ref, after_ref, third_ref, whole, down_out, hold, send_sems, recv_sems, local_sems, *, heads, n
):
    i = pl.program_id(0)
    last = pl.num_programs(0) - 1
    links = Links(send_sems, recv_sems, local_sems)
    spread = SpreadFar(links, column_ref, whole)
    pieces = len(spread.over_x)
    spread_z = SpreadZ(links, down_ref.at[1], from_z, hold, down_out, n)

    @pl.when(i == 0)
    def _():
        links.greet([CORE, X, Y] + z_ways(n))
        spread.start()
        spread_z.start()
        after_ref[...] = rows_ref[...] + biases_ref[5:6, :]

    def onward(*when):
        for step, k in when:
            pl.when(i == step)(functools.partial(spread.onward, k))

    onward((1, 0), (1, 1), (2, 3), (3, 5))

    width = q_out.shape[2]
    hd = width // heads
    mine = pl.ds(pl.multiple_of((links.tensor ^ i) * width, width), width)
    query = (dot_nn(x_ref[...], w_ref[0, :, :width]) + biases_ref[3:4, mine]).astype(BF16)
    key_value = dot_nn(enc_ref[...], w_ref[0, :, width : 3 * width])
    keys = key_value[:, :width].astype(BF16)
    values = (key_value[:, width:] + biases_ref[4:5, mine]).astype(BF16)
    q_out[0] = query
    k_out[0] = keys
    v_out[0] = values
    values_t = values.T
    scaled = query * jnp.asarray(1.0 / math.sqrt(hd), BF16)
    ok = lax.broadcasted_iota(jnp.int32, (keys.shape[0], 1), 0) < len_ref[0]
    scores = [dot_nt(keys[:, lanes_of(h, hd)[1]], head_only(scaled, h, hd)) for h in range(heads)]
    mixed = []
    for h in range(heads):
        part = slice(h * hd, (h + 1) * hd)
        s = jnp.where(ok, scores[h], NEGATIVE)
        largest = jnp.max(s, axis=0, keepdims=True)
        expos = jnp.exp(s - largest)
        total = jnp.sum(expos, axis=0, keepdims=True)
        mixed.append((dot_nn(values_t[part, :], expos.astype(BF16)) * (1.0 / total)).astype(BF16))
        ot_ref[0, part, :] = mixed[h]
        lse_ref[0, h : h + 1, :] = largest + jnp.log(total)
        if h == heads // 2 - 1:
            onward((1, 2), (2, 4), (3, 6))
    after_ref[...] += dot_nt(jnp.concatenate(mixed, 0).T, w_ref[0, :, 3 * width :])

    @pl.when(i == last)
    def _():
        def norm(rows):
            xhat, _ = normalized(after_ref[rows, :])
            third_ref[rows, :] = (xhat * norm_ref[2, 0:1, :] + norm_ref[2, 1:2, :]).astype(BF16)

        by_rows(after_ref.shape[0], 128, norm)
        for k in range(7, pieces):
            spread.onward(k)
        for k in range(pieces):
            spread.last(k)
        spread_z.end()
        spread.end()


def cross_forward(lengths, x, encoder, weights, biases, rows, norm, column, down, from_z, heads):
    count, model = x.shape
    n = encoder.shape[0]
    parts, _, columns = weights.shape
    width = columns // 4
    m, r, c = column.shape

    def by_part(*shape):
        return pl.BlockSpec((1,) + shape, lambda i: (i,) + (0,) * len(shape))

    return pl.pallas_call(
        functools.partial(cross_forward_kernel, heads=heads, n=2 * m),
        grid=(parts,),
        in_specs=[
            pl.BlockSpec(memory_space=pltpu.SMEM),
            const((count, model)),
            const((n, model)),
            by_part(model, columns),
            const(biases.shape),
            const((count, model)),
            const(norm.shape),
            ANY,
            ANY,
            ANY,
        ],
        out_specs=[
            by_part(count, width),
            by_part(n, width),
            by_part(n, width),
            by_part(width, count),
            by_part(heads, count),
            const((count, model)),
            const((count, model)),
            ANY,
            ANY,
        ],
        out_shape=[
            jax.ShapeDtypeStruct((parts, count, width), BF16),
            jax.ShapeDtypeStruct((parts, n, width), BF16),
            jax.ShapeDtypeStruct((parts, n, width), BF16),
            jax.ShapeDtypeStruct((parts, width, count), BF16),
            jax.ShapeDtypeStruct((parts, heads, count), F32),
            jax.ShapeDtypeStruct((count, model), F32),
            jax.ShapeDtypeStruct((count, model), BF16),
            jax.ShapeDtypeStruct((2, m, 2, r, c), BF16),
            jax.ShapeDtypeStruct((2, m, 2, r, c), BF16),
        ],
        scratch_shapes=[pltpu.VMEM((2, 2, r, c), BF16)] + link_scratch(32 + spread_z_copies(2 * m), 4),
        compiler_params=pltpu.CompilerParams(
            vmem_limit_bytes=VMEM_LIMIT, collective_id=2, has_side_effects=True
        ),
        cost_estimate=pl.CostEstimate(
            flops=24 * parts * count * n * width,
            bytes_accessed=8 * parts * n * width,
            transcendentals=parts * count * n * heads,
        ),
        name="cross_forward",
    )(lengths, x, encoder, weights, biases, rows, norm, column, down, from_z)


def feed_forward_kernel(
    x_ref, dy_ref, near_up, near_down, far_up, far_down, b_ref, after_ref, biases_ref, norm_ref,
    out_ref, rows_out, low_out, sums_ref, gup_ref, gdown_ref, bias_ref, from_x, from_y,
    xt_ref, dyt_ref, back_ref, give, got, diagonal, loaded, load_sems, send_sems, recv_sems, local_sems, *, chunks
):
    s = pl.program_id(0)
    links = Links(send_sems, recv_sems, local_sems)
    turn = s // chunks
    chunk = s % chunks
    pair = turn // 2
    slot = pair * chunks + chunk
    theirs = turn % 2 == 0
    y = links.dp % 2
    m, r = diagonal.shape[1], diagonal.shape[2]
    low, high = pl.ds(0, m // 2), pl.ds(m // 2, m - m // 2)
    links.used = 2 * chunks
    across = [
        links.copy(diagonal.at[:, low], from_x, X),
        links.copy(diagonal.at[:, high], from_y, Y),
    ]
    to_core = pltpu.make_async_remote_copy(
        src_ref=give.at[chunk],
        dst_ref=got.at[slot],
        send_sem=send_sems.at[slot],
        recv_sem=recv_sems.at[slot],
        device_id=links.partner(CORE),
        device_id_type=pl.DeviceIdType.MESH,
    )

    size = loaded.shape[3]

    def fetch(step, act):
        block = 3 - step // chunks
        slot = step % 2
        first = (step % chunks) * size

        def both(*sources):
            for k, source in enumerate(sources):
                columns = pl.ds(pl.multiple_of(first, size), size)
                act(pltpu.make_async_copy(source.at[:, columns], loaded.at[slot, k], load_sems.at[slot, k]))

        @pl.when(block >= 2)
        def _():
            both(far_up.at[block - 2], far_down.at[block - 2])

        @pl.when(block < 2)
        def _():
            both(near_up.at[block], near_down.at[block])

    @pl.when(s == 0)
    def _():
        fetch(0, lambda copy: copy.start())
        links.greet([CORE, X, Y])
        out_ref[...] = after_ref[...] + biases_ref[6:7, :]
        back_ref[...] = jnp.zeros_like(back_ref)
        xt_ref[...] = x_ref[...].T
        dyt_ref[...] = dy_ref[...].T
        sums_ref[...] = jnp.zeros_like(sums_ref)

    fetch(s, lambda copy: copy.wait())

    @pl.when(s + 1 < pl.num_programs(0))
    def _():
        fetch(s + 1, lambda copy: copy.start())

    up_ref, down_ref = loaded.at[s % 2, 0], loaded.at[s % 2, 1]
    lines = size // LANES
    line = ((links.tensor ^ (3 - turn)) * chunks + chunk) * lines
    shift = jnp.concatenate([b_ref[pl.ds(line + k, 1), :] for k in range(lines)], axis=1)
    pre_act = dot_nn(x_ref[...], up_ref[...]) + shift
    hidden_grad = dot_nn(dy_ref[...], down_ref[...])
    normal_cdf = 0.5 * (1.0 + lax.erf(pre_act * (1.0 / math.sqrt(2.0))))
    density = jnp.exp(-0.5 * pre_act * pre_act) * (1.0 / math.sqrt(2.0 * math.pi))
    hidden = (pre_act * normal_cdf).astype(BF16)
    pre_grad = (hidden_grad * (normal_cdf + pre_act * density)).astype(BF16)
    bias_ref[0] = jnp.sum(pre_grad.astype(F32), axis=0, keepdims=True)

    @pl.when(turn % 2 == 1)
    def _():
        to_core.wait_send()

    give[chunk, 0] = dot_nn(xt_ref[...], pre_grad).astype(BF16)
    give[chunk, 1] = dot_nn(dyt_ref[...], hidden).astype(BF16)
    out_ref[...] += dot_nt(hidden, down_ref[...])
    back_ref[...] += dot_nt(pre_grad, up_ref[...])

    @pl.when(theirs)
    def _():
        to_core.start()

    @pl.when(jnp.logical_not(theirs))
    def _():
        to_core.wait_recv()
        gup_ref[0] = (give[chunk, 0].astype(F32) + got[slot, 0].astype(F32)).astype(BF16)
        gdown_ref[0] = (give[chunk, 1].astype(F32) + got[slot, 1].astype(F32)).astype(BF16)

    for k in range(chunks):

        @pl.when(s == chunks + k)
        def _():
            def keep(z, carry):
                rows = pl.ds(pl.multiple_of((2 * z + 1 - y) * r, r), r)
                size = gup_ref.shape[2]
                diagonal[0, z, :, k * size : (k + 1) * size] = gup_ref[0, rows, :]
                diagonal[1, z, :, k * size : (k + 1) * size] = gdown_ref[0, rows, :]
                return carry

            lax.fori_loop(0, m, keep, 0)
            if k == chunks - 1:
                for copy in across:
                    copy.start()

    @pl.when(s == pl.num_programs(0) - 1)
    def _():
        def norm_back(rows):
            third = back_ref[rows, :]
            upstream = dy_ref[rows, :].astype(F32)
            rows_grad, gain_terms = norm_rows_back(after_ref[rows, :], third, norm_ref[2, 0:1, :])
            rows_grad = rows_grad + upstream
            low = rows_grad.astype(BF16)
            rows_out[rows, :] = rows_grad
            low_out[rows, :] = low
            for k, terms in enumerate((gain_terms, third, low.astype(F32), upstream)):
                sums_ref[k : k + 1, :] += jnp.sum(terms, axis=0, keepdims=True)

        by_rows(x_ref.shape[0], 128, norm_back)
        for copy in across:
            copy.wait()


def feed_forward(x, dy, weights, bias, after, biases, norm):
    rows, width = x.shape
    hidden = weights[0].shape[2]
    size = min(512, hidden)
    chunks = hidden // size

    n = lax.axis_size("dp")
    m, r = n // 2, width // n

    def block(s):
        return 3 - s // chunks

    def placed(s):
        turn = s // chunks
        return (1 - turn // 2, 0, (s % chunks) * (turn % 2))

    rows_spec = const((rows, width))
    grad_spec = pl.BlockSpec((1, width, size), placed)
    bias_spec = pl.BlockSpec((1, 1, size), lambda s: (block(s), 0, s % chunks))
    return pl.pallas_call(
        functools.partial(feed_forward_kernel, chunks=chunks),
        grid=(4 * chunks,),
        in_specs=[
            rows_spec,
            rows_spec,
            ANY,
            ANY,
            ANY,
            ANY,
            const(bias.shape),
            rows_spec,
            const(biases.shape),
            const(norm.shape),
        ],
        out_specs=[rows_spec, rows_spec, rows_spec, const((8, width)), grad_spec, grad_spec, bias_spec, ANY, ANY],
        out_shape=[
            jax.ShapeDtypeStruct((rows, width), F32),
            jax.ShapeDtypeStruct((rows, width), F32),
            jax.ShapeDtypeStruct((rows, width), BF16),
            jax.ShapeDtypeStruct((8, width), F32),
            jax.ShapeDtypeStruct((2, width, hidden), BF16),
            jax.ShapeDtypeStruct((2, width, hidden), BF16),
            jax.ShapeDtypeStruct((4, 1, hidden), F32),
            jax.ShapeDtypeStruct((2, m // 2, r, hidden), BF16),
            jax.ShapeDtypeStruct((2, m - m // 2, r, hidden), BF16),
        ],
        scratch_shapes=[
            pltpu.VMEM((width, rows), BF16),
            pltpu.VMEM((width, rows), BF16),
            pltpu.VMEM((rows, width), F32),
            pltpu.VMEM((chunks, 2, width, size), BF16),
            pltpu.VMEM((2 * chunks, 2, width, size), BF16),
            pltpu.VMEM((2, m, r, hidden), BF16),
            pltpu.VMEM((2, 2, width, size), BF16),
            pltpu.SemaphoreType.DMA((2, 2)),
        ]
        + link_scratch(2 * chunks + 2, 1),
        compiler_params=pltpu.CompilerParams(
            vmem_limit_bytes=VMEM_LIMIT, collective_id=3, has_side_effects=True
        ),
        cost_estimate=pl.CostEstimate(
            flops=48 * rows * width * hidden, bytes_accessed=40 * 2**20, transcendentals=8 * rows * hidden
        ),
        name="feed_forward",
    )(x, dy, *weights, bias, after, biases, norm)


def cross_backward_kernel(
    len_ref, low_ref, x_ref, enc_ref, w_ref, q_ref, k_ref, v_ref, mt_ref, lse_ref, up_ref, down_ref, from_x, from_y,
    back_ref, enc_out, grad_ref, bq_ref, bv_ref, up_out, down_out,
    low_t, x_t, enc_t, enc_acc, give, got, *scratch, heads, bk
):
    i = pl.program_id(0)
    last = pl.num_programs(0) - 1
    links = Links(*scratch[14:])
    sums = [
        Gather(links, ref.at[0], ref.at[1], from_x.at[k], from_y.at[k], scratch[7 * k : 7 * k + 7])
        for k, ref in enumerate((up_ref, down_ref))
    ]
    leave = [links.local(g.column, out) for g, out in zip(sums, (up_out, down_out))]
    pair = i // 2
    to_core = pltpu.make_async_remote_copy(
        src_ref=give,
        dst_ref=got.at[pair],
        send_sem=links.send_sems.at[links.used + pair],
        recv_sem=links.recv_sems.at[links.used + pair],
        device_id=links.partner(CORE),
        device_id_type=pl.DeviceIdType.MESH,
    )

    @pl.when(i == 0)
    def _():
        links.greet([CORE, X, Y])
        for g in sums:
            g.start()
        low_t[...] = low_ref[...].T
        x_t[...] = x_ref[...].T
        enc_t[...] = enc_ref[...].T
        back_ref[...] = jnp.zeros_like(back_ref)
        enc_acc[...] = jnp.zeros_like(enc_acc)

    @pl.when(i == 1)
    def _():
        for g in sums:
            g.middle()

    rows, width = q_ref.shape[1:]
    n = k_ref.shape[1]
    hd = width // heads
    scale = 1.0 / math.sqrt(hd)
    w_query, w_keyval, w_out = w_ref.at[0, :, :width], w_ref.at[0, :, width : 3 * width], w_ref.at[0, :, 3 * width :]
    grads = dot_nn(low_ref[...], w_out[...]).astype(BF16)
    mixed_t = mt_ref[0]
    products = grads.T.astype(F32) * mixed_t.astype(F32)
    inner = [jnp.sum(products[h * hd : (h + 1) * hd, :], axis=0, keepdims=True) for h in range(heads)]
    scaled = q_ref[0] * jnp.asarray(scale, BF16)
    q_heads = [head_only(scaled, h, hd) for h in range(heads)]
    d_heads = [head_only(grads, h, hd) for h in range(heads)]
    lse = lse_ref[0]
    keys_t = k_ref[0].T
    dq = [None] * heads
    dkv = []
    for j in range(n // bk):
        span = slice(j * bk, (j + 1) * bk)
        ok = j * bk + lax.broadcasted_iota(jnp.int32, (bk, 1), 0) < len_ref[0]
        scores = [dot_nt(k_ref[0, span, lanes_of(h, hd)[1]], q_heads[h]) for h in range(heads)]
        dprobs = [dot_nt(v_ref[0, span, lanes_of(h, hd)[1]], d_heads[h]) for h in range(heads)]
        dv_sums, dk_sums = {}, {}
        for h in range(heads):
            part = slice(h * hd, (h + 1) * hd)
            group, _ = lanes_of(h, hd)
            probs = jnp.exp(jnp.where(ok, scores[h], NEGATIVE) - lse[h : h + 1, :])
            ds = (probs * (dprobs[h] - inner[h])).astype(BF16)
            add_group(dv_sums, group, dot_nn(probs.astype(BF16), d_heads[h]))
            add_group(dk_sums, group, dot_nn(ds, q_heads[h]))
            dq_h = dot_nn(keys_t[part, span], ds)
            dq[h] = dq_h if dq[h] is None else dq[h] + dq_h
        block = jnp.concatenate([sums_of[g].astype(BF16) for sums_of in (dk_sums, dv_sums) for g in sorted(sums_of)], 1)
        enc_acc[span, :] += dot_nt(block, w_keyval[...])
        dkv.append(block)
    dq = (jnp.concatenate(dq, 0) * scale).astype(BF16).T
    dkv = jnp.concatenate(dkv, 0)
    bq_ref[0] = jnp.sum(dq.astype(F32), axis=0, keepdims=True)
    bv_ref[0] = jnp.sum(dkv[:, width:].astype(F32), axis=0, keepdims=True)
    back_ref[...] += dot_nt(dq, w_query[...])

    @pl.when(i % 2 == 1)
    def _():
        to_core.wait_send()

    give[:, :width] = dot_nn(x_t[...], dq).astype(BF16)
    give[:, width : 3 * width] = dot_nn(enc_t[...], dkv).astype(BF16)
    give[:, 3 * width :] = dot_nn(low_t[...], mixed_t.T).astype(BF16)

    @pl.when(i % 2 == 0)
    def _():
        to_core.start()

    @pl.when(i % 2 == 1)
    def _():
        to_core.wait_recv()
        grad_ref[0] = (give[...].astype(F32) + got[pair].astype(F32)).astype(BF16)

    @pl.when(i == last)
    def _():
        enc_out[...] = enc_acc[...].astype(BF16)
        for g, copy in zip(sums, leave):
            g.end()
            copy.start()
        for copy in leave:
            copy.wait()


def cross_backward(
    lengths, low, x, encoder, weights, queries, keys, values, mixed_t, lse, up_sum, down_sum, from_x, from_y, heads
):
    count, model = x.shape
    n = encoder.shape[0]
    parts, _, columns = weights.shape
    width = columns // 4
    _, m, _, r, c = up_sum.shape

    def by_part(*shape):
        return pl.BlockSpec((1,) + shape, lambda i: (i ^ 1,) + (0,) * len(shape))

    return pl.pallas_call(
        functools.partial(cross_backward_kernel, heads=heads, bk=256),
        grid=(parts,),
        in_specs=[
            pl.BlockSpec(memory_space=pltpu.SMEM),
            const((count, model)),
            const((count, model)),
            const((n, model)),
            by_part(model, columns),
            by_part(count, width),
            by_part(n, width),
            by_part(n, width),
            by_part(width, count),
            by_part(heads, count),
            ANY,
            ANY,
            ANY,
            ANY,
        ],
        out_specs=[
            const((count, model)),
            const((n, model)),
            pl.BlockSpec((1, model, columns), lambda i: (i // 2, 0, 0), pipeline_mode=pl.Buffered(1)),
            by_part(1, width),
            by_part(1, width),
            ANY,
            ANY,
        ],
        out_shape=[
            jax.ShapeDtypeStruct((count, model), F32),
            jax.ShapeDtypeStruct((n, model), BF16),
            jax.ShapeDtypeStruct((2, model, columns), BF16),
            jax.ShapeDtypeStruct((parts, 1, width), F32),
            jax.ShapeDtypeStruct((parts, 1, width), F32),
            jax.ShapeDtypeStruct((m, r, c), BF16),
            jax.ShapeDtypeStruct((m, r, c), BF16),
        ],
        scratch_shapes=[
            pltpu.VMEM((model, count), BF16),
            pltpu.VMEM((model, count), BF16),
            pltpu.VMEM((model, n), BF16),
            pltpu.VMEM((n, model), F32),
            pltpu.VMEM((model, columns), BF16),
            pltpu.VMEM((2, model, columns), BF16),
        ]
        + gather_scratch(m, r, c) * 2
        + link_scratch(10, 12),
        compiler_params=pltpu.CompilerParams(
            vmem_limit_bytes=60 * 2**20, collective_id=4, has_side_effects=True
        ),
        cost_estimate=pl.CostEstimate(
            flops=48 * parts * count * n * width,
            bytes_accessed=16 * parts * n * width,
            transcendentals=parts * count * n * heads,
        ),
        name="cross_backward",
    )(lengths, low, x, encoder, weights, queries, keys, values, mixed_t, lse, up_sum, down_sum, from_x, from_y)


def on_device(
    block_in,
    encoder_out,
    out_grad,
    bounds,
    enc_lengths,
    norm_params,
    w_qkv,
    w_self_out,
    w_cross_q,
    w_cross_kv,
    w_cross_out,
    w_up,
    w_down,
    biases,
    up_bias,
):
    groups_count = lax.axis_size("dp")
    width = w_cross_q.shape[1]
    hidden_width = w_up.shape[1]
    heads = H // 4
    own_rows, model_width = block_in.shape
    w_rows = w_cross_q.shape[0]

    first_in, self_w, cross_column, down_square = start_gather(
        block_in,
        norm_params,
        w_qkv,
        w_self_out,
        w_cross_q,
        w_cross_kv,
        w_cross_out,
        w_down,
    )
    self_w = self_w.reshape(model_width, 4 * width)

    self_safe = 1024
    queries, key_rows, value_rows, keys_t, self_mixed_t, self_lse, terms, cross_w, up_column, near_z = self_forward(
        bounds,
        first_in,
        self_w,
        biases,
        cross_column,
        w_up,
        down_square,
        heads,
        self_safe,
    )
    cross_w = cross_w.reshape(4, model_width, 4 * width)
    after_self, second_in, near_up, enc_all, near_down, far_z = sum_after_self(
        terms, block_in, biases, norm_params, up_column, encoder_out, down_square, near_z
    )

    cross_q, cross_k, cross_v, cross_mixed_t, cross_lse, after_cross, third_in, far_up, far_down = cross_forward(
        enc_lengths,
        second_in,
        enc_all,
        cross_w,
        biases,
        after_self,
        norm_params,
        up_column,
        down_square,
        far_z,
        heads,
    )

    output, cross_rows_grad, cross_low, ffn_sums, up_sum, down_sum, bias_up_parts, from_x, from_y = feed_forward(
        third_in,
        out_grad,
        [w.reshape(2, model_width, hidden_width) for w in (near_up, near_down, far_up, far_down)],
        up_bias.reshape(-1, LANES),
        after_cross,
        biases,
        norm_params,
    )

    by_shard = (2, groups_count // 2, 2, w_rows, hidden_width)
    second_grad, enc_terms, cross_sum, bias_cq_parts, bias_cv_parts, up_column, down_column = cross_backward(
        enc_lengths,
        cross_low,
        second_in,
        enc_all,
        cross_w,
        cross_q,
        cross_k,
        cross_v,
        cross_mixed_t,
        cross_lse,
        up_sum.reshape(by_shard),
        down_sum.reshape(by_shard),
        from_x,
        from_y,
        heads,
    )
    cross_sum = cross_sum.reshape(2, groups_count // 2, 2, w_rows, 4 * width)
    self_wide, self_rows_grad, self_sums, summed_down, diagonal = middle(
        second_grad, after_self, cross_rows_grad, norm_params, down_column, cross_sum
    )
    self_dq, self_dk, self_dv, summed_up, summed_cross, encoder_grad = self_backward(
        bounds,
        queries,
        key_rows,
        value_rows,
        keys_t,
        self_wide,
        self_w,
        self_mixed_t,
        self_lse,
        up_column,
        cross_sum,
        diagonal,
        enc_terms,
        heads,
        self_safe,
    )
    input_grad, summed_self, vectors = tail(
        self_dq,
        self_dk,
        self_dv,
        self_w,
        first_in,
        self_wide,
        self_mixed_t,
        block_in,
        self_rows_grad,
        norm_params,
        self_sums,
        ffn_sums,
        bias_cq_parts,
        bias_cv_parts,
        bias_up_parts,
    )
    scale = 1.0 / groups_count
    output, input_grad, encoder_grad, g_qkv, g_so, g_cq, g_ckv, g_co, g_up, g_down = results(
        output, input_grad, encoder_grad, summed_self, summed_cross, summed_up, summed_down, scale
    )
    vectors = vectors * scale
    return (
        output,
        input_grad,
        encoder_grad,
        vectors[:6].reshape(norm_params.shape),
        g_qkv,
        g_so,
        g_cq,
        g_ckv,
        g_co,
        g_up,
        g_down,
        vectors[6:13],
        vectors[13:17].reshape(-1),
    )


def solution(mesh):
    rows = P(("dp", "tensor"), None)
    placed = (
        rows,
        rows,
        rows,
        P("dp", None),
        P("dp"),
        P(),
        P("dp", None, "tensor"),
        P("tensor", "dp"),
        P("dp", "tensor"),
        P("dp", None, "tensor"),
        P("tensor", "dp"),
        P("dp", "tensor"),
        P("tensor", "dp"),
        P(),
        P(),
    )
    return jax.shard_map(
        on_device,
        mesh=mesh,
        in_specs=placed,
        out_specs=(
            rows,
            rows,
            rows,
            P(),
            P("dp", None, "tensor"),
            P("tensor", "dp"),
            P("dp", "tensor"),
            P("dp", None, "tensor"),
            P("tensor", "dp"),
            P("dp", "tensor"),
            P("tensor", "dp"),
            P(),
            P(),
        ),
        check_vma=False,
    )
```

```python
import functools
import math

import jax
import jax.numpy as jnp
from jax import lax
from jax.experimental import pallas as pl
from jax.experimental.pallas import tpu as pltpu
from jax.sharding import PartitionSpec as P

H = 16
EPSILON = 1e-05
NEGATIVE = -1e30
F32 = jnp.float32
BF16 = jnp.bfloat16
VMEM_LIMIT = 56 * 2**20


def dot_nt(a, b):
    return lax.dot_general(a, b, (((1,), (1,)), ((), ())), preferred_element_type=F32)


def dot_nn(a, b):
    return lax.dot_general(a, b, (((1,), (0,)), ((), ())), preferred_element_type=F32)


def dot_tn(a, b):
    return lax.dot_general(a, b, (((0,), (0,)), ((), ())), preferred_element_type=F32)


LANES = 128


def lanes_of(h, size):
    group = h * size // LANES
    return group, slice(group * LANES, (group + 1) * LANES)


def head_only(x, h, size):
    group, part = lanes_of(h, size)
    lane = group * LANES + lax.broadcasted_iota(jnp.int32, (x.shape[0], LANES), 1)
    return jnp.where((lane >= h * size) & (lane < (h + 1) * size), x[:, part], jnp.zeros((), x.dtype))


def add_group(sums, group, value):
    sums[group] = value if group not in sums else sums[group] + value


def self_bad(b_ref, q_start, k_start, bq, bk, causal):
    qi = q_start + lax.broadcasted_iota(jnp.int32, (1, bq), 1)
    kj = k_start + lax.broadcasted_iota(jnp.int32, (bk, 1), 0)
    bad = (qi >= b_ref[0, 1]) & ((kj >= b_ref[0, 0]) & (kj < b_ref[0, 1]))
    if causal:
        bad = bad | (kj > qi)
    return bad


def over_keys(i, bq, safe, block, between=()):
    def visit(j, c):
        for at_i, at_j, action in between:
            pl.when((i == at_i) & (j == at_j))(action)

        @pl.when(j < safe // bq)
        def _():
            block(j * bq, bq, 0, "none")

        @pl.when(j >= safe // bq)
        def _():
            block(j * bq, bq, 0, "segment")

        return c

    lax.fori_loop(0, i, visit, 0)
    half = bq // 2
    block(i * bq, half, 0, "causal")
    block(i * bq + half, half, half, "causal")


CORE = ("tensor", 1)
X = ("tensor", 2)
Y = ("dp", 1)
ANY = pl.BlockSpec(memory_space=pl.ANY)


class Links:
    def __init__(self, send_sems, recv_sems, local_sems):
        self.dp = lax.axis_index("dp")
        self.tensor = lax.axis_index("tensor")
        self.send_sems, self.recv_sems, self.local_sems = send_sems, recv_sems, local_sems
        self.used = 0
        self.used_local = 0

    def partner(self, way):
        axis, distance = way
        if axis == "tensor":
            return (self.dp, self.tensor ^ distance)
        return (self.dp ^ distance, self.tensor)

    def greet(self, ways):
        barrier = pltpu.get_barrier_semaphore()
        for way in ways:
            pl.semaphore_signal(
                barrier, inc=1, device_id=self.partner(way), device_id_type=pl.DeviceIdType.MESH
            )
        pl.semaphore_wait(barrier, len(ways))

    def copy(self, source, target, way):
        k = self.used
        self.used += 1
        return pltpu.make_async_remote_copy(
            src_ref=source,
            dst_ref=target,
            send_sem=self.send_sems.at[k],
            recv_sem=self.recv_sems.at[k],
            device_id=self.partner(way),
            device_id_type=pl.DeviceIdType.MESH,
        )

    def local(self, source, target):
        k = self.used_local
        self.used_local += 1
        return pltpu.make_async_copy(source, target, self.local_sems.at[k])


def link_scratch(copies, local):
    return [
        pltpu.SemaphoreType.DMA((copies,)),
        pltpu.SemaphoreType.DMA((copies,)),
        pltpu.SemaphoreType.DMA((local,)),
    ]


def z_distances(n):
    found = []
    m = n // 2
    while m > 1:
        m //= 2
        found.append(m)
    return found


def z_ways(n):
    return [("dp", 2 * distance) for distance in z_distances(n)]


def column_stages(links, shard, column, n):
    z = links.dp // 2
    held = [z]
    stages = []
    for distance in z_distances(n):
        stages.append(
            [
                (
                    links.copy(shard if k == 0 else column.at[index], column.at[index], ("dp", 2 * distance)),
                    index ^ distance,
                )
                for k, index in enumerate(held)
            ]
        )
        held = held + [index ^ distance for index in held]
    return stages


class Spread:
    def __init__(self, links, source, column, whole):
        y = links.dp % 2
        half = column.shape[0] // 2
        low, high = pl.ds(0, half), pl.ds(half, half)
        near, near_core, far, far_core = (whole.at[k] for k in range(4))
        self.load = links.local(source, column)
        self.own = links.local(column, near.at[:, y])
        self.first = [
            links.copy(column, near.at[:, y], Y),
            links.copy(column, far.at[:, y], X),
        ]
        self.core = [links.copy(column, near_core.at[:, y], CORE)]
        self.second = [
            links.copy(near.at[low, 1 - y], far.at[low, 1 - y], X),
            links.copy(far.at[high, y], far.at[high, y], Y),
        ]
        self.core_second = [
            links.copy(near.at[:, 1 - y], near_core.at[:, 1 - y], CORE),
            links.copy(far.at[:, y], far_core.at[:, y], CORE),
        ]
        self.core_third = [links.copy(far.at[:, 1 - y], far_core.at[:, 1 - y], CORE)]

    def start(self):
        self.load.start()
        self.load.wait()
        for copy in self.first + self.core + [self.own]:
            copy.start()

    def middle(self):
        for copy in self.first:
            copy.wait_recv()
        for copy in self.second + self.core_second:
            copy.start()

    def last(self):
        for copy in self.second:
            copy.wait_recv()
        for copy in self.core_third:
            copy.start()

    def end(self):
        self.own.wait()
        for copy in self.first + self.second:
            copy.wait_send()
        for copy in self.core + self.core_second + self.core_third:
            copy.wait()


def add_to(total_ref, other_ref):
    def one(k, c):
        total_ref[k] = (total_ref[k].astype(F32) + other_ref[k].astype(F32)).astype(BF16)
        return c

    lax.fori_loop(0, total_ref.shape[0], one, 0)


class Gather:
    def __init__(self, links, near, far, from_x, from_y, buffers):
        y = links.dp % 2
        self.column, self.over_y, self.over_x, self.add_y, self.add_x, self.sum_y, self.sum_x = buffers
        m = self.column.shape[0]
        low, high = pl.ds(0, m // 2), pl.ds(m // 2, m - m // 2)
        self.loads = [
            links.local(near.at[low, 1 - y], self.over_y),
            links.local(far.at[high, y], self.over_x),
            links.local(from_x, self.add_y),
            links.local(from_y, self.add_x),
            links.local(near.at[:, y], self.column),
        ]
        self.first = [
            links.copy(far.at[low, y], self.sum_x.at[low], X),
            links.copy(near.at[high, 1 - y], self.sum_y.at[high], Y),
        ]
        self.second = [
            links.copy(self.over_x, self.sum_x.at[high], X),
            links.copy(self.over_y, self.sum_y.at[low], Y),
        ]

    def start(self):
        for copy in self.first + self.loads:
            copy.start()

    def middle(self):
        for copy in self.loads:
            copy.wait()
        add_to(self.over_x, self.add_x)
        add_to(self.over_y, self.add_y)
        for copy in self.second:
            copy.start()

    def end(self):
        for copy in self.first + self.second:
            copy.wait_recv()
        add_to(self.column, self.sum_y)
        add_to(self.column, self.sum_x)
        for copy in self.first + self.second:
            copy.wait_send()


def gather_scratch(m, r, c):
    whole = pltpu.VMEM((m, r, c), BF16)
    half = pltpu.VMEM((m // 2, r, c), BF16)
    return [whole] + [half] * 4 + [whole] * 2


class GatherLast:
    def __init__(self, links, near, far, buffers):
        y = links.dp % 2
        self.column, self.over_x, self.diagonal, self.sum_y, self.sum_x = buffers
        self.loads = [links.local(far.at[:, y], self.over_x), links.local(near.at[:, y], self.column)]
        self.first = links.copy(far.at[:, 1 - y], self.diagonal, Y)
        self.over_y = links.copy(near.at[:, 1 - y], self.sum_y, Y)
        self.along_x = links.copy(self.over_x, self.sum_x, X)

    def start(self):
        self.first.start()
        for copy in self.loads:
            copy.start()

    def second(self):
        self.first.wait_recv()
        self.over_y.start()

    def middle(self):
        for copy in self.loads:
            copy.wait()
        add_to(self.over_x, self.diagonal)
        self.along_x.start()

    def end(self):
        self.over_y.wait_recv()
        self.along_x.wait_recv()
        add_to(self.column, self.sum_y)
        add_to(self.column, self.sum_x)
        for copy in (self.first, self.over_y, self.along_x):
            copy.wait_send()


class Collect:
    def __init__(self, links, column, slots):
        z = links.dp // 2
        self.column, self.slots, self.z = column, slots, z
        m = column.shape[0]
        distances = z_distances(2 * m)[::-1]
        self.stages = []
        first = 0
        for step, distance in enumerate(distances):
            kept = [0]
            for other in distances[step + 1 :]:
                kept = kept + [k ^ other for k in kept]
            self.stages.append(
                [
                    (links.copy(column.at[z ^ distance ^ k], slots.at[first + i], ("dp", 2 * distance)), first + i, z ^ k)
                    for i, k in enumerate(kept)
                ]
            )
            first += len(kept)

    def start(self, step):
        for copy, _, _ in self.stages[step]:
            copy.start()

    def finish(self, step):
        for copy, slot, index in self.stages[step]:
            copy.wait_recv()
            self.column[index] = (self.column[index].astype(F32) + self.slots[slot].astype(F32)).astype(BF16)

    def drain(self):
        for stage in self.stages:
            for copy, _, _ in stage:
                copy.wait_send()


class Square:
    def __init__(self, links, shard, out):
        y = links.dp % 2
        c = shard.shape[1]
        low, high = pl.ds(0, c // 2), pl.ds(c // 2, c // 2)
        self.own = links.local(shard, out.at[0, y])
        self.first = [links.copy(shard, out.at[0, y], Y), links.copy(shard, out.at[1, y], X)]
        self.second = [
            links.copy(out.at[0, 1 - y, :, low], out.at[1, 1 - y, :, low], X),
            links.copy(out.at[1, y, :, high], out.at[1, y, :, high], Y),
        ]

    def start(self):
        for copy in self.first + [self.own]:
            copy.start()

    def middle(self):
        for copy in self.first:
            copy.wait_recv()
        for copy in self.second:
            copy.start()

    def end(self):
        for copy in self.first:
            copy.wait_send()
        for copy in self.second:
            copy.wait()
        self.own.wait()


class SpreadZ:
    def __init__(self, links, own, other, hold, whole, n):
        z = links.dp // 2
        distances = z_distances(n)
        there = z ^ distances[0]
        final, core = whole.at[0], whole.at[1]
        self.loads = [links.local(own, hold.at[0]), links.local(other, hold.at[1])]
        self.stores = [links.local(hold.at[0], final.at[z]), links.local(hold.at[1], final.at[there])]
        self.core = [links.copy(hold.at[0], core.at[z], CORE), links.copy(hold.at[1], core.at[there], CORE)]
        held = [(hold.at[0], z), (hold.at[1], there)]
        self.stages, self.core_stages = [], []
        for distance in distances[1:]:
            came = [index ^ distance for _, index in held]
            self.stages.append([links.copy(ref, final.at[index], ("dp", 2 * distance)) for ref, index in held])
            self.core_stages.append([links.copy(final.at[index], core.at[index], CORE) for index in came])
            held = held + [(final.at[index], index) for index in came]

    def start(self):
        for copy in self.loads:
            copy.start()
        for copy in self.loads:
            copy.wait()
        for copy in self.stages[0] + self.stores + self.core:
            copy.start()

    def end(self):
        for step, (stage, core_stage) in enumerate(zip(self.stages, self.core_stages)):
            for copy, onward in zip(stage, core_stage):
                copy.wait_recv()
                onward.start()
            for copy in self.stages[step + 1] if step + 1 < len(self.stages) else []:
                copy.start()
        for copy in self.stores + self.core:
            copy.wait()
        for stage, core_stage in zip(self.stages, self.core_stages):
            for copy in stage:
                copy.wait_send()
            for copy in core_stage:
                copy.wait()


def spread_z_copies(n):
    return 2 * n


class SpreadFar:
    def __init__(self, links, column, whole):
        y = links.dp % 2
        far, far_core = whole.at[0], whole.at[1]
        m, _, c = column.shape
        step = max(m // 4, 1)
        self.over_x, self.over_y, self.core_x, self.core_y = [], [], [], []
        for k in range(m // step):
            for h in range(2):
                z, part = pl.ds(k * step, step), pl.ds(h * (c // 2), c // 2)
                own = far.at[z, y, :, part]
                other = far.at[z, 1 - y, :, part]
                self.over_x.append(links.copy(column.at[z, :, part], own, X))
                self.over_y.append(links.copy(own, own, Y))
                self.core_x.append(links.copy(own, far_core.at[z, y, :, part], CORE))
                self.core_y.append(links.copy(other, far_core.at[z, 1 - y, :, part], CORE))

    def start(self):
        for copy in self.over_x:
            copy.start()

    def onward(self, k):
        self.over_x[k].wait_recv()
        self.over_y[k].start()
        self.core_x[k].start()

    def last(self, k):
        self.over_y[k].wait_recv()
        self.core_y[k].start()

    def end(self):
        for copy in self.over_x + self.over_y:
            copy.wait_send()
        for copy in self.core_x + self.core_y:
            copy.wait()


class RowSum:
    def __init__(self, links, terms, buffers):
        self.near, self.far, self.got_near, self.got_far, self.got_x = buffers
        count = self.near.shape[0]

        def rows(distance):
            start = pl.multiple_of((links.tensor ^ distance) * count, count)
            return terms.at[pl.ds(start, count)]

        self.loads = [links.local(rows(0), self.near), links.local(rows(2), self.far)]
        self.core = [links.copy(rows(3), self.got_far, CORE), links.copy(rows(1), self.got_near, CORE)]
        self.over_x = links.copy(self.far, self.got_x, X)

    def start(self):
        for copy in self.loads[::-1] + self.core:
            copy.start()

    def middle(self):
        self.loads[1].wait()
        self.core[0].wait_recv()

        def add(rows):
            self.far[rows, :] = (self.far[rows, :].astype(F32) + self.got_far[rows, :].astype(F32)).astype(BF16)

        by_rows(self.far.shape[0], 64, add)
        self.over_x.start()

    def end(self):
        self.loads[0].wait()
        self.core[1].wait_recv()
        self.over_x.wait_recv()
        for copy in self.core + [self.over_x]:
            copy.wait_send()

    def total(self, rows):
        return self.near[rows, :].astype(F32) + self.got_near[rows, :].astype(F32) + self.got_x[rows, :].astype(F32)


def row_sum_scratch(count, width):
    return [pltpu.VMEM((count, width), BF16)] * 5


class Everywhere:
    def __init__(self, links, held, slots, ways):
        self.held, self.slots = held, slots
        self.copies = [links.copy(held.at[k], slots.at[k], way) for k, way in enumerate(ways)]

    def start(self, step):
        self.copies[step].start()

    def finish(self, step):
        self.copies[step].wait()
        self.held[step + 1] = self.held[step] + self.slots[step]


def everywhere_ways(n):
    return [CORE, X, Y] + z_ways(n)


def everywhere_scratch(k, c, n):
    steps = len(everywhere_ways(n))
    return [pltpu.VMEM((steps + 1, k, c), F32), pltpu.VMEM((steps, k, c), F32)]


def tail_kernel(
    dq_ref, dk_ref, dv_ref, w_ref, first_hbm, wide_hbm, mt_hbm, rows_hbm, grad_hbm, cross_hbm, norm_ref,
    self_ref, ffn_ref, cq_ref, cv_ref, up_ref,
    grad_out, weights_out, late_out, cross_out, give, acc, weights,
    first_ref, wide_ref, mt_ref, rows_ref, grad_ref, cross_ref, cross_slots, *scratch, n, step_rows
):
    links = Links(*scratch[-3:])
    loads = [
        links.local(source, target)
        for source, target in (
            (cross_hbm, cross_ref), (first_hbm, first_ref), (wide_hbm, wide_ref), (mt_hbm, mt_ref),
            (rows_hbm, rows_ref), (grad_hbm, grad_ref),
        )
    ]
    for copy in loads:
        copy.start()
    cross = Collect(links, cross_ref, cross_slots)
    member = links.tensor
    near, far, got_near, got_far, got_x = scratch[:5]
    columns, gots, slots = scratch[5:7], scratch[7:9], scratch[9:11]
    held, late_slots, sums, early_slots = scratch[11:15]
    count, model = near.shape
    width = dq_ref.shape[1]
    y = links.dp % 2
    c = columns[0].shape[2]
    m, _, r, _ = weights.shape
    half = count // 2
    parts = [pl.ds(0, half), pl.ds(half, half)]
    core_far = links.copy(give.at[0], got_far, CORE)
    core_near = links.copy(give.at[1], got_near, CORE)
    over_x = [links.copy(far.at[part], got_x.at[part], X) for part in parts]
    over_y, collects = [], []
    for k, (column, got, slot) in enumerate(zip(columns, gots, slots)):
        over_y.append(links.copy(weights.at[:, 1 - y, :, pl.ds(k * c, c)], got, Y))
        collects.append(Collect(links, column, slot))
    stages = len(collects[0].stages)
    late = Everywhere(links, held, late_slots, everywhere_ways(n))
    early = Everywhere(links, sums, early_slots, [CORE] + z_ways(n) + [Y, X])
    steps = len(late.copies)
    links.greet(everywhere_ways(n))

    def terms(distance, target):
        base = (member ^ distance) * count

        def one(rows):
            there = pl.ds(pl.multiple_of(base + rows.start, 128), 128)
            total = dot_nt(dq_ref[there, :], w_ref[:, :width])
            total = total + dot_nt(dk_ref[there, :], w_ref[:, width : 2 * width])
            target[rows, :] = (total + dot_nt(dv_ref[there, :], w_ref[:, 2 * width : 3 * width])).astype(BF16)

        by_rows(count, 128, one)

    def packed(k):
        for block in range(2 * m):
            span = slice(block * r, (block + 1) * r)
            weights[block // 2, block % 2, :, k * c : (k + 1) * c] = acc[span, k * c : (k + 1) * c].astype(BF16)
        columns[k][...] = weights[:, y, :, k * c : (k + 1) * c]

    loads[0].wait()
    cross.start(0)
    acc[...] = jnp.zeros_like(acc)
    loads[1].wait()

    def products(refs, at):
        def one(rows):
            source = first_ref[rows, :].T
            for k, ref in enumerate(refs):
                acc[:, (at + k) * width : (at + k + 1) * width] += dot_nn(source, ref[rows, :])

        return one

    by_rows(dq_ref.shape[0], step_rows, products((dq_ref, dk_ref), 0))
    packed(0)
    over_y[0].start()
    terms(3, give.at[0])
    core_far.start()
    terms(2, far)
    core_far.wait_recv()
    for part, copy in zip(parts, over_x):

        def add(rows, part=part):
            there = pl.ds(pl.multiple_of(part.start + rows.start, 64), 64)
            far[there, :] = (far[there, :].astype(F32) + got_far[there, :].astype(F32)).astype(BF16)

        by_rows(half, 64, add)
        copy.start()
    for copy in loads[2:]:
        copy.wait()

    def products_out(rows):
        acc[:, 3 * width :] += dot_nn(wide_ref[rows, :].T, mt_ref[:, rows].T)

    by_rows(dq_ref.shape[0], step_rows, products((dv_ref,), 2))
    by_rows(dq_ref.shape[0], step_rows, products_out)
    packed(1)
    over_y[1].start()
    terms(1, give.at[1])
    core_near.start()
    terms(0, near)
    for step in range(stages - 1):
        cross.finish(step)
        cross.start(step + 1)

    held[0] = jnp.zeros(held.shape[1:], F32)
    sums[0] = jnp.zeros(sums.shape[1:], F32)
    sums[0, 0:2, :] = self_ref[0:2, :]
    sums[0, 2:4, :] = ffn_ref[0:2, :]
    sums[0, 6:7, :] = self_ref[2:3, :]
    sums[0, 9:11, :] = ffn_ref[2:4, :]
    for distance in range(4):
        there = pl.ds(pl.multiple_of((member ^ distance) * width, width), width)
        sums[0, 7:8, there] = cq_ref[distance]
        sums[0, 8:9, there] = cv_ref[distance]
        sums[0, pl.ds(11 + (member ^ distance), 1), :] = up_ref[distance]
    here = pl.ds(pl.multiple_of(member * width, width), width)

    def column_sums(rows):
        sums[0, 4:5, here] += jnp.sum(dq_ref[rows, :].astype(F32), axis=0, keepdims=True)
        sums[0, 5:6, here] += jnp.sum(dv_ref[rows, :].astype(F32), axis=0, keepdims=True)

    by_rows(dq_ref.shape[0], step_rows, column_sums)
    early.start(0)

    def norm_back(part):
        def one(rows):
            rows = pl.ds(pl.multiple_of(part.start + rows.start, 64), 64)
            incoming = near[rows, :].astype(F32) + got_near[rows, :].astype(F32) + got_x[rows, :].astype(F32)
            rows_grad, gain_terms = norm_rows_back(rows_ref[rows, :].astype(F32), incoming, norm_ref[0, 0:1, :])
            grad_out[rows, :] = rows_grad + grad_ref[rows, :]
            held[0, 0:1, :] += jnp.sum(gain_terms, axis=0, keepdims=True)
            held[0, 1:2, :] += jnp.sum(incoming, axis=0, keepdims=True)

        by_rows(half, 64, one)

    def summed_y(k):
        over_y[k].wait_recv()
        add_to(columns[k], gots[k])
        collects[k].start(0)

    def next_z(k):
        for step in range(stages - 1):
            collects[k].finish(step)
            collects[k].start(step + 1)

    def last_z(k):
        collects[k].finish(stages - 1)
        weights_out[:, k * c : (k + 1) * c] = columns[k][collects[k].z].astype(F32)

    summed_y(0)
    early.finish(0)
    cross.finish(stages - 1)
    cross_out[...] = cross_ref[cross.z].astype(F32)
    core_near.wait_recv()
    over_x[0].wait_recv()
    norm_back(parts[0])
    next_z(0)
    for step in range(1, steps - 2):
        early.start(step)
        early.finish(step)
    over_x[1].wait_recv()
    norm_back(parts[1])
    late.start(0)
    summed_y(1)
    late.finish(0)
    late.start(1)
    early.start(steps - 2)
    last_z(0)
    early.finish(steps - 2)
    late.finish(1)
    late.start(2)
    early.start(steps - 1)
    next_z(1)
    early.finish(steps - 1)
    late.finish(2)
    late_out[2:, :] = sums[steps]
    for step in range(3, steps):
        late.start(step)
        late.finish(step)
    last_z(1)
    late_out[0:2, :] = held[steps, 0:2, :]
    for copy in over_x + over_y + [core_near, core_far]:
        copy.wait_send()
    for collect in collects + [cross]:
        collect.drain()


def tail(
    dq, dk, dv, w, first, wide, mixed_t, rows, grad, cross_column, norm, self_sums, ffn_sums, cq_sums, cv_sums, up_sums
):
    n = lax.axis_size("dp")
    count, model = rows.shape
    width = dq.shape[1]
    m, r, c = n // 2, model // n, 4 * width
    vectors = (16, model)
    vmem = pl.BlockSpec(memory_space=pltpu.VMEM)
    part = pltpu.VMEM((m, r, c // 2), BF16)
    return pl.pallas_call(
        functools.partial(tail_kernel, n=n, step_rows=512),
        in_specs=[vmem] * 4 + [ANY] * 6 + [vmem] * 6,
        out_specs=[vmem] * 4,
        out_shape=[
            jax.ShapeDtypeStruct((count, model), F32),
            jax.ShapeDtypeStruct((r, c), F32),
            jax.ShapeDtypeStruct((vectors[0] + 2, model), F32),
            jax.ShapeDtypeStruct(cross_column.shape[1:], F32),
        ],
        scratch_shapes=[
            pltpu.VMEM((2, count, model), BF16),
            pltpu.VMEM((model, c), F32),
            pltpu.VMEM((m, 2, r, c), BF16),
        ]
        + [pltpu.VMEM(v.shape, v.dtype) for v in (first, wide, mixed_t, rows, grad, cross_column, cross_column)]
        + row_sum_scratch(count, model)
        + [part] * 6
        + everywhere_scratch(8, model, n)
        + everywhere_scratch(*vectors, n)
        + link_scratch(6 + 3 * m + 2 * len(everywhere_ways(n)), 6),
        compiler_params=pltpu.CompilerParams(
            vmem_limit_bytes=VMEM_LIMIT, collective_id=7, has_side_effects=True
        ),
        cost_estimate=pl.CostEstimate(flops=0, bytes_accessed=100 * 2**20, transcendentals=0),
        name="tail",
    )(
        dq, dk, dv, w, first, wide, mixed_t, rows, grad, cross_column, norm,
        self_sums, ffn_sums, cq_sums, cv_sums, up_sums,
    )


def results_kernel(
    output_ref, grad_ref, enc_ref, self_ref, cross_ref, up_ref, down_ref, vectors_ref,
    output_out, grad_out, enc_out, qkv_out, so_out, cq_out, ckv_out, co_out, up_out, down_out,
    norm_out, biases_out, shift_out, *, scale
):
    output_out[...] = output_ref[...]
    grad_out[...] = grad_ref[...]
    enc_out[...] = enc_ref[...]
    width = cq_out.shape[1]

    @pl.when(pl.program_id(0) == 0)
    def _():
        for k in range(3):
            qkv_out[:, k, :] = self_ref[:, k * width : (k + 1) * width] * scale
        so_out[...] = (self_ref[:, 3 * width :] * scale).T
        cq_out[...] = cross_ref[:, :width] * scale
        for k in range(2):
            ckv_out[:, k, :] = cross_ref[:, (k + 1) * width : (k + 2) * width] * scale
        co_out[...] = (cross_ref[:, 3 * width :] * scale).T
        up_out[...] = up_ref[...] * scale
        down_out[...] = (down_ref[...] * scale).T
        vectors = vectors_ref[...] * scale
        for k in range(3):
            norm_out[k] = vectors[2 * k : 2 * k + 2, :]
        biases_out[...] = vectors[6:13, :]
        lines = vectors.shape[1] // LANES
        for k in range(shift_out.shape[0]):
            part = slice(k % lines * LANES, (k % lines + 1) * LANES)
            shift_out[k : k + 1, :] = vectors[13 + k // lines : 14 + k // lines, part]


def results(output, grad, encoder, self_w, cross_w, up, down, vectors, scale):
    r, c = self_w.shape
    width = c // 4
    steps = 4

    def rows(value):
        return pl.BlockSpec((value.shape[0] // steps, value.shape[1]), lambda i: (i, 0))

    shapes = [(r, 3, width), (width, r), (r, width), (r, 2, width), (width, r), up.shape, down.shape[::-1]]
    shapes += [(3, 2, output.shape[1]), (7, output.shape[1]), (4 * up.shape[1] // LANES, LANES)]
    return pl.pallas_call(
        functools.partial(results_kernel, scale=scale),
        grid=(steps,),
        in_specs=[rows(output), rows(grad), rows(encoder)] + [const(v.shape) for v in (self_w, cross_w, up, down, vectors)],
        out_specs=[rows(output), rows(grad), rows(encoder)] + [const(shape) for shape in shapes],
        out_shape=[jax.ShapeDtypeStruct(v.shape, F32) for v in (output, grad, encoder)]
        + [jax.ShapeDtypeStruct(shape, F32) for shape in shapes],
        compiler_params=pltpu.CompilerParams(vmem_limit_bytes=VMEM_LIMIT),
        cost_estimate=pl.CostEstimate(flops=0, bytes_accessed=20 * 2**20, transcendentals=0),
        name="results",
    )(output, grad, encoder, self_w, cross_w, up, down, vectors)


def start_kernel(
    in_ref, norm_ref, qkv_ref, so_ref, cq_ref, ckv_ref, co_ref, down_ref,
    rows_out, self_out, cross_out, down_out, rows_ref, self_ref, cross_ref, shard_ref, send_sems, recv_sems, local_sems, *, n
):
    links = Links(send_sems, recv_sems, local_sems)
    member, z, y = links.tensor, links.dp // 2, links.dp % 2
    count = rows_ref.shape[0]
    half = count // 2
    parts = [pl.ds(0, half), pl.ds(half, half)]

    def place(distance):
        return rows_out.at[pl.ds(pl.multiple_of((member ^ distance) * count, count), count)]

    over_x = [links.copy(rows_ref.at[part], place(0).at[part], X) for part in parts]
    over_core = [links.copy(rows_ref, place(0), CORE)]
    over_core += [links.copy(place(2).at[part], place(2).at[part], CORE) for part in parts]
    self_stages = column_stages(links, self_ref, self_out.at[:, y], n)
    cross_stages = column_stages(links, cross_ref, cross_out, n)
    over_y = [links.copy(self_ref, self_out.at[z, y], Y)]
    local = [
        links.local(rows_ref, place(0)),
        links.local(self_ref, self_out.at[z, y]),
        links.local(cross_ref, cross_out.at[z]),
    ]
    width = cq_ref.shape[1]
    for k in range(3):
        self_ref[:, k * width : (k + 1) * width] = qkv_ref[:, k, :]
    self_ref[:, 3 * width :] = so_ref[...].T
    cross_ref[:, :width] = cq_ref[...]
    for k in range(2):
        cross_ref[:, (k + 1) * width : (k + 2) * width] = ckv_ref[:, k, :]
    cross_ref[:, 3 * width :] = co_ref[...].T
    shard_ref[...] = down_ref[...].T
    square = Square(links, shard_ref, down_out)
    links.greet([CORE, X, Y] + z_ways(n))
    for copy in over_y + local[1:]:
        copy.start()
    for copy, _ in self_stages[0]:
        copy.start()
    for part, copy in zip(parts, over_x):

        def norm(rows, part=part):
            rows = pl.ds(pl.multiple_of(part.start + rows.start, 64), 64)
            xhat, _ = normalized(in_ref[rows, :].astype(F32))
            rows_ref[rows, :] = (xhat * norm_ref[0, 0:1, :] + norm_ref[0, 1:2, :]).astype(BF16)

        by_rows(half, 64, norm)
        copy.start()
    for copy in local[:1] + over_core[:1]:
        copy.start()
    square.start()
    for self_stage in self_stages:
        if self_stage is not self_stages[0]:
            for copy, _ in self_stage:
                copy.start()
        for copy, index in self_stage:
            copy.wait_recv()
            onward = links.copy(self_out.at[index, y], self_out.at[index, y], Y)
            onward.start()
            over_y.append(onward)
        if self_stage is self_stages[0]:
            for copy, _ in cross_stages[0]:
                copy.start()
    for cross_stage, later in zip(cross_stages, cross_stages[1:] + [[]]):
        for copy, _ in cross_stage:
            copy.wait_recv()
        for copy, _ in later:
            copy.start()
    for copy, onward in zip(over_x, over_core[1:]):
        copy.wait_recv()
        onward.start()
    square.middle()
    square.end()
    for copy in local + over_y + over_core:
        copy.wait()
    for copy in over_x:
        copy.wait_send()
    for stage in self_stages + cross_stages:
        for copy, _ in stage:
            copy.wait_send()


def start_gather(rows, norm, qkv, self_out, cross_q, cross_kv, cross_out, down):
    n = lax.axis_size("dp")
    r, c = cross_q.shape[0], 4 * cross_q.shape[1]
    return pl.pallas_call(
        functools.partial(start_kernel, n=n),
        in_specs=[pl.BlockSpec(memory_space=pltpu.VMEM)] * 8,
        out_specs=[ANY] * 4,
        out_shape=[
            jax.ShapeDtypeStruct((4 * rows.shape[0], rows.shape[1]), BF16),
            jax.ShapeDtypeStruct((n // 2, 2, r, c), BF16),
            jax.ShapeDtypeStruct((n // 2, r, c), BF16),
            jax.ShapeDtypeStruct((2, 2, r, down.shape[0]), BF16),
        ],
        scratch_shapes=[pltpu.VMEM(rows.shape, BF16)]
        + [pltpu.VMEM((r, c), BF16)] * 2
        + [pltpu.VMEM((r, down.shape[0]), BF16)]
        + link_scratch(2 * n + 12, 4),
        compiler_params=pltpu.CompilerParams(
            vmem_limit_bytes=VMEM_LIMIT, collective_id=0, has_side_effects=True
        ),
        cost_estimate=pl.CostEstimate(flops=0, bytes_accessed=100 * 2**20, transcendentals=0),
        name="start_gather",
    )(rows, norm, qkv, self_out, cross_q, cross_kv, cross_out, down)


def self_forward_kernel(
    b_ref, x_ref, w_ref, biases_ref, column_ref, up_ref, down_ref,
    q_out, k_ref, v_out, kt_out, ot_ref, lse_ref, terms_ref, whole, next_column, far_down,
    vt_ref, m_s, l_s, acc, column, send_sems, recv_sems, local_sems, *, heads, safe, n
):
    i = pl.program_id(0)
    last = pl.num_programs(0) - 1
    bq, width = q_out.shape
    links = Links(send_sems, recv_sems, local_sems)
    spread = Spread(links, column_ref, column, whole)
    stages = column_stages(links, up_ref, next_column, n)
    keep = links.local(up_ref, next_column.at[links.dp // 2])
    over_z = links.copy(down_ref.at[0], far_down, z_ways(n)[0])

    def next_stage(step):
        for copy, _ in stages[step]:
            copy.wait_recv()
        for copy, _ in stages[step + 1] if step + 1 < len(stages) else []:
            copy.start()

    @pl.when(i == 0)
    def _():
        links.greet([CORE, X, Y] + z_ways(n))
        for copy, _ in stages[0]:
            copy.start()
        spread.start()
        keep.start()

    def onward():
        next_stage(0)
        over_z.start()

    mine = pl.ds(pl.multiple_of(links.tensor * width, width), width)
    projected = dot_nn(x_ref[...], w_ref[:, : 3 * width])
    query = (projected[:, :width] + biases_ref[0:1, mine]).astype(BF16)
    key = projected[:, width : 2 * width].astype(BF16)
    value = (projected[:, 2 * width :] + biases_ref[1:2, mine]).astype(BF16)
    here = pl.ds(pl.multiple_of(i * bq, bq), bq)
    q_out[...] = query
    v_out[...] = value
    kt_out[...] = key.T
    k_ref[here, :] = key
    vt_ref[:, here] = value.T

    m_s[...] = jnp.full_like(m_s, NEGATIVE)
    l_s[...] = jnp.zeros_like(l_s)
    acc[...] = jnp.zeros_like(acc)
    hd = width // heads
    scaled = query * jnp.asarray(1.0 / math.sqrt(hd), BF16)
    q_heads = [head_only(scaled, h, hd) for h in range(heads)]

    def block(first, size, skip, mode):
        rows = pl.ds(pl.multiple_of(first, size), size)
        m_old = m_s[:, skip:]
        l_old = l_s[:, skip:]
        scores = [dot_nt(k_ref[rows, lanes_of(h, hd)[1]], q_heads[h][skip:]) for h in range(heads)]
        if mode != "none":
            bad = self_bad(b_ref, i * bq + skip, first, bq - skip, size, mode == "causal")
            scores = [jnp.where(bad, NEGATIVE, s) for s in scores]
        m_out, l_out, a_out = [], [], []
        for h in range(heads):
            part = slice(h * hd, (h + 1) * hd)
            m_new = jnp.maximum(m_old[h : h + 1, :], jnp.max(scores[h], axis=0, keepdims=True))
            shrink = jnp.exp(m_old[h : h + 1, :] - m_new)
            expos = jnp.exp(scores[h] - m_new)
            l_out.append(l_old[h : h + 1, :] * shrink + jnp.sum(expos, axis=0, keepdims=True))
            m_out.append(m_new)
            a_out.append(acc[part, skip:] * shrink + dot_nn(vt_ref[part, rows], expos.astype(BF16)))
        m_s[:, skip:] = jnp.concatenate(m_out, 0)
        l_s[:, skip:] = jnp.concatenate(l_out, 0)
        for h in range(heads):
            acc[h * hd : (h + 1) * hd, skip:] = a_out[h]

    over_keys(i, bq, safe, block, [(2, 0, onward), (3, 2, spread.middle), (4, 3, spread.last)])
    inverse = 1.0 / l_s[...]
    for h in range(heads):
        part = slice(h * hd, (h + 1) * hd)
        ot_ref[part, :] = (acc[part, :] * inverse[h : h + 1, :]).astype(BF16)
    lse_ref[...] = m_s[...] + jnp.log(l_s[...])
    terms_ref[...] = dot_nt(ot_ref[...].T, w_ref[:, 3 * width :]).astype(BF16)

    @pl.when(i == last)
    def _():
        for step in range(1, len(stages)):
            next_stage(step)
        over_z.wait()
        spread.end()
        for stage in stages:
            for copy, _ in stage:
                copy.wait_send()
        keep.wait()


def self_forward(bounds, x, w, biases, column, up, down, heads, safe):
    n, model = x.shape
    width = w.shape[1] // 4
    bq = 512
    dp = lax.axis_size("dp")
    m, r, c = column.shape
    by_rows_spec = pl.BlockSpec((bq, width), lambda i: (i, 0))
    by_columns_spec = pl.BlockSpec((width, bq), lambda i: (0, i))
    return pl.pallas_call(
        functools.partial(self_forward_kernel, heads=heads, safe=safe, n=dp),
        grid=(n // bq,),
        in_specs=[
            pl.BlockSpec(memory_space=pltpu.SMEM),
            pl.BlockSpec((bq, model), lambda i: (i, 0)),
            const((model, 4 * width)),
            const(biases.shape),
            ANY,
            const(up.shape),
            ANY,
        ],
        out_specs=[
            by_rows_spec,
            const((n, width)),
            by_rows_spec,
            by_columns_spec,
            by_columns_spec,
            pl.BlockSpec((heads, bq), lambda i: (0, i)),
            pl.BlockSpec((bq, model), lambda i: (i, 0)),
            ANY,
            ANY,
            ANY,
        ],
        out_shape=[
            jax.ShapeDtypeStruct((n, width), BF16),
            jax.ShapeDtypeStruct((n, width), BF16),
            jax.ShapeDtypeStruct((n, width), BF16),
            jax.ShapeDtypeStruct((width, n), BF16),
            jax.ShapeDtypeStruct((width, n), BF16),
            jax.ShapeDtypeStruct((heads, n), F32),
            jax.ShapeDtypeStruct((n, model), BF16),
            jax.ShapeDtypeStruct((4, m, 2, r, c), BF16),
            jax.ShapeDtypeStruct((m,) + up.shape, BF16),
            jax.ShapeDtypeStruct(down.shape[1:], BF16),
        ],
        scratch_shapes=[
            pltpu.VMEM((width, n), BF16),
            pltpu.VMEM((heads, bq), F32),
            pltpu.VMEM((heads, bq), F32),
            pltpu.VMEM((width, bq), F32),
            pltpu.VMEM((m, r, c), BF16),
        ]
        + link_scratch(9 + m, 3),
        compiler_params=pltpu.CompilerParams(
            vmem_limit_bytes=VMEM_LIMIT, collective_id=1, has_side_effects=True
        ),
        cost_estimate=pl.CostEstimate(
            flops=12 * n * n * width, bytes_accessed=8 * n * width, transcendentals=n * n * heads // 2
        ),
        name="self_forward",
    )(bounds, x, w, biases, column, up, down)


def after_self_kernel(
    terms_ref, rows_ref, biases_ref, norm_ref, column_ref, enc_ref, down_ref, from_z,
    after_out, second_out, whole_out, enc_out, down_out, far_down, *scratch, n
):
    links = Links(*scratch[-3:])
    rows_sum = RowSum(links, terms_ref, scratch[:5])
    column = scratch[5]
    spread = SpreadZ(links, down_ref.at[0], from_z, scratch[6], down_out, n)
    over_z = links.copy(down_ref.at[1], far_down, z_ways(n)[0])
    y = links.dp % 2
    near_out, core_out = whole_out.at[0], whole_out.at[1]
    load = links.local(column_ref, column)
    own = links.local(column, near_out.at[:, y])
    over_y = links.copy(column, near_out.at[:, y], Y)
    over_core = [
        links.copy(column, core_out.at[:, y], CORE),
        links.copy(near_out.at[:, 1 - y], core_out.at[:, 1 - y], CORE),
    ]
    enc_count = enc_ref.shape[0]

    def place(distance):
        return enc_out.at[pl.ds(pl.multiple_of((links.tensor ^ distance) * enc_count, enc_count), enc_count)]

    enc_x = links.copy(enc_ref, place(0), X)
    enc_core = [links.copy(enc_ref, place(0), CORE), links.copy(place(2), place(2), CORE)]
    enc_own = links.local(enc_ref, place(0))
    links.greet([CORE, X, Y] + z_ways(n))
    enc_x.start()
    rows_sum.start()
    load.start()
    over_z.start()
    load.wait()
    over_y.start()
    own.start()
    enc_own.start()
    spread.start()
    rows_sum.middle()
    over_core[0].start()
    enc_core[0].start()
    enc_x.wait_recv()
    enc_core[1].start()
    rows_sum.end()

    def norm(rows):
        after = rows_ref[rows, :].astype(F32) + rows_sum.total(rows) + biases_ref[2:3, :]
        after_out[rows, :] = after
        xhat, _ = normalized(after)
        second_out[rows, :] = (xhat * norm_ref[1, 0:1, :] + norm_ref[1, 1:2, :]).astype(BF16)

    by_rows(after_out.shape[0], 64, norm)
    over_y.wait_recv()
    over_core[1].start()
    enc_x.wait_send()
    over_y.wait_send()
    spread.end()
    over_z.wait()
    for copy in [own, enc_own] + over_core + enc_core:
        copy.wait()


def sum_after_self(terms, rows, biases, norm, column, encoder, down, from_z):
    count, model = rows.shape
    m, r, c = column.shape
    vmem = pl.BlockSpec(memory_space=pltpu.VMEM)
    return pl.pallas_call(
        functools.partial(after_self_kernel, n=2 * m),
        in_specs=[ANY, vmem, vmem, vmem, ANY, vmem, ANY, ANY],
        out_specs=[vmem, vmem, ANY, ANY, ANY, ANY],
        out_shape=[
            jax.ShapeDtypeStruct((count, model), F32),
            jax.ShapeDtypeStruct((count, model), BF16),
            jax.ShapeDtypeStruct((2, m, 2, r, c), BF16),
            jax.ShapeDtypeStruct((4 * encoder.shape[0], model), BF16),
            jax.ShapeDtypeStruct((2, m, 2, r, c), BF16),
            jax.ShapeDtypeStruct((2, r, c), BF16),
        ],
        scratch_shapes=row_sum_scratch(count, model)
        + [pltpu.VMEM((m, r, c), BF16), pltpu.VMEM((2, 2, r, c), BF16)]
        + link_scratch(10 + spread_z_copies(2 * m), 9),
        compiler_params=pltpu.CompilerParams(
            vmem_limit_bytes=VMEM_LIMIT, collective_id=8, has_side_effects=True
        ),
        cost_estimate=pl.CostEstimate(flops=0, bytes_accessed=100 * 2**20, transcendentals=0),
        name="sum_after_self",
    )(terms, rows, biases, norm, column, encoder, down, from_z)


def self_backward_kernel(
    b_ref, q_ref, k_ref, v_ref, kt_ref, w_ref, mt_ref, lse_ref, back_ref, rows_ref, above_ref, norm_ref,
    up_ref, down_ref, cross_ref, enc_ref,
    dq_ref, dk_ref, dv_ref, wide_out, grad_out, sums_ref, up_out, down_out, cross_out, enc_out,
    dka, dva, dqa, wide, *scratch, bq, heads, safe, n
):
    s = pl.program_id(0)
    last = pl.num_programs(0) - 1
    links = Links(*scratch[-3:])
    member = links.tensor
    x = member // 2
    later = (s // 2 + 1) // 2
    i = s * (1 - x) + ((s + 3) * (1 - later) + (4 - s) * later) * x
    cross = GatherLast(links, cross_ref.at[0], cross_ref.at[1], scratch[:5])
    keep_cross = links.local(cross.column, cross_out)
    columns, slots = scratch[5:7], scratch[7:9]
    sums_z = [Collect(links, column, slot) for column, slot in zip(columns, slots)]
    load_z = [links.local(ref, column) for ref, column in zip((up_ref, down_ref), columns)]
    enc = RowSum(links, enc_ref, scratch[9:14])
    stages = len(sums_z[0].stages)
    count = grad_out.shape[0]
    half = count // 2

    def place(distance, k=None):
        start = (member ^ distance) * count
        if k is None:
            return wide.at[pl.ds(pl.multiple_of(start, half), count)]
        return wide.at[pl.ds(pl.multiple_of(start + k * half, half), half)]

    over_x = [links.copy(place(0, k), place(0, k), X) for k in range(2)]
    over_core = links.copy(place(0), place(0), CORE)
    onward = [links.copy(place(2, k), place(2, k), CORE) for k in range(2)]
    keep_wide = links.local(wide, wide_out)

    def norm_back(k):
        def one(rows):
            rows = pl.ds(pl.multiple_of(k * half + rows.start, 64), 64)
            incoming = back_ref[rows, :]
            rows_grad, gain_terms = norm_rows_back(rows_ref[rows, :], incoming, norm_ref[1, 0:1, :])
            rows_grad = rows_grad + above_ref[rows, :]
            rounded = rows_grad.astype(BF16)
            grad_out[rows, :] = rows_grad
            wide[pl.ds(pl.multiple_of(member * count + rows.start, 64), 64), :] = rounded
            for row, terms in enumerate((gain_terms, incoming, rounded.astype(F32))):
                sums_ref[row : row + 1, :] += jnp.sum(terms, axis=0, keepdims=True)

        by_rows(half, 64, one)

    def arrive(k):
        over_x[k].wait_recv()
        onward[k].start()
        onward[k].wait_recv()

    @pl.when(s == 0)
    def _():
        links.greet([CORE, X, Y] + z_ways(n))
        for copy in load_z:
            copy.start()
        sums_ref[...] = jnp.zeros_like(sums_ref)
        for k in range(2):
            norm_back(k)
            over_x[k].start()
        over_core.start()
        cross.start()
        enc.start()
        for copy, total in zip(load_z, sums_z):
            copy.wait()
            total.start(0)
        dka[...] = jnp.zeros_like(dka)
        dva[...] = jnp.zeros_like(dva)
        over_core.wait_recv()

    @pl.when(s == 2)
    def _():
        arrive(0)
        pl.when(x == 1)(functools.partial(arrive, 1))
        cross.second()
        enc.middle()
        for step in range(stages - 1):
            for total in sums_z:
                total.finish(step)
            for total in sums_z:
                total.start(step + 1)

    @pl.when(s == 3)
    def _():
        pl.when(x == 0)(functools.partial(arrive, 1))
        cross.middle()
        keep_wide.start()

    width = k_ref.shape[1]
    hd = width // heads
    scale = 1.0 / math.sqrt(hd)
    here = pl.ds(pl.multiple_of(i * bq, bq), bq)
    grads = dot_nn(wide[here, :], w_ref[:, 3 * width :]).astype(BF16)
    products = grads.T.astype(F32) * mt_ref[:, here].astype(F32)
    inner = [jnp.sum(products[h * hd : (h + 1) * hd, :], axis=0, keepdims=True) for h in range(heads)]
    scaled = q_ref[here, :] * jnp.asarray(scale, BF16)
    q_heads = [head_only(scaled, h, hd) for h in range(heads)]
    d_heads = [head_only(grads, h, hd) for h in range(heads)]
    lse = lse_ref[:, here]
    dqa[...] = jnp.zeros_like(dqa)

    def block(first, size, skip, mode):
        rows = pl.ds(pl.multiple_of(first, size), size)
        scores = [dot_nt(k_ref[rows, lanes_of(h, hd)[1]], q_heads[h][skip:]) for h in range(heads)]
        dprobs = [dot_nt(v_ref[rows, lanes_of(h, hd)[1]], d_heads[h][skip:]) for h in range(heads)]
        if mode != "none":
            bad = self_bad(b_ref, i * bq + skip, first, bq - skip, size, mode == "causal")
            scores = [jnp.where(bad, NEGATIVE, s) for s in scores]
        dv_sums, dk_sums = {}, {}
        for h in range(heads):
            part = slice(h * hd, (h + 1) * hd)
            group, _ = lanes_of(h, hd)
            probs = jnp.exp(scores[h] - lse[h : h + 1, skip:])
            ds = (probs * (dprobs[h] - inner[h][:, skip:])).astype(BF16)
            add_group(dv_sums, group, dot_nn(probs.astype(BF16), d_heads[h][skip:]))
            add_group(dk_sums, group, dot_nn(ds, q_heads[h][skip:]))
            dqa[part, skip:] += dot_nn(kt_ref[part, rows], ds)
        for group in dv_sums:
            part = slice(group * LANES, (group + 1) * LANES)
            dva[rows, part] += dv_sums[group]
            dka[rows, part] += dk_sums[group]

    over_keys(i, bq, safe, block)
    dq_ref[here, :] = (dqa[...] * scale).astype(BF16).T

    @pl.when(s == last)
    def _():
        dk_ref[...] = dka[...].astype(BF16)
        dv_ref[...] = dva[...].astype(BF16)
        cross.end()
        keep_cross.start()
        for total, out in zip(sums_z, (up_out, down_out)):
            total.finish(stages - 1)
            out[...] = total.column[total.z].astype(F32)
            total.drain()
        enc.end()

        def store(rows):
            enc_out[rows, :] = enc.total(rows)

        by_rows(enc_out.shape[0], 64, store)
        for copy in over_x + onward + [over_core]:
            copy.wait_send()
        keep_wide.wait()
        keep_cross.wait()


def self_backward(
    bounds, queries, keys, values, keys_t, w, mixed_t, lse, back, rows, above, norm,
    up_column, down_column, cross_sum, enc_terms, heads, safe
):
    n, width = queries.shape
    count, model = rows.shape
    dp = lax.axis_size("dp")
    m, r, c = up_column.shape
    cross_c = cross_sum.shape[4]
    enc_shape = (enc_terms.shape[0] // 4, enc_terms.shape[1])
    bq = 512
    return pl.pallas_call(
        functools.partial(self_backward_kernel, bq=bq, heads=heads, safe=safe, n=dp),
        grid=(n // bq,),
        in_specs=[
            pl.BlockSpec(memory_space=pltpu.SMEM),
            const((n, width)),
            const((n, width)),
            const((n, width)),
            const((width, n)),
            const((model, 4 * width)),
            const((width, n)),
            const((heads, n)),
            const((count, model)),
            const((count, model)),
            const((count, model)),
            const(norm.shape),
        ]
        + [ANY] * 4,
        out_specs=[const((n, width))] * 3
        + [ANY, const((count, model)), const((8, model)), const((r, c)), const((r, c)), ANY, const(enc_shape)],
        out_shape=[jax.ShapeDtypeStruct((n, width), BF16)] * 3
        + [
            jax.ShapeDtypeStruct((n, model), BF16),
            jax.ShapeDtypeStruct((count, model), F32),
            jax.ShapeDtypeStruct((8, model), F32),
            jax.ShapeDtypeStruct((r, c), F32),
            jax.ShapeDtypeStruct((r, c), F32),
            jax.ShapeDtypeStruct((m, r, cross_c), BF16),
            jax.ShapeDtypeStruct(enc_shape, F32),
        ],
        scratch_shapes=[
            pltpu.VMEM((n, width), F32),
            pltpu.VMEM((n, width), F32),
            pltpu.VMEM((width, bq), F32),
            pltpu.VMEM((n, model), BF16),
        ]
        + [pltpu.VMEM((m, r, cross_c), BF16)] * 5
        + [pltpu.VMEM((m, r, c), BF16)] * 4
        + row_sum_scratch(*enc_shape)
        + link_scratch(11 + 2 * m, 8),
        compiler_params=pltpu.CompilerParams(
            vmem_limit_bytes=62 * 2**20, collective_id=5, has_side_effects=True
        ),
        cost_estimate=pl.CostEstimate(
            flops=24 * n * n * width, bytes_accessed=16 * n * width, transcendentals=n * n * heads // 2
        ),
        name="self_backward",
    )(
        bounds, queries, keys, values, keys_t, w, mixed_t, lse, back, rows, above, norm,
        up_column, down_column, cross_sum, enc_terms,
    )


def const(shape):
    return pl.BlockSpec(shape, lambda *_: (0,) * len(shape), pipeline_mode=pl.Buffered(1))


def normalized(rows):
    center = rows - jnp.mean(rows, axis=-1, keepdims=True)
    scale = lax.rsqrt(jnp.mean(center * center, axis=-1, keepdims=True) + EPSILON)
    return center * scale, scale


def norm_rows_back(rows, incoming, gain):
    xhat, scale = normalized(rows)
    e = incoming * gain
    inner = jnp.mean(e * xhat, axis=-1, keepdims=True)
    return scale * (e - jnp.mean(e, axis=-1, keepdims=True) - xhat * inner), incoming * xhat


def by_rows(count, step, body):
    def one(k, c):
        body(pl.ds(pl.multiple_of(k * step, step), step))
        return c

    lax.fori_loop(0, count // step, one, 0)


def cross_forward_kernel(
    len_ref, x_ref, enc_ref, w_ref, biases_ref, rows_ref, norm_ref, column_ref, down_ref, from_z,
    q_out, k_out, v_out, ot_ref, lse_ref, after_ref, third_ref, whole, down_out, hold, send_sems, recv_sems, local_sems, *, heads, n
):
    i = pl.program_id(0)
    last = pl.num_programs(0) - 1
    links = Links(send_sems, recv_sems, local_sems)
    spread = SpreadFar(links, column_ref, whole)
    pieces = len(spread.over_x)
    spread_z = SpreadZ(links, down_ref.at[1], from_z, hold, down_out, n)

    @pl.when(i == 0)
    def _():
        links.greet([CORE, X, Y] + z_ways(n))
        spread.start()
        spread_z.start()
        after_ref[...] = rows_ref[...] + biases_ref[5:6, :]

    def onward(*when):
        for step, k in when:
            pl.when(i == step)(functools.partial(spread.onward, k))

    onward((1, 0), (1, 1), (2, 3), (3, 5))

    width = q_out.shape[2]
    hd = width // heads
    mine = pl.ds(pl.multiple_of((links.tensor ^ i) * width, width), width)
    query = (dot_nn(x_ref[...], w_ref[0, :, :width]) + biases_ref[3:4, mine]).astype(BF16)
    key_value = dot_nn(enc_ref[...], w_ref[0, :, width : 3 * width])
    keys = key_value[:, :width].astype(BF16)
    values = (key_value[:, width:] + biases_ref[4:5, mine]).astype(BF16)
    q_out[0] = query
    k_out[0] = keys
    v_out[0] = values
    values_t = values.T
    scaled = query * jnp.asarray(1.0 / math.sqrt(hd), BF16)
    ok = lax.broadcasted_iota(jnp.int32, (keys.shape[0], 1), 0) < len_ref[0]
    scores = [dot_nt(keys[:, lanes_of(h, hd)[1]], head_only(scaled, h, hd)) for h in range(heads)]
    mixed = []
    for h in range(heads):
        part = slice(h * hd, (h + 1) * hd)
        s = jnp.where(ok, scores[h], NEGATIVE)
        largest = jnp.max(s, axis=0, keepdims=True)
        expos = jnp.exp(s - largest)
        total = jnp.sum(expos, axis=0, keepdims=True)
        mixed.append((dot_nn(values_t[part, :], expos.astype(BF16)) * (1.0 / total)).astype(BF16))
        ot_ref[0, part, :] = mixed[h]
        lse_ref[0, h : h + 1, :] = largest + jnp.log(total)
        if h == heads // 2 - 1:
            onward((1, 2), (2, 4), (3, 6))
    after_ref[...] += dot_nt(jnp.concatenate(mixed, 0).T, w_ref[0, :, 3 * width :])

    @pl.when(i == last)
    def _():
        def norm(rows):
            xhat, _ = normalized(after_ref[rows, :])
            third_ref[rows, :] = (xhat * norm_ref[2, 0:1, :] + norm_ref[2, 1:2, :]).astype(BF16)

        by_rows(after_ref.shape[0], 128, norm)
        for k in range(7, pieces):
            spread.onward(k)
        for k in range(pieces):
            spread.last(k)
        spread_z.end()
        spread.end()


def cross_forward(lengths, x, encoder, weights, biases, rows, norm, column, down, from_z, heads):
    count, model = x.shape
    n = encoder.shape[0]
    parts, _, columns = weights.shape
    width = columns // 4
    m, r, c = column.shape

    def by_part(*shape):
        return pl.BlockSpec((1,) + shape, lambda i: (i,) + (0,) * len(shape))

    return pl.pallas_call(
        functools.partial(cross_forward_kernel, heads=heads, n=2 * m),
        grid=(parts,),
        in_specs=[
            pl.BlockSpec(memory_space=pltpu.SMEM),
            const((count, model)),
            const((n, model)),
            by_part(model, columns),
            const(biases.shape),
            const((count, model)),
            const(norm.shape),
            ANY,
            ANY,
            ANY,
        ],
        out_specs=[
            by_part(count, width),
            by_part(n, width),
            by_part(n, width),
            by_part(width, count),
            by_part(heads, count),
            const((count, model)),
            const((count, model)),
            ANY,
            ANY,
        ],
        out_shape=[
            jax.ShapeDtypeStruct((parts, count, width), BF16),
            jax.ShapeDtypeStruct((parts, n, width), BF16),
            jax.ShapeDtypeStruct((parts, n, width), BF16),
            jax.ShapeDtypeStruct((parts, width, count), BF16),
            jax.ShapeDtypeStruct((parts, heads, count), F32),
            jax.ShapeDtypeStruct((count, model), F32),
            jax.ShapeDtypeStruct((count, model), BF16),
            jax.ShapeDtypeStruct((2, m, 2, r, c), BF16),
            jax.ShapeDtypeStruct((2, m, 2, r, c), BF16),
        ],
        scratch_shapes=[pltpu.VMEM((2, 2, r, c), BF16)] + link_scratch(32 + spread_z_copies(2 * m), 4),
        compiler_params=pltpu.CompilerParams(
            vmem_limit_bytes=VMEM_LIMIT, collective_id=2, has_side_effects=True
        ),
        cost_estimate=pl.CostEstimate(
            flops=24 * parts * count * n * width,
            bytes_accessed=8 * parts * n * width,
            transcendentals=parts * count * n * heads,
        ),
        name="cross_forward",
    )(lengths, x, encoder, weights, biases, rows, norm, column, down, from_z)


def feed_forward_kernel(
    x_ref, dy_ref, near_up, near_down, far_up, far_down, b_ref, after_ref, biases_ref, norm_ref,
    out_ref, rows_out, low_out, sums_ref, gup_ref, gdown_ref, bias_ref, from_x, from_y,
    xt_ref, dyt_ref, back_ref, give, got, diagonal, loaded, load_sems, send_sems, recv_sems, local_sems, *, chunks
):
    s = pl.program_id(0)
    links = Links(send_sems, recv_sems, local_sems)
    turn = s // chunks
    chunk = s % chunks
    pair = turn // 2
    slot = pair * chunks + chunk
    theirs = turn % 2 == 0
    y = links.dp % 2
    m, r = diagonal.shape[1], diagonal.shape[2]
    low, high = pl.ds(0, m // 2), pl.ds(m // 2, m - m // 2)
    links.used = 2 * chunks
    across = [
        links.copy(diagonal.at[:, low], from_x, X),
        links.copy(diagonal.at[:, high], from_y, Y),
    ]
    to_core = pltpu.make_async_remote_copy(
        src_ref=give.at[chunk],
        dst_ref=got.at[slot],
        send_sem=send_sems.at[slot],
        recv_sem=recv_sems.at[slot],
        device_id=links.partner(CORE),
        device_id_type=pl.DeviceIdType.MESH,
    )

    size = loaded.shape[3]

    def fetch(step, act):
        block = 3 - step // chunks
        slot = step % 2
        first = (step % chunks) * size

        def both(*sources):
            for k, source in enumerate(sources):
                columns = pl.ds(pl.multiple_of(first, size), size)
                act(pltpu.make_async_copy(source.at[:, columns], loaded.at[slot, k], load_sems.at[slot, k]))

        @pl.when(block >= 2)
        def _():
            both(far_up.at[block - 2], far_down.at[block - 2])

        @pl.when(block < 2)
        def _():
            both(near_up.at[block], near_down.at[block])

    @pl.when(s == 0)
    def _():
        fetch(0, lambda copy: copy.start())
        links.greet([CORE, X, Y])
        out_ref[...] = after_ref[...] + biases_ref[6:7, :]
        back_ref[...] = jnp.zeros_like(back_ref)
        xt_ref[...] = x_ref[...].T
        dyt_ref[...] = dy_ref[...].T
        sums_ref[...] = jnp.zeros_like(sums_ref)

    fetch(s, lambda copy: copy.wait())

    @pl.when(s + 1 < pl.num_programs(0))
    def _():
        fetch(s + 1, lambda copy: copy.start())

    up_ref, down_ref = loaded.at[s % 2, 0], loaded.at[s % 2, 1]
    lines = size // LANES
    line = ((links.tensor ^ (3 - turn)) * chunks + chunk) * lines
    shift = jnp.concatenate([b_ref[pl.ds(line + k, 1), :] for k in range(lines)], axis=1)
    pre_act = dot_nn(x_ref[...], up_ref[...]) + shift
    hidden_grad = dot_nn(dy_ref[...], down_ref[...])
    normal_cdf = 0.5 * (1.0 + lax.erf(pre_act * (1.0 / math.sqrt(2.0))))
    density = jnp.exp(-0.5 * pre_act * pre_act) * (1.0 / math.sqrt(2.0 * math.pi))
    hidden = (pre_act * normal_cdf).astype(BF16)
    pre_grad = (hidden_grad * (normal_cdf + pre_act * density)).astype(BF16)
    bias_ref[0] = jnp.sum(pre_grad.astype(F32), axis=0, keepdims=True)

    @pl.when(turn % 2 == 1)
    def _():
        to_core.wait_send()

    give[chunk, 0] = dot_nn(xt_ref[...], pre_grad).astype(BF16)
    give[chunk, 1] = dot_nn(dyt_ref[...], hidden).astype(BF16)
    out_ref[...] += dot_nt(hidden, down_ref[...])
    back_ref[...] += dot_nt(pre_grad, up_ref[...])

    @pl.when(theirs)
    def _():
        to_core.start()

    @pl.when(jnp.logical_not(theirs))
    def _():
        to_core.wait_recv()
        gup_ref[0] = (give[chunk, 0].astype(F32) + got[slot, 0].astype(F32)).astype(BF16)
        gdown_ref[0] = (give[chunk, 1].astype(F32) + got[slot, 1].astype(F32)).astype(BF16)

    for k in range(chunks):

        @pl.when(s == chunks + k)
        def _():
            def keep(z, carry):
                rows = pl.ds(pl.multiple_of((2 * z + 1 - y) * r, r), r)
                size = gup_ref.shape[2]
                diagonal[0, z, :, k * size : (k + 1) * size] = gup_ref[0, rows, :]
                diagonal[1, z, :, k * size : (k + 1) * size] = gdown_ref[0, rows, :]
                return carry

            lax.fori_loop(0, m, keep, 0)
            if k == chunks - 1:
                for copy in across:
                    copy.start()

    @pl.when(s == pl.num_programs(0) - 1)
    def _():
        def norm_back(rows):
            third = back_ref[rows, :]
            upstream = dy_ref[rows, :].astype(F32)
            rows_grad, gain_terms = norm_rows_back(after_ref[rows, :], third, norm_ref[2, 0:1, :])
            rows_grad = rows_grad + upstream
            low = rows_grad.astype(BF16)
            rows_out[rows, :] = rows_grad
            low_out[rows, :] = low
            for k, terms in enumerate((gain_terms, third, low.astype(F32), upstream)):
                sums_ref[k : k + 1, :] += jnp.sum(terms, axis=0, keepdims=True)

        by_rows(x_ref.shape[0], 128, norm_back)
        for copy in across:
            copy.wait()


def feed_forward(x, dy, weights, bias, after, biases, norm):
    rows, width = x.shape
    hidden = weights[0].shape[2]
    size = min(512, hidden)
    chunks = hidden // size

    n = lax.axis_size("dp")
    m, r = n // 2, width // n

    def block(s):
        return 3 - s // chunks

    def placed(s):
        turn = s // chunks
        return (1 - turn // 2, 0, (s % chunks) * (turn % 2))

    rows_spec = const((rows, width))
    grad_spec = pl.BlockSpec((1, width, size), placed)
    bias_spec = pl.BlockSpec((1, 1, size), lambda s: (block(s), 0, s % chunks))
    return pl.pallas_call(
        functools.partial(feed_forward_kernel, chunks=chunks),
        grid=(4 * chunks,),
        in_specs=[
            rows_spec,
            rows_spec,
            ANY,
            ANY,
            ANY,
            ANY,
            const(bias.shape),
            rows_spec,
            const(biases.shape),
            const(norm.shape),
        ],
        out_specs=[rows_spec, rows_spec, rows_spec, const((8, width)), grad_spec, grad_spec, bias_spec, ANY, ANY],
        out_shape=[
            jax.ShapeDtypeStruct((rows, width), F32),
            jax.ShapeDtypeStruct((rows, width), F32),
            jax.ShapeDtypeStruct((rows, width), BF16),
            jax.ShapeDtypeStruct((8, width), F32),
            jax.ShapeDtypeStruct((2, width, hidden), BF16),
            jax.ShapeDtypeStruct((2, width, hidden), BF16),
            jax.ShapeDtypeStruct((4, 1, hidden), F32),
            jax.ShapeDtypeStruct((2, m // 2, r, hidden), BF16),
            jax.ShapeDtypeStruct((2, m - m // 2, r, hidden), BF16),
        ],
        scratch_shapes=[
            pltpu.VMEM((width, rows), BF16),
            pltpu.VMEM((width, rows), BF16),
            pltpu.VMEM((rows, width), F32),
            pltpu.VMEM((chunks, 2, width, size), BF16),
            pltpu.VMEM((2 * chunks, 2, width, size), BF16),
            pltpu.VMEM((2, m, r, hidden), BF16),
            pltpu.VMEM((2, 2, width, size), BF16),
            pltpu.SemaphoreType.DMA((2, 2)),
        ]
        + link_scratch(2 * chunks + 2, 1),
        compiler_params=pltpu.CompilerParams(
            vmem_limit_bytes=VMEM_LIMIT, collective_id=3, has_side_effects=True
        ),
        cost_estimate=pl.CostEstimate(
            flops=48 * rows * width * hidden, bytes_accessed=40 * 2**20, transcendentals=8 * rows * hidden
        ),
        name="feed_forward",
    )(x, dy, *weights, bias, after, biases, norm)


def cross_backward_kernel(
    len_ref, low_ref, x_ref, enc_ref, w_ref, q_ref, k_ref, v_ref, mt_ref, lse_ref, up_ref, down_ref, from_x, from_y,
    back_ref, enc_out, grad_ref, bq_ref, bv_ref, up_out, down_out,
    low_t, x_t, enc_t, enc_acc, give, got, *scratch, heads, bk
):
    i = pl.program_id(0)
    last = pl.num_programs(0) - 1
    links = Links(*scratch[14:])
    sums = [
        Gather(links, ref.at[0], ref.at[1], from_x.at[k], from_y.at[k], scratch[7 * k : 7 * k + 7])
        for k, ref in enumerate((up_ref, down_ref))
    ]
    leave = [links.local(g.column, out) for g, out in zip(sums, (up_out, down_out))]
    pair = i // 2
    to_core = pltpu.make_async_remote_copy(
        src_ref=give,
        dst_ref=got.at[pair],
        send_sem=links.send_sems.at[links.used + pair],
        recv_sem=links.recv_sems.at[links.used + pair],
        device_id=links.partner(CORE),
        device_id_type=pl.DeviceIdType.MESH,
    )

    @pl.when(i == 0)
    def _():
        links.greet([CORE, X, Y])
        for g in sums:
            g.start()
        low_t[...] = low_ref[...].T
        x_t[...] = x_ref[...].T
        enc_t[...] = enc_ref[...].T
        back_ref[...] = jnp.zeros_like(back_ref)
        enc_acc[...] = jnp.zeros_like(enc_acc)

    @pl.when(i == 1)
    def _():
        for g in sums:
            g.middle()

    rows, width = q_ref.shape[1:]
    n = k_ref.shape[1]
    hd = width // heads
    scale = 1.0 / math.sqrt(hd)
    w_query, w_keyval, w_out = w_ref.at[0, :, :width], w_ref.at[0, :, width : 3 * width], w_ref.at[0, :, 3 * width :]
    grads = dot_nn(low_ref[...], w_out[...]).astype(BF16)
    mixed_t = mt_ref[0]
    products = grads.T.astype(F32) * mixed_t.astype(F32)
    inner = [jnp.sum(products[h * hd : (h + 1) * hd, :], axis=0, keepdims=True) for h in range(heads)]
    scaled = q_ref[0] * jnp.asarray(scale, BF16)
    q_heads = [head_only(scaled, h, hd) for h in range(heads)]
    d_heads = [head_only(grads, h, hd) for h in range(heads)]
    lse = lse_ref[0]
    keys_t = k_ref[0].T
    dq = [None] * heads
    dkv = []
    for j in range(n // bk):
        span = slice(j * bk, (j + 1) * bk)
        ok = j * bk + lax.broadcasted_iota(jnp.int32, (bk, 1), 0) < len_ref[0]
        scores = [dot_nt(k_ref[0, span, lanes_of(h, hd)[1]], q_heads[h]) for h in range(heads)]
        dprobs = [dot_nt(v_ref[0, span, lanes_of(h, hd)[1]], d_heads[h]) for h in range(heads)]
        dv_sums, dk_sums = {}, {}
        for h in range(heads):
            part = slice(h * hd, (h + 1) * hd)
            group, _ = lanes_of(h, hd)
            probs = jnp.exp(jnp.where(ok, scores[h], NEGATIVE) - lse[h : h + 1, :])
            ds = (probs * (dprobs[h] - inner[h])).astype(BF16)
            add_group(dv_sums, group, dot_nn(probs.astype(BF16), d_heads[h]))
            add_group(dk_sums, group, dot_nn(ds, q_heads[h]))
            dq_h = dot_nn(keys_t[part, span], ds)
            dq[h] = dq_h if dq[h] is None else dq[h] + dq_h
        block = jnp.concatenate([sums_of[g].astype(BF16) for sums_of in (dk_sums, dv_sums) for g in sorted(sums_of)], 1)
        enc_acc[span, :] += dot_nt(block, w_keyval[...])
        dkv.append(block)
    dq = (jnp.concatenate(dq, 0) * scale).astype(BF16).T
    dkv = jnp.concatenate(dkv, 0)
    bq_ref[0] = jnp.sum(dq.astype(F32), axis=0, keepdims=True)
    bv_ref[0] = jnp.sum(dkv[:, width:].astype(F32), axis=0, keepdims=True)
    back_ref[...] += dot_nt(dq, w_query[...])

    @pl.when(i % 2 == 1)
    def _():
        to_core.wait_send()

    give[:, :width] = dot_nn(x_t[...], dq).astype(BF16)
    give[:, width : 3 * width] = dot_nn(enc_t[...], dkv).astype(BF16)
    give[:, 3 * width :] = dot_nn(low_t[...], mixed_t.T).astype(BF16)

    @pl.when(i % 2 == 0)
    def _():
        to_core.start()

    @pl.when(i % 2 == 1)
    def _():
        to_core.wait_recv()
        grad_ref[0] = (give[...].astype(F32) + got[pair].astype(F32)).astype(BF16)

    @pl.when(i == last)
    def _():
        enc_out[...] = enc_acc[...].astype(BF16)
        for g, copy in zip(sums, leave):
            g.end()
            copy.start()
        for copy in leave:
            copy.wait()


def cross_backward(
    lengths, low, x, encoder, weights, queries, keys, values, mixed_t, lse, up_sum, down_sum, from_x, from_y, heads
):
    count, model = x.shape
    n = encoder.shape[0]
    parts, _, columns = weights.shape
    width = columns // 4
    _, m, _, r, c = up_sum.shape

    def by_part(*shape):
        return pl.BlockSpec((1,) + shape, lambda i: (i ^ 1,) + (0,) * len(shape))

    return pl.pallas_call(
        functools.partial(cross_backward_kernel, heads=heads, bk=256),
        grid=(parts,),
        in_specs=[
            pl.BlockSpec(memory_space=pltpu.SMEM),
            const((count, model)),
            const((count, model)),
            const((n, model)),
            by_part(model, columns),
            by_part(count, width),
            by_part(n, width),
            by_part(n, width),
            by_part(width, count),
            by_part(heads, count),
            ANY,
            ANY,
            ANY,
            ANY,
        ],
        out_specs=[
            const((count, model)),
            const((n, model)),
            pl.BlockSpec((1, model, columns), lambda i: (i // 2, 0, 0), pipeline_mode=pl.Buffered(1)),
            by_part(1, width),
            by_part(1, width),
            ANY,
            ANY,
        ],
        out_shape=[
            jax.ShapeDtypeStruct((count, model), F32),
            jax.ShapeDtypeStruct((n, model), BF16),
            jax.ShapeDtypeStruct((2, model, columns), BF16),
            jax.ShapeDtypeStruct((parts, 1, width), F32),
            jax.ShapeDtypeStruct((parts, 1, width), F32),
            jax.ShapeDtypeStruct((m, r, c), BF16),
            jax.ShapeDtypeStruct((m, r, c), BF16),
        ],
        scratch_shapes=[
            pltpu.VMEM((model, count), BF16),
            pltpu.VMEM((model, count), BF16),
            pltpu.VMEM((model, n), BF16),
            pltpu.VMEM((n, model), F32),
            pltpu.VMEM((model, columns), BF16),
            pltpu.VMEM((2, model, columns), BF16),
        ]
        + gather_scratch(m, r, c) * 2
        + link_scratch(10, 12),
        compiler_params=pltpu.CompilerParams(
            vmem_limit_bytes=60 * 2**20, collective_id=4, has_side_effects=True
        ),
        cost_estimate=pl.CostEstimate(
            flops=48 * parts * count * n * width,
            bytes_accessed=16 * parts * n * width,
            transcendentals=parts * count * n * heads,
        ),
        name="cross_backward",
    )(lengths, low, x, encoder, weights, queries, keys, values, mixed_t, lse, up_sum, down_sum, from_x, from_y)


def on_device(
    block_in,
    encoder_out,
    out_grad,
    bounds,
    enc_lengths,
    norm_params,
    w_qkv,
    w_self_out,
    w_cross_q,
    w_cross_kv,
    w_cross_out,
    w_up,
    w_down,
    biases,
    up_bias,
):
    groups_count = lax.axis_size("dp")
    width = w_cross_q.shape[1]
    hidden_width = w_up.shape[1]
    heads = H // 4
    own_rows, model_width = block_in.shape
    w_rows = w_cross_q.shape[0]

    first_in, self_w, cross_column, down_square = start_gather(
        block_in,
        norm_params,
        w_qkv,
        w_self_out,
        w_cross_q,
        w_cross_kv,
        w_cross_out,
        w_down,
    )
    self_w = self_w.reshape(model_width, 4 * width)

    self_safe = 1024
    queries, key_rows, value_rows, keys_t, self_mixed_t, self_lse, terms, cross_w, up_column, near_z = self_forward(
        bounds,
        first_in,
        self_w,
        biases,
        cross_column,
        w_up,
        down_square,
        heads,
        self_safe,
    )
    cross_w = cross_w.reshape(4, model_width, 4 * width)
    after_self, second_in, near_up, enc_all, near_down, far_z = sum_after_self(
        terms, block_in, biases, norm_params, up_column, encoder_out, down_square, near_z
    )

    cross_q, cross_k, cross_v, cross_mixed_t, cross_lse, after_cross, third_in, far_up, far_down = cross_forward(
        enc_lengths,
        second_in,
        enc_all,
        cross_w,
        biases,
        after_self,
        norm_params,
        up_column,
        down_square,
        far_z,
        heads,
    )

    output, cross_rows_grad, cross_low, ffn_sums, up_sum, down_sum, bias_up_parts, from_x, from_y = feed_forward(
        third_in,
        out_grad,
        [w.reshape(2, model_width, hidden_width) for w in (near_up, near_down, far_up, far_down)],
        up_bias.reshape(-1, LANES),
        after_cross,
        biases,
        norm_params,
    )

    by_shard = (2, groups_count // 2, 2, w_rows, hidden_width)
    second_grad, enc_terms, cross_sum, bias_cq_parts, bias_cv_parts, up_column, down_column = cross_backward(
        enc_lengths,
        cross_low,
        second_in,
        enc_all,
        cross_w,
        cross_q,
        cross_k,
        cross_v,
        cross_mixed_t,
        cross_lse,
        up_sum.reshape(by_shard),
        down_sum.reshape(by_shard),
        from_x,
        from_y,
        heads,
    )
    cross_sum = cross_sum.reshape(2, groups_count // 2, 2, w_rows, 4 * width)

    (
        self_dq, self_dk, self_dv, self_wide, self_rows_grad, self_sums,
        summed_up, summed_down, cross_column, encoder_grad,
    ) = self_backward(
        bounds,
        queries,
        key_rows,
        value_rows,
        keys_t,
        self_w,
        self_mixed_t,
        self_lse,
        second_grad,
        after_self,
        cross_rows_grad,
        norm_params,
        up_column,
        down_column,
        cross_sum,
        enc_terms,
        heads,
        self_safe,
    )
    input_grad, summed_self, vectors, summed_cross = tail(
        self_dq,
        self_dk,
        self_dv,
        self_w,
        first_in,
        self_wide,
        self_mixed_t,
        block_in,
        self_rows_grad,
        cross_column,
        norm_params,
        self_sums,
        ffn_sums,
        bias_cq_parts,
        bias_cv_parts,
        bias_up_parts,
    )
    output, input_grad, encoder_grad, *weights_and_vectors = results(
        output, input_grad, encoder_grad, summed_self, summed_cross, summed_up, summed_down, vectors, 1.0 / groups_count
    )
    g_qkv, g_so, g_cq, g_ckv, g_co, g_up, g_down, g_norm, g_biases, g_shift = weights_and_vectors
    return (
        output,
        input_grad,
        encoder_grad,
        g_norm,
        g_qkv,
        g_so,
        g_cq,
        g_ckv,
        g_co,
        g_up,
        g_down,
        g_biases,
        g_shift.reshape(-1),
    )


def solution(mesh):
    rows = P(("dp", "tensor"), None)
    placed = (
        rows,
        rows,
        rows,
        P("dp", None),
        P("dp"),
        P(),
        P("dp", None, "tensor"),
        P("tensor", "dp"),
        P("dp", "tensor"),
        P("dp", None, "tensor"),
        P("tensor", "dp"),
        P("dp", "tensor"),
        P("tensor", "dp"),
        P(),
        P(),
    )
    return jax.shard_map(
        on_device,
        mesh=mesh,
        in_specs=placed,
        out_specs=(
            rows,
            rows,
            rows,
            P(),
            P("dp", None, "tensor"),
            P("tensor", "dp"),
            P("dp", "tensor"),
            P("dp", None, "tensor"),
            P("tensor", "dp"),
            P("dp", "tensor"),
            P("tensor", "dp"),
            P(),
            P(),
        ),
        check_vma=False,
    )
```

```python
import functools
import math

import jax
import jax.numpy as jnp
from jax import lax
from jax.experimental import pallas as pl
from jax.experimental.pallas import tpu as pltpu
from jax.sharding import PartitionSpec as P

H = 16
EPSILON = 1e-05
NEGATIVE = -1e30
F32 = jnp.float32
BF16 = jnp.bfloat16
VMEM_LIMIT = 56 * 2**20


def dot_nt(a, b):
    return lax.dot_general(a, b, (((1,), (1,)), ((), ())), preferred_element_type=F32)


def dot_nn(a, b):
    return lax.dot_general(a, b, (((1,), (0,)), ((), ())), preferred_element_type=F32)


def dot_tn(a, b):
    return lax.dot_general(a, b, (((0,), (0,)), ((), ())), preferred_element_type=F32)


LANES = 128


def lanes_of(h, size):
    group = h * size // LANES
    return group, slice(group * LANES, (group + 1) * LANES)


def head_only(x, h, size):
    group, part = lanes_of(h, size)
    lane = group * LANES + lax.broadcasted_iota(jnp.int32, (x.shape[0], LANES), 1)
    return jnp.where((lane >= h * size) & (lane < (h + 1) * size), x[:, part], jnp.zeros((), x.dtype))


def add_group(sums, group, value):
    sums[group] = value if group not in sums else sums[group] + value


def self_bad(b_ref, q_start, k_start, bq, bk, causal):
    qi = q_start + lax.broadcasted_iota(jnp.int32, (1, bq), 1)
    kj = k_start + lax.broadcasted_iota(jnp.int32, (bk, 1), 0)
    bad = (qi >= b_ref[0, 1]) & ((kj >= b_ref[0, 0]) & (kj < b_ref[0, 1]))
    if causal:
        bad = bad | (kj > qi)
    return bad


def over_keys(i, bq, safe, block, between=()):
    def visit(j, c):
        for at_i, at_j, action in between:
            pl.when((i == at_i) & (j == at_j))(action)

        @pl.when(j < safe // bq)
        def _():
            block(j * bq, bq, 0, "none")

        @pl.when(j >= safe // bq)
        def _():
            block(j * bq, bq, 0, "segment")

        return c

    lax.fori_loop(0, i, visit, 0)
    half = bq // 2
    block(i * bq, half, 0, "causal")
    block(i * bq + half, half, half, "causal")


CORE = ("tensor", 1)
X = ("tensor", 2)
Y = ("dp", 1)
ANY = pl.BlockSpec(memory_space=pl.ANY)


class Links:
    def __init__(self, send_sems, recv_sems, local_sems):
        self.dp = lax.axis_index("dp")
        self.tensor = lax.axis_index("tensor")
        self.send_sems, self.recv_sems, self.local_sems = send_sems, recv_sems, local_sems
        self.used = 0
        self.used_local = 0

    def partner(self, way):
        axis, distance = way
        if axis == "tensor":
            return (self.dp, self.tensor ^ distance)
        return (self.dp ^ distance, self.tensor)

    def greet(self, ways):
        barrier = pltpu.get_barrier_semaphore()
        for way in ways:
            pl.semaphore_signal(
                barrier, inc=1, device_id=self.partner(way), device_id_type=pl.DeviceIdType.MESH
            )
        pl.semaphore_wait(barrier, len(ways))

    def copy(self, source, target, way):
        k = self.used
        self.used += 1
        return pltpu.make_async_remote_copy(
            src_ref=source,
            dst_ref=target,
            send_sem=self.send_sems.at[k],
            recv_sem=self.recv_sems.at[k],
            device_id=self.partner(way),
            device_id_type=pl.DeviceIdType.MESH,
        )

    def local(self, source, target):
        k = self.used_local
        self.used_local += 1
        return pltpu.make_async_copy(source, target, self.local_sems.at[k])


def link_scratch(copies, local):
    return [
        pltpu.SemaphoreType.DMA((copies,)),
        pltpu.SemaphoreType.DMA((copies,)),
        pltpu.SemaphoreType.DMA((local,)),
    ]


def z_distances(n):
    found = []
    m = n // 2
    while m > 1:
        m //= 2
        found.append(m)
    return found


def z_ways(n):
    return [("dp", 2 * distance) for distance in z_distances(n)]


def column_stages(links, shard, column, n):
    z = links.dp // 2
    held = [z]
    stages = []
    for distance in z_distances(n):
        stages.append(
            [
                (
                    links.copy(shard if k == 0 else column.at[index], column.at[index], ("dp", 2 * distance)),
                    index ^ distance,
                )
                for k, index in enumerate(held)
            ]
        )
        held = held + [index ^ distance for index in held]
    return stages


class Spread:
    def __init__(self, links, source, column, whole):
        y = links.dp % 2
        half = column.shape[0] // 2
        low, high = pl.ds(0, half), pl.ds(half, half)
        near, near_core, far, far_core = (whole.at[k] for k in range(4))
        self.load = links.local(source, column)
        self.own = links.local(column, near.at[:, y])
        self.first = [
            links.copy(column, near.at[:, y], Y),
            links.copy(column, far.at[:, y], X),
        ]
        self.core = [links.copy(column, near_core.at[:, y], CORE)]
        self.second = [
            links.copy(near.at[low, 1 - y], far.at[low, 1 - y], X),
            links.copy(far.at[high, y], far.at[high, y], Y),
        ]
        self.core_second = [
            links.copy(near.at[:, 1 - y], near_core.at[:, 1 - y], CORE),
            links.copy(far.at[:, y], far_core.at[:, y], CORE),
        ]
        self.core_third = [links.copy(far.at[:, 1 - y], far_core.at[:, 1 - y], CORE)]

    def start(self):
        self.load.start()
        self.load.wait()
        for copy in self.first + self.core + [self.own]:
            copy.start()

    def middle(self):
        for copy in self.first:
            copy.wait_recv()
        for copy in self.second + self.core_second:
            copy.start()

    def last(self):
        for copy in self.second:
            copy.wait_recv()
        for copy in self.core_third:
            copy.start()

    def end(self):
        self.own.wait()
        for copy in self.first + self.second:
            copy.wait_send()
        for copy in self.core + self.core_second + self.core_third:
            copy.wait()


def add_to(total_ref, other_ref):
    def one(k, c):
        total_ref[k] = (total_ref[k].astype(F32) + other_ref[k].astype(F32)).astype(BF16)
        return c

    lax.fori_loop(0, total_ref.shape[0], one, 0)


class Gather:
    def __init__(self, links, near, far, from_x, from_y, buffers):
        y = links.dp % 2
        self.column, self.over_y, self.over_x, self.add_y, self.add_x, self.sum_y, self.sum_x = buffers
        m = self.column.shape[0]
        low, high = pl.ds(0, m // 2), pl.ds(m // 2, m - m // 2)
        self.loads = [
            links.local(near.at[low, 1 - y], self.over_y),
            links.local(far.at[high, y], self.over_x),
            links.local(from_x, self.add_y),
            links.local(from_y, self.add_x),
            links.local(near.at[:, y], self.column),
        ]
        self.first = [
            links.copy(far.at[low, y], self.sum_x.at[low], X),
            links.copy(near.at[high, 1 - y], self.sum_y.at[high], Y),
        ]
        self.second = [
            links.copy(self.over_x, self.sum_x.at[high], X),
            links.copy(self.over_y, self.sum_y.at[low], Y),
        ]

    def start(self):
        for copy in self.first + self.loads:
            copy.start()

    def middle(self):
        for copy in self.loads:
            copy.wait()
        add_to(self.over_x, self.add_x)
        add_to(self.over_y, self.add_y)
        for copy in self.second:
            copy.start()

    def end(self):
        for copy in self.first + self.second:
            copy.wait_recv()
        add_to(self.column, self.sum_y)
        add_to(self.column, self.sum_x)
        for copy in self.first + self.second:
            copy.wait_send()


def gather_scratch(m, r, c):
    whole = pltpu.VMEM((m, r, c), BF16)
    half = pltpu.VMEM((m // 2, r, c), BF16)
    return [whole] + [half] * 4 + [whole] * 2


class GatherLast:
    def __init__(self, links, near, far, buffers):
        y = links.dp % 2
        self.column, self.over_x, self.diagonal, self.sum_y, self.sum_x = buffers
        self.loads = [links.local(far.at[:, y], self.over_x), links.local(near.at[:, y], self.column)]
        self.first = links.copy(far.at[:, 1 - y], self.diagonal, Y)
        self.over_y = links.copy(near.at[:, 1 - y], self.sum_y, Y)
        self.along_x = links.copy(self.over_x, self.sum_x, X)

    def start(self):
        self.first.start()
        for copy in self.loads:
            copy.start()

    def second(self):
        self.first.wait_recv()
        self.over_y.start()

    def middle(self):
        for copy in self.loads:
            copy.wait()
        add_to(self.over_x, self.diagonal)
        self.along_x.start()

    def end(self):
        self.over_y.wait_recv()
        self.along_x.wait_recv()
        add_to(self.column, self.sum_y)
        add_to(self.column, self.sum_x)
        for copy in (self.first, self.over_y, self.along_x):
            copy.wait_send()


class Collect:
    def __init__(self, links, column, slots):
        z = links.dp // 2
        self.column, self.slots, self.z = column, slots, z
        m = column.shape[0]
        distances = z_distances(2 * m)[::-1]
        self.stages = []
        first = 0
        for step, distance in enumerate(distances):
            kept = [0]
            for other in distances[step + 1 :]:
                kept = kept + [k ^ other for k in kept]
            self.stages.append(
                [
                    (links.copy(column.at[z ^ distance ^ k], slots.at[first + i], ("dp", 2 * distance)), first + i, z ^ k)
                    for i, k in enumerate(kept)
                ]
            )
            first += len(kept)

    def start(self, step):
        for copy, _, _ in self.stages[step]:
            copy.start()

    def finish(self, step):
        for copy, slot, index in self.stages[step]:
            copy.wait_recv()
            self.column[index] = (self.column[index].astype(F32) + self.slots[slot].astype(F32)).astype(BF16)

    def drain(self):
        for stage in self.stages:
            for copy, _, _ in stage:
                copy.wait_send()


class Square:
    def __init__(self, links, shard, out):
        y = links.dp % 2
        c = shard.shape[1]
        low, high = pl.ds(0, c // 2), pl.ds(c // 2, c // 2)
        self.own = links.local(shard, out.at[0, y])
        self.first = [links.copy(shard, out.at[0, y], Y), links.copy(shard, out.at[1, y], X)]
        self.second = [
            links.copy(out.at[0, 1 - y, :, low], out.at[1, 1 - y, :, low], X),
            links.copy(out.at[1, y, :, high], out.at[1, y, :, high], Y),
        ]

    def start(self):
        for copy in self.first + [self.own]:
            copy.start()

    def middle(self):
        for copy in self.first:
            copy.wait_recv()
        for copy in self.second:
            copy.start()

    def end(self):
        for copy in self.first:
            copy.wait_send()
        for copy in self.second:
            copy.wait()
        self.own.wait()


class SpreadZ:
    def __init__(self, links, own, other, hold, whole, n):
        z = links.dp // 2
        distances = z_distances(n)
        there = z ^ distances[0]
        final, core = whole.at[0], whole.at[1]
        self.loads = [links.local(own, hold.at[0]), links.local(other, hold.at[1])]
        self.stores = [links.local(hold.at[0], final.at[z]), links.local(hold.at[1], final.at[there])]
        self.core = [links.copy(hold.at[0], core.at[z], CORE), links.copy(hold.at[1], core.at[there], CORE)]
        held = [(hold.at[0], z), (hold.at[1], there)]
        self.stages, self.core_stages = [], []
        for distance in distances[1:]:
            came = [index ^ distance for _, index in held]
            self.stages.append([links.copy(ref, final.at[index], ("dp", 2 * distance)) for ref, index in held])
            self.core_stages.append([links.copy(final.at[index], core.at[index], CORE) for index in came])
            held = held + [(final.at[index], index) for index in came]

    def start(self):
        for copy in self.loads:
            copy.start()
        for copy in self.loads:
            copy.wait()
        for copy in self.stages[0] + self.stores + self.core:
            copy.start()

    def end(self):
        for step, (stage, core_stage) in enumerate(zip(self.stages, self.core_stages)):
            for copy, onward in zip(stage, core_stage):
                copy.wait_recv()
                onward.start()
            for copy in self.stages[step + 1] if step + 1 < len(self.stages) else []:
                copy.start()
        for copy in self.stores + self.core:
            copy.wait()
        for stage, core_stage in zip(self.stages, self.core_stages):
            for copy in stage:
                copy.wait_send()
            for copy in core_stage:
                copy.wait()


def spread_z_copies(n):
    return 2 * n


class SpreadFar:
    def __init__(self, links, column, whole):
        y = links.dp % 2
        far, far_core = whole.at[0], whole.at[1]
        m, _, c = column.shape
        step = max(m // 4, 1)
        self.over_x, self.over_y, self.core_x, self.core_y = [], [], [], []
        for k in range(m // step):
            for h in range(2):
                z, part = pl.ds(k * step, step), pl.ds(h * (c // 2), c // 2)
                own = far.at[z, y, :, part]
                other = far.at[z, 1 - y, :, part]
                self.over_x.append(links.copy(column.at[z, :, part], own, X))
                self.over_y.append(links.copy(own, own, Y))
                self.core_x.append(links.copy(own, far_core.at[z, y, :, part], CORE))
                self.core_y.append(links.copy(other, far_core.at[z, 1 - y, :, part], CORE))

    def start(self):
        for copy in self.over_x:
            copy.start()

    def onward(self, k):
        self.over_x[k].wait_recv()
        self.over_y[k].start()
        self.core_x[k].start()

    def last(self, k):
        self.over_y[k].wait_recv()
        self.core_y[k].start()

    def end(self):
        for copy in self.over_x + self.over_y:
            copy.wait_send()
        for copy in self.core_x + self.core_y:
            copy.wait()


class RowSum:
    def __init__(self, links, terms, buffers):
        self.near, self.far, self.got_near, self.got_far, self.got_x = buffers
        count = self.near.shape[0]

        def rows(distance):
            start = pl.multiple_of((links.tensor ^ distance) * count, count)
            return terms.at[pl.ds(start, count)]

        self.loads = [links.local(rows(0), self.near), links.local(rows(2), self.far)]
        self.core = [links.copy(rows(3), self.got_far, CORE), links.copy(rows(1), self.got_near, CORE)]
        self.over_x = links.copy(self.far, self.got_x, X)

    def start(self):
        for copy in self.loads[::-1] + self.core:
            copy.start()

    def middle(self):
        self.loads[1].wait()
        self.core[0].wait_recv()

        def add(rows):
            self.far[rows, :] = (self.far[rows, :].astype(F32) + self.got_far[rows, :].astype(F32)).astype(BF16)

        by_rows(self.far.shape[0], 64, add)
        self.over_x.start()

    def end(self):
        self.loads[0].wait()
        self.core[1].wait_recv()
        self.over_x.wait_recv()
        for copy in self.core + [self.over_x]:
            copy.wait_send()

    def total(self, rows):
        return self.near[rows, :].astype(F32) + self.got_near[rows, :].astype(F32) + self.got_x[rows, :].astype(F32)


def row_sum_scratch(count, width):
    return [pltpu.VMEM((count, width), BF16)] * 5


class Everywhere:
    def __init__(self, links, held, slots, ways):
        self.held, self.slots = held, slots
        self.copies = [links.copy(held.at[k], slots.at[k], way) for k, way in enumerate(ways)]

    def start(self, step):
        self.copies[step].start()

    def finish(self, step):
        self.copies[step].wait()
        self.held[step + 1] = self.held[step] + self.slots[step]


class Direct:
    def __init__(self, links, value, slots_tensor, slots_dp, n):
        self.value = value
        self.slots = (slots_tensor, slots_dp)
        self.me = (links.tensor, links.dp)
        self.copies = []
        for slots, me, axis, size in zip(self.slots, self.me, ("tensor", "dp"), (4, n)):
            self.copies.append([links.copy(value, slots.at[me], (axis, d)) for d in range(1, size)])

    def start(self, phase):
        for copy in self.copies[phase]:
            copy.start()

    def finish(self, phase):
        slots = self.slots[phase]
        slots[self.me[phase]] = self.value[...]
        for copy in self.copies[phase]:
            copy.wait()
        total = slots[0]
        for k in range(1, slots.shape[0]):
            total = total + slots[k]
        self.value[...] = total


def direct_ways(n):
    return [("tensor", d) for d in range(1, 4)] + [("dp", d) for d in range(1, n)]


def everywhere_ways(n):
    return [CORE, X, Y] + z_ways(n)


def everywhere_scratch(k, c, n):
    steps = len(everywhere_ways(n))
    return [pltpu.VMEM((steps + 1, k, c), F32), pltpu.VMEM((steps, k, c), F32)]


def tail_kernel(
    dq_ref, dk_ref, dv_ref, w_ref, first_hbm, wide_hbm, mt_hbm, rows_hbm, grad_hbm, cross_hbm, norm_ref,
    self_ref, ffn_ref, cq_ref, cv_ref, up_ref,
    grad_out, weights_out, late_out, cross_out, give, acc, weights,
    first_ref, wide_ref, mt_ref, rows_ref, grad_ref, cross_ref, cross_slots, *scratch, n, step_rows
):
    links = Links(*scratch[-3:])
    loads = [
        links.local(source, target)
        for source, target in (
            (cross_hbm, cross_ref), (first_hbm, first_ref), (wide_hbm, wide_ref), (mt_hbm, mt_ref),
            (rows_hbm, rows_ref), (grad_hbm, grad_ref),
        )
    ]
    for copy in loads:
        copy.start()
    cross = Collect(links, cross_ref, cross_slots)
    member = links.tensor
    near, far, got_near, got_far, got_x = scratch[:5]
    columns, gots, slots = scratch[5:7], scratch[7:9], scratch[9:11]
    late_tensor, late_dp, sums, early_slots, held, compact = scratch[11:17]
    count, model = near.shape
    width = dq_ref.shape[1]
    y = links.dp % 2
    c = columns[0].shape[2]
    m, _, r, _ = weights.shape
    half = count // 2
    parts = [pl.ds(0, half), pl.ds(half, half)]
    core_far = links.copy(give.at[0], got_far, CORE)
    core_near = links.copy(give.at[1], got_near, CORE)
    over_x = [links.copy(far.at[part], got_x.at[part], X) for part in parts]
    over_y, collects = [], []
    for k, (column, got, slot) in enumerate(zip(columns, gots, slots)):
        over_y.append(links.copy(weights.at[:, 1 - y, :, pl.ds(k * c, c)], got, Y))
        collects.append(Collect(links, column, slot))
    stages = len(collects[0].stages)
    late = Direct(links, compact, late_tensor, late_dp, n)
    early = Everywhere(links, sums, early_slots, [CORE] + z_ways(n) + [Y, X])
    steps = len(early.copies)
    links.greet(direct_ways(n))

    def terms(distance, target):
        base = (member ^ distance) * count

        def one(rows):
            there = pl.ds(pl.multiple_of(base + rows.start, 128), 128)
            total = dot_nt(dq_ref[there, :], w_ref[:, :width])
            total = total + dot_nt(dk_ref[there, :], w_ref[:, width : 2 * width])
            target[rows, :] = (total + dot_nt(dv_ref[there, :], w_ref[:, 2 * width : 3 * width])).astype(BF16)

        by_rows(count, 128, one)

    def packed(k):
        for block in range(2 * m):
            span = slice(block * r, (block + 1) * r)
            weights[block // 2, block % 2, :, k * c : (k + 1) * c] = acc[span, k * c : (k + 1) * c].astype(BF16)
        columns[k][...] = weights[:, y, :, k * c : (k + 1) * c]

    loads[0].wait()
    cross.start(0)
    acc[...] = jnp.zeros_like(acc)
    loads[1].wait()

    def products(refs, at):
        def one(rows):
            source = first_ref[rows, :].T
            for k, ref in enumerate(refs):
                acc[:, (at + k) * width : (at + k + 1) * width] += dot_nn(source, ref[rows, :])

        return one

    by_rows(dq_ref.shape[0], step_rows, products((dq_ref, dk_ref), 0))
    packed(0)
    over_y[0].start()
    terms(3, give.at[0])
    core_far.start()
    terms(2, far)
    core_far.wait_recv()
    for part, copy in zip(parts, over_x):

        def add(rows, part=part):
            there = pl.ds(pl.multiple_of(part.start + rows.start, 64), 64)
            far[there, :] = (far[there, :].astype(F32) + got_far[there, :].astype(F32)).astype(BF16)

        by_rows(half, 64, add)
        copy.start()
    for copy in loads[2:]:
        copy.wait()

    def products_out(rows):
        acc[:, 3 * width :] += dot_nn(wide_ref[rows, :].T, mt_ref[:, rows].T)

    by_rows(dq_ref.shape[0], step_rows, products((dv_ref,), 2))
    by_rows(dq_ref.shape[0], step_rows, products_out)
    packed(1)
    over_y[1].start()
    terms(1, give.at[1])
    core_near.start()
    terms(0, near)
    for step in range(stages - 1):
        cross.finish(step)
        cross.start(step + 1)

    held[...] = jnp.zeros_like(held)
    sums[0] = jnp.zeros(sums.shape[1:], F32)
    sums[0, 0:2, :] = self_ref[0:2, :]
    sums[0, 2:4, :] = ffn_ref[0:2, :]
    sums[0, 6:7, :] = self_ref[2:3, :]
    sums[0, 9:11, :] = ffn_ref[2:4, :]
    for distance in range(4):
        there = pl.ds(pl.multiple_of((member ^ distance) * width, width), width)
        sums[0, 7:8, there] = cq_ref[distance]
        sums[0, 8:9, there] = cv_ref[distance]
        sums[0, pl.ds(11 + (member ^ distance), 1), :] = up_ref[distance]
    here = pl.ds(pl.multiple_of(member * width, width), width)

    def column_sums(rows):
        sums[0, 4:5, here] += jnp.sum(dq_ref[rows, :].astype(F32), axis=0, keepdims=True)
        sums[0, 5:6, here] += jnp.sum(dv_ref[rows, :].astype(F32), axis=0, keepdims=True)

    by_rows(dq_ref.shape[0], step_rows, column_sums)
    early.start(0)

    def norm_back(part):
        def one(rows):
            rows = pl.ds(pl.multiple_of(part.start + rows.start, 64), 64)
            incoming = near[rows, :].astype(F32) + got_near[rows, :].astype(F32) + got_x[rows, :].astype(F32)
            rows_grad, gain_terms = norm_rows_back(rows_ref[rows, :].astype(F32), incoming, norm_ref[0, 0:1, :])
            grad_out[rows, :] = rows_grad + grad_ref[rows, :]
            held[0:1, :] += jnp.sum(gain_terms, axis=0, keepdims=True)
            held[1:2, :] += jnp.sum(incoming, axis=0, keepdims=True)

        by_rows(half, 64, one)

    def summed_y(k):
        over_y[k].wait_recv()
        add_to(columns[k], gots[k])
        collects[k].start(0)

    def next_z(k):
        for step in range(stages - 1):
            collects[k].finish(step)
            collects[k].start(step + 1)

    def last_z(k):
        collects[k].finish(stages - 1)
        weights_out[:, k * c : (k + 1) * c] = columns[k][collects[k].z].astype(F32)

    summed_y(0)
    early.finish(0)
    cross.finish(stages - 1)
    cross_out[...] = cross_ref[cross.z].astype(F32)
    core_near.wait_recv()
    over_x[0].wait_recv()
    norm_back(parts[0])
    next_z(0)
    summed_y(1)
    for step in range(1, steps - 1):
        early.start(step)
        early.finish(step)
    next_z(1)
    last_z(0)
    over_x[1].wait_recv()
    norm_back(parts[1])
    lines = model // LANES
    for k in range(2 * lines):
        compact[k : k + 1, :] = held[k // lines : k // lines + 1, k % lines * LANES : (k % lines + 1) * LANES]
    late.start(0)
    early.start(steps - 1)
    last_z(1)
    late.finish(0)
    late.start(1)
    early.finish(steps - 1)
    late_out[2:, :] = sums[steps]
    late.finish(1)
    for k in range(2 * lines):
        late_out[k // lines : k // lines + 1, k % lines * LANES : (k % lines + 1) * LANES] = compact[k : k + 1, :]
    for copy in over_x + over_y + [core_near, core_far]:
        copy.wait_send()
    for collect in collects + [cross]:
        collect.drain()


def tail(
    dq, dk, dv, w, first, wide, mixed_t, rows, grad, cross_column, norm, self_sums, ffn_sums, cq_sums, cv_sums, up_sums
):
    n = lax.axis_size("dp")
    count, model = rows.shape
    width = dq.shape[1]
    m, r, c = n // 2, model // n, 4 * width
    vectors = (16, model)
    vmem = pl.BlockSpec(memory_space=pltpu.VMEM)
    part = pltpu.VMEM((m, r, c // 2), BF16)
    return pl.pallas_call(
        functools.partial(tail_kernel, n=n, step_rows=512),
        in_specs=[vmem] * 4 + [ANY] * 6 + [vmem] * 6,
        out_specs=[vmem] * 4,
        out_shape=[
            jax.ShapeDtypeStruct((count, model), F32),
            jax.ShapeDtypeStruct((r, c), F32),
            jax.ShapeDtypeStruct((vectors[0] + 2, model), F32),
            jax.ShapeDtypeStruct(cross_column.shape[1:], F32),
        ],
        scratch_shapes=[
            pltpu.VMEM((2, count, model), BF16),
            pltpu.VMEM((model, c), F32),
            pltpu.VMEM((m, 2, r, c), BF16),
        ]
        + [pltpu.VMEM(v.shape, v.dtype) for v in (first, wide, mixed_t, rows, grad, cross_column, cross_column)]
        + row_sum_scratch(count, model)
        + [part] * 6
        + [pltpu.VMEM((size, 2 * model // LANES, LANES), F32) for size in (4, n)]
        + everywhere_scratch(*vectors, n)
        + [pltpu.VMEM((8, model), F32), pltpu.VMEM((2 * model // LANES, LANES), F32)]
        + link_scratch(6 + 3 * m + len(everywhere_ways(n)) + len(direct_ways(n)), 6),
        compiler_params=pltpu.CompilerParams(
            vmem_limit_bytes=VMEM_LIMIT, collective_id=7, has_side_effects=True
        ),
        cost_estimate=pl.CostEstimate(flops=0, bytes_accessed=100 * 2**20, transcendentals=0),
        name="tail",
    )(
        dq, dk, dv, w, first, wide, mixed_t, rows, grad, cross_column, norm,
        self_sums, ffn_sums, cq_sums, cv_sums, up_sums,
    )


def results_kernel(
    output_ref, grad_ref, enc_ref, self_ref, cross_ref, up_ref, down_ref, vectors_ref,
    output_out, grad_out, enc_out, qkv_out, so_out, cq_out, ckv_out, co_out, up_out, down_out,
    norm_out, biases_out, shift_out, *, scale
):
    output_out[...] = output_ref[...]
    grad_out[...] = grad_ref[...]
    enc_out[...] = enc_ref[...]
    width = cq_out.shape[1]

    @pl.when(pl.program_id(0) == 0)
    def _():
        for k in range(3):
            qkv_out[:, k, :] = self_ref[:, k * width : (k + 1) * width] * scale
        so_out[...] = (self_ref[:, 3 * width :] * scale).T
        cq_out[...] = cross_ref[:, :width] * scale
        for k in range(2):
            ckv_out[:, k, :] = cross_ref[:, (k + 1) * width : (k + 2) * width] * scale
        co_out[...] = (cross_ref[:, 3 * width :] * scale).T
        up_out[...] = up_ref[...] * scale
        down_out[...] = (down_ref[...] * scale).T
        vectors = vectors_ref[...] * scale
        for k in range(3):
            norm_out[k] = vectors[2 * k : 2 * k + 2, :]
        biases_out[...] = vectors[6:13, :]
        lines = vectors.shape[1] // LANES
        for k in range(shift_out.shape[0]):
            part = slice(k % lines * LANES, (k % lines + 1) * LANES)
            shift_out[k : k + 1, :] = vectors[13 + k // lines : 14 + k // lines, part]


def results(output, grad, encoder, self_w, cross_w, up, down, vectors, scale):
    r, c = self_w.shape
    width = c // 4
    steps = 4

    def rows(value):
        return pl.BlockSpec((value.shape[0] // steps, value.shape[1]), lambda i: (i, 0))

    shapes = [(r, 3, width), (width, r), (r, width), (r, 2, width), (width, r), up.shape, down.shape[::-1]]
    shapes += [(3, 2, output.shape[1]), (7, output.shape[1]), (4 * up.shape[1] // LANES, LANES)]
    return pl.pallas_call(
        functools.partial(results_kernel, scale=scale),
        grid=(steps,),
        in_specs=[rows(output), rows(grad), rows(encoder)] + [const(v.shape) for v in (self_w, cross_w, up, down, vectors)],
        out_specs=[rows(output), rows(grad), rows(encoder)] + [const(shape) for shape in shapes],
        out_shape=[jax.ShapeDtypeStruct(v.shape, F32) for v in (output, grad, encoder)]
        + [jax.ShapeDtypeStruct(shape, F32) for shape in shapes],
        compiler_params=pltpu.CompilerParams(vmem_limit_bytes=VMEM_LIMIT),
        cost_estimate=pl.CostEstimate(flops=0, bytes_accessed=20 * 2**20, transcendentals=0),
        name="results",
    )(output, grad, encoder, self_w, cross_w, up, down, vectors)


def start_kernel(
    in_ref, norm_ref, qkv_ref, so_ref, cq_ref, ckv_ref, co_ref, down_ref, enc_ref,
    rows_out, self_out, cross_out, down_out, enc_out, rows_ref, self_ref, cross_ref, shard_ref, send_sems, recv_sems, local_sems, *, n
):
    links = Links(send_sems, recv_sems, local_sems)
    member, z, y = links.tensor, links.dp // 2, links.dp % 2
    count = rows_ref.shape[0]
    half = count // 2
    parts = [pl.ds(0, half), pl.ds(half, half)]

    def place(distance):
        return rows_out.at[pl.ds(pl.multiple_of((member ^ distance) * count, count), count)]

    over_x = [links.copy(rows_ref.at[part], place(0).at[part], X) for part in parts]
    over_core = [links.copy(rows_ref, place(0), CORE)]
    over_core += [links.copy(place(2).at[part], place(2).at[part], CORE) for part in parts]
    self_stages = column_stages(links, self_ref, self_out.at[:, y], n)
    cross_stages = column_stages(links, cross_ref, cross_out, n)
    over_y = [links.copy(self_ref, self_out.at[z, y], Y)]
    local = [
        links.local(rows_ref, place(0)),
        links.local(self_ref, self_out.at[z, y]),
        links.local(cross_ref, cross_out.at[z]),
    ]
    width = cq_ref.shape[1]
    for k in range(3):
        self_ref[:, k * width : (k + 1) * width] = qkv_ref[:, k, :]
    self_ref[:, 3 * width :] = so_ref[...].T
    cross_ref[:, :width] = cq_ref[...]
    for k in range(2):
        cross_ref[:, (k + 1) * width : (k + 2) * width] = ckv_ref[:, k, :]
    cross_ref[:, 3 * width :] = co_ref[...].T
    shard_ref[...] = down_ref[...].T
    square = Square(links, shard_ref, down_out)
    enc_count = enc_ref.shape[0]

    def enc_place(distance):
        return enc_out.at[pl.ds(pl.multiple_of((member ^ distance) * enc_count, enc_count), enc_count)]

    enc_x = links.copy(enc_ref, enc_place(0), X)
    enc_core = [links.copy(enc_ref, enc_place(0), CORE), links.copy(enc_place(2), enc_place(2), CORE)]
    local.append(links.local(enc_ref, enc_place(0)))
    links.greet([CORE, X, Y] + z_ways(n))
    for copy in over_y + local[1:]:
        copy.start()
    for copy, _ in self_stages[0]:
        copy.start()
    for part, copy in zip(parts, over_x):

        def norm(rows, part=part):
            rows = pl.ds(pl.multiple_of(part.start + rows.start, 64), 64)
            xhat, _ = normalized(in_ref[rows, :].astype(F32))
            rows_ref[rows, :] = (xhat * norm_ref[0, 0:1, :] + norm_ref[0, 1:2, :]).astype(BF16)

        by_rows(half, 64, norm)
        copy.start()
    for copy in local[:1] + over_core[:1]:
        copy.start()
    square.start()
    enc_x.start()
    enc_core[0].start()
    for self_stage in self_stages:
        if self_stage is not self_stages[0]:
            for copy, _ in self_stage:
                copy.start()
        for copy, index in self_stage:
            copy.wait_recv()
            onward = links.copy(self_out.at[index, y], self_out.at[index, y], Y)
            onward.start()
            over_y.append(onward)
        if self_stage is self_stages[0]:
            for copy, _ in cross_stages[0]:
                copy.start()
    for cross_stage, later in zip(cross_stages, cross_stages[1:] + [[]]):
        for copy, _ in cross_stage:
            copy.wait_recv()
        for copy, _ in later:
            copy.start()
    for copy, onward in zip(over_x, over_core[1:]):
        copy.wait_recv()
        onward.start()
    square.middle()
    enc_x.wait_recv()
    enc_core[1].start()
    enc_x.wait_send()
    square.end()
    for copy in local + over_y + over_core + enc_core:
        copy.wait()
    for copy in over_x:
        copy.wait_send()
    for stage in self_stages + cross_stages:
        for copy, _ in stage:
            copy.wait_send()


def start_gather(rows, norm, qkv, self_out, cross_q, cross_kv, cross_out, down, encoder):
    n = lax.axis_size("dp")
    r, c = cross_q.shape[0], 4 * cross_q.shape[1]
    return pl.pallas_call(
        functools.partial(start_kernel, n=n),
        in_specs=[pl.BlockSpec(memory_space=pltpu.VMEM)] * 9,
        out_specs=[ANY] * 5,
        out_shape=[
            jax.ShapeDtypeStruct((4 * rows.shape[0], rows.shape[1]), BF16),
            jax.ShapeDtypeStruct((n // 2, 2, r, c), BF16),
            jax.ShapeDtypeStruct((n // 2, r, c), BF16),
            jax.ShapeDtypeStruct((2, 2, r, down.shape[0]), BF16),
            jax.ShapeDtypeStruct((4 * encoder.shape[0], encoder.shape[1]), BF16),
        ],
        scratch_shapes=[pltpu.VMEM(rows.shape, BF16)]
        + [pltpu.VMEM((r, c), BF16)] * 2
        + [pltpu.VMEM((r, down.shape[0]), BF16)]
        + link_scratch(2 * n + 15, 5),
        compiler_params=pltpu.CompilerParams(
            vmem_limit_bytes=VMEM_LIMIT, collective_id=0, has_side_effects=True
        ),
        cost_estimate=pl.CostEstimate(flops=0, bytes_accessed=100 * 2**20, transcendentals=0),
        name="start_gather",
    )(rows, norm, qkv, self_out, cross_q, cross_kv, cross_out, down, encoder)


def self_forward_kernel(
    b_ref, x_ref, w_ref, biases_ref, column_ref, up_ref, down_ref,
    q_out, k_ref, v_out, kt_out, ot_ref, lse_ref, terms_ref, whole, next_column, far_down,
    vt_ref, m_s, l_s, acc, column, send_sems, recv_sems, local_sems, *, heads, safe, n
):
    i = pl.program_id(0)
    last = pl.num_programs(0) - 1
    bq, width = q_out.shape
    links = Links(send_sems, recv_sems, local_sems)
    spread = Spread(links, column_ref, column, whole)
    stages = column_stages(links, up_ref, next_column, n)
    keep = links.local(up_ref, next_column.at[links.dp // 2])
    over_z = links.copy(down_ref.at[0], far_down, z_ways(n)[0])

    def next_stage(step):
        for copy, _ in stages[step]:
            copy.wait_recv()
        for copy, _ in stages[step + 1] if step + 1 < len(stages) else []:
            copy.start()

    @pl.when(i == 0)
    def _():
        links.greet([CORE, X, Y] + z_ways(n))
        for copy, _ in stages[0]:
            copy.start()
        spread.start()
        keep.start()

    def onward():
        next_stage(0)
        over_z.start()

    mine = pl.ds(pl.multiple_of(links.tensor * width, width), width)
    projected = dot_nn(x_ref[...], w_ref[:, : 3 * width])
    query = (projected[:, :width] + biases_ref[0:1, mine]).astype(BF16)
    key = projected[:, width : 2 * width].astype(BF16)
    value = (projected[:, 2 * width :] + biases_ref[1:2, mine]).astype(BF16)
    here = pl.ds(pl.multiple_of(i * bq, bq), bq)
    q_out[...] = query
    v_out[...] = value
    kt_out[...] = key.T
    k_ref[here, :] = key
    vt_ref[:, here] = value.T

    m_s[...] = jnp.full_like(m_s, NEGATIVE)
    l_s[...] = jnp.zeros_like(l_s)
    acc[...] = jnp.zeros_like(acc)
    hd = width // heads
    scaled = query * jnp.asarray(1.0 / math.sqrt(hd), BF16)
    q_heads = [head_only(scaled, h, hd) for h in range(heads)]

    def block(first, size, skip, mode):
        rows = pl.ds(pl.multiple_of(first, size), size)
        m_old = m_s[:, skip:]
        l_old = l_s[:, skip:]
        scores = [dot_nt(k_ref[rows, lanes_of(h, hd)[1]], q_heads[h][skip:]) for h in range(heads)]
        if mode != "none":
            bad = self_bad(b_ref, i * bq + skip, first, bq - skip, size, mode == "causal")
            scores = [jnp.where(bad, NEGATIVE, s) for s in scores]
        m_out, l_out, a_out = [], [], []
        for h in range(heads):
            part = slice(h * hd, (h + 1) * hd)
            m_new = jnp.maximum(m_old[h : h + 1, :], jnp.max(scores[h], axis=0, keepdims=True))
            shrink = jnp.exp(m_old[h : h + 1, :] - m_new)
            expos = jnp.exp(scores[h] - m_new)
            l_out.append(l_old[h : h + 1, :] * shrink + jnp.sum(expos, axis=0, keepdims=True))
            m_out.append(m_new)
            a_out.append(acc[part, skip:] * shrink + dot_nn(vt_ref[part, rows], expos.astype(BF16)))
        m_s[:, skip:] = jnp.concatenate(m_out, 0)
        l_s[:, skip:] = jnp.concatenate(l_out, 0)
        for h in range(heads):
            acc[h * hd : (h + 1) * hd, skip:] = a_out[h]

    over_keys(i, bq, safe, block, [(2, 0, onward), (3, 2, spread.middle), (4, 3, spread.last)])
    inverse = 1.0 / l_s[...]
    for h in range(heads):
        part = slice(h * hd, (h + 1) * hd)
        ot_ref[part, :] = (acc[part, :] * inverse[h : h + 1, :]).astype(BF16)
    lse_ref[...] = m_s[...] + jnp.log(l_s[...])
    terms_ref[...] = dot_nt(ot_ref[...].T, w_ref[:, 3 * width :]).astype(BF16)

    @pl.when(i == last)
    def _():
        for step in range(1, len(stages)):
            next_stage(step)
        over_z.wait()
        spread.end()
        for stage in stages:
            for copy, _ in stage:
                copy.wait_send()
        keep.wait()


def self_forward(bounds, x, w, biases, column, up, down, heads, safe):
    n, model = x.shape
    width = w.shape[1] // 4
    bq = 512
    dp = lax.axis_size("dp")
    m, r, c = column.shape
    by_rows_spec = pl.BlockSpec((bq, width), lambda i: (i, 0))
    by_columns_spec = pl.BlockSpec((width, bq), lambda i: (0, i))
    return pl.pallas_call(
        functools.partial(self_forward_kernel, heads=heads, safe=safe, n=dp),
        grid=(n // bq,),
        in_specs=[
            pl.BlockSpec(memory_space=pltpu.SMEM),
            pl.BlockSpec((bq, model), lambda i: (i, 0)),
            const((model, 4 * width)),
            const(biases.shape),
            ANY,
            const(up.shape),
            ANY,
        ],
        out_specs=[
            by_rows_spec,
            const((n, width)),
            by_rows_spec,
            by_columns_spec,
            by_columns_spec,
            pl.BlockSpec((heads, bq), lambda i: (0, i)),
            pl.BlockSpec((bq, model), lambda i: (i, 0)),
            ANY,
            ANY,
            ANY,
        ],
        out_shape=[
            jax.ShapeDtypeStruct((n, width), BF16),
            jax.ShapeDtypeStruct((n, width), BF16),
            jax.ShapeDtypeStruct((n, width), BF16),
            jax.ShapeDtypeStruct((width, n), BF16),
            jax.ShapeDtypeStruct((width, n), BF16),
            jax.ShapeDtypeStruct((heads, n), F32),
            jax.ShapeDtypeStruct((n, model), BF16),
            jax.ShapeDtypeStruct((4, m, 2, r, c), BF16),
            jax.ShapeDtypeStruct((m,) + up.shape, BF16),
            jax.ShapeDtypeStruct(down.shape[1:], BF16),
        ],
        scratch_shapes=[
            pltpu.VMEM((width, n), BF16),
            pltpu.VMEM((heads, bq), F32),
            pltpu.VMEM((heads, bq), F32),
            pltpu.VMEM((width, bq), F32),
            pltpu.VMEM((m, r, c), BF16),
        ]
        + link_scratch(9 + m, 3),
        compiler_params=pltpu.CompilerParams(
            vmem_limit_bytes=VMEM_LIMIT, collective_id=1, has_side_effects=True
        ),
        cost_estimate=pl.CostEstimate(
            flops=12 * n * n * width, bytes_accessed=8 * n * width, transcendentals=n * n * heads // 2
        ),
        name="self_forward",
    )(bounds, x, w, biases, column, up, down)


def after_self_kernel(
    terms_ref, rows_ref, biases_ref, norm_ref, column_ref, down_ref, from_z,
    after_out, second_out, whole_out, down_out, far_down, *scratch, n
):
    links = Links(*scratch[-3:])
    rows_sum = RowSum(links, terms_ref, scratch[:5])
    column = scratch[5]
    spread = SpreadZ(links, down_ref.at[0], from_z, scratch[6], down_out, n)
    over_z = links.copy(down_ref.at[1], far_down, z_ways(n)[0])
    y = links.dp % 2
    near_out, core_out = whole_out.at[0], whole_out.at[1]
    load = links.local(column_ref, column)
    own = links.local(column, near_out.at[:, y])
    over_y = links.copy(column, near_out.at[:, y], Y)
    over_core = [
        links.copy(column, core_out.at[:, y], CORE),
        links.copy(near_out.at[:, 1 - y], core_out.at[:, 1 - y], CORE),
    ]
    links.greet([CORE, X, Y] + z_ways(n))
    rows_sum.start()
    load.start()
    over_z.start()
    load.wait()
    over_y.start()
    own.start()
    rows_sum.middle()
    spread.start()
    over_core[0].start()
    rows_sum.end()

    def norm(rows):
        after = rows_ref[rows, :].astype(F32) + rows_sum.total(rows) + biases_ref[2:3, :]
        after_out[rows, :] = after
        xhat, _ = normalized(after)
        second_out[rows, :] = (xhat * norm_ref[1, 0:1, :] + norm_ref[1, 1:2, :]).astype(BF16)

    by_rows(after_out.shape[0], 64, norm)
    over_y.wait_recv()
    over_core[1].start()
    over_y.wait_send()
    spread.end()
    over_z.wait()
    for copy in [own] + over_core:
        copy.wait()


def sum_after_self(terms, rows, biases, norm, column, down, from_z):
    count, model = rows.shape
    m, r, c = column.shape
    vmem = pl.BlockSpec(memory_space=pltpu.VMEM)
    return pl.pallas_call(
        functools.partial(after_self_kernel, n=2 * m),
        in_specs=[ANY, vmem, vmem, vmem, ANY, ANY, ANY],
        out_specs=[vmem, vmem, ANY, ANY, ANY],
        out_shape=[
            jax.ShapeDtypeStruct((count, model), F32),
            jax.ShapeDtypeStruct((count, model), BF16),
            jax.ShapeDtypeStruct((2, m, 2, r, c), BF16),
            jax.ShapeDtypeStruct((2, m, 2, r, c), BF16),
            jax.ShapeDtypeStruct((2, r, c), BF16),
        ],
        scratch_shapes=row_sum_scratch(count, model)
        + [pltpu.VMEM((m, r, c), BF16), pltpu.VMEM((2, 2, r, c), BF16)]
        + link_scratch(7 + spread_z_copies(2 * m), 8),
        compiler_params=pltpu.CompilerParams(
            vmem_limit_bytes=VMEM_LIMIT, collective_id=8, has_side_effects=True
        ),
        cost_estimate=pl.CostEstimate(flops=0, bytes_accessed=100 * 2**20, transcendentals=0),
        name="sum_after_self",
    )(terms, rows, biases, norm, column, down, from_z)


def self_backward_kernel(
    b_ref, q_ref, k_ref, v_ref, kt_ref, w_ref, mt_ref, lse_ref, back_ref, rows_ref, above_ref, norm_ref,
    up_ref, down_ref, cross_ref, enc_ref,
    dq_ref, dk_ref, dv_ref, wide_out, grad_out, sums_ref, up_out, down_out, cross_out, enc_out,
    dka, dva, dqa, wide, *scratch, bq, heads, safe, n
):
    s = pl.program_id(0)
    last = pl.num_programs(0) - 1
    links = Links(*scratch[-3:])
    member = links.tensor
    x = member // 2
    later = (s // 2 + 1) // 2
    i = s * (1 - x) + ((s + 3) * (1 - later) + (4 - s) * later) * x
    cross = GatherLast(links, cross_ref.at[0], cross_ref.at[1], scratch[:5])
    keep_cross = links.local(cross.column, cross_out)
    columns, slots = scratch[5:7], scratch[7:9]
    sums_z = [Collect(links, column, slot) for column, slot in zip(columns, slots)]
    load_z = [links.local(ref, column) for ref, column in zip((up_ref, down_ref), columns)]
    enc = RowSum(links, enc_ref, scratch[9:14])
    stages = len(sums_z[0].stages)
    count = grad_out.shape[0]
    half = count // 2

    def place(distance, k=None):
        start = (member ^ distance) * count
        if k is None:
            return wide.at[pl.ds(pl.multiple_of(start, half), count)]
        return wide.at[pl.ds(pl.multiple_of(start + k * half, half), half)]

    over_x = [links.copy(place(0, k), place(0, k), X) for k in range(2)]
    over_core = links.copy(place(0), place(0), CORE)
    onward = [links.copy(place(2, k), place(2, k), CORE) for k in range(2)]
    keep_wide = links.local(wide, wide_out)

    def norm_back(k):
        def one(rows):
            rows = pl.ds(pl.multiple_of(k * half + rows.start, 64), 64)
            incoming = back_ref[rows, :]
            rows_grad, gain_terms = norm_rows_back(rows_ref[rows, :], incoming, norm_ref[1, 0:1, :])
            rows_grad = rows_grad + above_ref[rows, :]
            rounded = rows_grad.astype(BF16)
            grad_out[rows, :] = rows_grad
            wide[pl.ds(pl.multiple_of(member * count + rows.start, 64), 64), :] = rounded
            for row, terms in enumerate((gain_terms, incoming, rounded.astype(F32))):
                sums_ref[row : row + 1, :] += jnp.sum(terms, axis=0, keepdims=True)

        by_rows(half, 64, one)

    def arrive(k):
        over_x[k].wait_recv()
        onward[k].start()
        onward[k].wait_recv()

    @pl.when(s == 0)
    def _():
        links.greet([CORE, X, Y] + z_ways(n))
        for copy in load_z:
            copy.start()
        sums_ref[...] = jnp.zeros_like(sums_ref)
        for k in range(2):
            norm_back(k)
            over_x[k].start()
        over_core.start()
        cross.start()
        enc.start()
        for copy, total in zip(load_z, sums_z):
            copy.wait()
            total.start(0)
        dka[...] = jnp.zeros_like(dka)
        dva[...] = jnp.zeros_like(dva)
        over_core.wait_recv()

    @pl.when(s == 2)
    def _():
        arrive(0)
        pl.when(x == 1)(functools.partial(arrive, 1))
        cross.second()

        @pl.when(x == 1)
        def _():
            cross.middle()
            enc.middle()

        for step in range(stages - 1):
            for total in sums_z:
                total.finish(step)
            for total in sums_z:
                total.start(step + 1)

    @pl.when(s == 3)
    def _():
        @pl.when(x == 0)
        def _():
            arrive(1)
            cross.middle()
            enc.middle()

        keep_wide.start()

    width = k_ref.shape[1]
    hd = width // heads
    scale = 1.0 / math.sqrt(hd)
    here = pl.ds(pl.multiple_of(i * bq, bq), bq)
    grads = dot_nn(wide[here, :], w_ref[:, 3 * width :]).astype(BF16)
    products = grads.T.astype(F32) * mt_ref[:, here].astype(F32)
    inner = [jnp.sum(products[h * hd : (h + 1) * hd, :], axis=0, keepdims=True) for h in range(heads)]
    scaled = q_ref[here, :] * jnp.asarray(scale, BF16)
    q_heads = [head_only(scaled, h, hd) for h in range(heads)]
    d_heads = [head_only(grads, h, hd) for h in range(heads)]
    lse = lse_ref[:, here]
    dqa[...] = jnp.zeros_like(dqa)

    def block(first, size, skip, mode):
        rows = pl.ds(pl.multiple_of(first, size), size)
        scores = [dot_nt(k_ref[rows, lanes_of(h, hd)[1]], q_heads[h][skip:]) for h in range(heads)]
        dprobs = [dot_nt(v_ref[rows, lanes_of(h, hd)[1]], d_heads[h][skip:]) for h in range(heads)]
        if mode != "none":
            bad = self_bad(b_ref, i * bq + skip, first, bq - skip, size, mode == "causal")
            scores = [jnp.where(bad, NEGATIVE, s) for s in scores]
        dv_sums, dk_sums = {}, {}
        for h in range(heads):
            part = slice(h * hd, (h + 1) * hd)
            group, _ = lanes_of(h, hd)
            probs = jnp.exp(scores[h] - lse[h : h + 1, skip:])
            ds = (probs * (dprobs[h] - inner[h][:, skip:])).astype(BF16)
            add_group(dv_sums, group, dot_nn(probs.astype(BF16), d_heads[h][skip:]))
            add_group(dk_sums, group, dot_nn(ds, q_heads[h][skip:]))
            dqa[part, skip:] += dot_nn(kt_ref[part, rows], ds)
        for group in dv_sums:
            part = slice(group * LANES, (group + 1) * LANES)
            dva[rows, part] += dv_sums[group]
            dka[rows, part] += dk_sums[group]

    over_keys(i, bq, safe, block)
    dq_ref[here, :] = (dqa[...] * scale).astype(BF16).T

    @pl.when(s == last)
    def _():
        dk_ref[...] = dka[...].astype(BF16)
        dv_ref[...] = dva[...].astype(BF16)
        cross.end()
        keep_cross.start()
        for total, out in zip(sums_z, (up_out, down_out)):
            total.finish(stages - 1)
            out[...] = total.column[total.z].astype(F32)
            total.drain()
        enc.end()

        def store(rows):
            enc_out[rows, :] = enc.total(rows)

        by_rows(enc_out.shape[0], 64, store)
        for copy in over_x + onward + [over_core]:
            copy.wait_send()
        keep_wide.wait()
        keep_cross.wait()


def self_backward(
    bounds, queries, keys, values, keys_t, w, mixed_t, lse, back, rows, above, norm,
    up_column, down_column, cross_sum, enc_terms, heads, safe
):
    n, width = queries.shape
    count, model = rows.shape
    dp = lax.axis_size("dp")
    m, r, c = up_column.shape
    cross_c = cross_sum.shape[4]
    enc_shape = (enc_terms.shape[0] // 4, enc_terms.shape[1])
    bq = 512
    return pl.pallas_call(
        functools.partial(self_backward_kernel, bq=bq, heads=heads, safe=safe, n=dp),
        grid=(n // bq,),
        in_specs=[
            pl.BlockSpec(memory_space=pltpu.SMEM),
            const((n, width)),
            const((n, width)),
            const((n, width)),
            const((width, n)),
            const((model, 4 * width)),
            const((width, n)),
            const((heads, n)),
            const((count, model)),
            const((count, model)),
            const((count, model)),
            const(norm.shape),
        ]
        + [ANY] * 4,
        out_specs=[const((n, width))] * 3
        + [ANY, const((count, model)), const((8, model)), const((r, c)), const((r, c)), ANY, const(enc_shape)],
        out_shape=[jax.ShapeDtypeStruct((n, width), BF16)] * 3
        + [
            jax.ShapeDtypeStruct((n, model), BF16),
            jax.ShapeDtypeStruct((count, model), F32),
            jax.ShapeDtypeStruct((8, model), F32),
            jax.ShapeDtypeStruct((r, c), F32),
            jax.ShapeDtypeStruct((r, c), F32),
            jax.ShapeDtypeStruct((m, r, cross_c), BF16),
            jax.ShapeDtypeStruct(enc_shape, F32),
        ],
        scratch_shapes=[
            pltpu.VMEM((n, width), F32),
            pltpu.VMEM((n, width), F32),
            pltpu.VMEM((width, bq), F32),
            pltpu.VMEM((n, model), BF16),
        ]
        + [pltpu.VMEM((m, r, cross_c), BF16)] * 5
        + [pltpu.VMEM((m, r, c), BF16)] * 4
        + row_sum_scratch(*enc_shape)
        + link_scratch(11 + 2 * m, 8),
        compiler_params=pltpu.CompilerParams(
            vmem_limit_bytes=62 * 2**20, collective_id=5, has_side_effects=True
        ),
        cost_estimate=pl.CostEstimate(
            flops=24 * n * n * width, bytes_accessed=16 * n * width, transcendentals=n * n * heads // 2
        ),
        name="self_backward",
    )(
        bounds, queries, keys, values, keys_t, w, mixed_t, lse, back, rows, above, norm,
        up_column, down_column, cross_sum, enc_terms,
    )


def const(shape):
    return pl.BlockSpec(shape, lambda *_: (0,) * len(shape), pipeline_mode=pl.Buffered(1))


def normalized(rows):
    center = rows - jnp.mean(rows, axis=-1, keepdims=True)
    scale = lax.rsqrt(jnp.mean(center * center, axis=-1, keepdims=True) + EPSILON)
    return center * scale, scale


def norm_rows_back(rows, incoming, gain):
    xhat, scale = normalized(rows)
    e = incoming * gain
    inner = jnp.mean(e * xhat, axis=-1, keepdims=True)
    return scale * (e - jnp.mean(e, axis=-1, keepdims=True) - xhat * inner), incoming * xhat


def by_rows(count, step, body):
    def one(k, c):
        body(pl.ds(pl.multiple_of(k * step, step), step))
        return c

    lax.fori_loop(0, count // step, one, 0)


def cross_forward_kernel(
    len_ref, x_ref, enc_ref, w_ref, biases_ref, rows_ref, norm_ref, column_ref, down_ref, from_z,
    q_out, k_out, v_out, ot_ref, lse_ref, after_ref, third_ref, whole, down_out, hold, send_sems, recv_sems, local_sems, *, heads, n
):
    i = pl.program_id(0)
    last = pl.num_programs(0) - 1
    links = Links(send_sems, recv_sems, local_sems)
    spread = SpreadFar(links, column_ref, whole)
    pieces = len(spread.over_x)
    spread_z = SpreadZ(links, down_ref.at[1], from_z, hold, down_out, n)

    @pl.when(i == 0)
    def _():
        links.greet([CORE, X, Y] + z_ways(n))
        spread.start()
        spread_z.start()
        after_ref[...] = rows_ref[...] + biases_ref[5:6, :]

    def onward(*when):
        for step, k in when:
            pl.when(i == step)(functools.partial(spread.onward, k))

    onward((1, 0), (1, 1), (2, 4), (3, 6), (3, 7))

    width = q_out.shape[2]
    hd = width // heads
    mine = pl.ds(pl.multiple_of((links.tensor ^ i) * width, width), width)
    query = (dot_nn(x_ref[...], w_ref[0, :, :width]) + biases_ref[3:4, mine]).astype(BF16)
    key_value = dot_nn(enc_ref[...], w_ref[0, :, width : 3 * width])
    keys = key_value[:, :width].astype(BF16)
    values = (key_value[:, width:] + biases_ref[4:5, mine]).astype(BF16)
    q_out[0] = query
    k_out[0] = keys
    v_out[0] = values
    values_t = values.T
    scaled = query * jnp.asarray(1.0 / math.sqrt(hd), BF16)
    ok = lax.broadcasted_iota(jnp.int32, (keys.shape[0], 1), 0) < len_ref[0]
    scores = [dot_nt(keys[:, lanes_of(h, hd)[1]], head_only(scaled, h, hd)) for h in range(heads)]
    mixed = []
    for h in range(heads):
        part = slice(h * hd, (h + 1) * hd)
        s = jnp.where(ok, scores[h], NEGATIVE)
        largest = jnp.max(s, axis=0, keepdims=True)
        expos = jnp.exp(s - largest)
        total = jnp.sum(expos, axis=0, keepdims=True)
        mixed.append((dot_nn(values_t[part, :], expos.astype(BF16)) * (1.0 / total)).astype(BF16))
        ot_ref[0, part, :] = mixed[h]
        lse_ref[0, h : h + 1, :] = largest + jnp.log(total)
        if h == heads // 2 - 1:
            onward((1, 2), (1, 3), (2, 5))

            @pl.when(i == last)
            def _():
                for k in range(pieces // 2):
                    spread.last(k)
    after_ref[...] += dot_nt(jnp.concatenate(mixed, 0).T, w_ref[0, :, 3 * width :])

    @pl.when(i == last)
    def _():
        def norm(rows):
            xhat, _ = normalized(after_ref[rows, :])
            third_ref[rows, :] = (xhat * norm_ref[2, 0:1, :] + norm_ref[2, 1:2, :]).astype(BF16)

        by_rows(after_ref.shape[0], 128, norm)
        for k in range(pieces // 2, pieces):
            spread.last(k)
        spread_z.end()
        spread.end()


def cross_forward(lengths, x, encoder, weights, biases, rows, norm, column, down, from_z, heads):
    count, model = x.shape
    n = encoder.shape[0]
    parts, _, columns = weights.shape
    width = columns // 4
    m, r, c = column.shape

    def by_part(*shape):
        return pl.BlockSpec((1,) + shape, lambda i: (i,) + (0,) * len(shape))

    return pl.pallas_call(
        functools.partial(cross_forward_kernel, heads=heads, n=2 * m),
        grid=(parts,),
        in_specs=[
            pl.BlockSpec(memory_space=pltpu.SMEM),
            const((count, model)),
            const((n, model)),
            by_part(model, columns),
            const(biases.shape),
            const((count, model)),
            const(norm.shape),
            ANY,
            ANY,
            ANY,
        ],
        out_specs=[
            by_part(count, width),
            by_part(n, width),
            by_part(n, width),
            by_part(width, count),
            by_part(heads, count),
            const((count, model)),
            const((count, model)),
            ANY,
            ANY,
        ],
        out_shape=[
            jax.ShapeDtypeStruct((parts, count, width), BF16),
            jax.ShapeDtypeStruct((parts, n, width), BF16),
            jax.ShapeDtypeStruct((parts, n, width), BF16),
            jax.ShapeDtypeStruct((parts, width, count), BF16),
            jax.ShapeDtypeStruct((parts, heads, count), F32),
            jax.ShapeDtypeStruct((count, model), F32),
            jax.ShapeDtypeStruct((count, model), BF16),
            jax.ShapeDtypeStruct((2, m, 2, r, c), BF16),
            jax.ShapeDtypeStruct((2, m, 2, r, c), BF16),
        ],
        scratch_shapes=[pltpu.VMEM((2, 2, r, c), BF16)] + link_scratch(32 + spread_z_copies(2 * m), 4),
        compiler_params=pltpu.CompilerParams(
            vmem_limit_bytes=VMEM_LIMIT, collective_id=2, has_side_effects=True
        ),
        cost_estimate=pl.CostEstimate(
            flops=24 * parts * count * n * width,
            bytes_accessed=8 * parts * n * width,
            transcendentals=parts * count * n * heads,
        ),
        name="cross_forward",
    )(lengths, x, encoder, weights, biases, rows, norm, column, down, from_z)


def feed_forward_kernel(
    x_ref, dy_ref, near_up, near_down, far_up, far_down, b_ref, after_ref, biases_ref, norm_ref,
    out_ref, rows_out, low_out, sums_ref, gup_ref, gdown_ref, bias_ref, from_x, from_y,
    xt_ref, dyt_ref, back_ref, give, got, diagonal, loaded, load_sems, send_sems, recv_sems, local_sems, *, chunks
):
    s = pl.program_id(0)
    links = Links(send_sems, recv_sems, local_sems)
    turn = s // chunks
    chunk = s % chunks
    pair = turn // 2
    slot = pair * chunks + chunk
    theirs = turn % 2 == 0
    y = links.dp % 2
    m, r = diagonal.shape[1], diagonal.shape[2]
    low, high = pl.ds(0, m // 2), pl.ds(m // 2, m - m // 2)
    links.used = 2 * chunks
    across = [
        links.copy(diagonal.at[:, low], from_x, X),
        links.copy(diagonal.at[:, high], from_y, Y),
    ]
    to_core = pltpu.make_async_remote_copy(
        src_ref=give.at[chunk],
        dst_ref=got.at[slot],
        send_sem=send_sems.at[slot],
        recv_sem=recv_sems.at[slot],
        device_id=links.partner(CORE),
        device_id_type=pl.DeviceIdType.MESH,
    )

    size = loaded.shape[3]

    def fetch(step, act):
        block = 3 - step // chunks
        slot = step % 2
        first = (step % chunks) * size

        def both(*sources):
            for k, source in enumerate(sources):
                columns = pl.ds(pl.multiple_of(first, size), size)
                act(pltpu.make_async_copy(source.at[:, columns], loaded.at[slot, k], load_sems.at[slot, k]))

        @pl.when(block >= 2)
        def _():
            both(far_up.at[block - 2], far_down.at[block - 2])

        @pl.when(block < 2)
        def _():
            both(near_up.at[block], near_down.at[block])

    @pl.when(s == 0)
    def _():
        fetch(0, lambda copy: copy.start())
        links.greet([CORE, X, Y])
        out_ref[...] = after_ref[...] + biases_ref[6:7, :]
        back_ref[...] = jnp.zeros_like(back_ref)
        xt_ref[...] = x_ref[...].T
        dyt_ref[...] = dy_ref[...].T
        sums_ref[...] = jnp.zeros_like(sums_ref)

    fetch(s, lambda copy: copy.wait())

    @pl.when(s + 1 < pl.num_programs(0))
    def _():
        fetch(s + 1, lambda copy: copy.start())

    up_ref, down_ref = loaded.at[s % 2, 0], loaded.at[s % 2, 1]
    lines = size // LANES
    line = ((links.tensor ^ (3 - turn)) * chunks + chunk) * lines
    shift = jnp.concatenate([b_ref[pl.ds(line + k, 1), :] for k in range(lines)], axis=1)
    pre_act = dot_nn(x_ref[...], up_ref[...]) + shift
    hidden_grad = dot_nn(dy_ref[...], down_ref[...])
    normal_cdf = 0.5 * (1.0 + lax.erf(pre_act * (1.0 / math.sqrt(2.0))))
    density = jnp.exp(-0.5 * pre_act * pre_act) * (1.0 / math.sqrt(2.0 * math.pi))
    hidden = (pre_act * normal_cdf).astype(BF16)
    pre_grad = (hidden_grad * (normal_cdf + pre_act * density)).astype(BF16)
    bias_ref[0] = jnp.sum(pre_grad.astype(F32), axis=0, keepdims=True)

    @pl.when(turn % 2 == 1)
    def _():
        to_core.wait_send()

    give[chunk, 0] = dot_nn(xt_ref[...], pre_grad).astype(BF16)
    give[chunk, 1] = dot_nn(dyt_ref[...], hidden).astype(BF16)
    out_ref[...] += dot_nt(hidden, down_ref[...])
    back_ref[...] += dot_nt(pre_grad, up_ref[...])

    @pl.when(theirs)
    def _():
        to_core.start()

    @pl.when(jnp.logical_not(theirs))
    def _():
        to_core.wait_recv()
        gup_ref[0] = (give[chunk, 0].astype(F32) + got[slot, 0].astype(F32)).astype(BF16)
        gdown_ref[0] = (give[chunk, 1].astype(F32) + got[slot, 1].astype(F32)).astype(BF16)

    for k in range(chunks):

        @pl.when(s == chunks + k)
        def _():
            def keep(z, carry):
                rows = pl.ds(pl.multiple_of((2 * z + 1 - y) * r, r), r)
                size = gup_ref.shape[2]
                diagonal[0, z, :, k * size : (k + 1) * size] = gup_ref[0, rows, :]
                diagonal[1, z, :, k * size : (k + 1) * size] = gdown_ref[0, rows, :]
                return carry

            lax.fori_loop(0, m, keep, 0)
            if k == chunks - 1:
                for copy in across:
                    copy.start()

    @pl.when(s == pl.num_programs(0) - 1)
    def _():
        def norm_back(rows):
            third = back_ref[rows, :]
            upstream = dy_ref[rows, :].astype(F32)
            rows_grad, gain_terms = norm_rows_back(after_ref[rows, :], third, norm_ref[2, 0:1, :])
            rows_grad = rows_grad + upstream
            low = rows_grad.astype(BF16)
            rows_out[rows, :] = rows_grad
            low_out[rows, :] = low
            for k, terms in enumerate((gain_terms, third, low.astype(F32), upstream)):
                sums_ref[k : k + 1, :] += jnp.sum(terms, axis=0, keepdims=True)

        by_rows(x_ref.shape[0], 128, norm_back)
        for copy in across:
            copy.wait()


def feed_forward(x, dy, weights, bias, after, biases, norm):
    rows, width = x.shape
    hidden = weights[0].shape[2]
    size = min(512, hidden)
    chunks = hidden // size

    n = lax.axis_size("dp")
    m, r = n // 2, width // n

    def block(s):
        return 3 - s // chunks

    def placed(s):
        turn = s // chunks
        return (1 - turn // 2, 0, (s % chunks) * (turn % 2))

    rows_spec = const((rows, width))
    grad_spec = pl.BlockSpec((1, width, size), placed)
    bias_spec = pl.BlockSpec((1, 1, size), lambda s: (block(s), 0, s % chunks))
    return pl.pallas_call(
        functools.partial(feed_forward_kernel, chunks=chunks),
        grid=(4 * chunks,),
        in_specs=[
            rows_spec,
            rows_spec,
            ANY,
            ANY,
            ANY,
            ANY,
            const(bias.shape),
            rows_spec,
            const(biases.shape),
            const(norm.shape),
        ],
        out_specs=[rows_spec, rows_spec, rows_spec, const((8, width)), grad_spec, grad_spec, bias_spec, ANY, ANY],
        out_shape=[
            jax.ShapeDtypeStruct((rows, width), F32),
            jax.ShapeDtypeStruct((rows, width), F32),
            jax.ShapeDtypeStruct((rows, width), BF16),
            jax.ShapeDtypeStruct((8, width), F32),
            jax.ShapeDtypeStruct((2, width, hidden), BF16),
            jax.ShapeDtypeStruct((2, width, hidden), BF16),
            jax.ShapeDtypeStruct((4, 1, hidden), F32),
            jax.ShapeDtypeStruct((2, m // 2, r, hidden), BF16),
            jax.ShapeDtypeStruct((2, m - m // 2, r, hidden), BF16),
        ],
        scratch_shapes=[
            pltpu.VMEM((width, rows), BF16),
            pltpu.VMEM((width, rows), BF16),
            pltpu.VMEM((rows, width), F32),
            pltpu.VMEM((chunks, 2, width, size), BF16),
            pltpu.VMEM((2 * chunks, 2, width, size), BF16),
            pltpu.VMEM((2, m, r, hidden), BF16),
            pltpu.VMEM((2, 2, width, size), BF16),
            pltpu.SemaphoreType.DMA((2, 2)),
        ]
        + link_scratch(2 * chunks + 2, 1),
        compiler_params=pltpu.CompilerParams(
            vmem_limit_bytes=VMEM_LIMIT, collective_id=3, has_side_effects=True
        ),
        cost_estimate=pl.CostEstimate(
            flops=48 * rows * width * hidden, bytes_accessed=40 * 2**20, transcendentals=8 * rows * hidden
        ),
        name="feed_forward",
    )(x, dy, *weights, bias, after, biases, norm)


def cross_backward_kernel(
    len_ref, low_ref, x_ref, enc_ref, w_ref, q_ref, k_ref, v_ref, mt_ref, lse_ref, up_ref, down_ref, from_x, from_y,
    back_ref, enc_out, grad_ref, bq_ref, bv_ref, up_out, down_out,
    low_t, x_t, enc_t, enc_acc, give, got, *scratch, heads, bk
):
    i = pl.program_id(0)
    last = pl.num_programs(0) - 1
    links = Links(*scratch[14:])
    sums = [
        Gather(links, ref.at[0], ref.at[1], from_x.at[k], from_y.at[k], scratch[7 * k : 7 * k + 7])
        for k, ref in enumerate((up_ref, down_ref))
    ]
    leave = [links.local(g.column, out) for g, out in zip(sums, (up_out, down_out))]
    pair = i // 2
    to_core = pltpu.make_async_remote_copy(
        src_ref=give,
        dst_ref=got.at[pair],
        send_sem=links.send_sems.at[links.used + pair],
        recv_sem=links.recv_sems.at[links.used + pair],
        device_id=links.partner(CORE),
        device_id_type=pl.DeviceIdType.MESH,
    )

    @pl.when(i == 0)
    def _():
        links.greet([CORE, X, Y])
        for g in sums:
            g.start()
        low_t[...] = low_ref[...].T
        x_t[...] = x_ref[...].T
        enc_t[...] = enc_ref[...].T
        back_ref[...] = jnp.zeros_like(back_ref)
        enc_acc[...] = jnp.zeros_like(enc_acc)

    @pl.when(i == 1)
    def _():
        for g in sums:
            g.middle()

    rows, width = q_ref.shape[1:]
    n = k_ref.shape[1]
    hd = width // heads
    scale = 1.0 / math.sqrt(hd)
    w_query, w_keyval, w_out = w_ref.at[0, :, :width], w_ref.at[0, :, width : 3 * width], w_ref.at[0, :, 3 * width :]
    grads = dot_nn(low_ref[...], w_out[...]).astype(BF16)
    mixed_t = mt_ref[0]
    products = grads.T.astype(F32) * mixed_t.astype(F32)
    inner = [jnp.sum(products[h * hd : (h + 1) * hd, :], axis=0, keepdims=True) for h in range(heads)]
    scaled = q_ref[0] * jnp.asarray(scale, BF16)
    q_heads = [head_only(scaled, h, hd) for h in range(heads)]
    d_heads = [head_only(grads, h, hd) for h in range(heads)]
    lse = lse_ref[0]
    keys_t = k_ref[0].T
    dq = [None] * heads
    dkv = []
    for j in range(n // bk):
        span = slice(j * bk, (j + 1) * bk)
        ok = j * bk + lax.broadcasted_iota(jnp.int32, (bk, 1), 0) < len_ref[0]
        scores = [dot_nt(k_ref[0, span, lanes_of(h, hd)[1]], q_heads[h]) for h in range(heads)]
        dprobs = [dot_nt(v_ref[0, span, lanes_of(h, hd)[1]], d_heads[h]) for h in range(heads)]
        dv_sums, dk_sums = {}, {}
        for h in range(heads):
            part = slice(h * hd, (h + 1) * hd)
            group, _ = lanes_of(h, hd)
            probs = jnp.exp(jnp.where(ok, scores[h], NEGATIVE) - lse[h : h + 1, :])
            ds = (probs * (dprobs[h] - inner[h])).astype(BF16)
            add_group(dv_sums, group, dot_nn(probs.astype(BF16), d_heads[h]))
            add_group(dk_sums, group, dot_nn(ds, q_heads[h]))
            dq_h = dot_nn(keys_t[part, span], ds)
            dq[h] = dq_h if dq[h] is None else dq[h] + dq_h
        block = jnp.concatenate([sums_of[g].astype(BF16) for sums_of in (dk_sums, dv_sums) for g in sorted(sums_of)], 1)
        enc_acc[span, :] += dot_nt(block, w_keyval[...])
        dkv.append(block)
    dq = (jnp.concatenate(dq, 0) * scale).astype(BF16).T
    dkv = jnp.concatenate(dkv, 0)
    bq_ref[0] = jnp.sum(dq.astype(F32), axis=0, keepdims=True)
    bv_ref[0] = jnp.sum(dkv[:, width:].astype(F32), axis=0, keepdims=True)
    back_ref[...] += dot_nt(dq, w_query[...])

    @pl.when(i % 2 == 1)
    def _():
        to_core.wait_send()

    give[:, :width] = dot_nn(x_t[...], dq).astype(BF16)
    give[:, width : 3 * width] = dot_nn(enc_t[...], dkv).astype(BF16)
    give[:, 3 * width :] = dot_nn(low_t[...], mixed_t.T).astype(BF16)

    @pl.when(i % 2 == 0)
    def _():
        to_core.start()

    @pl.when(i % 2 == 1)
    def _():
        to_core.wait_recv()
        grad_ref[0] = (give[...].astype(F32) + got[pair].astype(F32)).astype(BF16)

    @pl.when(i == last)
    def _():
        enc_out[...] = enc_acc[...].astype(BF16)
        for g, copy in zip(sums, leave):
            g.end()
            copy.start()
        for copy in leave:
            copy.wait()


def cross_backward(
    lengths, low, x, encoder, weights, queries, keys, values, mixed_t, lse, up_sum, down_sum, from_x, from_y, heads
):
    count, model = x.shape
    n = encoder.shape[0]
    parts, _, columns = weights.shape
    width = columns // 4
    _, m, _, r, c = up_sum.shape

    def by_part(*shape):
        return pl.BlockSpec((1,) + shape, lambda i: (i ^ 1,) + (0,) * len(shape))

    return pl.pallas_call(
        functools.partial(cross_backward_kernel, heads=heads, bk=256),
        grid=(parts,),
        in_specs=[
            pl.BlockSpec(memory_space=pltpu.SMEM),
            const((count, model)),
            const((count, model)),
            const((n, model)),
            by_part(model, columns),
            by_part(count, width),
            by_part(n, width),
            by_part(n, width),
            by_part(width, count),
            by_part(heads, count),
            ANY,
            ANY,
            ANY,
            ANY,
        ],
        out_specs=[
            const((count, model)),
            const((n, model)),
            pl.BlockSpec((1, model, columns), lambda i: (i // 2, 0, 0), pipeline_mode=pl.Buffered(1)),
            by_part(1, width),
            by_part(1, width),
            ANY,
            ANY,
        ],
        out_shape=[
            jax.ShapeDtypeStruct((count, model), F32),
            jax.ShapeDtypeStruct((n, model), BF16),
            jax.ShapeDtypeStruct((2, model, columns), BF16),
            jax.ShapeDtypeStruct((parts, 1, width), F32),
            jax.ShapeDtypeStruct((parts, 1, width), F32),
            jax.ShapeDtypeStruct((m, r, c), BF16),
            jax.ShapeDtypeStruct((m, r, c), BF16),
        ],
        scratch_shapes=[
            pltpu.VMEM((model, count), BF16),
            pltpu.VMEM((model, count), BF16),
            pltpu.VMEM((model, n), BF16),
            pltpu.VMEM((n, model), F32),
            pltpu.VMEM((model, columns), BF16),
            pltpu.VMEM((2, model, columns), BF16),
        ]
        + gather_scratch(m, r, c) * 2
        + link_scratch(10, 12),
        compiler_params=pltpu.CompilerParams(
            vmem_limit_bytes=60 * 2**20, collective_id=4, has_side_effects=True
        ),
        cost_estimate=pl.CostEstimate(
            flops=48 * parts * count * n * width,
            bytes_accessed=16 * parts * n * width,
            transcendentals=parts * count * n * heads,
        ),
        name="cross_backward",
    )(lengths, low, x, encoder, weights, queries, keys, values, mixed_t, lse, up_sum, down_sum, from_x, from_y)


def on_device(
    block_in,
    encoder_out,
    out_grad,
    bounds,
    enc_lengths,
    norm_params,
    w_qkv,
    w_self_out,
    w_cross_q,
    w_cross_kv,
    w_cross_out,
    w_up,
    w_down,
    biases,
    up_bias,
):
    groups_count = lax.axis_size("dp")
    width = w_cross_q.shape[1]
    hidden_width = w_up.shape[1]
    heads = H // 4
    own_rows, model_width = block_in.shape
    w_rows = w_cross_q.shape[0]

    first_in, self_w, cross_column, down_square, enc_all = start_gather(
        block_in,
        norm_params,
        w_qkv,
        w_self_out,
        w_cross_q,
        w_cross_kv,
        w_cross_out,
        w_down,
        encoder_out,
    )
    self_w = self_w.reshape(model_width, 4 * width)

    self_safe = 1024
    queries, key_rows, value_rows, keys_t, self_mixed_t, self_lse, terms, cross_w, up_column, near_z = self_forward(
        bounds,
        first_in,
        self_w,
        biases,
        cross_column,
        w_up,
        down_square,
        heads,
        self_safe,
    )
    cross_w = cross_w.reshape(4, model_width, 4 * width)
    after_self, second_in, near_up, near_down, far_z = sum_after_self(
        terms, block_in, biases, norm_params, up_column, down_square, near_z
    )

    cross_q, cross_k, cross_v, cross_mixed_t, cross_lse, after_cross, third_in, far_up, far_down = cross_forward(
        enc_lengths,
        second_in,
        enc_all,
        cross_w,
        biases,
        after_self,
        norm_params,
        up_column,
        down_square,
        far_z,
        heads,
    )

    output, cross_rows_grad, cross_low, ffn_sums, up_sum, down_sum, bias_up_parts, from_x, from_y = feed_forward(
        third_in,
        out_grad,
        [w.reshape(2, model_width, hidden_width) for w in (near_up, near_down, far_up, far_down)],
        up_bias.reshape(-1, LANES),
        after_cross,
        biases,
        norm_params,
    )

    by_shard = (2, groups_count // 2, 2, w_rows, hidden_width)
    second_grad, enc_terms, cross_sum, bias_cq_parts, bias_cv_parts, up_column, down_column = cross_backward(
        enc_lengths,
        cross_low,
        second_in,
        enc_all,
        cross_w,
        cross_q,
        cross_k,
        cross_v,
        cross_mixed_t,
        cross_lse,
        up_sum.reshape(by_shard),
        down_sum.reshape(by_shard),
        from_x,
        from_y,
        heads,
    )
    cross_sum = cross_sum.reshape(2, groups_count // 2, 2, w_rows, 4 * width)

    (
        self_dq, self_dk, self_dv, self_wide, self_rows_grad, self_sums,
        summed_up, summed_down, cross_column, encoder_grad,
    ) = self_backward(
        bounds,
        queries,
        key_rows,
        value_rows,
        keys_t,
        self_w,
        self_mixed_t,
        self_lse,
        second_grad,
        after_self,
        cross_rows_grad,
        norm_params,
        up_column,
        down_column,
        cross_sum,
        enc_terms,
        heads,
        self_safe,
    )
    input_grad, summed_self, vectors, summed_cross = tail(
        self_dq,
        self_dk,
        self_dv,
        self_w,
        first_in,
        self_wide,
        self_mixed_t,
        block_in,
        self_rows_grad,
        cross_column,
        norm_params,
        self_sums,
        ffn_sums,
        bias_cq_parts,
        bias_cv_parts,
        bias_up_parts,
    )
    output, input_grad, encoder_grad, *weights_and_vectors = results(
        output, input_grad, encoder_grad, summed_self, summed_cross, summed_up, summed_down, vectors, 1.0 / groups_count
    )
    g_qkv, g_so, g_cq, g_ckv, g_co, g_up, g_down, g_norm, g_biases, g_shift = weights_and_vectors
    return (
        output,
        input_grad,
        encoder_grad,
        g_norm,
        g_qkv,
        g_so,
        g_cq,
        g_ckv,
        g_co,
        g_up,
        g_down,
        g_biases,
        g_shift.reshape(-1),
    )


def solution(mesh):
    rows = P(("dp", "tensor"), None)
    placed = (
        rows,
        rows,
        rows,
        P("dp", None),
        P("dp"),
        P(),
        P("dp", None, "tensor"),
        P("tensor", "dp"),
        P("dp", "tensor"),
        P("dp", None, "tensor"),
        P("tensor", "dp"),
        P("dp", "tensor"),
        P("tensor", "dp"),
        P(),
        P(),
    )
    return jax.shard_map(
        on_device,
        mesh=mesh,
        in_specs=placed,
        out_specs=(
            rows,
            rows,
            rows,
            P(),
            P("dp", None, "tensor"),
            P("tensor", "dp"),
            P("dp", "tensor"),
            P("dp", None, "tensor"),
            P("tensor", "dp"),
            P("dp", "tensor"),
            P("tensor", "dp"),
            P(),
            P(),
        ),
        check_vma=False,
    )
```

```python
import functools
import math

import jax
import jax.numpy as jnp
from jax import lax
from jax.experimental import pallas as pl
from jax.experimental.pallas import tpu as pltpu
from jax.sharding import PartitionSpec as P

H = 16
EPSILON = 1e-05
NEGATIVE = -1e30
F32 = jnp.float32
BF16 = jnp.bfloat16
VMEM_LIMIT = 56 * 2**20


def dot_nt(a, b):
    return lax.dot_general(a, b, (((1,), (1,)), ((), ())), preferred_element_type=F32)


def dot_nn(a, b):
    return lax.dot_general(a, b, (((1,), (0,)), ((), ())), preferred_element_type=F32)


def dot_tn(a, b):
    return lax.dot_general(a, b, (((0,), (0,)), ((), ())), preferred_element_type=F32)


LANES = 128


def lanes_of(h, size):
    group = h * size // LANES
    return group, slice(group * LANES, (group + 1) * LANES)


def head_only(x, h, size):
    group, part = lanes_of(h, size)
    lane = group * LANES + lax.broadcasted_iota(jnp.int32, (x.shape[0], LANES), 1)
    return jnp.where((lane >= h * size) & (lane < (h + 1) * size), x[:, part], jnp.zeros((), x.dtype))


def add_group(sums, group, value):
    sums[group] = value if group not in sums else sums[group] + value


def self_bad(b_ref, q_start, k_start, bq, bk, causal):
    qi = q_start + lax.broadcasted_iota(jnp.int32, (1, bq), 1)
    kj = k_start + lax.broadcasted_iota(jnp.int32, (bk, 1), 0)
    bad = (qi >= b_ref[0, 1]) & ((kj >= b_ref[0, 0]) & (kj < b_ref[0, 1]))
    if causal:
        bad = bad | (kj > qi)
    return bad


def over_keys(i, bq, safe, block, between=()):
    def visit(j, c):
        for at_i, at_j, action in between:
            pl.when((i == at_i) & (j == at_j))(action)

        @pl.when(j < safe // bq)
        def _():
            block(j * bq, bq, 0, "none")

        @pl.when(j >= safe // bq)
        def _():
            block(j * bq, bq, 0, "segment")

        return c

    lax.fori_loop(0, i, visit, 0)
    half = bq // 2
    block(i * bq, half, 0, "causal")
    block(i * bq + half, half, half, "causal")


CORE = ("tensor", 1)
X = ("tensor", 2)
Y = ("dp", 1)
ANY = pl.BlockSpec(memory_space=pl.ANY)


class Links:
    def __init__(self, send_sems, recv_sems, local_sems):
        self.dp = lax.axis_index("dp")
        self.tensor = lax.axis_index("tensor")
        self.send_sems, self.recv_sems, self.local_sems = send_sems, recv_sems, local_sems
        self.used = 0
        self.used_local = 0

    def partner(self, way):
        axis, distance = way
        if axis == "tensor":
            return (self.dp, self.tensor ^ distance)
        return (self.dp ^ distance, self.tensor)

    def greet(self, ways):
        barrier = pltpu.get_barrier_semaphore()
        for way in ways:
            pl.semaphore_signal(
                barrier, inc=1, device_id=self.partner(way), device_id_type=pl.DeviceIdType.MESH
            )
        pl.semaphore_wait(barrier, len(ways))

    def copy(self, source, target, way):
        k = self.used
        self.used += 1
        return pltpu.make_async_remote_copy(
            src_ref=source,
            dst_ref=target,
            send_sem=self.send_sems.at[k],
            recv_sem=self.recv_sems.at[k],
            device_id=self.partner(way),
            device_id_type=pl.DeviceIdType.MESH,
        )

    def local(self, source, target):
        k = self.used_local
        self.used_local += 1
        return pltpu.make_async_copy(source, target, self.local_sems.at[k])


def link_scratch(copies, local):
    return [
        pltpu.SemaphoreType.DMA((copies,)),
        pltpu.SemaphoreType.DMA((copies,)),
        pltpu.SemaphoreType.DMA((local,)),
    ]


def z_distances(n):
    found = []
    m = n // 2
    while m > 1:
        m //= 2
        found.append(m)
    return found


def z_ways(n):
    return [("dp", 2 * distance) for distance in z_distances(n)]


def column_stages(links, shard, column, n):
    z = links.dp // 2
    held = [z]
    stages = []
    for distance in z_distances(n):
        stages.append(
            [
                (
                    links.copy(shard if k == 0 else column.at[index], column.at[index], ("dp", 2 * distance)),
                    index ^ distance,
                )
                for k, index in enumerate(held)
            ]
        )
        held = held + [index ^ distance for index in held]
    return stages


class Spread:
    def __init__(self, links, source, column, whole):
        y = links.dp % 2
        half = column.shape[0] // 2
        low, high = pl.ds(0, half), pl.ds(half, half)
        near, near_core, far, far_core = (whole.at[k] for k in range(4))
        self.load = links.local(source, column)
        self.own = links.local(column, near.at[:, y])
        self.first = [
            links.copy(column, near.at[:, y], Y),
            links.copy(column, far.at[:, y], X),
        ]
        self.core = [links.copy(column, near_core.at[:, y], CORE)]
        self.second = [
            links.copy(near.at[low, 1 - y], far.at[low, 1 - y], X),
            links.copy(far.at[high, y], far.at[high, y], Y),
        ]
        self.core_second = [
            links.copy(near.at[:, 1 - y], near_core.at[:, 1 - y], CORE),
            links.copy(far.at[:, y], far_core.at[:, y], CORE),
        ]
        self.core_third = [links.copy(far.at[:, 1 - y], far_core.at[:, 1 - y], CORE)]

    def start(self):
        self.load.start()
        self.load.wait()
        for copy in self.first + self.core + [self.own]:
            copy.start()

    def middle(self):
        for copy in self.first:
            copy.wait_recv()
        for copy in self.second + self.core_second:
            copy.start()

    def last(self):
        for copy in self.second:
            copy.wait_recv()
        for copy in self.core_third:
            copy.start()

    def end(self):
        self.own.wait()
        for copy in self.first + self.second:
            copy.wait_send()
        for copy in self.core + self.core_second + self.core_third:
            copy.wait()


def add_to(total_ref, other_ref):
    def one(k, c):
        total_ref[k] = (total_ref[k].astype(F32) + other_ref[k].astype(F32)).astype(BF16)
        return c

    lax.fori_loop(0, total_ref.shape[0], one, 0)


class Gather:
    def __init__(self, links, near, far, from_x, from_y, buffers):
        y = links.dp % 2
        self.column, self.over_y, self.over_x, self.add_y, self.add_x, self.sum_y, self.sum_x = buffers
        m = self.column.shape[0]
        low, high = pl.ds(0, m // 2), pl.ds(m // 2, m - m // 2)
        self.loads = [
            links.local(near.at[low, 1 - y], self.over_y),
            links.local(far.at[high, y], self.over_x),
            links.local(from_x, self.add_y),
            links.local(from_y, self.add_x),
            links.local(near.at[:, y], self.column),
        ]
        self.first = [
            links.copy(far.at[low, y], self.sum_x.at[low], X),
            links.copy(near.at[high, 1 - y], self.sum_y.at[high], Y),
        ]
        self.second = [
            links.copy(self.over_x, self.sum_x.at[high], X),
            links.copy(self.over_y, self.sum_y.at[low], Y),
        ]

    def start(self):
        for copy in self.first + self.loads:
            copy.start()

    def middle(self):
        for copy in self.loads:
            copy.wait()
        add_to(self.over_x, self.add_x)
        add_to(self.over_y, self.add_y)
        for copy in self.second:
            copy.start()

    def end(self):
        for copy in self.first + self.second:
            copy.wait_recv()
        add_to(self.column, self.sum_y)
        add_to(self.column, self.sum_x)
        for copy in self.first + self.second:
            copy.wait_send()


def gather_scratch(m, r, c):
    whole = pltpu.VMEM((m, r, c), BF16)
    half = pltpu.VMEM((m // 2, r, c), BF16)
    return [whole] + [half] * 4 + [whole] * 2


class GatherLast:
    def __init__(self, links, near, far, buffers):
        y = links.dp % 2
        self.column, self.over_x, self.diagonal, self.sum_y, self.sum_x = buffers
        self.loads = [links.local(far.at[:, y], self.over_x), links.local(near.at[:, y], self.column)]
        self.first = links.copy(far.at[:, 1 - y], self.diagonal, Y)
        self.over_y = links.copy(near.at[:, 1 - y], self.sum_y, Y)
        self.along_x = links.copy(self.over_x, self.sum_x, X)

    def start(self):
        self.first.start()
        for copy in self.loads:
            copy.start()

    def second(self):
        self.first.wait_recv()
        self.over_y.start()

    def middle(self):
        for copy in self.loads:
            copy.wait()
        add_to(self.over_x, self.diagonal)
        self.along_x.start()

    def end(self):
        self.over_y.wait_recv()
        self.along_x.wait_recv()
        add_to(self.column, self.sum_y)
        add_to(self.column, self.sum_x)
        for copy in (self.first, self.over_y, self.along_x):
            copy.wait_send()


class Collect:
    def __init__(self, links, column, slots):
        z = links.dp // 2
        self.column, self.slots, self.z = column, slots, z
        m = column.shape[0]
        distances = z_distances(2 * m)[::-1]
        self.stages = []
        first = 0
        for step, distance in enumerate(distances):
            kept = [0]
            for other in distances[step + 1 :]:
                kept = kept + [k ^ other for k in kept]
            self.stages.append(
                [
                    (links.copy(column.at[z ^ distance ^ k], slots.at[first + i], ("dp", 2 * distance)), first + i, z ^ k)
                    for i, k in enumerate(kept)
                ]
            )
            first += len(kept)

    def start(self, step):
        for copy, _, _ in self.stages[step]:
            copy.start()

    def finish(self, step):
        for copy, slot, index in self.stages[step]:
            copy.wait_recv()
            self.column[index] = (self.column[index].astype(F32) + self.slots[slot].astype(F32)).astype(BF16)

    def drain(self):
        for stage in self.stages:
            for copy, _, _ in stage:
                copy.wait_send()


class Square:
    def __init__(self, links, shard, out):
        y = links.dp % 2
        c = shard.shape[1]
        low, high = pl.ds(0, c // 2), pl.ds(c // 2, c // 2)
        self.own = links.local(shard, out.at[0, y])
        self.first = [links.copy(shard, out.at[0, y], Y), links.copy(shard, out.at[1, y], X)]
        self.second = [
            links.copy(out.at[0, 1 - y, :, low], out.at[1, 1 - y, :, low], X),
            links.copy(out.at[1, y, :, high], out.at[1, y, :, high], Y),
        ]

    def start(self):
        for copy in self.first + [self.own]:
            copy.start()

    def middle(self):
        for copy in self.first:
            copy.wait_recv()
        for copy in self.second:
            copy.start()

    def end(self):
        for copy in self.first:
            copy.wait_send()
        for copy in self.second:
            copy.wait()
        self.own.wait()


class SpreadZ:
    def __init__(self, links, own, other, hold, whole, n):
        z = links.dp // 2
        distances = z_distances(n)
        there = z ^ distances[0]
        final, core = whole.at[0], whole.at[1]
        self.loads = [links.local(own, hold.at[0]), links.local(other, hold.at[1])]
        self.stores = [links.local(hold.at[0], final.at[z]), links.local(hold.at[1], final.at[there])]
        self.core = [links.copy(hold.at[0], core.at[z], CORE), links.copy(hold.at[1], core.at[there], CORE)]
        held = [(hold.at[0], z), (hold.at[1], there)]
        self.stages, self.core_stages = [], []
        for distance in distances[1:]:
            came = [index ^ distance for _, index in held]
            self.stages.append([links.copy(ref, final.at[index], ("dp", 2 * distance)) for ref, index in held])
            self.core_stages.append([links.copy(final.at[index], core.at[index], CORE) for index in came])
            held = held + [(final.at[index], index) for index in came]

    def start(self):
        for copy in self.loads:
            copy.start()
        for copy in self.loads:
            copy.wait()
        for copy in self.stages[0] + self.stores + self.core:
            copy.start()

    def end(self):
        for step, (stage, core_stage) in enumerate(zip(self.stages, self.core_stages)):
            for copy, onward in zip(stage, core_stage):
                copy.wait_recv()
                onward.start()
            for copy in self.stages[step + 1] if step + 1 < len(self.stages) else []:
                copy.start()
        for copy in self.stores + self.core:
            copy.wait()
        for stage, core_stage in zip(self.stages, self.core_stages):
            for copy in stage:
                copy.wait_send()
            for copy in core_stage:
                copy.wait()


def spread_z_copies(n):
    return 2 * n


class SpreadFar:
    def __init__(self, links, column, whole):
        y = links.dp % 2
        far, far_core = whole.at[0], whole.at[1]
        m, _, c = column.shape
        step = max(m // 4, 1)
        self.over_x, self.over_y, self.core_x, self.core_y = [], [], [], []
        for k in range(m // step):
            for h in range(2):
                z, part = pl.ds(k * step, step), pl.ds(h * (c // 2), c // 2)
                own = far.at[z, y, :, part]
                other = far.at[z, 1 - y, :, part]
                self.over_x.append(links.copy(column.at[z, :, part], own, X))
                self.over_y.append(links.copy(own, own, Y))
                self.core_x.append(links.copy(own, far_core.at[z, y, :, part], CORE))
                self.core_y.append(links.copy(other, far_core.at[z, 1 - y, :, part], CORE))

    def start(self):
        for copy in self.over_x:
            copy.start()

    def onward(self, k):
        self.over_x[k].wait_recv()
        self.over_y[k].start()
        self.core_x[k].start()

    def last(self, k):
        self.over_y[k].wait_recv()
        self.core_y[k].start()

    def end(self):
        for copy in self.over_x + self.over_y:
            copy.wait_send()
        for copy in self.core_x + self.core_y:
            copy.wait()


class RowSum:
    def __init__(self, links, terms, buffers):
        self.near, self.far, self.got_near, self.got_far, self.got_x = buffers
        count = self.near.shape[0]

        def rows(distance):
            start = pl.multiple_of((links.tensor ^ distance) * count, count)
            return terms.at[pl.ds(start, count)]

        self.loads = [links.local(rows(0), self.near), links.local(rows(2), self.far)]
        self.core = [links.copy(rows(3), self.got_far, CORE), links.copy(rows(1), self.got_near, CORE)]
        self.over_x = None if self.got_x is None else links.copy(self.far, self.got_x, X)

    def start(self):
        for copy in self.loads[::-1] + self.core:
            copy.start()

    def middle(self):
        self.loads[1].wait()
        self.core[0].wait_recv()

        def add(rows):
            self.far[rows, :] = (self.far[rows, :].astype(F32) + self.got_far[rows, :].astype(F32)).astype(BF16)

        by_rows(self.far.shape[0], 64, add)
        self.over_x.start()

    def core_end(self):
        for copy in self.loads + self.core:
            copy.wait()

    def end(self):
        self.loads[0].wait()
        self.core[1].wait_recv()
        self.over_x.wait_recv()
        for copy in self.core + [self.over_x]:
            copy.wait_send()

    def total(self, rows):
        return self.near[rows, :].astype(F32) + self.got_near[rows, :].astype(F32) + self.got_x[rows, :].astype(F32)


def row_sum_scratch(count, width):
    return [pltpu.VMEM((count, width), BF16)] * 5


class Everywhere:
    def __init__(self, links, held, slots, ways):
        self.held, self.slots = held, slots
        self.copies = [links.copy(held.at[k], slots.at[k], way) for k, way in enumerate(ways)]

    def start(self, step):
        self.copies[step].start()

    def finish(self, step):
        self.copies[step].wait()
        self.held[step + 1] = self.held[step] + self.slots[step]


class Direct:
    def __init__(self, links, value, slots_tensor, slots_dp, n):
        self.value = value
        self.slots = (slots_tensor, slots_dp)
        self.me = (links.tensor, links.dp)
        self.copies = []
        for slots, me, axis, size in zip(self.slots, self.me, ("tensor", "dp"), (4, n)):
            self.copies.append([links.copy(value, slots.at[me], (axis, d)) for d in range(1, size)])

    def start(self, phase):
        for copy in self.copies[phase]:
            copy.start()

    def finish(self, phase):
        slots = self.slots[phase]
        slots[self.me[phase]] = self.value[...]
        for copy in self.copies[phase]:
            copy.wait()
        total = slots[0]
        for k in range(1, slots.shape[0]):
            total = total + slots[k]
        self.value[...] = total


def direct_ways(n):
    return [("tensor", d) for d in range(1, 4)] + [("dp", d) for d in range(1, n)]


def everywhere_ways(n):
    return [CORE, X, Y] + z_ways(n)


def everywhere_scratch(k, c, n):
    steps = len(everywhere_ways(n))
    return [pltpu.VMEM((steps + 1, k, c), F32), pltpu.VMEM((steps, k, c), F32)]


def tail_kernel(
    dq_ref, dk_ref, dv_ref, w_ref, first_hbm, wide_hbm, mt_hbm, rows_hbm, grad_hbm, cross_hbm, norm_ref,
    self_ref, ffn_ref, cq_ref, cv_ref, up_ref, enc_near, enc_far,
    grad_out, weights_out, late_out, cross_out, enc_out, enc_got, give, acc, weights,
    first_ref, wide_ref, mt_ref, rows_ref, grad_ref, cross_ref, cross_slots, *scratch, n, step_rows
):
    links = Links(*scratch[-3:])
    loads = [
        links.local(source, target)
        for source, target in (
            (cross_hbm, cross_ref), (first_hbm, first_ref), (wide_hbm, wide_ref), (mt_hbm, mt_ref),
            (rows_hbm, rows_ref), (grad_hbm, grad_ref),
        )
    ]
    for copy in loads:
        copy.start()
    cross = Collect(links, cross_ref, cross_slots)
    member = links.tensor
    near, far, got_near, got_far, got_x = scratch[:5]
    columns, gots, slots = scratch[5:7], scratch[7:9], scratch[9:11]
    late_tensor, late_dp, sums, early_slots, held, compact = scratch[11:17]
    count, model = near.shape
    width = dq_ref.shape[1]
    y = links.dp % 2
    c = columns[0].shape[2]
    m, _, r, _ = weights.shape
    half = count // 2
    parts = [pl.ds(0, half), pl.ds(half, half)]
    core_far = links.copy(give.at[0], got_far, CORE)
    core_near = links.copy(give.at[1], got_near, CORE)
    over_x = [links.copy(far.at[part], got_x.at[part], X) for part in parts]
    over_y, collects = [], []
    for k, (column, got, slot) in enumerate(zip(columns, gots, slots)):
        over_y.append(links.copy(weights.at[:, 1 - y, :, pl.ds(k * c, c)], got, Y))
        collects.append(Collect(links, column, slot))
    stages = len(collects[0].stages)
    late = Direct(links, compact, late_tensor, late_dp, n)
    early = Everywhere(links, sums, early_slots, [CORE] + z_ways(n) + [Y, X])
    steps = len(early.copies)
    enc_x = links.copy(enc_far, enc_got, X)
    links.greet(direct_ways(n))
    enc_x.start()

    def terms(distance, target):
        base = (member ^ distance) * count

        def one(rows):
            there = pl.ds(pl.multiple_of(base + rows.start, 128), 128)
            total = dot_nt(dq_ref[there, :], w_ref[:, :width])
            total = total + dot_nt(dk_ref[there, :], w_ref[:, width : 2 * width])
            target[rows, :] = (total + dot_nt(dv_ref[there, :], w_ref[:, 2 * width : 3 * width])).astype(BF16)

        by_rows(count, 128, one)

    def packed(k):
        for block in range(2 * m):
            span = slice(block * r, (block + 1) * r)
            weights[block // 2, block % 2, :, k * c : (k + 1) * c] = acc[span, k * c : (k + 1) * c].astype(BF16)
        columns[k][...] = weights[:, y, :, k * c : (k + 1) * c]

    loads[0].wait()
    cross.start(0)
    acc[...] = jnp.zeros_like(acc)
    loads[1].wait()

    def products(refs, at):
        def one(rows):
            source = first_ref[rows, :].T
            for k, ref in enumerate(refs):
                acc[:, (at + k) * width : (at + k + 1) * width] += dot_nn(source, ref[rows, :])

        return one

    by_rows(dq_ref.shape[0], step_rows, products((dq_ref, dk_ref), 0))
    packed(0)
    over_y[0].start()
    terms(3, give.at[0])
    core_far.start()
    terms(2, far)
    core_far.wait_recv()
    for part, copy in zip(parts, over_x):

        def add(rows, part=part):
            there = pl.ds(pl.multiple_of(part.start + rows.start, 64), 64)
            far[there, :] = (far[there, :].astype(F32) + got_far[there, :].astype(F32)).astype(BF16)

        by_rows(half, 64, add)
        copy.start()
    for copy in loads[2:]:
        copy.wait()

    def products_out(rows):
        acc[:, 3 * width :] += dot_nn(wide_ref[rows, :].T, mt_ref[:, rows].T)

    held[...] = jnp.zeros_like(held)
    sums[0] = jnp.zeros(sums.shape[1:], F32)
    sums[0, 0:2, :] = self_ref[0:2, :]
    sums[0, 2:4, :] = ffn_ref[0:2, :]
    sums[0, 6:7, :] = self_ref[2:3, :]
    sums[0, 9:11, :] = ffn_ref[2:4, :]
    for distance in range(4):
        there = pl.ds(pl.multiple_of((member ^ distance) * width, width), width)
        sums[0, 7:8, there] = cq_ref[distance]
        sums[0, 8:9, there] = cv_ref[distance]
        sums[0, pl.ds(11 + (member ^ distance), 1), :] = up_ref[distance]
    here = pl.ds(pl.multiple_of(member * width, width), width)

    def column_sums(rows):
        sums[0, 4:5, here] += jnp.sum(dq_ref[rows, :].astype(F32), axis=0, keepdims=True)
        sums[0, 5:6, here] += jnp.sum(dv_ref[rows, :].astype(F32), axis=0, keepdims=True)

    by_rows(dq_ref.shape[0], step_rows, column_sums)
    early.start(0)

    def norm_back(part):
        def one(rows):
            rows = pl.ds(pl.multiple_of(part.start + rows.start, 64), 64)
            incoming = near[rows, :].astype(F32) + got_near[rows, :].astype(F32) + got_x[rows, :].astype(F32)
            rows_grad, gain_terms = norm_rows_back(rows_ref[rows, :].astype(F32), incoming, norm_ref[0, 0:1, :])
            grad_out[rows, :] = rows_grad + grad_ref[rows, :]
            held[0:1, :] += jnp.sum(gain_terms, axis=0, keepdims=True)
            held[1:2, :] += jnp.sum(incoming, axis=0, keepdims=True)

        by_rows(half, 64, one)

    def summed_y(k):
        over_y[k].wait_recv()
        add_to(columns[k], gots[k])
        collects[k].start(0)

    def next_z(k):
        for step in range(stages - 1):
            collects[k].finish(step)
            collects[k].start(step + 1)

    def last_z(k):
        collects[k].finish(stages - 1)
        weights_out[:, k * c : (k + 1) * c] = columns[k][collects[k].z].astype(F32)

    for step in range(stages - 1):
        cross.finish(step)
        cross.start(step + 1)
    by_rows(dq_ref.shape[0], step_rows, products((dv_ref,), 2))
    by_rows(dq_ref.shape[0], step_rows, products_out)
    packed(1)
    over_y[1].start()
    summed_y(0)
    early.finish(0)
    terms(1, give.at[1])
    core_near.start()
    terms(0, near)
    enc_x.wait_recv()
    enc_out[...] = enc_near[...] + enc_got[...].astype(F32)
    core_near.wait_recv()
    over_x[0].wait_recv()
    norm_back(parts[0])
    cross.finish(stages - 1)
    cross_out[...] = cross_ref[cross.z].astype(F32)
    next_z(0)
    summed_y(1)
    for step in range(1, steps - 2):
        early.start(step)
        early.finish(step)
    over_x[1].wait_recv()
    norm_back(parts[1])
    next_z(1)
    lines = model // LANES
    for k in range(2 * lines):
        compact[k : k + 1, :] = held[k // lines : k // lines + 1, k % lines * LANES : (k % lines + 1) * LANES]
    late.start(0)
    early.start(steps - 2)
    last_z(0)
    early.finish(steps - 2)
    late.finish(0)
    late.start(1)
    early.start(steps - 1)
    last_z(1)
    early.finish(steps - 1)
    late_out[2:, :] = sums[steps]
    late.finish(1)
    for k in range(2 * lines):
        late_out[k // lines : k // lines + 1, k % lines * LANES : (k % lines + 1) * LANES] = compact[k : k + 1, :]
    for copy in over_x + over_y + [core_near, core_far]:
        copy.wait_send()
    for collect in collects + [cross]:
        collect.drain()
    enc_x.wait_send()


def tail(
    dq, dk, dv, w, first, wide, mixed_t, rows, grad, cross_column, norm, self_sums, ffn_sums, cq_sums, cv_sums, up_sums,
    enc_near, enc_far,
):
    n = lax.axis_size("dp")
    count, model = rows.shape
    width = dq.shape[1]
    m, r, c = n // 2, model // n, 4 * width
    vectors = (16, model)
    vmem = pl.BlockSpec(memory_space=pltpu.VMEM)
    part = pltpu.VMEM((m, r, c // 2), BF16)
    return pl.pallas_call(
        functools.partial(tail_kernel, n=n, step_rows=512),
        in_specs=[vmem] * 4 + [ANY] * 6 + [vmem] * 8,
        out_specs=[vmem] * 5,
        out_shape=[
            jax.ShapeDtypeStruct((count, model), F32),
            jax.ShapeDtypeStruct((r, c), F32),
            jax.ShapeDtypeStruct((vectors[0] + 2, model), F32),
            jax.ShapeDtypeStruct(cross_column.shape[1:], F32),
            jax.ShapeDtypeStruct(enc_near.shape, F32),
        ],
        scratch_shapes=[
            pltpu.VMEM(enc_far.shape, BF16),
            pltpu.VMEM((2, count, model), BF16),
            pltpu.VMEM((model, c), F32),
            pltpu.VMEM((m, 2, r, c), BF16),
        ]
        + [pltpu.VMEM(v.shape, v.dtype) for v in (first, wide, mixed_t, rows, grad, cross_column, cross_column)]
        + row_sum_scratch(count, model)
        + [part] * 6
        + [pltpu.VMEM((size, 2 * model // LANES, LANES), F32) for size in (4, n)]
        + everywhere_scratch(*vectors, n)
        + [pltpu.VMEM((8, model), F32), pltpu.VMEM((2 * model // LANES, LANES), F32)]
        + link_scratch(7 + 3 * m + len(everywhere_ways(n)) + len(direct_ways(n)), 6),
        compiler_params=pltpu.CompilerParams(
            vmem_limit_bytes=VMEM_LIMIT, collective_id=7, has_side_effects=True
        ),
        cost_estimate=pl.CostEstimate(flops=0, bytes_accessed=100 * 2**20, transcendentals=0),
        name="tail",
    )(
        dq, dk, dv, w, first, wide, mixed_t, rows, grad, cross_column, norm,
        self_sums, ffn_sums, cq_sums, cv_sums, up_sums, enc_near, enc_far,
    )


def results_kernel(
    output_ref, grad_ref, enc_ref, self_ref, cross_ref, up_ref, down_ref, vectors_ref,
    output_out, grad_out, enc_out, qkv_out, so_out, cq_out, ckv_out, co_out, up_out, down_out,
    norm_out, biases_out, shift_out, *, scale
):
    output_out[...] = output_ref[...]
    grad_out[...] = grad_ref[...]
    enc_out[...] = enc_ref[...]
    width = cq_out.shape[1]

    @pl.when(pl.program_id(0) == 0)
    def _():
        for k in range(3):
            qkv_out[:, k, :] = self_ref[:, k * width : (k + 1) * width] * scale
        so_out[...] = (self_ref[:, 3 * width :] * scale).T
        cq_out[...] = cross_ref[:, :width] * scale
        for k in range(2):
            ckv_out[:, k, :] = cross_ref[:, (k + 1) * width : (k + 2) * width] * scale
        co_out[...] = (cross_ref[:, 3 * width :] * scale).T
        up_out[...] = up_ref[...] * scale
        down_out[...] = (down_ref[...] * scale).T
        vectors = vectors_ref[...] * scale
        for k in range(3):
            norm_out[k] = vectors[2 * k : 2 * k + 2, :]
        biases_out[...] = vectors[6:13, :]
        lines = vectors.shape[1] // LANES
        for k in range(shift_out.shape[0]):
            part = slice(k % lines * LANES, (k % lines + 1) * LANES)
            shift_out[k : k + 1, :] = vectors[13 + k // lines : 14 + k // lines, part]


def results(output, grad, encoder, self_w, cross_w, up, down, vectors, scale):
    r, c = self_w.shape
    width = c // 4
    steps = 4

    def rows(value):
        return pl.BlockSpec((value.shape[0] // steps, value.shape[1]), lambda i: (i, 0))

    shapes = [(r, 3, width), (width, r), (r, width), (r, 2, width), (width, r), up.shape, down.shape[::-1]]
    shapes += [(3, 2, output.shape[1]), (7, output.shape[1]), (4 * up.shape[1] // LANES, LANES)]
    return pl.pallas_call(
        functools.partial(results_kernel, scale=scale),
        grid=(steps,),
        in_specs=[rows(output), rows(grad), rows(encoder)] + [const(v.shape) for v in (self_w, cross_w, up, down, vectors)],
        out_specs=[rows(output), rows(grad), rows(encoder)] + [const(shape) for shape in shapes],
        out_shape=[jax.ShapeDtypeStruct(v.shape, F32) for v in (output, grad, encoder)]
        + [jax.ShapeDtypeStruct(shape, F32) for shape in shapes],
        compiler_params=pltpu.CompilerParams(vmem_limit_bytes=VMEM_LIMIT),
        cost_estimate=pl.CostEstimate(flops=0, bytes_accessed=20 * 2**20, transcendentals=0),
        name="results",
    )(output, grad, encoder, self_w, cross_w, up, down, vectors)


def start_kernel(
    in_ref, norm_ref, qkv_ref, so_ref, cq_ref, ckv_ref, co_ref, down_ref, enc_ref,
    rows_out, self_out, cross_out, down_out, enc_out, rows_ref, self_ref, cross_ref, shard_ref, send_sems, recv_sems, local_sems, *, n
):
    links = Links(send_sems, recv_sems, local_sems)
    member, z, y = links.tensor, links.dp // 2, links.dp % 2
    count = rows_ref.shape[0]
    half = count // 2
    parts = [pl.ds(0, half), pl.ds(half, half)]

    def place(distance):
        return rows_out.at[pl.ds(pl.multiple_of((member ^ distance) * count, count), count)]

    over_x = [links.copy(rows_ref.at[part], place(0).at[part], X) for part in parts]
    over_core = [links.copy(rows_ref, place(0), CORE)]
    over_core += [links.copy(place(2).at[part], place(2).at[part], CORE) for part in parts]
    self_stages = column_stages(links, self_ref, self_out.at[:, y], n)
    cross_stages = column_stages(links, cross_ref, cross_out, n)
    over_y = [links.copy(self_ref, self_out.at[z, y], Y)]
    local = [
        links.local(rows_ref, place(0)),
        links.local(self_ref, self_out.at[z, y]),
        links.local(cross_ref, cross_out.at[z]),
    ]
    width = cq_ref.shape[1]
    for k in range(3):
        self_ref[:, k * width : (k + 1) * width] = qkv_ref[:, k, :]
    self_ref[:, 3 * width :] = so_ref[...].T
    cross_ref[:, :width] = cq_ref[...]
    for k in range(2):
        cross_ref[:, (k + 1) * width : (k + 2) * width] = ckv_ref[:, k, :]
    cross_ref[:, 3 * width :] = co_ref[...].T
    shard_ref[...] = down_ref[...].T
    square = Square(links, shard_ref, down_out)
    enc_count = enc_ref.shape[0]

    def enc_place(distance):
        return enc_out.at[pl.ds(pl.multiple_of((member ^ distance) * enc_count, enc_count), enc_count)]

    enc_x = links.copy(enc_ref, enc_place(0), X)
    enc_core = [links.copy(enc_ref, enc_place(0), CORE), links.copy(enc_place(2), enc_place(2), CORE)]
    local.append(links.local(enc_ref, enc_place(0)))
    links.greet([CORE, X, Y] + z_ways(n))
    for copy in over_y + local[1:]:
        copy.start()
    for copy, _ in self_stages[0]:
        copy.start()
    for part, copy in zip(parts, over_x):

        def norm(rows, part=part):
            rows = pl.ds(pl.multiple_of(part.start + rows.start, 64), 64)
            xhat, _ = normalized(in_ref[rows, :].astype(F32))
            rows_ref[rows, :] = (xhat * norm_ref[0, 0:1, :] + norm_ref[0, 1:2, :]).astype(BF16)

        by_rows(half, 64, norm)
        copy.start()
    for copy in local[:1] + over_core[:1]:
        copy.start()
    square.start()
    enc_x.start()
    enc_core[0].start()
    for self_stage in self_stages:
        if self_stage is not self_stages[0]:
            for copy, _ in self_stage:
                copy.start()
        for copy, index in self_stage:
            copy.wait_recv()
            onward = links.copy(self_out.at[index, y], self_out.at[index, y], Y)
            onward.start()
            over_y.append(onward)
        if self_stage is self_stages[0]:
            for copy, _ in cross_stages[0]:
                copy.start()
    for cross_stage, later in zip(cross_stages, cross_stages[1:] + [[]]):
        for copy, _ in cross_stage:
            copy.wait_recv()
        for copy, _ in later:
            copy.start()
    for copy, onward in zip(over_x, over_core[1:]):
        copy.wait_recv()
        onward.start()
    square.middle()
    enc_x.wait_recv()
    enc_core[1].start()
    enc_x.wait_send()
    square.end()
    for copy in local + over_y + over_core + enc_core:
        copy.wait()
    for copy in over_x:
        copy.wait_send()
    for stage in self_stages + cross_stages:
        for copy, _ in stage:
            copy.wait_send()


def start_gather(rows, norm, qkv, self_out, cross_q, cross_kv, cross_out, down, encoder):
    n = lax.axis_size("dp")
    r, c = cross_q.shape[0], 4 * cross_q.shape[1]
    return pl.pallas_call(
        functools.partial(start_kernel, n=n),
        in_specs=[pl.BlockSpec(memory_space=pltpu.VMEM)] * 9,
        out_specs=[ANY] * 5,
        out_shape=[
            jax.ShapeDtypeStruct((4 * rows.shape[0], rows.shape[1]), BF16),
            jax.ShapeDtypeStruct((n // 2, 2, r, c), BF16),
            jax.ShapeDtypeStruct((n // 2, r, c), BF16),
            jax.ShapeDtypeStruct((2, 2, r, down.shape[0]), BF16),
            jax.ShapeDtypeStruct((4 * encoder.shape[0], encoder.shape[1]), BF16),
        ],
        scratch_shapes=[pltpu.VMEM(rows.shape, BF16)]
        + [pltpu.VMEM((r, c), BF16)] * 2
        + [pltpu.VMEM((r, down.shape[0]), BF16)]
        + link_scratch(2 * n + 15, 5),
        compiler_params=pltpu.CompilerParams(
            vmem_limit_bytes=VMEM_LIMIT, collective_id=0, has_side_effects=True
        ),
        cost_estimate=pl.CostEstimate(flops=0, bytes_accessed=100 * 2**20, transcendentals=0),
        name="start_gather",
    )(rows, norm, qkv, self_out, cross_q, cross_kv, cross_out, down, encoder)


def self_forward_kernel(
    b_ref, x_ref, w_ref, biases_ref, column_ref, up_ref, down_ref,
    q_out, k_ref, v_out, kt_out, ot_ref, lse_ref, terms_ref, whole, next_column, far_down,
    vt_ref, m_s, l_s, acc, column, send_sems, recv_sems, local_sems, *, heads, safe, n
):
    i = pl.program_id(0)
    last = pl.num_programs(0) - 1
    bq, width = q_out.shape
    links = Links(send_sems, recv_sems, local_sems)
    spread = Spread(links, column_ref, column, whole)
    stages = column_stages(links, up_ref, next_column, n)
    keep = links.local(up_ref, next_column.at[links.dp // 2])
    over_z = links.copy(down_ref.at[0], far_down, z_ways(n)[0])

    def next_stage(step):
        for copy, _ in stages[step]:
            copy.wait_recv()
        for copy, _ in stages[step + 1] if step + 1 < len(stages) else []:
            copy.start()

    @pl.when(i == 0)
    def _():
        links.greet([CORE, X, Y] + z_ways(n))
        for copy, _ in stages[0]:
            copy.start()
        spread.start()
        keep.start()

    def onward():
        next_stage(0)
        over_z.start()

    mine = pl.ds(pl.multiple_of(links.tensor * width, width), width)
    projected = dot_nn(x_ref[...], w_ref[:, : 3 * width])
    query = (projected[:, :width] + biases_ref[0:1, mine]).astype(BF16)
    key = projected[:, width : 2 * width].astype(BF16)
    value = (projected[:, 2 * width :] + biases_ref[1:2, mine]).astype(BF16)
    here = pl.ds(pl.multiple_of(i * bq, bq), bq)
    q_out[...] = query
    v_out[...] = value
    kt_out[...] = key.T
    k_ref[here, :] = key
    vt_ref[:, here] = value.T

    m_s[...] = jnp.full_like(m_s, NEGATIVE)
    l_s[...] = jnp.zeros_like(l_s)
    acc[...] = jnp.zeros_like(acc)
    hd = width // heads
    scaled = query * jnp.asarray(1.0 / math.sqrt(hd), BF16)
    q_heads = [head_only(scaled, h, hd) for h in range(heads)]

    def block(first, size, skip, mode):
        rows = pl.ds(pl.multiple_of(first, size), size)
        m_old = m_s[:, skip:]
        l_old = l_s[:, skip:]
        scores = [dot_nt(k_ref[rows, lanes_of(h, hd)[1]], q_heads[h][skip:]) for h in range(heads)]
        if mode != "none":
            bad = self_bad(b_ref, i * bq + skip, first, bq - skip, size, mode == "causal")
            scores = [jnp.where(bad, NEGATIVE, s) for s in scores]
        m_out, l_out, a_out = [], [], []
        for h in range(heads):
            part = slice(h * hd, (h + 1) * hd)
            m_new = jnp.maximum(m_old[h : h + 1, :], jnp.max(scores[h], axis=0, keepdims=True))
            shrink = jnp.exp(m_old[h : h + 1, :] - m_new)
            expos = jnp.exp(scores[h] - m_new)
            l_out.append(l_old[h : h + 1, :] * shrink + jnp.sum(expos, axis=0, keepdims=True))
            m_out.append(m_new)
            a_out.append(acc[part, skip:] * shrink + dot_nn(vt_ref[part, rows], expos.astype(BF16)))
        m_s[:, skip:] = jnp.concatenate(m_out, 0)
        l_s[:, skip:] = jnp.concatenate(l_out, 0)
        for h in range(heads):
            acc[h * hd : (h + 1) * hd, skip:] = a_out[h]

    over_keys(i, bq, safe, block, [(2, 0, onward), (3, 2, spread.middle), (4, 3, spread.last)])
    inverse = 1.0 / l_s[...]
    for h in range(heads):
        part = slice(h * hd, (h + 1) * hd)
        ot_ref[part, :] = (acc[part, :] * inverse[h : h + 1, :]).astype(BF16)
    lse_ref[...] = m_s[...] + jnp.log(l_s[...])
    terms_ref[...] = dot_nt(ot_ref[...].T, w_ref[:, 3 * width :]).astype(BF16)

    @pl.when(i == last)
    def _():
        for step in range(1, len(stages)):
            next_stage(step)
        over_z.wait()
        spread.end()
        for stage in stages:
            for copy, _ in stage:
                copy.wait_send()
        keep.wait()


def self_forward(bounds, x, w, biases, column, up, down, heads, safe):
    n, model = x.shape
    width = w.shape[1] // 4
    bq = 512
    dp = lax.axis_size("dp")
    m, r, c = column.shape
    by_rows_spec = pl.BlockSpec((bq, width), lambda i: (i, 0))
    by_columns_spec = pl.BlockSpec((width, bq), lambda i: (0, i))
    return pl.pallas_call(
        functools.partial(self_forward_kernel, heads=heads, safe=safe, n=dp),
        grid=(n // bq,),
        in_specs=[
            pl.BlockSpec(memory_space=pltpu.SMEM),
            pl.BlockSpec((bq, model), lambda i: (i, 0)),
            const((model, 4 * width)),
            const(biases.shape),
            ANY,
            const(up.shape),
            ANY,
        ],
        out_specs=[
            by_rows_spec,
            const((n, width)),
            by_rows_spec,
            by_columns_spec,
            by_columns_spec,
            pl.BlockSpec((heads, bq), lambda i: (0, i)),
            pl.BlockSpec((bq, model), lambda i: (i, 0)),
            ANY,
            ANY,
            ANY,
        ],
        out_shape=[
            jax.ShapeDtypeStruct((n, width), BF16),
            jax.ShapeDtypeStruct((n, width), BF16),
            jax.ShapeDtypeStruct((n, width), BF16),
            jax.ShapeDtypeStruct((width, n), BF16),
            jax.ShapeDtypeStruct((width, n), BF16),
            jax.ShapeDtypeStruct((heads, n), F32),
            jax.ShapeDtypeStruct((n, model), BF16),
            jax.ShapeDtypeStruct((4, m, 2, r, c), BF16),
            jax.ShapeDtypeStruct((m,) + up.shape, BF16),
            jax.ShapeDtypeStruct(down.shape[1:], BF16),
        ],
        scratch_shapes=[
            pltpu.VMEM((width, n), BF16),
            pltpu.VMEM((heads, bq), F32),
            pltpu.VMEM((heads, bq), F32),
            pltpu.VMEM((width, bq), F32),
            pltpu.VMEM((m, r, c), BF16),
        ]
        + link_scratch(9 + m, 3),
        compiler_params=pltpu.CompilerParams(
            vmem_limit_bytes=VMEM_LIMIT, collective_id=1, has_side_effects=True
        ),
        cost_estimate=pl.CostEstimate(
            flops=12 * n * n * width, bytes_accessed=8 * n * width, transcendentals=n * n * heads // 2
        ),
        name="self_forward",
    )(bounds, x, w, biases, column, up, down)


def after_self_kernel(
    terms_ref, rows_ref, biases_ref, norm_ref, column_ref, down_ref, from_z,
    after_out, second_out, whole_out, down_out, far_down, *scratch, n
):
    links = Links(*scratch[-3:])
    rows_sum = RowSum(links, terms_ref, scratch[:5])
    column = scratch[5]
    spread = SpreadZ(links, down_ref.at[0], from_z, scratch[6], down_out, n)
    over_z = links.copy(down_ref.at[1], far_down, z_ways(n)[0])
    y = links.dp % 2
    near_out, core_out = whole_out.at[0], whole_out.at[1]
    load = links.local(column_ref, column)
    own = links.local(column, near_out.at[:, y])
    over_y = links.copy(column, near_out.at[:, y], Y)
    over_core = [
        links.copy(column, core_out.at[:, y], CORE),
        links.copy(near_out.at[:, 1 - y], core_out.at[:, 1 - y], CORE),
    ]
    links.greet([CORE, X, Y] + z_ways(n))
    rows_sum.start()
    load.start()
    over_z.start()
    load.wait()
    over_y.start()
    own.start()
    rows_sum.middle()
    spread.start()
    over_core[0].start()
    rows_sum.end()

    def norm(rows):
        after = rows_ref[rows, :].astype(F32) + rows_sum.total(rows) + biases_ref[2:3, :]
        after_out[rows, :] = after
        xhat, _ = normalized(after)
        second_out[rows, :] = (xhat * norm_ref[1, 0:1, :] + norm_ref[1, 1:2, :]).astype(BF16)

    by_rows(after_out.shape[0], 64, norm)
    over_y.wait_recv()
    over_core[1].start()
    over_y.wait_send()
    spread.end()
    over_z.wait()
    for copy in [own] + over_core:
        copy.wait()


def sum_after_self(terms, rows, biases, norm, column, down, from_z):
    count, model = rows.shape
    m, r, c = column.shape
    vmem = pl.BlockSpec(memory_space=pltpu.VMEM)
    return pl.pallas_call(
        functools.partial(after_self_kernel, n=2 * m),
        in_specs=[ANY, vmem, vmem, vmem, ANY, ANY, ANY],
        out_specs=[vmem, vmem, ANY, ANY, ANY],
        out_shape=[
            jax.ShapeDtypeStruct((count, model), F32),
            jax.ShapeDtypeStruct((count, model), BF16),
            jax.ShapeDtypeStruct((2, m, 2, r, c), BF16),
            jax.ShapeDtypeStruct((2, m, 2, r, c), BF16),
            jax.ShapeDtypeStruct((2, r, c), BF16),
        ],
        scratch_shapes=row_sum_scratch(count, model)
        + [pltpu.VMEM((m, r, c), BF16), pltpu.VMEM((2, 2, r, c), BF16)]
        + link_scratch(7 + spread_z_copies(2 * m), 8),
        compiler_params=pltpu.CompilerParams(
            vmem_limit_bytes=VMEM_LIMIT, collective_id=8, has_side_effects=True
        ),
        cost_estimate=pl.CostEstimate(flops=0, bytes_accessed=100 * 2**20, transcendentals=0),
        name="sum_after_self",
    )(terms, rows, biases, norm, column, down, from_z)


def self_backward_kernel(
    b_ref, q_ref, k_ref, v_ref, kt_ref, w_ref, mt_ref, lse_ref, back_ref, rows_ref, above_ref, norm_ref,
    up_ref, down_ref, cross_ref, enc_ref,
    dq_ref, dk_ref, dv_ref, wide_out, grad_out, sums_ref, up_out, down_out, cross_out, enc_near, enc_far,
    dka, dva, dqa, wide, *scratch, bq, heads, safe, n
):
    s = pl.program_id(0)
    last = pl.num_programs(0) - 1
    links = Links(*scratch[-3:])
    member = links.tensor
    x = member // 2
    later = (s // 2 + 1) // 2
    i = s * (1 - x) + ((s + 3) * (1 - later) + (4 - s) * later) * x
    cross = GatherLast(links, cross_ref.at[0], cross_ref.at[1], scratch[:5])
    keep_cross = links.local(cross.column, cross_out)
    columns, slots = scratch[5:7], scratch[7:9]
    sums_z = [Collect(links, column, slot) for column, slot in zip(columns, slots)]
    load_z = [links.local(ref, column) for ref, column in zip((up_ref, down_ref), columns)]
    enc = RowSum(links, enc_ref, list(scratch[9:13]) + [None])
    stages = len(sums_z[0].stages)
    count = grad_out.shape[0]
    half = count // 2

    def place(distance, k=None):
        start = (member ^ distance) * count
        if k is None:
            return wide.at[pl.ds(pl.multiple_of(start, half), count)]
        return wide.at[pl.ds(pl.multiple_of(start + k * half, half), half)]

    over_x = [links.copy(place(0, k), place(0, k), X) for k in range(2)]
    over_core = links.copy(place(0), place(0), CORE)
    onward = [links.copy(place(2, k), place(2, k), CORE) for k in range(2)]
    keep_wide = links.local(wide, wide_out)

    def norm_back(k):
        def one(rows):
            rows = pl.ds(pl.multiple_of(k * half + rows.start, 64), 64)
            incoming = back_ref[rows, :]
            rows_grad, gain_terms = norm_rows_back(rows_ref[rows, :], incoming, norm_ref[1, 0:1, :])
            rows_grad = rows_grad + above_ref[rows, :]
            rounded = rows_grad.astype(BF16)
            grad_out[rows, :] = rows_grad
            wide[pl.ds(pl.multiple_of(member * count + rows.start, 64), 64), :] = rounded
            for row, terms in enumerate((gain_terms, incoming, rounded.astype(F32))):
                sums_ref[row : row + 1, :] += jnp.sum(terms, axis=0, keepdims=True)

        by_rows(half, 64, one)

    def arrive(k):
        over_x[k].wait_recv()
        onward[k].start()
        onward[k].wait_recv()

    @pl.when(s == 0)
    def _():
        links.greet([CORE, X, Y] + z_ways(n))
        for copy in load_z:
            copy.start()
        sums_ref[...] = jnp.zeros_like(sums_ref)
        for k in range(2):
            norm_back(k)
            over_x[k].start()
        over_core.start()
        cross.start()
        enc.start()
        for copy, total in zip(load_z, sums_z):
            copy.wait()
            total.start(0)
        dka[...] = jnp.zeros_like(dka)
        dva[...] = jnp.zeros_like(dva)
        over_core.wait_recv()

    @pl.when(s == 2)
    def _():
        arrive(0)
        pl.when(x == 1)(functools.partial(arrive, 1))
        pl.when(x == 0)(cross.second)
        for step in range(stages - 1):
            for total in sums_z:
                total.finish(step)
            for total in sums_z:
                total.start(step + 1)

    @pl.when(s == 3)
    def _():
        @pl.when(x == 0)
        def _():
            arrive(1)
            cross.middle()

        keep_wide.start()

    def cross_sums():
        @pl.when(x == 1)
        def _():
            cross.second()
            cross.middle()

    width = k_ref.shape[1]
    hd = width // heads
    scale = 1.0 / math.sqrt(hd)
    here = pl.ds(pl.multiple_of(i * bq, bq), bq)
    grads = dot_nn(wide[here, :], w_ref[:, 3 * width :]).astype(BF16)
    products = grads.T.astype(F32) * mt_ref[:, here].astype(F32)
    inner = [jnp.sum(products[h * hd : (h + 1) * hd, :], axis=0, keepdims=True) for h in range(heads)]
    scaled = q_ref[here, :] * jnp.asarray(scale, BF16)
    q_heads = [head_only(scaled, h, hd) for h in range(heads)]
    d_heads = [head_only(grads, h, hd) for h in range(heads)]
    lse = lse_ref[:, here]
    dqa[...] = jnp.zeros_like(dqa)

    def block(first, size, skip, mode):
        rows = pl.ds(pl.multiple_of(first, size), size)
        scores = [dot_nt(k_ref[rows, lanes_of(h, hd)[1]], q_heads[h][skip:]) for h in range(heads)]
        dprobs = [dot_nt(v_ref[rows, lanes_of(h, hd)[1]], d_heads[h][skip:]) for h in range(heads)]
        if mode != "none":
            bad = self_bad(b_ref, i * bq + skip, first, bq - skip, size, mode == "causal")
            scores = [jnp.where(bad, NEGATIVE, s) for s in scores]
        dv_sums, dk_sums = {}, {}
        for h in range(heads):
            part = slice(h * hd, (h + 1) * hd)
            group, _ = lanes_of(h, hd)
            probs = jnp.exp(scores[h] - lse[h : h + 1, skip:])
            ds = (probs * (dprobs[h] - inner[h][:, skip:])).astype(BF16)
            add_group(dv_sums, group, dot_nn(probs.astype(BF16), d_heads[h][skip:]))
            add_group(dk_sums, group, dot_nn(ds, q_heads[h][skip:]))
            dqa[part, skip:] += dot_nn(kt_ref[part, rows], ds)
        for group in dv_sums:
            part = slice(group * LANES, (group + 1) * LANES)
            dva[rows, part] += dv_sums[group]
            dka[rows, part] += dk_sums[group]

    over_keys(i, bq, safe, block, [(4, 3, cross_sums)])
    dq_ref[here, :] = (dqa[...] * scale).astype(BF16).T

    @pl.when(s == last)
    def _():
        dk_ref[...] = dka[...].astype(BF16)
        dv_ref[...] = dva[...].astype(BF16)
        cross.end()
        keep_cross.start()
        for total, out in zip(sums_z, (up_out, down_out)):
            total.finish(stages - 1)
            out[...] = total.column[total.z].astype(F32)
            total.drain()
        enc.core_end()

        def store(rows):
            enc_near[rows, :] = enc.near[rows, :].astype(F32) + enc.got_near[rows, :].astype(F32)
            enc_far[rows, :] = (enc.far[rows, :].astype(F32) + enc.got_far[rows, :].astype(F32)).astype(BF16)

        by_rows(enc_near.shape[0], 64, store)
        for copy in over_x + onward + [over_core]:
            copy.wait_send()
        keep_wide.wait()
        keep_cross.wait()


def self_backward(
    bounds, queries, keys, values, keys_t, w, mixed_t, lse, back, rows, above, norm,
    up_column, down_column, cross_sum, enc_terms, heads, safe
):
    n, width = queries.shape
    count, model = rows.shape
    dp = lax.axis_size("dp")
    m, r, c = up_column.shape
    cross_c = cross_sum.shape[4]
    enc_shape = (enc_terms.shape[0] // 4, enc_terms.shape[1])
    bq = 512
    return pl.pallas_call(
        functools.partial(self_backward_kernel, bq=bq, heads=heads, safe=safe, n=dp),
        grid=(n // bq,),
        in_specs=[
            pl.BlockSpec(memory_space=pltpu.SMEM),
            const((n, width)),
            const((n, width)),
            const((n, width)),
            const((width, n)),
            const((model, 4 * width)),
            const((width, n)),
            const((heads, n)),
            const((count, model)),
            const((count, model)),
            const((count, model)),
            const(norm.shape),
        ]
        + [ANY] * 4,
        out_specs=[const((n, width))] * 3
        + [ANY, const((count, model)), const((8, model)), const((r, c)), const((r, c)), ANY]
        + [const(enc_shape)] * 2,
        out_shape=[jax.ShapeDtypeStruct((n, width), BF16)] * 3
        + [
            jax.ShapeDtypeStruct((n, model), BF16),
            jax.ShapeDtypeStruct((count, model), F32),
            jax.ShapeDtypeStruct((8, model), F32),
            jax.ShapeDtypeStruct((r, c), F32),
            jax.ShapeDtypeStruct((r, c), F32),
            jax.ShapeDtypeStruct((m, r, cross_c), BF16),
            jax.ShapeDtypeStruct(enc_shape, F32),
            jax.ShapeDtypeStruct(enc_shape, BF16),
        ],
        scratch_shapes=[
            pltpu.VMEM((n, width), F32),
            pltpu.VMEM((n, width), F32),
            pltpu.VMEM((width, bq), F32),
            pltpu.VMEM((n, model), BF16),
        ]
        + [pltpu.VMEM((m, r, cross_c), BF16)] * 5
        + [pltpu.VMEM((m, r, c), BF16)] * 4
        + row_sum_scratch(*enc_shape)[:4]
        + link_scratch(11 + 2 * m, 8),
        compiler_params=pltpu.CompilerParams(
            vmem_limit_bytes=62 * 2**20, collective_id=5, has_side_effects=True
        ),
        cost_estimate=pl.CostEstimate(
            flops=24 * n * n * width, bytes_accessed=16 * n * width, transcendentals=n * n * heads // 2
        ),
        name="self_backward",
    )(
        bounds, queries, keys, values, keys_t, w, mixed_t, lse, back, rows, above, norm,
        up_column, down_column, cross_sum, enc_terms,
    )


def const(shape):
    return pl.BlockSpec(shape, lambda *_: (0,) * len(shape), pipeline_mode=pl.Buffered(1))


def normalized(rows):
    center = rows - jnp.mean(rows, axis=-1, keepdims=True)
    scale = lax.rsqrt(jnp.mean(center * center, axis=-1, keepdims=True) + EPSILON)
    return center * scale, scale


def norm_rows_back(rows, incoming, gain):
    xhat, scale = normalized(rows)
    e = incoming * gain
    inner = jnp.mean(e * xhat, axis=-1, keepdims=True)
    return scale * (e - jnp.mean(e, axis=-1, keepdims=True) - xhat * inner), incoming * xhat


def by_rows(count, step, body):
    def one(k, c):
        body(pl.ds(pl.multiple_of(k * step, step), step))
        return c

    lax.fori_loop(0, count // step, one, 0)


def cross_forward_kernel(
    len_ref, x_ref, enc_ref, w_ref, biases_ref, rows_ref, norm_ref, column_ref, down_ref, from_z,
    q_out, k_out, v_out, ot_ref, lse_ref, after_ref, third_ref, whole, down_out, hold, send_sems, recv_sems, local_sems, *, heads, n
):
    i = pl.program_id(0)
    last = pl.num_programs(0) - 1
    links = Links(send_sems, recv_sems, local_sems)
    spread = SpreadFar(links, column_ref, whole)
    pieces = len(spread.over_x)
    spread_z = SpreadZ(links, down_ref.at[1], from_z, hold, down_out, n)

    @pl.when(i == 0)
    def _():
        links.greet([CORE, X, Y] + z_ways(n))
        spread.start()
        spread_z.start()
        after_ref[...] = rows_ref[...] + biases_ref[5:6, :]

    def onward(*when):
        for step, k in when:
            pl.when(i == step)(functools.partial(spread.onward, k))

    onward((1, 0), (1, 1), (2, 4), (3, 6), (3, 7))

    width = q_out.shape[2]
    hd = width // heads
    mine = pl.ds(pl.multiple_of((links.tensor ^ i) * width, width), width)
    query = (dot_nn(x_ref[...], w_ref[0, :, :width]) + biases_ref[3:4, mine]).astype(BF16)
    key_value = dot_nn(enc_ref[...], w_ref[0, :, width : 3 * width])
    keys = key_value[:, :width].astype(BF16)
    values = (key_value[:, width:] + biases_ref[4:5, mine]).astype(BF16)
    q_out[0] = query
    k_out[0] = keys
    v_out[0] = values
    values_t = values.T
    scaled = query * jnp.asarray(1.0 / math.sqrt(hd), BF16)
    ok = lax.broadcasted_iota(jnp.int32, (keys.shape[0], 1), 0) < len_ref[0]
    scores = [dot_nt(keys[:, lanes_of(h, hd)[1]], head_only(scaled, h, hd)) for h in range(heads)]
    mixed = []
    for h in range(heads):
        part = slice(h * hd, (h + 1) * hd)
        s = jnp.where(ok, scores[h], NEGATIVE)
        largest = jnp.max(s, axis=0, keepdims=True)
        expos = jnp.exp(s - largest)
        total = jnp.sum(expos, axis=0, keepdims=True)
        mixed.append((dot_nn(values_t[part, :], expos.astype(BF16)) * (1.0 / total)).astype(BF16))
        ot_ref[0, part, :] = mixed[h]
        lse_ref[0, h : h + 1, :] = largest + jnp.log(total)
        if h == heads // 2 - 1:
            onward((1, 2), (1, 3), (2, 5))

            @pl.when(i == last)
            def _():
                for k in range(pieces // 2):
                    spread.last(k)
    after_ref[...] += dot_nt(jnp.concatenate(mixed, 0).T, w_ref[0, :, 3 * width :])

    @pl.when(i == last)
    def _():
        def norm(rows):
            xhat, _ = normalized(after_ref[rows, :])
            third_ref[rows, :] = (xhat * norm_ref[2, 0:1, :] + norm_ref[2, 1:2, :]).astype(BF16)

        by_rows(after_ref.shape[0], 128, norm)
        for k in range(pieces // 2, pieces):
            spread.last(k)
        spread_z.end()
        spread.end()


def cross_forward(lengths, x, encoder, weights, biases, rows, norm, column, down, from_z, heads):
    count, model = x.shape
    n = encoder.shape[0]
    parts, _, columns = weights.shape
    width = columns // 4
    m, r, c = column.shape

    def by_part(*shape):
        return pl.BlockSpec((1,) + shape, lambda i: (i,) + (0,) * len(shape))

    return pl.pallas_call(
        functools.partial(cross_forward_kernel, heads=heads, n=2 * m),
        grid=(parts,),
        in_specs=[
            pl.BlockSpec(memory_space=pltpu.SMEM),
            const((count, model)),
            const((n, model)),
            by_part(model, columns),
            const(biases.shape),
            const((count, model)),
            const(norm.shape),
            ANY,
            ANY,
            ANY,
        ],
        out_specs=[
            by_part(count, width),
            by_part(n, width),
            by_part(n, width),
            by_part(width, count),
            by_part(heads, count),
            const((count, model)),
            const((count, model)),
            ANY,
            ANY,
        ],
        out_shape=[
            jax.ShapeDtypeStruct((parts, count, width), BF16),
            jax.ShapeDtypeStruct((parts, n, width), BF16),
            jax.ShapeDtypeStruct((parts, n, width), BF16),
            jax.ShapeDtypeStruct((parts, width, count), BF16),
            jax.ShapeDtypeStruct((parts, heads, count), F32),
            jax.ShapeDtypeStruct((count, model), F32),
            jax.ShapeDtypeStruct((count, model), BF16),
            jax.ShapeDtypeStruct((2, m, 2, r, c), BF16),
            jax.ShapeDtypeStruct((2, m, 2, r, c), BF16),
        ],
        scratch_shapes=[pltpu.VMEM((2, 2, r, c), BF16)] + link_scratch(32 + spread_z_copies(2 * m), 4),
        compiler_params=pltpu.CompilerParams(
            vmem_limit_bytes=VMEM_LIMIT, collective_id=2, has_side_effects=True
        ),
        cost_estimate=pl.CostEstimate(
            flops=24 * parts * count * n * width,
            bytes_accessed=8 * parts * n * width,
            transcendentals=parts * count * n * heads,
        ),
        name="cross_forward",
    )(lengths, x, encoder, weights, biases, rows, norm, column, down, from_z)


def feed_forward_kernel(
    x_ref, dy_ref, near_up, near_down, far_up, far_down, b_ref, after_ref, biases_ref, norm_ref,
    out_ref, rows_out, low_out, sums_ref, gup_ref, gdown_ref, bias_ref, from_x, from_y,
    xt_ref, dyt_ref, back_ref, give, got, diagonal, loaded, load_sems, send_sems, recv_sems, local_sems, *, chunks
):
    s = pl.program_id(0)
    links = Links(send_sems, recv_sems, local_sems)
    turn = s // chunks
    chunk = s % chunks
    pair = turn // 2
    slot = pair * chunks + chunk
    theirs = turn % 2 == 0
    y = links.dp % 2
    m, r = diagonal.shape[1], diagonal.shape[2]
    low, high = pl.ds(0, m // 2), pl.ds(m // 2, m - m // 2)
    links.used = 2 * chunks
    across = [
        links.copy(diagonal.at[:, low], from_x, X),
        links.copy(diagonal.at[:, high], from_y, Y),
    ]
    to_core = pltpu.make_async_remote_copy(
        src_ref=give.at[chunk],
        dst_ref=got.at[slot],
        send_sem=send_sems.at[slot],
        recv_sem=recv_sems.at[slot],
        device_id=links.partner(CORE),
        device_id_type=pl.DeviceIdType.MESH,
    )

    size = loaded.shape[3]

    def fetch(step, act):
        block = 3 - step // chunks
        slot = step % 2
        first = (step % chunks) * size

        def both(*sources):
            for k, source in enumerate(sources):
                columns = pl.ds(pl.multiple_of(first, size), size)
                act(pltpu.make_async_copy(source.at[:, columns], loaded.at[slot, k], load_sems.at[slot, k]))

        @pl.when(block >= 2)
        def _():
            both(far_up.at[block - 2], far_down.at[block - 2])

        @pl.when(block < 2)
        def _():
            both(near_up.at[block], near_down.at[block])

    @pl.when(s == 0)
    def _():
        fetch(0, lambda copy: copy.start())
        links.greet([CORE, X, Y])
        out_ref[...] = after_ref[...] + biases_ref[6:7, :]
        back_ref[...] = jnp.zeros_like(back_ref)
        xt_ref[...] = x_ref[...].T
        dyt_ref[...] = dy_ref[...].T
        sums_ref[...] = jnp.zeros_like(sums_ref)

    fetch(s, lambda copy: copy.wait())

    @pl.when(s + 1 < pl.num_programs(0))
    def _():
        fetch(s + 1, lambda copy: copy.start())

    up_ref, down_ref = loaded.at[s % 2, 0], loaded.at[s % 2, 1]
    lines = size // LANES
    line = ((links.tensor ^ (3 - turn)) * chunks + chunk) * lines
    shift = jnp.concatenate([b_ref[pl.ds(line + k, 1), :] for k in range(lines)], axis=1)
    pre_act = dot_nn(x_ref[...], up_ref[...]) + shift
    hidden_grad = dot_nn(dy_ref[...], down_ref[...])
    normal_cdf = 0.5 * (1.0 + lax.erf(pre_act * (1.0 / math.sqrt(2.0))))
    density = jnp.exp(-0.5 * pre_act * pre_act) * (1.0 / math.sqrt(2.0 * math.pi))
    hidden = (pre_act * normal_cdf).astype(BF16)
    pre_grad = (hidden_grad * (normal_cdf + pre_act * density)).astype(BF16)
    bias_ref[0] = jnp.sum(pre_grad.astype(F32), axis=0, keepdims=True)

    @pl.when(turn % 2 == 1)
    def _():
        to_core.wait_send()

    give[chunk, 0] = dot_nn(xt_ref[...], pre_grad).astype(BF16)
    give[chunk, 1] = dot_nn(dyt_ref[...], hidden).astype(BF16)
    out_ref[...] += dot_nt(hidden, down_ref[...])
    back_ref[...] += dot_nt(pre_grad, up_ref[...])

    @pl.when(theirs)
    def _():
        to_core.start()

    @pl.when(jnp.logical_not(theirs))
    def _():
        to_core.wait_recv()
        gup_ref[0] = (give[chunk, 0].astype(F32) + got[slot, 0].astype(F32)).astype(BF16)
        gdown_ref[0] = (give[chunk, 1].astype(F32) + got[slot, 1].astype(F32)).astype(BF16)

    for k in range(chunks):

        @pl.when(s == chunks + k)
        def _():
            def keep(z, carry):
                rows = pl.ds(pl.multiple_of((2 * z + 1 - y) * r, r), r)
                size = gup_ref.shape[2]
                diagonal[0, z, :, k * size : (k + 1) * size] = gup_ref[0, rows, :]
                diagonal[1, z, :, k * size : (k + 1) * size] = gdown_ref[0, rows, :]
                return carry

            lax.fori_loop(0, m, keep, 0)
            if k == chunks - 1:
                for copy in across:
                    copy.start()

    @pl.when(s == pl.num_programs(0) - 1)
    def _():
        def norm_back(rows):
            third = back_ref[rows, :]
            upstream = dy_ref[rows, :].astype(F32)
            rows_grad, gain_terms = norm_rows_back(after_ref[rows, :], third, norm_ref[2, 0:1, :])
            rows_grad = rows_grad + upstream
            low = rows_grad.astype(BF16)
            rows_out[rows, :] = rows_grad
            low_out[rows, :] = low
            for k, terms in enumerate((gain_terms, third, low.astype(F32), upstream)):
                sums_ref[k : k + 1, :] += jnp.sum(terms, axis=0, keepdims=True)

        by_rows(x_ref.shape[0], 128, norm_back)
        for copy in across:
            copy.wait()


def feed_forward(x, dy, weights, bias, after, biases, norm):
    rows, width = x.shape
    hidden = weights[0].shape[2]
    size = min(512, hidden)
    chunks = hidden // size

    n = lax.axis_size("dp")
    m, r = n // 2, width // n

    def block(s):
        return 3 - s // chunks

    def placed(s):
        turn = s // chunks
        return (1 - turn // 2, 0, (s % chunks) * (turn % 2))

    rows_spec = const((rows, width))
    grad_spec = pl.BlockSpec((1, width, size), placed)
    bias_spec = pl.BlockSpec((1, 1, size), lambda s: (block(s), 0, s % chunks))
    return pl.pallas_call(
        functools.partial(feed_forward_kernel, chunks=chunks),
        grid=(4 * chunks,),
        in_specs=[
            rows_spec,
            rows_spec,
            ANY,
            ANY,
            ANY,
            ANY,
            const(bias.shape),
            rows_spec,
            const(biases.shape),
            const(norm.shape),
        ],
        out_specs=[rows_spec, rows_spec, rows_spec, const((8, width)), grad_spec, grad_spec, bias_spec, ANY, ANY],
        out_shape=[
            jax.ShapeDtypeStruct((rows, width), F32),
            jax.ShapeDtypeStruct((rows, width), F32),
            jax.ShapeDtypeStruct((rows, width), BF16),
            jax.ShapeDtypeStruct((8, width), F32),
            jax.ShapeDtypeStruct((2, width, hidden), BF16),
            jax.ShapeDtypeStruct((2, width, hidden), BF16),
            jax.ShapeDtypeStruct((4, 1, hidden), F32),
            jax.ShapeDtypeStruct((2, m // 2, r, hidden), BF16),
            jax.ShapeDtypeStruct((2, m - m // 2, r, hidden), BF16),
        ],
        scratch_shapes=[
            pltpu.VMEM((width, rows), BF16),
            pltpu.VMEM((width, rows), BF16),
            pltpu.VMEM((rows, width), F32),
            pltpu.VMEM((chunks, 2, width, size), BF16),
            pltpu.VMEM((2 * chunks, 2, width, size), BF16),
            pltpu.VMEM((2, m, r, hidden), BF16),
            pltpu.VMEM((2, 2, width, size), BF16),
            pltpu.SemaphoreType.DMA((2, 2)),
        ]
        + link_scratch(2 * chunks + 2, 1),
        compiler_params=pltpu.CompilerParams(
            vmem_limit_bytes=VMEM_LIMIT, collective_id=3, has_side_effects=True
        ),
        cost_estimate=pl.CostEstimate(
            flops=48 * rows * width * hidden, bytes_accessed=40 * 2**20, transcendentals=8 * rows * hidden
        ),
        name="feed_forward",
    )(x, dy, *weights, bias, after, biases, norm)


def cross_backward_kernel(
    len_ref, low_ref, x_ref, enc_ref, w_ref, q_ref, k_ref, v_ref, mt_ref, lse_ref, up_ref, down_ref, from_x, from_y,
    back_ref, enc_out, grad_ref, bq_ref, bv_ref, up_out, down_out,
    low_t, x_t, enc_t, enc_acc, give, got, *scratch, heads, bk
):
    i = pl.program_id(0)
    last = pl.num_programs(0) - 1
    links = Links(*scratch[14:])
    sums = [
        Gather(links, ref.at[0], ref.at[1], from_x.at[k], from_y.at[k], scratch[7 * k : 7 * k + 7])
        for k, ref in enumerate((up_ref, down_ref))
    ]
    leave = [links.local(g.column, out) for g, out in zip(sums, (up_out, down_out))]
    pair = i // 2
    to_core = pltpu.make_async_remote_copy(
        src_ref=give,
        dst_ref=got.at[pair],
        send_sem=links.send_sems.at[links.used + pair],
        recv_sem=links.recv_sems.at[links.used + pair],
        device_id=links.partner(CORE),
        device_id_type=pl.DeviceIdType.MESH,
    )

    @pl.when(i == 0)
    def _():
        links.greet([CORE, X, Y])
        for g in sums:
            g.start()
        low_t[...] = low_ref[...].T
        x_t[...] = x_ref[...].T
        enc_t[...] = enc_ref[...].T
        back_ref[...] = jnp.zeros_like(back_ref)
        enc_acc[...] = jnp.zeros_like(enc_acc)

    @pl.when(i == 1)
    def _():
        for g in sums:
            g.middle()

    rows, width = q_ref.shape[1:]
    n = k_ref.shape[1]
    hd = width // heads
    scale = 1.0 / math.sqrt(hd)
    w_query, w_keyval, w_out = w_ref.at[0, :, :width], w_ref.at[0, :, width : 3 * width], w_ref.at[0, :, 3 * width :]
    grads = dot_nn(low_ref[...], w_out[...]).astype(BF16)
    mixed_t = mt_ref[0]
    products = grads.T.astype(F32) * mixed_t.astype(F32)
    inner = [jnp.sum(products[h * hd : (h + 1) * hd, :], axis=0, keepdims=True) for h in range(heads)]
    scaled = q_ref[0] * jnp.asarray(scale, BF16)
    q_heads = [head_only(scaled, h, hd) for h in range(heads)]
    d_heads = [head_only(grads, h, hd) for h in range(heads)]
    lse = lse_ref[0]
    keys_t = k_ref[0].T
    dq = [None] * heads
    dkv = []
    for j in range(n // bk):
        span = slice(j * bk, (j + 1) * bk)
        ok = j * bk + lax.broadcasted_iota(jnp.int32, (bk, 1), 0) < len_ref[0]
        scores = [dot_nt(k_ref[0, span, lanes_of(h, hd)[1]], q_heads[h]) for h in range(heads)]
        dprobs = [dot_nt(v_ref[0, span, lanes_of(h, hd)[1]], d_heads[h]) for h in range(heads)]
        dv_sums, dk_sums = {}, {}
        for h in range(heads):
            part = slice(h * hd, (h + 1) * hd)
            group, _ = lanes_of(h, hd)
            probs = jnp.exp(jnp.where(ok, scores[h], NEGATIVE) - lse[h : h + 1, :])
            ds = (probs * (dprobs[h] - inner[h])).astype(BF16)
            add_group(dv_sums, group, dot_nn(probs.astype(BF16), d_heads[h]))
            add_group(dk_sums, group, dot_nn(ds, q_heads[h]))
            dq_h = dot_nn(keys_t[part, span], ds)
            dq[h] = dq_h if dq[h] is None else dq[h] + dq_h
        block = jnp.concatenate([sums_of[g].astype(BF16) for sums_of in (dk_sums, dv_sums) for g in sorted(sums_of)], 1)
        enc_acc[span, :] += dot_nt(block, w_keyval[...])
        dkv.append(block)
    dq = (jnp.concatenate(dq, 0) * scale).astype(BF16).T
    dkv = jnp.concatenate(dkv, 0)
    bq_ref[0] = jnp.sum(dq.astype(F32), axis=0, keepdims=True)
    bv_ref[0] = jnp.sum(dkv[:, width:].astype(F32), axis=0, keepdims=True)
    back_ref[...] += dot_nt(dq, w_query[...])

    @pl.when(i % 2 == 1)
    def _():
        to_core.wait_send()

    give[:, :width] = dot_nn(x_t[...], dq).astype(BF16)
    give[:, width : 3 * width] = dot_nn(enc_t[...], dkv).astype(BF16)
    give[:, 3 * width :] = dot_nn(low_t[...], mixed_t.T).astype(BF16)

    @pl.when(i % 2 == 0)
    def _():
        to_core.start()

    @pl.when(i % 2 == 1)
    def _():
        to_core.wait_recv()
        grad_ref[0] = (give[...].astype(F32) + got[pair].astype(F32)).astype(BF16)

    @pl.when(i == last)
    def _():
        enc_out[...] = enc_acc[...].astype(BF16)
        for g, copy in zip(sums, leave):
            g.end()
            copy.start()
        for copy in leave:
            copy.wait()


def cross_backward(
    lengths, low, x, encoder, weights, queries, keys, values, mixed_t, lse, up_sum, down_sum, from_x, from_y, heads
):
    count, model = x.shape
    n = encoder.shape[0]
    parts, _, columns = weights.shape
    width = columns // 4
    _, m, _, r, c = up_sum.shape

    def by_part(*shape):
        return pl.BlockSpec((1,) + shape, lambda i: (i ^ 1,) + (0,) * len(shape))

    return pl.pallas_call(
        functools.partial(cross_backward_kernel, heads=heads, bk=256),
        grid=(parts,),
        in_specs=[
            pl.BlockSpec(memory_space=pltpu.SMEM),
            const((count, model)),
            const((count, model)),
            const((n, model)),
            by_part(model, columns),
            by_part(count, width),
            by_part(n, width),
            by_part(n, width),
            by_part(width, count),
            by_part(heads, count),
            ANY,
            ANY,
            ANY,
            ANY,
        ],
        out_specs=[
            const((count, model)),
            const((n, model)),
            pl.BlockSpec((1, model, columns), lambda i: (i // 2, 0, 0), pipeline_mode=pl.Buffered(1)),
            by_part(1, width),
            by_part(1, width),
            ANY,
            ANY,
        ],
        out_shape=[
            jax.ShapeDtypeStruct((count, model), F32),
            jax.ShapeDtypeStruct((n, model), BF16),
            jax.ShapeDtypeStruct((2, model, columns), BF16),
            jax.ShapeDtypeStruct((parts, 1, width), F32),
            jax.ShapeDtypeStruct((parts, 1, width), F32),
            jax.ShapeDtypeStruct((m, r, c), BF16),
            jax.ShapeDtypeStruct((m, r, c), BF16),
        ],
        scratch_shapes=[
            pltpu.VMEM((model, count), BF16),
            pltpu.VMEM((model, count), BF16),
            pltpu.VMEM((model, n), BF16),
            pltpu.VMEM((n, model), F32),
            pltpu.VMEM((model, columns), BF16),
            pltpu.VMEM((2, model, columns), BF16),
        ]
        + gather_scratch(m, r, c) * 2
        + link_scratch(10, 12),
        compiler_params=pltpu.CompilerParams(
            vmem_limit_bytes=60 * 2**20, collective_id=4, has_side_effects=True
        ),
        cost_estimate=pl.CostEstimate(
            flops=48 * parts * count * n * width,
            bytes_accessed=16 * parts * n * width,
            transcendentals=parts * count * n * heads,
        ),
        name="cross_backward",
    )(lengths, low, x, encoder, weights, queries, keys, values, mixed_t, lse, up_sum, down_sum, from_x, from_y)


def on_device(
    block_in,
    encoder_out,
    out_grad,
    bounds,
    enc_lengths,
    norm_params,
    w_qkv,
    w_self_out,
    w_cross_q,
    w_cross_kv,
    w_cross_out,
    w_up,
    w_down,
    biases,
    up_bias,
):
    groups_count = lax.axis_size("dp")
    width = w_cross_q.shape[1]
    hidden_width = w_up.shape[1]
    heads = H // 4
    own_rows, model_width = block_in.shape
    w_rows = w_cross_q.shape[0]

    first_in, self_w, cross_column, down_square, enc_all = start_gather(
        block_in,
        norm_params,
        w_qkv,
        w_self_out,
        w_cross_q,
        w_cross_kv,
        w_cross_out,
        w_down,
        encoder_out,
    )
    self_w = self_w.reshape(model_width, 4 * width)

    self_safe = 1024
    queries, key_rows, value_rows, keys_t, self_mixed_t, self_lse, terms, cross_w, up_column, near_z = self_forward(
        bounds,
        first_in,
        self_w,
        biases,
        cross_column,
        w_up,
        down_square,
        heads,
        self_safe,
    )
    cross_w = cross_w.reshape(4, model_width, 4 * width)
    after_self, second_in, near_up, near_down, far_z = sum_after_self(
        terms, block_in, biases, norm_params, up_column, down_square, near_z
    )

    cross_q, cross_k, cross_v, cross_mixed_t, cross_lse, after_cross, third_in, far_up, far_down = cross_forward(
        enc_lengths,
        second_in,
        enc_all,
        cross_w,
        biases,
        after_self,
        norm_params,
        up_column,
        down_square,
        far_z,
        heads,
    )

    output, cross_rows_grad, cross_low, ffn_sums, up_sum, down_sum, bias_up_parts, from_x, from_y = feed_forward(
        third_in,
        out_grad,
        [w.reshape(2, model_width, hidden_width) for w in (near_up, near_down, far_up, far_down)],
        up_bias.reshape(-1, LANES),
        after_cross,
        biases,
        norm_params,
    )

    by_shard = (2, groups_count // 2, 2, w_rows, hidden_width)
    second_grad, enc_terms, cross_sum, bias_cq_parts, bias_cv_parts, up_column, down_column = cross_backward(
        enc_lengths,
        cross_low,
        second_in,
        enc_all,
        cross_w,
        cross_q,
        cross_k,
        cross_v,
        cross_mixed_t,
        cross_lse,
        up_sum.reshape(by_shard),
        down_sum.reshape(by_shard),
        from_x,
        from_y,
        heads,
    )
    cross_sum = cross_sum.reshape(2, groups_count // 2, 2, w_rows, 4 * width)

    (
        self_dq, self_dk, self_dv, self_wide, self_rows_grad, self_sums,
        summed_up, summed_down, cross_column, enc_near, enc_far,
    ) = self_backward(
        bounds,
        queries,
        key_rows,
        value_rows,
        keys_t,
        self_w,
        self_mixed_t,
        self_lse,
        second_grad,
        after_self,
        cross_rows_grad,
        norm_params,
        up_column,
        down_column,
        cross_sum,
        enc_terms,
        heads,
        self_safe,
    )
    input_grad, summed_self, vectors, summed_cross, encoder_grad = tail(
        self_dq,
        self_dk,
        self_dv,
        self_w,
        first_in,
        self_wide,
        self_mixed_t,
        block_in,
        self_rows_grad,
        cross_column,
        norm_params,
        self_sums,
        ffn_sums,
        bias_cq_parts,
        bias_cv_parts,
        bias_up_parts,
        enc_near,
        enc_far,
    )
    output, input_grad, encoder_grad, *weights_and_vectors = results(
        output, input_grad, encoder_grad, summed_self, summed_cross, summed_up, summed_down, vectors, 1.0 / groups_count
    )
    g_qkv, g_so, g_cq, g_ckv, g_co, g_up, g_down, g_norm, g_biases, g_shift = weights_and_vectors
    return (
        output,
        input_grad,
        encoder_grad,
        g_norm,
        g_qkv,
        g_so,
        g_cq,
        g_ckv,
        g_co,
        g_up,
        g_down,
        g_biases,
        g_shift.reshape(-1),
    )


def solution(mesh):
    rows = P(("dp", "tensor"), None)
    placed = (
        rows,
        rows,
        rows,
        P("dp", None),
        P("dp"),
        P(),
        P("dp", None, "tensor"),
        P("tensor", "dp"),
        P("dp", "tensor"),
        P("dp", None, "tensor"),
        P("tensor", "dp"),
        P("dp", "tensor"),
        P("tensor", "dp"),
        P(),
        P(),
    )
    return jax.shard_map(
        on_device,
        mesh=mesh,
        in_specs=placed,
        out_specs=(
            rows,
            rows,
            rows,
            P(),
            P("dp", None, "tensor"),
            P("tensor", "dp"),
            P("dp", "tensor"),
            P("dp", None, "tensor"),
            P("tensor", "dp"),
            P("dp", "tensor"),
            P("tensor", "dp"),
            P(),
            P(),
        ),
        check_vma=False,
    )
```

```python
import functools
import math

import jax
import jax.numpy as jnp
from jax import lax
from jax.experimental import pallas as pl
from jax.experimental.pallas import tpu as pltpu
from jax.sharding import PartitionSpec as P

H = 16
EPSILON = 1e-05
NEGATIVE = -1e30
F32 = jnp.float32
BF16 = jnp.bfloat16
VMEM_LIMIT = 56 * 2**20


def dot_nt(a, b):
    return lax.dot_general(a, b, (((1,), (1,)), ((), ())), preferred_element_type=F32)


def dot_nn(a, b):
    return lax.dot_general(a, b, (((1,), (0,)), ((), ())), preferred_element_type=F32)


def dot_tn(a, b):
    return lax.dot_general(a, b, (((0,), (0,)), ((), ())), preferred_element_type=F32)


LANES = 128


def lanes_of(h, size):
    group = h * size // LANES
    return group, slice(group * LANES, (group + 1) * LANES)


def head_only(x, h, size):
    group, part = lanes_of(h, size)
    lane = group * LANES + lax.broadcasted_iota(jnp.int32, (x.shape[0], LANES), 1)
    return jnp.where((lane >= h * size) & (lane < (h + 1) * size), x[:, part], jnp.zeros((), x.dtype))


def add_group(sums, group, value):
    sums[group] = value if group not in sums else sums[group] + value


def self_bad(b_ref, q_start, k_start, bq, bk, causal):
    qi = q_start + lax.broadcasted_iota(jnp.int32, (1, bq), 1)
    kj = k_start + lax.broadcasted_iota(jnp.int32, (bk, 1), 0)
    bad = (qi >= b_ref[0, 1]) & ((kj >= b_ref[0, 0]) & (kj < b_ref[0, 1]))
    if causal:
        bad = bad | (kj > qi)
    return bad


def over_keys(i, bq, safe, block, between=()):
    def visit(j, c):
        for at_i, at_j, action in between:
            pl.when((i == at_i) & (j == at_j))(action)

        @pl.when(j < safe // bq)
        def _():
            block(j * bq, bq, 0, "none")

        @pl.when(j >= safe // bq)
        def _():
            block(j * bq, bq, 0, "segment")

        return c

    lax.fori_loop(0, i, visit, 0)
    half = bq // 2
    block(i * bq, half, 0, "causal")
    block(i * bq + half, half, half, "causal")


CORE = ("tensor", 1)
X = ("tensor", 2)
Y = ("dp", 1)
ANY = pl.BlockSpec(memory_space=pl.ANY)


class Links:
    def __init__(self, send_sems, recv_sems, local_sems):
        self.dp = lax.axis_index("dp")
        self.tensor = lax.axis_index("tensor")
        self.send_sems, self.recv_sems, self.local_sems = send_sems, recv_sems, local_sems
        self.used = 0
        self.used_local = 0

    def partner(self, way):
        axis, distance = way
        if axis == "tensor":
            return (self.dp, self.tensor ^ distance)
        return (self.dp ^ distance, self.tensor)

    def greet(self, ways):
        barrier = pltpu.get_barrier_semaphore()
        for way in ways:
            pl.semaphore_signal(
                barrier, inc=1, device_id=self.partner(way), device_id_type=pl.DeviceIdType.MESH
            )
        pl.semaphore_wait(barrier, len(ways))

    def copy(self, source, target, way):
        k = self.used
        self.used += 1
        return pltpu.make_async_remote_copy(
            src_ref=source,
            dst_ref=target,
            send_sem=self.send_sems.at[k],
            recv_sem=self.recv_sems.at[k],
            device_id=self.partner(way),
            device_id_type=pl.DeviceIdType.MESH,
        )

    def local(self, source, target):
        k = self.used_local
        self.used_local += 1
        return pltpu.make_async_copy(source, target, self.local_sems.at[k])


def link_scratch(copies, local):
    return [
        pltpu.SemaphoreType.DMA((copies,)),
        pltpu.SemaphoreType.DMA((copies,)),
        pltpu.SemaphoreType.DMA((local,)),
    ]


def z_distances(n):
    found = []
    m = n // 2
    while m > 1:
        m //= 2
        found.append(m)
    return found


def z_ways(n):
    return [("dp", 2 * distance) for distance in z_distances(n)]


def column_stages(links, shard, column, n):
    z = links.dp // 2
    held = [z]
    stages = []
    for distance in z_distances(n):
        stages.append(
            [
                (
                    links.copy(shard if k == 0 else column.at[index], column.at[index], ("dp", 2 * distance)),
                    index ^ distance,
                )
                for k, index in enumerate(held)
            ]
        )
        held = held + [index ^ distance for index in held]
    return stages


class Spread:
    def __init__(self, links, source, column, whole):
        y = links.dp % 2
        half = column.shape[0] // 2
        low, high = pl.ds(0, half), pl.ds(half, half)
        near, near_core, far, far_core = (whole.at[k] for k in range(4))
        self.load = links.local(source, column)
        self.own = links.local(column, near.at[:, y])
        self.first = [
            links.copy(column, near.at[:, y], Y),
            links.copy(column, far.at[:, y], X),
        ]
        self.core = [links.copy(column, near_core.at[:, y], CORE)]
        self.second = [
            links.copy(near.at[low, 1 - y], far.at[low, 1 - y], X),
            links.copy(far.at[high, y], far.at[high, y], Y),
        ]
        self.core_second = [
            links.copy(near.at[:, 1 - y], near_core.at[:, 1 - y], CORE),
            links.copy(far.at[:, y], far_core.at[:, y], CORE),
        ]
        self.core_third = [links.copy(far.at[:, 1 - y], far_core.at[:, 1 - y], CORE)]

    def start(self):
        self.load.start()
        self.load.wait()
        for copy in self.first + self.core + [self.own]:
            copy.start()

    def middle(self):
        for copy in self.first:
            copy.wait_recv()
        for copy in self.second + self.core_second:
            copy.start()

    def last(self):
        for copy in self.second:
            copy.wait_recv()
        for copy in self.core_third:
            copy.start()

    def end(self):
        self.own.wait()
        for copy in self.first + self.second:
            copy.wait_send()
        for copy in self.core + self.core_second + self.core_third:
            copy.wait()


def add_to(total_ref, other_ref):
    def one(k, c):
        total_ref[k] = (total_ref[k].astype(F32) + other_ref[k].astype(F32)).astype(BF16)
        return c

    lax.fori_loop(0, total_ref.shape[0], one, 0)


class Gather:
    def __init__(self, links, near, far, from_x, from_y, buffers):
        y = links.dp % 2
        self.column, self.over_y, self.over_x, self.add_y, self.add_x, self.sum_y, self.sum_x = buffers
        m = self.column.shape[0]
        low, high = pl.ds(0, m // 2), pl.ds(m // 2, m - m // 2)
        self.loads = [
            links.local(near.at[low, 1 - y], self.over_y),
            links.local(far.at[high, y], self.over_x),
            links.local(from_x, self.add_y),
            links.local(from_y, self.add_x),
            links.local(near.at[:, y], self.column),
        ]
        self.first = [
            links.copy(far.at[low, y], self.sum_x.at[low], X),
            links.copy(near.at[high, 1 - y], self.sum_y.at[high], Y),
        ]
        self.second = [
            links.copy(self.over_x, self.sum_x.at[high], X),
            links.copy(self.over_y, self.sum_y.at[low], Y),
        ]

    def start(self):
        for copy in self.first + self.loads:
            copy.start()

    def middle(self):
        for copy in self.loads:
            copy.wait()
        add_to(self.over_x, self.add_x)
        add_to(self.over_y, self.add_y)
        for copy in self.second:
            copy.start()

    def end(self):
        for copy in self.first + self.second:
            copy.wait_recv()
        add_to(self.column, self.sum_y)
        add_to(self.column, self.sum_x)
        for copy in self.first + self.second:
            copy.wait_send()


def gather_scratch(m, r, c):
    whole = pltpu.VMEM((m, r, c), BF16)
    half = pltpu.VMEM((m // 2, r, c), BF16)
    return [whole] + [half] * 4 + [whole] * 2


class GatherLast:
    def __init__(self, links, near, far, buffers):
        y = links.dp % 2
        self.column, self.over_x, self.diagonal, self.sum_y, self.sum_x = buffers
        self.loads = [links.local(far.at[:, y], self.over_x), links.local(near.at[:, y], self.column)]
        self.first = links.copy(far.at[:, 1 - y], self.diagonal, Y)
        self.over_y = links.copy(near.at[:, 1 - y], self.sum_y, Y)
        self.along_x = links.copy(self.over_x, self.sum_x, X)

    def start(self):
        self.first.start()
        for copy in self.loads:
            copy.start()

    def second(self):
        self.first.wait_recv()
        self.over_y.start()

    def middle(self):
        for copy in self.loads:
            copy.wait()
        add_to(self.over_x, self.diagonal)
        self.along_x.start()

    def end(self):
        self.over_y.wait_recv()
        self.along_x.wait_recv()
        add_to(self.column, self.sum_y)
        add_to(self.column, self.sum_x)
        for copy in (self.first, self.over_y, self.along_x):
            copy.wait_send()


class Collect:
    def __init__(self, links, column, slots):
        z = links.dp // 2
        self.column, self.slots, self.z = column, slots, z
        m = column.shape[0]
        distances = z_distances(2 * m)[::-1]
        self.stages = []
        first = 0
        for step, distance in enumerate(distances):
            kept = [0]
            for other in distances[step + 1 :]:
                kept = kept + [k ^ other for k in kept]
            self.stages.append(
                [
                    (links.copy(column.at[z ^ distance ^ k], slots.at[first + i], ("dp", 2 * distance)), first + i, z ^ k)
                    for i, k in enumerate(kept)
                ]
            )
            first += len(kept)

    def start(self, step):
        for copy, _, _ in self.stages[step]:
            copy.start()

    def finish(self, step):
        for copy, slot, index in self.stages[step]:
            copy.wait_recv()
            self.column[index] = (self.column[index].astype(F32) + self.slots[slot].astype(F32)).astype(BF16)

    def drain(self):
        for stage in self.stages:
            for copy, _, _ in stage:
                copy.wait_send()


class Square:
    def __init__(self, links, shard, out):
        y = links.dp % 2
        c = shard.shape[1]
        low, high = pl.ds(0, c // 2), pl.ds(c // 2, c // 2)
        self.own = links.local(shard, out.at[0, y])
        self.first = [links.copy(shard, out.at[0, y], Y), links.copy(shard, out.at[1, y], X)]
        self.second = [
            links.copy(out.at[0, 1 - y, :, low], out.at[1, 1 - y, :, low], X),
            links.copy(out.at[1, y, :, high], out.at[1, y, :, high], Y),
        ]

    def start(self):
        for copy in self.first + [self.own]:
            copy.start()

    def middle(self):
        for copy in self.first:
            copy.wait_recv()
        for copy in self.second:
            copy.start()

    def end(self):
        for copy in self.first:
            copy.wait_send()
        for copy in self.second:
            copy.wait()
        self.own.wait()


class SpreadZ:
    def __init__(self, links, own, other, hold, whole, n):
        z = links.dp // 2
        distances = z_distances(n)
        there = z ^ distances[0]
        final, core = whole.at[0], whole.at[1]
        self.loads = [links.local(own, hold.at[0]), links.local(other, hold.at[1])]
        self.stores = [links.local(hold.at[0], final.at[z]), links.local(hold.at[1], final.at[there])]
        self.core = [links.copy(hold.at[0], core.at[z], CORE), links.copy(hold.at[1], core.at[there], CORE)]
        held = [(hold.at[0], z), (hold.at[1], there)]
        self.stages, self.core_stages = [], []
        for distance in distances[1:]:
            came = [index ^ distance for _, index in held]
            self.stages.append([links.copy(ref, final.at[index], ("dp", 2 * distance)) for ref, index in held])
            self.core_stages.append([links.copy(final.at[index], core.at[index], CORE) for index in came])
            held = held + [(final.at[index], index) for index in came]

    def start(self):
        for copy in self.loads:
            copy.start()
        for copy in self.loads:
            copy.wait()
        for copy in self.stages[0] + self.stores + self.core:
            copy.start()

    def onward(self):
        for step, (stage, core_stage) in enumerate(zip(self.stages, self.core_stages)):
            for copy, onward in zip(stage, core_stage):
                copy.wait_recv()
                onward.start()
            for copy in self.stages[step + 1] if step + 1 < len(self.stages) else []:
                copy.start()

    def end(self):
        for copy in self.stores + self.core:
            copy.wait()
        for stage, core_stage in zip(self.stages, self.core_stages):
            for copy in stage:
                copy.wait_send()
            for copy in core_stage:
                copy.wait()


def spread_z_copies(n):
    return 2 * n


class SpreadFar:
    def __init__(self, links, column, whole):
        y = links.dp % 2
        far, far_core = whole.at[0], whole.at[1]
        m, _, c = column.shape
        step = max(m // 4, 1)
        self.over_x, self.over_y, self.core_x, self.core_y = [], [], [], []
        for k in range(m // step):
            for h in range(2):
                z, part = pl.ds(k * step, step), pl.ds(h * (c // 2), c // 2)
                own = far.at[z, y, :, part]
                other = far.at[z, 1 - y, :, part]
                self.over_x.append(links.copy(column.at[z, :, part], own, X))
                self.over_y.append(links.copy(own, own, Y))
                self.core_x.append(links.copy(own, far_core.at[z, y, :, part], CORE))
                self.core_y.append(links.copy(other, far_core.at[z, 1 - y, :, part], CORE))

    def start(self):
        for copy in self.over_x:
            copy.start()

    def onward(self, k):
        self.over_x[k].wait_recv()
        self.over_y[k].start()
        self.core_x[k].start()

    def last(self, k):
        self.over_y[k].wait_recv()
        self.core_y[k].start()

    def end(self):
        for copy in self.over_x + self.over_y:
            copy.wait_send()
        for copy in self.core_x + self.core_y:
            copy.wait()


class RowSum:
    def __init__(self, links, terms, buffers):
        self.near, self.far, self.got_near, self.got_far, self.got_x = buffers
        count = self.near.shape[0]

        def rows(distance):
            start = pl.multiple_of((links.tensor ^ distance) * count, count)
            return terms.at[pl.ds(start, count)]

        self.loads = [links.local(rows(0), self.near), links.local(rows(2), self.far)]
        self.core = [links.copy(rows(3), self.got_far, CORE), links.copy(rows(1), self.got_near, CORE)]
        self.over_x = None if self.got_x is None else links.copy(self.far, self.got_x, X)

    def start(self):
        for copy in self.loads[::-1] + self.core:
            copy.start()

    def middle(self):
        self.loads[1].wait()
        self.core[0].wait_recv()

        def add(rows):
            self.far[rows, :] = (self.far[rows, :].astype(F32) + self.got_far[rows, :].astype(F32)).astype(BF16)

        by_rows(self.far.shape[0], 64, add)
        self.over_x.start()

    def core_end(self):
        for copy in self.loads + self.core:
            copy.wait()

    def end(self):
        self.loads[0].wait()
        self.core[1].wait_recv()
        self.over_x.wait_recv()
        for copy in self.core + [self.over_x]:
            copy.wait_send()

    def total(self, rows):
        return self.near[rows, :].astype(F32) + self.got_near[rows, :].astype(F32) + self.got_x[rows, :].astype(F32)


def row_sum_scratch(count, width):
    return [pltpu.VMEM((count, width), BF16)] * 5


class Everywhere:
    def __init__(self, links, held, slots, ways):
        self.held, self.slots = held, slots
        self.copies = [links.copy(held.at[k], slots.at[k], way) for k, way in enumerate(ways)]

    def start(self, step):
        self.copies[step].start()

    def finish(self, step):
        self.copies[step].wait()
        self.held[step + 1] = self.held[step] + self.slots[step]


class Direct:
    def __init__(self, links, value, slots_tensor, slots_dp, n):
        self.value = value
        self.slots = (slots_tensor, slots_dp)
        self.me = (links.tensor, links.dp)
        self.copies = []
        for slots, me, axis, size in zip(self.slots, self.me, ("tensor", "dp"), (4, n)):
            self.copies.append([links.copy(value, slots.at[me], (axis, d)) for d in range(1, size)])

    def start(self, phase):
        for copy in self.copies[phase]:
            copy.start()

    def finish(self, phase):
        slots = self.slots[phase]
        slots[self.me[phase]] = self.value[...]
        for copy in self.copies[phase]:
            copy.wait()
        total = slots[0]
        for k in range(1, slots.shape[0]):
            total = total + slots[k]
        self.value[...] = total


def direct_ways(n):
    return [("tensor", d) for d in range(1, 4)] + [("dp", d) for d in range(1, n)]


def everywhere_ways(n):
    return [CORE, X, Y] + z_ways(n)


def everywhere_scratch(k, c, n):
    steps = len(everywhere_ways(n))
    return [pltpu.VMEM((steps + 1, k, c), F32), pltpu.VMEM((steps, k, c), F32)]


def tail_kernel(
    dq_ref, dk_ref, dv_ref, w_ref, first_hbm, wide_hbm, mt_hbm, rows_hbm, grad_hbm, cross_hbm, norm_ref,
    self_ref, ffn_ref, cq_ref, cv_ref, up_ref, enc_near, enc_far,
    grad_out, weights_out, late_out, cross_out, enc_out, enc_got, give, acc, weights,
    first_ref, wide_ref, mt_ref, rows_ref, grad_ref, cross_ref, cross_slots, *scratch, n, step_rows
):
    links = Links(*scratch[-3:])
    loads = [
        links.local(source, target)
        for source, target in (
            (cross_hbm, cross_ref), (first_hbm, first_ref), (wide_hbm, wide_ref), (mt_hbm, mt_ref),
            (rows_hbm, rows_ref), (grad_hbm, grad_ref),
        )
    ]
    for copy in loads:
        copy.start()
    cross = Collect(links, cross_ref, cross_slots)
    member = links.tensor
    near, far, got_near, got_far, got_x = scratch[:5]
    columns, gots, slots = scratch[5:7], scratch[7:9], scratch[9:11]
    late_tensor, late_dp, sums, early_slots, held, compact = scratch[11:17]
    count, model = near.shape
    width = dq_ref.shape[1]
    y = links.dp % 2
    c = columns[0].shape[2]
    m, _, r, _ = weights.shape
    half = count // 2
    parts = [pl.ds(0, half), pl.ds(half, half)]
    core_far = links.copy(give.at[0], got_far, CORE)
    core_near = links.copy(give.at[1], got_near, CORE)
    over_x = [links.copy(far.at[part], got_x.at[part], X) for part in parts]
    over_y, collects = [], []
    for k, (column, got, slot) in enumerate(zip(columns, gots, slots)):
        over_y.append(links.copy(weights.at[:, 1 - y, :, pl.ds(k * c, c)], got, Y))
        collects.append(Collect(links, column, slot))
    stages = len(collects[0].stages)
    late = Direct(links, compact, late_tensor, late_dp, n)
    early = Everywhere(links, sums, early_slots, [CORE] + z_ways(n) + [Y, X])
    steps = len(early.copies)
    enc_x = links.copy(enc_far, enc_got, X)
    links.greet(direct_ways(n))
    enc_x.start()

    def terms(distance, target):
        base = (member ^ distance) * count

        def one(rows):
            there = pl.ds(pl.multiple_of(base + rows.start, 128), 128)
            total = dot_nt(dq_ref[there, :], w_ref[:, :width])
            total = total + dot_nt(dk_ref[there, :], w_ref[:, width : 2 * width])
            target[rows, :] = (total + dot_nt(dv_ref[there, :], w_ref[:, 2 * width : 3 * width])).astype(BF16)

        by_rows(count, 128, one)

    def packed(k):
        for block in range(2 * m):
            span = slice(block * r, (block + 1) * r)
            weights[block // 2, block % 2, :, k * c : (k + 1) * c] = acc[span, k * c : (k + 1) * c].astype(BF16)
        columns[k][...] = weights[:, y, :, k * c : (k + 1) * c]

    loads[0].wait()
    cross.start(0)
    acc[...] = jnp.zeros_like(acc)
    loads[1].wait()

    def products(refs, at):
        def one(rows):
            source = first_ref[rows, :].T
            for k, ref in enumerate(refs):
                acc[:, (at + k) * width : (at + k + 1) * width] += dot_nn(source, ref[rows, :])

        return one

    by_rows(dq_ref.shape[0], step_rows, products((dq_ref, dk_ref), 0))
    packed(0)
    over_y[0].start()
    terms(3, give.at[0])
    core_far.start()
    terms(2, far)
    core_far.wait_recv()
    for part, copy in zip(parts, over_x):

        def add(rows, part=part):
            there = pl.ds(pl.multiple_of(part.start + rows.start, 64), 64)
            far[there, :] = (far[there, :].astype(F32) + got_far[there, :].astype(F32)).astype(BF16)

        by_rows(half, 64, add)
        copy.start()
    for copy in loads[2:]:
        copy.wait()

    def products_out(rows):
        acc[:, 3 * width :] += dot_nn(wide_ref[rows, :].T, mt_ref[:, rows].T)

    held[...] = jnp.zeros_like(held)
    sums[0] = jnp.zeros(sums.shape[1:], F32)
    sums[0, 0:2, :] = self_ref[0:2, :]
    sums[0, 2:4, :] = ffn_ref[0:2, :]
    sums[0, 6:7, :] = self_ref[2:3, :]
    sums[0, 9:11, :] = ffn_ref[2:4, :]
    for distance in range(4):
        there = pl.ds(pl.multiple_of((member ^ distance) * width, width), width)
        sums[0, 7:8, there] = cq_ref[distance]
        sums[0, 8:9, there] = cv_ref[distance]
        sums[0, pl.ds(11 + (member ^ distance), 1), :] = up_ref[distance]
    here = pl.ds(pl.multiple_of(member * width, width), width)

    def column_sums(rows):
        sums[0, 4:5, here] += jnp.sum(dq_ref[rows, :].astype(F32), axis=0, keepdims=True)
        sums[0, 5:6, here] += jnp.sum(dv_ref[rows, :].astype(F32), axis=0, keepdims=True)

    by_rows(dq_ref.shape[0], step_rows, column_sums)
    early.start(0)

    def norm_back(part):
        def one(rows):
            rows = pl.ds(pl.multiple_of(part.start + rows.start, 64), 64)
            incoming = near[rows, :].astype(F32) + got_near[rows, :].astype(F32) + got_x[rows, :].astype(F32)
            rows_grad, gain_terms = norm_rows_back(rows_ref[rows, :].astype(F32), incoming, norm_ref[0, 0:1, :])
            grad_out[rows, :] = rows_grad + grad_ref[rows, :]
            held[0:1, :] += jnp.sum(gain_terms, axis=0, keepdims=True)
            held[1:2, :] += jnp.sum(incoming, axis=0, keepdims=True)

        by_rows(half, 64, one)

    def summed_y(k):
        over_y[k].wait_recv()
        add_to(columns[k], gots[k])
        collects[k].start(0)

    def next_z(k):
        for step in range(stages - 1):
            collects[k].finish(step)
            collects[k].start(step + 1)

    def last_z(k):
        collects[k].finish(stages - 1)
        weights_out[:, k * c : (k + 1) * c] = columns[k][collects[k].z].astype(F32)

    for step in range(stages - 1):
        cross.finish(step)
        cross.start(step + 1)
    by_rows(dq_ref.shape[0], step_rows, products((dv_ref,), 2))
    by_rows(dq_ref.shape[0], step_rows, products_out)
    packed(1)
    over_y[1].start()
    summed_y(0)
    early.finish(0)
    terms(1, give.at[1])
    core_near.start()
    terms(0, near)
    enc_x.wait_recv()
    enc_out[...] = enc_near[...] + enc_got[...].astype(F32)
    core_near.wait_recv()
    over_x[0].wait_recv()
    norm_back(parts[0])
    cross.finish(stages - 1)
    cross_out[...] = cross_ref[cross.z].astype(F32)
    next_z(0)
    summed_y(1)
    for step in range(1, steps - 2):
        early.start(step)
        early.finish(step)
    over_x[1].wait_recv()
    norm_back(parts[1])
    next_z(1)
    lines = model // LANES
    for k in range(2 * lines):
        compact[k : k + 1, :] = held[k // lines : k // lines + 1, k % lines * LANES : (k % lines + 1) * LANES]
    late.start(0)
    early.start(steps - 2)
    last_z(0)
    early.finish(steps - 2)
    late.finish(0)
    late.start(1)
    early.start(steps - 1)
    last_z(1)
    early.finish(steps - 1)
    late_out[2:, :] = sums[steps]
    late.finish(1)
    for k in range(2 * lines):
        late_out[k // lines : k // lines + 1, k % lines * LANES : (k % lines + 1) * LANES] = compact[k : k + 1, :]
    for copy in over_x + over_y + [core_near, core_far]:
        copy.wait_send()
    for collect in collects + [cross]:
        collect.drain()
    enc_x.wait_send()


def tail(
    dq, dk, dv, w, first, wide, mixed_t, rows, grad, cross_column, norm, self_sums, ffn_sums, cq_sums, cv_sums, up_sums,
    enc_near, enc_far,
):
    n = lax.axis_size("dp")
    count, model = rows.shape
    width = dq.shape[1]
    m, r, c = n // 2, model // n, 4 * width
    vectors = (16, model)
    vmem = pl.BlockSpec(memory_space=pltpu.VMEM)
    part = pltpu.VMEM((m, r, c // 2), BF16)
    return pl.pallas_call(
        functools.partial(tail_kernel, n=n, step_rows=512),
        in_specs=[vmem] * 4 + [ANY] * 6 + [vmem] * 8,
        out_specs=[vmem] * 5,
        out_shape=[
            jax.ShapeDtypeStruct((count, model), F32),
            jax.ShapeDtypeStruct((r, c), F32),
            jax.ShapeDtypeStruct((vectors[0] + 2, model), F32),
            jax.ShapeDtypeStruct(cross_column.shape[1:], F32),
            jax.ShapeDtypeStruct(enc_near.shape, F32),
        ],
        scratch_shapes=[
            pltpu.VMEM(enc_far.shape, BF16),
            pltpu.VMEM((2, count, model), BF16),
            pltpu.VMEM((model, c), F32),
            pltpu.VMEM((m, 2, r, c), BF16),
        ]
        + [pltpu.VMEM(v.shape, v.dtype) for v in (first, wide, mixed_t, rows, grad, cross_column, cross_column)]
        + row_sum_scratch(count, model)
        + [part] * 6
        + [pltpu.VMEM((size, 2 * model // LANES, LANES), F32) for size in (4, n)]
        + everywhere_scratch(*vectors, n)
        + [pltpu.VMEM((8, model), F32), pltpu.VMEM((2 * model // LANES, LANES), F32)]
        + link_scratch(7 + 3 * m + len(everywhere_ways(n)) + len(direct_ways(n)), 6),
        compiler_params=pltpu.CompilerParams(
            vmem_limit_bytes=VMEM_LIMIT, collective_id=7, has_side_effects=True
        ),
        cost_estimate=pl.CostEstimate(flops=0, bytes_accessed=100 * 2**20, transcendentals=0),
        name="tail",
    )(
        dq, dk, dv, w, first, wide, mixed_t, rows, grad, cross_column, norm,
        self_sums, ffn_sums, cq_sums, cv_sums, up_sums, enc_near, enc_far,
    )


def results_kernel(
    output_ref, grad_ref, enc_ref, self_ref, cross_ref, up_ref, down_ref, vectors_ref,
    output_out, grad_out, enc_out, qkv_out, so_out, cq_out, ckv_out, co_out, up_out, down_out,
    norm_out, biases_out, shift_out, *, scale
):
    output_out[...] = output_ref[...]
    grad_out[...] = grad_ref[...]
    enc_out[...] = enc_ref[...]
    width = cq_out.shape[1]

    @pl.when(pl.program_id(0) == 0)
    def _():
        for k in range(3):
            qkv_out[:, k, :] = self_ref[:, k * width : (k + 1) * width] * scale
        so_out[...] = (self_ref[:, 3 * width :] * scale).T
        cq_out[...] = cross_ref[:, :width] * scale
        for k in range(2):
            ckv_out[:, k, :] = cross_ref[:, (k + 1) * width : (k + 2) * width] * scale
        co_out[...] = (cross_ref[:, 3 * width :] * scale).T
        up_out[...] = up_ref[...] * scale
        down_out[...] = (down_ref[...] * scale).T
        vectors = vectors_ref[...] * scale
        for k in range(3):
            norm_out[k] = vectors[2 * k : 2 * k + 2, :]
        biases_out[...] = vectors[6:13, :]
        lines = vectors.shape[1] // LANES
        for k in range(shift_out.shape[0]):
            part = slice(k % lines * LANES, (k % lines + 1) * LANES)
            shift_out[k : k + 1, :] = vectors[13 + k // lines : 14 + k // lines, part]


def results(output, grad, encoder, self_w, cross_w, up, down, vectors, scale):
    r, c = self_w.shape
    width = c // 4
    steps = 2

    def rows(value):
        return pl.BlockSpec((value.shape[0] // steps, value.shape[1]), lambda i: (i, 0))

    shapes = [(r, 3, width), (width, r), (r, width), (r, 2, width), (width, r), up.shape, down.shape[::-1]]
    shapes += [(3, 2, output.shape[1]), (7, output.shape[1]), (4 * up.shape[1] // LANES, LANES)]
    return pl.pallas_call(
        functools.partial(results_kernel, scale=scale),
        grid=(steps,),
        in_specs=[rows(output), rows(grad), rows(encoder)] + [const(v.shape) for v in (self_w, cross_w, up, down, vectors)],
        out_specs=[rows(output), rows(grad), rows(encoder)] + [const(shape) for shape in shapes],
        out_shape=[jax.ShapeDtypeStruct(v.shape, F32) for v in (output, grad, encoder)]
        + [jax.ShapeDtypeStruct(shape, F32) for shape in shapes],
        compiler_params=pltpu.CompilerParams(vmem_limit_bytes=VMEM_LIMIT),
        cost_estimate=pl.CostEstimate(flops=0, bytes_accessed=20 * 2**20, transcendentals=0),
        name="results",
    )(output, grad, encoder, self_w, cross_w, up, down, vectors)


def start_kernel(
    in_ref, norm_ref, qkv_ref, so_ref, cq_ref, ckv_ref, co_ref, down_ref, enc_ref,
    rows_out, self_out, cross_out, down_out, enc_out, rows_ref, self_ref, cross_ref, shard_ref, send_sems, recv_sems, local_sems, *, n
):
    links = Links(send_sems, recv_sems, local_sems)
    member, z, y = links.tensor, links.dp // 2, links.dp % 2
    count = rows_ref.shape[0]
    half = count // 2
    parts = [pl.ds(0, half), pl.ds(half, half)]

    def place(distance):
        return rows_out.at[pl.ds(pl.multiple_of((member ^ distance) * count, count), count)]

    over_x = [links.copy(rows_ref.at[part], place(0).at[part], X) for part in parts]
    over_core = [links.copy(rows_ref, place(0), CORE)]
    over_core += [links.copy(place(2).at[part], place(2).at[part], CORE) for part in parts]
    self_stages = column_stages(links, self_ref, self_out.at[:, y], n)
    cross_stages = column_stages(links, cross_ref, cross_out, n)
    over_y = [links.copy(self_ref, self_out.at[z, y], Y)]
    local = [
        links.local(rows_ref, place(0)),
        links.local(self_ref, self_out.at[z, y]),
        links.local(cross_ref, cross_out.at[z]),
    ]
    width = cq_ref.shape[1]
    for k in range(3):
        self_ref[:, k * width : (k + 1) * width] = qkv_ref[:, k, :]
    self_ref[:, 3 * width :] = so_ref[...].T
    cross_ref[:, :width] = cq_ref[...]
    for k in range(2):
        cross_ref[:, (k + 1) * width : (k + 2) * width] = ckv_ref[:, k, :]
    cross_ref[:, 3 * width :] = co_ref[...].T
    shard_ref[...] = down_ref[...].T
    square = Square(links, shard_ref, down_out)
    enc_count = enc_ref.shape[0]

    def enc_place(distance):
        return enc_out.at[pl.ds(pl.multiple_of((member ^ distance) * enc_count, enc_count), enc_count)]

    enc_x = links.copy(enc_ref, enc_place(0), X)
    enc_core = [links.copy(enc_ref, enc_place(0), CORE), links.copy(enc_place(2), enc_place(2), CORE)]
    local.append(links.local(enc_ref, enc_place(0)))
    links.greet([CORE, X, Y] + z_ways(n))
    for copy in over_y + local[1:]:
        copy.start()
    for copy, _ in self_stages[0]:
        copy.start()
    for part, copy in zip(parts, over_x):

        def norm(rows, part=part):
            rows = pl.ds(pl.multiple_of(part.start + rows.start, 64), 64)
            xhat, _ = normalized(in_ref[rows, :].astype(F32))
            rows_ref[rows, :] = (xhat * norm_ref[0, 0:1, :] + norm_ref[0, 1:2, :]).astype(BF16)

        by_rows(half, 64, norm)
        copy.start()
    for copy in local[:1] + over_core[:1]:
        copy.start()
    square.start()
    enc_x.start()
    enc_core[0].start()
    for self_stage in self_stages:
        if self_stage is not self_stages[0]:
            for copy, _ in self_stage:
                copy.start()
        for copy, index in self_stage:
            copy.wait_recv()
            onward = links.copy(self_out.at[index, y], self_out.at[index, y], Y)
            onward.start()
            over_y.append(onward)
        if self_stage is self_stages[0]:
            for copy, _ in cross_stages[0]:
                copy.start()
    for cross_stage, later in zip(cross_stages, cross_stages[1:] + [[]]):
        for copy, _ in cross_stage:
            copy.wait_recv()
        for copy, _ in later:
            copy.start()
    for copy, onward in zip(over_x, over_core[1:]):
        copy.wait_recv()
        onward.start()
    square.middle()
    enc_x.wait_recv()
    enc_core[1].start()
    enc_x.wait_send()
    square.end()
    for copy in local + over_y + over_core + enc_core:
        copy.wait()
    for copy in over_x:
        copy.wait_send()
    for stage in self_stages + cross_stages:
        for copy, _ in stage:
            copy.wait_send()


def start_gather(rows, norm, qkv, self_out, cross_q, cross_kv, cross_out, down, encoder):
    n = lax.axis_size("dp")
    r, c = cross_q.shape[0], 4 * cross_q.shape[1]
    return pl.pallas_call(
        functools.partial(start_kernel, n=n),
        in_specs=[pl.BlockSpec(memory_space=pltpu.VMEM)] * 9,
        out_specs=[ANY] * 5,
        out_shape=[
            jax.ShapeDtypeStruct((4 * rows.shape[0], rows.shape[1]), BF16),
            jax.ShapeDtypeStruct((n // 2, 2, r, c), BF16),
            jax.ShapeDtypeStruct((n // 2, r, c), BF16),
            jax.ShapeDtypeStruct((2, 2, r, down.shape[0]), BF16),
            jax.ShapeDtypeStruct((4 * encoder.shape[0], encoder.shape[1]), BF16),
        ],
        scratch_shapes=[pltpu.VMEM(rows.shape, BF16)]
        + [pltpu.VMEM((r, c), BF16)] * 2
        + [pltpu.VMEM((r, down.shape[0]), BF16)]
        + link_scratch(2 * n + 15, 5),
        compiler_params=pltpu.CompilerParams(
            vmem_limit_bytes=VMEM_LIMIT, collective_id=0, has_side_effects=True
        ),
        cost_estimate=pl.CostEstimate(flops=0, bytes_accessed=100 * 2**20, transcendentals=0),
        name="start_gather",
    )(rows, norm, qkv, self_out, cross_q, cross_kv, cross_out, down, encoder)


def self_forward_kernel(
    b_ref, x_ref, w_ref, biases_ref, column_ref, up_ref, down_ref,
    q_out, k_ref, v_out, kt_out, ot_ref, lse_ref, terms_ref, whole, next_column, far_down,
    vt_ref, m_s, l_s, acc, column, send_sems, recv_sems, local_sems, *, heads, safe, n
):
    i = pl.program_id(0)
    last = pl.num_programs(0) - 1
    bq, width = q_out.shape
    links = Links(send_sems, recv_sems, local_sems)
    spread = Spread(links, column_ref, column, whole)
    stages = column_stages(links, up_ref, next_column, n)
    keep = links.local(up_ref, next_column.at[links.dp // 2])
    over_z = links.copy(down_ref.at[0], far_down, z_ways(n)[0])

    def next_stage(step):
        for copy, _ in stages[step]:
            copy.wait_recv()
        for copy, _ in stages[step + 1] if step + 1 < len(stages) else []:
            copy.start()

    @pl.when(i == 0)
    def _():
        links.greet([CORE, X, Y] + z_ways(n))
        for copy, _ in stages[0]:
            copy.start()
        spread.start()
        keep.start()

    def onward():
        next_stage(0)
        over_z.start()

    mine = pl.ds(pl.multiple_of(links.tensor * width, width), width)
    projected = dot_nn(x_ref[...], w_ref[:, : 3 * width])
    query = (projected[:, :width] + biases_ref[0:1, mine]).astype(BF16)
    key = projected[:, width : 2 * width].astype(BF16)
    value = (projected[:, 2 * width :] + biases_ref[1:2, mine]).astype(BF16)
    here = pl.ds(pl.multiple_of(i * bq, bq), bq)
    q_out[...] = query
    v_out[...] = value
    kt_out[...] = key.T
    k_ref[here, :] = key
    vt_ref[:, here] = value.T

    m_s[...] = jnp.full_like(m_s, NEGATIVE)
    l_s[...] = jnp.zeros_like(l_s)
    acc[...] = jnp.zeros_like(acc)
    hd = width // heads
    scaled = query * jnp.asarray(1.0 / math.sqrt(hd), BF16)
    q_heads = [head_only(scaled, h, hd) for h in range(heads)]

    def block(first, size, skip, mode):
        rows = pl.ds(pl.multiple_of(first, size), size)
        m_old = m_s[:, skip:]
        l_old = l_s[:, skip:]
        scores = [dot_nt(k_ref[rows, lanes_of(h, hd)[1]], q_heads[h][skip:]) for h in range(heads)]
        if mode != "none":
            bad = self_bad(b_ref, i * bq + skip, first, bq - skip, size, mode == "causal")
            scores = [jnp.where(bad, NEGATIVE, s) for s in scores]
        m_out, l_out, a_out = [], [], []
        for h in range(heads):
            part = slice(h * hd, (h + 1) * hd)
            m_new = jnp.maximum(m_old[h : h + 1, :], jnp.max(scores[h], axis=0, keepdims=True))
            shrink = jnp.exp(m_old[h : h + 1, :] - m_new)
            expos = jnp.exp(scores[h] - m_new)
            l_out.append(l_old[h : h + 1, :] * shrink + jnp.sum(expos, axis=0, keepdims=True))
            m_out.append(m_new)
            a_out.append(acc[part, skip:] * shrink + dot_nn(vt_ref[part, rows], expos.astype(BF16)))
        m_s[:, skip:] = jnp.concatenate(m_out, 0)
        l_s[:, skip:] = jnp.concatenate(l_out, 0)
        for h in range(heads):
            acc[h * hd : (h + 1) * hd, skip:] = a_out[h]

    over_keys(i, bq, safe, block, [(2, 0, onward), (3, 2, spread.middle), (4, 3, spread.last)])
    inverse = 1.0 / l_s[...]
    for h in range(heads):
        part = slice(h * hd, (h + 1) * hd)
        ot_ref[part, :] = (acc[part, :] * inverse[h : h + 1, :]).astype(BF16)
    lse_ref[...] = m_s[...] + jnp.log(l_s[...])
    terms_ref[...] = dot_nt(ot_ref[...].T, w_ref[:, 3 * width :]).astype(BF16)

    @pl.when(i == last)
    def _():
        for step in range(1, len(stages)):
            next_stage(step)
        over_z.wait()
        spread.end()
        for stage in stages:
            for copy, _ in stage:
                copy.wait_send()
        keep.wait()


def self_forward(bounds, x, w, biases, column, up, down, heads, safe):
    n, model = x.shape
    width = w.shape[1] // 4
    bq = 512
    dp = lax.axis_size("dp")
    m, r, c = column.shape
    by_rows_spec = pl.BlockSpec((bq, width), lambda i: (i, 0))
    by_columns_spec = pl.BlockSpec((width, bq), lambda i: (0, i))
    return pl.pallas_call(
        functools.partial(self_forward_kernel, heads=heads, safe=safe, n=dp),
        grid=(n // bq,),
        in_specs=[
            pl.BlockSpec(memory_space=pltpu.SMEM),
            pl.BlockSpec((bq, model), lambda i: (i, 0)),
            const((model, 4 * width)),
            const(biases.shape),
            ANY,
            const(up.shape),
            ANY,
        ],
        out_specs=[
            by_rows_spec,
            const((n, width)),
            by_rows_spec,
            by_columns_spec,
            by_columns_spec,
            pl.BlockSpec((heads, bq), lambda i: (0, i)),
            pl.BlockSpec((bq, model), lambda i: (i, 0)),
            ANY,
            ANY,
            ANY,
        ],
        out_shape=[
            jax.ShapeDtypeStruct((n, width), BF16),
            jax.ShapeDtypeStruct((n, width), BF16),
            jax.ShapeDtypeStruct((n, width), BF16),
            jax.ShapeDtypeStruct((width, n), BF16),
            jax.ShapeDtypeStruct((width, n), BF16),
            jax.ShapeDtypeStruct((heads, n), F32),
            jax.ShapeDtypeStruct((n, model), BF16),
            jax.ShapeDtypeStruct((4, m, 2, r, c), BF16),
            jax.ShapeDtypeStruct((m,) + up.shape, BF16),
            jax.ShapeDtypeStruct(down.shape[1:], BF16),
        ],
        scratch_shapes=[
            pltpu.VMEM((width, n), BF16),
            pltpu.VMEM((heads, bq), F32),
            pltpu.VMEM((heads, bq), F32),
            pltpu.VMEM((width, bq), F32),
            pltpu.VMEM((m, r, c), BF16),
        ]
        + link_scratch(9 + m, 3),
        compiler_params=pltpu.CompilerParams(
            vmem_limit_bytes=VMEM_LIMIT, collective_id=1, has_side_effects=True
        ),
        cost_estimate=pl.CostEstimate(
            flops=12 * n * n * width, bytes_accessed=8 * n * width, transcendentals=n * n * heads // 2
        ),
        name="self_forward",
    )(bounds, x, w, biases, column, up, down)


def after_self_kernel(
    terms_ref, rows_ref, biases_ref, norm_ref, column_ref, down_ref, from_z,
    after_out, second_out, whole_out, down_out, far_down, *scratch, n
):
    links = Links(*scratch[-3:])
    rows_sum = RowSum(links, terms_ref, scratch[:5])
    column = scratch[5]
    spread = SpreadZ(links, down_ref.at[0], from_z, scratch[6], down_out, n)
    over_z = links.copy(down_ref.at[1], far_down, z_ways(n)[0])
    y = links.dp % 2
    near_out, core_out = whole_out.at[0], whole_out.at[1]
    load = links.local(column_ref, column)
    own = links.local(column, near_out.at[:, y])
    over_y = links.copy(column, near_out.at[:, y], Y)
    over_core = [
        links.copy(column, core_out.at[:, y], CORE),
        links.copy(near_out.at[:, 1 - y], core_out.at[:, 1 - y], CORE),
    ]
    links.greet([CORE, X, Y] + z_ways(n))
    rows_sum.start()
    load.start()
    over_z.start()
    load.wait()
    over_y.start()
    own.start()
    rows_sum.middle()
    spread.start()
    over_core[0].start()
    over_y.wait_recv()
    over_core[1].start()
    rows_sum.end()
    spread.onward()

    def norm(rows):
        after = rows_ref[rows, :].astype(F32) + rows_sum.total(rows) + biases_ref[2:3, :]
        after_out[rows, :] = after
        xhat, _ = normalized(after)
        second_out[rows, :] = (xhat * norm_ref[1, 0:1, :] + norm_ref[1, 1:2, :]).astype(BF16)

    by_rows(after_out.shape[0], 64, norm)
    over_y.wait_send()
    spread.end()
    over_z.wait()
    for copy in [own] + over_core:
        copy.wait()


def sum_after_self(terms, rows, biases, norm, column, down, from_z):
    count, model = rows.shape
    m, r, c = column.shape
    vmem = pl.BlockSpec(memory_space=pltpu.VMEM)
    return pl.pallas_call(
        functools.partial(after_self_kernel, n=2 * m),
        in_specs=[ANY, vmem, vmem, vmem, ANY, ANY, ANY],
        out_specs=[vmem, vmem, ANY, ANY, ANY],
        out_shape=[
            jax.ShapeDtypeStruct((count, model), F32),
            jax.ShapeDtypeStruct((count, model), BF16),
            jax.ShapeDtypeStruct((2, m, 2, r, c), BF16),
            jax.ShapeDtypeStruct((2, m, 2, r, c), BF16),
            jax.ShapeDtypeStruct((2, r, c), BF16),
        ],
        scratch_shapes=row_sum_scratch(count, model)
        + [pltpu.VMEM((m, r, c), BF16), pltpu.VMEM((2, 2, r, c), BF16)]
        + link_scratch(7 + spread_z_copies(2 * m), 8),
        compiler_params=pltpu.CompilerParams(
            vmem_limit_bytes=VMEM_LIMIT, collective_id=8, has_side_effects=True
        ),
        cost_estimate=pl.CostEstimate(flops=0, bytes_accessed=100 * 2**20, transcendentals=0),
        name="sum_after_self",
    )(terms, rows, biases, norm, column, down, from_z)


def self_backward_kernel(
    b_ref, q_ref, k_ref, v_ref, kt_ref, w_ref, mt_ref, lse_ref, back_ref, rows_ref, above_ref, norm_ref,
    up_ref, down_ref, cross_ref, enc_ref,
    dq_ref, dk_ref, dv_ref, wide_out, grad_out, sums_ref, up_out, down_out, cross_out, enc_near, enc_far,
    dka, dva, dqa, wide, *scratch, bq, heads, safe, n
):
    s = pl.program_id(0)
    last = pl.num_programs(0) - 1
    links = Links(*scratch[-3:])
    member = links.tensor
    x, core = member // 2, member % 2
    second_core = (x == 1) & (core == 1)
    later = (s // 2 + 1) // 2
    i = s * (1 - x) + ((s + 3) * (1 - later) + (4 - s) * later) * x
    cross = GatherLast(links, cross_ref.at[0], cross_ref.at[1], scratch[:5])
    keep_cross = links.local(cross.column, cross_out)
    columns, slots = scratch[5:7], scratch[7:9]
    sums_z = [Collect(links, column, slot) for column, slot in zip(columns, slots)]
    load_z = [links.local(ref, column) for ref, column in zip((up_ref, down_ref), columns)]
    enc = RowSum(links, enc_ref, list(scratch[9:13]) + [None])
    stages = len(sums_z[0].stages)
    count = grad_out.shape[0]
    half = count // 2

    def place(distance, k=None):
        start = (member ^ distance) * count
        if k is None:
            return wide.at[pl.ds(pl.multiple_of(start, half), count)]
        return wide.at[pl.ds(pl.multiple_of(start + k * half, half), half)]

    over_x = [links.copy(place(0, k), place(0, k), X) for k in range(2)]
    over_core = links.copy(place(0), place(0), CORE)
    onward = [links.copy(place(2, k), place(2, k), CORE) for k in range(2)]
    keep_wide = links.local(wide, wide_out)

    def norm_back(k):
        def one(rows):
            rows = pl.ds(pl.multiple_of(k * half + rows.start, 64), 64)
            incoming = back_ref[rows, :]
            rows_grad, gain_terms = norm_rows_back(rows_ref[rows, :], incoming, norm_ref[1, 0:1, :])
            rows_grad = rows_grad + above_ref[rows, :]
            rounded = rows_grad.astype(BF16)
            grad_out[rows, :] = rows_grad
            wide[pl.ds(pl.multiple_of(member * count + rows.start, 64), 64), :] = rounded
            for row, terms in enumerate((gain_terms, incoming, rounded.astype(F32))):
                sums_ref[row : row + 1, :] += jnp.sum(terms, axis=0, keepdims=True)

        by_rows(half, 64, one)

    def arrive(k):
        over_x[k].wait_recv()
        onward[k].start()
        onward[k].wait_recv()

    @pl.when(s == 0)
    def _():
        links.greet([CORE, X, Y] + z_ways(n))
        for copy in load_z:
            copy.start()
        sums_ref[...] = jnp.zeros_like(sums_ref)
        for k in range(2):
            norm_back(k)
            pl.when(jnp.logical_not(second_core))(over_x[k].start)
        over_core.start()
        cross.start()
        enc.start()
        for copy, total in zip(load_z, sums_z):
            copy.wait()
            total.start(0)
        dka[...] = jnp.zeros_like(dka)
        dva[...] = jnp.zeros_like(dva)
        over_core.wait_recv()

    def next_z():
        for step in range(stages - 1):
            for total in sums_z:
                total.finish(step)
            for total in sums_z:
                total.start(step + 1)

    @pl.when((s == 2) & (x == 0) & (core == 0))
    def _():
        over_x[0].wait_recv()
        onward[0].start()

    @pl.when((s == 2) & (x == 0) & (core == 1))
    def _():
        onward[0].wait_recv()

    @pl.when((s == 2) & (x == 1))
    def _():
        arrive(0)
        arrive(1)

    @pl.when((s == 3) & (x == 0) & (core == 0))
    def _():
        over_x[1].wait_recv()
        onward[1].start()
        onward[0].wait_recv()

    @pl.when((s == 3) & (x == 0) & (core == 1))
    def _():
        over_x[0].wait_recv()
        onward[0].start()
        onward[1].wait_recv()

    @pl.when((s == 3) & (x == 0))
    def _():
        cross.second()
        cross.middle()
        next_z()

    @pl.when((s == 4) & (x == 0) & (core == 0))
    def _():
        onward[1].wait_recv()

    @pl.when((s == 4) & (x == 0) & (core == 1))
    def _():
        over_x[1].wait_recv()
        onward[1].start()

    @pl.when(s == 4)
    def _():
        keep_wide.start()

    def send_second():
        @pl.when(second_core)
        def _():
            for copy in over_x:
                copy.start()

    def z_sums():
        pl.when(x == 1)(next_z)

    def cross_sums():
        @pl.when(x == 1)
        def _():
            cross.second()
            cross.middle()

    width = k_ref.shape[1]
    hd = width // heads
    scale = 1.0 / math.sqrt(hd)
    here = pl.ds(pl.multiple_of(i * bq, bq), bq)
    grads = dot_nn(wide[here, :], w_ref[:, 3 * width :]).astype(BF16)
    products = grads.T.astype(F32) * mt_ref[:, here].astype(F32)
    inner = [jnp.sum(products[h * hd : (h + 1) * hd, :], axis=0, keepdims=True) for h in range(heads)]
    scaled = q_ref[here, :] * jnp.asarray(scale, BF16)
    q_heads = [head_only(scaled, h, hd) for h in range(heads)]
    d_heads = [head_only(grads, h, hd) for h in range(heads)]
    lse = lse_ref[:, here]
    dqa[...] = jnp.zeros_like(dqa)

    def block(first, size, skip, mode):
        rows = pl.ds(pl.multiple_of(first, size), size)
        scores = [dot_nt(k_ref[rows, lanes_of(h, hd)[1]], q_heads[h][skip:]) for h in range(heads)]
        dprobs = [dot_nt(v_ref[rows, lanes_of(h, hd)[1]], d_heads[h][skip:]) for h in range(heads)]
        if mode != "none":
            bad = self_bad(b_ref, i * bq + skip, first, bq - skip, size, mode == "causal")
            scores = [jnp.where(bad, NEGATIVE, s) for s in scores]
        dv_sums, dk_sums = {}, {}
        for h in range(heads):
            part = slice(h * hd, (h + 1) * hd)
            group, _ = lanes_of(h, hd)
            probs = jnp.exp(scores[h] - lse[h : h + 1, skip:])
            ds = (probs * (dprobs[h] - inner[h][:, skip:])).astype(BF16)
            add_group(dv_sums, group, dot_nn(probs.astype(BF16), d_heads[h][skip:]))
            add_group(dk_sums, group, dot_nn(ds, q_heads[h][skip:]))
            dqa[part, skip:] += dot_nn(kt_ref[part, rows], ds)
        for group in dv_sums:
            part = slice(group * LANES, (group + 1) * LANES)
            dva[rows, part] += dv_sums[group]
            dka[rows, part] += dk_sums[group]

    over_keys(i, bq, safe, block, [(3, 2, send_second), (4, 1, z_sums), (4, 3, cross_sums)])
    dq_ref[here, :] = (dqa[...] * scale).astype(BF16).T

    @pl.when(s == last)
    def _():
        dk_ref[...] = dka[...].astype(BF16)
        dv_ref[...] = dva[...].astype(BF16)
        cross.end()
        keep_cross.start()
        for total, out in zip(sums_z, (up_out, down_out)):
            total.finish(stages - 1)
            out[...] = total.column[total.z].astype(F32)
            total.drain()
        enc.core_end()

        def store(rows):
            enc_near[rows, :] = enc.near[rows, :].astype(F32) + enc.got_near[rows, :].astype(F32)
            enc_far[rows, :] = (enc.far[rows, :].astype(F32) + enc.got_far[rows, :].astype(F32)).astype(BF16)

        by_rows(enc_near.shape[0], 64, store)
        for copy in over_x + onward + [over_core]:
            copy.wait_send()
        keep_wide.wait()
        keep_cross.wait()


def self_backward(
    bounds, queries, keys, values, keys_t, w, mixed_t, lse, back, rows, above, norm,
    up_column, down_column, cross_sum, enc_terms, heads, safe
):
    n, width = queries.shape
    count, model = rows.shape
    dp = lax.axis_size("dp")
    m, r, c = up_column.shape
    cross_c = cross_sum.shape[4]
    enc_shape = (enc_terms.shape[0] // 4, enc_terms.shape[1])
    bq = 512
    return pl.pallas_call(
        functools.partial(self_backward_kernel, bq=bq, heads=heads, safe=safe, n=dp),
        grid=(n // bq,),
        in_specs=[
            pl.BlockSpec(memory_space=pltpu.SMEM),
            const((n, width)),
            const((n, width)),
            const((n, width)),
            const((width, n)),
            const((model, 4 * width)),
            const((width, n)),
            const((heads, n)),
            const((count, model)),
            const((count, model)),
            const((count, model)),
            const(norm.shape),
        ]
        + [ANY] * 4,
        out_specs=[const((n, width))] * 3
        + [ANY, const((count, model)), const((8, model)), const((r, c)), const((r, c)), ANY]
        + [const(enc_shape)] * 2,
        out_shape=[jax.ShapeDtypeStruct((n, width), BF16)] * 3
        + [
            jax.ShapeDtypeStruct((n, model), BF16),
            jax.ShapeDtypeStruct((count, model), F32),
            jax.ShapeDtypeStruct((8, model), F32),
            jax.ShapeDtypeStruct((r, c), F32),
            jax.ShapeDtypeStruct((r, c), F32),
            jax.ShapeDtypeStruct((m, r, cross_c), BF16),
            jax.ShapeDtypeStruct(enc_shape, F32),
            jax.ShapeDtypeStruct(enc_shape, BF16),
        ],
        scratch_shapes=[
            pltpu.VMEM((n, width), F32),
            pltpu.VMEM((n, width), F32),
            pltpu.VMEM((width, bq), F32),
            pltpu.VMEM((n, model), BF16),
        ]
        + [pltpu.VMEM((m, r, cross_c), BF16)] * 5
        + [pltpu.VMEM((m, r, c), BF16)] * 4
        + row_sum_scratch(*enc_shape)[:4]
        + link_scratch(11 + 2 * m, 8),
        compiler_params=pltpu.CompilerParams(
            vmem_limit_bytes=62 * 2**20, collective_id=5, has_side_effects=True
        ),
        cost_estimate=pl.CostEstimate(
            flops=24 * n * n * width, bytes_accessed=16 * n * width, transcendentals=n * n * heads // 2
        ),
        name="self_backward",
    )(
        bounds, queries, keys, values, keys_t, w, mixed_t, lse, back, rows, above, norm,
        up_column, down_column, cross_sum, enc_terms,
    )


def const(shape):
    return pl.BlockSpec(shape, lambda *_: (0,) * len(shape), pipeline_mode=pl.Buffered(1))


def normalized(rows):
    center = rows - jnp.mean(rows, axis=-1, keepdims=True)
    scale = lax.rsqrt(jnp.mean(center * center, axis=-1, keepdims=True) + EPSILON)
    return center * scale, scale


def norm_rows_back(rows, incoming, gain):
    xhat, scale = normalized(rows)
    e = incoming * gain
    inner = jnp.mean(e * xhat, axis=-1, keepdims=True)
    return scale * (e - jnp.mean(e, axis=-1, keepdims=True) - xhat * inner), incoming * xhat


def by_rows(count, step, body):
    def one(k, c):
        body(pl.ds(pl.multiple_of(k * step, step), step))
        return c

    lax.fori_loop(0, count // step, one, 0)


def cross_forward_kernel(
    len_ref, x_ref, enc_ref, w_ref, biases_ref, rows_ref, norm_ref, column_ref, down_ref, from_z,
    q_out, k_out, v_out, ot_ref, lse_ref, after_ref, third_ref, whole, down_out, hold, send_sems, recv_sems, local_sems, *, heads, n
):
    i = pl.program_id(0)
    last = pl.num_programs(0) - 1
    links = Links(send_sems, recv_sems, local_sems)
    spread = SpreadFar(links, column_ref, whole)
    pieces = len(spread.over_x)
    spread_z = SpreadZ(links, down_ref.at[1], from_z, hold, down_out, n)

    @pl.when(i == 0)
    def _():
        links.greet([CORE, X, Y] + z_ways(n))
        spread.start()
        spread_z.start()
        after_ref[...] = rows_ref[...] + biases_ref[5:6, :]

    def onward(*when):
        for step, k in when:
            pl.when(i == step)(functools.partial(spread.onward, k))

    onward((1, 0), (1, 1), (2, 4), (3, 6), (3, 7))

    width = q_out.shape[2]
    hd = width // heads
    mine = pl.ds(pl.multiple_of((links.tensor ^ i) * width, width), width)
    query = (dot_nn(x_ref[...], w_ref[0, :, :width]) + biases_ref[3:4, mine]).astype(BF16)
    key_value = dot_nn(enc_ref[...], w_ref[0, :, width : 3 * width])
    keys = key_value[:, :width].astype(BF16)
    values = (key_value[:, width:] + biases_ref[4:5, mine]).astype(BF16)
    q_out[0] = query
    k_out[0] = keys
    v_out[0] = values
    values_t = values.T
    scaled = query * jnp.asarray(1.0 / math.sqrt(hd), BF16)
    ok = lax.broadcasted_iota(jnp.int32, (keys.shape[0], 1), 0) < len_ref[0]
    scores = [dot_nt(keys[:, lanes_of(h, hd)[1]], head_only(scaled, h, hd)) for h in range(heads)]
    mixed = []
    for h in range(heads):
        part = slice(h * hd, (h + 1) * hd)
        s = jnp.where(ok, scores[h], NEGATIVE)
        largest = jnp.max(s, axis=0, keepdims=True)
        expos = jnp.exp(s - largest)
        total = jnp.sum(expos, axis=0, keepdims=True)
        mixed.append((dot_nn(values_t[part, :], expos.astype(BF16)) * (1.0 / total)).astype(BF16))
        ot_ref[0, part, :] = mixed[h]
        lse_ref[0, h : h + 1, :] = largest + jnp.log(total)
        if h == heads // 2 - 1:
            onward((1, 2), (1, 3), (2, 5))

            @pl.when(i == last)
            def _():
                for k in range(pieces // 2):
                    spread.last(k)
                spread_z.onward()
    after_ref[...] += dot_nt(jnp.concatenate(mixed, 0).T, w_ref[0, :, 3 * width :])

    @pl.when(i == last)
    def _():
        for k in range(pieces // 2, pieces):
            spread.last(k)

        def norm(rows):
            xhat, _ = normalized(after_ref[rows, :])
            third_ref[rows, :] = (xhat * norm_ref[2, 0:1, :] + norm_ref[2, 1:2, :]).astype(BF16)

        by_rows(after_ref.shape[0], 128, norm)
        spread_z.end()
        spread.end()


def cross_forward(lengths, x, encoder, weights, biases, rows, norm, column, down, from_z, heads):
    count, model = x.shape
    n = encoder.shape[0]
    parts, _, columns = weights.shape
    width = columns // 4
    m, r, c = column.shape

    def by_part(*shape):
        return pl.BlockSpec((1,) + shape, lambda i: (i,) + (0,) * len(shape))

    return pl.pallas_call(
        functools.partial(cross_forward_kernel, heads=heads, n=2 * m),
        grid=(parts,),
        in_specs=[
            pl.BlockSpec(memory_space=pltpu.SMEM),
            const((count, model)),
            const((n, model)),
            by_part(model, columns),
            const(biases.shape),
            const((count, model)),
            const(norm.shape),
            ANY,
            ANY,
            ANY,
        ],
        out_specs=[
            by_part(count, width),
            by_part(n, width),
            by_part(n, width),
            by_part(width, count),
            by_part(heads, count),
            const((count, model)),
            const((count, model)),
            ANY,
            ANY,
        ],
        out_shape=[
            jax.ShapeDtypeStruct((parts, count, width), BF16),
            jax.ShapeDtypeStruct((parts, n, width), BF16),
            jax.ShapeDtypeStruct((parts, n, width), BF16),
            jax.ShapeDtypeStruct((parts, width, count), BF16),
            jax.ShapeDtypeStruct((parts, heads, count), F32),
            jax.ShapeDtypeStruct((count, model), F32),
            jax.ShapeDtypeStruct((count, model), BF16),
            jax.ShapeDtypeStruct((2, m, 2, r, c), BF16),
            jax.ShapeDtypeStruct((2, m, 2, r, c), BF16),
        ],
        scratch_shapes=[pltpu.VMEM((2, 2, r, c), BF16)] + link_scratch(32 + spread_z_copies(2 * m), 4),
        compiler_params=pltpu.CompilerParams(
            vmem_limit_bytes=VMEM_LIMIT, collective_id=2, has_side_effects=True
        ),
        cost_estimate=pl.CostEstimate(
            flops=24 * parts * count * n * width,
            bytes_accessed=8 * parts * n * width,
            transcendentals=parts * count * n * heads,
        ),
        name="cross_forward",
    )(lengths, x, encoder, weights, biases, rows, norm, column, down, from_z)


def feed_forward_kernel(
    x_ref, dy_ref, near_up, near_down, far_up, far_down, b_ref, after_ref, biases_ref, norm_ref,
    out_ref, rows_out, low_out, sums_ref, gup_ref, gdown_ref, bias_ref, from_x, from_y,
    xt_ref, dyt_ref, back_ref, give, got, diagonal, loaded, load_sems, send_sems, recv_sems, local_sems, *, chunks
):
    s = pl.program_id(0)
    links = Links(send_sems, recv_sems, local_sems)
    turn = s // chunks
    chunk = s % chunks
    pair = turn // 2
    slot = pair * chunks + chunk
    theirs = turn % 2 == 0
    y = links.dp % 2
    m, r = diagonal.shape[1], diagonal.shape[2]
    low, high = pl.ds(0, m // 2), pl.ds(m // 2, m - m // 2)
    links.used = 2 * chunks
    across = [
        links.copy(diagonal.at[:, low], from_x, X),
        links.copy(diagonal.at[:, high], from_y, Y),
    ]
    to_core = pltpu.make_async_remote_copy(
        src_ref=give.at[chunk],
        dst_ref=got.at[slot],
        send_sem=send_sems.at[slot],
        recv_sem=recv_sems.at[slot],
        device_id=links.partner(CORE),
        device_id_type=pl.DeviceIdType.MESH,
    )

    size = loaded.shape[3]

    def fetch(step, act):
        block = 3 - step // chunks
        slot = step % 2
        first = (step % chunks) * size

        def both(*sources):
            for k, source in enumerate(sources):
                columns = pl.ds(pl.multiple_of(first, size), size)
                act(pltpu.make_async_copy(source.at[:, columns], loaded.at[slot, k], load_sems.at[slot, k]))

        @pl.when(block >= 2)
        def _():
            both(far_up.at[block - 2], far_down.at[block - 2])

        @pl.when(block < 2)
        def _():
            both(near_up.at[block], near_down.at[block])

    @pl.when(s == 0)
    def _():
        fetch(0, lambda copy: copy.start())
        links.greet([CORE, X, Y])
        out_ref[...] = after_ref[...] + biases_ref[6:7, :]
        back_ref[...] = jnp.zeros_like(back_ref)
        xt_ref[...] = x_ref[...].T
        dyt_ref[...] = dy_ref[...].T
        sums_ref[...] = jnp.zeros_like(sums_ref)

    fetch(s, lambda copy: copy.wait())

    @pl.when(s + 1 < pl.num_programs(0))
    def _():
        fetch(s + 1, lambda copy: copy.start())

    up_ref, down_ref = loaded.at[s % 2, 0], loaded.at[s % 2, 1]
    lines = size // LANES
    line = ((links.tensor ^ (3 - turn)) * chunks + chunk) * lines
    shift = jnp.concatenate([b_ref[pl.ds(line + k, 1), :] for k in range(lines)], axis=1)
    pre_act = dot_nn(x_ref[...], up_ref[...]) + shift
    hidden_grad = dot_nn(dy_ref[...], down_ref[...])
    normal_cdf = 0.5 * (1.0 + lax.erf(pre_act * (1.0 / math.sqrt(2.0))))
    density = jnp.exp(-0.5 * pre_act * pre_act) * (1.0 / math.sqrt(2.0 * math.pi))
    hidden = (pre_act * normal_cdf).astype(BF16)
    pre_grad = (hidden_grad * (normal_cdf + pre_act * density)).astype(BF16)
    bias_ref[0] = jnp.sum(pre_grad.astype(F32), axis=0, keepdims=True)

    @pl.when(turn % 2 == 1)
    def _():
        to_core.wait_send()

    give[chunk, 0] = dot_nn(xt_ref[...], pre_grad).astype(BF16)
    give[chunk, 1] = dot_nn(dyt_ref[...], hidden).astype(BF16)
    out_ref[...] += dot_nt(hidden, down_ref[...])
    back_ref[...] += dot_nt(pre_grad, up_ref[...])

    @pl.when(theirs)
    def _():
        to_core.start()

    @pl.when(jnp.logical_not(theirs))
    def _():
        to_core.wait_recv()
        gup_ref[0] = (give[chunk, 0].astype(F32) + got[slot, 0].astype(F32)).astype(BF16)
        gdown_ref[0] = (give[chunk, 1].astype(F32) + got[slot, 1].astype(F32)).astype(BF16)

    for k in range(chunks):

        @pl.when(s == chunks + k)
        def _():
            def keep(z, carry):
                rows = pl.ds(pl.multiple_of((2 * z + 1 - y) * r, r), r)
                size = gup_ref.shape[2]
                diagonal[0, z, :, k * size : (k + 1) * size] = gup_ref[0, rows, :]
                diagonal[1, z, :, k * size : (k + 1) * size] = gdown_ref[0, rows, :]
                return carry

            lax.fori_loop(0, m, keep, 0)
            if k == chunks - 1:
                for copy in across:
                    copy.start()

    @pl.when(s == pl.num_programs(0) - 1)
    def _():
        def norm_back(rows):
            third = back_ref[rows, :]
            upstream = dy_ref[rows, :].astype(F32)
            rows_grad, gain_terms = norm_rows_back(after_ref[rows, :], third, norm_ref[2, 0:1, :])
            rows_grad = rows_grad + upstream
            low = rows_grad.astype(BF16)
            rows_out[rows, :] = rows_grad
            low_out[rows, :] = low
            for k, terms in enumerate((gain_terms, third, low.astype(F32), upstream)):
                sums_ref[k : k + 1, :] += jnp.sum(terms, axis=0, keepdims=True)

        by_rows(x_ref.shape[0], 128, norm_back)
        for copy in across:
            copy.wait()


def feed_forward(x, dy, weights, bias, after, biases, norm):
    rows, width = x.shape
    hidden = weights[0].shape[2]
    size = min(512, hidden)
    chunks = hidden // size

    n = lax.axis_size("dp")
    m, r = n // 2, width // n

    def block(s):
        return 3 - s // chunks

    def placed(s):
        turn = s // chunks
        return (1 - turn // 2, 0, (s % chunks) * (turn % 2))

    rows_spec = const((rows, width))
    grad_spec = pl.BlockSpec((1, width, size), placed)
    bias_spec = pl.BlockSpec((1, 1, size), lambda s: (block(s), 0, s % chunks))
    return pl.pallas_call(
        functools.partial(feed_forward_kernel, chunks=chunks),
        grid=(4 * chunks,),
        in_specs=[
            rows_spec,
            rows_spec,
            ANY,
            ANY,
            ANY,
            ANY,
            const(bias.shape),
            rows_spec,
            const(biases.shape),
            const(norm.shape),
        ],
        out_specs=[rows_spec, rows_spec, rows_spec, const((8, width)), grad_spec, grad_spec, bias_spec, ANY, ANY],
        out_shape=[
            jax.ShapeDtypeStruct((rows, width), F32),
            jax.ShapeDtypeStruct((rows, width), F32),
            jax.ShapeDtypeStruct((rows, width), BF16),
            jax.ShapeDtypeStruct((8, width), F32),
            jax.ShapeDtypeStruct((2, width, hidden), BF16),
            jax.ShapeDtypeStruct((2, width, hidden), BF16),
            jax.ShapeDtypeStruct((4, 1, hidden), F32),
            jax.ShapeDtypeStruct((2, m // 2, r, hidden), BF16),
            jax.ShapeDtypeStruct((2, m - m // 2, r, hidden), BF16),
        ],
        scratch_shapes=[
            pltpu.VMEM((width, rows), BF16),
            pltpu.VMEM((width, rows), BF16),
            pltpu.VMEM((rows, width), F32),
            pltpu.VMEM((chunks, 2, width, size), BF16),
            pltpu.VMEM((2 * chunks, 2, width, size), BF16),
            pltpu.VMEM((2, m, r, hidden), BF16),
            pltpu.VMEM((2, 2, width, size), BF16),
            pltpu.SemaphoreType.DMA((2, 2)),
        ]
        + link_scratch(2 * chunks + 2, 1),
        compiler_params=pltpu.CompilerParams(
            vmem_limit_bytes=VMEM_LIMIT, collective_id=3, has_side_effects=True
        ),
        cost_estimate=pl.CostEstimate(
            flops=48 * rows * width * hidden, bytes_accessed=40 * 2**20, transcendentals=8 * rows * hidden
        ),
        name="feed_forward",
    )(x, dy, *weights, bias, after, biases, norm)


def cross_backward_kernel(
    len_ref, low_ref, x_ref, enc_ref, w_ref, q_ref, k_ref, v_ref, mt_ref, lse_ref, up_ref, down_ref, from_x, from_y,
    back_ref, enc_out, grad_ref, bq_ref, bv_ref, up_out, down_out,
    low_t, x_t, enc_t, enc_acc, give, got, *scratch, heads, bk
):
    i = pl.program_id(0)
    last = pl.num_programs(0) - 1
    links = Links(*scratch[14:])
    sums = [
        Gather(links, ref.at[0], ref.at[1], from_x.at[k], from_y.at[k], scratch[7 * k : 7 * k + 7])
        for k, ref in enumerate((up_ref, down_ref))
    ]
    leave = [links.local(g.column, out) for g, out in zip(sums, (up_out, down_out))]
    pair = i // 2
    to_core = pltpu.make_async_remote_copy(
        src_ref=give,
        dst_ref=got.at[pair],
        send_sem=links.send_sems.at[links.used + pair],
        recv_sem=links.recv_sems.at[links.used + pair],
        device_id=links.partner(CORE),
        device_id_type=pl.DeviceIdType.MESH,
    )

    @pl.when(i == 0)
    def _():
        links.greet([CORE, X, Y])
        for g in sums:
            g.start()
        low_t[...] = low_ref[...].T
        x_t[...] = x_ref[...].T
        enc_t[...] = enc_ref[...].T
        back_ref[...] = jnp.zeros_like(back_ref)
        enc_acc[...] = jnp.zeros_like(enc_acc)

    @pl.when(i == 1)
    def _():
        for g in sums:
            g.middle()

    rows, width = q_ref.shape[1:]
    n = k_ref.shape[1]
    hd = width // heads
    scale = 1.0 / math.sqrt(hd)
    w_query, w_keyval, w_out = w_ref.at[0, :, :width], w_ref.at[0, :, width : 3 * width], w_ref.at[0, :, 3 * width :]
    grads = dot_nn(low_ref[...], w_out[...]).astype(BF16)
    mixed_t = mt_ref[0]
    products = grads.T.astype(F32) * mixed_t.astype(F32)
    inner = [jnp.sum(products[h * hd : (h + 1) * hd, :], axis=0, keepdims=True) for h in range(heads)]
    scaled = q_ref[0] * jnp.asarray(scale, BF16)
    q_heads = [head_only(scaled, h, hd) for h in range(heads)]
    d_heads = [head_only(grads, h, hd) for h in range(heads)]
    lse = lse_ref[0]
    keys_t = k_ref[0].T
    dq = [None] * heads
    dkv = []
    for j in range(n // bk):
        span = slice(j * bk, (j + 1) * bk)
        ok = j * bk + lax.broadcasted_iota(jnp.int32, (bk, 1), 0) < len_ref[0]
        scores = [dot_nt(k_ref[0, span, lanes_of(h, hd)[1]], q_heads[h]) for h in range(heads)]
        dprobs = [dot_nt(v_ref[0, span, lanes_of(h, hd)[1]], d_heads[h]) for h in range(heads)]
        dv_sums, dk_sums = {}, {}
        for h in range(heads):
            part = slice(h * hd, (h + 1) * hd)
            group, _ = lanes_of(h, hd)
            probs = jnp.exp(jnp.where(ok, scores[h], NEGATIVE) - lse[h : h + 1, :])
            ds = (probs * (dprobs[h] - inner[h])).astype(BF16)
            add_group(dv_sums, group, dot_nn(probs.astype(BF16), d_heads[h]))
            add_group(dk_sums, group, dot_nn(ds, q_heads[h]))
            dq_h = dot_nn(keys_t[part, span], ds)
            dq[h] = dq_h if dq[h] is None else dq[h] + dq_h
        block = jnp.concatenate([sums_of[g].astype(BF16) for sums_of in (dk_sums, dv_sums) for g in sorted(sums_of)], 1)
        enc_acc[span, :] += dot_nt(block, w_keyval[...])
        dkv.append(block)
    dq = (jnp.concatenate(dq, 0) * scale).astype(BF16).T
    dkv = jnp.concatenate(dkv, 0)
    bq_ref[0] = jnp.sum(dq.astype(F32), axis=0, keepdims=True)
    bv_ref[0] = jnp.sum(dkv[:, width:].astype(F32), axis=0, keepdims=True)
    back_ref[...] += dot_nt(dq, w_query[...])

    @pl.when(i % 2 == 1)
    def _():
        to_core.wait_send()

    give[:, :width] = dot_nn(x_t[...], dq).astype(BF16)
    give[:, width : 3 * width] = dot_nn(enc_t[...], dkv).astype(BF16)
    give[:, 3 * width :] = dot_nn(low_t[...], mixed_t.T).astype(BF16)

    @pl.when(i % 2 == 0)
    def _():
        to_core.start()

    @pl.when(i % 2 == 1)
    def _():
        to_core.wait_recv()
        grad_ref[0] = (give[...].astype(F32) + got[pair].astype(F32)).astype(BF16)

    @pl.when(i == last)
    def _():
        enc_out[...] = enc_acc[...].astype(BF16)
        for g, copy in zip(sums, leave):
            g.end()
            copy.start()
        for copy in leave:
            copy.wait()


def cross_backward(
    lengths, low, x, encoder, weights, queries, keys, values, mixed_t, lse, up_sum, down_sum, from_x, from_y, heads
):
    count, model = x.shape
    n = encoder.shape[0]
    parts, _, columns = weights.shape
    width = columns // 4
    _, m, _, r, c = up_sum.shape

    def by_part(*shape):
        return pl.BlockSpec((1,) + shape, lambda i: (i ^ 1,) + (0,) * len(shape))

    return pl.pallas_call(
        functools.partial(cross_backward_kernel, heads=heads, bk=256),
        grid=(parts,),
        in_specs=[
            pl.BlockSpec(memory_space=pltpu.SMEM),
            const((count, model)),
            const((count, model)),
            const((n, model)),
            by_part(model, columns),
            by_part(count, width),
            by_part(n, width),
            by_part(n, width),
            by_part(width, count),
            by_part(heads, count),
            ANY,
            ANY,
            ANY,
            ANY,
        ],
        out_specs=[
            const((count, model)),
            const((n, model)),
            pl.BlockSpec((1, model, columns), lambda i: (i // 2, 0, 0), pipeline_mode=pl.Buffered(1)),
            by_part(1, width),
            by_part(1, width),
            ANY,
            ANY,
        ],
        out_shape=[
            jax.ShapeDtypeStruct((count, model), F32),
            jax.ShapeDtypeStruct((n, model), BF16),
            jax.ShapeDtypeStruct((2, model, columns), BF16),
            jax.ShapeDtypeStruct((parts, 1, width), F32),
            jax.ShapeDtypeStruct((parts, 1, width), F32),
            jax.ShapeDtypeStruct((m, r, c), BF16),
            jax.ShapeDtypeStruct((m, r, c), BF16),
        ],
        scratch_shapes=[
            pltpu.VMEM((model, count), BF16),
            pltpu.VMEM((model, count), BF16),
            pltpu.VMEM((model, n), BF16),
            pltpu.VMEM((n, model), F32),
            pltpu.VMEM((model, columns), BF16),
            pltpu.VMEM((2, model, columns), BF16),
        ]
        + gather_scratch(m, r, c) * 2
        + link_scratch(10, 12),
        compiler_params=pltpu.CompilerParams(
            vmem_limit_bytes=60 * 2**20, collective_id=4, has_side_effects=True
        ),
        cost_estimate=pl.CostEstimate(
            flops=48 * parts * count * n * width,
            bytes_accessed=16 * parts * n * width,
            transcendentals=parts * count * n * heads,
        ),
        name="cross_backward",
    )(lengths, low, x, encoder, weights, queries, keys, values, mixed_t, lse, up_sum, down_sum, from_x, from_y)


def on_device(
    block_in,
    encoder_out,
    out_grad,
    bounds,
    enc_lengths,
    norm_params,
    w_qkv,
    w_self_out,
    w_cross_q,
    w_cross_kv,
    w_cross_out,
    w_up,
    w_down,
    biases,
    up_bias,
):
    groups_count = lax.axis_size("dp")
    width = w_cross_q.shape[1]
    hidden_width = w_up.shape[1]
    heads = H // 4
    own_rows, model_width = block_in.shape
    w_rows = w_cross_q.shape[0]

    first_in, self_w, cross_column, down_square, enc_all = start_gather(
        block_in,
        norm_params,
        w_qkv,
        w_self_out,
        w_cross_q,
        w_cross_kv,
        w_cross_out,
        w_down,
        encoder_out,
    )
    self_w = self_w.reshape(model_width, 4 * width)

    self_safe = 1024
    queries, key_rows, value_rows, keys_t, self_mixed_t, self_lse, terms, cross_w, up_column, near_z = self_forward(
        bounds,
        first_in,
        self_w,
        biases,
        cross_column,
        w_up,
        down_square,
        heads,
        self_safe,
    )
    cross_w = cross_w.reshape(4, model_width, 4 * width)
    after_self, second_in, near_up, near_down, far_z = sum_after_self(
        terms, block_in, biases, norm_params, up_column, down_square, near_z
    )

    cross_q, cross_k, cross_v, cross_mixed_t, cross_lse, after_cross, third_in, far_up, far_down = cross_forward(
        enc_lengths,
        second_in,
        enc_all,
        cross_w,
        biases,
        after_self,
        norm_params,
        up_column,
        down_square,
        far_z,
        heads,
    )

    output, cross_rows_grad, cross_low, ffn_sums, up_sum, down_sum, bias_up_parts, from_x, from_y = feed_forward(
        third_in,
        out_grad,
        [w.reshape(2, model_width, hidden_width) for w in (near_up, near_down, far_up, far_down)],
        up_bias.reshape(-1, LANES),
        after_cross,
        biases,
        norm_params,
    )

    by_shard = (2, groups_count // 2, 2, w_rows, hidden_width)
    second_grad, enc_terms, cross_sum, bias_cq_parts, bias_cv_parts, up_column, down_column = cross_backward(
        enc_lengths,
        cross_low,
        second_in,
        enc_all,
        cross_w,
        cross_q,
        cross_k,
        cross_v,
        cross_mixed_t,
        cross_lse,
        up_sum.reshape(by_shard),
        down_sum.reshape(by_shard),
        from_x,
        from_y,
        heads,
    )
    cross_sum = cross_sum.reshape(2, groups_count // 2, 2, w_rows, 4 * width)

    (
        self_dq, self_dk, self_dv, self_wide, self_rows_grad, self_sums,
        summed_up, summed_down, cross_column, enc_near, enc_far,
    ) = self_backward(
        bounds,
        queries,
        key_rows,
        value_rows,
        keys_t,
        self_w,
        self_mixed_t,
        self_lse,
        second_grad,
        after_self,
        cross_rows_grad,
        norm_params,
        up_column,
        down_column,
        cross_sum,
        enc_terms,
        heads,
        self_safe,
    )
    input_grad, summed_self, vectors, summed_cross, encoder_grad = tail(
        self_dq,
        self_dk,
        self_dv,
        self_w,
        first_in,
        self_wide,
        self_mixed_t,
        block_in,
        self_rows_grad,
        cross_column,
        norm_params,
        self_sums,
        ffn_sums,
        bias_cq_parts,
        bias_cv_parts,
        bias_up_parts,
        enc_near,
        enc_far,
    )
    output, input_grad, encoder_grad, *weights_and_vectors = results(
        output, input_grad, encoder_grad, summed_self, summed_cross, summed_up, summed_down, vectors, 1.0 / groups_count
    )
    g_qkv, g_so, g_cq, g_ckv, g_co, g_up, g_down, g_norm, g_biases, g_shift = weights_and_vectors
    return (
        output,
        input_grad,
        encoder_grad,
        g_norm,
        g_qkv,
        g_so,
        g_cq,
        g_ckv,
        g_co,
        g_up,
        g_down,
        g_biases,
        g_shift.reshape(-1),
    )


def solution(mesh):
    rows = P(("dp", "tensor"), None)
    placed = (
        rows,
        rows,
        rows,
        P("dp", None),
        P("dp"),
        P(),
        P("dp", None, "tensor"),
        P("tensor", "dp"),
        P("dp", "tensor"),
        P("dp", None, "tensor"),
        P("tensor", "dp"),
        P("dp", "tensor"),
        P("tensor", "dp"),
        P(),
        P(),
    )
    return jax.shard_map(
        on_device,
        mesh=mesh,
        in_specs=placed,
        out_specs=(
            rows,
            rows,
            rows,
            P(),
            P("dp", None, "tensor"),
            P("tensor", "dp"),
            P("dp", "tensor"),
            P("dp", None, "tensor"),
            P("tensor", "dp"),
            P("dp", "tensor"),
            P("tensor", "dp"),
            P(),
            P(),
        ),
        check_vma=False,
    )
```

```python
import functools
import math

import jax
import jax.numpy as jnp
from jax import lax
from jax.experimental import pallas as pl
from jax.experimental.pallas import tpu as pltpu
from jax.sharding import PartitionSpec as P

H = 16
EPSILON = 1e-05
NEGATIVE = -1e30
F32 = jnp.float32
BF16 = jnp.bfloat16
VMEM_LIMIT = 56 * 2**20


def dot_nt(a, b):
    return lax.dot_general(a, b, (((1,), (1,)), ((), ())), preferred_element_type=F32)


def dot_nn(a, b):
    return lax.dot_general(a, b, (((1,), (0,)), ((), ())), preferred_element_type=F32)


def dot_tn(a, b):
    return lax.dot_general(a, b, (((0,), (0,)), ((), ())), preferred_element_type=F32)


LANES = 128


def lanes_of(h, size):
    group = h * size // LANES
    return group, slice(group * LANES, (group + 1) * LANES)


def head_only(x, h, size):
    group, part = lanes_of(h, size)
    lane = group * LANES + lax.broadcasted_iota(jnp.int32, (x.shape[0], LANES), 1)
    return jnp.where((lane >= h * size) & (lane < (h + 1) * size), x[:, part], jnp.zeros((), x.dtype))


def add_group(sums, group, value):
    sums[group] = value if group not in sums else sums[group] + value


def self_bad(b_ref, q_start, k_start, bq, bk, causal):
    qi = q_start + lax.broadcasted_iota(jnp.int32, (1, bq), 1)
    kj = k_start + lax.broadcasted_iota(jnp.int32, (bk, 1), 0)
    bad = (qi >= b_ref[0, 1]) & ((kj >= b_ref[0, 0]) & (kj < b_ref[0, 1]))
    if causal:
        bad = bad | (kj > qi)
    return bad


def over_keys(i, bq, safe, block, between=()):
    def visit(j, c):
        for at_i, at_j, action in between:
            pl.when((i == at_i) & (j == at_j))(action)

        @pl.when(j < safe // bq)
        def _():
            block(j * bq, bq, 0, "none")

        @pl.when(j >= safe // bq)
        def _():
            block(j * bq, bq, 0, "segment")

        return c

    lax.fori_loop(0, i, visit, 0)
    half = bq // 2
    block(i * bq, half, 0, "causal")
    block(i * bq + half, half, half, "causal")


CORE = ("tensor", 1)
X = ("tensor", 2)
Y = ("dp", 1)
ANY = pl.BlockSpec(memory_space=pl.ANY)


class Links:
    def __init__(self, send_sems, recv_sems, local_sems):
        self.dp = lax.axis_index("dp")
        self.tensor = lax.axis_index("tensor")
        self.send_sems, self.recv_sems, self.local_sems = send_sems, recv_sems, local_sems
        self.used = 0
        self.used_local = 0

    def partner(self, way):
        axis, distance = way
        if axis == "tensor":
            return (self.dp, self.tensor ^ distance)
        return (self.dp ^ distance, self.tensor)

    def greet(self, ways):
        barrier = pltpu.get_barrier_semaphore()
        for way in ways:
            pl.semaphore_signal(
                barrier, inc=1, device_id=self.partner(way), device_id_type=pl.DeviceIdType.MESH
            )
        pl.semaphore_wait(barrier, len(ways))

    def copy(self, source, target, way):
        k = self.used
        self.used += 1
        return pltpu.make_async_remote_copy(
            src_ref=source,
            dst_ref=target,
            send_sem=self.send_sems.at[k],
            recv_sem=self.recv_sems.at[k],
            device_id=self.partner(way),
            device_id_type=pl.DeviceIdType.MESH,
        )

    def local(self, source, target):
        k = self.used_local
        self.used_local += 1
        return pltpu.make_async_copy(source, target, self.local_sems.at[k])


def link_scratch(copies, local):
    return [
        pltpu.SemaphoreType.DMA((copies,)),
        pltpu.SemaphoreType.DMA((copies,)),
        pltpu.SemaphoreType.DMA((local,)),
    ]


def z_distances(n):
    found = []
    m = n // 2
    while m > 1:
        m //= 2
        found.append(m)
    return found


def z_ways(n):
    return [("dp", 2 * distance) for distance in z_distances(n)]


def column_stages(links, shard, column, n):
    z = links.dp // 2
    held = [z]
    stages = []
    for distance in z_distances(n):
        stages.append(
            [
                (
                    links.copy(shard if k == 0 else column.at[index], column.at[index], ("dp", 2 * distance)),
                    index ^ distance,
                )
                for k, index in enumerate(held)
            ]
        )
        held = held + [index ^ distance for index in held]
    return stages


class Spread:
    def __init__(self, links, source, column, whole):
        y = links.dp % 2
        half = column.shape[0] // 2
        low, high = pl.ds(0, half), pl.ds(half, half)
        near, near_core, far, far_core = (whole.at[k] for k in range(4))
        self.load = links.local(source, column)
        self.own = links.local(column, near.at[:, y])
        self.first = [
            links.copy(column, near.at[:, y], Y),
            links.copy(column, far.at[:, y], X),
        ]
        self.core = [links.copy(column, near_core.at[:, y], CORE)]
        self.second = [
            links.copy(near.at[low, 1 - y], far.at[low, 1 - y], X),
            links.copy(far.at[high, y], far.at[high, y], Y),
        ]
        self.core_second = [
            links.copy(near.at[:, 1 - y], near_core.at[:, 1 - y], CORE),
            links.copy(far.at[:, y], far_core.at[:, y], CORE),
        ]
        self.core_third = [links.copy(far.at[:, 1 - y], far_core.at[:, 1 - y], CORE)]

    def start(self):
        self.load.start()
        self.load.wait()
        for copy in self.first + self.core + [self.own]:
            copy.start()

    def middle(self):
        for copy in self.first:
            copy.wait_recv()
        for copy in self.second + self.core_second:
            copy.start()

    def last(self):
        for copy in self.second:
            copy.wait_recv()
        for copy in self.core_third:
            copy.start()

    def end(self):
        self.own.wait()
        for copy in self.first + self.second:
            copy.wait_send()
        for copy in self.core + self.core_second + self.core_third:
            copy.wait()


def add_to(total_ref, other_ref):
    def one(k, c):
        total_ref[k] = (total_ref[k].astype(F32) + other_ref[k].astype(F32)).astype(BF16)
        return c

    lax.fori_loop(0, total_ref.shape[0], one, 0)


class Gather:
    def __init__(self, links, near, far, from_x, from_y, buffers):
        y = links.dp % 2
        self.column, self.over_y, self.over_x, self.add_y, self.add_x, self.sum_y, self.sum_x = buffers
        m = self.column.shape[0]
        low, high = pl.ds(0, m // 2), pl.ds(m // 2, m - m // 2)
        self.loads = [
            links.local(near.at[low, 1 - y], self.over_y),
            links.local(far.at[high, y], self.over_x),
            links.local(from_x, self.add_y),
            links.local(from_y, self.add_x),
            links.local(near.at[:, y], self.column),
        ]
        self.first = [
            links.copy(far.at[low, y], self.sum_x.at[low], X),
            links.copy(near.at[high, 1 - y], self.sum_y.at[high], Y),
        ]
        self.second = [
            links.copy(self.over_x, self.sum_x.at[high], X),
            links.copy(self.over_y, self.sum_y.at[low], Y),
        ]

    def start(self):
        for copy in self.first + self.loads:
            copy.start()

    def middle(self):
        for copy in self.loads:
            copy.wait()
        add_to(self.over_x, self.add_x)
        add_to(self.over_y, self.add_y)
        for copy in self.second:
            copy.start()

    def end(self):
        for copy in self.first + self.second:
            copy.wait_recv()
        add_to(self.column, self.sum_y)
        add_to(self.column, self.sum_x)
        for copy in self.first + self.second:
            copy.wait_send()


def gather_scratch(m, r, c):
    whole = pltpu.VMEM((m, r, c), BF16)
    half = pltpu.VMEM((m // 2, r, c), BF16)
    return [whole] + [half] * 4 + [whole] * 2


class GatherLast:
    def __init__(self, links, near, far, buffers):
        y = links.dp % 2
        self.column, self.over_x, self.diagonal, self.sum_y, self.sum_x = buffers
        self.loads = [links.local(far.at[:, y], self.over_x), links.local(near.at[:, y], self.column)]
        self.first = links.copy(far.at[:, 1 - y], self.diagonal, Y)
        self.over_y = links.copy(near.at[:, 1 - y], self.sum_y, Y)
        self.along_x = links.copy(self.over_x, self.sum_x, X)

    def start(self):
        self.first.start()
        for copy in self.loads:
            copy.start()

    def second(self):
        self.first.wait_recv()
        self.over_y.start()

    def middle(self):
        for copy in self.loads:
            copy.wait()
        add_to(self.over_x, self.diagonal)
        self.along_x.start()

    def end(self):
        self.over_y.wait_recv()
        self.along_x.wait_recv()
        add_to(self.column, self.sum_y)
        add_to(self.column, self.sum_x)
        for copy in (self.first, self.over_y, self.along_x):
            copy.wait_send()


class Collect:
    def __init__(self, links, column, slots):
        z = links.dp // 2
        self.column, self.slots, self.z = column, slots, z
        m = column.shape[0]
        distances = z_distances(2 * m)[::-1]
        self.stages = []
        first = 0
        for step, distance in enumerate(distances):
            kept = [0]
            for other in distances[step + 1 :]:
                kept = kept + [k ^ other for k in kept]
            self.stages.append(
                [
                    (links.copy(column.at[z ^ distance ^ k], slots.at[first + i], ("dp", 2 * distance)), first + i, z ^ k)
                    for i, k in enumerate(kept)
                ]
            )
            first += len(kept)

    def start(self, step):
        for copy, _, _ in self.stages[step]:
            copy.start()

    def finish(self, step):
        for copy, slot, index in self.stages[step]:
            copy.wait_recv()
            self.column[index] = (self.column[index].astype(F32) + self.slots[slot].astype(F32)).astype(BF16)

    def drain(self):
        for stage in self.stages:
            for copy, _, _ in stage:
                copy.wait_send()


class Square:
    def __init__(self, links, shard, out):
        y = links.dp % 2
        c = shard.shape[1]
        low, high = pl.ds(0, c // 2), pl.ds(c // 2, c // 2)
        self.own = links.local(shard, out.at[0, y])
        self.first = [links.copy(shard, out.at[0, y], Y), links.copy(shard, out.at[1, y], X)]
        self.second = [
            links.copy(out.at[0, 1 - y, :, low], out.at[1, 1 - y, :, low], X),
            links.copy(out.at[1, y, :, high], out.at[1, y, :, high], Y),
        ]

    def start(self):
        for copy in self.first + [self.own]:
            copy.start()

    def middle(self):
        for copy in self.first:
            copy.wait_recv()
        for copy in self.second:
            copy.start()

    def end(self):
        for copy in self.first:
            copy.wait_send()
        for copy in self.second:
            copy.wait()
        self.own.wait()


class SpreadZ:
    def __init__(self, links, own, other, hold, whole, n):
        z = links.dp // 2
        distances = z_distances(n)
        there = z ^ distances[0]
        final, core = whole.at[0], whole.at[1]
        self.loads = [links.local(own, hold.at[0]), links.local(other, hold.at[1])]
        self.stores = [links.local(hold.at[0], final.at[z]), links.local(hold.at[1], final.at[there])]
        self.core = [links.copy(hold.at[0], core.at[z], CORE), links.copy(hold.at[1], core.at[there], CORE)]
        held = [(hold.at[0], z), (hold.at[1], there)]
        self.stages, self.core_stages = [], []
        for distance in distances[1:]:
            came = [index ^ distance for _, index in held]
            self.stages.append([links.copy(ref, final.at[index], ("dp", 2 * distance)) for ref, index in held])
            self.core_stages.append([links.copy(final.at[index], core.at[index], CORE) for index in came])
            held = held + [(final.at[index], index) for index in came]

    def start(self):
        for copy in self.loads:
            copy.start()
        for copy in self.loads:
            copy.wait()
        for copy in self.stages[0] + self.stores + self.core:
            copy.start()

    def onward(self):
        for step, (stage, core_stage) in enumerate(zip(self.stages, self.core_stages)):
            for copy, onward in zip(stage, core_stage):
                copy.wait_recv()
                onward.start()
            for copy in self.stages[step + 1] if step + 1 < len(self.stages) else []:
                copy.start()

    def end(self):
        for copy in self.stores + self.core:
            copy.wait()
        for stage, core_stage in zip(self.stages, self.core_stages):
            for copy in stage:
                copy.wait_send()
            for copy in core_stage:
                copy.wait()


def spread_z_copies(n):
    return 2 * n


class SpreadFar:
    def __init__(self, links, column, whole):
        y = links.dp % 2
        far, far_core = whole.at[0], whole.at[1]
        m, _, c = column.shape
        step = max(m // 4, 1)
        self.over_x, self.over_y, self.core_x, self.core_y = [], [], [], []
        for k in range(m // step):
            for h in range(2):
                z, part = pl.ds(k * step, step), pl.ds(h * (c // 2), c // 2)
                own = far.at[z, y, :, part]
                other = far.at[z, 1 - y, :, part]
                self.over_x.append(links.copy(column.at[z, :, part], own, X))
                self.over_y.append(links.copy(own, own, Y))
                self.core_x.append(links.copy(own, far_core.at[z, y, :, part], CORE))
                self.core_y.append(links.copy(other, far_core.at[z, 1 - y, :, part], CORE))

    def start(self):
        for copy in self.over_x:
            copy.start()

    def onward(self, k):
        self.over_x[k].wait_recv()
        self.over_y[k].start()
        self.core_x[k].start()

    def last(self, k):
        self.over_y[k].wait_recv()
        self.core_y[k].start()

    def end(self):
        for copy in self.over_x + self.over_y:
            copy.wait_send()
        for copy in self.core_x + self.core_y:
            copy.wait()


class RowSum:
    def __init__(self, links, terms, buffers):
        self.near, self.far, self.got_near, self.got_far, self.got_x = buffers
        count = self.near.shape[0]

        def rows(distance):
            start = pl.multiple_of((links.tensor ^ distance) * count, count)
            return terms.at[pl.ds(start, count)]

        self.loads = [links.local(rows(0), self.near), links.local(rows(2), self.far)]
        self.core = [links.copy(rows(3), self.got_far, CORE), links.copy(rows(1), self.got_near, CORE)]
        half = count // 2
        self.parts = [pl.ds(0, half), pl.ds(half, half)]
        self.over_x = []
        if self.got_x is not None:
            self.over_x = [links.copy(self.far.at[part], self.got_x.at[part], X) for part in self.parts]

    def start(self):
        for copy in self.loads[::-1] + self.core:
            copy.start()

    def middle(self):
        self.loads[1].wait()
        self.core[0].wait_recv()

        for part, copy in zip(self.parts, self.over_x):

            def add(rows, part=part):
                rows = pl.ds(pl.multiple_of(part.start + rows.start, 64), 64)
                self.far[rows, :] = (self.far[rows, :].astype(F32) + self.got_far[rows, :].astype(F32)).astype(BF16)

            by_rows(part.size, 64, add)
            copy.start()

    def core_end(self):
        for copy in self.loads + self.core:
            copy.wait()

    def end(self, k):
        if k == 0:
            self.loads[0].wait()
            self.core[1].wait_recv()
        self.over_x[k].wait_recv()

    def drain(self):
        for copy in self.core + self.over_x:
            copy.wait_send()

    def total(self, rows):
        return self.near[rows, :].astype(F32) + self.got_near[rows, :].astype(F32) + self.got_x[rows, :].astype(F32)


def row_sum_scratch(count, width):
    return [pltpu.VMEM((count, width), BF16)] * 5


class Everywhere:
    def __init__(self, links, held, slots, ways):
        self.held, self.slots = held, slots
        self.copies = [links.copy(held.at[k], slots.at[k], way) for k, way in enumerate(ways)]

    def start(self, step):
        self.copies[step].start()

    def finish(self, step):
        self.copies[step].wait()
        self.held[step + 1] = self.held[step] + self.slots[step]


class Direct:
    def __init__(self, links, value, slots_tensor, slots_dp, n):
        self.value = value
        self.slots = (slots_tensor, slots_dp)
        self.me = (links.tensor, links.dp)
        self.copies = []
        for slots, me, axis, size in zip(self.slots, self.me, ("tensor", "dp"), (4, n)):
            self.copies.append([links.copy(value, slots.at[me], (axis, d)) for d in range(1, size)])

    def start(self, phase):
        for copy in self.copies[phase]:
            copy.start()

    def finish(self, phase):
        slots = self.slots[phase]
        slots[self.me[phase]] = self.value[...]
        for copy in self.copies[phase]:
            copy.wait()
        total = slots[0]
        for k in range(1, slots.shape[0]):
            total = total + slots[k]
        self.value[...] = total


def direct_ways(n):
    return [("tensor", d) for d in range(1, 4)] + [("dp", d) for d in range(1, n)]


def everywhere_ways(n):
    return [CORE, X, Y] + z_ways(n)


def everywhere_scratch(k, c, n):
    steps = len(everywhere_ways(n))
    return [pltpu.VMEM((steps + 1, k, c), F32), pltpu.VMEM((steps, k, c), F32)]


def tail_kernel(
    dq_ref, dk_ref, dv_ref, w_ref, first_hbm, wide_hbm, mt_hbm, rows_hbm, grad_hbm, cross_hbm, norm_ref,
    self_ref, ffn_ref, cq_ref, cv_ref, up_ref, enc_near, enc_far,
    grad_out, weights_out, late_out, cross_out, enc_out, enc_got, give, acc, weights,
    first_ref, wide_ref, mt_ref, rows_ref, grad_ref, cross_ref, cross_slots, *scratch, n, step_rows
):
    links = Links(*scratch[-3:])
    loads = [
        links.local(source, target)
        for source, target in (
            (cross_hbm, cross_ref), (first_hbm, first_ref), (wide_hbm, wide_ref), (mt_hbm, mt_ref),
            (rows_hbm, rows_ref), (grad_hbm, grad_ref),
        )
    ]
    for copy in loads:
        copy.start()
    cross = Collect(links, cross_ref, cross_slots)
    member = links.tensor
    near, far, got_near, got_far, got_x = scratch[:5]
    columns, gots, slots = scratch[5:7], scratch[7:9], scratch[9:11]
    late_tensor, late_dp, sums, early_slots, held, compact = scratch[11:17]
    count, model = near.shape
    width = dq_ref.shape[1]
    y = links.dp % 2
    c = columns[0].shape[2]
    m, _, r, _ = weights.shape
    half = count // 2
    parts = [pl.ds(0, half), pl.ds(half, half)]
    core_far = links.copy(give.at[0], got_far, CORE)
    core_near = links.copy(give.at[1], got_near, CORE)
    over_x = [links.copy(far.at[part], got_x.at[part], X) for part in parts]
    over_y, collects = [], []
    for k, (column, got, slot) in enumerate(zip(columns, gots, slots)):
        over_y.append(links.copy(weights.at[:, 1 - y, :, pl.ds(k * c, c)], got, Y))
        collects.append(Collect(links, column, slot))
    stages = len(collects[0].stages)
    late = Direct(links, compact, late_tensor, late_dp, n)
    early = Everywhere(links, sums, early_slots, [CORE, Y, X] + z_ways(n))
    steps = len(early.copies)
    enc_x = links.copy(enc_far, enc_got, X)
    links.greet(direct_ways(n))
    enc_x.start()

    def terms(distance, target):
        base = (member ^ distance) * count

        def one(rows):
            there = pl.ds(pl.multiple_of(base + rows.start, 128), 128)
            total = dot_nt(dq_ref[there, :], w_ref[:, :width])
            total = total + dot_nt(dk_ref[there, :], w_ref[:, width : 2 * width])
            target[rows, :] = (total + dot_nt(dv_ref[there, :], w_ref[:, 2 * width : 3 * width])).astype(BF16)

        by_rows(count, 128, one)

    def packed(k):
        for block in range(2 * m):
            span = slice(block * r, (block + 1) * r)
            weights[block // 2, block % 2, :, k * c : (k + 1) * c] = acc[span, k * c : (k + 1) * c].astype(BF16)
        columns[k][...] = weights[:, y, :, k * c : (k + 1) * c]

    loads[0].wait()
    cross.start(0)
    acc[...] = jnp.zeros_like(acc)
    loads[1].wait()

    def products(refs, at):
        def one(rows):
            source = first_ref[rows, :].T
            for k, ref in enumerate(refs):
                acc[:, (at + k) * width : (at + k + 1) * width] += dot_nn(source, ref[rows, :])

        return one

    by_rows(dq_ref.shape[0], step_rows, products((dq_ref, dk_ref), 0))
    packed(0)
    over_y[0].start()
    terms(3, give.at[0])
    core_far.start()
    terms(2, far)
    core_far.wait_recv()
    for part, copy in zip(parts, over_x):

        def add(rows, part=part):
            there = pl.ds(pl.multiple_of(part.start + rows.start, 64), 64)
            far[there, :] = (far[there, :].astype(F32) + got_far[there, :].astype(F32)).astype(BF16)

        by_rows(half, 64, add)
        copy.start()
    for copy in loads[2:]:
        copy.wait()

    def products_out(rows):
        acc[:, 3 * width :] += dot_nn(wide_ref[rows, :].T, mt_ref[:, rows].T)

    held[...] = jnp.zeros_like(held)
    sums[0] = jnp.zeros(sums.shape[1:], F32)
    sums[0, 0:2, :] = self_ref[0:2, :]
    sums[0, 2:4, :] = ffn_ref[0:2, :]
    sums[0, 6:7, :] = self_ref[2:3, :]
    sums[0, 9:11, :] = ffn_ref[2:4, :]
    for distance in range(4):
        there = pl.ds(pl.multiple_of((member ^ distance) * width, width), width)
        sums[0, 7:8, there] = cq_ref[distance]
        sums[0, 8:9, there] = cv_ref[distance]
        sums[0, pl.ds(11 + (member ^ distance), 1), :] = up_ref[distance]
    here = pl.ds(pl.multiple_of(member * width, width), width)

    def column_sums(rows):
        sums[0, 4:5, here] += jnp.sum(dq_ref[rows, :].astype(F32), axis=0, keepdims=True)
        sums[0, 5:6, here] += jnp.sum(dv_ref[rows, :].astype(F32), axis=0, keepdims=True)

    by_rows(dq_ref.shape[0], step_rows, column_sums)
    early.start(0)

    def norm_back(part):
        def one(rows):
            rows = pl.ds(pl.multiple_of(part.start + rows.start, 64), 64)
            incoming = near[rows, :].astype(F32) + got_near[rows, :].astype(F32) + got_x[rows, :].astype(F32)
            rows_grad, gain_terms = norm_rows_back(rows_ref[rows, :].astype(F32), incoming, norm_ref[0, 0:1, :])
            grad_out[rows, :] = rows_grad + grad_ref[rows, :]
            held[0:1, :] += jnp.sum(gain_terms, axis=0, keepdims=True)
            held[1:2, :] += jnp.sum(incoming, axis=0, keepdims=True)

        by_rows(half, 64, one)

    def summed_y(k):
        over_y[k].wait_recv()
        add_to(columns[k], gots[k])
        collects[k].start(0)

    def next_z(k):
        for step in range(stages - 1):
            collects[k].finish(step)
            collects[k].start(step + 1)

    def last_z(k):
        collects[k].finish(stages - 1)
        weights_out[:, k * c : (k + 1) * c] = columns[k][collects[k].z].astype(F32)

    for step in range(stages - 1):
        cross.finish(step)
        cross.start(step + 1)
    by_rows(dq_ref.shape[0], step_rows, products((dv_ref,), 2))
    by_rows(dq_ref.shape[0], step_rows, products_out)
    packed(1)
    over_y[1].start()
    summed_y(0)
    early.finish(0)
    terms(1, give.at[1])
    core_near.start()
    terms(0, near)
    enc_x.wait_recv()
    enc_out[...] = enc_near[...] + enc_got[...].astype(F32)
    core_near.wait_recv()
    over_x[0].wait_recv()
    norm_back(parts[0])
    cross.finish(stages - 1)
    cross_out[...] = cross_ref[cross.z].astype(F32)
    next_z(0)
    summed_y(1)
    early.start(1)
    next_z(1)
    early.finish(1)
    over_x[1].wait_recv()
    norm_back(parts[1])
    lines = model // LANES
    for k in range(2 * lines):
        compact[k : k + 1, :] = held[k // lines : k // lines + 1, k % lines * LANES : (k % lines + 1) * LANES]
    late.start(0)
    early.start(2)
    last_z(0)
    early.finish(2)
    late.finish(0)
    late.start(1)
    early.start(3)
    last_z(1)
    early.finish(3)
    for step in range(4, steps):
        early.start(step)
        early.finish(step)
    late.finish(1)
    late_out[2:, :] = sums[steps]
    for k in range(2 * lines):
        late_out[k // lines : k // lines + 1, k % lines * LANES : (k % lines + 1) * LANES] = compact[k : k + 1, :]
    for copy in over_x + over_y + [core_near, core_far]:
        copy.wait_send()
    for collect in collects + [cross]:
        collect.drain()
    enc_x.wait_send()


def tail(
    dq, dk, dv, w, first, wide, mixed_t, rows, grad, cross_column, norm, self_sums, ffn_sums, cq_sums, cv_sums, up_sums,
    enc_near, enc_far,
):
    n = lax.axis_size("dp")
    count, model = rows.shape
    width = dq.shape[1]
    m, r, c = n // 2, model // n, 4 * width
    vectors = (16, model)
    vmem = pl.BlockSpec(memory_space=pltpu.VMEM)
    part = pltpu.VMEM((m, r, c // 2), BF16)
    return pl.pallas_call(
        functools.partial(tail_kernel, n=n, step_rows=512),
        in_specs=[vmem] * 4 + [ANY] * 6 + [vmem] * 8,
        out_specs=[vmem] * 5,
        out_shape=[
            jax.ShapeDtypeStruct((count, model), F32),
            jax.ShapeDtypeStruct((r, c), F32),
            jax.ShapeDtypeStruct((vectors[0] + 2, model), F32),
            jax.ShapeDtypeStruct(cross_column.shape[1:], F32),
            jax.ShapeDtypeStruct(enc_near.shape, F32),
        ],
        scratch_shapes=[
            pltpu.VMEM(enc_far.shape, BF16),
            pltpu.VMEM((2, count, model), BF16),
            pltpu.VMEM((model, c), F32),
            pltpu.VMEM((m, 2, r, c), BF16),
        ]
        + [pltpu.VMEM(v.shape, v.dtype) for v in (first, wide, mixed_t, rows, grad, cross_column, cross_column)]
        + row_sum_scratch(count, model)
        + [part] * 6
        + [pltpu.VMEM((size, 2 * model // LANES, LANES), F32) for size in (4, n)]
        + everywhere_scratch(*vectors, n)
        + [pltpu.VMEM((8, model), F32), pltpu.VMEM((2 * model // LANES, LANES), F32)]
        + link_scratch(7 + 3 * m + len(everywhere_ways(n)) + len(direct_ways(n)), 6),
        compiler_params=pltpu.CompilerParams(
            vmem_limit_bytes=VMEM_LIMIT, collective_id=7, has_side_effects=True
        ),
        cost_estimate=pl.CostEstimate(flops=0, bytes_accessed=100 * 2**20, transcendentals=0),
        name="tail",
    )(
        dq, dk, dv, w, first, wide, mixed_t, rows, grad, cross_column, norm,
        self_sums, ffn_sums, cq_sums, cv_sums, up_sums, enc_near, enc_far,
    )


def results_kernel(
    output_ref, grad_ref, enc_ref, self_ref, cross_ref, up_ref, down_ref, vectors_ref,
    output_out, grad_out, enc_out, qkv_out, so_out, cq_out, ckv_out, co_out, up_out, down_out,
    norm_out, biases_out, shift_out, *, scale
):
    output_out[...] = output_ref[...]
    grad_out[...] = grad_ref[...]
    enc_out[...] = enc_ref[...]
    width = cq_out.shape[1]

    @pl.when(pl.program_id(0) == 0)
    def _():
        for k in range(3):
            qkv_out[:, k, :] = self_ref[:, k * width : (k + 1) * width] * scale
        so_out[...] = (self_ref[:, 3 * width :] * scale).T
        cq_out[...] = cross_ref[:, :width] * scale
        for k in range(2):
            ckv_out[:, k, :] = cross_ref[:, (k + 1) * width : (k + 2) * width] * scale
        co_out[...] = (cross_ref[:, 3 * width :] * scale).T
        up_out[...] = up_ref[...] * scale
        down_out[...] = (down_ref[...] * scale).T
        vectors = vectors_ref[...] * scale
        for k in range(3):
            norm_out[k] = vectors[2 * k : 2 * k + 2, :]
        biases_out[...] = vectors[6:13, :]
        lines = vectors.shape[1] // LANES
        for k in range(shift_out.shape[0]):
            part = slice(k % lines * LANES, (k % lines + 1) * LANES)
            shift_out[k : k + 1, :] = vectors[13 + k // lines : 14 + k // lines, part]


def results(output, grad, encoder, self_w, cross_w, up, down, vectors, scale):
    r, c = self_w.shape
    width = c // 4
    steps = 2

    def rows(value):
        return pl.BlockSpec((value.shape[0] // steps, value.shape[1]), lambda i: (i, 0))

    shapes = [(r, 3, width), (width, r), (r, width), (r, 2, width), (width, r), up.shape, down.shape[::-1]]
    shapes += [(3, 2, output.shape[1]), (7, output.shape[1]), (4 * up.shape[1] // LANES, LANES)]
    return pl.pallas_call(
        functools.partial(results_kernel, scale=scale),
        grid=(steps,),
        in_specs=[rows(output), rows(grad), rows(encoder)] + [const(v.shape) for v in (self_w, cross_w, up, down, vectors)],
        out_specs=[rows(output), rows(grad), rows(encoder)] + [const(shape) for shape in shapes],
        out_shape=[jax.ShapeDtypeStruct(v.shape, F32) for v in (output, grad, encoder)]
        + [jax.ShapeDtypeStruct(shape, F32) for shape in shapes],
        compiler_params=pltpu.CompilerParams(vmem_limit_bytes=VMEM_LIMIT),
        cost_estimate=pl.CostEstimate(flops=0, bytes_accessed=20 * 2**20, transcendentals=0),
        name="results",
    )(output, grad, encoder, self_w, cross_w, up, down, vectors)


def start_kernel(
    in_ref, norm_ref, qkv_ref, so_ref, cq_ref, ckv_ref, co_ref, down_ref, enc_ref,
    rows_out, self_out, cross_out, down_out, enc_out, rows_ref, self_ref, cross_ref, shard_ref, send_sems, recv_sems, local_sems, *, n
):
    links = Links(send_sems, recv_sems, local_sems)
    member, z, y = links.tensor, links.dp // 2, links.dp % 2
    count = rows_ref.shape[0]
    half = count // 2
    parts = [pl.ds(0, half), pl.ds(half, half)]

    def place(distance):
        return rows_out.at[pl.ds(pl.multiple_of((member ^ distance) * count, count), count)]

    over_x = [links.copy(rows_ref.at[part], place(0).at[part], X) for part in parts]
    over_core = [links.copy(rows_ref, place(0), CORE)]
    over_core += [links.copy(place(2).at[part], place(2).at[part], CORE) for part in parts]
    self_stages = column_stages(links, self_ref, self_out.at[:, y], n)
    cross_stages = column_stages(links, cross_ref, cross_out, n)
    over_y = [links.copy(self_ref, self_out.at[z, y], Y)]
    local = [
        links.local(rows_ref, place(0)),
        links.local(self_ref, self_out.at[z, y]),
        links.local(cross_ref, cross_out.at[z]),
    ]
    width = cq_ref.shape[1]
    for k in range(3):
        self_ref[:, k * width : (k + 1) * width] = qkv_ref[:, k, :]
    self_ref[:, 3 * width :] = so_ref[...].T
    cross_ref[:, :width] = cq_ref[...]
    for k in range(2):
        cross_ref[:, (k + 1) * width : (k + 2) * width] = ckv_ref[:, k, :]
    cross_ref[:, 3 * width :] = co_ref[...].T
    shard_ref[...] = down_ref[...].T
    square = Square(links, shard_ref, down_out)
    enc_count = enc_ref.shape[0]

    def enc_place(distance):
        return enc_out.at[pl.ds(pl.multiple_of((member ^ distance) * enc_count, enc_count), enc_count)]

    enc_x = links.copy(enc_ref, enc_place(0), X)
    enc_core = [links.copy(enc_ref, enc_place(0), CORE), links.copy(enc_place(2), enc_place(2), CORE)]
    local.append(links.local(enc_ref, enc_place(0)))
    links.greet([CORE, X, Y] + z_ways(n))
    for copy in over_y + local[1:]:
        copy.start()
    for copy, _ in self_stages[0]:
        copy.start()
    for part, copy in zip(parts, over_x):

        def norm(rows, part=part):
            rows = pl.ds(pl.multiple_of(part.start + rows.start, 64), 64)
            xhat, _ = normalized(in_ref[rows, :].astype(F32))
            rows_ref[rows, :] = (xhat * norm_ref[0, 0:1, :] + norm_ref[0, 1:2, :]).astype(BF16)

        by_rows(half, 64, norm)
        copy.start()
    for copy in local[:1] + over_core[:1]:
        copy.start()
    square.start()
    enc_x.start()
    enc_core[0].start()
    for self_stage in self_stages:
        if self_stage is not self_stages[0]:
            for copy, _ in self_stage:
                copy.start()
        for copy, index in self_stage:
            copy.wait_recv()
            onward = links.copy(self_out.at[index, y], self_out.at[index, y], Y)
            onward.start()
            over_y.append(onward)
        if self_stage is self_stages[0]:
            for copy, _ in cross_stages[0]:
                copy.start()
    for cross_stage, later in zip(cross_stages, cross_stages[1:] + [[]]):
        for copy, _ in cross_stage:
            copy.wait_recv()
        for copy, _ in later:
            copy.start()
    for copy, onward in zip(over_x, over_core[1:]):
        copy.wait_recv()
        onward.start()
    square.middle()
    enc_x.wait_recv()
    enc_core[1].start()
    enc_x.wait_send()
    square.end()
    for copy in local + over_y + over_core + enc_core:
        copy.wait()
    for copy in over_x:
        copy.wait_send()
    for stage in self_stages + cross_stages:
        for copy, _ in stage:
            copy.wait_send()


def start_gather(rows, norm, qkv, self_out, cross_q, cross_kv, cross_out, down, encoder):
    n = lax.axis_size("dp")
    r, c = cross_q.shape[0], 4 * cross_q.shape[1]
    return pl.pallas_call(
        functools.partial(start_kernel, n=n),
        in_specs=[pl.BlockSpec(memory_space=pltpu.VMEM)] * 9,
        out_specs=[ANY] * 5,
        out_shape=[
            jax.ShapeDtypeStruct((4 * rows.shape[0], rows.shape[1]), BF16),
            jax.ShapeDtypeStruct((n // 2, 2, r, c), BF16),
            jax.ShapeDtypeStruct((n // 2, r, c), BF16),
            jax.ShapeDtypeStruct((2, 2, r, down.shape[0]), BF16),
            jax.ShapeDtypeStruct((4 * encoder.shape[0], encoder.shape[1]), BF16),
        ],
        scratch_shapes=[pltpu.VMEM(rows.shape, BF16)]
        + [pltpu.VMEM((r, c), BF16)] * 2
        + [pltpu.VMEM((r, down.shape[0]), BF16)]
        + link_scratch(2 * n + 15, 5),
        compiler_params=pltpu.CompilerParams(
            vmem_limit_bytes=VMEM_LIMIT, collective_id=0, has_side_effects=True
        ),
        cost_estimate=pl.CostEstimate(flops=0, bytes_accessed=100 * 2**20, transcendentals=0),
        name="start_gather",
    )(rows, norm, qkv, self_out, cross_q, cross_kv, cross_out, down, encoder)


def self_forward_kernel(
    b_ref, x_ref, w_ref, biases_ref, column_ref, up_ref, down_ref,
    q_out, k_ref, v_out, kt_out, ot_ref, lse_ref, terms_ref, whole, next_column, far_down,
    vt_ref, m_s, l_s, acc, column, send_sems, recv_sems, local_sems, *, heads, safe, n
):
    i = pl.program_id(0)
    last = pl.num_programs(0) - 1
    bq, width = q_out.shape
    links = Links(send_sems, recv_sems, local_sems)
    spread = Spread(links, column_ref, column, whole)
    stages = column_stages(links, up_ref, next_column, n)
    keep = links.local(up_ref, next_column.at[links.dp // 2])
    over_z = links.copy(down_ref.at[0], far_down, z_ways(n)[0])

    def next_stage(step):
        for copy, _ in stages[step]:
            copy.wait_recv()
        for copy, _ in stages[step + 1] if step + 1 < len(stages) else []:
            copy.start()

    @pl.when(i == 0)
    def _():
        links.greet([CORE, X, Y] + z_ways(n))
        for copy, _ in stages[0]:
            copy.start()
        spread.start()
        keep.start()

    def onward():
        next_stage(0)
        over_z.start()

    mine = pl.ds(pl.multiple_of(links.tensor * width, width), width)
    projected = dot_nn(x_ref[...], w_ref[:, : 3 * width])
    query = (projected[:, :width] + biases_ref[0:1, mine]).astype(BF16)
    key = projected[:, width : 2 * width].astype(BF16)
    value = (projected[:, 2 * width :] + biases_ref[1:2, mine]).astype(BF16)
    here = pl.ds(pl.multiple_of(i * bq, bq), bq)
    q_out[...] = query
    v_out[...] = value
    kt_out[...] = key.T
    k_ref[here, :] = key
    vt_ref[:, here] = value.T

    m_s[...] = jnp.full_like(m_s, NEGATIVE)
    l_s[...] = jnp.zeros_like(l_s)
    acc[...] = jnp.zeros_like(acc)
    hd = width // heads
    scaled = query * jnp.asarray(1.0 / math.sqrt(hd), BF16)
    q_heads = [head_only(scaled, h, hd) for h in range(heads)]

    def block(first, size, skip, mode):
        rows = pl.ds(pl.multiple_of(first, size), size)
        m_old = m_s[:, skip:]
        l_old = l_s[:, skip:]
        scores = [dot_nt(k_ref[rows, lanes_of(h, hd)[1]], q_heads[h][skip:]) for h in range(heads)]
        if mode != "none":
            bad = self_bad(b_ref, i * bq + skip, first, bq - skip, size, mode == "causal")
            scores = [jnp.where(bad, NEGATIVE, s) for s in scores]
        m_out, l_out, a_out = [], [], []
        for h in range(heads):
            part = slice(h * hd, (h + 1) * hd)
            m_new = jnp.maximum(m_old[h : h + 1, :], jnp.max(scores[h], axis=0, keepdims=True))
            shrink = jnp.exp(m_old[h : h + 1, :] - m_new)
            expos = jnp.exp(scores[h] - m_new)
            l_out.append(l_old[h : h + 1, :] * shrink + jnp.sum(expos, axis=0, keepdims=True))
            m_out.append(m_new)
            a_out.append(acc[part, skip:] * shrink + dot_nn(vt_ref[part, rows], expos.astype(BF16)))
        m_s[:, skip:] = jnp.concatenate(m_out, 0)
        l_s[:, skip:] = jnp.concatenate(l_out, 0)
        for h in range(heads):
            acc[h * hd : (h + 1) * hd, skip:] = a_out[h]

    over_keys(i, bq, safe, block, [(2, 0, onward), (3, 2, spread.middle), (4, 3, spread.last)])
    inverse = 1.0 / l_s[...]
    for h in range(heads):
        part = slice(h * hd, (h + 1) * hd)
        ot_ref[part, :] = (acc[part, :] * inverse[h : h + 1, :]).astype(BF16)
    lse_ref[...] = m_s[...] + jnp.log(l_s[...])
    terms_ref[...] = dot_nt(ot_ref[...].T, w_ref[:, 3 * width :]).astype(BF16)

    @pl.when(i == last)
    def _():
        for step in range(1, len(stages)):
            next_stage(step)
        over_z.wait()
        spread.end()
        for stage in stages:
            for copy, _ in stage:
                copy.wait_send()
        keep.wait()


def self_forward(bounds, x, w, biases, column, up, down, heads, safe):
    n, model = x.shape
    width = w.shape[1] // 4
    bq = 512
    dp = lax.axis_size("dp")
    m, r, c = column.shape
    by_rows_spec = pl.BlockSpec((bq, width), lambda i: (i, 0))
    by_columns_spec = pl.BlockSpec((width, bq), lambda i: (0, i))
    return pl.pallas_call(
        functools.partial(self_forward_kernel, heads=heads, safe=safe, n=dp),
        grid=(n // bq,),
        in_specs=[
            pl.BlockSpec(memory_space=pltpu.SMEM),
            pl.BlockSpec((bq, model), lambda i: (i, 0)),
            const((model, 4 * width)),
            const(biases.shape),
            ANY,
            const(up.shape),
            ANY,
        ],
        out_specs=[
            by_rows_spec,
            const((n, width)),
            by_rows_spec,
            by_columns_spec,
            by_columns_spec,
            pl.BlockSpec((heads, bq), lambda i: (0, i)),
            pl.BlockSpec((bq, model), lambda i: (i, 0)),
            ANY,
            ANY,
            ANY,
        ],
        out_shape=[
            jax.ShapeDtypeStruct((n, width), BF16),
            jax.ShapeDtypeStruct((n, width), BF16),
            jax.ShapeDtypeStruct((n, width), BF16),
            jax.ShapeDtypeStruct((width, n), BF16),
            jax.ShapeDtypeStruct((width, n), BF16),
            jax.ShapeDtypeStruct((heads, n), F32),
            jax.ShapeDtypeStruct((n, model), BF16),
            jax.ShapeDtypeStruct((4, m, 2, r, c), BF16),
            jax.ShapeDtypeStruct((m,) + up.shape, BF16),
            jax.ShapeDtypeStruct(down.shape[1:], BF16),
        ],
        scratch_shapes=[
            pltpu.VMEM((width, n), BF16),
            pltpu.VMEM((heads, bq), F32),
            pltpu.VMEM((heads, bq), F32),
            pltpu.VMEM((width, bq), F32),
            pltpu.VMEM((m, r, c), BF16),
        ]
        + link_scratch(9 + m, 3),
        compiler_params=pltpu.CompilerParams(
            vmem_limit_bytes=VMEM_LIMIT, collective_id=1, has_side_effects=True
        ),
        cost_estimate=pl.CostEstimate(
            flops=12 * n * n * width, bytes_accessed=8 * n * width, transcendentals=n * n * heads // 2
        ),
        name="self_forward",
    )(bounds, x, w, biases, column, up, down)


def after_self_kernel(
    terms_ref, rows_ref, biases_ref, norm_ref, column_ref, down_ref, from_z,
    after_out, second_out, whole_out, down_out, far_down, *scratch, n
):
    links = Links(*scratch[-3:])
    rows_sum = RowSum(links, terms_ref, scratch[:5])
    column = scratch[5]
    spread = SpreadZ(links, down_ref.at[0], from_z, scratch[6], down_out, n)
    over_z = links.copy(down_ref.at[1], far_down, z_ways(n)[0])
    y = links.dp % 2
    near_out, core_out = whole_out.at[0], whole_out.at[1]
    load = links.local(column_ref, column)
    own = links.local(column, near_out.at[:, y])
    over_y = links.copy(column, near_out.at[:, y], Y)
    over_core = [
        links.copy(column, core_out.at[:, y], CORE),
        links.copy(near_out.at[:, 1 - y], core_out.at[:, 1 - y], CORE),
    ]
    links.greet([CORE, X, Y] + z_ways(n))
    rows_sum.start()
    load.start()
    over_z.start()
    load.wait()
    over_y.start()
    own.start()
    rows_sum.middle()
    spread.start()
    over_core[0].start()
    over_y.wait_recv()
    over_core[1].start()

    def norm(part):
        def one(rows):
            rows = pl.ds(pl.multiple_of(part.start + rows.start, 64), 64)
            after = rows_ref[rows, :].astype(F32) + rows_sum.total(rows) + biases_ref[2:3, :]
            after_out[rows, :] = after
            xhat, _ = normalized(after)
            second_out[rows, :] = (xhat * norm_ref[1, 0:1, :] + norm_ref[1, 1:2, :]).astype(BF16)

        by_rows(part.size, 64, one)

    for k, part in enumerate(rows_sum.parts):
        rows_sum.end(k)
        if k == 1:
            spread.onward()
        norm(part)
    rows_sum.drain()
    over_y.wait_send()
    spread.end()
    over_z.wait()
    for copy in [own] + over_core:
        copy.wait()


def sum_after_self(terms, rows, biases, norm, column, down, from_z):
    count, model = rows.shape
    m, r, c = column.shape
    vmem = pl.BlockSpec(memory_space=pltpu.VMEM)
    return pl.pallas_call(
        functools.partial(after_self_kernel, n=2 * m),
        in_specs=[ANY, vmem, vmem, vmem, ANY, ANY, ANY],
        out_specs=[vmem, vmem, ANY, ANY, ANY],
        out_shape=[
            jax.ShapeDtypeStruct((count, model), F32),
            jax.ShapeDtypeStruct((count, model), BF16),
            jax.ShapeDtypeStruct((2, m, 2, r, c), BF16),
            jax.ShapeDtypeStruct((2, m, 2, r, c), BF16),
            jax.ShapeDtypeStruct((2, r, c), BF16),
        ],
        scratch_shapes=row_sum_scratch(count, model)
        + [pltpu.VMEM((m, r, c), BF16), pltpu.VMEM((2, 2, r, c), BF16)]
        + link_scratch(8 + spread_z_copies(2 * m), 8),
        compiler_params=pltpu.CompilerParams(
            vmem_limit_bytes=VMEM_LIMIT, collective_id=8, has_side_effects=True
        ),
        cost_estimate=pl.CostEstimate(flops=0, bytes_accessed=100 * 2**20, transcendentals=0),
        name="sum_after_self",
    )(terms, rows, biases, norm, column, down, from_z)


def self_backward_kernel(
    b_ref, q_ref, k_ref, v_ref, kt_ref, w_ref, mt_ref, lse_ref, back_ref, rows_ref, above_ref, norm_ref,
    up_ref, down_ref, cross_ref, enc_ref,
    dq_ref, dk_ref, dv_ref, wide_out, grad_out, sums_ref, up_out, down_out, cross_out, enc_near, enc_far,
    dka, dva, dqa, wide, *scratch, bq, heads, safe, n
):
    s = pl.program_id(0)
    last = pl.num_programs(0) - 1
    links = Links(*scratch[-3:])
    member = links.tensor
    x, core = member // 2, member % 2
    second_core = (x == 1) & (core == 1)
    later = (s // 2 + 1) // 2
    i = s * (1 - x) + ((s + 3) * (1 - later) + (4 - s) * later) * x
    cross = GatherLast(links, cross_ref.at[0], cross_ref.at[1], scratch[:5])
    keep_cross = links.local(cross.column, cross_out)
    columns, slots = scratch[5:7], scratch[7:9]
    sums_z = [Collect(links, column, slot) for column, slot in zip(columns, slots)]
    load_z = [links.local(ref, column) for ref, column in zip((up_ref, down_ref), columns)]
    enc = RowSum(links, enc_ref, list(scratch[9:13]) + [None])
    stages = len(sums_z[0].stages)
    count = grad_out.shape[0]
    half = count // 2

    def place(distance, k=None):
        start = (member ^ distance) * count
        if k is None:
            return wide.at[pl.ds(pl.multiple_of(start, half), count)]
        return wide.at[pl.ds(pl.multiple_of(start + k * half, half), half)]

    over_x = [links.copy(place(0, k), place(0, k), X) for k in range(2)]
    over_core = links.copy(place(0), place(0), CORE)
    onward = [links.copy(place(2, k), place(2, k), CORE) for k in range(2)]
    keep_wide = links.local(wide, wide_out)

    def norm_back(k):
        def one(rows):
            rows = pl.ds(pl.multiple_of(k * half + rows.start, 64), 64)
            incoming = back_ref[rows, :]
            rows_grad, gain_terms = norm_rows_back(rows_ref[rows, :], incoming, norm_ref[1, 0:1, :])
            rows_grad = rows_grad + above_ref[rows, :]
            rounded = rows_grad.astype(BF16)
            grad_out[rows, :] = rows_grad
            wide[pl.ds(pl.multiple_of(member * count + rows.start, 64), 64), :] = rounded
            for row, terms in enumerate((gain_terms, incoming, rounded.astype(F32))):
                sums_ref[row : row + 1, :] += jnp.sum(terms, axis=0, keepdims=True)

        by_rows(half, 64, one)

    def arrive(k):
        over_x[k].wait_recv()
        onward[k].start()
        onward[k].wait_recv()

    @pl.when(s == 0)
    def _():
        links.greet([CORE, X, Y] + z_ways(n))
        for copy in load_z:
            copy.start()
        sums_ref[...] = jnp.zeros_like(sums_ref)
        for k in range(2):
            norm_back(k)
            pl.when(jnp.logical_not(second_core))(over_x[k].start)
        over_core.start()
        cross.start()
        enc.start()
        for copy, total in zip(load_z, sums_z):
            copy.wait()
            total.start(0)
        dka[...] = jnp.zeros_like(dka)
        dva[...] = jnp.zeros_like(dva)
        over_core.wait_recv()

    def next_z():
        for step in range(stages - 1):
            for total in sums_z:
                total.finish(step)
            for total in sums_z:
                total.start(step + 1)

    @pl.when((s == 2) & (x == 0) & (core == 0))
    def _():
        over_x[0].wait_recv()
        onward[0].start()

    @pl.when((s == 2) & (x == 0) & (core == 1))
    def _():
        onward[0].wait_recv()

    @pl.when((s == 2) & (x == 1))
    def _():
        arrive(0)
        arrive(1)

    @pl.when((s == 3) & (x == 0) & (core == 0))
    def _():
        over_x[1].wait_recv()
        onward[1].start()
        onward[0].wait_recv()

    @pl.when((s == 3) & (x == 0) & (core == 1))
    def _():
        over_x[0].wait_recv()
        onward[0].start()
        onward[1].wait_recv()

    @pl.when((s == 3) & (x == 0))
    def _():
        cross.second()
        cross.middle()
        next_z()

    @pl.when((s == 4) & (x == 0) & (core == 0))
    def _():
        onward[1].wait_recv()

    @pl.when((s == 4) & (x == 0) & (core == 1))
    def _():
        over_x[1].wait_recv()
        onward[1].start()

    @pl.when(s == 4)
    def _():
        keep_wide.start()

    def send_second():
        @pl.when(second_core)
        def _():
            for copy in over_x:
                copy.start()

    def z_sums():
        pl.when(x == 1)(next_z)

    def cross_sums():
        @pl.when(x == 1)
        def _():
            cross.second()
            cross.middle()

    width = k_ref.shape[1]
    hd = width // heads
    scale = 1.0 / math.sqrt(hd)
    here = pl.ds(pl.multiple_of(i * bq, bq), bq)
    grads = dot_nn(wide[here, :], w_ref[:, 3 * width :]).astype(BF16)
    products = grads.T.astype(F32) * mt_ref[:, here].astype(F32)
    inner = [jnp.sum(products[h * hd : (h + 1) * hd, :], axis=0, keepdims=True) for h in range(heads)]
    scaled = q_ref[here, :] * jnp.asarray(scale, BF16)
    q_heads = [head_only(scaled, h, hd) for h in range(heads)]
    d_heads = [head_only(grads, h, hd) for h in range(heads)]
    lse = lse_ref[:, here]
    dqa[...] = jnp.zeros_like(dqa)

    def block(first, size, skip, mode):
        rows = pl.ds(pl.multiple_of(first, size), size)
        scores = [dot_nt(k_ref[rows, lanes_of(h, hd)[1]], q_heads[h][skip:]) for h in range(heads)]
        dprobs = [dot_nt(v_ref[rows, lanes_of(h, hd)[1]], d_heads[h][skip:]) for h in range(heads)]
        if mode != "none":
            bad = self_bad(b_ref, i * bq + skip, first, bq - skip, size, mode == "causal")
            scores = [jnp.where(bad, NEGATIVE, s) for s in scores]
        dv_sums, dk_sums = {}, {}
        for h in range(heads):
            part = slice(h * hd, (h + 1) * hd)
            group, _ = lanes_of(h, hd)
            probs = jnp.exp(scores[h] - lse[h : h + 1, skip:])
            ds = (probs * (dprobs[h] - inner[h][:, skip:])).astype(BF16)
            add_group(dv_sums, group, dot_nn(probs.astype(BF16), d_heads[h][skip:]))
            add_group(dk_sums, group, dot_nn(ds, q_heads[h][skip:]))
            dqa[part, skip:] += dot_nn(kt_ref[part, rows], ds)
        for group in dv_sums:
            part = slice(group * LANES, (group + 1) * LANES)
            dva[rows, part] += dv_sums[group]
            dka[rows, part] += dk_sums[group]

    over_keys(i, bq, safe, block, [(3, 2, send_second), (4, 1, z_sums), (4, 3, cross_sums)])
    dq_ref[here, :] = (dqa[...] * scale).astype(BF16).T

    @pl.when(s == last)
    def _():
        dk_ref[...] = dka[...].astype(BF16)
        dv_ref[...] = dva[...].astype(BF16)
        cross.end()
        keep_cross.start()
        for total, out in zip(sums_z, (up_out, down_out)):
            total.finish(stages - 1)
            out[...] = total.column[total.z].astype(F32)
            total.drain()
        enc.core_end()

        def store(rows):
            enc_near[rows, :] = enc.near[rows, :].astype(F32) + enc.got_near[rows, :].astype(F32)
            enc_far[rows, :] = (enc.far[rows, :].astype(F32) + enc.got_far[rows, :].astype(F32)).astype(BF16)

        by_rows(enc_near.shape[0], 64, store)
        for copy in over_x + onward + [over_core]:
            copy.wait_send()
        keep_wide.wait()
        keep_cross.wait()


def self_backward(
    bounds, queries, keys, values, keys_t, w, mixed_t, lse, back, rows, above, norm,
    up_column, down_column, cross_sum, enc_terms, heads, safe
):
    n, width = queries.shape
    count, model = rows.shape
    dp = lax.axis_size("dp")
    m, r, c = up_column.shape
    cross_c = cross_sum.shape[4]
    enc_shape = (enc_terms.shape[0] // 4, enc_terms.shape[1])
    bq = 512
    return pl.pallas_call(
        functools.partial(self_backward_kernel, bq=bq, heads=heads, safe=safe, n=dp),
        grid=(n // bq,),
        in_specs=[
            pl.BlockSpec(memory_space=pltpu.SMEM),
            const((n, width)),
            const((n, width)),
            const((n, width)),
            const((width, n)),
            const((model, 4 * width)),
            const((width, n)),
            const((heads, n)),
            const((count, model)),
            const((count, model)),
            const((count, model)),
            const(norm.shape),
        ]
        + [ANY] * 4,
        out_specs=[const((n, width))] * 3
        + [ANY, const((count, model)), const((8, model)), const((r, c)), const((r, c)), ANY]
        + [const(enc_shape)] * 2,
        out_shape=[jax.ShapeDtypeStruct((n, width), BF16)] * 3
        + [
            jax.ShapeDtypeStruct((n, model), BF16),
            jax.ShapeDtypeStruct((count, model), F32),
            jax.ShapeDtypeStruct((8, model), F32),
            jax.ShapeDtypeStruct((r, c), F32),
            jax.ShapeDtypeStruct((r, c), F32),
            jax.ShapeDtypeStruct((m, r, cross_c), BF16),
            jax.ShapeDtypeStruct(enc_shape, F32),
            jax.ShapeDtypeStruct(enc_shape, BF16),
        ],
        scratch_shapes=[
            pltpu.VMEM((n, width), F32),
            pltpu.VMEM((n, width), F32),
            pltpu.VMEM((width, bq), F32),
            pltpu.VMEM((n, model), BF16),
        ]
        + [pltpu.VMEM((m, r, cross_c), BF16)] * 5
        + [pltpu.VMEM((m, r, c), BF16)] * 4
        + row_sum_scratch(*enc_shape)[:4]
        + link_scratch(11 + 2 * m, 8),
        compiler_params=pltpu.CompilerParams(
            vmem_limit_bytes=62 * 2**20, collective_id=5, has_side_effects=True
        ),
        cost_estimate=pl.CostEstimate(
            flops=24 * n * n * width, bytes_accessed=16 * n * width, transcendentals=n * n * heads // 2
        ),
        name="self_backward",
    )(
        bounds, queries, keys, values, keys_t, w, mixed_t, lse, back, rows, above, norm,
        up_column, down_column, cross_sum, enc_terms,
    )


def const(shape):
    return pl.BlockSpec(shape, lambda *_: (0,) * len(shape), pipeline_mode=pl.Buffered(1))


def normalized(rows):
    center = rows - jnp.mean(rows, axis=-1, keepdims=True)
    scale = lax.rsqrt(jnp.mean(center * center, axis=-1, keepdims=True) + EPSILON)
    return center * scale, scale


def norm_rows_back(rows, incoming, gain):
    xhat, scale = normalized(rows)
    e = incoming * gain
    inner = jnp.mean(e * xhat, axis=-1, keepdims=True)
    return scale * (e - jnp.mean(e, axis=-1, keepdims=True) - xhat * inner), incoming * xhat


def by_rows(count, step, body):
    def one(k, c):
        body(pl.ds(pl.multiple_of(k * step, step), step))
        return c

    lax.fori_loop(0, count // step, one, 0)


def cross_forward_kernel(
    len_ref, x_ref, enc_ref, w_ref, biases_ref, rows_ref, norm_ref, column_ref, down_ref, from_z,
    q_out, k_out, v_out, ot_ref, lse_ref, after_ref, third_ref, whole, down_out, hold, send_sems, recv_sems, local_sems, *, heads, n
):
    i = pl.program_id(0)
    last = pl.num_programs(0) - 1
    links = Links(send_sems, recv_sems, local_sems)
    spread = SpreadFar(links, column_ref, whole)
    pieces = len(spread.over_x)
    spread_z = SpreadZ(links, down_ref.at[1], from_z, hold, down_out, n)

    @pl.when(i == 0)
    def _():
        links.greet([CORE, X, Y] + z_ways(n))
        spread.start()
        spread_z.start()
        after_ref[...] = rows_ref[...] + biases_ref[5:6, :]

    def onward(*when):
        for step, k in when:
            pl.when(i == step)(functools.partial(spread.onward, k))

    onward((1, 0), (1, 1), (2, 4), (3, 6), (3, 7))

    width = q_out.shape[2]
    hd = width // heads
    mine = pl.ds(pl.multiple_of((links.tensor ^ i) * width, width), width)
    query = (dot_nn(x_ref[...], w_ref[0, :, :width]) + biases_ref[3:4, mine]).astype(BF16)
    key_value = dot_nn(enc_ref[...], w_ref[0, :, width : 3 * width])
    keys = key_value[:, :width].astype(BF16)
    values = (key_value[:, width:] + biases_ref[4:5, mine]).astype(BF16)
    q_out[0] = query
    k_out[0] = keys
    v_out[0] = values
    values_t = values.T
    scaled = query * jnp.asarray(1.0 / math.sqrt(hd), BF16)
    ok = lax.broadcasted_iota(jnp.int32, (keys.shape[0], 1), 0) < len_ref[0]
    scores = [dot_nt(keys[:, lanes_of(h, hd)[1]], head_only(scaled, h, hd)) for h in range(heads)]
    mixed = []
    for h in range(heads):
        part = slice(h * hd, (h + 1) * hd)
        s = jnp.where(ok, scores[h], NEGATIVE)
        largest = jnp.max(s, axis=0, keepdims=True)
        expos = jnp.exp(s - largest)
        total = jnp.sum(expos, axis=0, keepdims=True)
        mixed.append((dot_nn(values_t[part, :], expos.astype(BF16)) * (1.0 / total)).astype(BF16))
        ot_ref[0, part, :] = mixed[h]
        lse_ref[0, h : h + 1, :] = largest + jnp.log(total)
        if h == heads // 2 - 1:
            onward((1, 2), (1, 3), (2, 5))

            @pl.when(i == last)
            def _():
                for k in range(pieces // 2):
                    spread.last(k)
                spread_z.onward()
    after_ref[...] += dot_nt(jnp.concatenate(mixed, 0).T, w_ref[0, :, 3 * width :])

    @pl.when(i == last)
    def _():
        for k in range(pieces // 2, pieces):
            spread.last(k)

        def norm(rows):
            xhat, _ = normalized(after_ref[rows, :])
            third_ref[rows, :] = (xhat * norm_ref[2, 0:1, :] + norm_ref[2, 1:2, :]).astype(BF16)

        by_rows(after_ref.shape[0], 128, norm)
        spread_z.end()
        spread.end()


def cross_forward(lengths, x, encoder, weights, biases, rows, norm, column, down, from_z, heads):
    count, model = x.shape
    n = encoder.shape[0]
    parts, _, columns = weights.shape
    width = columns // 4
    m, r, c = column.shape

    def by_part(*shape):
        return pl.BlockSpec((1,) + shape, lambda i: (i,) + (0,) * len(shape))

    return pl.pallas_call(
        functools.partial(cross_forward_kernel, heads=heads, n=2 * m),
        grid=(parts,),
        in_specs=[
            pl.BlockSpec(memory_space=pltpu.SMEM),
            const((count, model)),
            const((n, model)),
            by_part(model, columns),
            const(biases.shape),
            const((count, model)),
            const(norm.shape),
            ANY,
            ANY,
            ANY,
        ],
        out_specs=[
            by_part(count, width),
            by_part(n, width),
            by_part(n, width),
            by_part(width, count),
            by_part(heads, count),
            const((count, model)),
            const((count, model)),
            ANY,
            ANY,
        ],
        out_shape=[
            jax.ShapeDtypeStruct((parts, count, width), BF16),
            jax.ShapeDtypeStruct((parts, n, width), BF16),
            jax.ShapeDtypeStruct((parts, n, width), BF16),
            jax.ShapeDtypeStruct((parts, width, count), BF16),
            jax.ShapeDtypeStruct((parts, heads, count), F32),
            jax.ShapeDtypeStruct((count, model), F32),
            jax.ShapeDtypeStruct((count, model), BF16),
            jax.ShapeDtypeStruct((2, m, 2, r, c), BF16),
            jax.ShapeDtypeStruct((2, m, 2, r, c), BF16),
        ],
        scratch_shapes=[pltpu.VMEM((2, 2, r, c), BF16)] + link_scratch(32 + spread_z_copies(2 * m), 4),
        compiler_params=pltpu.CompilerParams(
            vmem_limit_bytes=VMEM_LIMIT, collective_id=2, has_side_effects=True
        ),
        cost_estimate=pl.CostEstimate(
            flops=24 * parts * count * n * width,
            bytes_accessed=8 * parts * n * width,
            transcendentals=parts * count * n * heads,
        ),
        name="cross_forward",
    )(lengths, x, encoder, weights, biases, rows, norm, column, down, from_z)


def feed_forward_kernel(
    x_ref, dy_ref, near_up, near_down, far_up, far_down, b_ref, after_ref, biases_ref, norm_ref,
    out_ref, rows_out, low_out, sums_ref, gup_ref, gdown_ref, bias_ref, from_x, from_y,
    xt_ref, dyt_ref, back_ref, give, got, diagonal, loaded, load_sems, send_sems, recv_sems, local_sems, *, chunks
):
    s = pl.program_id(0)
    links = Links(send_sems, recv_sems, local_sems)
    turn = s // chunks
    chunk = s % chunks
    pair = turn // 2
    slot = pair * chunks + chunk
    theirs = turn % 2 == 0
    y = links.dp % 2
    m, r = diagonal.shape[1], diagonal.shape[2]
    low, high = pl.ds(0, m // 2), pl.ds(m // 2, m - m // 2)
    links.used = 2 * chunks
    across = [
        links.copy(diagonal.at[:, low], from_x, X),
        links.copy(diagonal.at[:, high], from_y, Y),
    ]
    to_core = pltpu.make_async_remote_copy(
        src_ref=give.at[chunk],
        dst_ref=got.at[slot],
        send_sem=send_sems.at[slot],
        recv_sem=recv_sems.at[slot],
        device_id=links.partner(CORE),
        device_id_type=pl.DeviceIdType.MESH,
    )

    size = loaded.shape[3]

    def fetch(step, act):
        block = 3 - step // chunks
        slot = step % 2
        first = (step % chunks) * size

        def both(*sources):
            for k, source in enumerate(sources):
                columns = pl.ds(pl.multiple_of(first, size), size)
                act(pltpu.make_async_copy(source.at[:, columns], loaded.at[slot, k], load_sems.at[slot, k]))

        @pl.when(block >= 2)
        def _():
            both(far_up.at[block - 2], far_down.at[block - 2])

        @pl.when(block < 2)
        def _():
            both(near_up.at[block], near_down.at[block])

    @pl.when(s == 0)
    def _():
        fetch(0, lambda copy: copy.start())
        links.greet([CORE, X, Y])
        out_ref[...] = after_ref[...] + biases_ref[6:7, :]
        back_ref[...] = jnp.zeros_like(back_ref)
        xt_ref[...] = x_ref[...].T
        dyt_ref[...] = dy_ref[...].T
        sums_ref[...] = jnp.zeros_like(sums_ref)

    fetch(s, lambda copy: copy.wait())

    @pl.when(s + 1 < pl.num_programs(0))
    def _():
        fetch(s + 1, lambda copy: copy.start())

    up_ref, down_ref = loaded.at[s % 2, 0], loaded.at[s % 2, 1]
    lines = size // LANES
    line = ((links.tensor ^ (3 - turn)) * chunks + chunk) * lines
    shift = jnp.concatenate([b_ref[pl.ds(line + k, 1), :] for k in range(lines)], axis=1)
    pre_act = dot_nn(x_ref[...], up_ref[...]) + shift
    hidden_grad = dot_nn(dy_ref[...], down_ref[...])
    normal_cdf = 0.5 * (1.0 + lax.erf(pre_act * (1.0 / math.sqrt(2.0))))
    density = jnp.exp(-0.5 * pre_act * pre_act) * (1.0 / math.sqrt(2.0 * math.pi))
    hidden = (pre_act * normal_cdf).astype(BF16)
    pre_grad = (hidden_grad * (normal_cdf + pre_act * density)).astype(BF16)
    bias_ref[0] = jnp.sum(pre_grad.astype(F32), axis=0, keepdims=True)

    @pl.when(turn % 2 == 1)
    def _():
        to_core.wait_send()

    give[chunk, 0] = dot_nn(xt_ref[...], pre_grad).astype(BF16)
    give[chunk, 1] = dot_nn(dyt_ref[...], hidden).astype(BF16)
    out_ref[...] += dot_nt(hidden, down_ref[...])
    back_ref[...] += dot_nt(pre_grad, up_ref[...])

    @pl.when(theirs)
    def _():
        to_core.start()

    @pl.when(jnp.logical_not(theirs))
    def _():
        to_core.wait_recv()
        gup_ref[0] = (give[chunk, 0].astype(F32) + got[slot, 0].astype(F32)).astype(BF16)
        gdown_ref[0] = (give[chunk, 1].astype(F32) + got[slot, 1].astype(F32)).astype(BF16)

    for k in range(chunks):

        @pl.when(s == chunks + k)
        def _():
            def keep(z, carry):
                rows = pl.ds(pl.multiple_of((2 * z + 1 - y) * r, r), r)
                size = gup_ref.shape[2]
                diagonal[0, z, :, k * size : (k + 1) * size] = gup_ref[0, rows, :]
                diagonal[1, z, :, k * size : (k + 1) * size] = gdown_ref[0, rows, :]
                return carry

            lax.fori_loop(0, m, keep, 0)
            if k == chunks - 1:
                for copy in across:
                    copy.start()

    @pl.when(s == pl.num_programs(0) - 1)
    def _():
        def norm_back(rows):
            third = back_ref[rows, :]
            upstream = dy_ref[rows, :].astype(F32)
            rows_grad, gain_terms = norm_rows_back(after_ref[rows, :], third, norm_ref[2, 0:1, :])
            rows_grad = rows_grad + upstream
            low = rows_grad.astype(BF16)
            rows_out[rows, :] = rows_grad
            low_out[rows, :] = low
            for k, terms in enumerate((gain_terms, third, low.astype(F32), upstream)):
                sums_ref[k : k + 1, :] += jnp.sum(terms, axis=0, keepdims=True)

        by_rows(x_ref.shape[0], 128, norm_back)
        for copy in across:
            copy.wait()


def feed_forward(x, dy, weights, bias, after, biases, norm):
    rows, width = x.shape
    hidden = weights[0].shape[2]
    size = min(512, hidden)
    chunks = hidden // size

    n = lax.axis_size("dp")
    m, r = n // 2, width // n

    def block(s):
        return 3 - s // chunks

    def placed(s):
        turn = s // chunks
        return (1 - turn // 2, 0, (s % chunks) * (turn % 2))

    rows_spec = const((rows, width))
    grad_spec = pl.BlockSpec((1, width, size), placed)
    bias_spec = pl.BlockSpec((1, 1, size), lambda s: (block(s), 0, s % chunks))
    return pl.pallas_call(
        functools.partial(feed_forward_kernel, chunks=chunks),
        grid=(4 * chunks,),
        in_specs=[
            rows_spec,
            rows_spec,
            ANY,
            ANY,
            ANY,
            ANY,
            const(bias.shape),
            rows_spec,
            const(biases.shape),
            const(norm.shape),
        ],
        out_specs=[rows_spec, rows_spec, rows_spec, const((8, width)), grad_spec, grad_spec, bias_spec, ANY, ANY],
        out_shape=[
            jax.ShapeDtypeStruct((rows, width), F32),
            jax.ShapeDtypeStruct((rows, width), F32),
            jax.ShapeDtypeStruct((rows, width), BF16),
            jax.ShapeDtypeStruct((8, width), F32),
            jax.ShapeDtypeStruct((2, width, hidden), BF16),
            jax.ShapeDtypeStruct((2, width, hidden), BF16),
            jax.ShapeDtypeStruct((4, 1, hidden), F32),
            jax.ShapeDtypeStruct((2, m // 2, r, hidden), BF16),
            jax.ShapeDtypeStruct((2, m - m // 2, r, hidden), BF16),
        ],
        scratch_shapes=[
            pltpu.VMEM((width, rows), BF16),
            pltpu.VMEM((width, rows), BF16),
            pltpu.VMEM((rows, width), F32),
            pltpu.VMEM((chunks, 2, width, size), BF16),
            pltpu.VMEM((2 * chunks, 2, width, size), BF16),
            pltpu.VMEM((2, m, r, hidden), BF16),
            pltpu.VMEM((2, 2, width, size), BF16),
            pltpu.SemaphoreType.DMA((2, 2)),
        ]
        + link_scratch(2 * chunks + 2, 1),
        compiler_params=pltpu.CompilerParams(
            vmem_limit_bytes=VMEM_LIMIT, collective_id=3, has_side_effects=True
        ),
        cost_estimate=pl.CostEstimate(
            flops=48 * rows * width * hidden, bytes_accessed=40 * 2**20, transcendentals=8 * rows * hidden
        ),
        name="feed_forward",
    )(x, dy, *weights, bias, after, biases, norm)


def cross_backward_kernel(
    len_ref, low_ref, x_ref, enc_ref, w_ref, q_ref, k_ref, v_ref, mt_ref, lse_ref, up_ref, down_ref, from_x, from_y,
    back_ref, enc_out, grad_ref, bq_ref, bv_ref, up_out, down_out,
    low_t, x_t, enc_t, enc_acc, give, got, *scratch, heads, bk
):
    i = pl.program_id(0)
    last = pl.num_programs(0) - 1
    links = Links(*scratch[14:])
    sums = [
        Gather(links, ref.at[0], ref.at[1], from_x.at[k], from_y.at[k], scratch[7 * k : 7 * k + 7])
        for k, ref in enumerate((up_ref, down_ref))
    ]
    leave = [links.local(g.column, out) for g, out in zip(sums, (up_out, down_out))]
    pair = i // 2
    to_core = pltpu.make_async_remote_copy(
        src_ref=give,
        dst_ref=got.at[pair],
        send_sem=links.send_sems.at[links.used + pair],
        recv_sem=links.recv_sems.at[links.used + pair],
        device_id=links.partner(CORE),
        device_id_type=pl.DeviceIdType.MESH,
    )

    @pl.when(i == 0)
    def _():
        links.greet([CORE, X, Y])
        for g in sums:
            g.start()
        low_t[...] = low_ref[...].T
        x_t[...] = x_ref[...].T
        enc_t[...] = enc_ref[...].T
        back_ref[...] = jnp.zeros_like(back_ref)
        enc_acc[...] = jnp.zeros_like(enc_acc)

    @pl.when(i == 1)
    def _():
        for g in sums:
            g.middle()

    rows, width = q_ref.shape[1:]
    n = k_ref.shape[1]
    hd = width // heads
    scale = 1.0 / math.sqrt(hd)
    w_query, w_keyval, w_out = w_ref.at[0, :, :width], w_ref.at[0, :, width : 3 * width], w_ref.at[0, :, 3 * width :]
    grads = dot_nn(low_ref[...], w_out[...]).astype(BF16)
    mixed_t = mt_ref[0]
    products = grads.T.astype(F32) * mixed_t.astype(F32)
    inner = [jnp.sum(products[h * hd : (h + 1) * hd, :], axis=0, keepdims=True) for h in range(heads)]
    scaled = q_ref[0] * jnp.asarray(scale, BF16)
    q_heads = [head_only(scaled, h, hd) for h in range(heads)]
    d_heads = [head_only(grads, h, hd) for h in range(heads)]
    lse = lse_ref[0]
    keys_t = k_ref[0].T
    dq = [None] * heads
    dkv = []
    for j in range(n // bk):
        span = slice(j * bk, (j + 1) * bk)
        ok = j * bk + lax.broadcasted_iota(jnp.int32, (bk, 1), 0) < len_ref[0]
        scores = [dot_nt(k_ref[0, span, lanes_of(h, hd)[1]], q_heads[h]) for h in range(heads)]
        dprobs = [dot_nt(v_ref[0, span, lanes_of(h, hd)[1]], d_heads[h]) for h in range(heads)]
        dv_sums, dk_sums = {}, {}
        for h in range(heads):
            part = slice(h * hd, (h + 1) * hd)
            group, _ = lanes_of(h, hd)
            probs = jnp.exp(jnp.where(ok, scores[h], NEGATIVE) - lse[h : h + 1, :])
            ds = (probs * (dprobs[h] - inner[h])).astype(BF16)
            add_group(dv_sums, group, dot_nn(probs.astype(BF16), d_heads[h]))
            add_group(dk_sums, group, dot_nn(ds, q_heads[h]))
            dq_h = dot_nn(keys_t[part, span], ds)
            dq[h] = dq_h if dq[h] is None else dq[h] + dq_h
        block = jnp.concatenate([sums_of[g].astype(BF16) for sums_of in (dk_sums, dv_sums) for g in sorted(sums_of)], 1)
        enc_acc[span, :] += dot_nt(block, w_keyval[...])
        dkv.append(block)
    dq = (jnp.concatenate(dq, 0) * scale).astype(BF16).T
    dkv = jnp.concatenate(dkv, 0)
    bq_ref[0] = jnp.sum(dq.astype(F32), axis=0, keepdims=True)
    bv_ref[0] = jnp.sum(dkv[:, width:].astype(F32), axis=0, keepdims=True)
    back_ref[...] += dot_nt(dq, w_query[...])

    @pl.when(i % 2 == 1)
    def _():
        to_core.wait_send()

    give[:, :width] = dot_nn(x_t[...], dq).astype(BF16)
    give[:, width : 3 * width] = dot_nn(enc_t[...], dkv).astype(BF16)
    give[:, 3 * width :] = dot_nn(low_t[...], mixed_t.T).astype(BF16)

    @pl.when(i % 2 == 0)
    def _():
        to_core.start()

    @pl.when(i % 2 == 1)
    def _():
        to_core.wait_recv()
        grad_ref[0] = (give[...].astype(F32) + got[pair].astype(F32)).astype(BF16)

    @pl.when(i == last)
    def _():
        enc_out[...] = enc_acc[...].astype(BF16)
        for g, copy in zip(sums, leave):
            g.end()
            copy.start()
        for copy in leave:
            copy.wait()


def cross_backward(
    lengths, low, x, encoder, weights, queries, keys, values, mixed_t, lse, up_sum, down_sum, from_x, from_y, heads
):
    count, model = x.shape
    n = encoder.shape[0]
    parts, _, columns = weights.shape
    width = columns // 4
    _, m, _, r, c = up_sum.shape

    def by_part(*shape):
        return pl.BlockSpec((1,) + shape, lambda i: (i ^ 1,) + (0,) * len(shape))

    return pl.pallas_call(
        functools.partial(cross_backward_kernel, heads=heads, bk=256),
        grid=(parts,),
        in_specs=[
            pl.BlockSpec(memory_space=pltpu.SMEM),
            const((count, model)),
            const((count, model)),
            const((n, model)),
            by_part(model, columns),
            by_part(count, width),
            by_part(n, width),
            by_part(n, width),
            by_part(width, count),
            by_part(heads, count),
            ANY,
            ANY,
            ANY,
            ANY,
        ],
        out_specs=[
            const((count, model)),
            const((n, model)),
            pl.BlockSpec((1, model, columns), lambda i: (i // 2, 0, 0), pipeline_mode=pl.Buffered(1)),
            by_part(1, width),
            by_part(1, width),
            ANY,
            ANY,
        ],
        out_shape=[
            jax.ShapeDtypeStruct((count, model), F32),
            jax.ShapeDtypeStruct((n, model), BF16),
            jax.ShapeDtypeStruct((2, model, columns), BF16),
            jax.ShapeDtypeStruct((parts, 1, width), F32),
            jax.ShapeDtypeStruct((parts, 1, width), F32),
            jax.ShapeDtypeStruct((m, r, c), BF16),
            jax.ShapeDtypeStruct((m, r, c), BF16),
        ],
        scratch_shapes=[
            pltpu.VMEM((model, count), BF16),
            pltpu.VMEM((model, count), BF16),
            pltpu.VMEM((model, n), BF16),
            pltpu.VMEM((n, model), F32),
            pltpu.VMEM((model, columns), BF16),
            pltpu.VMEM((2, model, columns), BF16),
        ]
        + gather_scratch(m, r, c) * 2
        + link_scratch(10, 12),
        compiler_params=pltpu.CompilerParams(
            vmem_limit_bytes=60 * 2**20, collective_id=4, has_side_effects=True
        ),
        cost_estimate=pl.CostEstimate(
            flops=48 * parts * count * n * width,
            bytes_accessed=16 * parts * n * width,
            transcendentals=parts * count * n * heads,
        ),
        name="cross_backward",
    )(lengths, low, x, encoder, weights, queries, keys, values, mixed_t, lse, up_sum, down_sum, from_x, from_y)


def on_device(
    block_in,
    encoder_out,
    out_grad,
    bounds,
    enc_lengths,
    norm_params,
    w_qkv,
    w_self_out,
    w_cross_q,
    w_cross_kv,
    w_cross_out,
    w_up,
    w_down,
    biases,
    up_bias,
):
    groups_count = lax.axis_size("dp")
    width = w_cross_q.shape[1]
    hidden_width = w_up.shape[1]
    heads = H // 4
    own_rows, model_width = block_in.shape
    w_rows = w_cross_q.shape[0]

    first_in, self_w, cross_column, down_square, enc_all = start_gather(
        block_in,
        norm_params,
        w_qkv,
        w_self_out,
        w_cross_q,
        w_cross_kv,
        w_cross_out,
        w_down,
        encoder_out,
    )
    self_w = self_w.reshape(model_width, 4 * width)

    self_safe = 1024
    queries, key_rows, value_rows, keys_t, self_mixed_t, self_lse, terms, cross_w, up_column, near_z = self_forward(
        bounds,
        first_in,
        self_w,
        biases,
        cross_column,
        w_up,
        down_square,
        heads,
        self_safe,
    )
    cross_w = cross_w.reshape(4, model_width, 4 * width)
    after_self, second_in, near_up, near_down, far_z = sum_after_self(
        terms, block_in, biases, norm_params, up_column, down_square, near_z
    )

    cross_q, cross_k, cross_v, cross_mixed_t, cross_lse, after_cross, third_in, far_up, far_down = cross_forward(
        enc_lengths,
        second_in,
        enc_all,
        cross_w,
        biases,
        after_self,
        norm_params,
        up_column,
        down_square,
        far_z,
        heads,
    )

    output, cross_rows_grad, cross_low, ffn_sums, up_sum, down_sum, bias_up_parts, from_x, from_y = feed_forward(
        third_in,
        out_grad,
        [w.reshape(2, model_width, hidden_width) for w in (near_up, near_down, far_up, far_down)],
        up_bias.reshape(-1, LANES),
        after_cross,
        biases,
        norm_params,
    )

    by_shard = (2, groups_count // 2, 2, w_rows, hidden_width)
    second_grad, enc_terms, cross_sum, bias_cq_parts, bias_cv_parts, up_column, down_column = cross_backward(
        enc_lengths,
        cross_low,
        second_in,
        enc_all,
        cross_w,
        cross_q,
        cross_k,
        cross_v,
        cross_mixed_t,
        cross_lse,
        up_sum.reshape(by_shard),
        down_sum.reshape(by_shard),
        from_x,
        from_y,
        heads,
    )
    cross_sum = cross_sum.reshape(2, groups_count // 2, 2, w_rows, 4 * width)

    (
        self_dq, self_dk, self_dv, self_wide, self_rows_grad, self_sums,
        summed_up, summed_down, cross_column, enc_near, enc_far,
    ) = self_backward(
        bounds,
        queries,
        key_rows,
        value_rows,
        keys_t,
        self_w,
        self_mixed_t,
        self_lse,
        second_grad,
        after_self,
        cross_rows_grad,
        norm_params,
        up_column,
        down_column,
        cross_sum,
        enc_terms,
        heads,
        self_safe,
    )
    input_grad, summed_self, vectors, summed_cross, encoder_grad = tail(
        self_dq,
        self_dk,
        self_dv,
        self_w,
        first_in,
        self_wide,
        self_mixed_t,
        block_in,
        self_rows_grad,
        cross_column,
        norm_params,
        self_sums,
        ffn_sums,
        bias_cq_parts,
        bias_cv_parts,
        bias_up_parts,
        enc_near,
        enc_far,
    )
    output, input_grad, encoder_grad, *weights_and_vectors = results(
        output, input_grad, encoder_grad, summed_self, summed_cross, summed_up, summed_down, vectors, 1.0 / groups_count
    )
    g_qkv, g_so, g_cq, g_ckv, g_co, g_up, g_down, g_norm, g_biases, g_shift = weights_and_vectors
    return (
        output,
        input_grad,
        encoder_grad,
        g_norm,
        g_qkv,
        g_so,
        g_cq,
        g_ckv,
        g_co,
        g_up,
        g_down,
        g_biases,
        g_shift.reshape(-1),
    )


def solution(mesh):
    rows = P(("dp", "tensor"), None)
    placed = (
        rows,
        rows,
        rows,
        P("dp", None),
        P("dp"),
        P(),
        P("dp", None, "tensor"),
        P("tensor", "dp"),
        P("dp", "tensor"),
        P("dp", None, "tensor"),
        P("tensor", "dp"),
        P("dp", "tensor"),
        P("tensor", "dp"),
        P(),
        P(),
    )
    return jax.shard_map(
        on_device,
        mesh=mesh,
        in_specs=placed,
        out_specs=(
            rows,
            rows,
            rows,
            P(),
            P("dp", None, "tensor"),
            P("tensor", "dp"),
            P("dp", "tensor"),
            P("dp", None, "tensor"),
            P("tensor", "dp"),
            P("dp", "tensor"),
            P("tensor", "dp"),
            P(),
            P(),
        ),
        check_vma=False,
    )
```
